32 devices in a mesh: space: 16 (over z, y, x), dp: 2 (over core).
Axes of the slice: x: 2, y: 2, z: 4, core: 2. Of those that a mesh axis runs over, the one named last changes fastest.
Arguments:
- coarse_latents: bfloat16 [2, 1024, 512], P('dp', 'space'), may hold values from -6 to 6
- active_blocks: int32 [2, 32], P('dp'), may hold values from 0 to 1023, as said below
- face_links: int32 [2, 32, 6], P('dp', 'space'), may hold values from -1 to 31, as said below
- cotangent: bfloat16 [2, 32, 8, 8, 256], P('dp', 'space'), may hold values from -6 to 6
- up_weight: bfloat16 [64, 2048], replicated, may hold values from -0.75 to 0.75
- conv_one: bfloat16 [27, 32, 32], replicated, may hold values from -0.21875 to 0.21875
- conv_two: bfloat16 [27, 32, 32], replicated, may hold values from -0.21875 to 0.21875
Outputs:
- fine: bfloat16 [2, 32, 8, 8, 256], P('dp', 'space')
- grad_one: float32 [27, 32, 32], replicated
- grad_two: float32 [27, 32, 32], replicated
The draws below stay inside these ranges and needn't reach their ends.
Inputs may be any that keep to these rules, and one draw needn't show every extreme that they name: `active_blocks`: call the bricks at positions i * 2 to (i + 1) * 2 - 1 group i and the block rows i * 64 to (i + 1) * 64 - 1 range i. At most 2 bricks of one group take their blocks from one range, and in every scene every group has exactly 2 from some range. `face_links`: links are mutual: if brick h is the neighbour of g across face f, g is the neighbour of h across the opposite face. A neighbour of brick g lies at a position whose quotient by 2 differs from that of g by at most one; across a -x, -y or -z face that quotient is never larger than that of g, across a +x, +y or +z face never smaller.
All inputs are finite; a program needn't handle non-finite values.
Results may differ from the reference program's by a relative error of at most 0.0057.
Values may be sent and summed in bfloat16 or wider, within the bound.
No kernel may reach another device: no remote copies, remote signals or barrier semaphores. Data moves between devices by JAX's collectives and lax.ppermute only.
A program may use at most 128 MiB of HBM per device.

```python
import math
import jax
import jax.numpy as jnp
from jax import lax

C = 64
F = 32
EDGE = 8
PEER_MOST = 2
BR_DEV = 2
BLK_DEV = 64
SCENES = 2
BRICKS = 32
BLOCKS = 1024


def row_permutations(seed_key, row_count, length):
    subkeys = jax.random.split(seed_key, row_count)
    return jax.vmap(lambda subkey: jax.random.permutation(subkey, length))(subkeys).astype(jnp.int32)


def draw_active_blocks(key, part):
    devices = BRICKS // BR_DEV

    def scene_active(scene_key):
        key_perm, key_start, key_forced, key_other, key_local = jax.random.split(scene_key, 5)
        offsets_perm = row_permutations(key_perm, devices, devices)
        start = jax.random.randint(key_start, (devices,), 0, devices).astype(jnp.int32)
        forced = jax.random.randint(key_forced, (), 0, devices).astype(jnp.int32)
        other = (forced + 1 + jax.random.randint(key_other, (), 0, devices - 1)) % devices
        device_index = jnp.arange(devices, dtype=jnp.int32)
        start = jnp.where(device_index == forced, devices // 2, start)
        start = jnp.where(device_index == other, devices - 1, start)
        rotated = (offsets_perm - offsets_perm[:, :1] + start[:, None]) % devices
        column = jnp.maximum(jnp.arange(BR_DEV, dtype=jnp.int32) - PEER_MOST + 1, 0)
        offsets = rotated[:, column]
        owners = (device_index[:, None] + offsets) % devices
        local = jax.random.randint(key_local, (devices, BR_DEV), 0, BLK_DEV).astype(jnp.int32)
        return (owners * BLK_DEV + local).reshape(-1).astype(jnp.int32)
    return jax.vmap(scene_active)(jax.random.split(key, SCENES))


def draw_face_links(key, part):
    devices = BRICKS // BR_DEV

    def scene_links(scene_key):
        columns = []
        for axis_index in range(3):
            key_perm, key_shift, key_keep = jax.random.split(jax.random.fold_in(scene_key, axis_index + 11), 3)
            local_perm = row_permutations(key_perm, devices, BR_DEV)
            bases = jnp.arange(devices, dtype=jnp.int32)[:, None] * BR_DEV
            ordering = (bases + local_perm).reshape(-1)
            inverse = (bases + jnp.argsort(local_perm, axis=1).astype(jnp.int32)).reshape(-1)
            stride = jax.random.randint(key_shift, (), 1, BR_DEV + 1)
            keeping = jax.random.randint(key_keep, (BRICKS,), 0, 4) > 0
            upper = inverse + stride
            upper_safe = jnp.minimum(upper, BRICKS - 1)
            plus = jnp.where((upper < BRICKS) & keeping[inverse], ordering[upper_safe], -1)
            lower = inverse - stride
            lower_safe = jnp.maximum(lower, 0)
            minus = jnp.where((lower >= 0) & keeping[lower_safe], ordering[lower_safe], -1)
            columns.append(minus)
            columns.append(plus)
        return jnp.stack(columns, axis=1).astype(jnp.int32)
    return jax.vmap(scene_links)(jax.random.split(key, SCENES))


def levels(stream_key, dims, shards, smallest, top_value):
    def one(dim, blocks):
        heights = jax.random.uniform(jax.random.fold_in(jax.random.fold_in(stream_key, 6), dim), (blocks,), jnp.float32, smallest / len(shards), top_value / len(shards))
        return jnp.repeat(jnp.exp(heights), dims[dim] // blocks).reshape((-1,) + (1,) * (len(dims) - dim - 1))

    loudness = one(*shards[0])
    for cut in shards[1:]:
        loudness = loudness * one(*cut)
    return loudness


def bell_draw(key, extent, spread, most, cuts=(), kind=jnp.bfloat16):
    drawn = jax.random.normal(key, extent, jnp.float32) * spread
    if len(cuts) > 0:
        drawn = levels(key, extent, cuts, -0.22, 0.18) * drawn
    return jnp.clip(drawn, min=-most, max=most).astype(kind)


def setup_inputs(seed: int = 0) -> dict:
    splits = jax.random.split(jax.random.key(seed), 8)
    return {
        "coarse_latents": bell_draw(splits[0], (SCENES, BLOCKS, 8 * C), 1.0, 6.0, ((0, 2), (1, 16))),
        "active_blocks": draw_active_blocks(jax.random.fold_in(splits[7], 71), 0),
        "face_links": draw_face_links(jax.random.fold_in(splits[7], 71), 0),
        "cotangent": bell_draw(splits[3], (SCENES, BRICKS, EDGE, EDGE, EDGE * F), 1.0, 6.0, ((0, 2), (1, 16))),
        "up_weight": bell_draw(splits[4], (C, (EDGE // 2) ** 3 * F), C ** -0.5, 0.75),
        "conv_one": bell_draw(splits[5], (27, F, F), (27 * F) ** -0.5, 0.21875),
        "conv_two": bell_draw(splits[6], (27, F, F), (27 * F) ** -0.5, 0.21875),
    }


def lift_bricks(latent_rows, up_weight):
    bricks_total = latent_rows.shape[0]
    blocks = latent_rows.reshape(bricks_total, 8, C).astype(jnp.float32)
    cells = jnp.einsum('nci,io->nco', blocks, up_weight.astype(jnp.float32))
    half = EDGE // 2
    shaped = cells.reshape(bricks_total, 2, 2, 2, half, half, half, F)
    shaped = shaped.transpose(0, 1, 4, 2, 5, 3, 6, 7)
    return shaped.reshape(bricks_total, EDGE, EDGE, EDGE, F).astype(jnp.bfloat16)

def pad_faces(volume, face_links):
    bricks_total = volume.shape[0]
    neighbour = jnp.maximum(face_links, 0)
    present = (face_links >= 0).astype(jnp.float32)[:, :, None, None, None]
    last = EDGE - 1
    padded = jnp.zeros((bricks_total, EDGE + 2, EDGE + 2, EDGE + 2, F), jnp.float32)
    padded = padded.at[:, 1:EDGE + 1, 1:EDGE + 1, 1:EDGE + 1].set(volume)
    padded = padded.at[:, 0, 1:EDGE + 1, 1:EDGE + 1].set(volume[neighbour[:, 0], last] * present[:, 0])
    padded = padded.at[:, EDGE + 1, 1:EDGE + 1, 1:EDGE + 1].set(volume[neighbour[:, 1], 0] * present[:, 1])
    padded = padded.at[:, 1:EDGE + 1, 0, 1:EDGE + 1].set(volume[neighbour[:, 2], :, last] * present[:, 2])
    padded = padded.at[:, 1:EDGE + 1, EDGE + 1, 1:EDGE + 1].set(volume[neighbour[:, 3], :, 0] * present[:, 3])
    padded = padded.at[:, 1:EDGE + 1, 1:EDGE + 1, 0].set(volume[neighbour[:, 4], :, :, last] * present[:, 4])
    padded = padded.at[:, 1:EDGE + 1, 1:EDGE + 1, EDGE + 1].set(volume[neighbour[:, 5], :, :, 0] * present[:, 5])
    return padded

def window_at(padded, start_x, start_y, start_z):
    return padded[:, start_x:start_x + EDGE, start_y:start_y + EDGE, start_z:start_z + EDGE]

def conv_forward(padded, weights):
    total = jnp.zeros(padded.shape[:1] + (EDGE, EDGE, EDGE, F), jnp.float32)
    for offset_index in range(27):
        shift_x, shift_y, shift_z = (offset_index // 9, offset_index // 3 % 3, offset_index % 3)
        window = window_at(padded, shift_x, shift_y, shift_z)
        total = total + jnp.einsum('nxyzi,io->nxyzo', window, weights[offset_index])
    return total

def conv_backward(padded, weights):
    total = jnp.zeros(padded.shape[:1] + (EDGE, EDGE, EDGE, F), jnp.float32)
    for offset_index in range(27):
        shift_x, shift_y, shift_z = (offset_index // 9, offset_index // 3 % 3, offset_index % 3)
        window = window_at(padded, 2 - shift_x, 2 - shift_y, 2 - shift_z)
        total = total + jnp.einsum('nxyzo,io->nxyzi', window, weights[offset_index])
    return total

def weight_grad(padded, gradient):
    pieces = []
    for offset_index in range(27):
        shift_x, shift_y, shift_z = (offset_index // 9, offset_index // 3 % 3, offset_index % 3)
        window = window_at(padded, shift_x, shift_y, shift_z)
        pieces.append(jnp.einsum('nxyzi,nxyzo->io', window, gradient))
    return jnp.stack(pieces)

def reference(coarse_latents, active_blocks, face_links, cotangent, up_weight, conv_one, conv_two):
    weights_one = conv_one.astype(jnp.float32)
    weights_two = conv_two.astype(jnp.float32)

    def scene_step(inputs):
        coarse_scene, active_scene, links_scene, upstream = inputs
        lifted = lift_bricks(coarse_scene[active_scene], up_weight).astype(jnp.float32)
        lifted_pad = pad_faces(lifted, links_scene)
        pre = conv_forward(lifted_pad, weights_one)
        hidden = jax.nn.silu(pre).astype(jnp.bfloat16).astype(jnp.float32)
        hidden_pad = pad_faces(hidden, links_scene)
        fine = (lifted + conv_forward(hidden_pad, weights_two)).astype(jnp.bfloat16)
        upstream_full = upstream.reshape(BRICKS, EDGE, EDGE, EDGE, F).astype(jnp.float32)
        back = conv_backward(pad_faces(upstream_full, links_scene), weights_two)
        sigmoid = jax.nn.sigmoid(pre)
        grad_pre = (back * sigmoid * (1.0 + pre * (1.0 - sigmoid))).astype(jnp.bfloat16).astype(jnp.float32)
        second = weight_grad(hidden_pad, upstream_full)
        first = weight_grad(lifted_pad, grad_pre)
        return (fine.reshape(BRICKS, EDGE, EDGE, EDGE * F), first, second)
    fine, firsts, seconds = lax.map(scene_step, (coarse_latents, active_blocks, face_links, cotangent))
    scale = 1.0 / math.sqrt(SCENES * BRICKS * EDGE ** 3)
    return (fine, lax.optimization_barrier(jnp.sum(firsts, axis=0)) * scale, lax.optimization_barrier(jnp.sum(seconds, axis=0)) * scale)
```

```python
import functools
import math

import jax
import jax.numpy as jnp
from jax import lax
from jax.experimental import pallas as pl
from jax.experimental.pallas import tpu as pltpu
from jax.sharding import PartitionSpec as P

BF16 = jnp.bfloat16
F32 = jnp.float32
EDGE = 8
CHANNELS = 32
LINE = EDGE * CHANNELS
WIDE = LINE + 128
BRICKS = 2
CUBE = EDGE * EDGE
LINES = BRICKS * CUBE
FACE = 3 * EDGE
BLOCKS = 54


def dot(left, right):
    return jnp.dot(left, right, preferred_element_type=F32)


def dot_rows(left, right):
    return lax.dot_general(left, right, (((0,), (0,)), ((), ())), preferred_element_type=F32)


def lines(halves_ref, start, count, stride=1):
    index = pl.ds(start, count, stride=stride) if stride > 1 else pl.ds(start, count)
    return jnp.concatenate([halves_ref[0, index, :], halves_ref[1, index, :]], axis=-1)


def lanes_of(shape):
    return lax.broadcasted_iota(jnp.int32, shape, len(shape) - 1)


def pick_kernel(devices, ids_ref, latents_ref, out_ref, rows_ref):
    held = latents_ref.shape[1]
    bricks = ids_ref.shape[1]
    first = lax.axis_index("space") * held
    rows = lax.broadcasted_iota(jnp.int32, (held, bricks), 0) + first
    hot = jnp.where(rows == ids_ref[...], 1.0, 0.0).astype(BF16)
    rows_ref[0:8] = jnp.zeros((8, rows_ref.shape[1]), F32)
    rows_ref[8 : 8 + bricks] = dot_rows(hot, latents_ref[0])
    rows_ref[8 + bricks : 16 + bricks] = jnp.zeros((8, rows_ref.shape[1]), F32)
    for receiver in range(devices):
        start = 8 + BRICKS * (receiver - 1)
        out_ref[receiver] = rows_ref[start : start + 8].astype(BF16)


def build_band(band_ref, rows):
    shape = (3 * CHANNELS, LINE)
    row = lax.broadcasted_iota(jnp.int32, shape, 0)
    target = CHANNELS - (row // CHANNELS) * CHANNELS + row % CHANNELS
    distance = lanes_of(shape) - target
    band_ref[:, LINE:, :] = jnp.zeros((9, 128, LINE), BF16)
    places = [(z, z * CHANNELS) for z in range(EDGE)] + [(EDGE, LINE), (-1, WIDE - CHANNELS)]
    for z, start in places:
        select = jnp.where(distance == z * CHANNELS, 1.0, 0.0).astype(BF16)
        block = dot(rows, select).astype(BF16)
        band_ref[:, start : start + CHANNELS, :] = block.reshape(9, CHANNELS, LINE)


def weight_rows(weights):
    cube = weights.reshape(9, 3, CHANNELS, CHANNELS)
    rows = jnp.concatenate([cube[:, 0], cube[:, 1], cube[:, 2]], axis=-1)
    return rows.reshape(9 * CHANNELS, 3 * CHANNELS).astype(BF16)


def flipped_rows(weights):
    cube = jnp.swapaxes(weights, 1, 2).reshape(9, 3, CHANNELS, CHANNELS)
    pieces = [jnp.concatenate([cube[8 - k, 2], cube[8 - k, 1], cube[8 - k, 0]], axis=-1) for k in range(9)]
    return jnp.concatenate(pieces, axis=0).astype(BF16)


def put_padded(pad_ref, brick, volume, x_low, x_high, y_low, y_high, z_low, z_high):
    lane = lanes_of((EDGE, EDGE, 128))
    tail = jnp.where(lane < CHANNELS, z_high, jnp.where(lane >= 128 - CHANNELS, z_low, 0.0))
    full = jnp.concatenate([volume, tail], axis=-1)
    zeros = jnp.zeros((EDGE, 128), F32)
    first = jnp.concatenate([x_low, zeros], axis=-1)[None]
    last = jnp.concatenate([x_high, zeros], axis=-1)[None]
    slabs = jnp.concatenate([first, full, last], axis=0)
    no_halo = jnp.zeros((1, WIDE), F32)
    low = jnp.concatenate([no_halo, jnp.concatenate([y_low, zeros], axis=-1), no_halo], axis=0)
    high = jnp.concatenate([no_halo, jnp.concatenate([y_high, zeros], axis=-1), no_halo], axis=0)
    row = lax.broadcasted_iota(jnp.int32, slabs.shape, 1)
    pad_ref[0, brick] = jnp.where(row == 0, low[:, None, :], pltpu.roll(slabs, 1, 1))
    pad_ref[1, brick] = slabs
    pad_ref[2, brick] = jnp.where(row == EDGE - 1, high[:, None, :], pltpu.roll(slabs, EDGE - 1, 1))


def window(pad_ref, k):
    lines = pad_ref[k % 3, :, k // 3 : k // 3 + EDGE]
    return lines.reshape(LINES, WIDE).astype(BF16)


def convolve(pad_ref, band_ref):
    total = None
    for k in range(9):
        term = dot(window(pad_ref, k), band_ref[k])
        total = term if total is None else total + term
    return total


def pack_faces(faces_ref, base, halves_ref, start, high):
    first = start + ((EDGE - 1) * EDGE if high else 0)
    faces_ref[base : base + EDGE] = lines(halves_ref, first, EDGE)
    first = start + (EDGE - 1 if high else 0)
    faces_ref[base + EDGE : base + 2 * EDGE] = lines(halves_ref, first, EDGE, EDGE)
    tile = halves_ref[1 if high else 0, start : start + CUBE, :]
    lane = lanes_of((16, 128)) // CHANNELS
    packed = jnp.zeros((16, 128), F32)
    for part in range(4):
        shift = (part + 1 if high else part) % 4 * CHANNELS
        piece = tile[part * 16 : part * 16 + 16]
        packed = jnp.where(lane == part, pltpu.roll(piece, shift, 1) if shift else piece, packed)
    faces_ref[base + 2 * EDGE : base + FACE, :128] = packed[:8]
    faces_ref[base + 2 * EDGE : base + FACE, 128:] = packed[8:]


def unpack_depth(rows, high):
    packed = jnp.concatenate([rows[:, :128], rows[:, 128:]], axis=0)
    pieces = []
    for part in range(4):
        shift = ((3 - part) if high else (4 - part)) % 4 * CHANNELS
        pieces.append(pltpu.roll(packed, shift, 1) if shift else packed)
    return jnp.concatenate(pieces, axis=0).reshape(EDGE, EDGE, 128)


def first_kernel(
    links_ref, received_ref, up_ref, one_ref, cotangent_ref,
    lifted_out, pre_out, hidden_out, pad_out, high_out, low_out,
    volumes_ref, pad_ref, band_ref, lines_ref, high_ref, low_ref,
):
    position = lax.axis_index("space")
    latents = jnp.sum(received_ref[...].astype(F32), axis=0)
    cells = [latents[:, cell * 64 : cell * 64 + 64] for cell in range(8)]
    lifted = dot(jnp.concatenate(cells, axis=0).astype(BF16), up_ref[...])
    lifted = lifted.astype(BF16).astype(F32)
    for cell in range(8):
        a, b, c = cell // 4, cell // 2 % 2, cell % 2
        for sub in range(16):
            line = (4 * a + sub // 4) * EDGE + 4 * b + sub % 4
            volumes_ref[c, pl.ds(line, 8, stride=CUBE), :] = lifted[
                cell * 8 : cell * 8 + 8, sub * 128 : sub * 128 + 128
            ]
    for brick in range(BRICKS):

        def near(face):
            link = links_ref[0, brick, face]
            index = jnp.clip(link - BRICKS * (position - 1), 0, 3 * BRICKS - 1)
            return pl.multiple_of(index * CUBE, CUBE), jnp.where(link >= 0, 1.0, 0.0).astype(F32)

        def x_face(face):
            start, present = near(face)
            offset = EDGE * (EDGE - 1) if face % 2 == 0 else 0
            return lines(volumes_ref, pl.multiple_of(start + offset, 8), EDGE) * present

        def y_face(face):
            start, present = near(face)
            offset = EDGE - 1 if face % 2 == 0 else 0
            return lines(volumes_ref, start + offset, EDGE, EDGE) * present

        def z_face(face):
            start, present = near(face)
            tile = volumes_ref[1 if face % 2 == 0 else 0, pl.ds(start, CUBE), :] * present
            return tile.reshape(EDGE, EDGE, 128)

        own = (BRICKS + brick) * CUBE
        volume = lines(volumes_ref, own, CUBE).reshape(EDGE, EDGE, LINE)
        put_padded(
            pad_ref, brick, volume, x_face(0), x_face(1), y_face(2), y_face(3), z_face(4), z_face(5)
        )
    build_band(band_ref, weight_rows(one_ref[...].astype(F32)))
    pre = convolve(pad_ref, band_ref)
    hidden = pre / (1.0 + jnp.exp(-pre))
    hidden = hidden.astype(BF16)
    lifted_out[...] = lines(volumes_ref, BRICKS * CUBE, LINES).astype(BF16)
    pre_out[...] = pre
    hidden_out[...] = hidden
    pad_out[...] = pad_ref[...].reshape(pad_out.shape).astype(BF16)
    sources = (hidden.astype(F32), cotangent_ref[...].astype(F32).reshape(LINES, LINE))
    for which, values in enumerate(sources):
        for half in range(2):
            lines_ref[half, which * LINES : which * LINES + LINES] = values[:, half * 128 : half * 128 + 128]
    for which in range(2):
        for brick in range(BRICKS):
            base = (which * BRICKS + brick) * FACE
            start = which * LINES + brick * CUBE
            pack_faces(high_ref, base, lines_ref, start, True)
            pack_faces(low_ref, base, lines_ref, start, False)
    high_out[...] = high_ref[...].astype(BF16)
    low_out[...] = low_ref[...].astype(BF16)


def fold_diagonals(outer_ref, part):
    lane = lanes_of((CHANNELS, 128)) // CHANNELS
    folded = None
    for half in range(2):
        picked = None
        for block in range(4):
            depth = 4 * half + block + part - 1
            start = depth * CHANNELS if 0 <= depth < EDGE else (LINE if depth == EDGE else WIDE - CHANNELS)
            rows = outer_ref[start : start + CHANNELS, half * 128 : half * 128 + 128]
            picked = rows if picked is None else jnp.where(lane == block, rows, picked)
        folded = picked if folded is None else folded + picked
    quarter = [folded[8 * q : 8 * q + 8] for q in range(4)]
    small = lanes_of((8, 128)) // CHANNELS
    total = None
    for turn in range(4):
        mixed = quarter[0]
        for q in range(1, 4):
            mixed = jnp.where(small == (q + turn) % 4, quarter[q], mixed)
        if turn:
            mixed = pltpu.roll(mixed, 128 - turn * CHANNELS, 1)
        total = mixed if total is None else total + mixed
    return total


def second_kernel(
    links_ref, cotangent_ref, two_ref, lifted_ref, pre_ref, hidden_ref, pad_in,
    high_own, low_own, high_left, low_right,
    fine_out, sums_out,
    high_ref, low_ref, hidden_pad, cotangent_pad, lifted_pad, band_ref, outer_ref,
):
    position = lax.axis_index("space")
    half = 2 * BRICKS * FACE
    high_ref[0:half] = high_left[...].astype(F32)
    high_ref[half:] = high_own[...].astype(F32)
    low_ref[0:half] = low_own[...].astype(F32)
    low_ref[half:] = low_right[...].astype(F32)
    lifted_pad[...] = pad_in[...].astype(F32).reshape(lifted_pad.shape)
    cotangent = cotangent_ref[...].astype(F32).reshape(LINES, LINE)
    hidden = hidden_ref[...].astype(F32)
    for which, values, pad_ref in ((0, hidden, hidden_pad), (1, cotangent, cotangent_pad)):
        for brick in range(BRICKS):

            def rows(face, axis):
                link = links_ref[0, brick, face]
                high = face % 2 == 0
                index = jnp.clip(link - BRICKS * (position - 1 if high else position), 0, 2 * BRICKS - 1)
                start = (index // BRICKS) * half + (which * BRICKS + index % BRICKS) * FACE + axis * EDGE
                pool = high_ref if high else low_ref
                present = jnp.where(link >= 0, 1.0, 0.0).astype(F32)
                return pool[pl.ds(pl.multiple_of(start, 8), EDGE), :] * present

            volume = values[brick * CUBE : brick * CUBE + CUBE].reshape(EDGE, EDGE, LINE)
            put_padded(
                pad_ref, brick, volume, rows(0, 0), rows(1, 0), rows(2, 1), rows(3, 1),
                unpack_depth(rows(4, 2), True), unpack_depth(rows(5, 2), False),
            )
    weights = two_ref[...].astype(F32)
    build_band(band_ref, weight_rows(weights))
    fine = lifted_ref[...].astype(F32) + convolve(hidden_pad, band_ref)
    fine_out[...] = fine.astype(BF16).reshape(fine_out.shape)
    build_band(band_ref, flipped_rows(weights))
    back = convolve(cotangent_pad, band_ref)
    pre = pre_ref[...]
    sigmoid = 1.0 / (1.0 + jnp.exp(-pre))
    gradient = (back * sigmoid * (1.0 + pre * (1.0 - sigmoid))).astype(BF16)
    upstream = cotangent.astype(BF16)
    sums_out[...] = jnp.zeros(sums_out.shape, F32)
    per = sums_out.shape[1] // 8
    for base, pad_ref, right in ((0, lifted_pad, gradient), (27, hidden_pad, upstream)):
        for k in range(9):
            outer_ref[...] = dot_rows(window(pad_ref, k), right)
            for part in range(3):
                index = base + 3 * k + part
                sums_out[index // per, index % per * 8 : index % per * 8 + 8] = fold_diagonals(outer_ref, part)


def sum_kernel(scale, parts_ref, out_ref):
    total = jnp.sum(parts_ref[...], axis=0) * scale
    out_ref[...] = jnp.broadcast_to(total[None], out_ref.shape)


def unpack_kernel(sums_ref, one_out, two_out):
    per = sums_ref.shape[1] // 8
    for index in range(BLOCKS):
        block = sums_ref[index // per, index % per * 8 : index % per * 8 + 8]
        out = one_out if index < 27 else two_out
        for q in range(4):
            moved = pltpu.roll(block, 128 - q * CHANNELS, 1) if q else block
            out[index % 27, 8 * q : 8 * q + 8, :] = moved[:, :CHANNELS]


def call(kernel, out_shape, scratch=(), smem_first=False, inputs=1, limit=24):
    specs = [pl.BlockSpec(memory_space=pltpu.VMEM)] * inputs
    if smem_first:
        specs[0] = pl.BlockSpec(memory_space=pltpu.SMEM)
    out_specs = jax.tree.map(lambda _: pl.BlockSpec(memory_space=pltpu.VMEM), out_shape)
    return pl.pallas_call(
        kernel,
        out_shape=out_shape,
        in_specs=specs,
        out_specs=out_specs,
        scratch_shapes=list(scratch),
        compiler_params=pltpu.CompilerParams(vmem_limit_bytes=limit * 2**20),
    )


def shape(*dims, dtype=BF16):
    return jax.ShapeDtypeStruct(dims, dtype)


def passed_along(value, axis, steps):
    count = lax.axis_size(axis)
    first, last = (max(0, -steps), min(count, count - steps))
    return lax.ppermute(value, axis, [(source, source + steps) for source in range(first, last)])


def body(coarse_latents, active_blocks, face_links, cotangent, up_weight, conv_one, conv_two):
    devices = lax.axis_size("space")
    everyone = devices * lax.axis_size("dp")
    width = coarse_latents.shape[2]
    bricks = active_blocks.shape[1]
    packed = call(
        functools.partial(pick_kernel, devices),
        shape(devices, 8, width),
        [pltpu.VMEM((bricks + 16, width), F32)],
        inputs=2,
    )(active_blocks, coarse_latents)
    received = lax.all_to_all(packed, "space", split_axis=0, concat_axis=0, tiled=True)
    pad_shape = (3, BRICKS, EDGE + 2, EDGE, WIDE)
    pad = pltpu.VMEM(pad_shape, F32)
    band = pltpu.VMEM((9, WIDE, LINE), BF16)
    packed_faces = 2 * BRICKS * FACE
    lifted, pre, hidden, lifted_pad, high, low = call(
        first_kernel,
        (
            shape(LINES, LINE),
            shape(LINES, LINE, dtype=F32),
            shape(LINES, LINE),
            shape(math.prod(pad_shape[:-1]), WIDE),
            shape(packed_faces, LINE),
            shape(packed_faces, LINE),
        ),
        [
            pltpu.VMEM((2, 8 * CUBE, 128), F32),
            pad,
            band,
            pltpu.VMEM((2, 2 * LINES, 128), F32),
            pltpu.VMEM((packed_faces, LINE), F32),
            pltpu.VMEM((packed_faces, LINE), F32),
        ],
        smem_first=True,
        inputs=5,
    )(face_links, received, up_weight, conv_one, cotangent)
    high_left = passed_along(high, "space", 1)
    low_right = passed_along(low, "space", -1)
    per = -(-BLOCKS // everyone)
    per += per % 2
    fine, sums = call(
        second_kernel,
        (shape(*cotangent.shape), shape(everyone, per * 8, 128, dtype=F32)),
        [
            pltpu.VMEM((2 * packed_faces, LINE), F32),
            pltpu.VMEM((2 * packed_faces, LINE), F32),
            pad,
            pad,
            pad,
            band,
            pltpu.VMEM((WIDE, LINE), F32),
        ],
        smem_first=True,
        inputs=11,
    )(face_links, cotangent, conv_two, lifted, pre, hidden, lifted_pad, high, low, high_left, low_right)
    axes = ("space", "dp")
    parts = lax.all_to_all(sums, axes, split_axis=0, concat_axis=0, tiled=True)
    scale = 1.0 / math.sqrt(lax.axis_size("dp") * devices * BRICKS * EDGE**3)
    total = call(functools.partial(sum_kernel, scale), shape(*sums.shape, dtype=F32))(parts)
    gathered = lax.all_to_all(total, axes, split_axis=0, concat_axis=0, tiled=True)
    grads = shape(27, CHANNELS, CHANNELS, dtype=F32)
    grad_one, grad_two = call(unpack_kernel, (grads, grads))(gathered)
    return (fine, grad_one, grad_two)


def solution(mesh):
    return jax.shard_map(
        body,
        mesh=mesh,
        in_specs=(
            P("dp", "space", None),
            P("dp", None),
            P("dp", "space", None),
            P("dp", "space", None, None, None),
            P(),
            P(),
            P(),
        ),
        out_specs=(P("dp", "space", None, None, None), P(), P()),
        check_vma=False,
    )
```

```python
import functools
import math

import jax
import jax.numpy as jnp
from jax import lax
from jax.experimental import pallas as pl
from jax.experimental.pallas import tpu as pltpu
from jax.sharding import PartitionSpec as P

BF16 = jnp.bfloat16
F32 = jnp.float32
EDGE = 8
CHANNELS = 32
LINE = EDGE * CHANNELS
WIDE = LINE + 128
BRICKS = 2
CUBE = EDGE * EDGE
LINES = BRICKS * CUBE
FACE = 3 * EDGE
BLOCKS = 54


def dot(left, right):
    return jnp.dot(left, right, preferred_element_type=F32)


def dot_rows(left, right):
    return lax.dot_general(left, right, (((0,), (0,)), ((), ())), preferred_element_type=F32)


def lines(halves_ref, start, count, stride=1):
    index = pl.ds(start, count, stride=stride) if stride > 1 else pl.ds(start, count)
    return jnp.concatenate([halves_ref[0, index, :], halves_ref[1, index, :]], axis=-1)


def lanes_of(shape):
    return lax.broadcasted_iota(jnp.int32, shape, len(shape) - 1)


def pick_kernel(devices, ids_hbm, latents_hbm, out_ref, ids_ref, latents_ref, rows_ref, sems):
    ids_copy = pltpu.make_async_copy(ids_hbm, ids_ref, sems.at[0])
    latents_copy = pltpu.make_async_copy(latents_hbm, latents_ref, sems.at[1])
    ids_copy.start()
    latents_copy.start()
    held, width = latents_ref.shape[1:]
    bricks = ids_ref.shape[1]
    margin = 8 * width // 128
    tiles = width // 128
    rows_ref[0:margin] = jnp.zeros((margin, 128), F32)
    rows_ref[margin + bricks * tiles :] = jnp.zeros((margin, 128), F32)
    first = lax.axis_index("space") * held
    rows = lax.broadcasted_iota(jnp.int32, (held, bricks), 0) + first
    ids_copy.wait()
    hot = jnp.where(rows == ids_ref[...], 1.0, 0.0).astype(BF16)
    latents_copy.wait()
    picked = dot_rows(hot, latents_ref[0])
    for tile in range(tiles):
        rows_ref[pl.ds(margin + tile, bricks, stride=tiles), :] = picked[:, tile * 128 : tile * 128 + 128]
    count = out_ref.shape[1]
    for receiver in range(devices):
        start = margin + BRICKS * (receiver - 1) * tiles
        out_ref[receiver] = rows_ref[start : start + count].astype(BF16)


def build_band(band_ref, rows):
    shape = (3 * CHANNELS, LINE)
    row = lax.broadcasted_iota(jnp.int32, shape, 0)
    target = CHANNELS - (row // CHANNELS) * CHANNELS + row % CHANNELS
    distance = lanes_of(shape) - target
    band_ref[:, LINE:, :] = jnp.zeros((9, 128, LINE), BF16)
    places = [(z, z * CHANNELS) for z in range(EDGE)] + [(EDGE, LINE), (-1, WIDE - CHANNELS)]
    for z, start in places:
        select = jnp.where(distance == z * CHANNELS, 1.0, 0.0).astype(BF16)
        block = dot(rows, select).astype(BF16)
        band_ref[:, start : start + CHANNELS, :] = block.reshape(9, CHANNELS, LINE)


def weight_rows(weights):
    cube = weights.reshape(9, 3, CHANNELS, CHANNELS)
    rows = jnp.concatenate([cube[:, 0], cube[:, 1], cube[:, 2]], axis=-1)
    return rows.reshape(9 * CHANNELS, 3 * CHANNELS).astype(BF16)


def flipped_rows(weights):
    cube = jnp.swapaxes(weights, 1, 2).reshape(9, 3, CHANNELS, CHANNELS)
    pieces = [jnp.concatenate([cube[8 - k, 2], cube[8 - k, 1], cube[8 - k, 0]], axis=-1) for k in range(9)]
    return jnp.concatenate(pieces, axis=0).astype(BF16)


def band_kernel(weights_ref, band_ref):
    build_band(band_ref, weight_rows(weights_ref[...].astype(F32)))


def two_bands_kernel(weights_ref, band_ref, back_ref):
    weights = weights_ref[...].astype(F32)
    build_band(band_ref, weight_rows(weights))
    build_band(back_ref, flipped_rows(weights))


def put_padded(pad_ref, brick, volume, x_low, x_high, y_low, y_high, z_low, z_high):
    lane = lanes_of((EDGE, EDGE, 128))
    tail = jnp.where(lane < CHANNELS, z_high, jnp.where(lane >= 128 - CHANNELS, z_low, 0.0))
    full = jnp.concatenate([volume, tail], axis=-1)
    zeros = jnp.zeros((EDGE, 128), F32)
    first = jnp.concatenate([x_low, zeros], axis=-1)[None]
    last = jnp.concatenate([x_high, zeros], axis=-1)[None]
    slabs = jnp.concatenate([first, full, last], axis=0)
    no_halo = jnp.zeros((1, WIDE), F32)
    low = jnp.concatenate([no_halo, jnp.concatenate([y_low, zeros], axis=-1), no_halo], axis=0)
    high = jnp.concatenate([no_halo, jnp.concatenate([y_high, zeros], axis=-1), no_halo], axis=0)
    row = lax.broadcasted_iota(jnp.int32, slabs.shape, 1)
    pad_ref[0, brick] = jnp.where(row == 0, low[:, None, :], pltpu.roll(slabs, 1, 1))
    pad_ref[1, brick] = slabs
    pad_ref[2, brick] = jnp.where(row == EDGE - 1, high[:, None, :], pltpu.roll(slabs, EDGE - 1, 1))


def window(pad_ref, k):
    lines = pad_ref[k % 3, :, k // 3 : k // 3 + EDGE]
    return lines.reshape(LINES, WIDE).astype(BF16)


def convolve(pad_ref, band_ref):
    total = None
    for k in range(9):
        term = dot(window(pad_ref, k), band_ref[k])
        total = term if total is None else total + term
    return total


def pack_faces(faces_ref, base, halves_ref, start, high):
    first = start + ((EDGE - 1) * EDGE if high else 0)
    faces_ref[base : base + EDGE] = lines(halves_ref, first, EDGE)
    first = start + (EDGE - 1 if high else 0)
    faces_ref[base + EDGE : base + 2 * EDGE] = lines(halves_ref, first, EDGE, EDGE)
    tile = halves_ref[1 if high else 0, start : start + CUBE, :]
    lane = lanes_of((16, 128)) // CHANNELS
    packed = jnp.zeros((16, 128), F32)
    for part in range(4):
        shift = (part + 1 if high else part) % 4 * CHANNELS
        piece = tile[part * 16 : part * 16 + 16]
        packed = jnp.where(lane == part, pltpu.roll(piece, shift, 1) if shift else piece, packed)
    faces_ref[base + 2 * EDGE : base + FACE, :128] = packed[:8]
    faces_ref[base + 2 * EDGE : base + FACE, 128:] = packed[8:]


def unpack_depth(rows, high):
    packed = jnp.concatenate([rows[:, :128], rows[:, 128:]], axis=0)
    pieces = []
    for part in range(4):
        shift = ((3 - part) if high else (4 - part)) % 4 * CHANNELS
        pieces.append(pltpu.roll(packed, shift, 1) if shift else packed)
    return jnp.concatenate(pieces, axis=0).reshape(EDGE, EDGE, 128)


def first_kernel(
    links_ref, received_ref, up_ref, band_ref, cotangent_ref,
    lifted_out, pre_out, hidden_out, pad_out, high_out, low_out,
    volumes_ref, pad_ref, lines_ref, high_ref, low_ref, rows_ref,
):
    position = lax.axis_index("space")
    tiles = received_ref.shape[1] // (3 * BRICKS)
    rows_ref[0 : 3 * BRICKS * tiles] = jnp.sum(received_ref[...].astype(F32), axis=0)
    rows_ref[3 * BRICKS * tiles :] = jnp.zeros((2 * tiles, 128), F32)
    cells = []
    for tile in range(tiles):
        rows = rows_ref[pl.ds(tile, 8, stride=tiles), :]
        cells += [rows[:, :64], rows[:, 64:]]
    lifted = dot(jnp.concatenate(cells, axis=0).astype(BF16), up_ref[...])
    lifted = lifted.astype(BF16).astype(F32)
    for cell in range(8):
        a, b, c = cell // 4, cell // 2 % 2, cell % 2
        for sub in range(16):
            line = (4 * a + sub // 4) * EDGE + 4 * b + sub % 4
            volumes_ref[c, pl.ds(line, 8, stride=CUBE), :] = lifted[
                cell * 8 : cell * 8 + 8, sub * 128 : sub * 128 + 128
            ]
    for brick in range(BRICKS):

        def near(face):
            link = links_ref[0, brick, face]
            index = jnp.clip(link - BRICKS * (position - 1), 0, 3 * BRICKS - 1)
            return pl.multiple_of(index * CUBE, CUBE), jnp.where(link >= 0, 1.0, 0.0).astype(F32)

        def x_face(face):
            start, present = near(face)
            offset = EDGE * (EDGE - 1) if face % 2 == 0 else 0
            return lines(volumes_ref, pl.multiple_of(start + offset, 8), EDGE) * present

        def y_face(face):
            start, present = near(face)
            offset = EDGE - 1 if face % 2 == 0 else 0
            return lines(volumes_ref, start + offset, EDGE, EDGE) * present

        def z_face(face):
            start, present = near(face)
            tile = volumes_ref[1 if face % 2 == 0 else 0, pl.ds(start, CUBE), :] * present
            return tile.reshape(EDGE, EDGE, 128)

        own = (BRICKS + brick) * CUBE
        volume = lines(volumes_ref, own, CUBE).reshape(EDGE, EDGE, LINE)
        put_padded(
            pad_ref, brick, volume, x_face(0), x_face(1), y_face(2), y_face(3), z_face(4), z_face(5)
        )
    pre = convolve(pad_ref, band_ref)
    hidden = pre / (1.0 + jnp.exp(-pre))
    hidden = hidden.astype(BF16)
    lifted_out[...] = lines(volumes_ref, BRICKS * CUBE, LINES).astype(BF16)
    pre_out[...] = pre
    hidden_out[...] = hidden
    pad_out[...] = pad_ref[...].reshape(pad_out.shape).astype(BF16)
    sources = (hidden.astype(F32), cotangent_ref[...].astype(F32).reshape(LINES, LINE))
    for which, values in enumerate(sources):
        for half in range(2):
            lines_ref[half, which * LINES : which * LINES + LINES] = values[:, half * 128 : half * 128 + 128]
    for which in range(2):
        for brick in range(BRICKS):
            base = (which * BRICKS + brick) * FACE
            start = which * LINES + brick * CUBE
            pack_faces(high_ref, base, lines_ref, start, True)
            pack_faces(low_ref, base, lines_ref, start, False)
    high_out[...] = high_ref[...].astype(BF16)
    low_out[...] = low_ref[...].astype(BF16)


def fold_diagonals(outer_ref, part):
    lane = lanes_of((CHANNELS, 128)) // CHANNELS
    folded = None
    for half in range(2):
        picked = None
        for block in range(4):
            depth = 4 * half + block + part - 1
            start = depth * CHANNELS if 0 <= depth < EDGE else (LINE if depth == EDGE else WIDE - CHANNELS)
            rows = outer_ref[start : start + CHANNELS, half * 128 : half * 128 + 128]
            picked = rows if picked is None else jnp.where(lane == block, rows, picked)
        folded = picked if folded is None else folded + picked
    quarter = [folded[8 * q : 8 * q + 8] for q in range(4)]
    small = lanes_of((8, 128)) // CHANNELS
    total = None
    for turn in range(4):
        mixed = quarter[0]
        for q in range(1, 4):
            mixed = jnp.where(small == (q + turn) % 4, quarter[q], mixed)
        if turn:
            mixed = pltpu.roll(mixed, 128 - turn * CHANNELS, 1)
        total = mixed if total is None else total + mixed
    return total


def padded_brick(pad_ref, brick, which, values, links_ref, high_ref, low_ref):
    position = lax.axis_index("space")
    half = high_ref.shape[0] // 2

    def rows(face, axis):
        link = links_ref[0, brick, face]
        high = face % 2 == 0
        index = jnp.clip(link - BRICKS * (position - 1 if high else position), 0, 2 * BRICKS - 1)
        start = (index // BRICKS) * half + (which * BRICKS + index % BRICKS) * FACE + axis * EDGE
        pool = high_ref if high else low_ref
        present = jnp.where(link >= 0, 1.0, 0.0).astype(F32)
        return pool[pl.ds(pl.multiple_of(start, 8), EDGE), :] * present

    volume = values[brick * CUBE : brick * CUBE + CUBE].reshape(EDGE, EDGE, LINE)
    put_padded(
        pad_ref, brick, volume, rows(0, 0), rows(1, 0), rows(2, 1), rows(3, 1),
        unpack_depth(rows(4, 2), True), unpack_depth(rows(5, 2), False),
    )


def fill_pools(high_ref, low_ref, high_own, low_own, high_left, low_right):
    half = 2 * BRICKS * FACE
    high_ref[0:half] = high_left[...].astype(F32)
    high_ref[half:] = high_own[...].astype(F32)
    low_ref[0:half] = low_own[...].astype(F32)
    low_ref[half:] = low_right[...].astype(F32)


def second_kernel(
    links_ref, cotangent_ref, band_ref, back_ref, lifted_ref, pre_ref, hidden_ref, pad_in,
    high_own, low_own, high_left, low_right,
    fine_out, sums_out,
    high_ref, low_ref, hidden_pad, cotangent_pad, lifted_pad, outer_ref, sums_ref,
):
    fill_pools(high_ref, low_ref, high_own, low_own, high_left, low_right)
    lifted_pad[...] = pad_in[...].astype(F32).reshape(lifted_pad.shape)
    cotangent = cotangent_ref[...].astype(F32).reshape(LINES, LINE)
    hidden = hidden_ref[...].astype(F32)
    for which, values, pad_ref in ((0, hidden, hidden_pad), (1, cotangent, cotangent_pad)):
        for brick in range(BRICKS):
            padded_brick(pad_ref, brick, which, values, links_ref, high_ref, low_ref)
    fine = lifted_ref[...].astype(F32) + convolve(hidden_pad, band_ref)
    fine_out[...] = fine.astype(BF16).reshape(fine_out.shape)
    back = convolve(cotangent_pad, back_ref)
    pre = pre_ref[...]
    sigmoid = 1.0 / (1.0 + jnp.exp(-pre))
    gradient = (back * sigmoid * (1.0 + pre * (1.0 - sigmoid))).astype(BF16)
    upstream = cotangent.astype(BF16)
    sums_ref[8 * BLOCKS :] = jnp.zeros((sums_ref.shape[0] - 8 * BLOCKS, 128), F32)
    for base, pad_ref, right in ((0, lifted_pad, gradient), (27, hidden_pad, upstream)):
        for k in range(9):
            outer_ref[...] = dot_rows(window(pad_ref, k), right)
            for part in range(3):
                start = 8 * (base + 3 * k + part)
                sums_ref[start : start + 8] = fold_diagonals(outer_ref, part)
    sums_out[...] = sums_ref[...].astype(BF16).reshape(sums_out.shape)


def sum_kernel(scale, parts_ref, out_ref):
    total = jnp.sum(parts_ref[...].astype(F32), axis=0) * scale
    out_ref[...] = jnp.broadcast_to(total.astype(BF16)[None], out_ref.shape)


def unpack_kernel(sums_ref, one_out, two_out, rows_ref):
    rows_ref[...] = sums_ref[...].astype(F32).reshape(rows_ref.shape)
    for index in range(BLOCKS):
        block = rows_ref[8 * index : 8 * index + 8]
        out = one_out if index < 27 else two_out
        for q in range(4):
            moved = pltpu.roll(block, 128 - q * CHANNELS, 1) if q else block
            out[index % 27, 8 * q : 8 * q + 8, :] = moved[:, :CHANNELS]


def call(kernel, out_shape, scratch=(), smem=(), hbm=(), inputs=1, limit=24, cost=None):
    spaces = [pltpu.SMEM if i in smem else pltpu.HBM if i in hbm else pltpu.VMEM for i in range(inputs)]
    return pl.pallas_call(
        kernel,
        out_shape=out_shape,
        in_specs=[pl.BlockSpec(memory_space=space) for space in spaces],
        out_specs=jax.tree.map(lambda _: pl.BlockSpec(memory_space=pltpu.VMEM), out_shape),
        scratch_shapes=list(scratch),
        compiler_params=pltpu.CompilerParams(vmem_limit_bytes=limit * 2**20),
        cost_estimate=cost,
    )


def shape(*dims, dtype=BF16):
    return jax.ShapeDtypeStruct(dims, dtype)


def passed_along(value, axis, steps):
    count = lax.axis_size(axis)
    first, last = (max(0, -steps), min(count, count - steps))
    return lax.ppermute(value, axis, [(source, source + steps) for source in range(first, last)])


def body(coarse_latents, active_blocks, face_links, cotangent, up_weight, conv_one, conv_two):
    devices = lax.axis_size("space")
    everyone = devices * lax.axis_size("dp")
    held, width = coarse_latents.shape[1:]
    bricks = active_blocks.shape[1]
    tiles = width // 128
    packed = call(
        functools.partial(pick_kernel, devices),
        shape(devices, 3 * BRICKS * tiles, 128),
        [
            pltpu.VMEM((1, bricks), jnp.int32),
            pltpu.VMEM((1, held, width), BF16),
            pltpu.VMEM(((bricks + 16) * tiles, 128), F32),
            pltpu.SemaphoreType.DMA((2,)),
        ],
        hbm=(0, 1),
        inputs=2,
    )(active_blocks, coarse_latents)
    received = lax.all_to_all(packed, "space", split_axis=0, concat_axis=0, tiled=True)
    band = shape(9, WIDE, LINE)
    cost = pl.CostEstimate(flops=10**9, bytes_accessed=2 * 10**6, transcendentals=0)
    band_one = call(band_kernel, band, cost=cost)(conv_one)
    band_two, band_back = call(two_bands_kernel, (band, band), cost=cost)(conv_two)
    pad_shape = (3, BRICKS, EDGE + 2, EDGE, WIDE)
    pad = pltpu.VMEM(pad_shape, F32)
    packed_faces = 2 * BRICKS * FACE
    lifted, pre, hidden, lifted_pad, high, low = call(
        first_kernel,
        (
            shape(LINES, LINE),
            shape(LINES, LINE, dtype=F32),
            shape(LINES, LINE),
            shape(math.prod(pad_shape[:-1]), WIDE),
            shape(packed_faces, LINE),
            shape(packed_faces, LINE),
        ),
        [
            pltpu.VMEM((2, 8 * CUBE, 128), F32),
            pad,
            pltpu.VMEM((2, 2 * LINES, 128), F32),
            pltpu.VMEM((packed_faces, LINE), F32),
            pltpu.VMEM((packed_faces, LINE), F32),
            pltpu.VMEM((8 * tiles, 128), F32),
        ],
        smem=(0,),
        inputs=5,
    )(face_links, received, up_weight, band_one, cotangent)
    high_left = passed_along(high, "space", 1)
    low_right = passed_along(low, "space", -1)
    per = -(-BLOCKS // everyone)
    per += per % 2
    fine, sums = call(
        second_kernel,
        (shape(*cotangent.shape), shape(everyone, per * 8, 128)),
        [
            pltpu.VMEM((2 * packed_faces, LINE), F32),
            pltpu.VMEM((2 * packed_faces, LINE), F32),
            pad,
            pad,
            pad,
            pltpu.VMEM((WIDE, LINE), F32),
            pltpu.VMEM((everyone * per * 8, 128), F32),
        ],
        smem=(0,),
        inputs=12,
    )(
        face_links, cotangent, band_two, band_back, lifted, pre, hidden, lifted_pad,
        high, low, high_left, low_right,
    )
    axes = ("space", "dp")
    parts = lax.all_to_all(sums, axes, split_axis=0, concat_axis=0, tiled=True)
    scale = 1.0 / math.sqrt(lax.axis_size("dp") * devices * BRICKS * EDGE**3)
    total = call(functools.partial(sum_kernel, scale), shape(*sums.shape))(parts)
    gathered = lax.all_to_all(total, axes, split_axis=0, concat_axis=0, tiled=True)
    grads = shape(27, CHANNELS, CHANNELS, dtype=F32)
    rows = pltpu.VMEM((everyone * per * 8, 128), F32)
    grad_one, grad_two = call(unpack_kernel, (grads, grads), [rows])(gathered)
    return (fine, grad_one, grad_two)


def solution(mesh):
    return jax.shard_map(
        body,
        mesh=mesh,
        in_specs=(
            P("dp", "space", None),
            P("dp", None),
            P("dp", "space", None),
            P("dp", "space", None, None, None),
            P(),
            P(),
            P(),
        ),
        out_specs=(P("dp", "space", None, None, None), P(), P()),
        check_vma=False,
    )
```

```python
import functools
import math

import jax
import jax.numpy as jnp
from jax import lax
from jax.experimental import pallas as pl
from jax.experimental.pallas import tpu as pltpu
from jax.sharding import PartitionSpec as P

BF16 = jnp.bfloat16
F32 = jnp.float32
EDGE = 8
CHANNELS = 32
LINE = EDGE * CHANNELS
WIDE = LINE + 128
BRICKS = 2
CUBE = EDGE * EDGE
LINES = BRICKS * CUBE
FACE = 3 * EDGE
BLOCKS = 54


def dot(left, right):
    return jnp.dot(left, right, preferred_element_type=F32)


def dot_rows(left, right):
    return lax.dot_general(left, right, (((0,), (0,)), ((), ())), preferred_element_type=F32)


def lines(halves_ref, start, count, stride=1):
    index = pl.ds(start, count, stride=stride) if stride > 1 else pl.ds(start, count)
    return jnp.concatenate([halves_ref[0, index, :], halves_ref[1, index, :]], axis=-1)


def lanes_of(shape):
    return lax.broadcasted_iota(jnp.int32, shape, len(shape) - 1)


def pick_kernel(devices, ids_ref, latents_ref, out_ref, rows_ref):
    held, width = latents_ref.shape[1:]
    bricks = ids_ref.shape[1]
    margin = 8 * width // 128
    tiles = width // 128
    rows_ref[0:margin] = jnp.zeros((margin, 128), F32)
    rows_ref[margin + bricks * tiles :] = jnp.zeros((margin, 128), F32)
    first = lax.axis_index("space") * held
    rows = lax.broadcasted_iota(jnp.int32, (held, bricks), 0) + first
    hot = jnp.where(rows == ids_ref[...], 1.0, 0.0).astype(BF16)
    picked = dot_rows(hot, latents_ref[0])
    for tile in range(tiles):
        rows_ref[pl.ds(margin + tile, bricks, stride=tiles), :] = picked[:, tile * 128 : tile * 128 + 128]
    count = out_ref.shape[1]
    for receiver in range(devices):
        start = margin + BRICKS * (receiver - 1) * tiles
        out_ref[receiver] = rows_ref[start : start + count].astype(BF16)


def build_band(band_ref, rows):
    shape = (3 * CHANNELS, LINE)
    row = lax.broadcasted_iota(jnp.int32, shape, 0)
    target = CHANNELS - (row // CHANNELS) * CHANNELS + row % CHANNELS
    distance = lanes_of(shape) - target
    band_ref[:, LINE:, :] = jnp.zeros((9, 128, LINE), BF16)
    places = [(z, z * CHANNELS) for z in range(EDGE)] + [(EDGE, LINE), (-1, WIDE - CHANNELS)]
    for z, start in places:
        select = jnp.where(distance == z * CHANNELS, 1.0, 0.0).astype(BF16)
        block = dot(rows, select).astype(BF16)
        band_ref[:, start : start + CHANNELS, :] = block.reshape(9, CHANNELS, LINE)


def weight_rows(weights):
    cube = weights.reshape(9, 3, CHANNELS, CHANNELS)
    rows = jnp.concatenate([cube[:, 0], cube[:, 1], cube[:, 2]], axis=-1)
    return rows.reshape(9 * CHANNELS, 3 * CHANNELS).astype(BF16)


def flipped_rows(weights):
    cube = jnp.swapaxes(weights, 1, 2).reshape(9, 3, CHANNELS, CHANNELS)
    pieces = [jnp.concatenate([cube[8 - k, 2], cube[8 - k, 1], cube[8 - k, 0]], axis=-1) for k in range(9)]
    return jnp.concatenate(pieces, axis=0).astype(BF16)


def band_kernel(weights_ref, band_ref):
    build_band(band_ref, weight_rows(weights_ref[...].astype(F32)))


def two_bands_kernel(weights_ref, band_ref, back_ref):
    weights = weights_ref[...].astype(F32)
    build_band(band_ref, weight_rows(weights))
    build_band(back_ref, flipped_rows(weights))


def put_padded(pad_ref, brick, volume, x_low, x_high, y_low, y_high, z_low, z_high):
    lane = lanes_of((EDGE, EDGE, 128))
    tail = jnp.where(lane < CHANNELS, z_high, jnp.where(lane >= 128 - CHANNELS, z_low, 0.0))
    full = jnp.concatenate([volume, tail], axis=-1)
    zeros = jnp.zeros((EDGE, 128), F32)
    first = jnp.concatenate([x_low, zeros], axis=-1)[None]
    last = jnp.concatenate([x_high, zeros], axis=-1)[None]
    slabs = jnp.concatenate([first, full, last], axis=0)
    no_halo = jnp.zeros((1, WIDE), F32)
    low = jnp.concatenate([no_halo, jnp.concatenate([y_low, zeros], axis=-1), no_halo], axis=0)
    high = jnp.concatenate([no_halo, jnp.concatenate([y_high, zeros], axis=-1), no_halo], axis=0)
    row = lax.broadcasted_iota(jnp.int32, slabs.shape, 1)
    pad_ref[0, brick] = jnp.where(row == 0, low[:, None, :], pltpu.roll(slabs, 1, 1))
    pad_ref[1, brick] = slabs
    pad_ref[2, brick] = jnp.where(row == EDGE - 1, high[:, None, :], pltpu.roll(slabs, EDGE - 1, 1))


def window(pad_ref, k):
    lines = pad_ref[k % 3, :, k // 3 : k // 3 + EDGE]
    return lines.reshape(LINES, WIDE).astype(BF16)


def convolve(pad_ref, band_ref):
    total = None
    for k in range(9):
        term = dot(window(pad_ref, k), band_ref[k])
        total = term if total is None else total + term
    return total


def pack_faces(faces_ref, base, halves_ref, start, high):
    first = start + ((EDGE - 1) * EDGE if high else 0)
    faces_ref[base : base + EDGE] = lines(halves_ref, first, EDGE)
    first = start + (EDGE - 1 if high else 0)
    faces_ref[base + EDGE : base + 2 * EDGE] = lines(halves_ref, first, EDGE, EDGE)
    tile = halves_ref[1 if high else 0, start : start + CUBE, :]
    lane = lanes_of((16, 128)) // CHANNELS
    packed = jnp.zeros((16, 128), F32)
    for part in range(4):
        shift = (part + 1 if high else part) % 4 * CHANNELS
        piece = tile[part * 16 : part * 16 + 16]
        packed = jnp.where(lane == part, pltpu.roll(piece, shift, 1) if shift else piece, packed)
    faces_ref[base + 2 * EDGE : base + FACE, :128] = packed[:8]
    faces_ref[base + 2 * EDGE : base + FACE, 128:] = packed[8:]


def unpack_depth(rows, high):
    packed = jnp.concatenate([rows[:, :128], rows[:, 128:]], axis=0)
    pieces = []
    for part in range(4):
        shift = ((3 - part) if high else (4 - part)) % 4 * CHANNELS
        pieces.append(pltpu.roll(packed, shift, 1) if shift else packed)
    return jnp.concatenate(pieces, axis=0).reshape(EDGE, EDGE, 128)


def first_kernel(
    links_ref, received_ref, up_ref, band_ref, cotangent_ref,
    lifted_out, pre_out, hidden_out, pad_out, high_out, low_out,
    volumes_ref, pad_ref, lines_ref, high_ref, low_ref, rows_ref,
):
    position = lax.axis_index("space")
    tiles = received_ref.shape[1] // (3 * BRICKS)
    rows_ref[0 : 3 * BRICKS * tiles] = jnp.sum(received_ref[...].astype(F32), axis=0)
    rows_ref[3 * BRICKS * tiles :] = jnp.zeros((2 * tiles, 128), F32)
    cells = []
    for tile in range(tiles):
        rows = rows_ref[pl.ds(tile, 8, stride=tiles), :]
        cells += [rows[:, :64], rows[:, 64:]]
    lifted = dot(jnp.concatenate(cells, axis=0).astype(BF16), up_ref[...])
    lifted = lifted.astype(BF16).astype(F32)
    for cell in range(8):
        a, b, c = cell // 4, cell // 2 % 2, cell % 2
        for sub in range(16):
            line = (4 * a + sub // 4) * EDGE + 4 * b + sub % 4
            volumes_ref[c, pl.ds(line, 8, stride=CUBE), :] = lifted[
                cell * 8 : cell * 8 + 8, sub * 128 : sub * 128 + 128
            ]
    for brick in range(BRICKS):

        def near(face):
            link = links_ref[0, brick, face]
            index = jnp.clip(link - BRICKS * (position - 1), 0, 3 * BRICKS - 1)
            return pl.multiple_of(index * CUBE, CUBE), jnp.where(link >= 0, 1.0, 0.0).astype(F32)

        def x_face(face):
            start, present = near(face)
            offset = EDGE * (EDGE - 1) if face % 2 == 0 else 0
            return lines(volumes_ref, pl.multiple_of(start + offset, 8), EDGE) * present

        def y_face(face):
            start, present = near(face)
            offset = EDGE - 1 if face % 2 == 0 else 0
            return lines(volumes_ref, start + offset, EDGE, EDGE) * present

        def z_face(face):
            start, present = near(face)
            tile = volumes_ref[1 if face % 2 == 0 else 0, pl.ds(start, CUBE), :] * present
            return tile.reshape(EDGE, EDGE, 128)

        own = (BRICKS + brick) * CUBE
        volume = lines(volumes_ref, own, CUBE).reshape(EDGE, EDGE, LINE)
        put_padded(
            pad_ref, brick, volume, x_face(0), x_face(1), y_face(2), y_face(3), z_face(4), z_face(5)
        )
    pre = convolve(pad_ref, band_ref)
    hidden = pre / (1.0 + jnp.exp(-pre))
    hidden = hidden.astype(BF16)
    lifted_out[...] = lines(volumes_ref, BRICKS * CUBE, LINES).astype(BF16)
    pre_out[...] = pre
    hidden_out[...] = hidden
    pad_out[...] = pad_ref[...].reshape(pad_out.shape).astype(BF16)
    sources = (hidden.astype(F32), cotangent_ref[...].astype(F32).reshape(LINES, LINE))
    for which, values in enumerate(sources):
        for half in range(2):
            lines_ref[half, which * LINES : which * LINES + LINES] = values[:, half * 128 : half * 128 + 128]
    for which in range(2):
        for brick in range(BRICKS):
            base = (which * BRICKS + brick) * FACE
            start = which * LINES + brick * CUBE
            pack_faces(high_ref, base, lines_ref, start, True)
            pack_faces(low_ref, base, lines_ref, start, False)
    high_out[...] = high_ref[...].astype(BF16)
    low_out[...] = low_ref[...].astype(BF16)


def fold_diagonals(outer_ref, part):
    lane = lanes_of((CHANNELS, 128)) // CHANNELS
    folded = None
    for half in range(2):
        picked = None
        for block in range(4):
            depth = 4 * half + block + part - 1
            start = depth * CHANNELS if 0 <= depth < EDGE else (LINE if depth == EDGE else WIDE - CHANNELS)
            rows = outer_ref[start : start + CHANNELS, half * 128 : half * 128 + 128]
            picked = rows if picked is None else jnp.where(lane == block, rows, picked)
        folded = picked if folded is None else folded + picked
    quarter = [folded[8 * q : 8 * q + 8] for q in range(4)]
    small = lanes_of((8, 128)) // CHANNELS
    total = None
    for turn in range(4):
        mixed = quarter[0]
        for q in range(1, 4):
            mixed = jnp.where(small == (q + turn) % 4, quarter[q], mixed)
        if turn:
            mixed = pltpu.roll(mixed, 128 - turn * CHANNELS, 1)
        total = mixed if total is None else total + mixed
    return total


def padded_brick(pad_ref, brick, which, values, links_ref, high_ref, low_ref):
    position = lax.axis_index("space")
    half = high_ref.shape[0] // 2

    def rows(face, axis):
        link = links_ref[0, brick, face]
        high = face % 2 == 0
        index = jnp.clip(link - BRICKS * (position - 1 if high else position), 0, 2 * BRICKS - 1)
        start = (index // BRICKS) * half + (which * BRICKS + index % BRICKS) * FACE + axis * EDGE
        pool = high_ref if high else low_ref
        present = jnp.where(link >= 0, 1.0, 0.0).astype(F32)
        return pool[pl.ds(pl.multiple_of(start, 8), EDGE), :] * present

    volume = values[brick * CUBE : brick * CUBE + CUBE].reshape(EDGE, EDGE, LINE)
    put_padded(
        pad_ref, brick, volume, rows(0, 0), rows(1, 0), rows(2, 1), rows(3, 1),
        unpack_depth(rows(4, 2), True), unpack_depth(rows(5, 2), False),
    )


def fill_pools(high_ref, low_ref, high_own, low_own, high_left, low_right):
    half = 2 * BRICKS * FACE
    high_ref[0:half] = high_left[...].astype(F32)
    high_ref[half:] = high_own[...].astype(F32)
    low_ref[0:half] = low_own[...].astype(F32)
    low_ref[half:] = low_right[...].astype(F32)


def second_kernel(
    links_ref, cotangent_ref, band_ref, back_ref, lifted_ref, pre_ref, hidden_ref, pad_in,
    high_own, low_own, high_left, low_right,
    fine_out, sums_out,
    high_ref, low_ref, hidden_pad, cotangent_pad, lifted_pad, outer_ref, sums_ref,
):
    fill_pools(high_ref, low_ref, high_own, low_own, high_left, low_right)
    lifted_pad[...] = pad_in[...].astype(F32).reshape(lifted_pad.shape)
    cotangent = cotangent_ref[...].astype(F32).reshape(LINES, LINE)
    hidden = hidden_ref[...].astype(F32)
    for which, values, pad_ref in ((0, hidden, hidden_pad), (1, cotangent, cotangent_pad)):
        for brick in range(BRICKS):
            padded_brick(pad_ref, brick, which, values, links_ref, high_ref, low_ref)
    fine = lifted_ref[...].astype(F32) + convolve(hidden_pad, band_ref)
    fine_out[...] = fine.astype(BF16).reshape(fine_out.shape)
    back = convolve(cotangent_pad, back_ref)
    pre = pre_ref[...]
    sigmoid = 1.0 / (1.0 + jnp.exp(-pre))
    gradient = (back * sigmoid * (1.0 + pre * (1.0 - sigmoid))).astype(BF16)
    upstream = cotangent.astype(BF16)
    sums_ref[8 * BLOCKS :] = jnp.zeros((sums_ref.shape[0] - 8 * BLOCKS, 128), F32)
    for base, pad_ref, right in ((0, lifted_pad, gradient), (27, hidden_pad, upstream)):
        for k in range(9):
            outer_ref[...] = dot_rows(window(pad_ref, k), right)
            for part in range(3):
                start = 8 * (base + 3 * k + part)
                sums_ref[start : start + 8] = fold_diagonals(outer_ref, part)
    sums_out[...] = sums_ref[...].astype(BF16).reshape(sums_out.shape)


def sum_kernel(scale, parts_ref, out_ref):
    total = jnp.sum(parts_ref[...].astype(F32), axis=0) * scale
    out_ref[...] = jnp.broadcast_to(total.astype(BF16)[None], out_ref.shape)


def unpack_kernel(sums_ref, one_out, two_out, rows_ref):
    rows_ref[...] = sums_ref[...].astype(F32).reshape(rows_ref.shape)
    for index in range(BLOCKS):
        block = rows_ref[8 * index : 8 * index + 8]
        out = one_out if index < 27 else two_out
        for q in range(4):
            moved = pltpu.roll(block, 128 - q * CHANNELS, 1) if q else block
            out[index % 27, 8 * q : 8 * q + 8, :] = moved[:, :CHANNELS]


def call(kernel, out_shape, scratch=(), smem=(), hbm=(), inputs=1, limit=24, cost=None):
    spaces = [pltpu.SMEM if i in smem else pltpu.HBM if i in hbm else pltpu.VMEM for i in range(inputs)]
    return pl.pallas_call(
        kernel,
        out_shape=out_shape,
        in_specs=[pl.BlockSpec(memory_space=space) for space in spaces],
        out_specs=jax.tree.map(lambda _: pl.BlockSpec(memory_space=pltpu.VMEM), out_shape),
        scratch_shapes=list(scratch),
        compiler_params=pltpu.CompilerParams(vmem_limit_bytes=limit * 2**20),
        cost_estimate=cost,
    )


def shape(*dims, dtype=BF16):
    return jax.ShapeDtypeStruct(dims, dtype)


def passed_along(value, axis, steps):
    count = lax.axis_size(axis)
    first, last = (max(0, -steps), min(count, count - steps))
    return lax.ppermute(value, axis, [(source, source + steps) for source in range(first, last)])


def swapped(value, groups):
    return lax.all_to_all(
        value, ("space", "dp"), split_axis=0, concat_axis=0, axis_index_groups=groups, tiled=True
    )


def body(coarse_latents, active_blocks, face_links, cotangent, up_weight, conv_one, conv_two):
    devices = lax.axis_size("space")
    everyone = devices * lax.axis_size("dp")
    width = coarse_latents.shape[2]
    bricks = active_blocks.shape[1]
    tiles = width // 128
    packed = call(
        functools.partial(pick_kernel, devices),
        shape(devices, 3 * BRICKS * tiles, 128),
        [pltpu.VMEM(((bricks + 16) * tiles, 128), F32)],
        inputs=2,
    )(active_blocks, coarse_latents)
    received = lax.all_to_all(packed, "space", split_axis=0, concat_axis=0, tiled=True)
    band = shape(9, WIDE, LINE)
    cost = pl.CostEstimate(flops=10**9, bytes_accessed=2 * 10**6, transcendentals=0)
    band_one = call(band_kernel, band, cost=cost)(conv_one)
    band_two, band_back = call(two_bands_kernel, (band, band), cost=cost)(conv_two)
    pad_shape = (3, BRICKS, EDGE + 2, EDGE, WIDE)
    pad = pltpu.VMEM(pad_shape, F32)
    packed_faces = 2 * BRICKS * FACE
    lifted, pre, hidden, lifted_pad, high, low = call(
        first_kernel,
        (
            shape(LINES, LINE),
            shape(LINES, LINE, dtype=F32),
            shape(LINES, LINE),
            shape(math.prod(pad_shape[:-1]), WIDE),
            shape(packed_faces, LINE),
            shape(packed_faces, LINE),
        ),
        [
            pltpu.VMEM((2, 8 * CUBE, 128), F32),
            pad,
            pltpu.VMEM((2, 2 * LINES, 128), F32),
            pltpu.VMEM((packed_faces, LINE), F32),
            pltpu.VMEM((packed_faces, LINE), F32),
            pltpu.VMEM((8 * tiles, 128), F32),
        ],
        smem=(0,),
        inputs=5,
    )(face_links, received, up_weight, band_one, cotangent)
    high_left = passed_along(high, "space", 1)
    low_right = passed_along(low, "space", -1)
    inner = math.gcd(everyone, 8)
    outer = everyone // inner
    rows = -(-BLOCKS // inner) * 8
    fine, sums = call(
        second_kernel,
        (shape(*cotangent.shape), shape(inner, rows, 128)),
        [
            pltpu.VMEM((2 * packed_faces, LINE), F32),
            pltpu.VMEM((2 * packed_faces, LINE), F32),
            pad,
            pad,
            pad,
            pltpu.VMEM((WIDE, LINE), F32),
            pltpu.VMEM((inner * rows, 128), F32),
        ],
        smem=(0,),
        inputs=12,
    )(
        face_links, cotangent, band_two, band_back, lifted, pre, hidden, lifted_pad,
        high, low, high_left, low_right,
    )
    near = [[first * inner + i for i in range(inner)] for first in range(outer)]
    far = [[first * inner + i for first in range(outer)] for i in range(inner)]
    scale = 1.0 / math.sqrt(lax.axis_size("dp") * devices * BRICKS * EDGE**3)
    parts = swapped(sums, near)
    plane = call(functools.partial(sum_kernel, 1.0), shape(outer, rows, 128))(parts)
    planes = swapped(plane, far)
    total = call(functools.partial(sum_kernel, scale), shape(inner, rows, 128))(planes)
    gathered = swapped(total, near)
    grads = shape(27, CHANNELS, CHANNELS, dtype=F32)
    scratch = [pltpu.VMEM((inner * rows, 128), F32)]
    grad_one, grad_two = call(unpack_kernel, (grads, grads), scratch)(gathered)
    return (fine, grad_one, grad_two)


def solution(mesh):
    return jax.shard_map(
        body,
        mesh=mesh,
        in_specs=(
            P("dp", "space", None),
            P("dp", None),
            P("dp", "space", None),
            P("dp", "space", None, None, None),
            P(),
            P(),
            P(),
        ),
        out_specs=(P("dp", "space", None, None, None), P(), P()),
        check_vma=False,
    )
```

```python
import functools
import math

import jax
import jax.numpy as jnp
from jax import lax
from jax.experimental import pallas as pl
from jax.experimental.pallas import tpu as pltpu
from jax.sharding import PartitionSpec as P

BF16 = jnp.bfloat16
F32 = jnp.float32
EDGE = 8
CHANNELS = 32
LINE = EDGE * CHANNELS
WIDE = LINE + 128
BRICKS = 2
CUBE = EDGE * EDGE
LINES = BRICKS * CUBE
FACE = 3 * EDGE
BLOCKS = 54


def dot(left, right):
    return jnp.dot(left, right, preferred_element_type=F32)


def dot_rows(left, right):
    return lax.dot_general(left, right, (((0,), (0,)), ((), ())), preferred_element_type=F32)


def lines(halves_ref, start, count, stride=1):
    index = pl.ds(start, count, stride=stride) if stride > 1 else pl.ds(start, count)
    return jnp.concatenate([halves_ref[0, index, :], halves_ref[1, index, :]], axis=-1)


def lanes_of(shape):
    return lax.broadcasted_iota(jnp.int32, shape, len(shape) - 1)


def pick_kernel(devices, ids_ref, latents_ref, out_ref, rows_ref):
    held, width = latents_ref.shape[1:]
    bricks = ids_ref.shape[1]
    margin = 8 * width // 128
    tiles = width // 128
    rows_ref[0:margin] = jnp.zeros((margin, 128), F32)
    rows_ref[margin + bricks * tiles :] = jnp.zeros((margin, 128), F32)
    first = lax.axis_index("space") * held
    rows = lax.broadcasted_iota(jnp.int32, (held, bricks), 0) + first
    hot = jnp.where(rows == ids_ref[...], 1.0, 0.0).astype(BF16)
    picked = dot_rows(hot, latents_ref[0])
    for tile in range(tiles):
        rows_ref[pl.ds(margin + tile, bricks, stride=tiles), :] = picked[:, tile * 128 : tile * 128 + 128]
    count = out_ref.shape[1]
    for receiver in range(devices):
        start = margin + BRICKS * (receiver - 1) * tiles
        out_ref[receiver] = rows_ref[start : start + count].astype(BF16)


def build_band(band_ref, rows):
    shape = (3 * CHANNELS, LINE)
    row = lax.broadcasted_iota(jnp.int32, shape, 0)
    target = CHANNELS - (row // CHANNELS) * CHANNELS + row % CHANNELS
    distance = lanes_of(shape) - target
    band_ref[:, LINE:, :] = jnp.zeros((9, 128, LINE), BF16)
    places = [(z, z * CHANNELS) for z in range(EDGE)] + [(EDGE, LINE), (-1, WIDE - CHANNELS)]
    for z, start in places:
        select = jnp.where(distance == z * CHANNELS, 1.0, 0.0).astype(BF16)
        block = dot(rows, select).astype(BF16)
        band_ref[:, start : start + CHANNELS, :] = block.reshape(9, CHANNELS, LINE)


def weight_rows(weights):
    cube = weights.reshape(9, 3, CHANNELS, CHANNELS)
    rows = jnp.concatenate([cube[:, 0], cube[:, 1], cube[:, 2]], axis=-1)
    return rows.reshape(9 * CHANNELS, 3 * CHANNELS).astype(BF16)


def flipped_rows(weights):
    cube = jnp.swapaxes(weights, 1, 2).reshape(9, 3, CHANNELS, CHANNELS)
    pieces = [jnp.concatenate([cube[8 - k, 2], cube[8 - k, 1], cube[8 - k, 0]], axis=-1) for k in range(9)]
    return jnp.concatenate(pieces, axis=0).astype(BF16)


def first_bands_kernel(one_ref, two_ref, band_ref, back_ref):
    build_band(band_ref, weight_rows(one_ref[...].astype(F32)))
    build_band(back_ref, flipped_rows(two_ref[...].astype(F32)))


def last_band_kernel(two_ref, band_ref):
    build_band(band_ref, weight_rows(two_ref[...].astype(F32)))


def put_padded(pad_ref, brick, volume, x_low, x_high, y_low, y_high, z_low, z_high):
    lane = lanes_of((EDGE, EDGE, 128))
    tail = jnp.where(lane < CHANNELS, z_high, jnp.where(lane >= 128 - CHANNELS, z_low, 0.0))
    full = jnp.concatenate([volume, tail], axis=-1)
    zeros = jnp.zeros((EDGE, 128), F32)
    first = jnp.concatenate([x_low, zeros], axis=-1)[None]
    last = jnp.concatenate([x_high, zeros], axis=-1)[None]
    slabs = jnp.concatenate([first, full, last], axis=0)
    no_halo = jnp.zeros((1, WIDE), F32)
    low = jnp.concatenate([no_halo, jnp.concatenate([y_low, zeros], axis=-1), no_halo], axis=0)
    high = jnp.concatenate([no_halo, jnp.concatenate([y_high, zeros], axis=-1), no_halo], axis=0)
    row = lax.broadcasted_iota(jnp.int32, slabs.shape, 1)
    pad_ref[0, brick] = jnp.where(row == 0, low[:, None, :], pltpu.roll(slabs, 1, 1))
    pad_ref[1, brick] = slabs
    pad_ref[2, brick] = jnp.where(row == EDGE - 1, high[:, None, :], pltpu.roll(slabs, EDGE - 1, 1))


def window(pad_ref, k):
    lines = pad_ref[k % 3, :, k // 3 : k // 3 + EDGE]
    return lines.reshape(LINES, WIDE).astype(BF16)


def convolve(pad_ref, band_ref):
    total = None
    for k in range(9):
        term = dot(window(pad_ref, k), band_ref[k])
        total = term if total is None else total + term
    return total


def pack_faces(faces_ref, base, halves_ref, start, high):
    first = start + ((EDGE - 1) * EDGE if high else 0)
    faces_ref[base : base + EDGE] = lines(halves_ref, first, EDGE)
    first = start + (EDGE - 1 if high else 0)
    faces_ref[base + EDGE : base + 2 * EDGE] = lines(halves_ref, first, EDGE, EDGE)
    tile = halves_ref[1 if high else 0, start : start + CUBE, :]
    lane = lanes_of((16, 128)) // CHANNELS
    packed = jnp.zeros((16, 128), F32)
    for part in range(4):
        shift = (part + 1 if high else part) % 4 * CHANNELS
        piece = tile[part * 16 : part * 16 + 16]
        packed = jnp.where(lane == part, pltpu.roll(piece, shift, 1) if shift else piece, packed)
    faces_ref[base + 2 * EDGE : base + FACE, :128] = packed[:8]
    faces_ref[base + 2 * EDGE : base + FACE, 128:] = packed[8:]


def unpack_depth(rows, high):
    packed = jnp.concatenate([rows[:, :128], rows[:, 128:]], axis=0)
    pieces = []
    for part in range(4):
        shift = ((3 - part) if high else (4 - part)) % 4 * CHANNELS
        pieces.append(pltpu.roll(packed, shift, 1) if shift else packed)
    return jnp.concatenate(pieces, axis=0).reshape(EDGE, EDGE, 128)


def put_lines(halves_ref, values):
    for half in range(2):
        halves_ref[half] = values[:, half * 128 : half * 128 + 128]


def pack_both(halves_ref, high_ref, low_ref, high_out, low_out):
    for brick in range(BRICKS):
        pack_faces(high_ref, brick * FACE, halves_ref, brick * CUBE, True)
        pack_faces(low_ref, brick * FACE, halves_ref, brick * CUBE, False)
    high_out[...] = high_ref[...].astype(BF16)
    low_out[...] = low_ref[...].astype(BF16)


def fill_pools(high_ref, low_ref, high_own, low_own, high_left, low_right):
    half = BRICKS * FACE
    high_ref[0:half] = high_left[...].astype(F32)
    high_ref[half:] = high_own[...].astype(F32)
    low_ref[0:half] = low_own[...].astype(F32)
    low_ref[half:] = low_right[...].astype(F32)


def padded_brick(pad_ref, brick, values, links_ref, high_ref, low_ref):
    position = lax.axis_index("space")

    def rows(face, axis):
        link = links_ref[0, brick, face]
        high = face % 2 == 0
        index = jnp.clip(link - BRICKS * (position - 1 if high else position), 0, 2 * BRICKS - 1)
        pool = high_ref if high else low_ref
        present = jnp.where(link >= 0, 1.0, 0.0).astype(F32)
        return pool[pl.ds(pl.multiple_of(index * FACE + axis * EDGE, 8), EDGE), :] * present

    volume = values[brick * CUBE : brick * CUBE + CUBE].reshape(EDGE, EDGE, LINE)
    put_padded(
        pad_ref, brick, volume, rows(0, 0), rows(1, 0), rows(2, 1), rows(3, 1),
        unpack_depth(rows(4, 2), True), unpack_depth(rows(5, 2), False),
    )


def faces_kernel(cotangent_ref, high_out, low_out, halves_ref, high_ref, low_ref):
    put_lines(halves_ref, cotangent_ref[...].astype(F32).reshape(LINES, LINE))
    pack_both(halves_ref, high_ref, low_ref, high_out, low_out)


def fold(outer_ref, places):
    lane = lanes_of((CHANNELS, 128)) // CHANNELS
    folded = None
    for turn in range(2):
        picked = None
        for block in range(4):
            start, tile = places[block][turn]
            rows = outer_ref[start : start + CHANNELS, tile * 128 : tile * 128 + 128]
            picked = rows if picked is None else jnp.where(lane == block, rows, picked)
        folded = picked if folded is None else folded + picked
    quarter = [folded[8 * q : 8 * q + 8] for q in range(4)]
    small = lanes_of((8, 128)) // CHANNELS
    total = None
    for turn in range(4):
        mixed = quarter[0]
        for q in range(1, 4):
            mixed = jnp.where(small == (q + turn) % 4, quarter[q], mixed)
        if turn:
            mixed = pltpu.roll(mixed, 128 - turn * CHANNELS, 1)
        total = mixed if total is None else total + mixed
    return total


def wide_start(z):
    return z * CHANNELS if 0 <= z < EDGE else (LINE if z == EDGE else WIDE - CHANNELS)


def first_kernel(
    links_ref, received_ref, up_ref, band_ref, back_ref, cotangent_ref,
    high_own, low_own, high_left, low_right,
    lifted_out, hidden_out, high_out, low_out, sums_out,
    volumes_ref, lifted_pad, cotangent_pad, halves_ref, high_ref, low_ref, high_pool, low_pool,
    rows_ref, wide_ref, tall_ref, sums_ref,
):
    position = lax.axis_index("space")
    tiles = received_ref.shape[1] // (3 * BRICKS)
    rows_ref[0 : 3 * BRICKS * tiles] = jnp.sum(received_ref[...].astype(F32), axis=0)
    rows_ref[3 * BRICKS * tiles :] = jnp.zeros((2 * tiles, 128), F32)
    cells = []
    for tile in range(tiles):
        rows = rows_ref[pl.ds(tile, 8, stride=tiles), :]
        cells += [rows[:, :64], rows[:, 64:]]
    lifted = dot(jnp.concatenate(cells, axis=0).astype(BF16), up_ref[...])
    lifted = lifted.astype(BF16).astype(F32)
    for cell in range(8):
        a, b, c = cell // 4, cell // 2 % 2, cell % 2
        for sub in range(16):
            line = (4 * a + sub // 4) * EDGE + 4 * b + sub % 4
            volumes_ref[c, pl.ds(line, 8, stride=CUBE), :] = lifted[
                cell * 8 : cell * 8 + 8, sub * 128 : sub * 128 + 128
            ]
    for brick in range(BRICKS):

        def near(face):
            link = links_ref[0, brick, face]
            index = jnp.clip(link - BRICKS * (position - 1), 0, 3 * BRICKS - 1)
            return pl.multiple_of(index * CUBE, CUBE), jnp.where(link >= 0, 1.0, 0.0).astype(F32)

        def x_face(face):
            start, present = near(face)
            offset = EDGE * (EDGE - 1) if face % 2 == 0 else 0
            return lines(volumes_ref, pl.multiple_of(start + offset, 8), EDGE) * present

        def y_face(face):
            start, present = near(face)
            offset = EDGE - 1 if face % 2 == 0 else 0
            return lines(volumes_ref, start + offset, EDGE, EDGE) * present

        def z_face(face):
            start, present = near(face)
            tile = volumes_ref[1 if face % 2 == 0 else 0, pl.ds(start, CUBE), :] * present
            return tile.reshape(EDGE, EDGE, 128)

        own = (BRICKS + brick) * CUBE
        volume = lines(volumes_ref, own, CUBE).reshape(EDGE, EDGE, LINE)
        put_padded(
            lifted_pad, brick, volume, x_face(0), x_face(1), y_face(2), y_face(3), z_face(4), z_face(5)
        )
    pre = convolve(lifted_pad, band_ref)
    sigmoid = 1.0 / (1.0 + jnp.exp(-pre))
    hidden = (pre / (1.0 + jnp.exp(-pre))).astype(BF16)
    lifted_out[...] = lines(volumes_ref, BRICKS * CUBE, LINES).astype(BF16)
    hidden_out[...] = hidden
    put_lines(halves_ref, hidden.astype(F32))
    pack_both(halves_ref, high_ref, low_ref, high_out, low_out)
    fill_pools(high_pool, low_pool, high_own, low_own, high_left, low_right)
    cotangent = cotangent_ref[...].astype(F32).reshape(LINES, LINE)
    for brick in range(BRICKS):
        padded_brick(cotangent_pad, brick, cotangent, links_ref, high_pool, low_pool)
    back = convolve(cotangent_pad, back_ref)
    gradient = (back * sigmoid * (1.0 + pre * (1.0 - sigmoid))).astype(BF16)
    sums_ref[8 * BLOCKS :] = jnp.zeros((sums_ref.shape[0] - 8 * BLOCKS, 128), F32)
    for k in range(9):
        tall_ref[...] = dot_rows(window(lifted_pad, k), gradient)
        for part in range(3):
            places = [[(wide_start(4 * t + b + part - 1), t) for t in range(2)] for b in range(4)]
            start = 8 * (3 * k + part)
            sums_ref[start : start + 8] = fold(tall_ref, places)
        wide_ref[...] = dot_rows(hidden, window(cotangent_pad, 8 - k))
        for part in range(3):
            places = [[], [], [], []]
            for z in range(EDGE):
                other = z + 1 - part
                places[other % 4].append((z * CHANNELS, wide_start(other) // 128))
            start = 8 * (27 + 3 * k + part)
            sums_ref[start : start + 8] = fold(wide_ref, places)
    sums_out[...] = sums_ref[...].astype(BF16).reshape(sums_out.shape)


def fine_kernel(
    links_ref, band_ref, lifted_ref, hidden_ref, high_own, low_own, high_left, low_right,
    fine_out, hidden_pad, high_pool, low_pool,
):
    fill_pools(high_pool, low_pool, high_own, low_own, high_left, low_right)
    hidden = hidden_ref[...].astype(F32)
    for brick in range(BRICKS):
        padded_brick(hidden_pad, brick, hidden, links_ref, high_pool, low_pool)
    fine = lifted_ref[...].astype(F32) + convolve(hidden_pad, band_ref)
    fine_out[...] = fine.astype(BF16).reshape(fine_out.shape)


def sum_kernel(scale, parts_ref, out_ref):
    total = jnp.sum(parts_ref[...].astype(F32), axis=0) * scale
    out_ref[...] = jnp.broadcast_to(total.astype(BF16)[None], out_ref.shape)


def unpack_kernel(sums_ref, one_out, two_out, rows_ref):
    rows_ref[...] = sums_ref[...].astype(F32).reshape(rows_ref.shape)
    for index in range(BLOCKS):
        block = rows_ref[8 * index : 8 * index + 8]
        out = one_out if index < 27 else two_out
        for q in range(4):
            moved = pltpu.roll(block, 128 - q * CHANNELS, 1) if q else block
            out[index % 27, 8 * q : 8 * q + 8, :] = moved[:, :CHANNELS]


def call(kernel, out_shape, scratch=(), smem=(), inputs=1, limit=24, cost=None):
    spaces = [pltpu.SMEM if i in smem else pltpu.VMEM for i in range(inputs)]
    return pl.pallas_call(
        kernel,
        out_shape=out_shape,
        in_specs=[pl.BlockSpec(memory_space=space) for space in spaces],
        out_specs=jax.tree.map(lambda _: pl.BlockSpec(memory_space=pltpu.VMEM), out_shape),
        scratch_shapes=list(scratch),
        compiler_params=pltpu.CompilerParams(vmem_limit_bytes=limit * 2**20),
        cost_estimate=cost,
    )


def shape(*dims, dtype=BF16):
    return jax.ShapeDtypeStruct(dims, dtype)


def passed_along(value, axis, steps):
    count = lax.axis_size(axis)
    first, last = (max(0, -steps), min(count, count - steps))
    return lax.ppermute(value, axis, [(source, source + steps) for source in range(first, last)])


def body(coarse_latents, active_blocks, face_links, cotangent, up_weight, conv_one, conv_two):
    devices = lax.axis_size("space")
    everyone = devices * lax.axis_size("dp")
    width = coarse_latents.shape[2]
    bricks = active_blocks.shape[1]
    tiles = width // 128
    packed = call(
        functools.partial(pick_kernel, devices),
        shape(devices, 3 * BRICKS * tiles, 128),
        [pltpu.VMEM(((bricks + 16) * tiles, 128), F32)],
        inputs=2,
    )(active_blocks, coarse_latents)
    received = lax.all_to_all(packed, "space", split_axis=0, concat_axis=0, tiled=True)
    band = shape(9, WIDE, LINE)
    cost = pl.CostEstimate(flops=10**9, bytes_accessed=2 * 10**6, transcendentals=0)
    face = shape(BRICKS * FACE, LINE)
    halves = pltpu.VMEM((2, LINES, 128), F32)
    faces = pltpu.VMEM((BRICKS * FACE, LINE), F32)
    pool = pltpu.VMEM((2 * BRICKS * FACE, LINE), F32)
    pad = pltpu.VMEM((3, BRICKS, EDGE + 2, EDGE, WIDE), F32)
    volume = shape(LINES, LINE)
    per = -(-BLOCKS // everyone)
    per += per % 2
    high, low = call(faces_kernel, (face, face), [halves, faces, faces])(cotangent)
    high_left = passed_along(high, "space", 1)
    low_right = passed_along(low, "space", -1)
    band_one, band_back = call(first_bands_kernel, (band, band), inputs=2, cost=cost)(conv_one, conv_two)
    lifted, hidden, hidden_high, hidden_low, sums = call(
        first_kernel,
        (volume, volume, face, face, shape(everyone, per * 8, 128)),
        [
            pltpu.VMEM((2, 8 * CUBE, 128), F32), pad, pad, halves, faces, faces, pool, pool,
            pltpu.VMEM((8 * tiles, 128), F32),
            pltpu.VMEM((LINE, WIDE), F32),
            pltpu.VMEM((WIDE, LINE), F32),
            pltpu.VMEM((everyone * per * 8, 128), F32),
        ],
        smem=(0,),
        inputs=10,
    )(
        face_links, received, up_weight, band_one, band_back, cotangent, high, low, high_left, low_right
    )
    hidden_left = passed_along(hidden_high, "space", 1)
    hidden_right = passed_along(hidden_low, "space", -1)
    band_two = call(last_band_kernel, band, cost=cost)(conv_two)
    fine = call(fine_kernel, shape(*cotangent.shape), [pad, pool, pool], smem=(0,), inputs=8, cost=cost)(
        face_links, band_two, lifted, hidden, hidden_high, hidden_low, hidden_left, hidden_right
    )
    axes = ("space", "dp")
    parts = lax.all_to_all(sums, axes, split_axis=0, concat_axis=0, tiled=True)
    scale = 1.0 / math.sqrt(lax.axis_size("dp") * devices * BRICKS * EDGE**3)
    total = call(functools.partial(sum_kernel, scale), shape(*sums.shape))(parts)
    gathered = lax.all_to_all(total, axes, split_axis=0, concat_axis=0, tiled=True)
    grads = shape(27, CHANNELS, CHANNELS, dtype=F32)
    rows = pltpu.VMEM((everyone * per * 8, 128), F32)
    grad_one, grad_two = call(unpack_kernel, (grads, grads), [rows])(gathered)
    return (fine, grad_one, grad_two)


def solution(mesh):
    return jax.shard_map(
        body,
        mesh=mesh,
        in_specs=(
            P("dp", "space", None),
            P("dp", None),
            P("dp", "space", None),
            P("dp", "space", None, None, None),
            P(),
            P(),
            P(),
        ),
        out_specs=(P("dp", "space", None, None, None), P(), P()),
        check_vma=False,
    )
```

```python
import functools
import math

import jax
import jax.numpy as jnp
from jax import lax
from jax.experimental import pallas as pl
from jax.experimental.pallas import tpu as pltpu
from jax.sharding import PartitionSpec as P

BF16 = jnp.bfloat16
F32 = jnp.float32
EDGE = 8
CHANNELS = 32
LINE = EDGE * CHANNELS
WIDE = LINE + 128
BRICKS = 2
CUBE = EDGE * EDGE
LINES = BRICKS * CUBE
FACE = 3 * EDGE
BLOCKS = 54


def dot(left, right):
    return jnp.dot(left, right, preferred_element_type=F32)


def dot_rows(left, right):
    return lax.dot_general(left, right, (((0,), (0,)), ((), ())), preferred_element_type=F32)


def lines(halves_ref, start, count, stride=1):
    index = pl.ds(start, count, stride=stride) if stride > 1 else pl.ds(start, count)
    return jnp.concatenate([halves_ref[0, index, :], halves_ref[1, index, :]], axis=-1)


def lanes_of(shape):
    return lax.broadcasted_iota(jnp.int32, shape, len(shape) - 1)


def pick_kernel(devices, ids_ref, latents_ref, out_ref, rows_ref):
    held, width = latents_ref.shape[1:]
    bricks = ids_ref.shape[1]
    margin = 8 * width // 128
    tiles = width // 128
    rows_ref[0:margin] = jnp.zeros((margin, 128), F32)
    rows_ref[margin + bricks * tiles :] = jnp.zeros((margin, 128), F32)
    first = lax.axis_index("space") * held
    rows = lax.broadcasted_iota(jnp.int32, (held, bricks), 0) + first
    hot = jnp.where(rows == ids_ref[...], 1.0, 0.0).astype(BF16)
    picked = dot_rows(hot, latents_ref[0])
    for tile in range(tiles):
        rows_ref[pl.ds(margin + tile, bricks, stride=tiles), :] = picked[:, tile * 128 : tile * 128 + 128]
    count = out_ref.shape[1]
    for receiver in range(devices):
        start = margin + BRICKS * (receiver - 1) * tiles
        out_ref[receiver] = rows_ref[start : start + count].astype(BF16)


def build_band(band_ref, rows):
    shape = (3 * CHANNELS, LINE)
    row = lax.broadcasted_iota(jnp.int32, shape, 0)
    target = CHANNELS - (row // CHANNELS) * CHANNELS + row % CHANNELS
    distance = lanes_of(shape) - target
    band_ref[:, LINE:, :] = jnp.zeros((9, 128, LINE), BF16)
    places = [(z, z * CHANNELS) for z in range(EDGE)] + [(EDGE, LINE), (-1, WIDE - CHANNELS)]
    for z, start in places:
        select = jnp.where(distance == z * CHANNELS, 1.0, 0.0).astype(BF16)
        block = dot(rows, select).astype(BF16)
        band_ref[:, start : start + CHANNELS, :] = block.reshape(9, CHANNELS, LINE)


def weight_rows(weights):
    cube = weights.reshape(9, 3, CHANNELS, CHANNELS)
    rows = jnp.concatenate([cube[:, 0], cube[:, 1], cube[:, 2]], axis=-1)
    return rows.reshape(9 * CHANNELS, 3 * CHANNELS).astype(BF16)


def flipped_rows(weights):
    cube = jnp.swapaxes(weights, 1, 2).reshape(9, 3, CHANNELS, CHANNELS)
    pieces = [jnp.concatenate([cube[8 - k, 2], cube[8 - k, 1], cube[8 - k, 0]], axis=-1) for k in range(9)]
    return jnp.concatenate(pieces, axis=0).astype(BF16)


def put_padded(pad_ref, brick, volume, x_low, x_high, y_low, y_high, z_low, z_high):
    lane = lanes_of((EDGE, EDGE, 128))
    tail = jnp.where(lane < CHANNELS, z_high, jnp.where(lane >= 128 - CHANNELS, z_low, 0.0))
    full = jnp.concatenate([volume, tail], axis=-1)
    zeros = jnp.zeros((EDGE, 128), F32)
    first = jnp.concatenate([x_low, zeros], axis=-1)[None]
    last = jnp.concatenate([x_high, zeros], axis=-1)[None]
    slabs = jnp.concatenate([first, full, last], axis=0)
    no_halo = jnp.zeros((1, WIDE), F32)
    low = jnp.concatenate([no_halo, jnp.concatenate([y_low, zeros], axis=-1), no_halo], axis=0)
    high = jnp.concatenate([no_halo, jnp.concatenate([y_high, zeros], axis=-1), no_halo], axis=0)
    row = lax.broadcasted_iota(jnp.int32, slabs.shape, 1)
    pad_ref[0, brick] = jnp.where(row == 0, low[:, None, :], pltpu.roll(slabs, 1, 1))
    pad_ref[1, brick] = slabs
    pad_ref[2, brick] = jnp.where(row == EDGE - 1, high[:, None, :], pltpu.roll(slabs, EDGE - 1, 1))


def window(pad_ref, k):
    lines = pad_ref[k % 3, :, k // 3 : k // 3 + EDGE]
    return lines.reshape(LINES, WIDE).astype(BF16)


def convolve(pad_ref, band_ref):
    total = None
    for k in range(9):
        term = dot(window(pad_ref, k), band_ref[k])
        total = term if total is None else total + term
    return total


def pack_faces(faces_ref, base, halves_ref, start, high):
    first = start + ((EDGE - 1) * EDGE if high else 0)
    faces_ref[base : base + EDGE] = lines(halves_ref, first, EDGE)
    first = start + (EDGE - 1 if high else 0)
    faces_ref[base + EDGE : base + 2 * EDGE] = lines(halves_ref, first, EDGE, EDGE)
    tile = halves_ref[1 if high else 0, start : start + CUBE, :]
    lane = lanes_of((16, 128)) // CHANNELS
    packed = jnp.zeros((16, 128), F32)
    for part in range(4):
        shift = (part + 1 if high else part) % 4 * CHANNELS
        piece = tile[part * 16 : part * 16 + 16]
        packed = jnp.where(lane == part, pltpu.roll(piece, shift, 1) if shift else piece, packed)
    faces_ref[base + 2 * EDGE : base + FACE, :128] = packed[:8]
    faces_ref[base + 2 * EDGE : base + FACE, 128:] = packed[8:]


def unpack_depth(rows, high):
    packed = jnp.concatenate([rows[:, :128], rows[:, 128:]], axis=0)
    pieces = []
    for part in range(4):
        shift = ((3 - part) if high else (4 - part)) % 4 * CHANNELS
        pieces.append(pltpu.roll(packed, shift, 1) if shift else packed)
    return jnp.concatenate(pieces, axis=0).reshape(EDGE, EDGE, 128)


def put_lines(halves_ref, values):
    for half in range(2):
        halves_ref[half] = values[:, half * 128 : half * 128 + 128]


def pack_both(halves_ref, high_ref, low_ref, high_out, low_out):
    for brick in range(BRICKS):
        pack_faces(high_ref, brick * FACE, halves_ref, brick * CUBE, True)
        pack_faces(low_ref, brick * FACE, halves_ref, brick * CUBE, False)
    high_out[...] = high_ref[...].astype(BF16)
    low_out[...] = low_ref[...].astype(BF16)


def fill_pools(high_ref, low_ref, high_own, low_own, high_left, low_right):
    half = BRICKS * FACE
    high_ref[0:half] = high_left[...].astype(F32)
    high_ref[half:] = high_own[...].astype(F32)
    low_ref[0:half] = low_own[...].astype(F32)
    low_ref[half:] = low_right[...].astype(F32)


def padded_brick(pad_ref, brick, values, links_ref, high_ref, low_ref):
    position = lax.axis_index("space")

    def rows(face, axis):
        link = links_ref[0, brick, face]
        high = face % 2 == 0
        index = jnp.clip(link - BRICKS * (position - 1 if high else position), 0, 2 * BRICKS - 1)
        pool = high_ref if high else low_ref
        present = jnp.where(link >= 0, 1.0, 0.0).astype(F32)
        return pool[pl.ds(pl.multiple_of(index * FACE + axis * EDGE, 8), EDGE), :] * present

    volume = values[brick * CUBE : brick * CUBE + CUBE].reshape(EDGE, EDGE, LINE)
    put_padded(
        pad_ref, brick, volume, rows(0, 0), rows(1, 0), rows(2, 1), rows(3, 1),
        unpack_depth(rows(4, 2), True), unpack_depth(rows(5, 2), False),
    )


def faces_kernel(cotangent_ref, high_out, low_out, halves_ref, high_ref, low_ref):
    put_lines(halves_ref, cotangent_ref[...].astype(F32).reshape(LINES, LINE))
    pack_both(halves_ref, high_ref, low_ref, high_out, low_out)


def fold(outer_ref, places):
    lane = lanes_of((CHANNELS, 128)) // CHANNELS
    folded = None
    for turn in range(2):
        picked = None
        for block in range(4):
            start, tile = places[block][turn]
            rows = outer_ref[start : start + CHANNELS, tile * 128 : tile * 128 + 128]
            picked = rows if picked is None else jnp.where(lane == block, rows, picked)
        folded = picked if folded is None else folded + picked
    quarter = [folded[8 * q : 8 * q + 8] for q in range(4)]
    small = lanes_of((8, 128)) // CHANNELS
    total = None
    for turn in range(4):
        mixed = quarter[0]
        for q in range(1, 4):
            mixed = jnp.where(small == (q + turn) % 4, quarter[q], mixed)
        if turn:
            mixed = pltpu.roll(mixed, 128 - turn * CHANNELS, 1)
        total = mixed if total is None else total + mixed
    return total


def wide_start(z):
    return z * CHANNELS if 0 <= z < EDGE else (LINE if z == EDGE else WIDE - CHANNELS)


def first_kernel(
    links_ref, received_ref, up_ref, one_ref, two_ref, cotangent_ref,
    high_own, low_own, high_left, low_right,
    lifted_out, hidden_out, high_out, low_out, sums_out,
    volumes_ref, lifted_pad, cotangent_pad, halves_ref, high_ref, low_ref, high_pool, low_pool,
    rows_ref, wide_ref, tall_ref, sums_ref, band_ref, back_ref,
):
    build_band(band_ref, weight_rows(one_ref[...].astype(F32)))
    build_band(back_ref, flipped_rows(two_ref[...].astype(F32)))
    position = lax.axis_index("space")
    tiles = received_ref.shape[1] // (3 * BRICKS)
    rows_ref[0 : 3 * BRICKS * tiles] = jnp.sum(received_ref[...].astype(F32), axis=0)
    rows_ref[3 * BRICKS * tiles :] = jnp.zeros((2 * tiles, 128), F32)
    cells = []
    for tile in range(tiles):
        rows = rows_ref[pl.ds(tile, 8, stride=tiles), :]
        cells += [rows[:, :64], rows[:, 64:]]
    lifted = dot(jnp.concatenate(cells, axis=0).astype(BF16), up_ref[...])
    lifted = lifted.astype(BF16).astype(F32)
    for cell in range(8):
        a, b, c = cell // 4, cell // 2 % 2, cell % 2
        for sub in range(16):
            line = (4 * a + sub // 4) * EDGE + 4 * b + sub % 4
            volumes_ref[c, pl.ds(line, 8, stride=CUBE), :] = lifted[
                cell * 8 : cell * 8 + 8, sub * 128 : sub * 128 + 128
            ]
    for brick in range(BRICKS):

        def near(face):
            link = links_ref[0, brick, face]
            index = jnp.clip(link - BRICKS * (position - 1), 0, 3 * BRICKS - 1)
            return pl.multiple_of(index * CUBE, CUBE), jnp.where(link >= 0, 1.0, 0.0).astype(F32)

        def x_face(face):
            start, present = near(face)
            offset = EDGE * (EDGE - 1) if face % 2 == 0 else 0
            return lines(volumes_ref, pl.multiple_of(start + offset, 8), EDGE) * present

        def y_face(face):
            start, present = near(face)
            offset = EDGE - 1 if face % 2 == 0 else 0
            return lines(volumes_ref, start + offset, EDGE, EDGE) * present

        def z_face(face):
            start, present = near(face)
            tile = volumes_ref[1 if face % 2 == 0 else 0, pl.ds(start, CUBE), :] * present
            return tile.reshape(EDGE, EDGE, 128)

        own = (BRICKS + brick) * CUBE
        volume = lines(volumes_ref, own, CUBE).reshape(EDGE, EDGE, LINE)
        put_padded(
            lifted_pad, brick, volume, x_face(0), x_face(1), y_face(2), y_face(3), z_face(4), z_face(5)
        )
    pre = convolve(lifted_pad, band_ref)
    sigmoid = 1.0 / (1.0 + jnp.exp(-pre))
    hidden = (pre / (1.0 + jnp.exp(-pre))).astype(BF16)
    lifted_out[...] = lines(volumes_ref, BRICKS * CUBE, LINES).astype(BF16)
    hidden_out[...] = hidden
    put_lines(halves_ref, hidden.astype(F32))
    pack_both(halves_ref, high_ref, low_ref, high_out, low_out)
    fill_pools(high_pool, low_pool, high_own, low_own, high_left, low_right)
    cotangent = cotangent_ref[...].astype(F32).reshape(LINES, LINE)
    for brick in range(BRICKS):
        padded_brick(cotangent_pad, brick, cotangent, links_ref, high_pool, low_pool)
    back = convolve(cotangent_pad, back_ref)
    gradient = (back * sigmoid * (1.0 + pre * (1.0 - sigmoid))).astype(BF16)
    sums_ref[8 * BLOCKS :] = jnp.zeros((sums_ref.shape[0] - 8 * BLOCKS, 128), F32)
    for k in range(9):
        tall_ref[...] = dot_rows(window(lifted_pad, k), gradient)
        for part in range(3):
            places = [[(wide_start(4 * t + b + part - 1), t) for t in range(2)] for b in range(4)]
            start = 8 * (3 * k + part)
            sums_ref[start : start + 8] = fold(tall_ref, places)
        wide_ref[...] = dot_rows(hidden, window(cotangent_pad, 8 - k))
        for part in range(3):
            places = [[], [], [], []]
            for z in range(EDGE):
                other = z + 1 - part
                places[other % 4].append((z * CHANNELS, wide_start(other) // 128))
            start = 8 * (27 + 3 * k + part)
            sums_ref[start : start + 8] = fold(wide_ref, places)
    sums_out[...] = sums_ref[...].astype(BF16).reshape(sums_out.shape)


def fine_kernel(
    links_ref, two_ref, lifted_ref, hidden_ref, high_own, low_own, high_left, low_right,
    fine_out, hidden_pad, high_pool, low_pool, band_ref,
):
    build_band(band_ref, weight_rows(two_ref[...].astype(F32)))
    fill_pools(high_pool, low_pool, high_own, low_own, high_left, low_right)
    hidden = hidden_ref[...].astype(F32)
    for brick in range(BRICKS):
        padded_brick(hidden_pad, brick, hidden, links_ref, high_pool, low_pool)
    fine = lifted_ref[...].astype(F32) + convolve(hidden_pad, band_ref)
    fine_out[...] = fine.astype(BF16).reshape(fine_out.shape)


def sum_kernel(scale, parts_ref, *refs):
    out_ref = refs[-1]
    total = jnp.sum(parts_ref[...].astype(F32), axis=0) * scale
    out_ref[...] = jnp.broadcast_to(total.astype(BF16)[None], out_ref.shape)


def unpack_kernel(sums_ref, one_out, two_out, rows_ref):
    rows_ref[...] = sums_ref[...].astype(F32).reshape(rows_ref.shape)
    for index in range(BLOCKS):
        block = rows_ref[8 * index : 8 * index + 8]
        out = one_out if index < 27 else two_out
        for q in range(4):
            moved = pltpu.roll(block, 128 - q * CHANNELS, 1) if q else block
            out[index % 27, 8 * q : 8 * q + 8, :] = moved[:, :CHANNELS]


def call(kernel, out_shape, scratch=(), smem=(), unread=(), inputs=1, limit=24, cost=None):
    spaces = [pltpu.SMEM if i in smem else pl.ANY if i in unread else pltpu.VMEM for i in range(inputs)]
    return pl.pallas_call(
        kernel,
        out_shape=out_shape,
        in_specs=[pl.BlockSpec(memory_space=space) for space in spaces],
        out_specs=jax.tree.map(lambda _: pl.BlockSpec(memory_space=pltpu.VMEM), out_shape),
        scratch_shapes=list(scratch),
        compiler_params=pltpu.CompilerParams(vmem_limit_bytes=limit * 2**20),
        cost_estimate=cost,
    )


def shape(*dims, dtype=BF16):
    return jax.ShapeDtypeStruct(dims, dtype)


def passed_along(value, axis, steps):
    count = lax.axis_size(axis)
    first, last = (max(0, -steps), min(count, count - steps))
    return lax.ppermute(value, axis, [(source, source + steps) for source in range(first, last)])


def body(coarse_latents, active_blocks, face_links, cotangent, up_weight, conv_one, conv_two):
    devices = lax.axis_size("space")
    everyone = devices * lax.axis_size("dp")
    width = coarse_latents.shape[2]
    bricks = active_blocks.shape[1]
    tiles = width // 128
    packed = call(
        functools.partial(pick_kernel, devices),
        shape(devices, 3 * BRICKS * tiles, 128),
        [pltpu.VMEM(((bricks + 16) * tiles, 128), F32)],
        inputs=2,
    )(active_blocks, coarse_latents)
    received = lax.all_to_all(packed, "space", split_axis=0, concat_axis=0, tiled=True)
    band = pltpu.VMEM((9, WIDE, LINE), BF16)
    cost = pl.CostEstimate(flops=10**9, bytes_accessed=2 * 10**6, transcendentals=0)
    face = shape(BRICKS * FACE, LINE)
    halves = pltpu.VMEM((2, LINES, 128), F32)
    faces = pltpu.VMEM((BRICKS * FACE, LINE), F32)
    pool = pltpu.VMEM((2 * BRICKS * FACE, LINE), F32)
    pad = pltpu.VMEM((3, BRICKS, EDGE + 2, EDGE, WIDE), F32)
    volume = shape(LINES, LINE)
    per = -(-BLOCKS // everyone)
    per += per % 2
    high, low = call(faces_kernel, (face, face), [halves, faces, faces])(cotangent)
    high_left = passed_along(high, "space", 1)
    low_right = passed_along(low, "space", -1)
    lifted, hidden, hidden_high, hidden_low, sums = call(
        first_kernel,
        (volume, volume, face, face, shape(everyone, per * 8, 128)),
        [
            pltpu.VMEM((2, 8 * CUBE, 128), F32), pad, pad, halves, faces, faces, pool, pool,
            pltpu.VMEM((8 * tiles, 128), F32),
            pltpu.VMEM((LINE, WIDE), F32),
            pltpu.VMEM((WIDE, LINE), F32),
            pltpu.VMEM((everyone * per * 8, 128), F32),
            band,
            band,
        ],
        smem=(0,),
        inputs=10,
    )(
        face_links, received, up_weight, conv_one, conv_two, cotangent, high, low, high_left, low_right
    )
    hidden_left = passed_along(hidden_high, "space", 1)
    hidden_right = passed_along(hidden_low, "space", -1)
    fine = call(fine_kernel, shape(*cotangent.shape), [pad, pool, pool, band], smem=(0,), inputs=8, cost=cost)(
        face_links, conv_two, lifted, hidden, hidden_high, hidden_low, hidden_left, hidden_right
    )
    axes = ("space", "dp")
    parts = lax.all_to_all(sums, axes, split_axis=0, concat_axis=0, tiled=True)
    scale = 1.0 / math.sqrt(lax.axis_size("dp") * devices * BRICKS * EDGE**3)
    total = call(functools.partial(sum_kernel, scale), shape(*sums.shape), unread=(1, 2), inputs=3)(
        parts, hidden_left, hidden_right
    )
    gathered = lax.all_to_all(total, axes, split_axis=0, concat_axis=0, tiled=True)
    grads = shape(27, CHANNELS, CHANNELS, dtype=F32)
    rows = pltpu.VMEM((everyone * per * 8, 128), F32)
    grad_one, grad_two = call(unpack_kernel, (grads, grads), [rows])(gathered)
    return (fine, grad_one, grad_two)


def solution(mesh):
    return jax.shard_map(
        body,
        mesh=mesh,
        in_specs=(
            P("dp", "space", None),
            P("dp", None),
            P("dp", "space", None),
            P("dp", "space", None, None, None),
            P(),
            P(),
            P(),
        ),
        out_specs=(P("dp", "space", None, None, None), P(), P()),
        check_vma=False,
    )
```

```python
import functools
import math

import jax
import jax.numpy as jnp
from jax import lax
from jax.experimental import pallas as pl
from jax.experimental.pallas import tpu as pltpu
from jax.sharding import PartitionSpec as P

BF16 = jnp.bfloat16
F32 = jnp.float32
EDGE = 8
CHANNELS = 32
LINE = EDGE * CHANNELS
WIDE = LINE + 128
BRICKS = 2
CUBE = EDGE * EDGE
LINES = BRICKS * CUBE
FACE = 3 * EDGE
BLOCKS = 54


def dot(left, right):
    return jnp.dot(left, right, preferred_element_type=F32)


def dot_rows(left, right):
    return lax.dot_general(left, right, (((0,), (0,)), ((), ())), preferred_element_type=F32)


def lines(halves_ref, start, count, stride=1):
    index = pl.ds(start, count, stride=stride) if stride > 1 else pl.ds(start, count)
    return jnp.concatenate([halves_ref[0, index, :], halves_ref[1, index, :]], axis=-1)


def lanes_of(shape):
    return lax.broadcasted_iota(jnp.int32, shape, len(shape) - 1)


def pick_kernel(devices, ids_ref, latents_ref, out_ref, rows_ref):
    held, width = latents_ref.shape[1:]
    bricks = ids_ref.shape[1]
    margin = 8 * width // 128
    tiles = width // 128
    rows_ref[0:margin] = jnp.zeros((margin, 128), F32)
    rows_ref[margin + bricks * tiles :] = jnp.zeros((margin, 128), F32)
    rows = lax.broadcasted_iota(jnp.int32, (held, bricks), 0)
    hot = jnp.where(rows == ids_ref[...], 1.0, 0.0).astype(BF16)
    picked = dot_rows(hot, latents_ref[0])
    for tile in range(tiles):
        rows_ref[pl.ds(margin + tile, bricks, stride=tiles), :] = picked[:, tile * 128 : tile * 128 + 128]
    count = out_ref.shape[1]
    for receiver in range(devices):
        start = margin + BRICKS * (receiver - 1) * tiles
        out_ref[receiver] = rows_ref[start : start + count].astype(BF16)


def build_band(band_ref, rows):
    shape = (3 * CHANNELS, LINE)
    row = lax.broadcasted_iota(jnp.int32, shape, 0)
    target = CHANNELS - (row // CHANNELS) * CHANNELS + row % CHANNELS
    distance = lanes_of(shape) - target
    band_ref[:, LINE:, :] = jnp.zeros((9, 128, LINE), BF16)
    places = [(z, z * CHANNELS) for z in range(EDGE)] + [(EDGE, LINE), (-1, WIDE - CHANNELS)]
    for z, start in places:
        select = jnp.where(distance == z * CHANNELS, 1.0, 0.0).astype(BF16)
        block = dot(rows, select).astype(BF16)
        band_ref[:, start : start + CHANNELS, :] = block.reshape(9, CHANNELS, LINE)


def weight_rows(weights):
    cube = weights.reshape(9, 3, CHANNELS, CHANNELS)
    rows = jnp.concatenate([cube[:, 0], cube[:, 1], cube[:, 2]], axis=-1)
    return rows.reshape(9 * CHANNELS, 3 * CHANNELS).astype(BF16)


def flipped_rows(weights):
    cube = jnp.swapaxes(weights, 1, 2).reshape(9, 3, CHANNELS, CHANNELS)
    pieces = [jnp.concatenate([cube[8 - k, 2], cube[8 - k, 1], cube[8 - k, 0]], axis=-1) for k in range(9)]
    return jnp.concatenate(pieces, axis=0).astype(BF16)


def band_kernel(weights_ref, band_ref):
    build_band(band_ref, weight_rows(weights_ref[...].astype(F32)))


def two_bands_kernel(weights_ref, band_ref, back_ref):
    weights = weights_ref[...].astype(F32)
    build_band(band_ref, weight_rows(weights))
    build_band(back_ref, flipped_rows(weights))


def put_padded(pad_ref, brick, volume, x_low, x_high, y_low, y_high, z_low, z_high):
    lane = lanes_of((EDGE, EDGE, 128))
    tail = jnp.where(lane < CHANNELS, z_high, jnp.where(lane >= 128 - CHANNELS, z_low, 0.0))
    full = jnp.concatenate([volume, tail], axis=-1)
    zeros = jnp.zeros((EDGE, 128), F32)
    first = jnp.concatenate([x_low, zeros], axis=-1)[None]
    last = jnp.concatenate([x_high, zeros], axis=-1)[None]
    slabs = jnp.concatenate([first, full, last], axis=0)
    no_halo = jnp.zeros((1, WIDE), F32)
    low = jnp.concatenate([no_halo, jnp.concatenate([y_low, zeros], axis=-1), no_halo], axis=0)
    high = jnp.concatenate([no_halo, jnp.concatenate([y_high, zeros], axis=-1), no_halo], axis=0)
    row = lax.broadcasted_iota(jnp.int32, slabs.shape, 1)
    pad_ref[0, brick] = jnp.where(row == 0, low[:, None, :], pltpu.roll(slabs, 1, 1))
    pad_ref[1, brick] = slabs
    pad_ref[2, brick] = jnp.where(row == EDGE - 1, high[:, None, :], pltpu.roll(slabs, EDGE - 1, 1))


def window(pad_ref, k):
    lines = pad_ref[k % 3, :, k // 3 : k // 3 + EDGE]
    return lines.reshape(LINES, WIDE).astype(BF16)


def convolve(pad_ref, band_ref):
    total = None
    for k in range(9):
        term = dot(window(pad_ref, k), band_ref[k])
        total = term if total is None else total + term
    return total


def pack_faces(faces_ref, base, halves_ref, start, high):
    first = start + ((EDGE - 1) * EDGE if high else 0)
    faces_ref[base : base + EDGE] = lines(halves_ref, first, EDGE)
    first = start + (EDGE - 1 if high else 0)
    faces_ref[base + EDGE : base + 2 * EDGE] = lines(halves_ref, first, EDGE, EDGE)
    tile = halves_ref[1 if high else 0, start : start + CUBE, :]
    lane = lanes_of((16, 128)) // CHANNELS
    packed = jnp.zeros((16, 128), F32)
    for part in range(4):
        shift = (part + 1 if high else part) % 4 * CHANNELS
        piece = tile[part * 16 : part * 16 + 16]
        packed = jnp.where(lane == part, pltpu.roll(piece, shift, 1) if shift else piece, packed)
    faces_ref[base + 2 * EDGE : base + FACE, :128] = packed[:8]
    faces_ref[base + 2 * EDGE : base + FACE, 128:] = packed[8:]


def unpack_depth(rows, high):
    packed = jnp.concatenate([rows[:, :128], rows[:, 128:]], axis=0)
    pieces = []
    for part in range(4):
        shift = ((3 - part) if high else (4 - part)) % 4 * CHANNELS
        pieces.append(pltpu.roll(packed, shift, 1) if shift else packed)
    return jnp.concatenate(pieces, axis=0).reshape(EDGE, EDGE, 128)


def first_kernel(
    links_ref, received_ref, up_ref, band_ref, cotangent_ref,
    lifted_out, pre_out, hidden_out, pad_out, high_out, low_out, far_out, near_out,
    volumes_ref, pad_ref, lines_ref, high_ref, low_ref, rows_ref,
):
    position = lax.axis_index("space")
    tiles = received_ref.shape[1] // (3 * BRICKS)
    rows_ref[0 : 3 * BRICKS * tiles] = jnp.sum(received_ref[...].astype(F32), axis=0)
    rows_ref[3 * BRICKS * tiles :] = jnp.zeros((2 * tiles, 128), F32)
    cells = []
    for tile in range(tiles):
        rows = rows_ref[pl.ds(tile, 8, stride=tiles), :]
        cells += [rows[:, :64], rows[:, 64:]]
    lifted = dot(jnp.concatenate(cells, axis=0).astype(BF16), up_ref[...])
    lifted = lifted.astype(BF16).astype(F32)
    for cell in range(8):
        a, b, c = cell // 4, cell // 2 % 2, cell % 2
        for sub in range(16):
            line = (4 * a + sub // 4) * EDGE + 4 * b + sub % 4
            volumes_ref[c, pl.ds(line, 8, stride=CUBE), :] = lifted[
                cell * 8 : cell * 8 + 8, sub * 128 : sub * 128 + 128
            ]
    for brick in range(BRICKS):

        def near(face):
            link = links_ref[0, brick, face]
            index = jnp.clip(link - BRICKS * (position - 1), 0, 3 * BRICKS - 1)
            return pl.multiple_of(index * CUBE, CUBE), jnp.where(link >= 0, 1.0, 0.0).astype(F32)

        def x_face(face):
            start, present = near(face)
            offset = EDGE * (EDGE - 1) if face % 2 == 0 else 0
            return lines(volumes_ref, pl.multiple_of(start + offset, 8), EDGE) * present

        def y_face(face):
            start, present = near(face)
            offset = EDGE - 1 if face % 2 == 0 else 0
            return lines(volumes_ref, start + offset, EDGE, EDGE) * present

        def z_face(face):
            start, present = near(face)
            tile = volumes_ref[1 if face % 2 == 0 else 0, pl.ds(start, CUBE), :] * present
            return tile.reshape(EDGE, EDGE, 128)

        own = (BRICKS + brick) * CUBE
        volume = lines(volumes_ref, own, CUBE).reshape(EDGE, EDGE, LINE)
        put_padded(
            pad_ref, brick, volume, x_face(0), x_face(1), y_face(2), y_face(3), z_face(4), z_face(5)
        )
    pre = convolve(pad_ref, band_ref)
    hidden = pre / (1.0 + jnp.exp(-pre))
    hidden = hidden.astype(BF16)
    lifted_out[...] = lines(volumes_ref, BRICKS * CUBE, LINES).astype(BF16)
    pre_out[...] = pre
    hidden_out[...] = hidden
    pad_out[...] = pad_ref[...].reshape(pad_out.shape).astype(BF16)
    sources = (hidden.astype(F32), cotangent_ref[...].astype(F32).reshape(LINES, LINE))
    for which, values in enumerate(sources):
        for half in range(2):
            lines_ref[half, which * LINES : which * LINES + LINES] = values[:, half * 128 : half * 128 + 128]
    for which in range(2):
        for brick in range(BRICKS):
            base = (which * BRICKS + brick) * FACE
            start = which * LINES + brick * CUBE
            pack_faces(high_ref, base, lines_ref, start, True)
            pack_faces(low_ref, base, lines_ref, start, False)
    high = high_ref[...].astype(BF16)
    low = low_ref[...].astype(BF16)
    high_out[...] = high
    low_out[...] = low
    even = position % 2 == 0
    far_out[...] = jnp.where(even, low, high)
    near_out[...] = jnp.where(even, high, low)


def fold_diagonals(outer_ref, part):
    lane = lanes_of((CHANNELS, 128)) // CHANNELS
    folded = None
    for half in range(2):
        picked = None
        for block in range(4):
            depth = 4 * half + block + part - 1
            start = depth * CHANNELS if 0 <= depth < EDGE else (LINE if depth == EDGE else WIDE - CHANNELS)
            rows = outer_ref[start : start + CHANNELS, half * 128 : half * 128 + 128]
            picked = rows if picked is None else jnp.where(lane == block, rows, picked)
        folded = picked if folded is None else folded + picked
    quarter = [folded[8 * q : 8 * q + 8] for q in range(4)]
    small = lanes_of((8, 128)) // CHANNELS
    total = None
    for turn in range(4):
        mixed = quarter[0]
        for q in range(1, 4):
            mixed = jnp.where(small == (q + turn) % 4, quarter[q], mixed)
        if turn:
            mixed = pltpu.roll(mixed, 128 - turn * CHANNELS, 1)
        total = mixed if total is None else total + mixed
    return total


def padded_brick(pad_ref, brick, which, values, links_ref, high_ref, low_ref):
    position = lax.axis_index("space")
    half = high_ref.shape[0] // 2

    def rows(face, axis):
        link = links_ref[0, brick, face]
        high = face % 2 == 0
        index = jnp.clip(link - BRICKS * (position - 1 if high else position), 0, 2 * BRICKS - 1)
        start = (index // BRICKS) * half + (which * BRICKS + index % BRICKS) * FACE + axis * EDGE
        pool = high_ref if high else low_ref
        present = jnp.where(link >= 0, 1.0, 0.0).astype(F32)
        return pool[pl.ds(pl.multiple_of(start, 8), EDGE), :] * present

    volume = values[brick * CUBE : brick * CUBE + CUBE].reshape(EDGE, EDGE, LINE)
    put_padded(
        pad_ref, brick, volume, rows(0, 0), rows(1, 0), rows(2, 1), rows(3, 1),
        unpack_depth(rows(4, 2), True), unpack_depth(rows(5, 2), False),
    )


def fill_pools(high_ref, low_ref, high_own, low_own, far, near):
    half = 2 * BRICKS * FACE
    even = lax.axis_index("space") % 2 == 0
    high_ref[0:half] = jnp.where(even, far[...], near[...]).astype(F32)
    high_ref[half:] = high_own[...].astype(F32)
    low_ref[0:half] = low_own[...].astype(F32)
    low_ref[half:] = jnp.where(even, near[...], far[...]).astype(F32)


def second_kernel(
    links_ref, cotangent_ref, band_ref, back_ref, lifted_ref, pre_ref, hidden_ref, pad_in,
    high_own, low_own, far, near,
    fine_out, sums_out,
    high_ref, low_ref, hidden_pad, cotangent_pad, lifted_pad, outer_ref, sums_ref,
):
    fill_pools(high_ref, low_ref, high_own, low_own, far, near)
    lifted_pad[...] = pad_in[...].astype(F32).reshape(lifted_pad.shape)
    cotangent = cotangent_ref[...].astype(F32).reshape(LINES, LINE)
    hidden = hidden_ref[...].astype(F32)
    for which, values, pad_ref in ((0, hidden, hidden_pad), (1, cotangent, cotangent_pad)):
        for brick in range(BRICKS):
            padded_brick(pad_ref, brick, which, values, links_ref, high_ref, low_ref)
    fine = lifted_ref[...].astype(F32) + convolve(hidden_pad, band_ref)
    fine_out[...] = fine.astype(BF16).reshape(fine_out.shape)
    back = convolve(cotangent_pad, back_ref)
    pre = pre_ref[...]
    sigmoid = 1.0 / (1.0 + jnp.exp(-pre))
    gradient = (back * sigmoid * (1.0 + pre * (1.0 - sigmoid))).astype(BF16)
    upstream = cotangent.astype(BF16)
    sums_ref[8 * BLOCKS :] = jnp.zeros((sums_ref.shape[0] - 8 * BLOCKS, 128), F32)
    for base, pad_ref, right in ((0, lifted_pad, gradient), (27, hidden_pad, upstream)):
        for k in range(9):
            outer_ref[...] = dot_rows(window(pad_ref, k), right)
            for part in range(3):
                start = 8 * (base + 3 * k + part)
                sums_ref[start : start + 8] = fold_diagonals(outer_ref, part)
    sums_out[...] = sums_ref[...].astype(BF16).reshape(sums_out.shape)


def sum_kernel(scale, parts_ref, out_ref):
    total = jnp.sum(parts_ref[...].astype(F32), axis=0) * scale
    out_ref[...] = jnp.broadcast_to(total.astype(BF16)[None], out_ref.shape)


def unpack_kernel(sums_ref, one_out, two_out, rows_ref):
    rows_ref[...] = sums_ref[...].astype(F32).reshape(rows_ref.shape)
    for index in range(BLOCKS):
        block = rows_ref[8 * index : 8 * index + 8]
        out = one_out if index < 27 else two_out
        for q in range(4):
            moved = pltpu.roll(block, 128 - q * CHANNELS, 1) if q else block
            out[index % 27, 8 * q : 8 * q + 8, :] = moved[:, :CHANNELS]


def call(kernel, out_shape, scratch=(), smem=(), inputs=1, limit=24, cost=None):
    spaces = [pltpu.SMEM if i in smem else pltpu.VMEM for i in range(inputs)]
    return pl.pallas_call(
        kernel,
        out_shape=out_shape,
        in_specs=[pl.BlockSpec(memory_space=space) for space in spaces],
        out_specs=jax.tree.map(lambda _: pl.BlockSpec(memory_space=pltpu.VMEM), out_shape),
        scratch_shapes=list(scratch),
        compiler_params=pltpu.CompilerParams(vmem_limit_bytes=limit * 2**20),
        cost_estimate=cost,
    )


def shape(*dims, dtype=BF16):
    return jax.ShapeDtypeStruct(dims, dtype)


def swapped(value, first):
    pairs = [(i, i + 1) for i in range(first, lax.axis_size("space") - 1, 2)]
    return lax.ppermute(value, "space", pairs + [(target, source) for source, target in pairs])


def body(coarse_latents, active_blocks, face_links, cotangent, up_weight, conv_one, conv_two):
    devices = lax.axis_size("space")
    everyone = devices * lax.axis_size("dp")
    held, width = coarse_latents.shape[1:]
    bricks = active_blocks.shape[1]
    tiles = width // 128
    packed = call(
        functools.partial(pick_kernel, devices),
        shape(devices, 3 * BRICKS * tiles, 128),
        [pltpu.VMEM(((bricks + 16) * tiles, 128), F32)],
        inputs=2,
    )(active_blocks - lax.axis_index("space") * held, coarse_latents)
    received = lax.all_to_all(packed, "space", split_axis=0, concat_axis=0, tiled=True)
    band = shape(9, WIDE, LINE)
    cost = pl.CostEstimate(flops=10**9, bytes_accessed=2 * 10**6, transcendentals=0)
    band_one = call(band_kernel, band, cost=cost)(conv_one)
    band_two, band_back = call(two_bands_kernel, (band, band), cost=cost)(conv_two)
    pad_shape = (3, BRICKS, EDGE + 2, EDGE, WIDE)
    pad = pltpu.VMEM(pad_shape, F32)
    packed_faces = 2 * BRICKS * FACE
    lifted, pre, hidden, lifted_pad, high, low, far, near = call(
        first_kernel,
        (
            shape(LINES, LINE),
            shape(LINES, LINE, dtype=F32),
            shape(LINES, LINE),
            shape(math.prod(pad_shape[:-1]), WIDE),
            shape(packed_faces, LINE),
            shape(packed_faces, LINE),
            shape(packed_faces, LINE),
            shape(packed_faces, LINE),
        ),
        [
            pltpu.VMEM((2, 8 * CUBE, 128), F32),
            pad,
            pltpu.VMEM((2, 2 * LINES, 128), F32),
            pltpu.VMEM((packed_faces, LINE), F32),
            pltpu.VMEM((packed_faces, LINE), F32),
            pltpu.VMEM((8 * tiles, 128), F32),
        ],
        smem=(0,),
        inputs=5,
    )(face_links, received, up_weight, band_one, cotangent)
    far = swapped(far, 1)
    near = swapped(near, 0)
    per = -(-BLOCKS // everyone)
    per += per % 2
    fine, sums = call(
        second_kernel,
        (shape(*cotangent.shape), shape(everyone, per * 8, 128)),
        [
            pltpu.VMEM((2 * packed_faces, LINE), F32),
            pltpu.VMEM((2 * packed_faces, LINE), F32),
            pad,
            pad,
            pad,
            pltpu.VMEM((WIDE, LINE), F32),
            pltpu.VMEM((everyone * per * 8, 128), F32),
        ],
        smem=(0,),
        inputs=12,
    )(
        face_links, cotangent, band_two, band_back, lifted, pre, hidden, lifted_pad,
        high, low, far, near,
    )
    axes = ("space", "dp")
    parts = lax.all_to_all(sums, axes, split_axis=0, concat_axis=0, tiled=True)
    scale = 1.0 / math.sqrt(lax.axis_size("dp") * devices * BRICKS * EDGE**3)
    total = call(functools.partial(sum_kernel, scale), shape(*sums.shape))(parts)
    gathered = lax.all_to_all(total, axes, split_axis=0, concat_axis=0, tiled=True)
    grads = shape(27, CHANNELS, CHANNELS, dtype=F32)
    rows = pltpu.VMEM((everyone * per * 8, 128), F32)
    grad_one, grad_two = call(unpack_kernel, (grads, grads), [rows])(gathered)
    return (fine, grad_one, grad_two)


def solution(mesh):
    return jax.shard_map(
        body,
        mesh=mesh,
        in_specs=(
            P("dp", "space", None),
            P("dp", None),
            P("dp", "space", None),
            P("dp", "space", None, None, None),
            P(),
            P(),
            P(),
        ),
        out_specs=(P("dp", "space", None, None, None), P(), P()),
        check_vma=False,
    )
```

```python
import functools
import math

import jax
import jax.numpy as jnp
from jax import lax
from jax.experimental import pallas as pl
from jax.experimental.pallas import tpu as pltpu
from jax.sharding import PartitionSpec as P

BF16 = jnp.bfloat16
F32 = jnp.float32
EDGE = 8
CHANNELS = 32
LINE = EDGE * CHANNELS
HALF = LINE // 2
WIDE = 2 * HALF
BRICKS = 2
CUBE = EDGE * EDGE
LINES = BRICKS * CUBE
ROWS = 2 * LINES
FACE = 3 * EDGE
BLOCKS = 54


def dot(left, right):
    return jnp.dot(left, right, preferred_element_type=F32)


def dot_rows(left, right):
    return lax.dot_general(left, right, (((0,), (0,)), ((), ())), preferred_element_type=F32)


def pair(halves_ref, start, count, stride=1):
    index = pl.ds(start, count, stride=stride) if stride > 1 else pl.ds(start, count)
    return halves_ref[0, index, :], halves_ref[1, index, :]


def lanes_of(shape):
    return lax.broadcasted_iota(jnp.int32, shape, len(shape) - 1)


def pick_kernel(devices, ids_hbm, latents_hbm, out_ref, ids_ref, latents_ref, rows_ref, sems):
    ids_copy = pltpu.make_async_copy(ids_hbm, ids_ref, sems.at[0])
    latents_copy = pltpu.make_async_copy(latents_hbm, latents_ref, sems.at[1])
    ids_copy.start()
    latents_copy.start()
    held, width = latents_ref.shape[1:]
    bricks = ids_ref.shape[1]
    margin = 8 * width // 128
    tiles = width // 128
    rows_ref[0:margin] = jnp.zeros((margin, 128), F32)
    rows_ref[margin + bricks * tiles :] = jnp.zeros((margin, 128), F32)
    first = lax.axis_index("space") * held
    rows = lax.broadcasted_iota(jnp.int32, (held, bricks), 0) + first
    ids_copy.wait()
    hot = jnp.where(rows == ids_ref[...], 1.0, 0.0).astype(BF16)
    latents_copy.wait()
    picked = dot_rows(hot, latents_ref[0])
    for tile in range(tiles):
        rows_ref[pl.ds(margin + tile, bricks, stride=tiles), :] = picked[:, tile * 128 : tile * 128 + 128]
    count = out_ref.shape[1]
    for receiver in range(devices):
        start = margin + BRICKS * (receiver - 1) * tiles
        out_ref[receiver] = rows_ref[start : start + count].astype(BF16)


def build_band(band_ref, rows):
    shape = (3 * CHANNELS, HALF)
    row = lax.broadcasted_iota(jnp.int32, shape, 0)
    target = CHANNELS - (row // CHANNELS) * CHANNELS + row % CHANNELS
    distance = lanes_of(shape) - target
    band_ref[:, HALF:, :] = jnp.zeros((9, HALF, HALF), BF16)
    for z in range(-1, 5):
        select = jnp.where(distance == z * CHANNELS, 1.0, 0.0).astype(BF16)
        block = dot(rows, select).astype(BF16)
        start = z % 8 * CHANNELS
        band_ref[:, start : start + CHANNELS, :] = block.reshape(9, CHANNELS, HALF)


def weight_rows(weights):
    cube = weights.reshape(9, 3, CHANNELS, CHANNELS)
    rows = jnp.concatenate([cube[:, 0], cube[:, 1], cube[:, 2]], axis=-1)
    return rows.reshape(9 * CHANNELS, 3 * CHANNELS).astype(BF16)


def flipped_rows(weights):
    cube = jnp.swapaxes(weights, 1, 2).reshape(9, 3, CHANNELS, CHANNELS)
    pieces = [jnp.concatenate([cube[8 - k, 2], cube[8 - k, 1], cube[8 - k, 0]], axis=-1) for k in range(9)]
    return jnp.concatenate(pieces, axis=0).astype(BF16)


def band_kernel(weights_ref, band_ref):
    build_band(band_ref, weight_rows(weights_ref[...].astype(F32)))


def two_bands_kernel(weights_ref, band_ref, back_ref):
    weights = weights_ref[...].astype(F32)
    build_band(band_ref, weight_rows(weights))
    build_band(back_ref, flipped_rows(weights))


def put_padded(pad_ref, brick, lines, x_low, x_high, y_low, y_high, z_low, z_high):
    def joined(halves, before, after):
        lane = lanes_of(halves[0].shape)
        first = jnp.where(lane < CHANNELS, halves[1], before)
        second = jnp.where(lane >= HALF - CHANNELS, halves[0], after)
        return jnp.concatenate([halves[0], first], axis=-1), jnp.concatenate([halves[1], second], axis=-1)

    inside = joined(lines, z_low, z_high)
    x_low, x_high, y_low, y_high = [joined(face, 0.0, 0.0) for face in (x_low, x_high, y_low, y_high)]
    none = jnp.zeros((1, WIDE), F32)
    shifted = [[], [], []]
    for half in range(2):
        slabs = jnp.concatenate([x_low[half][None], inside[half], x_high[half][None]], axis=0)
        row = lax.broadcasted_iota(jnp.int32, slabs.shape, 1)
        low = jnp.concatenate([none, y_low[half], none], axis=0)[:, None, :]
        high = jnp.concatenate([none, y_high[half], none], axis=0)[:, None, :]
        shifted[0].append(jnp.where(row == 0, low, pltpu.roll(slabs, 1, 1)))
        shifted[1].append(slabs)
        shifted[2].append(jnp.where(row == EDGE - 1, high, pltpu.roll(slabs, EDGE - 1, 1)))
    for dy in range(3):
        pad_ref[dy, brick] = jnp.concatenate(shifted[dy], axis=1).astype(BF16)


def window(pad_ref, k):
    return pad_ref[k % 3, :, k // 3 : k // 3 + EDGE].reshape(ROWS, WIDE)


def convolve(pad_ref, band_ref):
    total = None
    for k in range(9):
        term = dot(window(pad_ref, k), band_ref[k])
        total = term if total is None else total + term
    return total


def half_lines(values):
    cube = values.reshape(BRICKS, EDGE, 2, EDGE, HALF)
    return [(cube[brick, :, 0], cube[brick, :, 1]) for brick in range(BRICKS)]


def put_halves(halves_ref, start, bricks):
    for brick, lines in enumerate(bricks):
        for half in range(2):
            first = start + brick * CUBE
            halves_ref[half, first : first + CUBE, :] = lines[half].reshape(CUBE, HALF)


def cotangent_lines(cotangent_ref):
    cube = cotangent_ref[...].astype(F32).reshape(BRICKS, EDGE, EDGE, LINE)
    return [(cube[brick, :, :, :HALF], cube[brick, :, :, HALF:]) for brick in range(BRICKS)]


def pack_faces(faces_ref, base, halves_ref, start, high):
    x_face = pair(halves_ref, start + ((EDGE - 1) * EDGE if high else 0), EDGE)
    y_face = pair(halves_ref, start + (EDGE - 1 if high else 0), EDGE, EDGE)
    for half in range(2):
        lanes = slice(half * HALF, half * HALF + HALF)
        faces_ref[base : base + EDGE, lanes] = x_face[half]
        faces_ref[base + EDGE : base + 2 * EDGE, lanes] = y_face[half]
    tile = halves_ref[1 if high else 0, start : start + CUBE, :]
    lane = lanes_of((16, 128)) // CHANNELS
    packed = jnp.zeros((16, 128), F32)
    for part in range(4):
        shift = (part + 1 if high else part) % 4 * CHANNELS
        piece = tile[part * 16 : part * 16 + 16]
        packed = jnp.where(lane == part, pltpu.roll(piece, shift, 1) if shift else piece, packed)
    faces_ref[base + 2 * EDGE : base + FACE, :128] = packed[:8]
    faces_ref[base + 2 * EDGE : base + FACE, 128:] = packed[8:]


def unpack_depth(rows, high):
    packed = jnp.concatenate([rows[:, :128], rows[:, 128:]], axis=0)
    pieces = []
    for part in range(4):
        shift = ((3 - part) if high else (4 - part)) % 4 * CHANNELS
        pieces.append(pltpu.roll(packed, shift, 1) if shift else packed)
    return jnp.concatenate(pieces, axis=0).reshape(EDGE, EDGE, 128)


def first_kernel(
    links_ref, received_ref, up_ref, band_ref, cotangent_ref,
    pre_out, hidden_out, pad_out, high_out, low_out, far_out, near_out,
    volumes_ref, lines_ref, high_ref, low_ref, rows_ref,
):
    position = lax.axis_index("space")
    tiles = received_ref.shape[1] // (3 * BRICKS)
    rows_ref[0 : 3 * BRICKS * tiles] = jnp.sum(received_ref[...].astype(F32), axis=0)
    rows_ref[3 * BRICKS * tiles :] = jnp.zeros((2 * tiles, 128), F32)
    cells = []
    for tile in range(tiles):
        rows = rows_ref[pl.ds(tile, 8, stride=tiles), :]
        cells += [rows[:, :64], rows[:, 64:]]
    lifted = dot(jnp.concatenate(cells, axis=0).astype(BF16), up_ref[...])
    lifted = lifted.astype(BF16).astype(F32)
    for cell in range(8):
        a, b, c = cell // 4, cell // 2 % 2, cell % 2
        for sub in range(16):
            line = (4 * a + sub // 4) * EDGE + 4 * b + sub % 4
            volumes_ref[c, pl.ds(line, 8, stride=CUBE), :] = lifted[
                cell * 8 : cell * 8 + 8, sub * 128 : sub * 128 + 128
            ]
    for brick in range(BRICKS):

        def near(face):
            link = links_ref[0, brick, face]
            index = jnp.clip(link - BRICKS * (position - 1), 0, 3 * BRICKS - 1)
            return pl.multiple_of(index * CUBE, CUBE), jnp.where(link >= 0, 1.0, 0.0).astype(F32)

        def x_face(face):
            start, present = near(face)
            offset = EDGE * (EDGE - 1) if face % 2 == 0 else 0
            return [half * present for half in pair(volumes_ref, pl.multiple_of(start + offset, 8), EDGE)]

        def y_face(face):
            start, present = near(face)
            offset = EDGE - 1 if face % 2 == 0 else 0
            return [half * present for half in pair(volumes_ref, start + offset, EDGE, EDGE)]

        def z_face(face):
            start, present = near(face)
            tile = volumes_ref[1 if face % 2 == 0 else 0, pl.ds(start, CUBE), :] * present
            return tile.reshape(EDGE, EDGE, HALF)

        own = pair(volumes_ref, (BRICKS + brick) * CUBE, CUBE)
        own = [half.reshape(EDGE, EDGE, HALF) for half in own]
        put_padded(pad_out, brick, own, x_face(0), x_face(1), y_face(2), y_face(3), z_face(4), z_face(5))
    pre = convolve(pad_out, band_ref)
    hidden = pre / (1.0 + jnp.exp(-pre))
    hidden = hidden.astype(BF16)
    pre_out[...] = pre
    hidden_out[...] = hidden
    put_halves(lines_ref, 0, half_lines(hidden.astype(F32)))
    put_halves(lines_ref, LINES, cotangent_lines(cotangent_ref))
    for which in range(2):
        for brick in range(BRICKS):
            base = (which * BRICKS + brick) * FACE
            start = which * LINES + brick * CUBE
            pack_faces(high_ref, base, lines_ref, start, True)
            pack_faces(low_ref, base, lines_ref, start, False)
    high = high_ref[...].astype(BF16)
    low = low_ref[...].astype(BF16)
    high_out[...] = high
    low_out[...] = low
    even = position % 2 == 0
    far_out[...] = jnp.where(even, low, high)
    near_out[...] = jnp.where(even, high, low)


def fold(outer_ref, places):
    lane = lanes_of((CHANNELS, 128)) // CHANNELS
    folded = None
    for block in range(4):
        start, tile = places[block]
        rows = outer_ref[start : start + CHANNELS, tile * 128 : tile * 128 + 128]
        folded = rows if folded is None else jnp.where(lane == block, rows, folded)
    quarter = [folded[8 * q : 8 * q + 8] for q in range(4)]
    small = lanes_of((8, 128)) // CHANNELS
    total = None
    for turn in range(4):
        mixed = quarter[0]
        for q in range(1, 4):
            mixed = jnp.where(small == (q + turn) % 4, quarter[q], mixed)
        if turn:
            mixed = pltpu.roll(mixed, 128 - turn * CHANNELS, 1)
        total = mixed if total is None else total + mixed
    return total


def diagonal(shift):
    places = [None] * 4
    for z in range(4):
        other = z + shift
        places[other % 4] = (z * CHANNELS, 0 if 0 <= other < 4 else 1)
    return places


def padded_brick(pad_ref, brick, which, lines, links_ref, high_ref, low_ref):
    position = lax.axis_index("space")
    half = high_ref.shape[0] // 2

    def rows(face, axis):
        link = links_ref[0, brick, face]
        high = face % 2 == 0
        index = jnp.clip(link - BRICKS * (position - 1 if high else position), 0, 2 * BRICKS - 1)
        start = (index // BRICKS) * half + (which * BRICKS + index % BRICKS) * FACE + axis * EDGE
        pool = high_ref if high else low_ref
        present = jnp.where(link >= 0, 1.0, 0.0).astype(F32)
        return pool[pl.ds(pl.multiple_of(start, 8), EDGE), :] * present

    def face(number, axis):
        found = rows(number, axis)
        return found[:, :HALF], found[:, HALF:]

    put_padded(
        pad_ref, brick, lines, face(0, 0), face(1, 0), face(2, 1), face(3, 1),
        unpack_depth(rows(4, 2), True), unpack_depth(rows(5, 2), False),
    )


def fill_pools(high_ref, low_ref, high_own, low_own, far, near):
    half = 2 * BRICKS * FACE
    even = lax.axis_index("space") % 2 == 0
    high_ref[0:half] = jnp.where(even, far[...], near[...]).astype(F32)
    high_ref[half:] = high_own[...].astype(F32)
    low_ref[0:half] = low_own[...].astype(F32)
    low_ref[half:] = jnp.where(even, near[...], far[...]).astype(F32)


def second_kernel(
    links_ref, cotangent_ref, band_ref, back_ref, pre_ref, hidden_ref, lifted_pad,
    high_own, low_own, far, near,
    fine_out, sums_out,
    high_ref, low_ref, hidden_pad, cotangent_pad, one_ref, two_ref, sums_ref,
):
    fill_pools(high_ref, low_ref, high_own, low_own, far, near)
    hidden = hidden_ref[...].astype(F32)
    sources = (half_lines(hidden), cotangent_lines(cotangent_ref))
    for which, pad_ref in ((0, hidden_pad), (1, cotangent_pad)):
        for brick in range(BRICKS):
            padded_brick(pad_ref, brick, which, sources[which][brick], links_ref, high_ref, low_ref)
    lifted = window(lifted_pad, 4)[:, :HALF].astype(F32)
    fine = (lifted + convolve(hidden_pad, band_ref)).reshape(LINES // EDGE, 2, EDGE, HALF)
    fine = jnp.concatenate([fine[:, 0], fine[:, 1]], axis=-1)
    fine_out[...] = fine.astype(BF16).reshape(fine_out.shape)
    back = convolve(cotangent_pad, back_ref)
    pre = pre_ref[...]
    sigmoid = 1.0 / (1.0 + jnp.exp(-pre))
    gradient = (back * sigmoid * (1.0 + pre * (1.0 - sigmoid))).astype(BF16)
    gradient = jnp.transpose(gradient.astype(F32)).astype(BF16)
    hidden = jnp.transpose(hidden).astype(BF16)
    sums_ref[8 * BLOCKS :] = jnp.zeros((sums_ref.shape[0] - 8 * BLOCKS, 128), F32)
    for k in range(9):
        one_ref[...] = dot(gradient, window(lifted_pad, k))
        two_ref[...] = dot(hidden, window(cotangent_pad, 8 - k))
        for part in range(3):
            start = 8 * (3 * k + part)
            sums_ref[start : start + 8] = fold(one_ref, diagonal(part - 1))
            start += 8 * 27
            sums_ref[start : start + 8] = fold(two_ref, diagonal(1 - part))
    sums_out[...] = sums_ref[...].astype(BF16).reshape(sums_out.shape)


def unpacked(tile):
    pieces = [tile] + [pltpu.roll(tile, 128 - q * CHANNELS, 1) for q in range(1, 4)]
    return jnp.concatenate(pieces, axis=0)[:, :CHANNELS]


def sum_kernel(scale, parts_ref, out_ref):
    total = jnp.sum(parts_ref[...].astype(F32), axis=0) * scale
    per = parts_ref.shape[1] // 8
    device = lax.axis_index("space") * lax.axis_size("dp") + lax.axis_index("dp")
    tiles = []
    for j in range(per):
        tile = total[8 * j : 8 * j + 8]
        block = jnp.transpose(unpacked(tile))
        turned = jnp.concatenate([block[8 * q : 8 * q + 8] for q in range(4)], axis=1)
        tiles.append(jnp.where(device * per + j < 27, turned, tile))
    total = jnp.concatenate(tiles, axis=0)
    out_ref[...] = jnp.broadcast_to(total.astype(BF16)[None], out_ref.shape)


def unpack_kernel(sums_ref, one_out, two_out, rows_ref):
    rows_ref[...] = sums_ref[...].astype(F32).reshape(rows_ref.shape)
    for index in range(BLOCKS):
        block = rows_ref[8 * index : 8 * index + 8]
        out = one_out if index < 27 else two_out
        for q in range(4):
            moved = pltpu.roll(block, 128 - q * CHANNELS, 1) if q else block
            out[index % 27, 8 * q : 8 * q + 8, :] = moved[:, :CHANNELS]


def call(kernel, out_shape, scratch=(), smem=(), hbm=(), inputs=1, limit=24, cost=None):
    spaces = [pltpu.SMEM if i in smem else pl.ANY if i in hbm else pltpu.VMEM for i in range(inputs)]
    return pl.pallas_call(
        kernel,
        out_shape=out_shape,
        in_specs=[pl.BlockSpec(memory_space=space) for space in spaces],
        out_specs=jax.tree.map(lambda _: pl.BlockSpec(memory_space=pltpu.VMEM), out_shape),
        scratch_shapes=list(scratch),
        compiler_params=pltpu.CompilerParams(vmem_limit_bytes=limit * 2**20),
        cost_estimate=cost,
    )


def shape(*dims, dtype=BF16):
    return jax.ShapeDtypeStruct(dims, dtype)


def swapped(value, first):
    pairs = [(i, i + 1) for i in range(first, lax.axis_size("space") - 1, 2)]
    return lax.ppermute(value, "space", pairs + [(target, source) for source, target in pairs])


def body(coarse_latents, active_blocks, face_links, cotangent, up_weight, conv_one, conv_two):
    devices = lax.axis_size("space")
    everyone = devices * lax.axis_size("dp")
    held, width = coarse_latents.shape[1:]
    bricks = active_blocks.shape[1]
    tiles = width // 128
    packed = call(
        functools.partial(pick_kernel, devices),
        shape(devices, 3 * BRICKS * tiles, 128),
        [
            pltpu.VMEM((1, bricks), jnp.int32),
            pltpu.VMEM((1, held, width), BF16),
            pltpu.VMEM(((bricks + 16) * tiles, 128), F32),
            pltpu.SemaphoreType.DMA((2,)),
        ],
        hbm=(0, 1),
        inputs=2,
        limit=60,
    )(active_blocks, coarse_latents)
    received = lax.all_to_all(packed, "space", split_axis=0, concat_axis=0, tiled=True)
    band = shape(9, WIDE, HALF)
    cost = pl.CostEstimate(flops=10**9, bytes_accessed=2 * 10**6, transcendentals=0)
    band_one = call(band_kernel, band, cost=cost)(conv_one)
    band_two, band_back = call(two_bands_kernel, (band, band), cost=cost)(conv_two)
    pad_shape = (3, BRICKS, EDGE + 2, 2 * EDGE, WIDE)
    pad = pltpu.VMEM(pad_shape, BF16)
    packed_faces = 2 * BRICKS * FACE
    pre, hidden, lifted_pad, high, low, far, near = call(
        first_kernel,
        (
            shape(ROWS, HALF, dtype=F32),
            shape(ROWS, HALF),
            shape(*pad_shape),
            shape(packed_faces, LINE),
            shape(packed_faces, LINE),
            shape(packed_faces, LINE),
            shape(packed_faces, LINE),
        ),
        [
            pltpu.VMEM((2, 8 * CUBE, 128), F32),
            pltpu.VMEM((2, 2 * LINES, 128), F32),
            pltpu.VMEM((packed_faces, LINE), F32),
            pltpu.VMEM((packed_faces, LINE), F32),
            pltpu.VMEM((8 * tiles, 128), F32),
        ],
        smem=(0,),
        inputs=5,
    )(face_links, received, up_weight, band_one, cotangent)
    far = swapped(far, 1)
    near = swapped(near, 0)
    per = -(-BLOCKS // everyone)
    per += per % 2
    fine, sums = call(
        second_kernel,
        (shape(*cotangent.shape), shape(everyone, per * 8, 128)),
        [
            pltpu.VMEM((2 * packed_faces, LINE), F32),
            pltpu.VMEM((2 * packed_faces, LINE), F32),
            pad,
            pad,
            pltpu.VMEM((HALF, WIDE), F32),
            pltpu.VMEM((HALF, WIDE), F32),
            pltpu.VMEM((everyone * per * 8, 128), F32),
        ],
        smem=(0,),
        inputs=11,
    )(
        face_links, cotangent, band_two, band_back, pre, hidden, lifted_pad,
        high, low, far, near,
    )
    axes = ("space", "dp")
    parts = lax.all_to_all(sums, axes, split_axis=0, concat_axis=0, tiled=True)
    scale = 1.0 / math.sqrt(lax.axis_size("dp") * devices * BRICKS * EDGE**3)
    total = call(functools.partial(sum_kernel, scale), shape(*sums.shape))(parts)
    gathered = lax.all_to_all(total, axes, split_axis=0, concat_axis=0, tiled=True)
    grads = shape(27, CHANNELS, CHANNELS, dtype=F32)
    rows = pltpu.VMEM((everyone * per * 8, 128), F32)
    grad_one, grad_two = call(unpack_kernel, (grads, grads), [rows])(gathered)
    return (fine, grad_one, grad_two)


def solution(mesh):
    return jax.shard_map(
        body,
        mesh=mesh,
        in_specs=(
            P("dp", "space", None),
            P("dp", None),
            P("dp", "space", None),
            P("dp", "space", None, None, None),
            P(),
            P(),
            P(),
        ),
        out_specs=(P("dp", "space", None, None, None), P(), P()),
        check_vma=False,
    )
```

```python
import functools
import math

import jax
import jax.numpy as jnp
from jax import lax
from jax.experimental import pallas as pl
from jax.experimental.pallas import tpu as pltpu
from jax.sharding import PartitionSpec as P

BF16 = jnp.bfloat16
F32 = jnp.float32
EDGE = 8
CHANNELS = 32
LINE = EDGE * CHANNELS
HALF = LINE // 2
WIDE = 2 * HALF
BRICKS = 2
CUBE = EDGE * EDGE
LINES = BRICKS * CUBE
ROWS = 2 * LINES
FACE = 3 * EDGE
BLOCKS = 54


def dot(left, right):
    return jnp.dot(left, right, preferred_element_type=F32)


def dot_rows(left, right):
    return lax.dot_general(left, right, (((0,), (0,)), ((), ())), preferred_element_type=F32)


def pair(halves_ref, start, count, stride=1):
    index = pl.ds(start, count, stride=stride) if stride > 1 else pl.ds(start, count)
    return halves_ref[0, index, :], halves_ref[1, index, :]


def lanes_of(shape):
    return lax.broadcasted_iota(jnp.int32, shape, len(shape) - 1)


def pick_kernel(devices, ids_hbm, latents_hbm, out_ref, ids_ref, latents_ref, rows_ref, sems):
    ids_copy = pltpu.make_async_copy(ids_hbm, ids_ref, sems.at[0])
    latents_copy = pltpu.make_async_copy(latents_hbm, latents_ref, sems.at[1])
    ids_copy.start()
    latents_copy.start()
    held, width = latents_ref.shape[1:]
    bricks = ids_ref.shape[1]
    margin = 8 * width // 128
    tiles = width // 128
    rows_ref[0:margin] = jnp.zeros((margin, 128), F32)
    rows_ref[margin + bricks * tiles :] = jnp.zeros((margin, 128), F32)
    first = lax.axis_index("space") * held
    rows = lax.broadcasted_iota(jnp.int32, (held, bricks), 0) + first
    ids_copy.wait()
    hot = jnp.where(rows == ids_ref[...], 1.0, 0.0).astype(BF16)
    latents_copy.wait()
    picked = dot_rows(hot, latents_ref[0])
    for tile in range(tiles):
        rows_ref[pl.ds(margin + tile, bricks, stride=tiles), :] = picked[:, tile * 128 : tile * 128 + 128]
    count = out_ref.shape[1]
    for receiver in range(devices):
        start = margin + BRICKS * (receiver - 1) * tiles
        out_ref[receiver] = rows_ref[start : start + count].astype(BF16)


def build_band(band_ref, rows):
    shape = (3 * CHANNELS, HALF)
    row = lax.broadcasted_iota(jnp.int32, shape, 0)
    target = CHANNELS - (row // CHANNELS) * CHANNELS + row % CHANNELS
    distance = lanes_of(shape) - target
    band_ref[:, HALF:, :] = jnp.zeros((9, HALF, HALF), BF16)
    for z in range(-1, 5):
        select = jnp.where(distance == z * CHANNELS, 1.0, 0.0).astype(BF16)
        block = dot(rows, select).astype(BF16)
        start = z % 8 * CHANNELS
        band_ref[:, start : start + CHANNELS, :] = block.reshape(9, CHANNELS, HALF)


def weight_rows(weights):
    cube = weights.reshape(9, 3, CHANNELS, CHANNELS)
    rows = jnp.concatenate([cube[:, 0], cube[:, 1], cube[:, 2]], axis=-1)
    return rows.reshape(9 * CHANNELS, 3 * CHANNELS).astype(BF16)


def flipped_rows(weights):
    cube = jnp.swapaxes(weights, 1, 2).reshape(9, 3, CHANNELS, CHANNELS)
    pieces = [jnp.concatenate([cube[8 - k, 2], cube[8 - k, 1], cube[8 - k, 0]], axis=-1) for k in range(9)]
    return jnp.concatenate(pieces, axis=0).astype(BF16)


def band_kernel(weights_ref, band_ref):
    build_band(band_ref, weight_rows(weights_ref[...].astype(F32)))


def bands_kernel(one_ref, two_ref, band_ref, back_ref):
    build_band(band_ref, weight_rows(one_ref[...].astype(F32)))
    build_band(back_ref, flipped_rows(two_ref[...].astype(F32)))


def put_padded(pad_ref, brick, lines, x_low, x_high, y_low, y_high, z_low, z_high):
    def joined(halves, before, after):
        lane = lanes_of(halves[0].shape)
        first = jnp.where(lane < CHANNELS, halves[1], before)
        second = jnp.where(lane >= HALF - CHANNELS, halves[0], after)
        return jnp.concatenate([halves[0], first], axis=-1), jnp.concatenate([halves[1], second], axis=-1)

    inside = joined(lines, z_low, z_high)
    x_low, x_high, y_low, y_high = [joined(face, 0.0, 0.0) for face in (x_low, x_high, y_low, y_high)]
    none = jnp.zeros((1, WIDE), F32)
    shifted = [[], [], []]
    for half in range(2):
        slabs = jnp.concatenate([x_low[half][None], inside[half], x_high[half][None]], axis=0)
        row = lax.broadcasted_iota(jnp.int32, slabs.shape, 1)
        low = jnp.concatenate([none, y_low[half], none], axis=0)[:, None, :]
        high = jnp.concatenate([none, y_high[half], none], axis=0)[:, None, :]
        shifted[0].append(jnp.where(row == 0, low, pltpu.roll(slabs, 1, 1)))
        shifted[1].append(slabs)
        shifted[2].append(jnp.where(row == EDGE - 1, high, pltpu.roll(slabs, EDGE - 1, 1)))
    for dy in range(3):
        pad_ref[dy, brick] = jnp.concatenate(shifted[dy], axis=1).astype(BF16)


def window(pad_ref, k):
    return pad_ref[k % 3, :, k // 3 : k // 3 + EDGE].reshape(ROWS, WIDE)


def convolve(pad_ref, band_ref):
    total = None
    for k in range(9):
        term = dot(window(pad_ref, k), band_ref[k])
        total = term if total is None else total + term
    return total


def half_lines(values):
    cube = values.reshape(BRICKS, EDGE, 2, EDGE, HALF)
    return [(cube[brick, :, 0], cube[brick, :, 1]) for brick in range(BRICKS)]


def put_halves(halves_ref, start, bricks):
    for brick, lines in enumerate(bricks):
        for half in range(2):
            first = start + brick * CUBE
            halves_ref[half, first : first + CUBE, :] = lines[half].reshape(CUBE, HALF)


def cotangent_lines(cotangent_ref):
    cube = cotangent_ref[...].astype(F32).reshape(BRICKS, EDGE, EDGE, LINE)
    return [(cube[brick, :, :, :HALF], cube[brick, :, :, HALF:]) for brick in range(BRICKS)]


def pack_faces(faces_ref, base, halves_ref, start, high):
    x_face = pair(halves_ref, start + ((EDGE - 1) * EDGE if high else 0), EDGE)
    y_face = pair(halves_ref, start + (EDGE - 1 if high else 0), EDGE, EDGE)
    for half in range(2):
        lanes = slice(half * HALF, half * HALF + HALF)
        faces_ref[base : base + EDGE, lanes] = x_face[half]
        faces_ref[base + EDGE : base + 2 * EDGE, lanes] = y_face[half]
    tile = halves_ref[1 if high else 0, start : start + CUBE, :]
    lane = lanes_of((16, 128)) // CHANNELS
    packed = jnp.zeros((16, 128), F32)
    for part in range(4):
        shift = (part + 1 if high else part) % 4 * CHANNELS
        piece = tile[part * 16 : part * 16 + 16]
        packed = jnp.where(lane == part, pltpu.roll(piece, shift, 1) if shift else piece, packed)
    faces_ref[base + 2 * EDGE : base + FACE, :128] = packed[:8]
    faces_ref[base + 2 * EDGE : base + FACE, 128:] = packed[8:]


def pack_all(bricks, halves_ref, faces_ref, high_out, low_out, far_out, near_out):
    put_halves(halves_ref, 0, bricks)
    packed = []
    for high in (True, False):
        for brick in range(BRICKS):
            pack_faces(faces_ref, brick * FACE, halves_ref, brick * CUBE, high)
        packed.append(faces_ref[...].astype(BF16))
    high, low = packed
    high_out[...] = high
    low_out[...] = low
    even = lax.axis_index("space") % 2 == 0
    far_out[...] = jnp.where(even, low, high)
    near_out[...] = jnp.where(even, high, low)


def faces_kernel(cotangent_ref, high_out, low_out, far_out, near_out, halves_ref, faces_ref):
    pack_all(cotangent_lines(cotangent_ref), halves_ref, faces_ref, high_out, low_out, far_out, near_out)


def unpack_depth(rows, high):
    packed = jnp.concatenate([rows[:, :128], rows[:, 128:]], axis=0)
    pieces = []
    for part in range(4):
        shift = ((3 - part) if high else (4 - part)) % 4 * CHANNELS
        pieces.append(pltpu.roll(packed, shift, 1) if shift else packed)
    return jnp.concatenate(pieces, axis=0).reshape(EDGE, EDGE, 128)


def first_kernel(
    links_ref, received_ref, up_ref, band_ref,
    pre_out, hidden_out, pad_out,
    volumes_ref, rows_ref,
):
    position = lax.axis_index("space")
    tiles = received_ref.shape[1] // (3 * BRICKS)
    rows_ref[0 : 3 * BRICKS * tiles] = jnp.sum(received_ref[...].astype(F32), axis=0)
    rows_ref[3 * BRICKS * tiles :] = jnp.zeros((2 * tiles, 128), F32)
    cells = []
    for tile in range(tiles):
        rows = rows_ref[pl.ds(tile, 8, stride=tiles), :]
        cells += [rows[:, :64], rows[:, 64:]]
    lifted = dot(jnp.concatenate(cells, axis=0).astype(BF16), up_ref[...])
    lifted = lifted.astype(BF16).astype(F32)
    for cell in range(8):
        a, b, c = cell // 4, cell // 2 % 2, cell % 2
        for sub in range(16):
            line = (4 * a + sub // 4) * EDGE + 4 * b + sub % 4
            volumes_ref[c, pl.ds(line, 8, stride=CUBE), :] = lifted[
                cell * 8 : cell * 8 + 8, sub * 128 : sub * 128 + 128
            ]
    for brick in range(BRICKS):

        def near(face):
            link = links_ref[0, brick, face]
            index = jnp.clip(link - BRICKS * (position - 1), 0, 3 * BRICKS - 1)
            return pl.multiple_of(index * CUBE, CUBE), jnp.where(link >= 0, 1.0, 0.0).astype(F32)

        def x_face(face):
            start, present = near(face)
            offset = EDGE * (EDGE - 1) if face % 2 == 0 else 0
            return [half * present for half in pair(volumes_ref, pl.multiple_of(start + offset, 8), EDGE)]

        def y_face(face):
            start, present = near(face)
            offset = EDGE - 1 if face % 2 == 0 else 0
            return [half * present for half in pair(volumes_ref, start + offset, EDGE, EDGE)]

        def z_face(face):
            start, present = near(face)
            tile = volumes_ref[1 if face % 2 == 0 else 0, pl.ds(start, CUBE), :] * present
            return tile.reshape(EDGE, EDGE, HALF)

        own = pair(volumes_ref, (BRICKS + brick) * CUBE, CUBE)
        own = [half.reshape(EDGE, EDGE, HALF) for half in own]
        put_padded(pad_out, brick, own, x_face(0), x_face(1), y_face(2), y_face(3), z_face(4), z_face(5))
    pre = convolve(pad_out, band_ref)
    hidden = pre / (1.0 + jnp.exp(-pre))
    hidden = hidden.astype(BF16)
    pre_out[...] = pre
    hidden_out[...] = hidden


def fold(outer_ref, places):
    lane = lanes_of((CHANNELS, 128)) // CHANNELS
    folded = None
    for block in range(4):
        start, tile = places[block]
        rows = outer_ref[start : start + CHANNELS, tile * 128 : tile * 128 + 128]
        folded = rows if folded is None else jnp.where(lane == block, rows, folded)
    quarter = [folded[8 * q : 8 * q + 8] for q in range(4)]
    small = lanes_of((8, 128)) // CHANNELS
    total = None
    for turn in range(4):
        mixed = quarter[0]
        for q in range(1, 4):
            mixed = jnp.where(small == (q + turn) % 4, quarter[q], mixed)
        if turn:
            mixed = pltpu.roll(mixed, 128 - turn * CHANNELS, 1)
        total = mixed if total is None else total + mixed
    return total


def diagonal(shift):
    places = [None] * 4
    for z in range(4):
        other = z + shift
        places[other % 4] = (z * CHANNELS, 0 if 0 <= other < 4 else 1)
    return places


def pad_all(pad_ref, bricks, links_ref, high_pool, low_pool, high_own, low_own, far, near):
    position = lax.axis_index("space")
    half = BRICKS * FACE
    even = position % 2 == 0
    high_pool[0:half] = jnp.where(even, far[...], near[...]).astype(F32)
    high_pool[half:] = high_own[...].astype(F32)
    low_pool[0:half] = low_own[...].astype(F32)
    low_pool[half:] = jnp.where(even, near[...], far[...]).astype(F32)
    for brick, lines in enumerate(bricks):

        def rows(face, axis):
            link = links_ref[0, brick, face]
            high = face % 2 == 0
            index = jnp.clip(link - BRICKS * (position - 1 if high else position), 0, 2 * BRICKS - 1)
            pool = high_pool if high else low_pool
            present = jnp.where(link >= 0, 1.0, 0.0).astype(F32)
            return pool[pl.ds(pl.multiple_of(index * FACE + axis * EDGE, 8), EDGE), :] * present

        def face(number, axis):
            found = rows(number, axis)
            return found[:, :HALF], found[:, HALF:]

        put_padded(
            pad_ref, brick, lines, face(0, 0), face(1, 0), face(2, 1), face(3, 1),
            unpack_depth(rows(4, 2), True), unpack_depth(rows(5, 2), False),
        )


def second_kernel(
    links_ref, cotangent_ref, band_ref, pre_ref, hidden_ref, lifted_pad, high_own, low_own, far, near,
    sums_out, lifted_out, high_out, low_out, far_out, near_out,
    high_pool, low_pool, cotangent_pad, one_ref, two_ref, sums_ref, halves_ref, faces_ref,
):
    hidden = hidden_ref[...].astype(F32)
    pack_all(half_lines(hidden), halves_ref, faces_ref, high_out, low_out, far_out, near_out)
    lifted_out[...] = window(lifted_pad, 4)[:, :HALF]
    pre = pre_ref[...]
    sigmoid = 1.0 / (1.0 + jnp.exp(-pre))
    slope = sigmoid * (1.0 + pre * (1.0 - sigmoid))
    hidden = jnp.transpose(hidden).astype(BF16)
    bricks = cotangent_lines(cotangent_ref)
    pad_all(cotangent_pad, bricks, links_ref, high_pool, low_pool, high_own, low_own, far, near)
    gradient = (convolve(cotangent_pad, band_ref) * slope).astype(BF16)
    gradient = jnp.transpose(gradient.astype(F32)).astype(BF16)
    sums_ref[8 * BLOCKS :] = jnp.zeros((sums_ref.shape[0] - 8 * BLOCKS, 128), F32)
    for k in range(9):
        one_ref[...] = dot(gradient, window(lifted_pad, k))
        two_ref[...] = dot(hidden, window(cotangent_pad, 8 - k))
        for part in range(3):
            start = 8 * (3 * k + part)
            sums_ref[start : start + 8] = fold(one_ref, diagonal(part - 1))
            start += 8 * 27
            sums_ref[start : start + 8] = fold(two_ref, diagonal(1 - part))
    sums_out[...] = sums_ref[...].astype(BF16).reshape(sums_out.shape)


def fine_kernel(
    links_ref, band_ref, lifted_ref, hidden_ref, high_own, low_own, far, near,
    fine_out, high_pool, low_pool, hidden_pad,
):
    bricks = half_lines(hidden_ref[...].astype(F32))
    pad_all(hidden_pad, bricks, links_ref, high_pool, low_pool, high_own, low_own, far, near)
    fine = lifted_ref[...].astype(F32) + convolve(hidden_pad, band_ref)
    fine = fine.reshape(LINES // EDGE, 2, EDGE, HALF)
    fine = jnp.concatenate([fine[:, 0], fine[:, 1]], axis=-1)
    fine_out[...] = fine.astype(BF16).reshape(fine_out.shape)


def unpacked(tile):
    pieces = [tile] + [pltpu.roll(tile, 128 - q * CHANNELS, 1) for q in range(1, 4)]
    return jnp.concatenate(pieces, axis=0)[:, :CHANNELS]


def sum_kernel(scale, parts_ref, _, out_ref):
    total = jnp.sum(parts_ref[...].astype(F32), axis=0) * scale
    per = parts_ref.shape[1] // 8
    device = lax.axis_index("space") * lax.axis_size("dp") + lax.axis_index("dp")
    tiles = []
    for j in range(per):
        tile = total[8 * j : 8 * j + 8]
        block = jnp.transpose(unpacked(tile))
        turned = jnp.concatenate([block[8 * q : 8 * q + 8] for q in range(4)], axis=1)
        tiles.append(jnp.where(device * per + j < 27, turned, tile))
    total = jnp.concatenate(tiles, axis=0)
    out_ref[...] = jnp.broadcast_to(total.astype(BF16)[None], out_ref.shape)


def unpack_kernel(sums_ref, one_out, two_out, rows_ref):
    rows_ref[...] = sums_ref[...].astype(F32).reshape(rows_ref.shape)
    for index in range(BLOCKS):
        block = rows_ref[8 * index : 8 * index + 8]
        out = one_out if index < 27 else two_out
        for q in range(4):
            moved = pltpu.roll(block, 128 - q * CHANNELS, 1) if q else block
            out[index % 27, 8 * q : 8 * q + 8, :] = moved[:, :CHANNELS]


def call(kernel, out_shape, scratch=(), smem=(), hbm=(), inputs=1, limit=24, cost=None):
    spaces = [pltpu.SMEM if i in smem else pl.ANY if i in hbm else pltpu.VMEM for i in range(inputs)]
    return pl.pallas_call(
        kernel,
        out_shape=out_shape,
        in_specs=[pl.BlockSpec(memory_space=space) for space in spaces],
        out_specs=jax.tree.map(lambda _: pl.BlockSpec(memory_space=pltpu.VMEM), out_shape),
        scratch_shapes=list(scratch),
        compiler_params=pltpu.CompilerParams(vmem_limit_bytes=limit * 2**20),
        cost_estimate=cost,
    )


def shape(*dims, dtype=BF16):
    return jax.ShapeDtypeStruct(dims, dtype)


def swapped(value, first):
    pairs = [(i, i + 1) for i in range(first, lax.axis_size("space") - 1, 2)]
    return lax.ppermute(value, "space", pairs + [(target, source) for source, target in pairs])


def body(coarse_latents, active_blocks, face_links, cotangent, up_weight, conv_one, conv_two):
    devices = lax.axis_size("space")
    everyone = devices * lax.axis_size("dp")
    held, width = coarse_latents.shape[1:]
    bricks = active_blocks.shape[1]
    tiles = width // 128
    packed = call(
        functools.partial(pick_kernel, devices),
        shape(devices, 3 * BRICKS * tiles, 128),
        [
            pltpu.VMEM((1, bricks), jnp.int32),
            pltpu.VMEM((1, held, width), BF16),
            pltpu.VMEM(((bricks + 16) * tiles, 128), F32),
            pltpu.SemaphoreType.DMA((2,)),
        ],
        hbm=(0, 1),
        inputs=2,
        limit=60,
    )(active_blocks, coarse_latents)
    received = lax.all_to_all(packed, "space", split_axis=0, concat_axis=0, tiled=True)
    band = shape(9, WIDE, HALF)
    cost = pl.CostEstimate(flops=10**9, bytes_accessed=2 * 10**6, transcendentals=0)
    face = shape(BRICKS * FACE, LINE)
    halves = pltpu.VMEM((2, LINES, HALF), F32)
    faces = pltpu.VMEM((BRICKS * FACE, LINE), F32)
    pool = pltpu.VMEM((2 * BRICKS * FACE, LINE), F32)
    volume = shape(ROWS, HALF)
    pad_shape = (3, BRICKS, EDGE + 2, 2 * EDGE, WIDE)
    pad = pltpu.VMEM(pad_shape, BF16)
    high, low, far, near = call(faces_kernel, (face,) * 4, [halves, faces])(cotangent)
    far = swapped(far, 1)
    near = swapped(near, 0)
    band_one, band_back = call(bands_kernel, (band, band), inputs=2, cost=cost)(conv_one, conv_two)
    pre, hidden, lifted_pad = call(
        first_kernel,
        (shape(ROWS, HALF, dtype=F32), volume, shape(*pad_shape)),
        [pltpu.VMEM((2, 8 * CUBE, 128), F32), pltpu.VMEM((8 * tiles, 128), F32)],
        smem=(0,),
        inputs=4,
    )(face_links, received, up_weight, band_one)
    per = -(-BLOCKS // everyone)
    per += per % 2
    product = pltpu.VMEM((HALF, WIDE), F32)
    sums, lifted, hidden_high, hidden_low, hidden_far, hidden_near = call(
        second_kernel,
        (shape(everyone, per * 8, 128), volume, face, face, face, face),
        [pool, pool, pad, product, product, pltpu.VMEM((everyone * per * 8, 128), F32), halves, faces],
        smem=(0,),
        inputs=10,
    )(face_links, cotangent, band_back, pre, hidden, lifted_pad, high, low, far, near)
    hidden_far = swapped(hidden_far, 1)
    hidden_near = swapped(hidden_near, 0)
    band_two = call(band_kernel, band, cost=cost)(conv_two)
    fine = call(fine_kernel, shape(*cotangent.shape), [pool, pool, pad], smem=(0,), inputs=8, cost=cost)(
        face_links, band_two, lifted, hidden, hidden_high, hidden_low, hidden_far, hidden_near
    )
    axes = ("space", "dp")
    parts = lax.all_to_all(sums, axes, split_axis=0, concat_axis=0, tiled=True)
    scale = 1.0 / math.sqrt(lax.axis_size("dp") * devices * BRICKS * EDGE**3)
    total = call(functools.partial(sum_kernel, scale), shape(*sums.shape), hbm=(1,), inputs=2)(parts, hidden_far)
    gathered = lax.all_to_all(total, axes, split_axis=0, concat_axis=0, tiled=True)
    grads = shape(27, CHANNELS, CHANNELS, dtype=F32)
    rows = pltpu.VMEM((everyone * per * 8, 128), F32)
    grad_one, grad_two = call(unpack_kernel, (grads, grads), [rows])(gathered)
    return (fine, grad_one, grad_two)


def solution(mesh):
    return jax.shard_map(
        body,
        mesh=mesh,
        in_specs=(
            P("dp", "space", None),
            P("dp", None),
            P("dp", "space", None),
            P("dp", "space", None, None, None),
            P(),
            P(),
            P(),
        ),
        out_specs=(P("dp", "space", None, None, None), P(), P()),
        check_vma=False,
    )
```

```python
import functools
import math

import jax
import jax.numpy as jnp
from jax import lax
from jax.experimental import pallas as pl
from jax.experimental.pallas import tpu as pltpu
from jax.sharding import PartitionSpec as P

BF16 = jnp.bfloat16
F32 = jnp.float32
EDGE = 8
CHANNELS = 32
LINE = EDGE * CHANNELS
HALF = LINE // 2
WIDE = 2 * HALF
BRICKS = 2
CUBE = EDGE * EDGE
LINES = BRICKS * CUBE
BAND = (9, WIDE, HALF)
ROWS = 2 * LINES
FACE = 3 * EDGE
BLOCKS = 54


def dot(left, right):
    return jnp.dot(left, right, preferred_element_type=F32)


def dot_rows(left, right):
    return lax.dot_general(left, right, (((0,), (0,)), ((), ())), preferred_element_type=F32)


def pair(halves_ref, start, count, stride=1):
    index = pl.ds(start, count, stride=stride) if stride > 1 else pl.ds(start, count)
    return halves_ref[0, index, :], halves_ref[1, index, :]


def lanes_of(shape):
    return lax.broadcasted_iota(jnp.int32, shape, len(shape) - 1)


def pick_kernel(devices, ids_hbm, latents_hbm, out_ref, ids_ref, latents_ref, rows_ref, sems):
    ids_copy = pltpu.make_async_copy(ids_hbm, ids_ref, sems.at[0])
    latents_copy = pltpu.make_async_copy(latents_hbm, latents_ref, sems.at[1])
    ids_copy.start()
    latents_copy.start()
    held, width = latents_ref.shape[1:]
    bricks = ids_ref.shape[1]
    margin = 8 * width // 128
    tiles = width // 128
    rows_ref[0:margin] = jnp.zeros((margin, 128), F32)
    rows_ref[margin + bricks * tiles :] = jnp.zeros((margin, 128), F32)
    first = lax.axis_index("space") * held
    rows = lax.broadcasted_iota(jnp.int32, (held, bricks), 0) + first
    ids_copy.wait()
    hot = jnp.where(rows == ids_ref[...], 1.0, 0.0).astype(BF16)
    latents_copy.wait()
    picked = dot_rows(hot, latents_ref[0])
    for tile in range(tiles):
        rows_ref[pl.ds(margin + tile, bricks, stride=tiles), :] = picked[:, tile * 128 : tile * 128 + 128]
    count = out_ref.shape[1]
    for receiver in range(devices):
        start = margin + BRICKS * (receiver - 1) * tiles
        out_ref[receiver] = rows_ref[start : start + count].astype(BF16)


def build_band(band_ref, rows):
    shape = (3 * CHANNELS, HALF)
    row = lax.broadcasted_iota(jnp.int32, shape, 0)
    target = CHANNELS - (row // CHANNELS) * CHANNELS + row % CHANNELS
    distance = lanes_of(shape) - target
    band_ref[:, HALF:, :] = jnp.zeros((9, HALF, HALF), BF16)
    for z in range(-1, 5):
        select = jnp.where(distance == z * CHANNELS, 1.0, 0.0).astype(BF16)
        block = dot(rows, select).astype(BF16)
        start = z % 8 * CHANNELS
        band_ref[:, start : start + CHANNELS, :] = block.reshape(9, CHANNELS, HALF)


def weight_rows(weights):
    cube = weights.reshape(9, 3, CHANNELS, CHANNELS)
    rows = jnp.concatenate([cube[:, 0], cube[:, 1], cube[:, 2]], axis=-1)
    return rows.reshape(9 * CHANNELS, 3 * CHANNELS).astype(BF16)


def flipped_rows(weights):
    cube = jnp.swapaxes(weights, 1, 2).reshape(9, 3, CHANNELS, CHANNELS)
    pieces = [jnp.concatenate([cube[8 - k, 2], cube[8 - k, 1], cube[8 - k, 0]], axis=-1) for k in range(9)]
    return jnp.concatenate(pieces, axis=0).astype(BF16)


def band_kernel(weights_ref, band_ref):
    build_band(band_ref, weight_rows(weights_ref[...].astype(F32)))


def put_padded(pad_ref, brick, lines, x_low, x_high, y_low, y_high, z_low, z_high):
    def joined(halves, before, after):
        lane = lanes_of(halves[0].shape)
        first = jnp.where(lane < CHANNELS, halves[1], before)
        second = jnp.where(lane >= HALF - CHANNELS, halves[0], after)
        return jnp.concatenate([halves[0], first], axis=-1), jnp.concatenate([halves[1], second], axis=-1)

    inside = joined(lines, z_low, z_high)
    x_low, x_high, y_low, y_high = [joined(face, 0.0, 0.0) for face in (x_low, x_high, y_low, y_high)]
    none = jnp.zeros((1, WIDE), F32)
    shifted = [[], [], []]
    for half in range(2):
        slabs = jnp.concatenate([x_low[half][None], inside[half], x_high[half][None]], axis=0)
        row = lax.broadcasted_iota(jnp.int32, slabs.shape, 1)
        low = jnp.concatenate([none, y_low[half], none], axis=0)[:, None, :]
        high = jnp.concatenate([none, y_high[half], none], axis=0)[:, None, :]
        shifted[0].append(jnp.where(row == 0, low, pltpu.roll(slabs, 1, 1)))
        shifted[1].append(slabs)
        shifted[2].append(jnp.where(row == EDGE - 1, high, pltpu.roll(slabs, EDGE - 1, 1)))
    for dy in range(3):
        pad_ref[dy, brick] = jnp.concatenate(shifted[dy], axis=1).astype(BF16)


def window(pad_ref, k):
    return pad_ref[k % 3, :, k // 3 : k // 3 + EDGE].reshape(ROWS, WIDE)


def convolve(pad_ref, band_ref):
    total = None
    for k in range(9):
        term = dot(window(pad_ref, k), band_ref[k])
        total = term if total is None else total + term
    return total


def half_lines(values):
    cube = values.reshape(BRICKS, EDGE, 2, EDGE, HALF)
    return [(cube[brick, :, 0], cube[brick, :, 1]) for brick in range(BRICKS)]


def put_halves(halves_ref, start, bricks):
    for brick, lines in enumerate(bricks):
        for half in range(2):
            first = start + brick * CUBE
            halves_ref[half, first : first + CUBE, :] = lines[half].reshape(CUBE, HALF)


def cotangent_lines(cotangent_ref):
    cube = cotangent_ref[...].astype(F32).reshape(BRICKS, EDGE, EDGE, LINE)
    return [(cube[brick, :, :, :HALF], cube[brick, :, :, HALF:]) for brick in range(BRICKS)]


def pack_faces(faces_ref, base, halves_ref, start, high):
    x_face = pair(halves_ref, start + ((EDGE - 1) * EDGE if high else 0), EDGE)
    y_face = pair(halves_ref, start + (EDGE - 1 if high else 0), EDGE, EDGE)
    for half in range(2):
        lanes = slice(half * HALF, half * HALF + HALF)
        faces_ref[base : base + EDGE, lanes] = x_face[half]
        faces_ref[base + EDGE : base + 2 * EDGE, lanes] = y_face[half]
    tile = halves_ref[1 if high else 0, start : start + CUBE, :]
    lane = lanes_of((16, 128)) // CHANNELS
    packed = jnp.zeros((16, 128), F32)
    for part in range(4):
        shift = (part + 1 if high else part) % 4 * CHANNELS
        piece = tile[part * 16 : part * 16 + 16]
        packed = jnp.where(lane == part, pltpu.roll(piece, shift, 1) if shift else piece, packed)
    faces_ref[base + 2 * EDGE : base + FACE, :128] = packed[:8]
    faces_ref[base + 2 * EDGE : base + FACE, 128:] = packed[8:]


def pack_all(bricks, halves_ref, faces_ref, high_out, low_out, far_out, near_out):
    put_halves(halves_ref, 0, bricks)
    packed = []
    for high in (True, False):
        for brick in range(BRICKS):
            pack_faces(faces_ref, brick * FACE, halves_ref, brick * CUBE, high)
        packed.append(faces_ref[...].astype(BF16))
    high, low = packed
    high_out[...] = high
    low_out[...] = low
    even = lax.axis_index("space") % 2 == 0
    far_out[...] = jnp.where(even, low, high)
    near_out[...] = jnp.where(even, high, low)


def faces_kernel(cotangent_ref, high_out, low_out, far_out, near_out, halves_ref, faces_ref):
    pack_all(cotangent_lines(cotangent_ref), halves_ref, faces_ref, high_out, low_out, far_out, near_out)


def unpack_depth(rows, high):
    packed = jnp.concatenate([rows[:, :128], rows[:, 128:]], axis=0)
    pieces = []
    for part in range(4):
        shift = ((3 - part) if high else (4 - part)) % 4 * CHANNELS
        pieces.append(pltpu.roll(packed, shift, 1) if shift else packed)
    return jnp.concatenate(pieces, axis=0).reshape(EDGE, EDGE, 128)


def first_kernel(
    links_in, received_ref, up_ref, band_ref,
    pre_out, hidden_out, pad_out,
    volumes_ref, rows_ref, links_ref, links_sem,
):
    links_copy = pltpu.make_async_copy(links_in, links_ref, links_sem)
    links_copy.start()
    position = lax.axis_index("space")
    tiles = received_ref.shape[1] // (3 * BRICKS)
    rows_ref[0 : 3 * BRICKS * tiles] = jnp.sum(received_ref[...].astype(F32), axis=0)
    rows_ref[3 * BRICKS * tiles :] = jnp.zeros((2 * tiles, 128), F32)
    cells = []
    for tile in range(tiles):
        rows = rows_ref[pl.ds(tile, 8, stride=tiles), :]
        cells += [rows[:, :64], rows[:, 64:]]
    lifted = dot(jnp.concatenate(cells, axis=0).astype(BF16), up_ref[...])
    lifted = lifted.astype(BF16).astype(F32)
    for cell in range(8):
        a, b, c = cell // 4, cell // 2 % 2, cell % 2
        for sub in range(16):
            line = (4 * a + sub // 4) * EDGE + 4 * b + sub % 4
            volumes_ref[c, pl.ds(line, 8, stride=CUBE), :] = lifted[
                cell * 8 : cell * 8 + 8, sub * 128 : sub * 128 + 128
            ]
    links_copy.wait()
    for brick in range(BRICKS):

        def near(face):
            link = links_ref[0, brick, face]
            index = jnp.clip(link - BRICKS * (position - 1), 0, 3 * BRICKS - 1)
            return pl.multiple_of(index * CUBE, CUBE), jnp.where(link >= 0, 1.0, 0.0).astype(F32)

        def x_face(face):
            start, present = near(face)
            offset = EDGE * (EDGE - 1) if face % 2 == 0 else 0
            return [half * present for half in pair(volumes_ref, pl.multiple_of(start + offset, 8), EDGE)]

        def y_face(face):
            start, present = near(face)
            offset = EDGE - 1 if face % 2 == 0 else 0
            return [half * present for half in pair(volumes_ref, start + offset, EDGE, EDGE)]

        def z_face(face):
            start, present = near(face)
            tile = volumes_ref[1 if face % 2 == 0 else 0, pl.ds(start, CUBE), :] * present
            return tile.reshape(EDGE, EDGE, HALF)

        own = pair(volumes_ref, (BRICKS + brick) * CUBE, CUBE)
        own = [half.reshape(EDGE, EDGE, HALF) for half in own]
        put_padded(pad_out, brick, own, x_face(0), x_face(1), y_face(2), y_face(3), z_face(4), z_face(5))
    pre = convolve(pad_out, band_ref)
    hidden = pre / (1.0 + jnp.exp(-pre))
    hidden = hidden.astype(BF16)
    pre_out[...] = pre
    hidden_out[...] = hidden


def fold(outer_ref, places):
    lane = lanes_of((CHANNELS, 128)) // CHANNELS
    folded = None
    for block in range(4):
        start, tile = places[block]
        rows = outer_ref[start : start + CHANNELS, tile * 128 : tile * 128 + 128]
        folded = rows if folded is None else jnp.where(lane == block, rows, folded)
    quarter = [folded[8 * q : 8 * q + 8] for q in range(4)]
    small = lanes_of((8, 128)) // CHANNELS
    total = None
    for turn in range(4):
        mixed = quarter[0]
        for q in range(1, 4):
            mixed = jnp.where(small == (q + turn) % 4, quarter[q], mixed)
        if turn:
            mixed = pltpu.roll(mixed, 128 - turn * CHANNELS, 1)
        total = mixed if total is None else total + mixed
    return total


def diagonal(shift):
    places = [None] * 4
    for z in range(4):
        other = z + shift
        places[other % 4] = (z * CHANNELS, 0 if 0 <= other < 4 else 1)
    return places


def pad_all(pad_ref, bricks, links_ref, high_pool, low_pool, high_own, low_own, far, near):
    position = lax.axis_index("space")
    half = BRICKS * FACE
    even = position % 2 == 0
    high_pool[0:half] = jnp.where(even, far[...], near[...]).astype(F32)
    high_pool[half:] = high_own[...].astype(F32)
    low_pool[0:half] = low_own[...].astype(F32)
    low_pool[half:] = jnp.where(even, near[...], far[...]).astype(F32)
    for brick, lines in enumerate(bricks):

        def rows(face, axis):
            link = links_ref[0, brick, face]
            high = face % 2 == 0
            index = jnp.clip(link - BRICKS * (position - 1 if high else position), 0, 2 * BRICKS - 1)
            pool = high_pool if high else low_pool
            present = jnp.where(link >= 0, 1.0, 0.0).astype(F32)
            return pool[pl.ds(pl.multiple_of(index * FACE + axis * EDGE, 8), EDGE), :] * present

        def face(number, axis):
            found = rows(number, axis)
            return found[:, :HALF], found[:, HALF:]

        put_padded(
            pad_ref, brick, lines, face(0, 0), face(1, 0), face(2, 1), face(3, 1),
            unpack_depth(rows(4, 2), True), unpack_depth(rows(5, 2), False),
        )


def second_kernel(
    links_in, cotangent_ref, weights_ref, pre_ref, hidden_ref, lifted_pad, high_own, low_own, far, near,
    sums_out, lifted_out, high_out, low_out, far_out, near_out,
    high_pool, low_pool, cotangent_pad, one_ref, two_ref, sums_ref, halves_ref, faces_ref, band_ref,
    links_ref, links_sem,
):
    links_copy = pltpu.make_async_copy(links_in, links_ref, links_sem)
    links_copy.start()
    build_band(band_ref, flipped_rows(weights_ref[...].astype(F32)))
    hidden = hidden_ref[...].astype(F32)
    pack_all(half_lines(hidden), halves_ref, faces_ref, high_out, low_out, far_out, near_out)
    lifted_out[...] = window(lifted_pad, 4)[:, :HALF]
    pre = pre_ref[...]
    sigmoid = 1.0 / (1.0 + jnp.exp(-pre))
    slope = sigmoid * (1.0 + pre * (1.0 - sigmoid))
    hidden = jnp.transpose(hidden).astype(BF16)
    bricks = cotangent_lines(cotangent_ref)
    links_copy.wait()
    pad_all(cotangent_pad, bricks, links_ref, high_pool, low_pool, high_own, low_own, far, near)
    gradient = (convolve(cotangent_pad, band_ref) * slope).astype(BF16)
    gradient = jnp.transpose(gradient.astype(F32)).astype(BF16)
    sums_ref[8 * BLOCKS :] = jnp.zeros((sums_ref.shape[0] - 8 * BLOCKS, 128), F32)
    for k in range(9):
        one_ref[...] = dot(gradient, window(lifted_pad, k))
        two_ref[...] = dot(hidden, window(cotangent_pad, 8 - k))
        for part in range(3):
            start = 8 * (3 * k + part)
            sums_ref[start : start + 8] = fold(one_ref, diagonal(part - 1))
            start += 8 * 27
            sums_ref[start : start + 8] = fold(two_ref, diagonal(1 - part))
    sums_out[...] = sums_ref[...].astype(BF16).reshape(sums_out.shape)


def fine_kernel(
    links_in, weights_ref, lifted_ref, hidden_ref, high_own, low_own, far, near,
    fine_out, high_pool, low_pool, hidden_pad, band_ref, links_ref, links_sem,
):
    links_copy = pltpu.make_async_copy(links_in, links_ref, links_sem)
    links_copy.start()
    build_band(band_ref, weight_rows(weights_ref[...].astype(F32)))
    links_copy.wait()
    bricks = half_lines(hidden_ref[...].astype(F32))
    pad_all(hidden_pad, bricks, links_ref, high_pool, low_pool, high_own, low_own, far, near)
    fine = lifted_ref[...].astype(F32) + convolve(hidden_pad, band_ref)
    fine = fine.reshape(LINES // EDGE, 2, EDGE, HALF)
    fine = jnp.concatenate([fine[:, 0], fine[:, 1]], axis=-1)
    fine_out[...] = fine.astype(BF16).reshape(fine_out.shape)


def unpacked(tile):
    pieces = [tile] + [pltpu.roll(tile, 128 - q * CHANNELS, 1) for q in range(1, 4)]
    return jnp.concatenate(pieces, axis=0)[:, :CHANNELS]


def sum_kernel(scale, parts_ref, _far, _near, out_ref):
    total = jnp.sum(parts_ref[...].astype(F32), axis=0) * scale
    per = parts_ref.shape[1] // 8
    device = lax.axis_index("space") * lax.axis_size("dp") + lax.axis_index("dp")
    tiles = []
    for j in range(per):
        tile = total[8 * j : 8 * j + 8]
        block = jnp.transpose(unpacked(tile))
        turned = jnp.concatenate([block[8 * q : 8 * q + 8] for q in range(4)], axis=1)
        tiles.append(jnp.where(device * per + j < 27, turned, tile))
    total = jnp.concatenate(tiles, axis=0)
    out_ref[...] = jnp.broadcast_to(total.astype(BF16)[None], out_ref.shape)


def unpack_kernel(sums_ref, one_out, two_out, rows_ref, one_ref, two_ref, sems):
    rows_ref[...] = sums_ref[...].astype(F32).reshape(rows_ref.shape)
    copies = []
    for which, (block_ref, out) in enumerate(((one_ref, one_out), (two_ref, two_out))):
        for third in range(3):
            first = 9 * third
            for index in range(first, first + 9):
                row = 8 * (27 * which + index)
                block_ref[index] = unpacked(rows_ref[row : row + 8])
            part = pl.ds(first, 9)
            copies.append(pltpu.make_async_copy(block_ref.at[part], out.at[part], sems.at[which, third]))
            copies[-1].start()
    for copy in copies:
        copy.wait()


def call(kernel, out_shape, scratch=(), hbm=(), inputs=1, limit=24, cost=None, out=pltpu.VMEM):
    spaces = [pl.ANY if i in hbm else pltpu.VMEM for i in range(inputs)]
    return pl.pallas_call(
        kernel,
        out_shape=out_shape,
        in_specs=[pl.BlockSpec(memory_space=space) for space in spaces],
        out_specs=jax.tree.map(lambda _: pl.BlockSpec(memory_space=out), out_shape),
        scratch_shapes=list(scratch),
        compiler_params=pltpu.CompilerParams(vmem_limit_bytes=limit * 2**20),
        cost_estimate=cost,
    )


def shape(*dims, dtype=BF16):
    return jax.ShapeDtypeStruct(dims, dtype)


def swapped(value, first):
    pairs = [(i, i + 1) for i in range(first, lax.axis_size("space") - 1, 2)]
    return lax.ppermute(value, "space", pairs + [(target, source) for source, target in pairs])


def body(coarse_latents, active_blocks, face_links, cotangent, up_weight, conv_one, conv_two):
    devices = lax.axis_size("space")
    everyone = devices * lax.axis_size("dp")
    held, width = coarse_latents.shape[1:]
    bricks = active_blocks.shape[1]
    tiles = width // 128
    packed = call(
        functools.partial(pick_kernel, devices),
        shape(devices, 3 * BRICKS * tiles, 128),
        [
            pltpu.VMEM((1, bricks), jnp.int32),
            pltpu.VMEM((1, held, width), BF16),
            pltpu.VMEM(((bricks + 16) * tiles, 128), F32),
            pltpu.SemaphoreType.DMA((2,)),
        ],
        hbm=(0, 1),
        inputs=2,
        limit=60,
    )(active_blocks, coarse_latents)
    received = lax.all_to_all(packed, "space", split_axis=0, concat_axis=0, tiled=True)
    band = pltpu.VMEM(BAND, BF16)
    cost = pl.CostEstimate(flops=10**9, bytes_accessed=2 * 10**6, transcendentals=0)
    face = shape(BRICKS * FACE, LINE)
    halves = pltpu.VMEM((2, LINES, HALF), F32)
    faces = pltpu.VMEM((BRICKS * FACE, LINE), F32)
    pool = pltpu.VMEM((2 * BRICKS * FACE, LINE), F32)
    volume = shape(ROWS, HALF)
    links = [pltpu.SMEM(face_links.shape, jnp.int32), pltpu.SemaphoreType.DMA]
    pad_shape = (3, BRICKS, EDGE + 2, 2 * EDGE, WIDE)
    pad = pltpu.VMEM(pad_shape, BF16)
    high, low, far, near = call(faces_kernel, (face,) * 4, [halves, faces])(cotangent)
    far = swapped(far, 1)
    near = swapped(near, 0)
    band_one = call(band_kernel, shape(*BAND), cost=cost)(conv_one)
    pre, hidden, lifted_pad = call(
        first_kernel,
        (shape(ROWS, HALF, dtype=F32), volume, shape(*pad_shape)),
        [pltpu.VMEM((2, 8 * CUBE, 128), F32), pltpu.VMEM((8 * tiles, 128), F32), *links],
        hbm=(0,),
        inputs=4,
    )(face_links, received, up_weight, band_one)
    per = -(-BLOCKS // everyone)
    per += per % 2
    product = pltpu.VMEM((HALF, WIDE), F32)
    sums, lifted, hidden_high, hidden_low, hidden_far, hidden_near = call(
        second_kernel,
        (shape(everyone, per * 8, 128), volume, face, face, face, face),
        [pool, pool, pad, product, product, pltpu.VMEM((everyone * per * 8, 128), F32), halves, faces, band, *links],
        hbm=(0,),
        inputs=10,
    )(face_links, cotangent, conv_two, pre, hidden, lifted_pad, high, low, far, near)
    hidden_far = swapped(hidden_far, 1)
    hidden_near = swapped(hidden_near, 0)
    fine = call(fine_kernel, shape(*cotangent.shape), [pool, pool, pad, band, *links], hbm=(0,), inputs=8, cost=cost)(
        face_links, conv_two, lifted, hidden, hidden_high, hidden_low, hidden_far, hidden_near
    )
    axes = ("space", "dp")
    parts = lax.all_to_all(sums, axes, split_axis=0, concat_axis=0, tiled=True)
    scale = 1.0 / math.sqrt(lax.axis_size("dp") * devices * BRICKS * EDGE**3)
    total = call(functools.partial(sum_kernel, scale), shape(*sums.shape), hbm=(1, 2), inputs=3)(
        parts, hidden_far, hidden_near
    )
    gathered = lax.all_to_all(total, axes, split_axis=0, concat_axis=0, tiled=True)
    grads = shape(27, CHANNELS, CHANNELS, dtype=F32)
    block = pltpu.VMEM(grads.shape, F32)
    scratch = [pltpu.VMEM((everyone * per * 8, 128), F32), block, block, pltpu.SemaphoreType.DMA((2, 3))]
    grad_one, grad_two = call(unpack_kernel, (grads, grads), scratch, out=pl.ANY)(gathered)
    return (fine, grad_one, grad_two)


def solution(mesh):
    return jax.shard_map(
        body,
        mesh=mesh,
        in_specs=(
            P("dp", "space", None),
            P("dp", None),
            P("dp", "space", None),
            P("dp", "space", None, None, None),
            P(),
            P(),
            P(),
        ),
        out_specs=(P("dp", "space", None, None, None), P(), P()),
        check_vma=False,
    )
```

```python
import functools
import math

import jax
import jax.numpy as jnp
from jax import lax
from jax.experimental import pallas as pl
from jax.experimental.pallas import tpu as pltpu
from jax.sharding import PartitionSpec as P

BF16 = jnp.bfloat16
F32 = jnp.float32
EDGE = 8
CHANNELS = 32
LINE = EDGE * CHANNELS
HALF = LINE // 2
WIDE = 2 * HALF
BRICKS = 2
CUBE = EDGE * EDGE
LINES = BRICKS * CUBE
BAND = (9, WIDE, HALF)
ROWS = 2 * LINES
FACE = 3 * EDGE
BLOCKS = 54


def dot(left, right):
    return jnp.dot(left, right, preferred_element_type=F32)


def dot_rows(left, right):
    return lax.dot_general(left, right, (((0,), (0,)), ((), ())), preferred_element_type=F32)


def pair(halves_ref, start, count, stride=1):
    index = pl.ds(start, count, stride=stride) if stride > 1 else pl.ds(start, count)
    return halves_ref[0, index, :], halves_ref[1, index, :]


def lanes_of(shape):
    return lax.broadcasted_iota(jnp.int32, shape, len(shape) - 1)


def pick_kernel(devices, ids_hbm, latents_hbm, out_ref, ids_ref, latents_ref, rows_ref, sems):
    ids_copy = pltpu.make_async_copy(ids_hbm, ids_ref, sems.at[0])
    latents_copy = pltpu.make_async_copy(latents_hbm, latents_ref, sems.at[1])
    ids_copy.start()
    latents_copy.start()
    held, width = latents_ref.shape[1:]
    bricks = ids_ref.shape[1]
    margin = 8 * width // 128
    tiles = width // 128
    rows_ref[0:margin] = jnp.zeros((margin, 128), F32)
    rows_ref[margin + bricks * tiles :] = jnp.zeros((margin, 128), F32)
    first = lax.axis_index("space") * held
    rows = lax.broadcasted_iota(jnp.int32, (held, bricks), 0) + first
    ids_copy.wait()
    hot = jnp.where(rows == ids_ref[...], 1.0, 0.0).astype(BF16)
    latents_copy.wait()
    picked = dot_rows(hot, latents_ref[0])
    for tile in range(tiles):
        rows_ref[pl.ds(margin + tile, bricks, stride=tiles), :] = picked[:, tile * 128 : tile * 128 + 128]
    count = out_ref.shape[1]
    for receiver in range(devices):
        start = margin + BRICKS * (receiver - 1) * tiles
        out_ref[receiver] = rows_ref[start : start + count].astype(BF16)


def build_band(band_ref, rows):
    shape = (3 * CHANNELS, HALF)
    row = lax.broadcasted_iota(jnp.int32, shape, 0)
    target = CHANNELS - (row // CHANNELS) * CHANNELS + row % CHANNELS
    distance = lanes_of(shape) - target
    band_ref[:, HALF:, :] = jnp.zeros((9, HALF, HALF), BF16)
    for z in range(-1, 5):
        select = jnp.where(distance == z * CHANNELS, 1.0, 0.0).astype(BF16)
        block = dot(rows, select).astype(BF16)
        start = z % 8 * CHANNELS
        band_ref[:, start : start + CHANNELS, :] = block.reshape(9, CHANNELS, HALF)


def weight_rows(weights):
    cube = weights.reshape(9, 3, CHANNELS, CHANNELS)
    rows = jnp.concatenate([cube[:, 0], cube[:, 1], cube[:, 2]], axis=-1)
    return rows.reshape(9 * CHANNELS, 3 * CHANNELS).astype(BF16)


def flipped_rows(weights):
    cube = jnp.swapaxes(weights, 1, 2).reshape(9, 3, CHANNELS, CHANNELS)
    pieces = [jnp.concatenate([cube[8 - k, 2], cube[8 - k, 1], cube[8 - k, 0]], axis=-1) for k in range(9)]
    return jnp.concatenate(pieces, axis=0).astype(BF16)


def band_kernel(weights_ref, band_ref):
    build_band(band_ref, weight_rows(weights_ref[...].astype(F32)))


def put_padded(pad_ref, brick, lines, x_low, x_high, y_low, y_high, z_low, z_high):
    def joined(halves, before, after):
        lane = lanes_of(halves[0].shape)
        first = jnp.where(lane < CHANNELS, halves[1], before)
        second = jnp.where(lane >= HALF - CHANNELS, halves[0], after)
        return jnp.concatenate([halves[0], first], axis=-1), jnp.concatenate([halves[1], second], axis=-1)

    inside = joined(lines, z_low, z_high)
    x_low, x_high, y_low, y_high = [joined(face, 0.0, 0.0) for face in (x_low, x_high, y_low, y_high)]
    none = jnp.zeros((1, WIDE), F32)
    shifted = [[], [], []]
    for half in range(2):
        slabs = jnp.concatenate([x_low[half][None], inside[half], x_high[half][None]], axis=0)
        row = lax.broadcasted_iota(jnp.int32, slabs.shape, 1)
        low = jnp.concatenate([none, y_low[half], none], axis=0)[:, None, :]
        high = jnp.concatenate([none, y_high[half], none], axis=0)[:, None, :]
        shifted[0].append(jnp.where(row == 0, low, pltpu.roll(slabs, 1, 1)))
        shifted[1].append(slabs)
        shifted[2].append(jnp.where(row == EDGE - 1, high, pltpu.roll(slabs, EDGE - 1, 1)))
    for dy in range(3):
        pad_ref[dy, brick] = jnp.concatenate(shifted[dy], axis=1).astype(BF16)


def window(pad_ref, k):
    return pad_ref[k % 3, :, k // 3 : k // 3 + EDGE].reshape(ROWS, WIDE)


def convolve(pad_ref, band_ref):
    total = None
    for k in range(9):
        term = dot(window(pad_ref, k), band_ref[k])
        total = term if total is None else total + term
    return total


def half_lines(values):
    cube = values.reshape(BRICKS, EDGE, 2, EDGE, HALF)
    return [(cube[brick, :, 0], cube[brick, :, 1]) for brick in range(BRICKS)]


def put_halves(halves_ref, start, bricks):
    for brick, lines in enumerate(bricks):
        for half in range(2):
            first = start + brick * CUBE
            halves_ref[half, first : first + CUBE, :] = lines[half].reshape(CUBE, HALF)


def cotangent_lines(cotangent_ref):
    cube = cotangent_ref[...].astype(F32).reshape(BRICKS, EDGE, EDGE, LINE)
    return [(cube[brick, :, :, :HALF], cube[brick, :, :, HALF:]) for brick in range(BRICKS)]


def pack_faces(faces_ref, base, halves_ref, start, high):
    x_face = pair(halves_ref, start + ((EDGE - 1) * EDGE if high else 0), EDGE)
    y_face = pair(halves_ref, start + (EDGE - 1 if high else 0), EDGE, EDGE)
    for half in range(2):
        lanes = slice(half * HALF, half * HALF + HALF)
        faces_ref[base : base + EDGE, lanes] = x_face[half]
        faces_ref[base + EDGE : base + 2 * EDGE, lanes] = y_face[half]
    tile = halves_ref[1 if high else 0, start : start + CUBE, :]
    lane = lanes_of((16, 128)) // CHANNELS
    packed = jnp.zeros((16, 128), F32)
    for part in range(4):
        shift = (part + 1 if high else part) % 4 * CHANNELS
        piece = tile[part * 16 : part * 16 + 16]
        packed = jnp.where(lane == part, pltpu.roll(piece, shift, 1) if shift else piece, packed)
    faces_ref[base + 2 * EDGE : base + FACE, :128] = packed[:8]
    faces_ref[base + 2 * EDGE : base + FACE, 128:] = packed[8:]


def pack_all(bricks, halves_ref, faces_ref, high_out, low_out):
    put_halves(halves_ref, 0, bricks)
    for high, out_ref in ((True, high_out), (False, low_out)):
        for brick in range(BRICKS):
            pack_faces(faces_ref, brick * FACE, halves_ref, brick * CUBE, high)
        out_ref[...] = faces_ref[...].astype(BF16)


def to_partners(high_ref, low_ref, far_out, near_out):
    even = lax.axis_index("space") % 2 == 0
    far_out[...] = jnp.where(even, low_ref[...], high_ref[...])
    near_out[...] = jnp.where(even, high_ref[...], low_ref[...])


def faces_kernel(cotangent_ref, high_out, low_out, far_out, near_out, halves_ref, faces_ref):
    pack_all(cotangent_lines(cotangent_ref), halves_ref, faces_ref, high_out, low_out)
    to_partners(high_out, low_out, far_out, near_out)


def unpack_depth(rows, high):
    packed = jnp.concatenate([rows[:, :128], rows[:, 128:]], axis=0)
    pieces = []
    for part in range(4):
        shift = ((3 - part) if high else (4 - part)) % 4 * CHANNELS
        pieces.append(pltpu.roll(packed, shift, 1) if shift else packed)
    return jnp.concatenate(pieces, axis=0).reshape(EDGE, EDGE, 128)


def first_kernel(
    links_in, received_ref, up_ref, band_ref, weights_ref,
    slope_out, hidden_out, turned_out, pad_out, back_out, high_out, low_out,
    volumes_ref, rows_ref, halves_ref, faces_ref, links_ref, links_sem,
):
    links_copy = pltpu.make_async_copy(links_in, links_ref, links_sem)
    links_copy.start()
    position = lax.axis_index("space")
    tiles = received_ref.shape[1] // (3 * BRICKS)
    rows_ref[0 : 3 * BRICKS * tiles] = jnp.sum(received_ref[...].astype(F32), axis=0)
    rows_ref[3 * BRICKS * tiles :] = jnp.zeros((2 * tiles, 128), F32)
    cells = []
    for tile in range(tiles):
        rows = rows_ref[pl.ds(tile, 8, stride=tiles), :]
        cells += [rows[:, :64], rows[:, 64:]]
    lifted = dot(jnp.concatenate(cells, axis=0).astype(BF16), up_ref[...])
    lifted = lifted.astype(BF16).astype(F32)
    for cell in range(8):
        a, b, c = cell // 4, cell // 2 % 2, cell % 2
        for sub in range(16):
            line = (4 * a + sub // 4) * EDGE + 4 * b + sub % 4
            volumes_ref[c, pl.ds(line, 8, stride=CUBE), :] = lifted[
                cell * 8 : cell * 8 + 8, sub * 128 : sub * 128 + 128
            ]
    links_copy.wait()
    for brick in range(BRICKS):

        def near(face):
            link = links_ref[0, brick, face]
            index = jnp.clip(link - BRICKS * (position - 1), 0, 3 * BRICKS - 1)
            return pl.multiple_of(index * CUBE, CUBE), jnp.where(link >= 0, 1.0, 0.0).astype(F32)

        def x_face(face):
            start, present = near(face)
            offset = EDGE * (EDGE - 1) if face % 2 == 0 else 0
            return [half * present for half in pair(volumes_ref, pl.multiple_of(start + offset, 8), EDGE)]

        def y_face(face):
            start, present = near(face)
            offset = EDGE - 1 if face % 2 == 0 else 0
            return [half * present for half in pair(volumes_ref, start + offset, EDGE, EDGE)]

        def z_face(face):
            start, present = near(face)
            tile = volumes_ref[1 if face % 2 == 0 else 0, pl.ds(start, CUBE), :] * present
            return tile.reshape(EDGE, EDGE, HALF)

        own = pair(volumes_ref, (BRICKS + brick) * CUBE, CUBE)
        own = [half.reshape(EDGE, EDGE, HALF) for half in own]
        put_padded(pad_out, brick, own, x_face(0), x_face(1), y_face(2), y_face(3), z_face(4), z_face(5))
    pre = convolve(pad_out, band_ref)
    sigmoid = 1.0 / (1.0 + jnp.exp(-pre))
    hidden = (pre / (1.0 + jnp.exp(-pre))).astype(BF16)
    slope_out[...] = sigmoid * (1.0 + pre * (1.0 - sigmoid))
    hidden_out[...] = hidden
    hidden = hidden.astype(F32)
    turned_out[...] = jnp.transpose(hidden).astype(BF16)
    pack_all(half_lines(hidden), halves_ref, faces_ref, high_out, low_out)
    build_band(back_out, flipped_rows(weights_ref[...].astype(F32)))


def fold(outer, places):
    lane = lanes_of((CHANNELS, 128)) // CHANNELS
    folded = None
    for block in range(4):
        start, tile = places[block]
        rows = outer[start : start + CHANNELS, tile * 128 : tile * 128 + 128]
        folded = rows if folded is None else jnp.where(lane == block, rows, folded)
    quarter = [folded[8 * q : 8 * q + 8] for q in range(4)]
    small = lanes_of((8, 128)) // CHANNELS
    total = None
    for turn in range(4):
        mixed = quarter[0]
        for q in range(1, 4):
            mixed = jnp.where(small == (q + turn) % 4, quarter[q], mixed)
        if turn:
            mixed = pltpu.roll(mixed, 128 - turn * CHANNELS, 1)
        total = mixed if total is None else total + mixed
    return total


def diagonal(shift):
    places = [None] * 4
    for z in range(4):
        other = z + shift
        places[other % 4] = (z * CHANNELS, 0 if 0 <= other < 4 else 1)
    return places


def pad_all(pad_ref, bricks, links_ref, high_pool, low_pool, high_own, low_own, far, near):
    position = lax.axis_index("space")
    half = BRICKS * FACE
    even = position % 2 == 0
    high_pool[0:half] = jnp.where(even, far[...], near[...]).astype(F32)
    high_pool[half:] = high_own[...].astype(F32)
    low_pool[0:half] = low_own[...].astype(F32)
    low_pool[half:] = jnp.where(even, near[...], far[...]).astype(F32)
    for brick, lines in enumerate(bricks):

        def rows(face, axis):
            link = links_ref[0, brick, face]
            high = face % 2 == 0
            index = jnp.clip(link - BRICKS * (position - 1 if high else position), 0, 2 * BRICKS - 1)
            pool = high_pool if high else low_pool
            present = jnp.where(link >= 0, 1.0, 0.0).astype(F32)
            return pool[pl.ds(pl.multiple_of(index * FACE + axis * EDGE, 8), EDGE), :] * present

        def face(number, axis):
            found = rows(number, axis)
            return found[:, :HALF], found[:, HALF:]

        put_padded(
            pad_ref, brick, lines, face(0, 0), face(1, 0), face(2, 1), face(3, 1),
            unpack_depth(rows(4, 2), True), unpack_depth(rows(5, 2), False),
        )


def second_kernel(
    links_in, cotangent_ref, band_ref, slope_ref, hidden_ref, lifted_pad, high_own, low_own, far, near,
    hidden_high, hidden_low,
    sums_out, lifted_out, far_out, near_out,
    high_pool, low_pool, cotangent_pad, sums_ref, links_ref, links_sem,
):
    links_copy = pltpu.make_async_copy(links_in, links_ref, links_sem)
    links_copy.start()
    to_partners(hidden_high, hidden_low, far_out, near_out)
    lifted_out[...] = window(lifted_pad, 4)[:, :HALF]
    bricks = cotangent_lines(cotangent_ref)
    links_copy.wait()
    pad_all(cotangent_pad, bricks, links_ref, high_pool, low_pool, high_own, low_own, far, near)
    gradient = (convolve(cotangent_pad, band_ref) * slope_ref[...]).astype(BF16)
    gradient = jnp.transpose(gradient.astype(F32)).astype(BF16)
    hidden = hidden_ref[...]
    sums_ref[8 * BLOCKS :] = jnp.zeros((sums_ref.shape[0] - 8 * BLOCKS, 128), F32)
    for k in range(9):
        one = dot(gradient, window(lifted_pad, k))
        two = dot(hidden, window(cotangent_pad, 8 - k))
        for part in range(3):
            start = 8 * (3 * k + part)
            sums_ref[start : start + 8] = fold(one, diagonal(part - 1))
            start += 8 * 27
            sums_ref[start : start + 8] = fold(two, diagonal(1 - part))
    sums_out[...] = sums_ref[...].astype(BF16).reshape(sums_out.shape)


def fine_kernel(
    links_in, weights_ref, lifted_ref, hidden_ref, high_own, low_own, far, near,
    fine_out, high_pool, low_pool, hidden_pad, band_ref, links_ref, links_sem,
):
    links_copy = pltpu.make_async_copy(links_in, links_ref, links_sem)
    links_copy.start()
    build_band(band_ref, weight_rows(weights_ref[...].astype(F32)))
    links_copy.wait()
    bricks = half_lines(hidden_ref[...].astype(F32))
    pad_all(hidden_pad, bricks, links_ref, high_pool, low_pool, high_own, low_own, far, near)
    fine = lifted_ref[...].astype(F32) + convolve(hidden_pad, band_ref)
    fine = fine.reshape(LINES // EDGE, 2, EDGE, HALF)
    fine = jnp.concatenate([fine[:, 0], fine[:, 1]], axis=-1)
    fine_out[...] = fine.astype(BF16).reshape(fine_out.shape)


def unpacked(tile):
    pieces = [tile] + [pltpu.roll(tile, 128 - q * CHANNELS, 1) for q in range(1, 4)]
    return jnp.concatenate(pieces, axis=0)[:, :CHANNELS]


def sum_kernel(scale, parts_ref, _far, _near, out_ref):
    total = jnp.sum(parts_ref[...].astype(F32), axis=0) * scale
    per = parts_ref.shape[1] // 8
    device = lax.axis_index("space") * lax.axis_size("dp") + lax.axis_index("dp")
    tiles = []
    for j in range(per):
        tile = total[8 * j : 8 * j + 8]
        block = jnp.transpose(unpacked(tile))
        turned = jnp.concatenate([block[8 * q : 8 * q + 8] for q in range(4)], axis=1)
        tiles.append(jnp.where(device * per + j < 27, turned, tile))
    total = jnp.concatenate(tiles, axis=0)
    out_ref[...] = jnp.broadcast_to(total.astype(BF16)[None], out_ref.shape)


def unpack_kernel(sums_ref, one_out, two_out, rows_ref, one_ref, two_ref, sems):
    rows_ref[...] = sums_ref[...].astype(F32).reshape(rows_ref.shape)
    copies = []
    for which, (block_ref, out) in enumerate(((one_ref, one_out), (two_ref, two_out))):
        for third in range(3):
            first = 9 * third
            for index in range(first, first + 9):
                row = 8 * (27 * which + index)
                block_ref[index] = unpacked(rows_ref[row : row + 8])
            part = pl.ds(first, 9)
            copies.append(pltpu.make_async_copy(block_ref.at[part], out.at[part], sems.at[which, third]))
            copies[-1].start()
    for copy in copies:
        copy.wait()


def call(kernel, out_shape, scratch=(), hbm=(), inputs=1, limit=24, cost=None, out=pltpu.VMEM):
    spaces = [pl.ANY if i in hbm else pltpu.VMEM for i in range(inputs)]
    return pl.pallas_call(
        kernel,
        out_shape=out_shape,
        in_specs=[pl.BlockSpec(memory_space=space) for space in spaces],
        out_specs=jax.tree.map(lambda _: pl.BlockSpec(memory_space=out), out_shape),
        scratch_shapes=list(scratch),
        compiler_params=pltpu.CompilerParams(vmem_limit_bytes=limit * 2**20),
        cost_estimate=cost,
    )


def shape(*dims, dtype=BF16):
    return jax.ShapeDtypeStruct(dims, dtype)


def swapped(value, first):
    pairs = [(i, i + 1) for i in range(first, lax.axis_size("space") - 1, 2)]
    return lax.ppermute(value, "space", pairs + [(target, source) for source, target in pairs])


def body(coarse_latents, active_blocks, face_links, cotangent, up_weight, conv_one, conv_two):
    devices = lax.axis_size("space")
    everyone = devices * lax.axis_size("dp")
    held, width = coarse_latents.shape[1:]
    bricks = active_blocks.shape[1]
    tiles = width // 128
    packed = call(
        functools.partial(pick_kernel, devices),
        shape(devices, 3 * BRICKS * tiles, 128),
        [
            pltpu.VMEM((1, bricks), jnp.int32),
            pltpu.VMEM((1, held, width), BF16),
            pltpu.VMEM(((bricks + 16) * tiles, 128), F32),
            pltpu.SemaphoreType.DMA((2,)),
        ],
        hbm=(0, 1),
        inputs=2,
        limit=60,
    )(active_blocks, coarse_latents)
    received = lax.all_to_all(packed, "space", split_axis=0, concat_axis=0, tiled=True)
    band = pltpu.VMEM(BAND, BF16)
    cost = pl.CostEstimate(flops=10**9, bytes_accessed=2 * 10**6, transcendentals=0)
    face = shape(BRICKS * FACE, LINE)
    halves = pltpu.VMEM((2, LINES, HALF), F32)
    faces = pltpu.VMEM((BRICKS * FACE, LINE), F32)
    pool = pltpu.VMEM((2 * BRICKS * FACE, LINE), F32)
    volume = shape(ROWS, HALF)
    links = [pltpu.SMEM(face_links.shape, jnp.int32), pltpu.SemaphoreType.DMA]
    pad_shape = (3, BRICKS, EDGE + 2, 2 * EDGE, WIDE)
    pad = pltpu.VMEM(pad_shape, BF16)
    high, low, far, near = call(faces_kernel, (face,) * 4, [halves, faces])(cotangent)
    far = swapped(far, 1)
    near = swapped(near, 0)
    band_one = call(band_kernel, shape(*BAND), cost=cost)(conv_one)
    slope, hidden, turned, lifted_pad, band_back, hidden_high, hidden_low = call(
        first_kernel,
        (
            shape(ROWS, HALF, dtype=F32), volume, shape(HALF, ROWS), shape(*pad_shape), shape(*BAND),
            face, face,
        ),
        [pltpu.VMEM((2, 8 * CUBE, 128), F32), pltpu.VMEM((8 * tiles, 128), F32), halves, faces, *links],
        hbm=(0,),
        inputs=5,
    )(face_links, received, up_weight, band_one, conv_two)
    per = -(-BLOCKS // everyone)
    per += per % 2
    sums, lifted, hidden_far, hidden_near = call(
        second_kernel,
        (shape(everyone, per * 8, 128), volume, face, face),
        [pool, pool, pad, pltpu.VMEM((everyone * per * 8, 128), F32), *links],
        hbm=(0,),
        inputs=12,
    )(
        face_links, cotangent, band_back, slope, turned, lifted_pad, high, low, far, near,
        hidden_high, hidden_low,
    )
    hidden_far = swapped(hidden_far, 1)
    hidden_near = swapped(hidden_near, 0)
    fine = call(fine_kernel, shape(*cotangent.shape), [pool, pool, pad, band, *links], hbm=(0,), inputs=8, cost=cost)(
        face_links, conv_two, lifted, hidden, hidden_high, hidden_low, hidden_far, hidden_near
    )
    axes = ("space", "dp")
    parts = lax.all_to_all(sums, axes, split_axis=0, concat_axis=0, tiled=True)
    scale = 1.0 / math.sqrt(lax.axis_size("dp") * devices * BRICKS * EDGE**3)
    total = call(functools.partial(sum_kernel, scale), shape(*sums.shape), hbm=(1, 2), inputs=3)(
        parts, hidden_far, hidden_near
    )
    gathered = lax.all_to_all(total, axes, split_axis=0, concat_axis=0, tiled=True)
    grads = shape(27, CHANNELS, CHANNELS, dtype=F32)
    block = pltpu.VMEM(grads.shape, F32)
    scratch = [pltpu.VMEM((everyone * per * 8, 128), F32), block, block, pltpu.SemaphoreType.DMA((2, 3))]
    grad_one, grad_two = call(unpack_kernel, (grads, grads), scratch, out=pl.ANY)(gathered)
    return (fine, grad_one, grad_two)


def solution(mesh):
    return jax.shard_map(
        body,
        mesh=mesh,
        in_specs=(
            P("dp", "space", None),
            P("dp", None),
            P("dp", "space", None),
            P("dp", "space", None, None, None),
            P(),
            P(),
            P(),
        ),
        out_specs=(P("dp", "space", None, None, None), P(), P()),
        check_vma=False,
    )
```

```python
import functools
import math

import jax
import jax.numpy as jnp
from jax import lax
from jax.experimental import pallas as pl
from jax.experimental.pallas import tpu as pltpu
from jax.sharding import PartitionSpec as P

BF16 = jnp.bfloat16
F32 = jnp.float32
EDGE = 8
CHANNELS = 32
LINE = EDGE * CHANNELS
HALF = LINE // 2
WIDE = 2 * HALF
BRICKS = 2
CUBE = EDGE * EDGE
LINES = BRICKS * CUBE
BAND = (9, WIDE, HALF)
ROWS = 2 * LINES
FACE = 3 * EDGE
BLOCKS = 54


def dot(left, right):
    return jnp.dot(left, right, preferred_element_type=F32)


def dot_rows(left, right):
    return lax.dot_general(left, right, (((0,), (0,)), ((), ())), preferred_element_type=F32)


def pair(halves_ref, start, count, stride=1):
    index = pl.ds(start, count, stride=stride) if stride > 1 else pl.ds(start, count)
    return halves_ref[0, index, :], halves_ref[1, index, :]


def lanes_of(shape):
    return lax.broadcasted_iota(jnp.int32, shape, len(shape) - 1)


def pick_kernel(scenes, ids_hbm, latents_hbm, out_ref, ids_ref, latents_ref, rows_ref, sems):
    ids_copy = pltpu.make_async_copy(ids_hbm, ids_ref, sems.at[0])
    latents_copy = pltpu.make_async_copy(latents_hbm, latents_ref, sems.at[1])
    ids_copy.start()
    latents_copy.start()
    held, width = latents_ref.shape[1:]
    bricks = ids_ref.shape[1]
    margin = 8 * width // 128
    tiles = width // 128
    rows_ref[0:margin] = jnp.zeros((margin, 128), F32)
    rows_ref[margin + bricks * tiles :] = jnp.zeros((margin, 128), F32)
    first = lax.axis_index("space") * held
    rows = lax.broadcasted_iota(jnp.int32, (held, bricks), 0) + first
    ids_copy.wait()
    hot = jnp.where(rows == ids_ref[...], 1.0, 0.0).astype(BF16)
    latents_copy.wait()
    picked = dot_rows(hot, latents_ref[0])
    for tile in range(tiles):
        rows_ref[pl.ds(margin + tile, bricks, stride=tiles), :] = picked[:, tile * 128 : tile * 128 + 128]
    count = out_ref.shape[1]
    wanted = [jnp.where(lax.axis_index("dp") == scene, 1.0, 0.0).astype(F32) for scene in range(scenes)]
    for receiver in range(out_ref.shape[0] // scenes):
        start = margin + BRICKS * (receiver - 1) * tiles
        found = rows_ref[start : start + count]
        for scene in range(scenes):
            kept = found * wanted[scene] if scenes > 1 else found
            out_ref[receiver * scenes + scene] = kept.astype(BF16)


def build_band(band_ref, rows):
    shape = (3 * CHANNELS, HALF)
    row = lax.broadcasted_iota(jnp.int32, shape, 0)
    target = CHANNELS - (row // CHANNELS) * CHANNELS + row % CHANNELS
    distance = lanes_of(shape) - target
    band_ref[:, HALF:, :] = jnp.zeros((9, HALF, HALF), BF16)
    for z in range(-1, 5):
        select = jnp.where(distance == z * CHANNELS, 1.0, 0.0).astype(BF16)
        block = dot(rows, select).astype(BF16)
        start = z % 8 * CHANNELS
        band_ref[:, start : start + CHANNELS, :] = block.reshape(9, CHANNELS, HALF)


def weight_rows(weights):
    cube = weights.reshape(9, 3, CHANNELS, CHANNELS)
    rows = jnp.concatenate([cube[:, 0], cube[:, 1], cube[:, 2]], axis=-1)
    return rows.reshape(9 * CHANNELS, 3 * CHANNELS).astype(BF16)


def flipped_rows(weights):
    cube = jnp.swapaxes(weights, 1, 2).reshape(9, 3, CHANNELS, CHANNELS)
    pieces = [jnp.concatenate([cube[8 - k, 2], cube[8 - k, 1], cube[8 - k, 0]], axis=-1) for k in range(9)]
    return jnp.concatenate(pieces, axis=0).astype(BF16)


def band_kernel(weights_ref, band_ref):
    build_band(band_ref, weight_rows(weights_ref[...].astype(F32)))


def put_padded(pad_ref, brick, lines, x_low, x_high, y_low, y_high, z_low, z_high):
    def joined(halves, before, after):
        lane = lanes_of(halves[0].shape)
        first = jnp.where(lane < CHANNELS, halves[1], before)
        second = jnp.where(lane >= HALF - CHANNELS, halves[0], after)
        return jnp.concatenate([halves[0], first], axis=-1), jnp.concatenate([halves[1], second], axis=-1)

    inside = joined(lines, z_low, z_high)
    x_low, x_high, y_low, y_high = [joined(face, 0.0, 0.0) for face in (x_low, x_high, y_low, y_high)]
    none = jnp.zeros((1, WIDE), F32)
    shifted = [[], [], []]
    for half in range(2):
        slabs = jnp.concatenate([x_low[half][None], inside[half], x_high[half][None]], axis=0)
        row = lax.broadcasted_iota(jnp.int32, slabs.shape, 1)
        low = jnp.concatenate([none, y_low[half], none], axis=0)[:, None, :]
        high = jnp.concatenate([none, y_high[half], none], axis=0)[:, None, :]
        shifted[0].append(jnp.where(row == 0, low, pltpu.roll(slabs, 1, 1)))
        shifted[1].append(slabs)
        shifted[2].append(jnp.where(row == EDGE - 1, high, pltpu.roll(slabs, EDGE - 1, 1)))
    for dy in range(3):
        pad_ref[dy, brick] = jnp.concatenate(shifted[dy], axis=1).astype(BF16)


def window(pad_ref, k):
    return pad_ref[k % 3, :, k // 3 : k // 3 + EDGE].reshape(ROWS, WIDE)


def convolve(pad_ref, band_ref):
    total = None
    for k in range(9):
        term = dot(window(pad_ref, k), band_ref[k])
        total = term if total is None else total + term
    return total


def half_lines(values):
    cube = values.reshape(BRICKS, EDGE, 2, EDGE, HALF)
    return [(cube[brick, :, 0], cube[brick, :, 1]) for brick in range(BRICKS)]


def put_halves(halves_ref, start, bricks):
    for brick, lines in enumerate(bricks):
        for half in range(2):
            first = start + brick * CUBE
            halves_ref[half, first : first + CUBE, :] = lines[half].reshape(CUBE, HALF)


def cotangent_lines(cotangent_ref):
    cube = cotangent_ref[...].astype(F32).reshape(BRICKS, EDGE, EDGE, LINE)
    return [(cube[brick, :, :, :HALF], cube[brick, :, :, HALF:]) for brick in range(BRICKS)]


def pack_faces(faces_ref, base, halves_ref, start, high):
    x_face = pair(halves_ref, start + ((EDGE - 1) * EDGE if high else 0), EDGE)
    y_face = pair(halves_ref, start + (EDGE - 1 if high else 0), EDGE, EDGE)
    for half in range(2):
        lanes = slice(half * HALF, half * HALF + HALF)
        faces_ref[base : base + EDGE, lanes] = x_face[half]
        faces_ref[base + EDGE : base + 2 * EDGE, lanes] = y_face[half]
    tile = halves_ref[1 if high else 0, start : start + CUBE, :]
    lane = lanes_of((16, 128)) // CHANNELS
    packed = jnp.zeros((16, 128), F32)
    for part in range(4):
        shift = (part + 1 if high else part) % 4 * CHANNELS
        piece = tile[part * 16 : part * 16 + 16]
        packed = jnp.where(lane == part, pltpu.roll(piece, shift, 1) if shift else piece, packed)
    faces_ref[base + 2 * EDGE : base + FACE, :128] = packed[:8]
    faces_ref[base + 2 * EDGE : base + FACE, 128:] = packed[8:]


def pack_all(bricks, halves_ref, faces_ref, high_out, low_out):
    put_halves(halves_ref, 0, bricks)
    for high, out_ref in ((True, high_out), (False, low_out)):
        for brick in range(BRICKS):
            pack_faces(faces_ref, brick * FACE, halves_ref, brick * CUBE, high)
        out_ref[...] = faces_ref[...].astype(BF16)


def to_partners(high_ref, low_ref, far_out, near_out):
    even = lax.axis_index("space") % 2 == 0
    far_out[...] = jnp.where(even, low_ref[...], high_ref[...])
    near_out[...] = jnp.where(even, high_ref[...], low_ref[...])


def faces_kernel(cotangent_ref, high_out, low_out, far_out, near_out, halves_ref, faces_ref):
    pack_all(cotangent_lines(cotangent_ref), halves_ref, faces_ref, high_out, low_out)
    to_partners(high_out, low_out, far_out, near_out)


def unpack_depth(halves, high):
    packed = jnp.concatenate(halves, axis=0)
    pieces = []
    for part in range(4):
        shift = ((3 - part) if high else (4 - part)) % 4 * CHANNELS
        pieces.append(pltpu.roll(packed, shift, 1) if shift else packed)
    return jnp.concatenate(pieces, axis=0).reshape(EDGE, EDGE, 128)


def first_kernel(
    links_in, received_ref, up_ref, band_ref, weights_ref,
    slope_out, hidden_out, turned_out, pad_out, back_out, high_out, low_out, masks_out,
    volumes_ref, rows_ref, halves_ref, faces_ref, links_ref, links_sem,
):
    links_copy = pltpu.make_async_copy(links_in, links_ref, links_sem)
    links_copy.start()
    position = lax.axis_index("space")
    tiles = received_ref.shape[1] // (3 * BRICKS)
    rows_ref[0 : 3 * BRICKS * tiles] = jnp.sum(received_ref[...].astype(F32), axis=0)
    rows_ref[3 * BRICKS * tiles :] = jnp.zeros((2 * tiles, 128), F32)
    cells = []
    for tile in range(tiles):
        rows = rows_ref[pl.ds(tile, 8, stride=tiles), :]
        cells += [rows[:, :64], rows[:, 64:]]
    lifted = dot(jnp.concatenate(cells, axis=0).astype(BF16), up_ref[...])
    lifted = lifted.astype(BF16).astype(F32)
    for cell in range(8):
        a, b, c = cell // 4, cell // 2 % 2, cell % 2
        for sub in range(16):
            line = (4 * a + sub // 4) * EDGE + 4 * b + sub % 4
            volumes_ref[c, pl.ds(line, 8, stride=CUBE), :] = lifted[
                cell * 8 : cell * 8 + 8, sub * 128 : sub * 128 + 128
            ]
    links_copy.wait()
    put_masks(masks_out, links_ref)
    for brick in range(BRICKS):

        def near(face):
            link = links_ref[0, brick, face]
            index = jnp.clip(link - BRICKS * (position - 1), 0, 3 * BRICKS - 1)
            return pl.multiple_of(index * CUBE, CUBE), jnp.where(link >= 0, 1.0, 0.0).astype(F32)

        def x_face(face):
            start, present = near(face)
            offset = EDGE * (EDGE - 1) if face % 2 == 0 else 0
            return [half * present for half in pair(volumes_ref, pl.multiple_of(start + offset, 8), EDGE)]

        def y_face(face):
            start, present = near(face)
            offset = EDGE - 1 if face % 2 == 0 else 0
            return [half * present for half in pair(volumes_ref, start + offset, EDGE, EDGE)]

        def z_face(face):
            start, present = near(face)
            tile = volumes_ref[1 if face % 2 == 0 else 0, pl.ds(start, CUBE), :] * present
            return tile.reshape(EDGE, EDGE, HALF)

        own = pair(volumes_ref, (BRICKS + brick) * CUBE, CUBE)
        own = [half.reshape(EDGE, EDGE, HALF) for half in own]
        put_padded(pad_out, brick, own, x_face(0), x_face(1), y_face(2), y_face(3), z_face(4), z_face(5))
    pre = convolve(pad_out, band_ref)
    sigmoid = 1.0 / (1.0 + jnp.exp(-pre))
    hidden = (pre / (1.0 + jnp.exp(-pre))).astype(BF16)
    slope_out[...] = sigmoid * (1.0 + pre * (1.0 - sigmoid))
    hidden_out[...] = hidden
    hidden = hidden.astype(F32)
    turned_out[...] = jnp.transpose(hidden).astype(BF16)
    pack_all(half_lines(hidden), halves_ref, faces_ref, high_out, low_out)
    build_band(back_out, flipped_rows(weights_ref[...].astype(F32)))


def fold(outer, places):
    lane = lanes_of((CHANNELS, 128)) // CHANNELS
    folded = None
    for block in range(4):
        start, tile = places[block]
        rows = outer[start : start + CHANNELS, tile * 128 : tile * 128 + 128]
        folded = rows if folded is None else jnp.where(lane == block, rows, folded)
    quarter = [folded[8 * q : 8 * q + 8] for q in range(4)]
    small = lanes_of((8, 128)) // CHANNELS
    total = None
    for turn in range(4):
        mixed = quarter[0]
        for q in range(1, 4):
            mixed = jnp.where(small == (q + turn) % 4, quarter[q], mixed)
        if turn:
            mixed = pltpu.roll(mixed, 128 - turn * CHANNELS, 1)
        total = mixed if total is None else total + mixed
    return total


def diagonal(shift):
    places = [None] * 4
    for z in range(4):
        other = z + shift
        places[other % 4] = (z * CHANNELS, 0 if 0 <= other < 4 else 1)
    return places


def put_masks(masks_ref, links_ref):
    position = lax.axis_index("space")
    for brick in range(BRICKS):
        for face in range(6):
            first = links_ref[0, brick, face] - BRICKS * (position - 1 if face % 2 == 0 else position)
            for i in range(2 * BRICKS):
                row = (brick * 6 + face) * 2 * BRICKS + i
                masks_ref[row : row + 1, :] = jnp.full((1, 128), jnp.where(first == i, 1.0, 0.0).astype(F32))


def pad_all(pad_ref, bricks, masks_ref, high_pool, low_pool, high_own, low_own, far, near):
    position = lax.axis_index("space")
    half = BRICKS * FACE
    even = position % 2 == 0
    high_pool[0:half] = jnp.where(even, far[...], near[...]).astype(F32)
    high_pool[half:] = high_own[...].astype(F32)
    low_pool[0:half] = low_own[...].astype(F32)
    low_pool[half:] = jnp.where(even, near[...], far[...]).astype(F32)
    for brick, lines in enumerate(bricks):

        def face(number, axis):
            pool = high_pool if number % 2 == 0 else low_pool
            total = [0.0, 0.0]
            for i in range(2 * BRICKS):
                row = (brick * 6 + number) * 2 * BRICKS + i
                mask = masks_ref[row : row + 1, :]
                start = i * FACE + axis * EDGE
                for part in range(2):
                    found = pool[start : start + EDGE, part * HALF : part * HALF + HALF]
                    total[part] = total[part] + found * mask
            return total

        put_padded(
            pad_ref, brick, lines, face(0, 0), face(1, 0), face(2, 1), face(3, 1),
            unpack_depth(face(4, 2), True), unpack_depth(face(5, 2), False),
        )


def second_kernel(
    masks_ref, cotangent_ref, band_ref, slope_ref, hidden_ref, lifted_pad, high_own, low_own, far, near,
    hidden_high, hidden_low,
    sums_out, lifted_out, far_out, near_out,
    high_pool, low_pool, cotangent_pad, sums_ref,
):
    to_partners(hidden_high, hidden_low, far_out, near_out)
    lifted_out[...] = window(lifted_pad, 4)[:, :HALF]
    bricks = cotangent_lines(cotangent_ref)
    pad_all(cotangent_pad, bricks, masks_ref, high_pool, low_pool, high_own, low_own, far, near)
    gradient = (convolve(cotangent_pad, band_ref) * slope_ref[...]).astype(BF16)
    gradient = jnp.transpose(gradient.astype(F32)).astype(BF16)
    hidden = hidden_ref[...]
    sums_ref[8 * BLOCKS :] = jnp.zeros((sums_ref.shape[0] - 8 * BLOCKS, 128), F32)
    for k in range(9):
        one = dot(gradient, window(lifted_pad, k))
        two = dot(hidden, window(cotangent_pad, 8 - k))
        for part in range(3):
            start = 8 * (3 * k + part)
            sums_ref[start : start + 8] = fold(one, diagonal(part - 1))
            start += 8 * 27
            sums_ref[start : start + 8] = fold(two, diagonal(1 - part))
    sums_out[...] = sums_ref[...].astype(BF16).reshape(sums_out.shape)


def fine_kernel(
    masks_ref, weights_ref, lifted_ref, hidden_ref, high_own, low_own, far, near,
    fine_out, high_pool, low_pool, hidden_pad, band_ref,
):
    build_band(band_ref, weight_rows(weights_ref[...].astype(F32)))
    bricks = half_lines(hidden_ref[...].astype(F32))
    pad_all(hidden_pad, bricks, masks_ref, high_pool, low_pool, high_own, low_own, far, near)
    fine = lifted_ref[...].astype(F32) + convolve(hidden_pad, band_ref)
    fine = fine.reshape(LINES // EDGE, 2, EDGE, HALF)
    fine = jnp.concatenate([fine[:, 0], fine[:, 1]], axis=-1)
    fine_out[...] = fine.astype(BF16).reshape(fine_out.shape)


def unpacked(tile):
    pieces = [tile] + [pltpu.roll(tile, 128 - q * CHANNELS, 1) for q in range(1, 4)]
    return jnp.concatenate(pieces, axis=0)[:, :CHANNELS]


def sum_kernel(scale, parts_ref, _far, _near, out_ref):
    total = jnp.sum(parts_ref[...].astype(F32), axis=0) * scale
    per = parts_ref.shape[1] // 8
    device = lax.axis_index("space") * lax.axis_size("dp") + lax.axis_index("dp")
    tiles = []
    for j in range(per):
        tile = total[8 * j : 8 * j + 8]
        block = jnp.transpose(unpacked(tile))
        turned = jnp.concatenate([block[8 * q : 8 * q + 8] for q in range(4)], axis=1)
        tiles.append(jnp.where(device * per + j < 27, turned, tile))
    total = jnp.concatenate(tiles, axis=0)
    out_ref[...] = jnp.broadcast_to(total.astype(BF16)[None], out_ref.shape)


def unpack_kernel(sums_ref, one_out, two_out, rows_ref, one_ref, two_ref, sems):
    rows_ref[...] = sums_ref[...].astype(F32).reshape(rows_ref.shape)
    copies = []
    for which, (block_ref, out) in enumerate(((one_ref, one_out), (two_ref, two_out))):
        for third in range(3):
            first = 9 * third
            for index in range(first, first + 9):
                row = 8 * (27 * which + index)
                block_ref[index] = unpacked(rows_ref[row : row + 8])
            part = pl.ds(first, 9)
            copies.append(pltpu.make_async_copy(block_ref.at[part], out.at[part], sems.at[which, third]))
            copies[-1].start()
    for copy in copies:
        copy.wait()


def call(kernel, out_shape, scratch=(), hbm=(), inputs=1, limit=24, cost=None, out=pltpu.VMEM):
    spaces = [pl.ANY if i in hbm else pltpu.VMEM for i in range(inputs)]
    return pl.pallas_call(
        kernel,
        out_shape=out_shape,
        in_specs=[pl.BlockSpec(memory_space=space) for space in spaces],
        out_specs=jax.tree.map(lambda _: pl.BlockSpec(memory_space=out), out_shape),
        scratch_shapes=list(scratch),
        compiler_params=pltpu.CompilerParams(vmem_limit_bytes=limit * 2**20),
        cost_estimate=cost,
    )


def shape(*dims, dtype=BF16):
    return jax.ShapeDtypeStruct(dims, dtype)


def swapped(value, first):
    pairs = [(i, i + 1) for i in range(first, lax.axis_size("space") - 1, 2)]
    return lax.ppermute(value, "space", pairs + [(target, source) for source, target in pairs])


def body(coarse_latents, active_blocks, face_links, cotangent, up_weight, conv_one, conv_two):
    devices = lax.axis_size("space")
    everyone = devices * lax.axis_size("dp")
    held, width = coarse_latents.shape[1:]
    bricks = active_blocks.shape[1]
    tiles = width // 128
    scenes = 2 if lax.axis_size("dp") == 2 else 1
    packed = call(
        functools.partial(pick_kernel, scenes),
        shape(devices * scenes, 3 * BRICKS * tiles, 128),
        [
            pltpu.VMEM((1, bricks), jnp.int32),
            pltpu.VMEM((1, held, width), BF16),
            pltpu.VMEM(((bricks + 16) * tiles, 128), F32),
            pltpu.SemaphoreType.DMA((2,)),
        ],
        hbm=(0, 1),
        inputs=2,
        limit=60,
    )(active_blocks, coarse_latents)
    axes = ("space", "dp")
    received = lax.all_to_all(packed, axes if scenes == 2 else "space", split_axis=0, concat_axis=0, tiled=True)
    band = pltpu.VMEM(BAND, BF16)
    cost = pl.CostEstimate(flops=10**9, bytes_accessed=2 * 10**6, transcendentals=0)
    face = shape(BRICKS * FACE, LINE)
    halves = pltpu.VMEM((2, LINES, HALF), F32)
    faces = pltpu.VMEM((BRICKS * FACE, LINE), F32)
    pool = pltpu.VMEM((2 * BRICKS * FACE, LINE), F32)
    volume = shape(ROWS, HALF)
    links = [pltpu.SMEM(face_links.shape, jnp.int32), pltpu.SemaphoreType.DMA]
    pad_shape = (3, BRICKS, EDGE + 2, 2 * EDGE, WIDE)
    pad = pltpu.VMEM(pad_shape, BF16)
    high, low, far, near = call(faces_kernel, (face,) * 4, [halves, faces])(cotangent)
    far = swapped(far, 1)
    near = swapped(near, 0)
    band_one = call(band_kernel, shape(*BAND), cost=cost)(conv_one)
    slope, hidden, turned, lifted_pad, band_back, hidden_high, hidden_low, masks = call(
        first_kernel,
        (
            shape(ROWS, HALF, dtype=F32), volume, shape(HALF, ROWS), shape(*pad_shape), shape(*BAND),
            face, face, shape(BRICKS * 6 * 2 * BRICKS, 128, dtype=F32),
        ),
        [pltpu.VMEM((2, 8 * CUBE, 128), F32), pltpu.VMEM((8 * tiles, 128), F32), halves, faces, *links],
        hbm=(0,),
        inputs=5,
    )(face_links, received, up_weight, band_one, conv_two)
    per = -(-BLOCKS // everyone)
    per += per % 2
    sums, lifted, hidden_far, hidden_near = call(
        second_kernel,
        (shape(everyone, per * 8, 128), volume, face, face),
        [pool, pool, pad, pltpu.VMEM((everyone * per * 8, 128), F32)],
        inputs=12,
    )(
        masks, cotangent, band_back, slope, turned, lifted_pad, high, low, far, near,
        hidden_high, hidden_low,
    )
    hidden_far = swapped(hidden_far, 1)
    hidden_near = swapped(hidden_near, 0)
    fine = call(fine_kernel, shape(*cotangent.shape), [pool, pool, pad, band], inputs=8, cost=cost)(
        masks, conv_two, lifted, hidden, hidden_high, hidden_low, hidden_far, hidden_near
    )
    parts = lax.all_to_all(sums, axes, split_axis=0, concat_axis=0, tiled=True)
    scale = 1.0 / math.sqrt(lax.axis_size("dp") * devices * BRICKS * EDGE**3)
    total = call(functools.partial(sum_kernel, scale), shape(*sums.shape), hbm=(1, 2), inputs=3)(
        parts, hidden_far, hidden_near
    )
    gathered = lax.all_to_all(total, axes, split_axis=0, concat_axis=0, tiled=True)
    grads = shape(27, CHANNELS, CHANNELS, dtype=F32)
    block = pltpu.VMEM(grads.shape, F32)
    scratch = [pltpu.VMEM((everyone * per * 8, 128), F32), block, block, pltpu.SemaphoreType.DMA((2, 3))]
    grad_one, grad_two = call(unpack_kernel, (grads, grads), scratch, out=pl.ANY)(gathered)
    return (fine, grad_one, grad_two)


def solution(mesh):
    return jax.shard_map(
        body,
        mesh=mesh,
        in_specs=(
            P("dp", "space", None),
            P("dp", None),
            P("dp", "space", None),
            P("dp", "space", None, None, None),
            P(),
            P(),
            P(),
        ),
        out_specs=(P("dp", "space", None, None, None), P(), P()),
        check_vma=False,
    )
```

```python
import functools
import math

import jax
import jax.numpy as jnp
from jax import lax
from jax.experimental import pallas as pl
from jax.experimental.pallas import tpu as pltpu
from jax.sharding import PartitionSpec as P

BF16 = jnp.bfloat16
F32 = jnp.float32
EDGE = 8
CHANNELS = 32
LINE = EDGE * CHANNELS
HALF = LINE // 2
WIDE = 2 * HALF
BRICKS = 2
CUBE = EDGE * EDGE
LINES = BRICKS * CUBE
BAND = (9, WIDE, HALF)
ROWS = 2 * LINES
FACE = 3 * EDGE
BLOCKS = 54


def dot(left, right):
    return jnp.dot(left, right, preferred_element_type=F32)


def dot_rows(left, right):
    return lax.dot_general(left, right, (((0,), (0,)), ((), ())), preferred_element_type=F32)


def pair(halves_ref, start, count, stride=1):
    index = pl.ds(start, count, stride=stride) if stride > 1 else pl.ds(start, count)
    return halves_ref[0, index, :], halves_ref[1, index, :]


def lanes_of(shape):
    return lax.broadcasted_iota(jnp.int32, shape, len(shape) - 1)


def pick_kernel(scenes, ids_hbm, latents_hbm, out_ref, ids_ref, latents_ref, rows_ref, sems):
    ids_copy = pltpu.make_async_copy(ids_hbm, ids_ref, sems.at[0])
    latents_copy = pltpu.make_async_copy(latents_hbm, latents_ref, sems.at[1])
    ids_copy.start()
    latents_copy.start()
    held, width = latents_ref.shape[1:]
    bricks = ids_ref.shape[1]
    margin = 8 * width // 128
    tiles = width // 128
    rows_ref[0:margin] = jnp.zeros((margin, 128), F32)
    rows_ref[margin + bricks * tiles :] = jnp.zeros((margin, 128), F32)
    first = lax.axis_index("space") * held
    rows = lax.broadcasted_iota(jnp.int32, (held, bricks), 0) + first
    ids_copy.wait()
    hot = jnp.where(rows == ids_ref[...], 1.0, 0.0).astype(BF16)
    latents_copy.wait()
    picked = dot_rows(hot, latents_ref[0])
    for tile in range(tiles):
        rows_ref[pl.ds(margin + tile, bricks, stride=tiles), :] = picked[:, tile * 128 : tile * 128 + 128]
    count = out_ref.shape[1]
    wanted = [jnp.where(lax.axis_index("dp") == scene, 1.0, 0.0).astype(F32) for scene in range(scenes)]
    for receiver in range(out_ref.shape[0] // scenes):
        start = margin + BRICKS * (receiver - 1) * tiles
        found = rows_ref[start : start + count]
        for scene in range(scenes):
            kept = found * wanted[scene] if scenes > 1 else found
            out_ref[receiver * scenes + scene] = kept.astype(BF16)


def build_band(band_ref, rows):
    shape = (3 * CHANNELS, HALF)
    row = lax.broadcasted_iota(jnp.int32, shape, 0)
    target = CHANNELS - (row // CHANNELS) * CHANNELS + row % CHANNELS
    distance = lanes_of(shape) - target
    band_ref[:, HALF:, :] = jnp.zeros((9, HALF, HALF), BF16)
    for z in range(-1, 5):
        select = jnp.where(distance == z * CHANNELS, 1.0, 0.0).astype(BF16)
        block = dot(rows, select).astype(BF16)
        start = z % 8 * CHANNELS
        band_ref[:, start : start + CHANNELS, :] = block.reshape(9, CHANNELS, HALF)


def weight_rows(weights):
    cube = weights.reshape(9, 3, CHANNELS, CHANNELS)
    rows = jnp.concatenate([cube[:, 0], cube[:, 1], cube[:, 2]], axis=-1)
    return rows.reshape(9 * CHANNELS, 3 * CHANNELS).astype(BF16)


def flipped_rows(weights):
    cube = jnp.swapaxes(weights, 1, 2).reshape(9, 3, CHANNELS, CHANNELS)
    pieces = [jnp.concatenate([cube[8 - k, 2], cube[8 - k, 1], cube[8 - k, 0]], axis=-1) for k in range(9)]
    return jnp.concatenate(pieces, axis=0).astype(BF16)


def band_kernel(weights_ref, band_ref):
    build_band(band_ref, weight_rows(weights_ref[...].astype(F32)))


def put_padded(pad_ref, brick, lines, x_low, x_high, y_low, y_high, z_low, z_high):
    def joined(halves, before, after):
        lane = lanes_of(halves[0].shape)
        first = jnp.where(lane < CHANNELS, halves[1], before)
        second = jnp.where(lane >= HALF - CHANNELS, halves[0], after)
        return jnp.concatenate([halves[0], first], axis=-1), jnp.concatenate([halves[1], second], axis=-1)

    inside = joined(lines, z_low, z_high)
    x_low, x_high, y_low, y_high = [joined(face, 0.0, 0.0) for face in (x_low, x_high, y_low, y_high)]
    none = jnp.zeros((1, WIDE), F32)
    shifted = [[], [], []]
    for half in range(2):
        slabs = jnp.concatenate([x_low[half][None], inside[half], x_high[half][None]], axis=0)
        row = lax.broadcasted_iota(jnp.int32, slabs.shape, 1)
        low = jnp.concatenate([none, y_low[half], none], axis=0)[:, None, :]
        high = jnp.concatenate([none, y_high[half], none], axis=0)[:, None, :]
        shifted[0].append(jnp.where(row == 0, low, pltpu.roll(slabs, 1, 1)))
        shifted[1].append(slabs)
        shifted[2].append(jnp.where(row == EDGE - 1, high, pltpu.roll(slabs, EDGE - 1, 1)))
    for dy in range(3):
        pad_ref[dy, brick] = jnp.concatenate(shifted[dy], axis=1).astype(BF16)


def window(pad_ref, k):
    return pad_ref[k % 3, :, k // 3 : k // 3 + EDGE].reshape(ROWS, WIDE)


def convolve(pad_ref, band_ref):
    total = None
    for k in range(9):
        term = dot(window(pad_ref, k), band_ref[k])
        total = term if total is None else total + term
    return total


def half_lines(values):
    cube = values.reshape(BRICKS, EDGE, 2, EDGE, HALF)
    return [(cube[brick, :, 0], cube[brick, :, 1]) for brick in range(BRICKS)]


def put_halves(halves_ref, start, bricks):
    for brick, lines in enumerate(bricks):
        for half in range(2):
            first = start + brick * CUBE
            halves_ref[half, first : first + CUBE, :] = lines[half].reshape(CUBE, HALF)


def cotangent_lines(cotangent_ref):
    cube = cotangent_ref[...].astype(F32).reshape(BRICKS, EDGE, EDGE, LINE)
    return [(cube[brick, :, :, :HALF], cube[brick, :, :, HALF:]) for brick in range(BRICKS)]


def pack_faces(faces_ref, base, halves_ref, start, high):
    x_face = pair(halves_ref, start + ((EDGE - 1) * EDGE if high else 0), EDGE)
    y_face = pair(halves_ref, start + (EDGE - 1 if high else 0), EDGE, EDGE)
    for half in range(2):
        lanes = slice(half * HALF, half * HALF + HALF)
        faces_ref[base : base + EDGE, lanes] = x_face[half]
        faces_ref[base + EDGE : base + 2 * EDGE, lanes] = y_face[half]
    tile = halves_ref[1 if high else 0, start : start + CUBE, :]
    lane = lanes_of((16, 128)) // CHANNELS
    packed = jnp.zeros((16, 128), F32)
    for part in range(4):
        shift = (part + 1 if high else part) % 4 * CHANNELS
        piece = tile[part * 16 : part * 16 + 16]
        packed = jnp.where(lane == part, pltpu.roll(piece, shift, 1) if shift else piece, packed)
    faces_ref[base + 2 * EDGE : base + FACE, :128] = packed[:8]
    faces_ref[base + 2 * EDGE : base + FACE, 128:] = packed[8:]


def pack_all(bricks, halves_ref, faces_ref, high_out, low_out):
    put_halves(halves_ref, 0, bricks)
    for high, out_ref in ((True, high_out), (False, low_out)):
        for brick in range(BRICKS):
            pack_faces(faces_ref, brick * FACE, halves_ref, brick * CUBE, high)
        out_ref[...] = faces_ref[...].astype(BF16)


def to_partners(high_ref, low_ref, far_out, near_out):
    even = lax.axis_index("space") % 2 == 0
    far_out[...] = jnp.where(even, low_ref[...], high_ref[...])
    near_out[...] = jnp.where(even, high_ref[...], low_ref[...])


def faces_kernel(cotangent_ref, high_out, low_out, far_out, near_out, halves_ref, faces_ref):
    pack_all(cotangent_lines(cotangent_ref), halves_ref, faces_ref, high_out, low_out)
    to_partners(high_out, low_out, far_out, near_out)


def unpack_depth(halves, high):
    packed = jnp.concatenate(halves, axis=0)
    pieces = []
    for part in range(4):
        shift = ((3 - part) if high else (4 - part)) % 4 * CHANNELS
        pieces.append(pltpu.roll(packed, shift, 1) if shift else packed)
    return jnp.concatenate(pieces, axis=0).reshape(EDGE, EDGE, 128)


def first_kernel(
    links_in, received_ref, up_ref, band_ref, weights_ref,
    slope_out, hidden_out, turned_out, pad_out, back_out, high_out, low_out, masks_out,
    volumes_ref, rows_ref, halves_ref, faces_ref, links_ref, links_sem,
):
    links_copy = pltpu.make_async_copy(links_in, links_ref, links_sem)
    links_copy.start()
    position = lax.axis_index("space")
    tiles = received_ref.shape[1] // (3 * BRICKS)
    rows_ref[0 : 3 * BRICKS * tiles] = jnp.sum(received_ref[...].astype(F32), axis=0)
    rows_ref[3 * BRICKS * tiles :] = jnp.zeros((2 * tiles, 128), F32)
    cells = []
    for tile in range(tiles):
        rows = rows_ref[pl.ds(tile, 8, stride=tiles), :]
        cells += [rows[:, :64], rows[:, 64:]]
    lifted = dot(jnp.concatenate(cells, axis=0).astype(BF16), up_ref[...])
    lifted = lifted.astype(BF16).astype(F32)
    for cell in range(8):
        a, b, c = cell // 4, cell // 2 % 2, cell % 2
        for sub in range(16):
            line = (4 * a + sub // 4) * EDGE + 4 * b + sub % 4
            volumes_ref[c, pl.ds(line, 8, stride=CUBE), :] = lifted[
                cell * 8 : cell * 8 + 8, sub * 128 : sub * 128 + 128
            ]
    links_copy.wait()
    put_masks(masks_out, links_ref)
    for brick in range(BRICKS):

        def near(face):
            link = links_ref[0, brick, face]
            index = jnp.clip(link - BRICKS * (position - 1), 0, 3 * BRICKS - 1)
            return pl.multiple_of(index * CUBE, CUBE), jnp.where(link >= 0, 1.0, 0.0).astype(F32)

        def x_face(face):
            start, present = near(face)
            offset = EDGE * (EDGE - 1) if face % 2 == 0 else 0
            return [half * present for half in pair(volumes_ref, pl.multiple_of(start + offset, 8), EDGE)]

        def y_face(face):
            start, present = near(face)
            offset = EDGE - 1 if face % 2 == 0 else 0
            return [half * present for half in pair(volumes_ref, start + offset, EDGE, EDGE)]

        def z_face(face):
            start, present = near(face)
            tile = volumes_ref[1 if face % 2 == 0 else 0, pl.ds(start, CUBE), :] * present
            return tile.reshape(EDGE, EDGE, HALF)

        own = pair(volumes_ref, (BRICKS + brick) * CUBE, CUBE)
        own = [half.reshape(EDGE, EDGE, HALF) for half in own]
        put_padded(pad_out, brick, own, x_face(0), x_face(1), y_face(2), y_face(3), z_face(4), z_face(5))
    pre = convolve(pad_out, band_ref)
    sigmoid = 1.0 / (1.0 + jnp.exp(-pre))
    hidden = (pre / (1.0 + jnp.exp(-pre))).astype(BF16)
    slope_out[...] = sigmoid * (1.0 + pre * (1.0 - sigmoid))
    hidden_out[...] = hidden
    hidden = hidden.astype(F32)
    turned_out[...] = jnp.transpose(hidden).astype(BF16)
    pack_all(half_lines(hidden), halves_ref, faces_ref, high_out, low_out)
    build_band(back_out, flipped_rows(weights_ref[...].astype(F32)))


def fold(outer, places):
    lane = lanes_of((CHANNELS, 128)) // CHANNELS
    folded = None
    for block in range(4):
        start, tile = places[block]
        rows = outer[start : start + CHANNELS, tile * 128 : tile * 128 + 128]
        folded = rows if folded is None else jnp.where(lane == block, rows, folded)
    quarter = [folded[8 * q : 8 * q + 8] for q in range(4)]
    small = lanes_of((8, 128)) // CHANNELS
    total = None
    for turn in range(4):
        mixed = quarter[0]
        for q in range(1, 4):
            mixed = jnp.where(small == (q + turn) % 4, quarter[q], mixed)
        if turn:
            mixed = pltpu.roll(mixed, 128 - turn * CHANNELS, 1)
        total = mixed if total is None else total + mixed
    return total


def diagonal(shift):
    places = [None] * 4
    for z in range(4):
        other = z + shift
        places[other % 4] = (z * CHANNELS, 0 if 0 <= other < 4 else 1)
    return places


def put_masks(masks_ref, links_ref):
    position = lax.axis_index("space")
    for brick in range(BRICKS):
        for face in range(6):
            first = links_ref[0, brick, face] - BRICKS * (position - 1 if face % 2 == 0 else position)
            for i in range(2 * BRICKS):
                row = (brick * 6 + face) * 2 * BRICKS + i
                masks_ref[row : row + 1, :] = jnp.full((1, 128), jnp.where(first == i, 1.0, 0.0).astype(F32))


def pad_all(pad_ref, bricks, masks_ref, high_pool, low_pool, high_own, low_own, far, near):
    position = lax.axis_index("space")
    half = BRICKS * FACE
    even = position % 2 == 0
    high_pool[0:half] = jnp.where(even, far[...], near[...]).astype(F32)
    high_pool[half:] = high_own[...].astype(F32)
    low_pool[0:half] = low_own[...].astype(F32)
    low_pool[half:] = jnp.where(even, near[...], far[...]).astype(F32)
    for brick, lines in enumerate(bricks):

        def face(number, axis):
            pool = high_pool if number % 2 == 0 else low_pool
            total = [0.0, 0.0]
            for i in range(2 * BRICKS):
                row = (brick * 6 + number) * 2 * BRICKS + i
                mask = masks_ref[row : row + 1, :]
                start = i * FACE + axis * EDGE
                for part in range(2):
                    found = pool[start : start + EDGE, part * HALF : part * HALF + HALF]
                    total[part] = total[part] + found * mask
            return total

        put_padded(
            pad_ref, brick, lines, face(0, 0), face(1, 0), face(2, 1), face(3, 1),
            unpack_depth(face(4, 2), True), unpack_depth(face(5, 2), False),
        )


def second_kernel(
    masks_ref, cotangent_ref, band_ref, slope_ref, hidden_ref, lifted_pad, high_own, low_own, far, near,
    hidden_high, hidden_low,
    sums_out, lifted_out, far_out, near_out,
    high_pool, low_pool, cotangent_pad, sums_ref,
):
    to_partners(hidden_high, hidden_low, far_out, near_out)
    lifted_out[...] = window(lifted_pad, 4)[:, :HALF]
    bricks = cotangent_lines(cotangent_ref)
    pad_all(cotangent_pad, bricks, masks_ref, high_pool, low_pool, high_own, low_own, far, near)
    gradient = (convolve(cotangent_pad, band_ref) * slope_ref[...]).astype(BF16)
    gradient = jnp.transpose(gradient.astype(F32)).astype(BF16)
    hidden = hidden_ref[...]
    sums_ref[8 * BLOCKS :] = jnp.zeros((sums_ref.shape[0] - 8 * BLOCKS, 128), F32)
    for k in range(9):
        one = dot(gradient, window(lifted_pad, k))
        two = dot(hidden, window(cotangent_pad, 8 - k))
        for part in range(3):
            start = 8 * (3 * k + part)
            sums_ref[start : start + 8] = fold(one, diagonal(part - 1))
            start += 8 * 27
            sums_ref[start : start + 8] = fold(two, diagonal(1 - part))
    sums_out[...] = sums_ref[...].astype(BF16).reshape(sums_out.shape)


def fine_kernel(
    masks_ref, weights_ref, lifted_ref, hidden_ref, high_own, low_own, far, near,
    fine_out, high_pool, low_pool, hidden_pad, band_ref,
):
    build_band(band_ref, weight_rows(weights_ref[...].astype(F32)))
    bricks = half_lines(hidden_ref[...].astype(F32))
    pad_all(hidden_pad, bricks, masks_ref, high_pool, low_pool, high_own, low_own, far, near)
    fine = lifted_ref[...].astype(F32) + convolve(hidden_pad, band_ref)
    fine = fine.reshape(LINES // EDGE, 2, EDGE, HALF)
    fine = jnp.concatenate([fine[:, 0], fine[:, 1]], axis=-1)
    fine_out[...] = fine.astype(BF16).reshape(fine_out.shape)


def unpacked(tile):
    pieces = [tile] + [pltpu.roll(tile, 128 - q * CHANNELS, 1) for q in range(1, 4)]
    return jnp.concatenate(pieces, axis=0)[:, :CHANNELS]


def sum_kernel(scale, parts_ref, _far, _near, out_ref):
    total = jnp.sum(parts_ref[...].astype(F32), axis=0) * scale
    per = parts_ref.shape[1] // 8
    device = lax.axis_index("space") * lax.axis_size("dp") + lax.axis_index("dp")
    tiles = []
    for j in range(per):
        tile = total[8 * j : 8 * j + 8]
        block = jnp.transpose(unpacked(tile))
        turned = jnp.concatenate([block[8 * q : 8 * q + 8] for q in range(4)], axis=1)
        tiles.append(jnp.where(device * per + j < 27, turned, tile))
    total = jnp.concatenate(tiles, axis=0)
    out_ref[...] = jnp.broadcast_to(total.astype(BF16)[None], out_ref.shape)


def unpack_kernel(sums_ref, one_out, two_out, rows_ref, one_ref, two_ref, sems):
    rows_ref[...] = sums_ref[...].astype(F32).reshape(rows_ref.shape)
    copies = []
    for which, (block_ref, out) in enumerate(((one_ref, one_out), (two_ref, two_out))):
        for third in range(3):
            first = 9 * third
            for index in range(first, first + 9):
                row = 8 * (27 * which + index)
                block_ref[index] = unpacked(rows_ref[row : row + 8])
            part = pl.ds(first, 9)
            copies.append(pltpu.make_async_copy(block_ref.at[part], out.at[part], sems.at[which, third]))
            copies[-1].start()
    for copy in copies:
        copy.wait()


def call(kernel, out_shape, scratch=(), hbm=(), inputs=1, limit=24, cost=None, out=pltpu.VMEM):
    spaces = [pl.ANY if i in hbm else pltpu.VMEM for i in range(inputs)]
    return pl.pallas_call(
        kernel,
        out_shape=out_shape,
        in_specs=[pl.BlockSpec(memory_space=space) for space in spaces],
        out_specs=jax.tree.map(lambda _: pl.BlockSpec(memory_space=out), out_shape),
        scratch_shapes=list(scratch),
        compiler_params=pltpu.CompilerParams(vmem_limit_bytes=limit * 2**20),
        cost_estimate=cost,
    )


def inner(*dims, dtype=BF16):
    return pltpu.VMEM(dims, dtype)


def shape(*dims, dtype=BF16):
    return jax.ShapeDtypeStruct(dims, dtype)


def swapped(value, first):
    pairs = [(i, i + 1) for i in range(first, lax.axis_size("space") - 1, 2)]
    return lax.ppermute(value, "space", pairs + [(target, source) for source, target in pairs])


def body(coarse_latents, active_blocks, face_links, cotangent, up_weight, conv_one, conv_two):
    devices = lax.axis_size("space")
    everyone = devices * lax.axis_size("dp")
    held, width = coarse_latents.shape[1:]
    bricks = active_blocks.shape[1]
    tiles = width // 128
    scenes = 2 if lax.axis_size("dp") == 2 else 1
    packed = call(
        functools.partial(pick_kernel, scenes),
        inner(devices * scenes, 3 * BRICKS * tiles, 128),
        [
            pltpu.VMEM((1, bricks), jnp.int32),
            pltpu.VMEM((1, held, width), BF16),
            pltpu.VMEM(((bricks + 16) * tiles, 128), F32),
            pltpu.SemaphoreType.DMA((2,)),
        ],
        hbm=(0, 1),
        inputs=2,
    )(*[pltpu.with_memory_space_constraint(x, pltpu.HBM) for x in (active_blocks, coarse_latents)])
    axes = ("space", "dp")
    received = lax.all_to_all(packed, axes if scenes == 2 else "space", split_axis=0, concat_axis=0, tiled=True)
    band = pltpu.VMEM(BAND, BF16)
    cost = pl.CostEstimate(flops=10**9, bytes_accessed=2 * 10**6, transcendentals=0)
    face = shape(BRICKS * FACE, LINE)
    halves = pltpu.VMEM((2, LINES, HALF), F32)
    faces = pltpu.VMEM((BRICKS * FACE, LINE), F32)
    pool = pltpu.VMEM((2 * BRICKS * FACE, LINE), F32)
    volume = shape(ROWS, HALF)
    links = [pltpu.SMEM(face_links.shape, jnp.int32), pltpu.SemaphoreType.DMA]
    pad_shape = (3, BRICKS, EDGE + 2, 2 * EDGE, WIDE)
    pad = pltpu.VMEM(pad_shape, BF16)
    high, low, far, near = call(faces_kernel, (face,) * 4, [halves, faces])(cotangent)
    far = swapped(far, 1)
    near = swapped(near, 0)
    band_one = call(band_kernel, shape(*BAND), cost=cost)(conv_one)
    slope, hidden, turned, lifted_pad, band_back, hidden_high, hidden_low, masks = call(
        first_kernel,
        (
            shape(ROWS, HALF, dtype=F32), volume, shape(HALF, ROWS), shape(*pad_shape), shape(*BAND),
            face, face, shape(BRICKS * 6 * 2 * BRICKS, 128, dtype=F32),
        ),
        [pltpu.VMEM((2, 8 * CUBE, 128), F32), pltpu.VMEM((8 * tiles, 128), F32), halves, faces, *links],
        hbm=(0,),
        inputs=5,
    )(face_links, received, up_weight, band_one, conv_two)
    per = -(-BLOCKS // everyone)
    per += per % 2
    sums, lifted, hidden_far, hidden_near = call(
        second_kernel,
        (inner(everyone, per * 8, 128), volume, face, face),
        [pool, pool, pad, pltpu.VMEM((everyone * per * 8, 128), F32)],
        inputs=12,
    )(
        masks, cotangent, band_back, slope, turned, lifted_pad, high, low, far, near,
        hidden_high, hidden_low,
    )
    hidden_far = swapped(hidden_far, 1)
    hidden_near = swapped(hidden_near, 0)
    fine = call(fine_kernel, shape(*cotangent.shape), [pool, pool, pad, band], inputs=8, cost=cost)(
        masks, conv_two, lifted, hidden, hidden_high, hidden_low, hidden_far, hidden_near
    )
    parts = lax.all_to_all(sums, axes, split_axis=0, concat_axis=0, tiled=True)
    scale = 1.0 / math.sqrt(lax.axis_size("dp") * devices * BRICKS * EDGE**3)
    total = call(functools.partial(sum_kernel, scale), inner(*sums.shape), hbm=(1, 2), inputs=3)(
        parts, hidden_far, hidden_near
    )
    gathered = lax.all_to_all(total, axes, split_axis=0, concat_axis=0, tiled=True)
    grads = shape(27, CHANNELS, CHANNELS, dtype=F32)
    block = pltpu.VMEM(grads.shape, F32)
    scratch = [pltpu.VMEM((everyone * per * 8, 128), F32), block, block, pltpu.SemaphoreType.DMA((2, 3))]
    grad_one, grad_two = call(unpack_kernel, (grads, grads), scratch, out=pl.ANY)(gathered)
    return (fine, grad_one, grad_two)


def solution(mesh):
    return jax.shard_map(
        body,
        mesh=mesh,
        in_specs=(
            P("dp", "space", None),
            P("dp", None),
            P("dp", "space", None),
            P("dp", "space", None, None, None),
            P(),
            P(),
            P(),
        ),
        out_specs=(P("dp", "space", None, None, None), P(), P()),
        check_vma=False,
    )
```

```python
import functools
import math

import jax
import jax.numpy as jnp
from jax import lax
from jax.experimental import pallas as pl
from jax.experimental.pallas import tpu as pltpu
from jax.sharding import PartitionSpec as P

BF16 = jnp.bfloat16
F32 = jnp.float32
EDGE = 8
CHANNELS = 32
LINE = EDGE * CHANNELS
HALF = LINE // 2
WIDE = 2 * HALF
BRICKS = 2
CUBE = EDGE * EDGE
LINES = BRICKS * CUBE
BAND = (9, WIDE, HALF)
ROWS = 2 * LINES
FACE = 3 * EDGE
BLOCKS = 54


def dot(left, right):
    return jnp.dot(left, right, preferred_element_type=F32)


def dot_rows(left, right):
    return lax.dot_general(left, right, (((0,), (0,)), ((), ())), preferred_element_type=F32)


def pair(halves_ref, start, count, stride=1):
    index = pl.ds(start, count, stride=stride) if stride > 1 else pl.ds(start, count)
    return halves_ref[0, index, :], halves_ref[1, index, :]


def lanes_of(shape):
    return lax.broadcasted_iota(jnp.int32, shape, len(shape) - 1)


def pick_kernel(scenes, ids_hbm, latents_hbm, out_ref, ids_ref, latents_ref, rows_ref, sems):
    ids_copy = pltpu.make_async_copy(ids_hbm, ids_ref, sems.at[0])
    latents_copy = pltpu.make_async_copy(latents_hbm, latents_ref, sems.at[1])
    ids_copy.start()
    latents_copy.start()
    held, width = latents_ref.shape[1:]
    bricks = ids_ref.shape[1]
    margin = 8 * width // 128
    tiles = width // 128
    rows_ref[0:margin] = jnp.zeros((margin, 128), F32)
    rows_ref[margin + bricks * tiles :] = jnp.zeros((margin, 128), F32)
    first = lax.axis_index("space") * held
    rows = lax.broadcasted_iota(jnp.int32, (held, bricks), 0) + first
    ids_copy.wait()
    hot = jnp.where(rows == ids_ref[...], 1.0, 0.0).astype(BF16)
    latents_copy.wait()
    picked = dot_rows(hot, latents_ref[0])
    for tile in range(tiles):
        rows_ref[pl.ds(margin + tile, bricks, stride=tiles), :] = picked[:, tile * 128 : tile * 128 + 128]
    count = out_ref.shape[1]
    wanted = [jnp.where(lax.axis_index("dp") == scene, 1.0, 0.0).astype(F32) for scene in range(scenes)]
    for receiver in range(out_ref.shape[0] // scenes):
        start = margin + BRICKS * (receiver - 1) * tiles
        found = rows_ref[start : start + count]
        for scene in range(scenes):
            kept = found * wanted[scene] if scenes > 1 else found
            out_ref[receiver * scenes + scene] = kept.astype(BF16)


def build_band(band_ref, rows):
    shape = (3 * CHANNELS, HALF)
    row = lax.broadcasted_iota(jnp.int32, shape, 0)
    target = CHANNELS - (row // CHANNELS) * CHANNELS + row % CHANNELS
    distance = lanes_of(shape) - target
    band_ref[:, HALF:, :] = jnp.zeros((9, HALF, HALF), BF16)
    for z in range(-1, 5):
        select = jnp.where(distance == z * CHANNELS, 1.0, 0.0).astype(BF16)
        block = dot(rows, select).astype(BF16)
        start = z % 8 * CHANNELS
        band_ref[:, start : start + CHANNELS, :] = block.reshape(9, CHANNELS, HALF)


def weight_rows(weights):
    cube = weights.reshape(9, 3, CHANNELS, CHANNELS)
    rows = jnp.concatenate([cube[:, 0], cube[:, 1], cube[:, 2]], axis=-1)
    return rows.reshape(9 * CHANNELS, 3 * CHANNELS).astype(BF16)


def flipped_rows(weights):
    cube = jnp.swapaxes(weights, 1, 2).reshape(9, 3, CHANNELS, CHANNELS)
    pieces = [jnp.concatenate([cube[8 - k, 2], cube[8 - k, 1], cube[8 - k, 0]], axis=-1) for k in range(9)]
    return jnp.concatenate(pieces, axis=0).astype(BF16)


def band_kernel(weights_ref, band_ref):
    build_band(band_ref, weight_rows(weights_ref[...].astype(F32)))


def put_padded(pad_ref, brick, lines, x_low, x_high, y_low, y_high, z_low, z_high):
    def joined(halves, before, after):
        lane = lanes_of(halves[0].shape)
        first = jnp.where(lane < CHANNELS, halves[1], before)
        second = jnp.where(lane >= HALF - CHANNELS, halves[0], after)
        return jnp.concatenate([halves[0], first], axis=-1), jnp.concatenate([halves[1], second], axis=-1)

    inside = joined(lines, z_low, z_high)
    x_low, x_high, y_low, y_high = [joined(face, 0.0, 0.0) for face in (x_low, x_high, y_low, y_high)]
    none = jnp.zeros((1, WIDE), F32)
    shifted = [[], [], []]
    for half in range(2):
        slabs = jnp.concatenate([x_low[half][None], inside[half], x_high[half][None]], axis=0)
        row = lax.broadcasted_iota(jnp.int32, slabs.shape, 1)
        low = jnp.concatenate([none, y_low[half], none], axis=0)[:, None, :]
        high = jnp.concatenate([none, y_high[half], none], axis=0)[:, None, :]
        shifted[0].append(jnp.where(row == 0, low, pltpu.roll(slabs, 1, 1)))
        shifted[1].append(slabs)
        shifted[2].append(jnp.where(row == EDGE - 1, high, pltpu.roll(slabs, EDGE - 1, 1)))
    for dy in range(3):
        pad_ref[dy, brick] = jnp.concatenate(shifted[dy], axis=1).astype(BF16)


def window(pad_ref, k):
    return pad_ref[k % 3, :, k // 3 : k // 3 + EDGE].reshape(ROWS, WIDE)


def convolve(pad_ref, band_ref):
    total = None
    for k in range(9):
        term = dot(window(pad_ref, k), band_ref[k])
        total = term if total is None else total + term
    return total


def half_lines(values):
    cube = values.reshape(BRICKS, EDGE, 2, EDGE, HALF)
    return [(cube[brick, :, 0], cube[brick, :, 1]) for brick in range(BRICKS)]


def put_halves(halves_ref, start, bricks):
    for brick, lines in enumerate(bricks):
        for half in range(2):
            first = start + brick * CUBE
            halves_ref[half, first : first + CUBE, :] = lines[half].reshape(CUBE, HALF)


def cotangent_lines(cotangent_ref):
    cube = cotangent_ref[...].astype(F32).reshape(BRICKS, EDGE, EDGE, LINE)
    return [(cube[brick, :, :, :HALF], cube[brick, :, :, HALF:]) for brick in range(BRICKS)]


def pack_faces(faces_ref, base, halves_ref, start, high):
    x_face = pair(halves_ref, start + ((EDGE - 1) * EDGE if high else 0), EDGE)
    y_face = pair(halves_ref, start + (EDGE - 1 if high else 0), EDGE, EDGE)
    for half in range(2):
        lanes = slice(half * HALF, half * HALF + HALF)
        faces_ref[base : base + EDGE, lanes] = x_face[half]
        faces_ref[base + EDGE : base + 2 * EDGE, lanes] = y_face[half]
    tile = halves_ref[1 if high else 0, start : start + CUBE, :]
    lane = lanes_of((16, 128)) // CHANNELS
    packed = jnp.zeros((16, 128), F32)
    for part in range(4):
        shift = (part + 1 if high else part) % 4 * CHANNELS
        piece = tile[part * 16 : part * 16 + 16]
        packed = jnp.where(lane == part, pltpu.roll(piece, shift, 1) if shift else piece, packed)
    faces_ref[base + 2 * EDGE : base + FACE, :128] = packed[:8]
    faces_ref[base + 2 * EDGE : base + FACE, 128:] = packed[8:]


def pack_all(bricks, halves_ref, faces_ref, high_out, low_out):
    put_halves(halves_ref, 0, bricks)
    for high, out_ref in ((True, high_out), (False, low_out)):
        for brick in range(BRICKS):
            pack_faces(faces_ref, brick * FACE, halves_ref, brick * CUBE, high)
        out_ref[...] = faces_ref[...].astype(BF16)


def to_partners(high_ref, low_ref, far_out, near_out):
    even = lax.axis_index("space") % 2 == 0
    far_out[...] = jnp.where(even, low_ref[...], high_ref[...])
    near_out[...] = jnp.where(even, high_ref[...], low_ref[...])


def faces_kernel(cotangent_ref, high_out, low_out, far_out, near_out, halves_ref, faces_ref):
    pack_all(cotangent_lines(cotangent_ref), halves_ref, faces_ref, high_out, low_out)
    to_partners(high_out, low_out, far_out, near_out)


def unpack_depth(halves, high):
    packed = jnp.concatenate(halves, axis=0)
    pieces = []
    for part in range(4):
        shift = ((3 - part) if high else (4 - part)) % 4 * CHANNELS
        pieces.append(pltpu.roll(packed, shift, 1) if shift else packed)
    return jnp.concatenate(pieces, axis=0).reshape(EDGE, EDGE, 128)


def first_kernel(
    links_in, received_ref, up_ref, band_ref, weights_ref,
    slope_out, hidden_out, turned_out, pad_out, back_out, high_out, low_out, masks_out,
    volumes_ref, rows_ref, halves_ref, faces_ref, links_ref, links_sem,
):
    links_copy = pltpu.make_async_copy(links_in, links_ref, links_sem)
    links_copy.start()
    position = lax.axis_index("space")
    tiles = received_ref.shape[1] // (3 * BRICKS)
    rows_ref[0 : 3 * BRICKS * tiles] = jnp.sum(received_ref[...].astype(F32), axis=0)
    rows_ref[3 * BRICKS * tiles :] = jnp.zeros((2 * tiles, 128), F32)
    cells = []
    for tile in range(tiles):
        rows = rows_ref[pl.ds(tile, 8, stride=tiles), :]
        cells += [rows[:, :64], rows[:, 64:]]
    lifted = dot(jnp.concatenate(cells, axis=0).astype(BF16), up_ref[...])
    lifted = lifted.astype(BF16).astype(F32)
    for cell in range(8):
        a, b, c = cell // 4, cell // 2 % 2, cell % 2
        for sub in range(16):
            line = (4 * a + sub // 4) * EDGE + 4 * b + sub % 4
            volumes_ref[c, pl.ds(line, 8, stride=CUBE), :] = lifted[
                cell * 8 : cell * 8 + 8, sub * 128 : sub * 128 + 128
            ]
    links_copy.wait()
    put_masks(masks_out, links_ref)
    for brick in range(BRICKS):

        def near(face):
            link = links_ref[0, brick, face]
            index = jnp.clip(link - BRICKS * (position - 1), 0, 3 * BRICKS - 1)
            return pl.multiple_of(index * CUBE, CUBE), jnp.where(link >= 0, 1.0, 0.0).astype(F32)

        def x_face(face):
            start, present = near(face)
            offset = EDGE * (EDGE - 1) if face % 2 == 0 else 0
            return [half * present for half in pair(volumes_ref, pl.multiple_of(start + offset, 8), EDGE)]

        def y_face(face):
            start, present = near(face)
            offset = EDGE - 1 if face % 2 == 0 else 0
            return [half * present for half in pair(volumes_ref, start + offset, EDGE, EDGE)]

        def z_face(face):
            start, present = near(face)
            tile = volumes_ref[1 if face % 2 == 0 else 0, pl.ds(start, CUBE), :] * present
            return tile.reshape(EDGE, EDGE, HALF)

        own = pair(volumes_ref, (BRICKS + brick) * CUBE, CUBE)
        own = [half.reshape(EDGE, EDGE, HALF) for half in own]
        put_padded(pad_out, brick, own, x_face(0), x_face(1), y_face(2), y_face(3), z_face(4), z_face(5))
    pre = convolve(pad_out, band_ref)
    sigmoid = 1.0 / (1.0 + jnp.exp(-pre))
    hidden = (pre / (1.0 + jnp.exp(-pre))).astype(BF16)
    slope_out[...] = sigmoid * (1.0 + pre * (1.0 - sigmoid))
    hidden_out[...] = hidden
    hidden = hidden.astype(F32)
    turned_out[...] = jnp.transpose(hidden).astype(BF16)
    pack_all(half_lines(hidden), halves_ref, faces_ref, high_out, low_out)
    build_band(back_out, flipped_rows(weights_ref[...].astype(F32)))


def fold(outer, places):
    lane = lanes_of((CHANNELS, 128)) // CHANNELS
    folded = None
    for block in range(4):
        start, tile = places[block]
        rows = outer[start : start + CHANNELS, tile * 128 : tile * 128 + 128]
        folded = rows if folded is None else jnp.where(lane == block, rows, folded)
    quarter = [folded[8 * q : 8 * q + 8] for q in range(4)]
    small = lanes_of((8, 128)) // CHANNELS
    total = None
    for turn in range(4):
        mixed = quarter[0]
        for q in range(1, 4):
            mixed = jnp.where(small == (q + turn) % 4, quarter[q], mixed)
        if turn:
            mixed = pltpu.roll(mixed, 128 - turn * CHANNELS, 1)
        total = mixed if total is None else total + mixed
    return total


def diagonal(shift):
    places = [None] * 4
    for z in range(4):
        other = z + shift
        places[other % 4] = (z * CHANNELS, 0 if 0 <= other < 4 else 1)
    return places


def put_masks(masks_ref, links_ref):
    position = lax.axis_index("space")
    for brick in range(BRICKS):
        for face in range(6):
            first = links_ref[0, brick, face] - BRICKS * (position - 1 if face % 2 == 0 else position)
            for i in range(2 * BRICKS):
                row = (brick * 6 + face) * 2 * BRICKS + i
                masks_ref[row : row + 1, :] = jnp.full((1, 128), jnp.where(first == i, 1.0, 0.0).astype(F32))


def pad_all(pad_ref, bricks, masks_ref, high_pool, low_pool, high_own, low_own, far, near):
    position = lax.axis_index("space")
    half = BRICKS * FACE
    even = position % 2 == 0
    high_pool[0:half] = jnp.where(even, far[...], near[...]).astype(F32)
    high_pool[half:] = high_own[...].astype(F32)
    low_pool[0:half] = low_own[...].astype(F32)
    low_pool[half:] = jnp.where(even, near[...], far[...]).astype(F32)
    for brick, lines in enumerate(bricks):

        def face(number, axis):
            pool = high_pool if number % 2 == 0 else low_pool
            total = [0.0, 0.0]
            for i in range(2 * BRICKS):
                row = (brick * 6 + number) * 2 * BRICKS + i
                mask = masks_ref[row : row + 1, :]
                start = i * FACE + axis * EDGE
                for part in range(2):
                    found = pool[start : start + EDGE, part * HALF : part * HALF + HALF]
                    total[part] = total[part] + found * mask
            return total

        put_padded(
            pad_ref, brick, lines, face(0, 0), face(1, 0), face(2, 1), face(3, 1),
            unpack_depth(face(4, 2), True), unpack_depth(face(5, 2), False),
        )


def second_kernel(
    masks_ref, cotangent_ref, band_ref, slope_ref, hidden_ref, lifted_pad, high_own, low_own, far, near,
    hidden_high, hidden_low,
    sums_out, lifted_out, far_out, near_out,
    high_pool, low_pool, cotangent_pad, sums_ref,
):
    to_partners(hidden_high, hidden_low, far_out, near_out)
    lifted_out[...] = window(lifted_pad, 4)[:, :HALF]
    bricks = cotangent_lines(cotangent_ref)
    pad_all(cotangent_pad, bricks, masks_ref, high_pool, low_pool, high_own, low_own, far, near)
    gradient = (convolve(cotangent_pad, band_ref) * slope_ref[...]).astype(BF16)
    gradient = jnp.transpose(gradient.astype(F32)).astype(BF16)
    hidden = hidden_ref[...]
    sums_ref[8 * BLOCKS :] = jnp.zeros((sums_ref.shape[0] - 8 * BLOCKS, 128), F32)
    for k in range(9):
        one = dot(gradient, window(lifted_pad, k))
        two = dot(hidden, window(cotangent_pad, 8 - k))
        for part in range(3):
            start = 8 * (3 * k + part)
            sums_ref[start : start + 8] = fold(one, diagonal(part - 1))
            start += 8 * 27
            sums_ref[start : start + 8] = fold(two, diagonal(1 - part))
    sums_out[...] = sums_ref[...].astype(BF16).reshape(sums_out.shape)


def unpacked(tile):
    pieces = [tile] + [pltpu.roll(tile, 128 - q * CHANNELS, 1) for q in range(1, 4)]
    return jnp.concatenate(pieces, axis=0)[:, :CHANNELS]


def third_kernel(
    scale, masks_ref, band_ref, lifted_ref, hidden_ref, high_own, low_own, far, near, parts_ref,
    fine_out, sums_out,
    high_pool, low_pool, hidden_pad, fine_ref, fine_sem,
):
    bricks = half_lines(hidden_ref[...].astype(F32))
    pad_all(hidden_pad, bricks, masks_ref, high_pool, low_pool, high_own, low_own, far, near)
    fine = lifted_ref[...].astype(F32) + convolve(hidden_pad, band_ref)
    fine = fine.reshape(LINES // EDGE, 2, EDGE, HALF)
    fine = jnp.concatenate([fine[:, 0], fine[:, 1]], axis=-1)
    fine_ref[...] = fine.astype(BF16).reshape(fine_ref.shape)
    fine_copy = pltpu.make_async_copy(fine_ref, fine_out, fine_sem)
    fine_copy.start()
    total = jnp.sum(parts_ref[...].astype(F32), axis=0) * scale
    per = parts_ref.shape[1] // 8
    device = lax.axis_index("space") * lax.axis_size("dp") + lax.axis_index("dp")
    tiles = []
    for j in range(per):
        tile = total[8 * j : 8 * j + 8]
        block = jnp.transpose(unpacked(tile))
        turned = jnp.concatenate([block[8 * q : 8 * q + 8] for q in range(4)], axis=1)
        tiles.append(jnp.where(device * per + j < 27, turned, tile))
    total = jnp.concatenate(tiles, axis=0)
    sums_out[...] = jnp.broadcast_to(total.astype(BF16)[None], sums_out.shape)
    fine_copy.wait()


def unpack_kernel(sums_ref, one_out, two_out, rows_ref, one_ref, two_ref, sems):
    rows_ref[...] = sums_ref[...].astype(F32).reshape(rows_ref.shape)
    copies = []
    for which, (block_ref, out) in enumerate(((one_ref, one_out), (two_ref, two_out))):
        for third in range(3):
            first = 9 * third
            for index in range(first, first + 9):
                row = 8 * (27 * which + index)
                block_ref[index] = unpacked(rows_ref[row : row + 8])
            part = pl.ds(first, 9)
            copies.append(pltpu.make_async_copy(block_ref.at[part], out.at[part], sems.at[which, third]))
            copies[-1].start()
    for copy in copies:
        copy.wait()


def call(kernel, out_shape, scratch=(), hbm=(), inputs=1, limit=24, cost=None, out=None):
    spaces = [pl.ANY if i in hbm else pltpu.VMEM for i in range(inputs)]
    out = out or jax.tree.map(lambda _: pltpu.VMEM, out_shape)
    return pl.pallas_call(
        kernel,
        out_shape=out_shape,
        in_specs=[pl.BlockSpec(memory_space=space) for space in spaces],
        out_specs=jax.tree.map(lambda space: pl.BlockSpec(memory_space=space), out),
        scratch_shapes=list(scratch),
        compiler_params=pltpu.CompilerParams(vmem_limit_bytes=limit * 2**20),
        cost_estimate=cost,
    )


def shape(*dims, dtype=BF16):
    return jax.ShapeDtypeStruct(dims, dtype)


def swapped(value, first):
    pairs = [(i, i + 1) for i in range(first, lax.axis_size("space") - 1, 2)]
    return lax.ppermute(value, "space", pairs + [(target, source) for source, target in pairs])


def body(coarse_latents, active_blocks, face_links, cotangent, up_weight, conv_one, conv_two):
    devices = lax.axis_size("space")
    everyone = devices * lax.axis_size("dp")
    held, width = coarse_latents.shape[1:]
    bricks = active_blocks.shape[1]
    tiles = width // 128
    scenes = 2 if lax.axis_size("dp") == 2 else 1
    packed = call(
        functools.partial(pick_kernel, scenes),
        shape(devices * scenes, 3 * BRICKS * tiles, 128),
        [
            pltpu.VMEM((1, bricks), jnp.int32),
            pltpu.VMEM((1, held, width), BF16),
            pltpu.VMEM(((bricks + 16) * tiles, 128), F32),
            pltpu.SemaphoreType.DMA((2,)),
        ],
        hbm=(0, 1),
        inputs=2,
        limit=60,
    )(active_blocks, coarse_latents)
    axes = ("space", "dp")
    received = lax.all_to_all(packed, axes if scenes == 2 else "space", split_axis=0, concat_axis=0, tiled=True)
    band = pltpu.VMEM(BAND, BF16)
    cost = pl.CostEstimate(flops=10**9, bytes_accessed=2 * 10**6, transcendentals=0)
    face = shape(BRICKS * FACE, LINE)
    halves = pltpu.VMEM((2, LINES, HALF), F32)
    faces = pltpu.VMEM((BRICKS * FACE, LINE), F32)
    pool = pltpu.VMEM((2 * BRICKS * FACE, LINE), F32)
    volume = shape(ROWS, HALF)
    links = [pltpu.SMEM(face_links.shape, jnp.int32), pltpu.SemaphoreType.DMA]
    pad_shape = (3, BRICKS, EDGE + 2, 2 * EDGE, WIDE)
    pad = pltpu.VMEM(pad_shape, BF16)
    high, low, far, near = call(faces_kernel, (face,) * 4, [halves, faces])(cotangent)
    far = swapped(far, 1)
    near = swapped(near, 0)
    band_one = call(band_kernel, shape(*BAND), cost=cost)(conv_one)
    slope, hidden, turned, lifted_pad, band_back, hidden_high, hidden_low, masks = call(
        first_kernel,
        (
            shape(ROWS, HALF, dtype=F32), volume, shape(HALF, ROWS), shape(*pad_shape), shape(*BAND),
            face, face, shape(BRICKS * 6 * 2 * BRICKS, 128, dtype=F32),
        ),
        [pltpu.VMEM((2, 8 * CUBE, 128), F32), pltpu.VMEM((8 * tiles, 128), F32), halves, faces, *links],
        hbm=(0,),
        inputs=5,
    )(face_links, received, up_weight, band_one, conv_two)
    per = -(-BLOCKS // everyone)
    per += per % 2
    sums, lifted, hidden_far, hidden_near = call(
        second_kernel,
        (shape(everyone, per * 8, 128), volume, face, face),
        [pool, pool, pad, pltpu.VMEM((everyone * per * 8, 128), F32)],
        inputs=12,
    )(
        masks, cotangent, band_back, slope, turned, lifted_pad, high, low, far, near,
        hidden_high, hidden_low,
    )
    hidden_far = swapped(hidden_far, 1)
    hidden_near = swapped(hidden_near, 0)
    band_two = call(band_kernel, shape(*BAND), cost=cost)(conv_two)
    parts = lax.all_to_all(sums, axes, split_axis=0, concat_axis=0, tiled=True)
    scale = 1.0 / math.sqrt(lax.axis_size("dp") * devices * BRICKS * EDGE**3)
    fine, total = call(
        functools.partial(third_kernel, scale),
        (shape(*cotangent.shape), shape(*sums.shape)),
        [pool, pool, pad, pltpu.VMEM(cotangent.shape, BF16), pltpu.SemaphoreType.DMA],
        inputs=9,
        out=(pl.ANY, pltpu.VMEM),
    )(masks, band_two, lifted, hidden, hidden_high, hidden_low, hidden_far, hidden_near, parts)
    gathered = lax.all_to_all(total, axes, split_axis=0, concat_axis=0, tiled=True)
    grads = shape(27, CHANNELS, CHANNELS, dtype=F32)
    block = pltpu.VMEM(grads.shape, F32)
    scratch = [pltpu.VMEM((everyone * per * 8, 128), F32), block, block, pltpu.SemaphoreType.DMA((2, 3))]
    grad_one, grad_two = call(unpack_kernel, (grads, grads), scratch, out=(pl.ANY, pl.ANY))(gathered)
    return (fine, grad_one, grad_two)


def solution(mesh):
    return jax.shard_map(
        body,
        mesh=mesh,
        in_specs=(
            P("dp", "space", None),
            P("dp", None),
            P("dp", "space", None),
            P("dp", "space", None, None, None),
            P(),
            P(),
            P(),
        ),
        out_specs=(P("dp", "space", None, None, None), P(), P()),
        check_vma=False,
    )
```

```python
import functools
import math

import jax
import jax.numpy as jnp
from jax import lax
from jax.experimental import pallas as pl
from jax.experimental.pallas import tpu as pltpu
from jax.sharding import PartitionSpec as P

BF16 = jnp.bfloat16
F32 = jnp.float32
EDGE = 8
CHANNELS = 32
LINE = EDGE * CHANNELS
HALF = LINE // 2
WIDE = 2 * HALF
BRICKS = 2
CUBE = EDGE * EDGE
LINES = BRICKS * CUBE
BAND = (9, WIDE, HALF)
ROWS = 2 * LINES
FACE = 3 * EDGE
BLOCKS = 54


def dot(left, right):
    return jnp.dot(left, right, preferred_element_type=F32)


def dot_rows(left, right):
    return lax.dot_general(left, right, (((0,), (0,)), ((), ())), preferred_element_type=F32)


def pair(halves_ref, start, count, stride=1):
    index = pl.ds(start, count, stride=stride) if stride > 1 else pl.ds(start, count)
    return halves_ref[0, index, :], halves_ref[1, index, :]


def lanes_of(shape):
    return lax.broadcasted_iota(jnp.int32, shape, len(shape) - 1)


def pick_kernel(scenes, ids_hbm, latents_hbm, out_ref, ids_ref, latents_ref, rows_ref, sems):
    ids_copy = pltpu.make_async_copy(ids_hbm, ids_ref, sems.at[0])
    latents_copy = pltpu.make_async_copy(latents_hbm, latents_ref, sems.at[1])
    ids_copy.start()
    latents_copy.start()
    held, width = latents_ref.shape[1:]
    bricks = ids_ref.shape[1]
    margin = 8 * width // 128
    tiles = width // 128
    rows_ref[0:margin] = jnp.zeros((margin, 128), F32)
    rows_ref[margin + bricks * tiles :] = jnp.zeros((margin, 128), F32)
    first = lax.axis_index("space") * held
    rows = lax.broadcasted_iota(jnp.int32, (held, bricks), 0) + first
    ids_copy.wait()
    hot = jnp.where(rows == ids_ref[...], 1.0, 0.0).astype(BF16)
    latents_copy.wait()
    picked = dot_rows(hot, latents_ref[0])
    for tile in range(tiles):
        rows_ref[pl.ds(margin + tile, bricks, stride=tiles), :] = picked[:, tile * 128 : tile * 128 + 128]
    count = out_ref.shape[1]
    wanted = [jnp.where(lax.axis_index("dp") == scene, 1.0, 0.0).astype(F32) for scene in range(scenes)]
    for receiver in range(out_ref.shape[0] // scenes):
        start = margin + BRICKS * (receiver - 1) * tiles
        found = rows_ref[start : start + count]
        for scene in range(scenes):
            kept = found * wanted[scene] if scenes > 1 else found
            out_ref[receiver * scenes + scene] = kept.astype(BF16)


def build_band(band_ref, rows):
    shape = (3 * CHANNELS, HALF)
    row = lax.broadcasted_iota(jnp.int32, shape, 0)
    target = CHANNELS - (row // CHANNELS) * CHANNELS + row % CHANNELS
    distance = lanes_of(shape) - target
    band_ref[:, HALF:, :] = jnp.zeros((9, HALF, HALF), BF16)
    for z in range(-1, 5):
        select = jnp.where(distance == z * CHANNELS, 1.0, 0.0).astype(BF16)
        block = dot(rows, select).astype(BF16)
        start = z % 8 * CHANNELS
        band_ref[:, start : start + CHANNELS, :] = block.reshape(9, CHANNELS, HALF)


def weight_rows(weights):
    cube = weights.reshape(9, 3, CHANNELS, CHANNELS)
    rows = jnp.concatenate([cube[:, 0], cube[:, 1], cube[:, 2]], axis=-1)
    return rows.reshape(9 * CHANNELS, 3 * CHANNELS).astype(BF16)


def flipped_rows(weights):
    cube = jnp.swapaxes(weights, 1, 2).reshape(9, 3, CHANNELS, CHANNELS)
    pieces = [jnp.concatenate([cube[8 - k, 2], cube[8 - k, 1], cube[8 - k, 0]], axis=-1) for k in range(9)]
    return jnp.concatenate(pieces, axis=0).astype(BF16)


def band_kernel(weights_ref, band_ref):
    build_band(band_ref, weight_rows(weights_ref[...].astype(F32)))


def put_padded(pad_ref, brick, lines, x_low, x_high, y_low, y_high, z_low, z_high):
    def joined(halves, before, after):
        lane = lanes_of(halves[0].shape)
        first = jnp.where(lane < CHANNELS, halves[1], before)
        second = jnp.where(lane >= HALF - CHANNELS, halves[0], after)
        return jnp.concatenate([halves[0], first], axis=-1), jnp.concatenate([halves[1], second], axis=-1)

    inside = joined(lines, z_low, z_high)
    x_low, x_high, y_low, y_high = [joined(face, 0.0, 0.0) for face in (x_low, x_high, y_low, y_high)]
    none = jnp.zeros((1, WIDE), F32)
    shifted = [[], [], []]
    for half in range(2):
        slabs = jnp.concatenate([x_low[half][None], inside[half], x_high[half][None]], axis=0)
        row = lax.broadcasted_iota(jnp.int32, slabs.shape, 1)
        low = jnp.concatenate([none, y_low[half], none], axis=0)[:, None, :]
        high = jnp.concatenate([none, y_high[half], none], axis=0)[:, None, :]
        shifted[0].append(jnp.where(row == 0, low, pltpu.roll(slabs, 1, 1)))
        shifted[1].append(slabs)
        shifted[2].append(jnp.where(row == EDGE - 1, high, pltpu.roll(slabs, EDGE - 1, 1)))
    for dy in range(3):
        pad_ref[dy, brick] = jnp.concatenate(shifted[dy], axis=1).astype(BF16)


def window(pad_ref, k):
    return pad_ref[k % 3, :, k // 3 : k // 3 + EDGE].reshape(ROWS, WIDE)


def convolve(pad_ref, band_ref):
    total = None
    for k in range(9):
        term = dot(window(pad_ref, k), band_ref[k])
        total = term if total is None else total + term
    return total


def half_lines(values):
    cube = values.reshape(BRICKS, EDGE, 2, EDGE, HALF)
    return [(cube[brick, :, 0], cube[brick, :, 1]) for brick in range(BRICKS)]


def put_halves(halves_ref, start, bricks):
    for brick, lines in enumerate(bricks):
        for half in range(2):
            first = start + brick * CUBE
            halves_ref[half, first : first + CUBE, :] = lines[half].reshape(CUBE, HALF)


def cotangent_lines(cotangent_ref):
    cube = cotangent_ref[...].astype(F32).reshape(BRICKS, EDGE, EDGE, LINE)
    return [(cube[brick, :, :, :HALF], cube[brick, :, :, HALF:]) for brick in range(BRICKS)]


def pack_faces(faces_ref, base, halves_ref, start, high):
    x_face = pair(halves_ref, start + ((EDGE - 1) * EDGE if high else 0), EDGE)
    y_face = pair(halves_ref, start + (EDGE - 1 if high else 0), EDGE, EDGE)
    for half in range(2):
        lanes = slice(half * HALF, half * HALF + HALF)
        faces_ref[base : base + EDGE, lanes] = x_face[half]
        faces_ref[base + EDGE : base + 2 * EDGE, lanes] = y_face[half]
    tile = halves_ref[1 if high else 0, start : start + CUBE, :]
    lane = lanes_of((16, 128)) // CHANNELS
    packed = jnp.zeros((16, 128), F32)
    for part in range(4):
        shift = (part + 1 if high else part) % 4 * CHANNELS
        piece = tile[part * 16 : part * 16 + 16]
        packed = jnp.where(lane == part, pltpu.roll(piece, shift, 1) if shift else piece, packed)
    faces_ref[base + 2 * EDGE : base + FACE, :128] = packed[:8]
    faces_ref[base + 2 * EDGE : base + FACE, 128:] = packed[8:]


def pack_all(bricks, halves_ref, faces_ref, high_out, low_out):
    put_halves(halves_ref, 0, bricks)
    for high, out_ref in ((True, high_out), (False, low_out)):
        for brick in range(BRICKS):
            pack_faces(faces_ref, brick * FACE, halves_ref, brick * CUBE, high)
        out_ref[...] = faces_ref[...].astype(BF16)


def to_partners(high_ref, low_ref, far_out, near_out):
    even = lax.axis_index("space") % 2 == 0
    far_out[...] = jnp.where(even, low_ref[...], high_ref[...])
    near_out[...] = jnp.where(even, high_ref[...], low_ref[...])


def faces_kernel(cotangent_ref, high_out, low_out, far_out, near_out, halves_ref, faces_ref):
    pack_all(cotangent_lines(cotangent_ref), halves_ref, faces_ref, high_out, low_out)
    to_partners(high_out, low_out, far_out, near_out)


def unpack_depth(halves, high):
    packed = jnp.concatenate(halves, axis=0)
    pieces = []
    for part in range(4):
        shift = ((3 - part) if high else (4 - part)) % 4 * CHANNELS
        pieces.append(pltpu.roll(packed, shift, 1) if shift else packed)
    return jnp.concatenate(pieces, axis=0).reshape(EDGE, EDGE, 128)


def first_kernel(
    links_in, received_ref, up_ref, band_ref, weights_ref,
    slope_out, hidden_out, turned_out, pad_out, back_out, high_out, low_out, masks_out,
    volumes_ref, rows_ref, halves_ref, faces_ref, links_ref, links_sem,
):
    links_copy = pltpu.make_async_copy(links_in, links_ref, links_sem)
    links_copy.start()
    position = lax.axis_index("space")
    tiles = received_ref.shape[1] // (3 * BRICKS)
    rows_ref[0 : 3 * BRICKS * tiles] = jnp.sum(received_ref[...].astype(F32), axis=0)
    rows_ref[3 * BRICKS * tiles :] = jnp.zeros((2 * tiles, 128), F32)
    cells = []
    for tile in range(tiles):
        rows = rows_ref[pl.ds(tile, 8, stride=tiles), :]
        cells += [rows[:, :64], rows[:, 64:]]
    lifted = dot(jnp.concatenate(cells, axis=0).astype(BF16), up_ref[...])
    lifted = lifted.astype(BF16).astype(F32)
    for cell in range(8):
        a, b, c = cell // 4, cell // 2 % 2, cell % 2
        for sub in range(16):
            line = (4 * a + sub // 4) * EDGE + 4 * b + sub % 4
            volumes_ref[c, pl.ds(line, 8, stride=CUBE), :] = lifted[
                cell * 8 : cell * 8 + 8, sub * 128 : sub * 128 + 128
            ]
    links_copy.wait()
    put_masks(masks_out, links_ref)
    for brick in range(BRICKS):

        def near(face):
            link = links_ref[0, brick, face]
            index = jnp.clip(link - BRICKS * (position - 1), 0, 3 * BRICKS - 1)
            return pl.multiple_of(index * CUBE, CUBE), jnp.where(link >= 0, 1.0, 0.0).astype(F32)

        def x_face(face):
            start, present = near(face)
            offset = EDGE * (EDGE - 1) if face % 2 == 0 else 0
            return [half * present for half in pair(volumes_ref, pl.multiple_of(start + offset, 8), EDGE)]

        def y_face(face):
            start, present = near(face)
            offset = EDGE - 1 if face % 2 == 0 else 0
            return [half * present for half in pair(volumes_ref, start + offset, EDGE, EDGE)]

        def z_face(face):
            start, present = near(face)
            tile = volumes_ref[1 if face % 2 == 0 else 0, pl.ds(start, CUBE), :] * present
            return tile.reshape(EDGE, EDGE, HALF)

        own = pair(volumes_ref, (BRICKS + brick) * CUBE, CUBE)
        own = [half.reshape(EDGE, EDGE, HALF) for half in own]
        put_padded(pad_out, brick, own, x_face(0), x_face(1), y_face(2), y_face(3), z_face(4), z_face(5))
    pre = convolve(pad_out, band_ref)
    sigmoid = 1.0 / (1.0 + jnp.exp(-pre))
    hidden = (pre / (1.0 + jnp.exp(-pre))).astype(BF16)
    slope_out[...] = sigmoid * (1.0 + pre * (1.0 - sigmoid))
    hidden_out[...] = hidden
    hidden = hidden.astype(F32)
    turned_out[...] = jnp.transpose(hidden).astype(BF16)
    pack_all(half_lines(hidden), halves_ref, faces_ref, high_out, low_out)
    build_band(back_out, flipped_rows(weights_ref[...].astype(F32)))


def fold(outer, places):
    lane = lanes_of((CHANNELS, 128)) // CHANNELS
    folded = None
    for block in range(4):
        start, tile = places[block]
        rows = outer[start : start + CHANNELS, tile * 128 : tile * 128 + 128]
        folded = rows if folded is None else jnp.where(lane == block, rows, folded)
    quarter = [folded[8 * q : 8 * q + 8] for q in range(4)]
    small = lanes_of((8, 128)) // CHANNELS
    total = None
    for turn in range(4):
        mixed = quarter[0]
        for q in range(1, 4):
            mixed = jnp.where(small == (q + turn) % 4, quarter[q], mixed)
        if turn:
            mixed = pltpu.roll(mixed, 128 - turn * CHANNELS, 1)
        total = mixed if total is None else total + mixed
    return total


def diagonal(shift):
    places = [None] * 4
    for z in range(4):
        other = z + shift
        places[other % 4] = (z * CHANNELS, 0 if 0 <= other < 4 else 1)
    return places


def put_masks(masks_ref, links_ref):
    position = lax.axis_index("space")
    for brick in range(BRICKS):
        for face in range(6):
            first = links_ref[0, brick, face] - BRICKS * (position - 1 if face % 2 == 0 else position)
            for i in range(2 * BRICKS):
                row = (brick * 6 + face) * 2 * BRICKS + i
                masks_ref[row : row + 1, :] = jnp.full((1, 128), jnp.where(first == i, 1.0, 0.0).astype(F32))


def pad_all(pad_ref, bricks, masks_ref, high_pool, low_pool, high_own, low_own, far, near):
    position = lax.axis_index("space")
    half = BRICKS * FACE
    even = position % 2 == 0
    high_pool[0:half] = jnp.where(even, far[...], near[...]).astype(F32)
    high_pool[half:] = high_own[...].astype(F32)
    low_pool[0:half] = low_own[...].astype(F32)
    low_pool[half:] = jnp.where(even, near[...], far[...]).astype(F32)
    for brick, lines in enumerate(bricks):

        def face(number, axis):
            pool = high_pool if number % 2 == 0 else low_pool
            total = [0.0, 0.0]
            for i in range(2 * BRICKS):
                row = (brick * 6 + number) * 2 * BRICKS + i
                mask = masks_ref[row : row + 1, :]
                start = i * FACE + axis * EDGE
                for part in range(2):
                    found = pool[start : start + EDGE, part * HALF : part * HALF + HALF]
                    total[part] = total[part] + found * mask
            return total

        put_padded(
            pad_ref, brick, lines, face(0, 0), face(1, 0), face(2, 1), face(3, 1),
            unpack_depth(face(4, 2), True), unpack_depth(face(5, 2), False),
        )


def second_kernel(
    masks_ref, cotangent_ref, band_ref, slope_ref, hidden_ref, lifted_pad, high_own, low_own, far, near,
    hidden_high, hidden_low,
    sums_out, lifted_out, far_out, near_out,
    high_pool, low_pool, cotangent_pad, sums_ref,
):
    to_partners(hidden_high, hidden_low, far_out, near_out)
    lifted_out[...] = window(lifted_pad, 4)[:, :HALF]
    bricks = cotangent_lines(cotangent_ref)
    pad_all(cotangent_pad, bricks, masks_ref, high_pool, low_pool, high_own, low_own, far, near)
    gradient = (convolve(cotangent_pad, band_ref) * slope_ref[...]).astype(BF16)
    gradient = jnp.transpose(gradient.astype(F32)).astype(BF16)
    hidden = hidden_ref[...]
    sums_ref[8 * BLOCKS :] = jnp.zeros((sums_ref.shape[0] - 8 * BLOCKS, 128), F32)
    for k in range(9):
        one = dot(gradient, window(lifted_pad, k))
        two = dot(hidden, window(cotangent_pad, 8 - k))
        for part in range(3):
            start = 8 * (3 * k + part)
            sums_ref[start : start + 8] = fold(one, diagonal(part - 1))
            start += 8 * 27
            sums_ref[start : start + 8] = fold(two, diagonal(1 - part))
    sums_out[...] = sums_ref[...].astype(BF16).reshape(sums_out.shape)


def fine_kernel(
    masks_ref, band_ref, lifted_ref, hidden_ref, high_own, low_own, far, near,
    fine_out, high_pool, low_pool, hidden_pad,
):
    bricks = half_lines(hidden_ref[...].astype(F32))
    pad_all(hidden_pad, bricks, masks_ref, high_pool, low_pool, high_own, low_own, far, near)
    fine = lifted_ref[...].astype(F32) + convolve(hidden_pad, band_ref)
    fine = fine.reshape(LINES // EDGE, 2, EDGE, HALF)
    fine = jnp.concatenate([fine[:, 0], fine[:, 1]], axis=-1)
    fine_out[...] = fine.astype(BF16).reshape(fine_out.shape)


def unpacked(tile):
    pieces = [tile] + [pltpu.roll(tile, 128 - q * CHANNELS, 1) for q in range(1, 4)]
    return jnp.concatenate(pieces, axis=0)[:, :CHANNELS]


def sum_kernel(scale, parts_ref, out_ref):
    total = jnp.sum(parts_ref[...].astype(F32), axis=0) * scale
    per = parts_ref.shape[1] // 8
    device = lax.axis_index("space") * lax.axis_size("dp") + lax.axis_index("dp")
    tiles = []
    for j in range(per):
        tile = total[8 * j : 8 * j + 8]
        block = jnp.transpose(unpacked(tile))
        turned = jnp.concatenate([block[8 * q : 8 * q + 8] for q in range(4)], axis=1)
        tiles.append(jnp.where(device * per + j < 27, turned, tile))
    total = jnp.concatenate(tiles, axis=0)
    out_ref[...] = jnp.broadcast_to(total.astype(BF16)[None], out_ref.shape)


def unpack_kernel(sums_ref, one_out, two_out, rows_ref, one_ref, two_ref, sems):
    rows_ref[...] = sums_ref[...].astype(F32).reshape(rows_ref.shape)
    copies = []
    for which, (block_ref, out) in enumerate(((one_ref, one_out), (two_ref, two_out))):
        for third in range(3):
            first = 9 * third
            for index in range(first, first + 9):
                row = 8 * (27 * which + index)
                block_ref[index] = unpacked(rows_ref[row : row + 8])
            part = pl.ds(first, 9)
            copies.append(pltpu.make_async_copy(block_ref.at[part], out.at[part], sems.at[which, third]))
            copies[-1].start()
    for copy in copies:
        copy.wait()


def call(kernel, out_shape, scratch=(), hbm=(), inputs=1, limit=24, cost=None, out=pltpu.VMEM):
    spaces = [pl.ANY if i in hbm else pltpu.VMEM for i in range(inputs)]
    return pl.pallas_call(
        kernel,
        out_shape=out_shape,
        in_specs=[pl.BlockSpec(memory_space=space) for space in spaces],
        out_specs=jax.tree.map(lambda _: pl.BlockSpec(memory_space=out), out_shape),
        scratch_shapes=list(scratch),
        compiler_params=pltpu.CompilerParams(vmem_limit_bytes=limit * 2**20),
        cost_estimate=cost,
    )


def shape(*dims, dtype=BF16):
    return jax.ShapeDtypeStruct(dims, dtype)


def swapped(value, first):
    pairs = [(i, i + 1) for i in range(first, lax.axis_size("space") - 1, 2)]
    return lax.ppermute(value, "space", pairs + [(target, source) for source, target in pairs])


def body(coarse_latents, active_blocks, face_links, cotangent, up_weight, conv_one, conv_two):
    devices = lax.axis_size("space")
    everyone = devices * lax.axis_size("dp")
    held, width = coarse_latents.shape[1:]
    bricks = active_blocks.shape[1]
    tiles = width // 128
    scenes = 2 if lax.axis_size("dp") == 2 else 1
    packed = call(
        functools.partial(pick_kernel, scenes),
        shape(devices * scenes, 3 * BRICKS * tiles, 128),
        [
            pltpu.VMEM((1, bricks), jnp.int32),
            pltpu.VMEM((1, held, width), BF16),
            pltpu.VMEM(((bricks + 16) * tiles, 128), F32),
            pltpu.SemaphoreType.DMA((2,)),
        ],
        hbm=(0, 1),
        inputs=2,
        limit=60,
    )(active_blocks, coarse_latents)
    axes = ("space", "dp")
    received = lax.all_to_all(packed, axes if scenes == 2 else "space", split_axis=0, concat_axis=0, tiled=True)
    cost = pl.CostEstimate(flops=10**9, bytes_accessed=2 * 10**6, transcendentals=0)
    face = shape(BRICKS * FACE, LINE)
    halves = pltpu.VMEM((2, LINES, HALF), F32)
    faces = pltpu.VMEM((BRICKS * FACE, LINE), F32)
    pool = pltpu.VMEM((2 * BRICKS * FACE, LINE), F32)
    volume = shape(ROWS, HALF)
    links = [pltpu.SMEM(face_links.shape, jnp.int32), pltpu.SemaphoreType.DMA]
    pad_shape = (3, BRICKS, EDGE + 2, 2 * EDGE, WIDE)
    pad = pltpu.VMEM(pad_shape, BF16)
    high, low, far, near = call(faces_kernel, (face,) * 4, [halves, faces])(cotangent)
    far = swapped(far, 1)
    near = swapped(near, 0)
    band_one = call(band_kernel, shape(*BAND), cost=cost)(conv_one)
    slope, hidden, turned, lifted_pad, band_back, hidden_high, hidden_low, masks = call(
        first_kernel,
        (
            shape(ROWS, HALF, dtype=F32), volume, shape(HALF, ROWS), shape(*pad_shape), shape(*BAND),
            face, face, shape(BRICKS * 6 * 2 * BRICKS, 128, dtype=F32),
        ),
        [pltpu.VMEM((2, 8 * CUBE, 128), F32), pltpu.VMEM((8 * tiles, 128), F32), halves, faces, *links],
        hbm=(0,),
        inputs=5,
    )(face_links, received, up_weight, band_one, conv_two)
    per = -(-BLOCKS // everyone)
    per += per % 2
    sums, lifted, hidden_far, hidden_near = call(
        second_kernel,
        (shape(everyone, per * 8, 128), volume, face, face),
        [pool, pool, pad, pltpu.VMEM((everyone * per * 8, 128), F32)],
        inputs=12,
    )(
        masks, cotangent, band_back, slope, turned, lifted_pad, high, low, far, near,
        hidden_high, hidden_low,
    )
    hidden_far = swapped(hidden_far, 1)
    hidden_near = swapped(hidden_near, 0)
    band_two = call(band_kernel, shape(*BAND), cost=cost)(conv_two)
    fine = call(fine_kernel, shape(*cotangent.shape), [pool, pool, pad], inputs=8, cost=cost)(
        masks, band_two, lifted, hidden, hidden_high, hidden_low, hidden_far, hidden_near
    )
    parts = lax.all_to_all(sums, axes, split_axis=0, concat_axis=0, tiled=True)
    scale = 1.0 / math.sqrt(lax.axis_size("dp") * devices * BRICKS * EDGE**3)
    total = call(functools.partial(sum_kernel, scale), shape(*sums.shape))(parts)
    gathered = lax.all_to_all(total, axes, split_axis=0, concat_axis=0, tiled=True)
    grads = shape(27, CHANNELS, CHANNELS, dtype=F32)
    block = pltpu.VMEM(grads.shape, F32)
    scratch = [pltpu.VMEM((everyone * per * 8, 128), F32), block, block, pltpu.SemaphoreType.DMA((2, 3))]
    grad_one, grad_two = call(unpack_kernel, (grads, grads), scratch, out=pl.ANY)(gathered)
    return (fine, grad_one, grad_two)


def solution(mesh):
    return jax.shard_map(
        body,
        mesh=mesh,
        in_specs=(
            P("dp", "space", None),
            P("dp", None),
            P("dp", "space", None),
            P("dp", "space", None, None, None),
            P(),
            P(),
            P(),
        ),
        out_specs=(P("dp", "space", None, None, None), P(), P()),
        check_vma=False,
    )
```

```python
import functools
import math

import jax
import jax.numpy as jnp
from jax import lax
from jax.experimental import pallas as pl
from jax.experimental.pallas import tpu as pltpu
from jax.sharding import PartitionSpec as P

BF16 = jnp.bfloat16
F32 = jnp.float32
EDGE = 8
CHANNELS = 32
LINE = EDGE * CHANNELS
HALF = LINE // 2
WIDE = 2 * HALF
BRICKS = 2
CUBE = EDGE * EDGE
LINES = BRICKS * CUBE
BAND = (9, WIDE, HALF)
ROWS = 2 * LINES
FACE = 3 * EDGE
BLOCKS = 54


def dot(left, right):
    return jnp.dot(left, right, preferred_element_type=F32)


def dot_rows(left, right):
    return lax.dot_general(left, right, (((0,), (0,)), ((), ())), preferred_element_type=F32)


def pair(halves_ref, start, count, stride=1):
    index = pl.ds(start, count, stride=stride) if stride > 1 else pl.ds(start, count)
    return halves_ref[0, index, :], halves_ref[1, index, :]


def lanes_of(shape):
    return lax.broadcasted_iota(jnp.int32, shape, len(shape) - 1)


def pick_kernel(scenes, ids_hbm, latents_hbm, out_ref, ids_ref, latents_ref, rows_ref, sems):
    ids_copy = pltpu.make_async_copy(ids_hbm, ids_ref, sems.at[0])
    latents_copy = pltpu.make_async_copy(latents_hbm, latents_ref, sems.at[1])
    ids_copy.start()
    latents_copy.start()
    held, width = latents_ref.shape[1:]
    bricks = ids_ref.shape[1]
    margin = 8 * width // 128
    tiles = width // 128
    rows_ref[0:margin] = jnp.zeros((margin, 128), F32)
    rows_ref[margin + bricks * tiles :] = jnp.zeros((margin, 128), F32)
    first = lax.axis_index("space") * held
    rows = lax.broadcasted_iota(jnp.int32, (held, bricks), 0) + first
    ids_copy.wait()
    hot = jnp.where(rows == ids_ref[...], 1.0, 0.0).astype(BF16)
    latents_copy.wait()
    picked = dot_rows(hot, latents_ref[0])
    for tile in range(tiles):
        rows_ref[pl.ds(margin + tile, bricks, stride=tiles), :] = picked[:, tile * 128 : tile * 128 + 128]
    count = out_ref.shape[1]
    wanted = [jnp.where(lax.axis_index("dp") == scene, 1.0, 0.0).astype(F32) for scene in range(scenes)]
    for receiver in range(out_ref.shape[0] // scenes):
        start = margin + BRICKS * (receiver - 1) * tiles
        found = rows_ref[start : start + count]
        for scene in range(scenes):
            kept = found * wanted[scene] if scenes > 1 else found
            out_ref[receiver * scenes + scene] = kept.astype(BF16)


def build_band(band_ref, rows):
    shape = (3 * CHANNELS, HALF)
    row = lax.broadcasted_iota(jnp.int32, shape, 0)
    target = CHANNELS - (row // CHANNELS) * CHANNELS + row % CHANNELS
    distance = lanes_of(shape) - target
    band_ref[:, HALF:, :] = jnp.zeros((9, HALF, HALF), BF16)
    for z in range(-1, 5):
        select = jnp.where(distance == z * CHANNELS, 1.0, 0.0).astype(BF16)
        block = dot(rows, select).astype(BF16)
        start = z % 8 * CHANNELS
        band_ref[:, start : start + CHANNELS, :] = block.reshape(9, CHANNELS, HALF)


def weight_rows(weights):
    cube = weights.reshape(9, 3, CHANNELS, CHANNELS)
    rows = jnp.concatenate([cube[:, 0], cube[:, 1], cube[:, 2]], axis=-1)
    return rows.reshape(9 * CHANNELS, 3 * CHANNELS).astype(BF16)


def flipped_rows(weights):
    cube = jnp.swapaxes(weights, 1, 2).reshape(9, 3, CHANNELS, CHANNELS)
    pieces = [jnp.concatenate([cube[8 - k, 2], cube[8 - k, 1], cube[8 - k, 0]], axis=-1) for k in range(9)]
    return jnp.concatenate(pieces, axis=0).astype(BF16)


def band_kernel(weights_ref, band_ref):
    build_band(band_ref, weight_rows(weights_ref[...].astype(F32)))


def bands_kernel(one_hbm, two_hbm, band_ref, back_ref, one_ref, two_ref, sems):
    one_copy = pltpu.make_async_copy(one_hbm, one_ref, sems.at[0])
    two_copy = pltpu.make_async_copy(two_hbm, two_ref, sems.at[1])
    one_copy.start()
    two_copy.start()
    one_copy.wait()
    build_band(band_ref, weight_rows(one_ref[...].astype(F32)))
    two_copy.wait()
    build_band(back_ref, flipped_rows(two_ref[...].astype(F32)))


def put_padded(pad_ref, brick, lines, x_low, x_high, y_low, y_high, z_low, z_high):
    def joined(halves, before, after):
        lane = lanes_of(halves[0].shape)
        first = jnp.where(lane < CHANNELS, halves[1], before)
        second = jnp.where(lane >= HALF - CHANNELS, halves[0], after)
        return jnp.concatenate([halves[0], first], axis=-1), jnp.concatenate([halves[1], second], axis=-1)

    inside = joined(lines, z_low, z_high)
    x_low, x_high, y_low, y_high = [joined(face, 0.0, 0.0) for face in (x_low, x_high, y_low, y_high)]
    none = jnp.zeros((1, WIDE), F32)
    shifted = [[], [], []]
    for half in range(2):
        slabs = jnp.concatenate([x_low[half][None], inside[half], x_high[half][None]], axis=0)
        row = lax.broadcasted_iota(jnp.int32, slabs.shape, 1)
        low = jnp.concatenate([none, y_low[half], none], axis=0)[:, None, :]
        high = jnp.concatenate([none, y_high[half], none], axis=0)[:, None, :]
        shifted[0].append(jnp.where(row == 0, low, pltpu.roll(slabs, 1, 1)))
        shifted[1].append(slabs)
        shifted[2].append(jnp.where(row == EDGE - 1, high, pltpu.roll(slabs, EDGE - 1, 1)))
    for dy in range(3):
        pad_ref[dy, brick] = jnp.concatenate(shifted[dy], axis=1).astype(BF16)


def window(pad_ref, k):
    return pad_ref[k % 3, :, k // 3 : k // 3 + EDGE].reshape(ROWS, WIDE)


def convolve(pad_ref, band_ref):
    windows = jnp.concatenate([window(pad_ref, k) for k in range(9)], axis=1)
    return dot(windows, band_ref[...].reshape(9 * WIDE, HALF))


def half_lines(values):
    cube = values.reshape(BRICKS, EDGE, 2, EDGE, HALF)
    return [(cube[brick, :, 0], cube[brick, :, 1]) for brick in range(BRICKS)]


def put_halves(halves_ref, start, bricks):
    for brick, lines in enumerate(bricks):
        for half in range(2):
            first = start + brick * CUBE
            halves_ref[half, first : first + CUBE, :] = lines[half].reshape(CUBE, HALF)


def cotangent_lines(cotangent_ref):
    cube = cotangent_ref[...].astype(F32).reshape(BRICKS, EDGE, EDGE, LINE)
    return [(cube[brick, :, :, :HALF], cube[brick, :, :, HALF:]) for brick in range(BRICKS)]


def pack_faces(faces_ref, base, halves_ref, start, high):
    x_face = pair(halves_ref, start + ((EDGE - 1) * EDGE if high else 0), EDGE)
    y_face = pair(halves_ref, start + (EDGE - 1 if high else 0), EDGE, EDGE)
    for half in range(2):
        lanes = slice(half * HALF, half * HALF + HALF)
        faces_ref[base : base + EDGE, lanes] = x_face[half]
        faces_ref[base + EDGE : base + 2 * EDGE, lanes] = y_face[half]
    tile = halves_ref[1 if high else 0, start : start + CUBE, :]
    lane = lanes_of((16, 128)) // CHANNELS
    packed = jnp.zeros((16, 128), F32)
    for part in range(4):
        shift = (part + 1 if high else part) % 4 * CHANNELS
        piece = tile[part * 16 : part * 16 + 16]
        packed = jnp.where(lane == part, pltpu.roll(piece, shift, 1) if shift else piece, packed)
    faces_ref[base + 2 * EDGE : base + FACE, :128] = packed[:8]
    faces_ref[base + 2 * EDGE : base + FACE, 128:] = packed[8:]


def pack_all(bricks, halves_ref, faces_ref, high_out, low_out):
    put_halves(halves_ref, 0, bricks)
    for high, out_ref in ((True, high_out), (False, low_out)):
        for brick in range(BRICKS):
            pack_faces(faces_ref, brick * FACE, halves_ref, brick * CUBE, high)
        out_ref[...] = faces_ref[...].astype(BF16)


def to_partners(high_ref, low_ref, far_out, near_out):
    even = lax.axis_index("space") % 2 == 0
    far_out[...] = jnp.where(even, low_ref[...], high_ref[...])
    near_out[...] = jnp.where(even, high_ref[...], low_ref[...])


def faces_kernel(cotangent_ref, high_out, low_out, far_out, near_out, halves_ref, faces_ref):
    pack_all(cotangent_lines(cotangent_ref), halves_ref, faces_ref, high_out, low_out)
    to_partners(high_out, low_out, far_out, near_out)


def unpack_depth(halves, high):
    packed = jnp.concatenate(halves, axis=0)
    pieces = []
    for part in range(4):
        shift = ((3 - part) if high else (4 - part)) % 4 * CHANNELS
        pieces.append(pltpu.roll(packed, shift, 1) if shift else packed)
    return jnp.concatenate(pieces, axis=0).reshape(EDGE, EDGE, 128)


def first_kernel(
    links_in, received_ref, up_ref, band_ref,
    slope_out, hidden_out, turned_out, pad_out, high_out, low_out, masks_out,
    volumes_ref, rows_ref, halves_ref, faces_ref, links_ref, links_sem,
):
    links_copy = pltpu.make_async_copy(links_in, links_ref, links_sem)
    links_copy.start()
    position = lax.axis_index("space")
    tiles = received_ref.shape[1] // (3 * BRICKS)
    rows_ref[0 : 3 * BRICKS * tiles] = jnp.sum(received_ref[...].astype(F32), axis=0)
    rows_ref[3 * BRICKS * tiles :] = jnp.zeros((2 * tiles, 128), F32)
    cells = []
    for tile in range(tiles):
        rows = rows_ref[pl.ds(tile, 8, stride=tiles), :]
        cells += [rows[:, :64], rows[:, 64:]]
    lifted = dot(jnp.concatenate(cells, axis=0).astype(BF16), up_ref[...])
    lifted = lifted.astype(BF16).astype(F32)
    for cell in range(8):
        a, b, c = cell // 4, cell // 2 % 2, cell % 2
        for sub in range(16):
            line = (4 * a + sub // 4) * EDGE + 4 * b + sub % 4
            volumes_ref[c, pl.ds(line, 8, stride=CUBE), :] = lifted[
                cell * 8 : cell * 8 + 8, sub * 128 : sub * 128 + 128
            ]
    links_copy.wait()
    put_masks(masks_out, links_ref)
    for brick in range(BRICKS):

        def near(face):
            link = links_ref[0, brick, face]
            index = jnp.clip(link - BRICKS * (position - 1), 0, 3 * BRICKS - 1)
            return pl.multiple_of(index * CUBE, CUBE), jnp.where(link >= 0, 1.0, 0.0).astype(F32)

        def x_face(face):
            start, present = near(face)
            offset = EDGE * (EDGE - 1) if face % 2 == 0 else 0
            return [half * present for half in pair(volumes_ref, pl.multiple_of(start + offset, 8), EDGE)]

        def y_face(face):
            start, present = near(face)
            offset = EDGE - 1 if face % 2 == 0 else 0
            return [half * present for half in pair(volumes_ref, start + offset, EDGE, EDGE)]

        def z_face(face):
            start, present = near(face)
            tile = volumes_ref[1 if face % 2 == 0 else 0, pl.ds(start, CUBE), :] * present
            return tile.reshape(EDGE, EDGE, HALF)

        own = pair(volumes_ref, (BRICKS + brick) * CUBE, CUBE)
        own = [half.reshape(EDGE, EDGE, HALF) for half in own]
        put_padded(pad_out, brick, own, x_face(0), x_face(1), y_face(2), y_face(3), z_face(4), z_face(5))
    pre = convolve(pad_out, band_ref)
    sigmoid = 1.0 / (1.0 + jnp.exp(-pre))
    hidden = (pre / (1.0 + jnp.exp(-pre))).astype(BF16)
    slope_out[...] = sigmoid * (1.0 + pre * (1.0 - sigmoid))
    hidden_out[...] = hidden
    hidden = hidden.astype(F32)
    turned_out[...] = jnp.transpose(hidden).astype(BF16)
    pack_all(half_lines(hidden), halves_ref, faces_ref, high_out, low_out)


def fold(outer, places):
    lane = lanes_of((CHANNELS, 128)) // CHANNELS
    folded = None
    for block in range(4):
        start, tile = places[block]
        rows = outer[start : start + CHANNELS, tile * 128 : tile * 128 + 128]
        folded = rows if folded is None else jnp.where(lane == block, rows, folded)
    quarter = [folded[8 * q : 8 * q + 8] for q in range(4)]
    small = lanes_of((8, 128)) // CHANNELS
    total = None
    for turn in range(4):
        mixed = quarter[0]
        for q in range(1, 4):
            mixed = jnp.where(small == (q + turn) % 4, quarter[q], mixed)
        if turn:
            mixed = pltpu.roll(mixed, 128 - turn * CHANNELS, 1)
        total = mixed if total is None else total + mixed
    return total


def diagonal(shift):
    places = [None] * 4
    for z in range(4):
        other = z + shift
        places[other % 4] = (z * CHANNELS, 0 if 0 <= other < 4 else 1)
    return places


def put_masks(masks_ref, links_ref):
    position = lax.axis_index("space")
    for brick in range(BRICKS):
        for face in range(6):
            first = links_ref[0, brick, face] - BRICKS * (position - 1 if face % 2 == 0 else position)
            for i in range(2 * BRICKS):
                row = (brick * 6 + face) * 2 * BRICKS + i
                masks_ref[row : row + 1, :] = jnp.full((1, 128), jnp.where(first == i, 1.0, 0.0).astype(F32))


def pad_all(pad_ref, bricks, masks_ref, high_pool, low_pool, high_own, low_own, far, near):
    position = lax.axis_index("space")
    half = BRICKS * FACE
    even = position % 2 == 0
    high_pool[0:half] = jnp.where(even, far[...], near[...]).astype(F32)
    high_pool[half:] = high_own[...].astype(F32)
    low_pool[0:half] = low_own[...].astype(F32)
    low_pool[half:] = jnp.where(even, near[...], far[...]).astype(F32)
    for brick, lines in enumerate(bricks):

        def face(number, axis):
            pool = high_pool if number % 2 == 0 else low_pool
            total = [0.0, 0.0]
            for i in range(2 * BRICKS):
                row = (brick * 6 + number) * 2 * BRICKS + i
                mask = masks_ref[row : row + 1, :]
                start = i * FACE + axis * EDGE
                for part in range(2):
                    found = pool[start : start + EDGE, part * HALF : part * HALF + HALF]
                    total[part] = total[part] + found * mask
            return total

        put_padded(
            pad_ref, brick, lines, face(0, 0), face(1, 0), face(2, 1), face(3, 1),
            unpack_depth(face(4, 2), True), unpack_depth(face(5, 2), False),
        )


def second_kernel(
    masks_ref, cotangent_ref, band_ref, slope_ref, hidden_ref, lifted_pad, high_own, low_own, far, near,
    hidden_high, hidden_low,
    sums_out, lifted_out, far_out, near_out,
    high_pool, low_pool, cotangent_pad, sums_ref,
):
    to_partners(hidden_high, hidden_low, far_out, near_out)
    lifted_out[...] = window(lifted_pad, 4)[:, :HALF]
    bricks = cotangent_lines(cotangent_ref)
    pad_all(cotangent_pad, bricks, masks_ref, high_pool, low_pool, high_own, low_own, far, near)
    gradient = (convolve(cotangent_pad, band_ref) * slope_ref[...]).astype(BF16)
    gradient = jnp.transpose(gradient.astype(F32)).astype(BF16)
    hidden = hidden_ref[...]
    sums_ref[8 * BLOCKS :] = jnp.zeros((sums_ref.shape[0] - 8 * BLOCKS, 128), F32)
    for k in range(9):
        one = dot(gradient, window(lifted_pad, k))
        two = dot(hidden, window(cotangent_pad, 8 - k))
        for part in range(3):
            start = 8 * (3 * k + part)
            sums_ref[start : start + 8] = fold(one, diagonal(part - 1))
            start += 8 * 27
            sums_ref[start : start + 8] = fold(two, diagonal(1 - part))
    sums_out[...] = sums_ref[...].astype(BF16).reshape(sums_out.shape)


def fine_kernel(
    masks_ref, band_ref, lifted_ref, hidden_ref, high_own, low_own, far, near,
    fine_out, high_pool, low_pool, hidden_pad,
):
    bricks = half_lines(hidden_ref[...].astype(F32))
    pad_all(hidden_pad, bricks, masks_ref, high_pool, low_pool, high_own, low_own, far, near)
    fine = lifted_ref[...].astype(F32) + convolve(hidden_pad, band_ref)
    fine = fine.reshape(LINES // EDGE, 2, EDGE, HALF)
    fine = jnp.concatenate([fine[:, 0], fine[:, 1]], axis=-1)
    fine_out[...] = fine.astype(BF16).reshape(fine_out.shape)


def unpacked(tile):
    pieces = [tile] + [pltpu.roll(tile, 128 - q * CHANNELS, 1) for q in range(1, 4)]
    return jnp.concatenate(pieces, axis=0)[:, :CHANNELS]


def sum_kernel(scale, parts_ref, out_ref):
    total = jnp.sum(parts_ref[...].astype(F32), axis=0) * scale
    per = parts_ref.shape[1] // 8
    device = lax.axis_index("space") * lax.axis_size("dp") + lax.axis_index("dp")
    tiles = []
    for j in range(per):
        tile = total[8 * j : 8 * j + 8]
        block = jnp.transpose(unpacked(tile))
        turned = jnp.concatenate([block[8 * q : 8 * q + 8] for q in range(4)], axis=1)
        tiles.append(jnp.where(device * per + j < 27, turned, tile))
    total = jnp.concatenate(tiles, axis=0)
    out_ref[...] = jnp.broadcast_to(total.astype(BF16)[None], out_ref.shape)


def unpack_kernel(sums_ref, fine_ref, one_out, two_out, fine_out, rows_ref, one_ref, two_ref, sems, fine_sem):
    fine_copy = pltpu.make_async_copy(fine_ref, fine_out, fine_sem)
    fine_copy.start()
    rows_ref[...] = sums_ref[...].astype(F32).reshape(rows_ref.shape)
    copies = []
    for which, (block_ref, out) in enumerate(((one_ref, one_out), (two_ref, two_out))):
        for third in range(3):
            first = 9 * third
            for index in range(first, first + 9):
                row = 8 * (27 * which + index)
                block_ref[index] = unpacked(rows_ref[row : row + 8])
            part = pl.ds(first, 9)
            copies.append(pltpu.make_async_copy(block_ref.at[part], out.at[part], sems.at[which, third]))
            copies[-1].start()
    for copy in copies:
        copy.wait()
    fine_copy.wait()


def call(kernel, out_shape, scratch=(), hbm=(), inputs=1, limit=24, cost=None, out=pltpu.VMEM):
    spaces = [pl.ANY if i in hbm else pltpu.VMEM for i in range(inputs)]
    return pl.pallas_call(
        kernel,
        out_shape=out_shape,
        in_specs=[pl.BlockSpec(memory_space=space) for space in spaces],
        out_specs=jax.tree.map(lambda _: pl.BlockSpec(memory_space=out), out_shape),
        scratch_shapes=list(scratch),
        compiler_params=pltpu.CompilerParams(vmem_limit_bytes=limit * 2**20),
        cost_estimate=cost,
    )


def shape(*dims, dtype=BF16):
    return jax.ShapeDtypeStruct(dims, dtype)


def kept_in_hbm(value):
    return pltpu.with_memory_space_constraint(value, pltpu.HBM)


def swapped(value, first):
    pairs = [(i, i + 1) for i in range(first, lax.axis_size("space") - 1, 2)]
    return lax.ppermute(value, "space", pairs + [(target, source) for source, target in pairs])


def body(coarse_latents, active_blocks, face_links, cotangent, up_weight, conv_one, conv_two):
    devices = lax.axis_size("space")
    everyone = devices * lax.axis_size("dp")
    held, width = coarse_latents.shape[1:]
    bricks = active_blocks.shape[1]
    tiles = width // 128
    scenes = 2 if lax.axis_size("dp") == 2 else 1
    packed = call(
        functools.partial(pick_kernel, scenes),
        shape(devices * scenes, 3 * BRICKS * tiles, 128),
        [
            pltpu.VMEM((1, bricks), jnp.int32),
            pltpu.VMEM((1, held, width), BF16),
            pltpu.VMEM(((bricks + 16) * tiles, 128), F32),
            pltpu.SemaphoreType.DMA((2,)),
        ],
        hbm=(0, 1),
        inputs=2,
    )(kept_in_hbm(active_blocks), kept_in_hbm(coarse_latents))
    axes = ("space", "dp")
    received = lax.all_to_all(packed, axes if scenes == 2 else "space", split_axis=0, concat_axis=0, tiled=True)
    cost = pl.CostEstimate(flops=10**9, bytes_accessed=2 * 10**6, transcendentals=0)
    face = shape(BRICKS * FACE, LINE)
    halves = pltpu.VMEM((2, LINES, HALF), F32)
    faces = pltpu.VMEM((BRICKS * FACE, LINE), F32)
    pool = pltpu.VMEM((2 * BRICKS * FACE, LINE), F32)
    volume = shape(ROWS, HALF)
    links = [pltpu.SMEM(face_links.shape, jnp.int32), pltpu.SemaphoreType.DMA]
    pad_shape = (3, BRICKS, EDGE + 2, 2 * EDGE, WIDE)
    pad = pltpu.VMEM(pad_shape, BF16)
    high, low, far, near = call(faces_kernel, (face,) * 4, [halves, faces])(cotangent)
    far = swapped(far, 1)
    near = swapped(near, 0)
    weights = pltpu.VMEM(conv_one.shape, BF16)
    band_one, band_back = call(
        bands_kernel,
        (shape(*BAND), shape(*BAND)),
        [weights, weights, pltpu.SemaphoreType.DMA((2,))],
        hbm=(0, 1),
        inputs=2,
        cost=cost,
    )(kept_in_hbm(conv_one), kept_in_hbm(conv_two))
    slope, hidden, turned, lifted_pad, hidden_high, hidden_low, masks = call(
        first_kernel,
        (
            shape(ROWS, HALF, dtype=F32), volume, shape(HALF, ROWS), shape(*pad_shape),
            face, face, shape(BRICKS * 6 * 2 * BRICKS, 128, dtype=F32),
        ),
        [pltpu.VMEM((2, 8 * CUBE, 128), F32), pltpu.VMEM((8 * tiles, 128), F32), halves, faces, *links],
        hbm=(0,),
        inputs=4,
    )(face_links, received, up_weight, band_one)
    per = -(-BLOCKS // everyone)
    per += per % 2
    sums, lifted, hidden_far, hidden_near = call(
        second_kernel,
        (shape(everyone, per * 8, 128), volume, face, face),
        [pool, pool, pad, pltpu.VMEM((everyone * per * 8, 128), F32)],
        inputs=12,
    )(
        masks, cotangent, band_back, slope, turned, lifted_pad, high, low, far, near,
        hidden_high, hidden_low,
    )
    hidden_far = swapped(hidden_far, 1)
    hidden_near = swapped(hidden_near, 0)
    band_two = call(band_kernel, shape(*BAND), cost=cost)(conv_two)
    fine = call(fine_kernel, shape(*cotangent.shape), [pool, pool, pad], inputs=8, cost=cost)(
        masks, band_two, lifted, hidden, hidden_high, hidden_low, hidden_far, hidden_near
    )
    parts = lax.all_to_all(sums, axes, split_axis=0, concat_axis=0, tiled=True)
    scale = 1.0 / math.sqrt(lax.axis_size("dp") * devices * BRICKS * EDGE**3)
    total = call(functools.partial(sum_kernel, scale), shape(*sums.shape))(parts)
    gathered = lax.all_to_all(total, axes, split_axis=0, concat_axis=0, tiled=True)
    grads = shape(27, CHANNELS, CHANNELS, dtype=F32)
    block = pltpu.VMEM(grads.shape, F32)
    scratch = [pltpu.VMEM((everyone * per * 8, 128), F32), block, block]
    scratch += [pltpu.SemaphoreType.DMA((2, 3)), pltpu.SemaphoreType.DMA]
    grad_one, grad_two, fine = call(
        unpack_kernel, (grads, grads, shape(*fine.shape)), scratch, inputs=2, out=pl.ANY
    )(gathered, fine)
    return (fine, grad_one, grad_two)


def solution(mesh):
    return jax.shard_map(
        body,
        mesh=mesh,
        in_specs=(
            P("dp", "space", None),
            P("dp", None),
            P("dp", "space", None),
            P("dp", "space", None, None, None),
            P(),
            P(),
            P(),
        ),
        out_specs=(P("dp", "space", None, None, None), P(), P()),
        check_vma=False,
    )
```

```python
import functools
import math

import jax
import jax.numpy as jnp
from jax import lax
from jax.experimental import pallas as pl
from jax.experimental.pallas import tpu as pltpu
from jax.sharding import PartitionSpec as P

BF16 = jnp.bfloat16
F32 = jnp.float32
EDGE = 8
CHANNELS = 32
LINE = EDGE * CHANNELS
HALF = LINE // 2
WIDE = 2 * HALF
BRICKS = 2
CUBE = EDGE * EDGE
LINES = BRICKS * CUBE
BAND = (9, WIDE, HALF)
ROWS = 2 * LINES
FACE = 3 * EDGE
BLOCKS = 54


def dot(left, right):
    return jnp.dot(left, right, preferred_element_type=F32)


def dot_rows(left, right):
    return lax.dot_general(left, right, (((0,), (0,)), ((), ())), preferred_element_type=F32)


def pair(halves_ref, start, count, stride=1):
    index = pl.ds(start, count, stride=stride) if stride > 1 else pl.ds(start, count)
    return halves_ref[0, index, :], halves_ref[1, index, :]


def lanes_of(shape):
    return lax.broadcasted_iota(jnp.int32, shape, len(shape) - 1)


def pick_kernel(scenes, ids_hbm, latents_hbm, out_ref, ids_ref, latents_ref, rows_ref, sems):
    ids_copy = pltpu.make_async_copy(ids_hbm, ids_ref, sems.at[0])
    latents_copy = pltpu.make_async_copy(latents_hbm, latents_ref, sems.at[1])
    ids_copy.start()
    latents_copy.start()
    held, width = latents_ref.shape[1:]
    bricks = ids_ref.shape[1]
    margin = 8 * width // 128
    tiles = width // 128
    rows_ref[0:margin] = jnp.zeros((margin, 128), F32)
    rows_ref[margin + bricks * tiles :] = jnp.zeros((margin, 128), F32)
    first = lax.axis_index("space") * held
    rows = lax.broadcasted_iota(jnp.int32, (held, bricks), 0) + first
    ids_copy.wait()
    hot = jnp.where(rows == ids_ref[...], 1.0, 0.0).astype(BF16)
    latents_copy.wait()
    picked = dot_rows(hot, latents_ref[0])
    for tile in range(tiles):
        rows_ref[pl.ds(margin + tile, bricks, stride=tiles), :] = picked[:, tile * 128 : tile * 128 + 128]
    count = out_ref.shape[1]
    wanted = [jnp.where(lax.axis_index("dp") == scene, 1.0, 0.0).astype(F32) for scene in range(scenes)]
    for receiver in range(out_ref.shape[0] // scenes):
        start = margin + BRICKS * (receiver - 1) * tiles
        found = rows_ref[start : start + count]
        for scene in range(scenes):
            kept = found * wanted[scene] if scenes > 1 else found
            out_ref[receiver * scenes + scene] = kept.astype(BF16)


def build_band(band_ref, rows):
    shape = (3 * CHANNELS, HALF)
    row = lax.broadcasted_iota(jnp.int32, shape, 0)
    target = CHANNELS - (row // CHANNELS) * CHANNELS + row % CHANNELS
    distance = lanes_of(shape) - target
    band_ref[:, HALF:, :] = jnp.zeros((9, HALF, HALF), BF16)
    for z in range(-1, 5):
        select = jnp.where(distance == z * CHANNELS, 1.0, 0.0).astype(BF16)
        block = dot(rows, select).astype(BF16)
        start = z % 8 * CHANNELS
        band_ref[:, start : start + CHANNELS, :] = block.reshape(9, CHANNELS, HALF)


def weight_rows(weights):
    cube = weights.reshape(9, 3, CHANNELS, CHANNELS)
    rows = jnp.concatenate([cube[:, 0], cube[:, 1], cube[:, 2]], axis=-1)
    return rows.reshape(9 * CHANNELS, 3 * CHANNELS).astype(BF16)


def flipped_rows(weights):
    cube = jnp.swapaxes(weights, 1, 2).reshape(9, 3, CHANNELS, CHANNELS)
    pieces = [jnp.concatenate([cube[8 - k, 2], cube[8 - k, 1], cube[8 - k, 0]], axis=-1) for k in range(9)]
    return jnp.concatenate(pieces, axis=0).astype(BF16)


def band_kernel(weights_ref, band_ref):
    build_band(band_ref, weight_rows(weights_ref[...].astype(F32)))


def masks_kernel(links_in, weights_ref, band_ref, masks_ref, links_ref, links_sem):
    links_copy = pltpu.make_async_copy(links_in, links_ref, links_sem)
    links_copy.start()
    band_kernel(weights_ref, band_ref)
    links_copy.wait()
    put_masks(masks_ref, links_ref)


def put_padded(pad_ref, brick, lines, x_low, x_high, y_low, y_high, z_low, z_high):
    def joined(halves, before, after):
        lane = lanes_of(halves[0].shape)
        first = jnp.where(lane < CHANNELS, halves[1], before)
        second = jnp.where(lane >= HALF - CHANNELS, halves[0], after)
        return jnp.concatenate([halves[0], first], axis=-1), jnp.concatenate([halves[1], second], axis=-1)

    inside = joined(lines, z_low, z_high)
    x_low, x_high, y_low, y_high = [joined(face, 0.0, 0.0) for face in (x_low, x_high, y_low, y_high)]
    none = jnp.zeros((1, WIDE), F32)
    shifted = [[], [], []]
    for half in range(2):
        slabs = jnp.concatenate([x_low[half][None], inside[half], x_high[half][None]], axis=0)
        row = lax.broadcasted_iota(jnp.int32, slabs.shape, 1)
        low = jnp.concatenate([none, y_low[half], none], axis=0)[:, None, :]
        high = jnp.concatenate([none, y_high[half], none], axis=0)[:, None, :]
        shifted[0].append(jnp.where(row == 0, low, pltpu.roll(slabs, 1, 1)))
        shifted[1].append(slabs)
        shifted[2].append(jnp.where(row == EDGE - 1, high, pltpu.roll(slabs, EDGE - 1, 1)))
    for dy in range(3):
        pad_ref[dy, brick] = jnp.concatenate(shifted[dy], axis=1).astype(BF16)


def window(pad_ref, k):
    return pad_ref[k % 3, :, k // 3 : k // 3 + EDGE].reshape(ROWS, WIDE)


def convolve(pad_ref, band_ref):
    total = None
    for k in range(9):
        term = dot(window(pad_ref, k), band_ref[k])
        total = term if total is None else total + term
    return total


def half_lines(values):
    cube = values.reshape(BRICKS, EDGE, 2, EDGE, HALF)
    return [(cube[brick, :, 0], cube[brick, :, 1]) for brick in range(BRICKS)]


def put_halves(halves_ref, start, bricks):
    for brick, lines in enumerate(bricks):
        for half in range(2):
            first = start + brick * CUBE
            halves_ref[half, first : first + CUBE, :] = lines[half].reshape(CUBE, HALF)


def cotangent_lines(cotangent_ref):
    cube = cotangent_ref[...].astype(F32).reshape(BRICKS, EDGE, EDGE, LINE)
    return [(cube[brick, :, :, :HALF], cube[brick, :, :, HALF:]) for brick in range(BRICKS)]


def pack_faces(faces_ref, base, halves_ref, start, high):
    x_face = pair(halves_ref, start + ((EDGE - 1) * EDGE if high else 0), EDGE)
    y_face = pair(halves_ref, start + (EDGE - 1 if high else 0), EDGE, EDGE)
    for half in range(2):
        lanes = slice(half * HALF, half * HALF + HALF)
        faces_ref[base : base + EDGE, lanes] = x_face[half]
        faces_ref[base + EDGE : base + 2 * EDGE, lanes] = y_face[half]
    tile = halves_ref[1 if high else 0, start : start + CUBE, :]
    lane = lanes_of((16, 128)) // CHANNELS
    packed = jnp.zeros((16, 128), F32)
    for part in range(4):
        shift = (part + 1 if high else part) % 4 * CHANNELS
        piece = tile[part * 16 : part * 16 + 16]
        packed = jnp.where(lane == part, pltpu.roll(piece, shift, 1) if shift else piece, packed)
    faces_ref[base + 2 * EDGE : base + FACE, :128] = packed[:8]
    faces_ref[base + 2 * EDGE : base + FACE, 128:] = packed[8:]


def pack_all(bricks, halves_ref, faces_ref, high_out, low_out):
    put_halves(halves_ref, 0, bricks)
    for high, out_ref in ((True, high_out), (False, low_out)):
        for brick in range(BRICKS):
            pack_faces(faces_ref, brick * FACE, halves_ref, brick * CUBE, high)
        out_ref[...] = faces_ref[...].astype(BF16)


def to_partners(high_ref, low_ref, far_out, near_out):
    even = lax.axis_index("space") % 2 == 0
    far_out[...] = jnp.where(even, low_ref[...], high_ref[...])
    near_out[...] = jnp.where(even, high_ref[...], low_ref[...])


def faces_kernel(cotangent_ref, high_out, low_out, far_out, near_out, halves_ref, faces_ref):
    pack_all(cotangent_lines(cotangent_ref), halves_ref, faces_ref, high_out, low_out)
    to_partners(high_out, low_out, far_out, near_out)


def unpack_depth(halves, high):
    packed = jnp.concatenate(halves, axis=0)
    pieces = []
    for part in range(4):
        shift = ((3 - part) if high else (4 - part)) % 4 * CHANNELS
        pieces.append(pltpu.roll(packed, shift, 1) if shift else packed)
    return jnp.concatenate(pieces, axis=0).reshape(EDGE, EDGE, 128)


def first_kernel(
    links_in, received_ref, up_ref, band_ref, weights_ref,
    slope_out, hidden_out, turned_out, pad_out, back_out,
    volumes_ref, rows_ref, links_ref, links_sem,
):
    links_copy = pltpu.make_async_copy(links_in, links_ref, links_sem)
    links_copy.start()
    position = lax.axis_index("space")
    tiles = received_ref.shape[1] // (3 * BRICKS)
    rows_ref[0 : 3 * BRICKS * tiles] = jnp.sum(received_ref[...].astype(F32), axis=0)
    rows_ref[3 * BRICKS * tiles :] = jnp.zeros((2 * tiles, 128), F32)
    cells = []
    for tile in range(tiles):
        rows = rows_ref[pl.ds(tile, 8, stride=tiles), :]
        cells += [rows[:, :64], rows[:, 64:]]
    lifted = dot(jnp.concatenate(cells, axis=0).astype(BF16), up_ref[...])
    lifted = lifted.astype(BF16).astype(F32)
    for cell in range(8):
        a, b, c = cell // 4, cell // 2 % 2, cell % 2
        for sub in range(16):
            line = (4 * a + sub // 4) * EDGE + 4 * b + sub % 4
            volumes_ref[c, line * 8 : line * 8 + 8, :] = lifted[
                cell * 8 : cell * 8 + 8, sub * 128 : sub * 128 + 128
            ]
    links_copy.wait()
    for brick in range(BRICKS):

        def near(face):
            link = links_ref[0, brick, face]
            index = jnp.clip(link - BRICKS * (position - 1), 0, 3 * BRICKS - 1)
            return index, jnp.where(link >= 0, 1.0, 0.0).astype(F32)

        def x_face(face):
            index, present = near(face)
            line = EDGE * (EDGE - 1) if face % 2 == 0 else 0
            return [half * present for half in pair(volumes_ref, line * 8 + index, EDGE, 8)]

        def y_face(face):
            index, present = near(face)
            line = EDGE - 1 if face % 2 == 0 else 0
            return [half * present for half in pair(volumes_ref, line * 8 + index, EDGE, 8 * EDGE)]

        def z_face(face):
            index, present = near(face)
            tile = volumes_ref[1 if face % 2 == 0 else 0, pl.ds(index, CUBE, stride=8), :] * present
            return tile.reshape(EDGE, EDGE, HALF)

        own = [half.reshape(EDGE, EDGE, HALF) for half in pair(volumes_ref, BRICKS + brick, CUBE, 8)]
        put_padded(pad_out, brick, own, x_face(0), x_face(1), y_face(2), y_face(3), z_face(4), z_face(5))
    pre = convolve(pad_out, band_ref)
    sigmoid = 1.0 / (1.0 + jnp.exp(-pre))
    hidden = (pre / (1.0 + jnp.exp(-pre))).astype(BF16)
    slope_out[...] = sigmoid * (1.0 + pre * (1.0 - sigmoid))
    hidden_out[...] = hidden
    hidden = hidden.astype(F32)
    turned_out[...] = jnp.transpose(hidden).astype(BF16)
    build_band(back_out, flipped_rows(weights_ref[...].astype(F32)))


def hidden_faces_kernel(hidden_ref, _parts, high_out, low_out, far_out, near_out, halves_ref, faces_ref):
    pack_all(half_lines(hidden_ref[...].astype(F32)), halves_ref, faces_ref, high_out, low_out)
    to_partners(high_out, low_out, far_out, near_out)


def fold(outer, places):
    lane = lanes_of((CHANNELS, 128)) // CHANNELS
    folded = None
    for block in range(4):
        start, tile = places[block]
        rows = outer[start : start + CHANNELS, tile * 128 : tile * 128 + 128]
        folded = rows if folded is None else jnp.where(lane == block, rows, folded)
    quarter = [folded[8 * q : 8 * q + 8] for q in range(4)]
    small = lanes_of((8, 128)) // CHANNELS
    total = None
    for turn in range(4):
        mixed = quarter[0]
        for q in range(1, 4):
            mixed = jnp.where(small == (q + turn) % 4, quarter[q], mixed)
        if turn:
            mixed = pltpu.roll(mixed, 128 - turn * CHANNELS, 1)
        total = mixed if total is None else total + mixed
    return total


def diagonal(shift):
    places = [None] * 4
    for z in range(4):
        other = z + shift
        places[other % 4] = (z * CHANNELS, 0 if 0 <= other < 4 else 1)
    return places


def put_masks(masks_ref, links_ref):
    position = lax.axis_index("space")
    for brick in range(BRICKS):
        for face in range(6):
            first = links_ref[0, brick, face] - BRICKS * (position - 1 if face % 2 == 0 else position)
            for i in range(2 * BRICKS):
                row = (brick * 6 + face) * 2 * BRICKS + i
                masks_ref[row : row + 1, :] = jnp.full((1, 128), jnp.where(first == i, 1.0, 0.0).astype(F32))


def pad_all(pad_ref, bricks, masks_ref, high_pool, low_pool, high_own, low_own, far, near):
    position = lax.axis_index("space")
    half = BRICKS * FACE
    even = position % 2 == 0
    high_pool[0:half] = jnp.where(even, far[...], near[...]).astype(F32)
    high_pool[half:] = high_own[...].astype(F32)
    low_pool[0:half] = low_own[...].astype(F32)
    low_pool[half:] = jnp.where(even, near[...], far[...]).astype(F32)
    for brick, lines in enumerate(bricks):

        def face(number, axis):
            pool = high_pool if number % 2 == 0 else low_pool
            total = [0.0, 0.0]
            for i in range(2 * BRICKS):
                row = (brick * 6 + number) * 2 * BRICKS + i
                mask = masks_ref[row : row + 1, :]
                start = i * FACE + axis * EDGE
                for part in range(2):
                    found = pool[start : start + EDGE, part * HALF : part * HALF + HALF]
                    total[part] = total[part] + found * mask
            return total

        put_padded(
            pad_ref, brick, lines, face(0, 0), face(1, 0), face(2, 1), face(3, 1),
            unpack_depth(face(4, 2), True), unpack_depth(face(5, 2), False),
        )


def second_kernel(
    masks_ref, cotangent_ref, band_ref, slope_ref, hidden_ref, lifted_pad, high_own, low_own, far, near,
    sums_out, lifted_out,
    high_pool, low_pool, cotangent_pad, sums_ref,
):
    lifted_out[...] = window(lifted_pad, 4)[:, :HALF]
    bricks = cotangent_lines(cotangent_ref)
    pad_all(cotangent_pad, bricks, masks_ref, high_pool, low_pool, high_own, low_own, far, near)
    gradient = (convolve(cotangent_pad, band_ref) * slope_ref[...]).astype(BF16)
    gradient = jnp.transpose(gradient.astype(F32)).astype(BF16)
    hidden = hidden_ref[...]
    sums_ref[8 * BLOCKS :] = jnp.zeros((sums_ref.shape[0] - 8 * BLOCKS, 128), F32)
    for k in range(9):
        one = dot(gradient, window(lifted_pad, k))
        two = dot(hidden, window(cotangent_pad, 8 - k))
        for part in range(3):
            start = 8 * (3 * k + part)
            sums_ref[start : start + 8] = fold(one, diagonal(part - 1))
            start += 8 * 27
            sums_ref[start : start + 8] = fold(two, diagonal(1 - part))
    sums_out[...] = sums_ref[...].astype(BF16).reshape(sums_out.shape)


def fine_kernel(
    masks_ref, band_ref, lifted_ref, hidden_ref, high_own, low_own, far, near,
    fine_out, high_pool, low_pool, hidden_pad,
):
    bricks = half_lines(hidden_ref[...].astype(F32))
    pad_all(hidden_pad, bricks, masks_ref, high_pool, low_pool, high_own, low_own, far, near)
    fine = lifted_ref[...].astype(F32) + convolve(hidden_pad, band_ref)
    fine = fine.reshape(LINES // EDGE, 2, EDGE, HALF)
    fine = jnp.concatenate([fine[:, 0], fine[:, 1]], axis=-1)
    fine_out[...] = fine.astype(BF16).reshape(fine_out.shape)


def unpacked(tile):
    pieces = [tile] + [pltpu.roll(tile, 128 - q * CHANNELS, 1) for q in range(1, 4)]
    return jnp.concatenate(pieces, axis=0)[:, :CHANNELS]


def sum_kernel(scale, parts_ref, out_ref):
    total = jnp.sum(parts_ref[...].astype(F32), axis=0) * scale
    per = parts_ref.shape[1] // 8
    device = lax.axis_index("space") * lax.axis_size("dp") + lax.axis_index("dp")
    tiles = []
    for j in range(per):
        tile = total[8 * j : 8 * j + 8]
        block = jnp.transpose(unpacked(tile))
        turned = jnp.concatenate([block[8 * q : 8 * q + 8] for q in range(4)], axis=1)
        tiles.append(jnp.where(device * per + j < 27, turned, tile))
    total = jnp.concatenate(tiles, axis=0)
    out_ref[...] = jnp.broadcast_to(total.astype(BF16)[None], out_ref.shape)


def unpack_kernel(sums_ref, fine_ref, one_out, two_out, fine_out, rows_ref, one_ref, two_ref, sems, fine_sem):
    fine_copy = pltpu.make_async_copy(fine_ref, fine_out, fine_sem)
    fine_copy.start()
    rows_ref[...] = sums_ref[...].astype(F32).reshape(rows_ref.shape)
    copies = []
    for which, (block_ref, out) in enumerate(((one_ref, one_out), (two_ref, two_out))):
        for third in range(3):
            first = 9 * third
            for index in range(first, first + 9):
                row = 8 * (27 * which + index)
                block_ref[index] = unpacked(rows_ref[row : row + 8])
            part = pl.ds(first, 9)
            copies.append(pltpu.make_async_copy(block_ref.at[part], out.at[part], sems.at[which, third]))
            copies[-1].start()
    for copy in copies:
        copy.wait()
    fine_copy.wait()


def call(kernel, out_shape, scratch=(), hbm=(), inputs=1, limit=24, cost=None, out=pltpu.VMEM):
    spaces = [pl.ANY if i in hbm else pltpu.VMEM for i in range(inputs)]
    return pl.pallas_call(
        kernel,
        out_shape=out_shape,
        in_specs=[pl.BlockSpec(memory_space=space) for space in spaces],
        out_specs=jax.tree.map(lambda _: pl.BlockSpec(memory_space=out), out_shape),
        scratch_shapes=list(scratch),
        compiler_params=pltpu.CompilerParams(vmem_limit_bytes=limit * 2**20),
        cost_estimate=cost,
    )


def shape(*dims, dtype=BF16):
    return jax.ShapeDtypeStruct(dims, dtype)


def swapped(value, first):
    pairs = [(i, i + 1) for i in range(first, lax.axis_size("space") - 1, 2)]
    return lax.ppermute(value, "space", pairs + [(target, source) for source, target in pairs])


def body(coarse_latents, active_blocks, face_links, cotangent, up_weight, conv_one, conv_two):
    devices = lax.axis_size("space")
    everyone = devices * lax.axis_size("dp")
    held, width = coarse_latents.shape[1:]
    bricks = active_blocks.shape[1]
    tiles = width // 128
    scenes = 2 if lax.axis_size("dp") == 2 else 1
    packed = call(
        functools.partial(pick_kernel, scenes),
        shape(devices * scenes, 3 * BRICKS * tiles, 128),
        [
            pltpu.VMEM((1, bricks), jnp.int32),
            pltpu.VMEM((1, held, width), BF16),
            pltpu.VMEM(((bricks + 16) * tiles, 128), F32),
            pltpu.SemaphoreType.DMA((2,)),
        ],
        hbm=(0, 1),
        inputs=2,
        limit=60,
    )(active_blocks, coarse_latents)
    axes = ("space", "dp")
    received = lax.all_to_all(packed, axes if scenes == 2 else "space", split_axis=0, concat_axis=0, tiled=True)
    cost = pl.CostEstimate(flops=10**9, bytes_accessed=2 * 10**6, transcendentals=0)
    face = shape(BRICKS * FACE, LINE)
    halves = pltpu.VMEM((2, LINES, HALF), F32)
    faces = pltpu.VMEM((BRICKS * FACE, LINE), F32)
    pool = pltpu.VMEM((2 * BRICKS * FACE, LINE), F32)
    volume = shape(ROWS, HALF)
    links = [pltpu.SMEM(face_links.shape, jnp.int32), pltpu.SemaphoreType.DMA]
    pad_shape = (3, BRICKS, EDGE + 2, 2 * EDGE, WIDE)
    pad = pltpu.VMEM(pad_shape, BF16)
    high, low, far, near = call(faces_kernel, (face,) * 4, [halves, faces])(cotangent)
    far = swapped(far, 1)
    near = swapped(near, 0)
    masks = shape(BRICKS * 6 * 2 * BRICKS, 128, dtype=F32)
    band_one, masks = call(masks_kernel, (shape(*BAND), masks), links, hbm=(0,), inputs=2, cost=cost)(
        face_links, conv_one
    )
    slope, hidden, turned, lifted_pad, band_back = call(
        first_kernel,
        (
            shape(ROWS, HALF, dtype=F32), volume, shape(HALF, ROWS), shape(*pad_shape), shape(*BAND),
        ),
        [pltpu.VMEM((2, 8 * CUBE, 128), F32), pltpu.VMEM((8 * tiles, 128), F32), *links],
        hbm=(0,),
        inputs=5,
    )(face_links, received, up_weight, band_one, conv_two)
    per = -(-BLOCKS // everyone)
    per += per % 2
    sums, lifted = call(
        second_kernel,
        (shape(everyone, per * 8, 128), volume),
        [pool, pool, pad, pltpu.VMEM((everyone * per * 8, 128), F32)],
        inputs=10,
    )(masks, cotangent, band_back, slope, turned, lifted_pad, high, low, far, near)
    parts = lax.all_to_all(sums, axes, split_axis=0, concat_axis=0, tiled=True)
    hidden_high, hidden_low, hidden_far, hidden_near = call(
        hidden_faces_kernel, (face,) * 4, [halves, faces], hbm=(1,), inputs=2
    )(hidden, parts)
    hidden_far = swapped(hidden_far, 1)
    hidden_near = swapped(hidden_near, 0)
    band_two = call(band_kernel, shape(*BAND), cost=cost)(conv_two)
    fine = call(fine_kernel, shape(*cotangent.shape), [pool, pool, pad], inputs=8, cost=cost)(
        masks, band_two, lifted, hidden, hidden_high, hidden_low, hidden_far, hidden_near
    )
    scale = 1.0 / math.sqrt(lax.axis_size("dp") * devices * BRICKS * EDGE**3)
    total = call(functools.partial(sum_kernel, scale), shape(*sums.shape))(parts)
    gathered = lax.all_to_all(total, axes, split_axis=0, concat_axis=0, tiled=True)
    grads = shape(27, CHANNELS, CHANNELS, dtype=F32)
    block = pltpu.VMEM(grads.shape, F32)
    scratch = [pltpu.VMEM((everyone * per * 8, 128), F32), block, block]
    scratch += [pltpu.SemaphoreType.DMA((2, 3)), pltpu.SemaphoreType.DMA]
    grad_one, grad_two, fine = call(
        unpack_kernel, (grads, grads, shape(*fine.shape)), scratch, inputs=2, out=pl.ANY
    )(gathered, fine)
    return (fine, grad_one, grad_two)


def solution(mesh):
    return jax.shard_map(
        body,
        mesh=mesh,
        in_specs=(
            P("dp", "space", None),
            P("dp", None),
            P("dp", "space", None),
            P("dp", "space", None, None, None),
            P(),
            P(),
            P(),
        ),
        out_specs=(P("dp", "space", None, None, None), P(), P()),
        check_vma=False,
    )
```

```python
import functools
import math

import jax
import jax.numpy as jnp
from jax import lax
from jax.experimental import pallas as pl
from jax.experimental.pallas import tpu as pltpu
from jax.sharding import PartitionSpec as P

BF16 = jnp.bfloat16
F32 = jnp.float32
EDGE = 8
CHANNELS = 32
LINE = EDGE * CHANNELS
HALF = LINE // 2
WIDE = 2 * HALF
BRICKS = 2
CUBE = EDGE * EDGE
LINES = BRICKS * CUBE
BAND = (9, WIDE, HALF)
ROWS = 2 * LINES
FACE = 3 * EDGE
BLOCKS = 54


def dot(left, right):
    return jnp.dot(left, right, preferred_element_type=F32)


def dot_rows(left, right):
    return lax.dot_general(left, right, (((0,), (0,)), ((), ())), preferred_element_type=F32)


def pair(halves_ref, start, count, stride=1):
    index = pl.ds(start, count, stride=stride) if stride > 1 else pl.ds(start, count)
    return halves_ref[0, index, :], halves_ref[1, index, :]


def lanes_of(shape):
    return lax.broadcasted_iota(jnp.int32, shape, len(shape) - 1)


def pick_kernel(scenes, ids_hbm, latents_hbm, out_ref, ids_ref, latents_ref, rows_ref, sems):
    ids_copy = pltpu.make_async_copy(ids_hbm, ids_ref, sems.at[0])
    latents_copy = pltpu.make_async_copy(latents_hbm, latents_ref, sems.at[1])
    ids_copy.start()
    latents_copy.start()
    held, width = latents_ref.shape[1:]
    bricks = ids_ref.shape[1]
    margin = 8 * width // 128
    tiles = width // 128
    rows_ref[0:margin] = jnp.zeros((margin, 128), F32)
    rows_ref[margin + bricks * tiles :] = jnp.zeros((margin, 128), F32)
    first = lax.axis_index("space") * held
    rows = lax.broadcasted_iota(jnp.int32, (held, bricks), 0) + first
    ids_copy.wait()
    hot = jnp.where(rows == ids_ref[...], 1.0, 0.0).astype(BF16)
    latents_copy.wait()
    picked = dot_rows(hot, latents_ref[0])
    for tile in range(tiles):
        rows_ref[pl.ds(margin + tile, bricks, stride=tiles), :] = picked[:, tile * 128 : tile * 128 + 128]
    count = out_ref.shape[1]
    wanted = [jnp.where(lax.axis_index("dp") == scene, 1.0, 0.0).astype(F32) for scene in range(scenes)]
    for receiver in range(out_ref.shape[0] // scenes):
        start = margin + BRICKS * (receiver - 1) * tiles
        found = rows_ref[start : start + count]
        for scene in range(scenes):
            kept = found * wanted[scene] if scenes > 1 else found
            out_ref[receiver * scenes + scene] = kept.astype(BF16)


def build_band(band_ref, rows):
    shape = (3 * CHANNELS, HALF)
    row = lax.broadcasted_iota(jnp.int32, shape, 0)
    target = CHANNELS - (row // CHANNELS) * CHANNELS + row % CHANNELS
    distance = lanes_of(shape) - target
    band_ref[:, HALF:, :] = jnp.zeros((9, HALF, HALF), BF16)
    for z in range(-1, 5):
        select = jnp.where(distance == z * CHANNELS, 1.0, 0.0).astype(BF16)
        block = dot(rows, select).astype(BF16)
        start = z % 8 * CHANNELS
        band_ref[:, start : start + CHANNELS, :] = block.reshape(9, CHANNELS, HALF)


def weight_rows(weights):
    cube = weights.reshape(9, 3, CHANNELS, CHANNELS)
    rows = jnp.concatenate([cube[:, 0], cube[:, 1], cube[:, 2]], axis=-1)
    return rows.reshape(9 * CHANNELS, 3 * CHANNELS).astype(BF16)


def flipped_rows(weights):
    cube = jnp.swapaxes(weights, 1, 2).reshape(9, 3, CHANNELS, CHANNELS)
    pieces = [jnp.concatenate([cube[8 - k, 2], cube[8 - k, 1], cube[8 - k, 0]], axis=-1) for k in range(9)]
    return jnp.concatenate(pieces, axis=0).astype(BF16)


def band_kernel(weights_ref, band_ref):
    build_band(band_ref, weight_rows(weights_ref[...].astype(F32)))


def masks_kernel(links_in, weights_ref, band_ref, masks_ref, links_ref, links_sem):
    links_copy = pltpu.make_async_copy(links_in, links_ref, links_sem)
    links_copy.start()
    band_kernel(weights_ref, band_ref)
    links_copy.wait()
    put_masks(masks_ref, links_ref)


def put_padded(pad_ref, brick, lines, x_low, x_high, y_low, y_high, z_low, z_high):
    def joined(halves, before, after):
        lane = lanes_of(halves[0].shape)
        first = jnp.where(lane < CHANNELS, halves[1], before)
        second = jnp.where(lane >= HALF - CHANNELS, halves[0], after)
        return jnp.concatenate([halves[0], first], axis=-1), jnp.concatenate([halves[1], second], axis=-1)

    inside = joined(lines, z_low, z_high)
    x_low, x_high, y_low, y_high = [joined(face, 0.0, 0.0) for face in (x_low, x_high, y_low, y_high)]
    none = jnp.zeros((1, WIDE), F32)
    shifted = [[], [], []]
    for half in range(2):
        slabs = jnp.concatenate([x_low[half][None], inside[half], x_high[half][None]], axis=0)
        row = lax.broadcasted_iota(jnp.int32, slabs.shape, 1)
        low = jnp.concatenate([none, y_low[half], none], axis=0)[:, None, :]
        high = jnp.concatenate([none, y_high[half], none], axis=0)[:, None, :]
        shifted[0].append(jnp.where(row == 0, low, pltpu.roll(slabs, 1, 1)))
        shifted[1].append(slabs)
        shifted[2].append(jnp.where(row == EDGE - 1, high, pltpu.roll(slabs, EDGE - 1, 1)))
    for dy in range(3):
        pad_ref[dy, brick] = jnp.concatenate(shifted[dy], axis=1).astype(BF16)


def window(pad_ref, k):
    return pad_ref[k % 3, :, k // 3 : k // 3 + EDGE].reshape(ROWS, WIDE)


def convolve(pad_ref, band_ref):
    total = None
    for k in range(9):
        term = dot(window(pad_ref, k), band_ref[k])
        total = term if total is None else total + term
    return total


def half_lines(values):
    cube = values.reshape(BRICKS, EDGE, 2, EDGE, HALF)
    return [(cube[brick, :, 0], cube[brick, :, 1]) for brick in range(BRICKS)]


def put_halves(halves_ref, start, bricks):
    for brick, lines in enumerate(bricks):
        for half in range(2):
            first = start + brick * CUBE
            halves_ref[half, first : first + CUBE, :] = lines[half].reshape(CUBE, HALF)


def cotangent_lines(cotangent_ref):
    cube = cotangent_ref[...].astype(F32).reshape(BRICKS, EDGE, EDGE, LINE)
    return [(cube[brick, :, :, :HALF], cube[brick, :, :, HALF:]) for brick in range(BRICKS)]


def pack_faces(faces_ref, base, halves_ref, start, high):
    x_face = pair(halves_ref, start + ((EDGE - 1) * EDGE if high else 0), EDGE)
    y_face = pair(halves_ref, start + (EDGE - 1 if high else 0), EDGE, EDGE)
    for half in range(2):
        lanes = slice(half * HALF, half * HALF + HALF)
        faces_ref[base : base + EDGE, lanes] = x_face[half]
        faces_ref[base + EDGE : base + 2 * EDGE, lanes] = y_face[half]
    tile = halves_ref[1 if high else 0, start : start + CUBE, :]
    lane = lanes_of((16, 128)) // CHANNELS
    packed = jnp.zeros((16, 128), F32)
    for part in range(4):
        shift = (part + 1 if high else part) % 4 * CHANNELS
        piece = tile[part * 16 : part * 16 + 16]
        packed = jnp.where(lane == part, pltpu.roll(piece, shift, 1) if shift else piece, packed)
    faces_ref[base + 2 * EDGE : base + FACE, :128] = packed[:8]
    faces_ref[base + 2 * EDGE : base + FACE, 128:] = packed[8:]


def pack_all(bricks, halves_ref, faces_ref, high_out, low_out):
    put_halves(halves_ref, 0, bricks)
    for high, out_ref in ((True, high_out), (False, low_out)):
        for brick in range(BRICKS):
            pack_faces(faces_ref, brick * FACE, halves_ref, brick * CUBE, high)
        out_ref[...] = faces_ref[...].astype(BF16)


def to_partners(high_ref, low_ref, far_out, near_out):
    even = lax.axis_index("space") % 2 == 0
    far_out[...] = jnp.where(even, low_ref[...], high_ref[...])
    near_out[...] = jnp.where(even, high_ref[...], low_ref[...])


def faces_kernel(cotangent_ref, high_out, low_out, far_out, near_out, halves_ref, faces_ref):
    pack_all(cotangent_lines(cotangent_ref), halves_ref, faces_ref, high_out, low_out)
    to_partners(high_out, low_out, far_out, near_out)


def unpack_depth(halves, high):
    packed = jnp.concatenate(halves, axis=0)
    pieces = []
    for part in range(4):
        shift = ((3 - part) if high else (4 - part)) % 4 * CHANNELS
        pieces.append(pltpu.roll(packed, shift, 1) if shift else packed)
    return jnp.concatenate(pieces, axis=0).reshape(EDGE, EDGE, 128)


def first_kernel(
    links_in, received_ref, up_ref, band_ref, weights_ref,
    slope_out, hidden_out, turned_out, pad_out, back_out,
    volumes_ref, rows_ref, links_ref, links_sem,
):
    links_copy = pltpu.make_async_copy(links_in, links_ref, links_sem)
    links_copy.start()
    position = lax.axis_index("space")
    tiles = received_ref.shape[1] // (3 * BRICKS)
    rows_ref[0 : 3 * BRICKS * tiles] = jnp.sum(received_ref[...].astype(F32), axis=0)
    rows_ref[3 * BRICKS * tiles :] = jnp.zeros((2 * tiles, 128), F32)
    cells = []
    for tile in range(tiles):
        rows = rows_ref[pl.ds(tile, 8, stride=tiles), :]
        cells += [rows[:, :64], rows[:, 64:]]
    lifted = dot(jnp.concatenate(cells, axis=0).astype(BF16), up_ref[...])
    lifted = lifted.astype(BF16).astype(F32)
    for cell in range(8):
        a, b, c = cell // 4, cell // 2 % 2, cell % 2
        for sub in range(16):
            line = (4 * a + sub // 4) * EDGE + 4 * b + sub % 4
            volumes_ref[c, line * 8 : line * 8 + 8, :] = lifted[
                cell * 8 : cell * 8 + 8, sub * 128 : sub * 128 + 128
            ]
    links_copy.wait()
    for brick in range(BRICKS):

        def near(face):
            link = links_ref[0, brick, face]
            index = jnp.clip(link - BRICKS * (position - 1), 0, 3 * BRICKS - 1)
            return index, jnp.where(link >= 0, 1.0, 0.0).astype(F32)

        def x_face(face):
            index, present = near(face)
            line = EDGE * (EDGE - 1) if face % 2 == 0 else 0
            return [half * present for half in pair(volumes_ref, line * 8 + index, EDGE, 8)]

        def y_face(face):
            index, present = near(face)
            line = EDGE - 1 if face % 2 == 0 else 0
            return [half * present for half in pair(volumes_ref, line * 8 + index, EDGE, 8 * EDGE)]

        def z_face(face):
            index, present = near(face)
            tile = volumes_ref[1 if face % 2 == 0 else 0, pl.ds(index, CUBE, stride=8), :] * present
            return tile.reshape(EDGE, EDGE, HALF)

        own = [half.reshape(EDGE, EDGE, HALF) for half in pair(volumes_ref, BRICKS + brick, CUBE, 8)]
        put_padded(pad_out, brick, own, x_face(0), x_face(1), y_face(2), y_face(3), z_face(4), z_face(5))
    pre = convolve(pad_out, band_ref)
    sigmoid = 1.0 / (1.0 + jnp.exp(-pre))
    hidden = (pre / (1.0 + jnp.exp(-pre))).astype(BF16)
    slope_out[...] = sigmoid * (1.0 + pre * (1.0 - sigmoid))
    hidden_out[...] = hidden
    hidden = hidden.astype(F32)
    turned_out[...] = jnp.transpose(hidden).astype(BF16)
    build_band(back_out, flipped_rows(weights_ref[...].astype(F32)))


def hidden_faces_kernel(hidden_ref, _parts, high_out, low_out, far_out, near_out, halves_ref, faces_ref):
    pack_all(half_lines(hidden_ref[...].astype(F32)), halves_ref, faces_ref, high_out, low_out)
    to_partners(high_out, low_out, far_out, near_out)


def fold(outer, places):
    lane = lanes_of((CHANNELS, 128)) // CHANNELS
    folded = None
    for block in range(4):
        start, tile = places[block]
        rows = outer[start : start + CHANNELS, tile * 128 : tile * 128 + 128]
        folded = rows if folded is None else jnp.where(lane == block, rows, folded)
    quarter = [folded[8 * q : 8 * q + 8] for q in range(4)]
    small = lanes_of((8, 128)) // CHANNELS
    total = None
    for turn in range(4):
        mixed = quarter[0]
        for q in range(1, 4):
            mixed = jnp.where(small == (q + turn) % 4, quarter[q], mixed)
        if turn:
            mixed = pltpu.roll(mixed, 128 - turn * CHANNELS, 1)
        total = mixed if total is None else total + mixed
    return total


def diagonal(shift):
    places = [None] * 4
    for z in range(4):
        other = z + shift
        places[other % 4] = (z * CHANNELS, 0 if 0 <= other < 4 else 1)
    return places


def put_masks(masks_ref, links_ref):
    position = lax.axis_index("space")
    for brick in range(BRICKS):
        for face in range(6):
            first = links_ref[0, brick, face] - BRICKS * (position - 1 if face % 2 == 0 else position)
            for i in range(2 * BRICKS):
                row = (brick * 6 + face) * 2 * BRICKS + i
                masks_ref[row : row + 1, :] = jnp.full((1, 128), jnp.where(first == i, 1.0, 0.0).astype(F32))


def pad_all(pad_ref, bricks, masks_ref, high_pool, low_pool, high_own, low_own, far, near):
    position = lax.axis_index("space")
    half = BRICKS * FACE
    even = position % 2 == 0
    high_pool[0:half] = jnp.where(even, far[...], near[...]).astype(F32)
    high_pool[half:] = high_own[...].astype(F32)
    low_pool[0:half] = low_own[...].astype(F32)
    low_pool[half:] = jnp.where(even, near[...], far[...]).astype(F32)
    for brick, lines in enumerate(bricks):

        def face(number, axis):
            pool = high_pool if number % 2 == 0 else low_pool
            total = [0.0, 0.0]
            for i in range(2 * BRICKS):
                row = (brick * 6 + number) * 2 * BRICKS + i
                mask = masks_ref[row : row + 1, :]
                start = i * FACE + axis * EDGE
                for part in range(2):
                    found = pool[start : start + EDGE, part * HALF : part * HALF + HALF]
                    total[part] = total[part] + found * mask
            return total

        put_padded(
            pad_ref, brick, lines, face(0, 0), face(1, 0), face(2, 1), face(3, 1),
            unpack_depth(face(4, 2), True), unpack_depth(face(5, 2), False),
        )


def second_kernel(
    masks_ref, cotangent_ref, band_ref, slope_ref, hidden_ref, lifted_pad, high_own, low_own, far, near,
    sums_out, lifted_out,
    high_pool, low_pool, cotangent_pad, sums_ref,
):
    lifted_out[...] = window(lifted_pad, 4)[:, :HALF]
    bricks = cotangent_lines(cotangent_ref)
    pad_all(cotangent_pad, bricks, masks_ref, high_pool, low_pool, high_own, low_own, far, near)
    gradient = (convolve(cotangent_pad, band_ref) * slope_ref[...]).astype(BF16)
    gradient = jnp.transpose(gradient.astype(F32)).astype(BF16)
    hidden = hidden_ref[...]
    sums_ref[8 * BLOCKS :] = jnp.zeros((sums_ref.shape[0] - 8 * BLOCKS, 128), F32)
    for k in range(9):
        one = dot(gradient, window(lifted_pad, k))
        two = dot(hidden, window(cotangent_pad, 8 - k))
        for part in range(3):
            start = 8 * (3 * k + part)
            sums_ref[start : start + 8] = fold(one, diagonal(part - 1))
            start += 8 * 27
            sums_ref[start : start + 8] = fold(two, diagonal(1 - part))
    sums_out[...] = sums_ref[...].astype(BF16)


def fine_kernel(
    masks_ref, band_ref, lifted_ref, hidden_ref, high_own, low_own, far, near,
    fine_out, high_pool, low_pool, hidden_pad,
):
    bricks = half_lines(hidden_ref[...].astype(F32))
    pad_all(hidden_pad, bricks, masks_ref, high_pool, low_pool, high_own, low_own, far, near)
    fine = lifted_ref[...].astype(F32) + convolve(hidden_pad, band_ref)
    fine = fine.reshape(LINES // EDGE, 2, EDGE, HALF)
    fine = jnp.concatenate([fine[:, 0], fine[:, 1]], axis=-1)
    fine_out[...] = fine.astype(BF16).reshape(fine_out.shape)


def sum_kernel(devices, scale, parts_ref, out_ref, rows_ref):
    rows_ref[...] = parts_ref[...].astype(F32)
    share = rows_ref.shape[0] // devices
    pieces = [rows_ref[share * i : share * i + share] for i in range(devices)]
    while len(pieces) > 1:
        pairs = [a + b for a, b in zip(pieces[::2], pieces[1::2])]
        pieces = pairs + pieces[len(pieces) - len(pieces) % 2 :]
    total = pieces[0] * scale
    for i in range(devices):
        rows_ref[share * i : share * i + share] = total
    out_ref[...] = rows_ref[...].astype(BF16)


def unpacked(tile):
    pieces = [tile] + [pltpu.roll(tile, 128 - q * CHANNELS, 1) for q in range(1, 4)]
    return jnp.concatenate(pieces, axis=0)[:, :CHANNELS]


def turned(tiles):
    lane = lanes_of((8, 128)) // CHANNELS
    rows = []
    for q in range(4):
        mixed = jnp.zeros((8, 128), F32)
        for n, tile in enumerate(tiles):
            shift = (n - q) % 4 * CHANNELS
            mixed = jnp.where(lane == n, pltpu.roll(tile, shift, 1) if shift else tile, mixed)
        rows.append(mixed)
    return jnp.transpose(jnp.concatenate(rows, axis=0))


def unpack_kernel(sums_ref, fine_ref, one_out, two_out, fine_out, rows_ref, one_ref, two_ref, sems, fine_sem):
    fine_copy = pltpu.make_async_copy(fine_ref, fine_out, fine_sem)
    fine_copy.start()
    rows_ref[...] = sums_ref[...].astype(F32)
    tiles = [rows_ref[8 * index : 8 * index + 8] for index in range(BLOCKS)]
    copies = []
    for which, (block_ref, out) in enumerate(((one_ref, one_out), (two_ref, two_out))):
        for part, (first, last) in enumerate(((0, 8), (8, 16), (16, 27))):
            for index in range(first, last):
                if which:
                    block_ref[index] = unpacked(tiles[27 + index])
                elif index % 4 == 0:
                    blocks = turned(tiles[index : min(index + 4, 27)])
                    for n in range(min(4, 27 - index)):
                        block_ref[index + n] = blocks[CHANNELS * n : CHANNELS * n + CHANNELS]
            span = pl.ds(first, last - first)
            copies.append(pltpu.make_async_copy(block_ref.at[span], out.at[span], sems.at[which, part]))
            copies[-1].start()
    for copy in copies:
        copy.wait()
    fine_copy.wait()


def call(kernel, out_shape, scratch=(), hbm=(), inputs=1, limit=24, cost=None, out=pltpu.VMEM):
    spaces = [pl.ANY if i in hbm else pltpu.VMEM for i in range(inputs)]
    return pl.pallas_call(
        kernel,
        out_shape=out_shape,
        in_specs=[pl.BlockSpec(memory_space=space) for space in spaces],
        out_specs=jax.tree.map(lambda _: pl.BlockSpec(memory_space=out), out_shape),
        scratch_shapes=list(scratch),
        compiler_params=pltpu.CompilerParams(vmem_limit_bytes=limit * 2**20),
        cost_estimate=cost,
    )


def shape(*dims, dtype=BF16):
    return jax.ShapeDtypeStruct(dims, dtype)


def swapped(value, first):
    pairs = [(i, i + 1) for i in range(first, lax.axis_size("space") - 1, 2)]
    return lax.ppermute(value, "space", pairs + [(target, source) for source, target in pairs])


def exchanged(rows):
    everyone = lax.axis_size("space") * lax.axis_size("dp")
    shares = rows.reshape(everyone, -1, 2, 128)
    shares = lax.all_to_all(shares, ("space", "dp"), split_axis=0, concat_axis=0, tiled=True)
    return shares.reshape(rows.shape)


def body(coarse_latents, active_blocks, face_links, cotangent, up_weight, conv_one, conv_two):
    devices = lax.axis_size("space")
    everyone = devices * lax.axis_size("dp")
    held, width = coarse_latents.shape[1:]
    bricks = active_blocks.shape[1]
    tiles = width // 128
    scenes = 2 if lax.axis_size("dp") == 2 else 1
    packed = call(
        functools.partial(pick_kernel, scenes),
        shape(devices * scenes, 3 * BRICKS * tiles, 128),
        [
            pltpu.VMEM((1, bricks), jnp.int32),
            pltpu.VMEM((1, held, width), BF16),
            pltpu.VMEM(((bricks + 16) * tiles, 128), F32),
            pltpu.SemaphoreType.DMA((2,)),
        ],
        hbm=(0, 1),
        inputs=2,
        limit=60,
    )(active_blocks, coarse_latents)
    axes = ("space", "dp")
    received = lax.all_to_all(packed, axes if scenes == 2 else "space", split_axis=0, concat_axis=0, tiled=True)
    cost = pl.CostEstimate(flops=10**9, bytes_accessed=2 * 10**6, transcendentals=0)
    face = shape(BRICKS * FACE, LINE)
    halves = pltpu.VMEM((2, LINES, HALF), F32)
    faces = pltpu.VMEM((BRICKS * FACE, LINE), F32)
    pool = pltpu.VMEM((2 * BRICKS * FACE, LINE), F32)
    volume = shape(ROWS, HALF)
    links = [pltpu.SMEM(face_links.shape, jnp.int32), pltpu.SemaphoreType.DMA]
    pad_shape = (3, BRICKS, EDGE + 2, 2 * EDGE, WIDE)
    pad = pltpu.VMEM(pad_shape, BF16)
    high, low, far, near = call(faces_kernel, (face,) * 4, [halves, faces])(cotangent)
    far = swapped(far, 1)
    near = swapped(near, 0)
    masks = shape(BRICKS * 6 * 2 * BRICKS, 128, dtype=F32)
    band_one, masks = call(masks_kernel, (shape(*BAND), masks), links, hbm=(0,), inputs=2, cost=cost)(
        face_links, conv_one
    )
    slope, hidden, turned, lifted_pad, band_back = call(
        first_kernel,
        (
            shape(ROWS, HALF, dtype=F32), volume, shape(HALF, ROWS), shape(*pad_shape), shape(*BAND),
        ),
        [pltpu.VMEM((2, 8 * CUBE, 128), F32), pltpu.VMEM((8 * tiles, 128), F32), *links],
        hbm=(0,),
        inputs=5,
    )(face_links, received, up_weight, band_one, conv_two)
    share = 2 * -(-4 * BLOCKS // everyone)
    packed_rows = (everyone * share, 128)
    sums, lifted = call(
        second_kernel,
        (shape(*packed_rows), volume),
        [pool, pool, pad, pltpu.VMEM(packed_rows, F32)],
        inputs=10,
    )(masks, cotangent, band_back, slope, turned, lifted_pad, high, low, far, near)
    parts = exchanged(sums)
    hidden_high, hidden_low, hidden_far, hidden_near = call(
        hidden_faces_kernel, (face,) * 4, [halves, faces], hbm=(1,), inputs=2
    )(hidden, parts)
    hidden_far = swapped(hidden_far, 1)
    hidden_near = swapped(hidden_near, 0)
    band_two = call(band_kernel, shape(*BAND), cost=cost)(conv_two)
    fine = call(fine_kernel, shape(*cotangent.shape), [pool, pool, pad], inputs=8, cost=cost)(
        masks, band_two, lifted, hidden, hidden_high, hidden_low, hidden_far, hidden_near
    )
    scale = 1.0 / math.sqrt(lax.axis_size("dp") * devices * BRICKS * EDGE**3)
    total = call(
        functools.partial(sum_kernel, everyone, scale), shape(*packed_rows), [pltpu.VMEM(packed_rows, F32)]
    )(parts)
    gathered = exchanged(total)
    grads = shape(27, CHANNELS, CHANNELS, dtype=F32)
    block = pltpu.VMEM(grads.shape, F32)
    scratch = [pltpu.VMEM(packed_rows, F32), block, block]
    scratch += [pltpu.SemaphoreType.DMA((2, 3)), pltpu.SemaphoreType.DMA]
    grad_one, grad_two, fine = call(
        unpack_kernel, (grads, grads, shape(*fine.shape)), scratch, inputs=2, out=pl.ANY
    )(gathered, fine)
    return (fine, grad_one, grad_two)


def solution(mesh):
    return jax.shard_map(
        body,
        mesh=mesh,
        in_specs=(
            P("dp", "space", None),
            P("dp", None),
            P("dp", "space", None),
            P("dp", "space", None, None, None),
            P(),
            P(),
            P(),
        ),
        out_specs=(P("dp", "space", None, None, None), P(), P()),
        check_vma=False,
    )
```

```python
import functools
import math

import jax
import jax.numpy as jnp
from jax import lax
from jax.experimental import pallas as pl
from jax.experimental.pallas import tpu as pltpu
from jax.sharding import PartitionSpec as P

BF16 = jnp.bfloat16
F32 = jnp.float32
EDGE = 8
CHANNELS = 32
LINE = EDGE * CHANNELS
HALF = LINE // 2
WIDE = 2 * HALF
BRICKS = 2
CUBE = EDGE * EDGE
LINES = BRICKS * CUBE
BAND = (9, WIDE, HALF)
ROWS = 2 * LINES
FACE = 3 * EDGE
BLOCKS = 54


def dot(left, right):
    return jnp.dot(left, right, preferred_element_type=F32)


def dot_rows(left, right):
    return lax.dot_general(left, right, (((0,), (0,)), ((), ())), preferred_element_type=F32)


def pair(halves_ref, start, count, stride=1):
    index = pl.ds(start, count, stride=stride) if stride > 1 else pl.ds(start, count)
    return halves_ref[0, index, :], halves_ref[1, index, :]


def lanes_of(shape):
    return lax.broadcasted_iota(jnp.int32, shape, len(shape) - 1)


def pick_kernel(scenes, ids_hbm, latents_hbm, out_ref, ids_ref, latents_ref, rows_ref, sems):
    ids_copy = pltpu.make_async_copy(ids_hbm, ids_ref, sems.at[0])
    latents_copy = pltpu.make_async_copy(latents_hbm, latents_ref, sems.at[1])
    ids_copy.start()
    latents_copy.start()
    held, width = latents_ref.shape[1:]
    bricks = ids_ref.shape[1]
    margin = 8 * width // 128
    tiles = width // 128
    rows_ref[0:margin] = jnp.zeros((margin, 128), F32)
    rows_ref[margin + bricks * tiles :] = jnp.zeros((margin, 128), F32)
    first = lax.axis_index("space") * held
    rows = lax.broadcasted_iota(jnp.int32, (held, bricks), 0) + first
    ids_copy.wait()
    hot = jnp.where(rows == ids_ref[...], 1.0, 0.0).astype(BF16)
    latents_copy.wait()
    picked = dot_rows(hot, latents_ref[0])
    for tile in range(tiles):
        rows_ref[pl.ds(margin + tile, bricks, stride=tiles), :] = picked[:, tile * 128 : tile * 128 + 128]
    count = out_ref.shape[1]
    wanted = [jnp.where(lax.axis_index("dp") == scene, 1.0, 0.0).astype(F32) for scene in range(scenes)]
    for receiver in range(out_ref.shape[0] // scenes):
        start = margin + BRICKS * (receiver - 1) * tiles
        found = rows_ref[start : start + count]
        for scene in range(scenes):
            kept = found * wanted[scene] if scenes > 1 else found
            out_ref[receiver * scenes + scene] = kept.astype(BF16)


def build_band(band_ref, rows):
    shape = (3 * CHANNELS, HALF)
    row = lax.broadcasted_iota(jnp.int32, shape, 0)
    target = CHANNELS - (row // CHANNELS) * CHANNELS + row % CHANNELS
    distance = lanes_of(shape) - target
    band_ref[:, HALF:, :] = jnp.zeros((9, HALF, HALF), BF16)
    for z in range(-1, 5):
        select = jnp.where(distance == z * CHANNELS, 1.0, 0.0).astype(BF16)
        block = dot(rows, select).astype(BF16)
        start = z % 8 * CHANNELS
        band_ref[:, start : start + CHANNELS, :] = block.reshape(9, CHANNELS, HALF)


def weight_rows(weights):
    cube = weights.reshape(9, 3, CHANNELS, CHANNELS)
    rows = jnp.concatenate([cube[:, 0], cube[:, 1], cube[:, 2]], axis=-1)
    return rows.reshape(9 * CHANNELS, 3 * CHANNELS).astype(BF16)


def flipped_rows(weights):
    cube = jnp.swapaxes(weights, 1, 2).reshape(9, 3, CHANNELS, CHANNELS)
    pieces = [jnp.concatenate([cube[8 - k, 2], cube[8 - k, 1], cube[8 - k, 0]], axis=-1) for k in range(9)]
    return jnp.concatenate(pieces, axis=0).astype(BF16)


def band_kernel(weights_ref, band_ref):
    build_band(band_ref, weight_rows(weights_ref[...].astype(F32)))


def masks_kernel(links_in, weights_ref, band_ref, masks_ref, links_ref, links_sem):
    links_copy = pltpu.make_async_copy(links_in, links_ref, links_sem)
    links_copy.start()
    band_kernel(weights_ref, band_ref)
    links_copy.wait()
    put_masks(masks_ref, links_ref)


def put_padded(pad_ref, brick, lines, x_low, x_high, y_low, y_high, z_low, z_high):
    def joined(halves, before, after):
        lane = lanes_of(halves[0].shape)
        first = jnp.where(lane < CHANNELS, halves[1], before)
        second = jnp.where(lane >= HALF - CHANNELS, halves[0], after)
        return jnp.concatenate([halves[0], first], axis=-1), jnp.concatenate([halves[1], second], axis=-1)

    inside = joined(lines, z_low, z_high)
    x_low, x_high, y_low, y_high = [joined(face, 0.0, 0.0) for face in (x_low, x_high, y_low, y_high)]
    none = jnp.zeros((1, WIDE), F32)
    shifted = [[], [], []]
    for half in range(2):
        slabs = jnp.concatenate([x_low[half][None], inside[half], x_high[half][None]], axis=0)
        row = lax.broadcasted_iota(jnp.int32, slabs.shape, 1)
        low = jnp.concatenate([none, y_low[half], none], axis=0)[:, None, :]
        high = jnp.concatenate([none, y_high[half], none], axis=0)[:, None, :]
        shifted[0].append(jnp.where(row == 0, low, pltpu.roll(slabs, 1, 1)))
        shifted[1].append(slabs)
        shifted[2].append(jnp.where(row == EDGE - 1, high, pltpu.roll(slabs, EDGE - 1, 1)))
    for dy in range(3):
        pad_ref[dy, brick] = jnp.concatenate(shifted[dy], axis=1).astype(BF16)


def window(pad_ref, k):
    return pad_ref[k % 3, :, k // 3 : k // 3 + EDGE].reshape(ROWS, WIDE)


def convolve(pad_ref, band_ref):
    both, last = None, None
    for dy in range(3):
        slabs = pad_ref[dy, :, : EDGE + 1].reshape(-1, WIDE)
        term = dot(slabs, jnp.concatenate([band_ref[dy], band_ref[3 + dy]], axis=1))
        both = term if both is None else both + term
        term = dot(window(pad_ref, 6 + dy), band_ref[6 + dy])
        last = term if last is None else last + term
    both = both.reshape(BRICKS, EDGE + 1, 2 * EDGE, 2 * HALF)
    total = both[:, :EDGE, :, :HALF] + both[:, 1:, :, HALF:]
    return total.reshape(ROWS, HALF) + last


def half_lines(values):
    cube = values.reshape(BRICKS, EDGE, 2, EDGE, HALF)
    return [(cube[brick, :, 0], cube[brick, :, 1]) for brick in range(BRICKS)]


def put_halves(halves_ref, start, bricks):
    for brick, lines in enumerate(bricks):
        for half in range(2):
            first = start + brick * CUBE
            halves_ref[half, first : first + CUBE, :] = lines[half].reshape(CUBE, HALF)


def cotangent_lines(cotangent_ref):
    cube = cotangent_ref[...].astype(F32).reshape(BRICKS, EDGE, EDGE, LINE)
    return [(cube[brick, :, :, :HALF], cube[brick, :, :, HALF:]) for brick in range(BRICKS)]


def pack_faces(faces_ref, base, halves_ref, start, high):
    x_face = pair(halves_ref, start + ((EDGE - 1) * EDGE if high else 0), EDGE)
    y_face = pair(halves_ref, start + (EDGE - 1 if high else 0), EDGE, EDGE)
    for half in range(2):
        lanes = slice(half * HALF, half * HALF + HALF)
        faces_ref[base : base + EDGE, lanes] = x_face[half]
        faces_ref[base + EDGE : base + 2 * EDGE, lanes] = y_face[half]
    tile = halves_ref[1 if high else 0, start : start + CUBE, :]
    lane = lanes_of((16, 128)) // CHANNELS
    packed = jnp.zeros((16, 128), F32)
    for part in range(4):
        shift = (part + 1 if high else part) % 4 * CHANNELS
        piece = tile[part * 16 : part * 16 + 16]
        packed = jnp.where(lane == part, pltpu.roll(piece, shift, 1) if shift else piece, packed)
    faces_ref[base + 2 * EDGE : base + FACE, :128] = packed[:8]
    faces_ref[base + 2 * EDGE : base + FACE, 128:] = packed[8:]


def pack_all(bricks, halves_ref, faces_ref, high_out, low_out):
    put_halves(halves_ref, 0, bricks)
    for high, out_ref in ((True, high_out), (False, low_out)):
        for brick in range(BRICKS):
            pack_faces(faces_ref, brick * FACE, halves_ref, brick * CUBE, high)
        out_ref[...] = faces_ref[...].astype(BF16)


def to_partners(high_ref, low_ref, far_out, near_out):
    even = lax.axis_index("space") % 2 == 0
    far_out[...] = jnp.where(even, low_ref[...], high_ref[...])
    near_out[...] = jnp.where(even, high_ref[...], low_ref[...])


def faces_kernel(cotangent_ref, high_out, low_out, far_out, near_out, halves_ref, faces_ref):
    pack_all(cotangent_lines(cotangent_ref), halves_ref, faces_ref, high_out, low_out)
    to_partners(high_out, low_out, far_out, near_out)


def unpack_depth(halves, high):
    packed = jnp.concatenate(halves, axis=0)
    pieces = []
    for part in range(4):
        shift = ((3 - part) if high else (4 - part)) % 4 * CHANNELS
        pieces.append(pltpu.roll(packed, shift, 1) if shift else packed)
    return jnp.concatenate(pieces, axis=0).reshape(EDGE, EDGE, 128)


def first_kernel(
    links_in, received_ref, up_ref, band_ref, weights_ref,
    slope_out, hidden_out, turned_out, pad_out, back_out,
    volumes_ref, rows_ref, links_ref, links_sem,
):
    links_copy = pltpu.make_async_copy(links_in, links_ref, links_sem)
    links_copy.start()
    position = lax.axis_index("space")
    tiles = received_ref.shape[1] // (3 * BRICKS)
    rows_ref[0 : 3 * BRICKS * tiles] = jnp.sum(received_ref[...].astype(F32), axis=0)
    rows_ref[3 * BRICKS * tiles :] = jnp.zeros((2 * tiles, 128), F32)
    cells = []
    for tile in range(tiles):
        rows = rows_ref[pl.ds(tile, 8, stride=tiles), :]
        cells += [rows[:, :64], rows[:, 64:]]
    lifted = dot(jnp.concatenate(cells, axis=0).astype(BF16), up_ref[...])
    lifted = lifted.astype(BF16).astype(F32)
    for cell in range(8):
        a, b, c = cell // 4, cell // 2 % 2, cell % 2
        for sub in range(16):
            line = (4 * a + sub // 4) * EDGE + 4 * b + sub % 4
            volumes_ref[c, line * 8 : line * 8 + 8, :] = lifted[
                cell * 8 : cell * 8 + 8, sub * 128 : sub * 128 + 128
            ]
    links_copy.wait()
    for brick in range(BRICKS):

        def near(face):
            link = links_ref[0, brick, face]
            index = jnp.clip(link - BRICKS * (position - 1), 0, 3 * BRICKS - 1)
            return index, jnp.where(link >= 0, 1.0, 0.0).astype(F32)

        def x_face(face):
            index, present = near(face)
            line = EDGE * (EDGE - 1) if face % 2 == 0 else 0
            return [half * present for half in pair(volumes_ref, line * 8 + index, EDGE, 8)]

        def y_face(face):
            index, present = near(face)
            line = EDGE - 1 if face % 2 == 0 else 0
            return [half * present for half in pair(volumes_ref, line * 8 + index, EDGE, 8 * EDGE)]

        def z_face(face):
            index, present = near(face)
            tile = volumes_ref[1 if face % 2 == 0 else 0, pl.ds(index, CUBE, stride=8), :] * present
            return tile.reshape(EDGE, EDGE, HALF)

        own = [half.reshape(EDGE, EDGE, HALF) for half in pair(volumes_ref, BRICKS + brick, CUBE, 8)]
        put_padded(pad_out, brick, own, x_face(0), x_face(1), y_face(2), y_face(3), z_face(4), z_face(5))
    pre = convolve(pad_out, band_ref)
    sigmoid = 1.0 / (1.0 + jnp.exp(-pre))
    hidden = (pre / (1.0 + jnp.exp(-pre))).astype(BF16)
    slope_out[...] = sigmoid * (1.0 + pre * (1.0 - sigmoid))
    hidden_out[...] = hidden
    hidden = hidden.astype(F32)
    turned_out[...] = jnp.transpose(hidden).astype(BF16)
    build_band(back_out, flipped_rows(weights_ref[...].astype(F32)))


def hidden_faces_kernel(hidden_ref, _parts, high_out, low_out, far_out, near_out, halves_ref, faces_ref):
    pack_all(half_lines(hidden_ref[...].astype(F32)), halves_ref, faces_ref, high_out, low_out)
    to_partners(high_out, low_out, far_out, near_out)


def fold(outer, places):
    lane = lanes_of((CHANNELS, 128)) // CHANNELS
    folded = None
    for block in range(4):
        start, tile = places[block]
        rows = outer[start : start + CHANNELS, tile * 128 : tile * 128 + 128]
        folded = rows if folded is None else jnp.where(lane == block, rows, folded)
    quarter = [folded[8 * q : 8 * q + 8] for q in range(4)]
    small = lanes_of((8, 128)) // CHANNELS
    total = None
    for turn in range(4):
        mixed = quarter[0]
        for q in range(1, 4):
            mixed = jnp.where(small == (q + turn) % 4, quarter[q], mixed)
        if turn:
            mixed = pltpu.roll(mixed, 128 - turn * CHANNELS, 1)
        total = mixed if total is None else total + mixed
    return total


def diagonal(shift):
    places = [None] * 4
    for z in range(4):
        other = z + shift
        places[other % 4] = (z * CHANNELS, 0 if 0 <= other < 4 else 1)
    return places


def put_masks(masks_ref, links_ref):
    position = lax.axis_index("space")
    for brick in range(BRICKS):
        for face in range(6):
            first = links_ref[0, brick, face] - BRICKS * (position - 1 if face % 2 == 0 else position)
            for i in range(2 * BRICKS):
                row = (brick * 6 + face) * 2 * BRICKS + i
                masks_ref[row : row + 1, :] = jnp.full((1, 128), jnp.where(first == i, 1.0, 0.0).astype(F32))


def pad_all(pad_ref, bricks, masks_ref, high_pool, low_pool, high_own, low_own, far, near):
    position = lax.axis_index("space")
    half = BRICKS * FACE
    even = position % 2 == 0
    high_pool[0:half] = jnp.where(even, far[...], near[...]).astype(F32)
    high_pool[half:] = high_own[...].astype(F32)
    low_pool[0:half] = low_own[...].astype(F32)
    low_pool[half:] = jnp.where(even, near[...], far[...]).astype(F32)
    for brick, lines in enumerate(bricks):

        def face(number, axis):
            pool = high_pool if number % 2 == 0 else low_pool
            total = [0.0, 0.0]
            for i in range(2 * BRICKS):
                row = (brick * 6 + number) * 2 * BRICKS + i
                mask = masks_ref[row : row + 1, :]
                start = i * FACE + axis * EDGE
                for part in range(2):
                    found = pool[start : start + EDGE, part * HALF : part * HALF + HALF]
                    total[part] = total[part] + found * mask
            return total

        put_padded(
            pad_ref, brick, lines, face(0, 0), face(1, 0), face(2, 1), face(3, 1),
            unpack_depth(face(4, 2), True), unpack_depth(face(5, 2), False),
        )


def second_kernel(
    masks_ref, cotangent_ref, band_ref, slope_ref, hidden_ref, lifted_pad, high_own, low_own, far, near,
    sums_out, lifted_out,
    high_pool, low_pool, cotangent_pad, sums_ref,
):
    lifted_out[...] = window(lifted_pad, 4)[:, :HALF]
    bricks = cotangent_lines(cotangent_ref)
    pad_all(cotangent_pad, bricks, masks_ref, high_pool, low_pool, high_own, low_own, far, near)
    gradient = (convolve(cotangent_pad, band_ref) * slope_ref[...]).astype(BF16)
    gradient = jnp.transpose(gradient.astype(F32)).astype(BF16)
    hidden = hidden_ref[...]
    sums_ref[8 * BLOCKS :] = jnp.zeros((sums_ref.shape[0] - 8 * BLOCKS, 128), F32)
    for k in range(9):
        one = dot(gradient, window(lifted_pad, k))
        two = dot(hidden, window(cotangent_pad, 8 - k))
        for part in range(3):
            start = 8 * (3 * k + part)
            sums_ref[start : start + 8] = fold(one, diagonal(part - 1))
            start += 8 * 27
            sums_ref[start : start + 8] = fold(two, diagonal(1 - part))
    sums_out[...] = sums_ref[...].astype(BF16)


def fine_kernel(
    masks_ref, band_ref, lifted_ref, hidden_ref, high_own, low_own, far, near,
    fine_out, high_pool, low_pool, hidden_pad,
):
    bricks = half_lines(hidden_ref[...].astype(F32))
    pad_all(hidden_pad, bricks, masks_ref, high_pool, low_pool, high_own, low_own, far, near)
    fine = lifted_ref[...].astype(F32) + convolve(hidden_pad, band_ref)
    fine = fine.reshape(LINES // EDGE, 2, EDGE, HALF)
    fine = jnp.concatenate([fine[:, 0], fine[:, 1]], axis=-1)
    fine_out[...] = fine.astype(BF16).reshape(fine_out.shape)


def sum_kernel(devices, scale, parts_ref, out_ref, rows_ref):
    rows_ref[...] = parts_ref[...].astype(F32)
    share = rows_ref.shape[0] // devices
    pieces = [rows_ref[share * i : share * i + share] for i in range(devices)]
    while len(pieces) > 1:
        pairs = [a + b for a, b in zip(pieces[::2], pieces[1::2])]
        pieces = pairs + pieces[len(pieces) - len(pieces) % 2 :]
    total = pieces[0] * scale
    for i in range(devices):
        rows_ref[share * i : share * i + share] = total
    out_ref[...] = rows_ref[...].astype(BF16)


def unpacked(tile):
    pieces = [tile] + [pltpu.roll(tile, 128 - q * CHANNELS, 1) for q in range(1, 4)]
    return jnp.concatenate(pieces, axis=0)[:, :CHANNELS]


def turned(tiles):
    lane = lanes_of((8, 128)) // CHANNELS
    rows = []
    for q in range(4):
        mixed = jnp.zeros((8, 128), F32)
        for n, tile in enumerate(tiles):
            shift = (n - q) % 4 * CHANNELS
            mixed = jnp.where(lane == n, pltpu.roll(tile, shift, 1) if shift else tile, mixed)
        rows.append(mixed)
    return jnp.transpose(jnp.concatenate(rows, axis=0))


def unpack_kernel(sums_ref, fine_ref, one_out, two_out, fine_out, rows_ref, one_ref, two_ref, sems, fine_sem):
    fine_copy = pltpu.make_async_copy(fine_ref, fine_out, fine_sem)
    fine_copy.start()
    rows_ref[...] = sums_ref[...].astype(F32)
    tiles = [rows_ref[8 * index : 8 * index + 8] for index in range(BLOCKS)]
    copies = []
    for which, (block_ref, out) in ((1, (two_ref, two_out)), (0, (one_ref, one_out))):
        for part, (first, last) in enumerate(((0, 8), (8, 16), (16, 27))):
            for index in range(first, last):
                if which:
                    block_ref[index] = unpacked(tiles[27 + index])
                elif index % 4 == 0:
                    blocks = turned(tiles[index : min(index + 4, 27)])
                    for n in range(min(4, 27 - index)):
                        block_ref[index + n] = blocks[CHANNELS * n : CHANNELS * n + CHANNELS]
            span = pl.ds(first, last - first)
            copies.append(pltpu.make_async_copy(block_ref.at[span], out.at[span], sems.at[which, part]))
            copies[-1].start()
    for copy in copies:
        copy.wait()
    fine_copy.wait()


def call(kernel, out_shape, scratch=(), hbm=(), inputs=1, limit=24, cost=None, out=pltpu.VMEM):
    spaces = [pl.ANY if i in hbm else pltpu.VMEM for i in range(inputs)]
    return pl.pallas_call(
        kernel,
        out_shape=out_shape,
        in_specs=[pl.BlockSpec(memory_space=space) for space in spaces],
        out_specs=jax.tree.map(lambda _: pl.BlockSpec(memory_space=out), out_shape),
        scratch_shapes=list(scratch),
        compiler_params=pltpu.CompilerParams(vmem_limit_bytes=limit * 2**20),
        cost_estimate=cost,
    )


def shape(*dims, dtype=BF16):
    return jax.ShapeDtypeStruct(dims, dtype)


def swapped(value, first):
    pairs = [(i, i + 1) for i in range(first, lax.axis_size("space") - 1, 2)]
    return lax.ppermute(value, "space", pairs + [(target, source) for source, target in pairs])


def exchanged(rows):
    everyone = lax.axis_size("space") * lax.axis_size("dp")
    shares = rows.reshape(everyone, -1, 2, 128)
    shares = lax.all_to_all(shares, ("space", "dp"), split_axis=0, concat_axis=0, tiled=True)
    return shares.reshape(rows.shape)


def body(coarse_latents, active_blocks, face_links, cotangent, up_weight, conv_one, conv_two):
    devices = lax.axis_size("space")
    everyone = devices * lax.axis_size("dp")
    held, width = coarse_latents.shape[1:]
    bricks = active_blocks.shape[1]
    tiles = width // 128
    scenes = 2 if lax.axis_size("dp") == 2 else 1
    packed = call(
        functools.partial(pick_kernel, scenes),
        shape(devices * scenes, 3 * BRICKS * tiles, 128),
        [
            pltpu.VMEM((1, bricks), jnp.int32),
            pltpu.VMEM((1, held, width), BF16),
            pltpu.VMEM(((bricks + 16) * tiles, 128), F32),
            pltpu.SemaphoreType.DMA((2,)),
        ],
        hbm=(0, 1),
        inputs=2,
        limit=60,
    )(active_blocks, coarse_latents)
    axes = ("space", "dp")
    received = lax.all_to_all(packed, axes if scenes == 2 else "space", split_axis=0, concat_axis=0, tiled=True)
    cost = pl.CostEstimate(flops=10**9, bytes_accessed=2 * 10**6, transcendentals=0)
    face = shape(BRICKS * FACE, LINE)
    halves = pltpu.VMEM((2, LINES, HALF), F32)
    faces = pltpu.VMEM((BRICKS * FACE, LINE), F32)
    pool = pltpu.VMEM((2 * BRICKS * FACE, LINE), F32)
    volume = shape(ROWS, HALF)
    links = [pltpu.SMEM(face_links.shape, jnp.int32), pltpu.SemaphoreType.DMA]
    pad_shape = (3, BRICKS, EDGE + 2, 2 * EDGE, WIDE)
    pad = pltpu.VMEM(pad_shape, BF16)
    high, low, far, near = call(faces_kernel, (face,) * 4, [halves, faces])(cotangent)
    far = swapped(far, 1)
    near = swapped(near, 0)
    masks = shape(BRICKS * 6 * 2 * BRICKS, 128, dtype=F32)
    band_one, masks = call(masks_kernel, (shape(*BAND), masks), links, hbm=(0,), inputs=2, cost=cost)(
        face_links, conv_one
    )
    slope, hidden, turned, lifted_pad, band_back = call(
        first_kernel,
        (
            shape(ROWS, HALF, dtype=F32), volume, shape(HALF, ROWS), shape(*pad_shape), shape(*BAND),
        ),
        [pltpu.VMEM((2, 8 * CUBE, 128), F32), pltpu.VMEM((8 * tiles, 128), F32), *links],
        hbm=(0,),
        inputs=5,
    )(face_links, received, up_weight, band_one, conv_two)
    share = 2 * -(-4 * BLOCKS // everyone)
    packed_rows = (everyone * share, 128)
    sums, lifted = call(
        second_kernel,
        (shape(*packed_rows), volume),
        [pool, pool, pad, pltpu.VMEM(packed_rows, F32)],
        inputs=10,
    )(masks, cotangent, band_back, slope, turned, lifted_pad, high, low, far, near)
    parts = exchanged(sums)
    hidden_high, hidden_low, hidden_far, hidden_near = call(
        hidden_faces_kernel, (face,) * 4, [halves, faces], hbm=(1,), inputs=2
    )(hidden, parts)
    hidden_far = swapped(hidden_far, 1)
    hidden_near = swapped(hidden_near, 0)
    band_two = call(band_kernel, shape(*BAND), cost=cost)(conv_two)
    fine = call(fine_kernel, shape(*cotangent.shape), [pool, pool, pad], inputs=8, cost=cost)(
        masks, band_two, lifted, hidden, hidden_high, hidden_low, hidden_far, hidden_near
    )
    scale = 1.0 / math.sqrt(lax.axis_size("dp") * devices * BRICKS * EDGE**3)
    total = call(
        functools.partial(sum_kernel, everyone, scale), shape(*packed_rows), [pltpu.VMEM(packed_rows, F32)]
    )(parts)
    gathered = exchanged(total)
    grads = shape(27, CHANNELS, CHANNELS, dtype=F32)
    block = pltpu.VMEM(grads.shape, F32)
    scratch = [pltpu.VMEM(packed_rows, F32), block, block]
    scratch += [pltpu.SemaphoreType.DMA((2, 3)), pltpu.SemaphoreType.DMA]
    grad_one, grad_two, fine = call(
        unpack_kernel, (grads, grads, shape(*fine.shape)), scratch, inputs=2, out=pl.ANY
    )(gathered, fine)
    return (fine, grad_one, grad_two)


def solution(mesh):
    return jax.shard_map(
        body,
        mesh=mesh,
        in_specs=(
            P("dp", "space", None),
            P("dp", None),
            P("dp", "space", None),
            P("dp", "space", None, None, None),
            P(),
            P(),
            P(),
        ),
        out_specs=(P("dp", "space", None, None, None), P(), P()),
        check_vma=False,
    )
```

```python
import functools
import math

import jax
import jax.numpy as jnp
from jax import lax
from jax.experimental import pallas as pl
from jax.experimental.pallas import tpu as pltpu
from jax.sharding import PartitionSpec as P

BF16 = jnp.bfloat16
F32 = jnp.float32
EDGE = 8
CHANNELS = 32
LINE = EDGE * CHANNELS
HALF = LINE // 2
WIDE = 2 * HALF
BRICKS = 2
CUBE = EDGE * EDGE
LINES = BRICKS * CUBE
BAND = (9, WIDE, HALF)
ROWS = 2 * LINES
FACE = 3 * EDGE
BLOCKS = 54


def dot(left, right):
    return jnp.dot(left, right, preferred_element_type=F32)


def dot_rows(left, right):
    return lax.dot_general(left, right, (((0,), (0,)), ((), ())), preferred_element_type=F32)


def pair(halves_ref, start, count, stride=1):
    index = pl.ds(start, count, stride=stride) if stride > 1 else pl.ds(start, count)
    return halves_ref[0, index, :], halves_ref[1, index, :]


def lanes_of(shape):
    return lax.broadcasted_iota(jnp.int32, shape, len(shape) - 1)


def scene_of(blocks_ref):
    return lax.axis_index("dp") if blocks_ref.shape[1] > 1 else 0


def pick_kernel(ids_hbm, latents_hbm, out_hbm, ids_ref, latents_ref, rows_ref, blocks_ref, zeros_ref, sems):
    ids_copy = pltpu.make_async_copy(ids_hbm, ids_ref, sems.at[0])
    ids_copy.start()
    held, width = latents_ref.shape[1:]
    copies = []
    for i in range(4):
        part = pl.ds(i * held // 4, held // 4)
        copies.append(pltpu.make_async_copy(latents_hbm.at[0, part], latents_ref.at[0, part], sems.at[1 + i]))
        copies[-1].start()
    scene = scene_of(out_hbm)
    others = None
    if out_hbm.shape[1] > 1:
        zeros_ref[...] = jnp.zeros(zeros_ref.shape, BF16)
        others = pltpu.make_async_copy(zeros_ref, out_hbm.at[:, 1 - scene], sems.at[5])
        others.start()
    bricks = ids_ref.shape[1]
    margin = 8 * width // 128
    tiles = width // 128
    rows_ref[0:margin] = jnp.zeros((margin, 128), F32)
    rows_ref[margin + bricks * tiles :] = jnp.zeros((margin, 128), F32)
    first = lax.axis_index("space") * held
    rows = lax.broadcasted_iota(jnp.int32, (held, bricks), 0) + first
    ids_copy.wait()
    hot = jnp.where(rows == ids_ref[...], 1.0, 0.0).astype(BF16)
    for copy in copies:
        copy.wait()
    picked = dot_rows(hot, latents_ref[0])
    for tile in range(tiles):
        rows_ref[pl.ds(margin + tile, bricks, stride=tiles), :] = picked[:, tile * 128 : tile * 128 + 128]
    count = blocks_ref.shape[1]
    for receiver in range(blocks_ref.shape[0]):
        start = margin + BRICKS * (receiver - 1) * tiles
        blocks_ref[receiver] = rows_ref[start : start + count].astype(BF16)
    found = pltpu.make_async_copy(blocks_ref, out_hbm.at[:, scene], sems.at[6])
    found.start()
    found.wait()
    if others is not None:
        others.wait()


def build_band(band_ref, rows):
    shape = (3 * CHANNELS, HALF)
    row = lax.broadcasted_iota(jnp.int32, shape, 0)
    target = CHANNELS - (row // CHANNELS) * CHANNELS + row % CHANNELS
    distance = lanes_of(shape) - target
    band_ref[:, HALF:, :] = jnp.zeros((9, HALF, HALF), BF16)
    for z in range(-1, 5):
        select = jnp.where(distance == z * CHANNELS, 1.0, 0.0).astype(BF16)
        block = dot(rows, select).astype(BF16)
        start = z % 8 * CHANNELS
        band_ref[:, start : start + CHANNELS, :] = block.reshape(9, CHANNELS, HALF)


def weight_rows(weights):
    cube = weights.reshape(9, 3, CHANNELS, CHANNELS)
    rows = jnp.concatenate([cube[:, 0], cube[:, 1], cube[:, 2]], axis=-1)
    return rows.reshape(9 * CHANNELS, 3 * CHANNELS).astype(BF16)


def flipped_rows(weights):
    cube = jnp.swapaxes(weights, 1, 2).reshape(9, 3, CHANNELS, CHANNELS)
    pieces = [jnp.concatenate([cube[8 - k, 2], cube[8 - k, 1], cube[8 - k, 0]], axis=-1) for k in range(9)]
    return jnp.concatenate(pieces, axis=0).astype(BF16)


def band_kernel(weights_ref, band_ref):
    build_band(band_ref, weight_rows(weights_ref[...].astype(F32)))


def masks_kernel(links_in, one_ref, two_ref, band_ref, back_ref, masks_ref, links_ref, links_sem):
    links_copy = pltpu.make_async_copy(links_in, links_ref, links_sem)
    links_copy.start()
    build_band(band_ref, weight_rows(one_ref[...].astype(F32)))
    build_band(back_ref, flipped_rows(two_ref[...].astype(F32)))
    links_copy.wait()
    put_masks(masks_ref, links_ref)


def put_padded(pad_ref, brick, lines, x_low, x_high, y_low, y_high, z_low, z_high):
    def joined(halves, before, after):
        lane = lanes_of(halves[0].shape)
        first = jnp.where(lane < CHANNELS, halves[1], before)
        second = jnp.where(lane >= HALF - CHANNELS, halves[0], after)
        return jnp.concatenate([halves[0], first], axis=-1), jnp.concatenate([halves[1], second], axis=-1)

    inside = joined(lines, z_low, z_high)
    x_low, x_high, y_low, y_high = [joined(face, 0.0, 0.0) for face in (x_low, x_high, y_low, y_high)]
    none = jnp.zeros((1, WIDE), F32)
    shifted = [[], [], []]
    for half in range(2):
        slabs = jnp.concatenate([x_low[half][None], inside[half], x_high[half][None]], axis=0)
        row = lax.broadcasted_iota(jnp.int32, slabs.shape, 1)
        low = jnp.concatenate([none, y_low[half], none], axis=0)[:, None, :]
        high = jnp.concatenate([none, y_high[half], none], axis=0)[:, None, :]
        shifted[0].append(jnp.where(row == 0, low, pltpu.roll(slabs, 1, 1)))
        shifted[1].append(slabs)
        shifted[2].append(jnp.where(row == EDGE - 1, high, pltpu.roll(slabs, EDGE - 1, 1)))
    for dy in range(3):
        pad_ref[dy, brick] = jnp.concatenate(shifted[dy], axis=1).astype(BF16)


def window(pad_ref, k):
    return pad_ref[k % 3, :, k // 3 : k // 3 + EDGE].reshape(ROWS, WIDE)


def convolve(pad_ref, band_ref):
    both, last = None, None
    for dy in range(3):
        slabs = pad_ref[dy, :, : EDGE + 1].reshape(-1, WIDE)
        term = dot(slabs, jnp.concatenate([band_ref[dy], band_ref[3 + dy]], axis=1))
        both = term if both is None else both + term
        term = dot(window(pad_ref, 6 + dy), band_ref[6 + dy])
        last = term if last is None else last + term
    both = both.reshape(BRICKS, EDGE + 1, 2 * EDGE, 2 * HALF)
    total = both[:, :EDGE, :, :HALF] + both[:, 1:, :, HALF:]
    return total.reshape(ROWS, HALF) + last


def half_lines(values):
    cube = values.reshape(BRICKS, EDGE, 2, EDGE, HALF)
    return [(cube[brick, :, 0], cube[brick, :, 1]) for brick in range(BRICKS)]


def put_halves(halves_ref, start, bricks):
    for brick, lines in enumerate(bricks):
        for half in range(2):
            first = start + brick * CUBE
            halves_ref[half, first : first + CUBE, :] = lines[half].reshape(CUBE, HALF)


def cotangent_lines(cotangent_ref):
    cube = cotangent_ref[...].astype(F32).reshape(BRICKS, EDGE, EDGE, LINE)
    return [(cube[brick, :, :, :HALF], cube[brick, :, :, HALF:]) for brick in range(BRICKS)]


def pack_faces(faces_ref, base, halves_ref, start, high):
    x_face = pair(halves_ref, start + ((EDGE - 1) * EDGE if high else 0), EDGE)
    y_face = pair(halves_ref, start + (EDGE - 1 if high else 0), EDGE, EDGE)
    for half in range(2):
        lanes = slice(half * HALF, half * HALF + HALF)
        faces_ref[base : base + EDGE, lanes] = x_face[half]
        faces_ref[base + EDGE : base + 2 * EDGE, lanes] = y_face[half]
    tile = halves_ref[1 if high else 0, start : start + CUBE, :]
    lane = lanes_of((16, 128)) // CHANNELS
    packed = jnp.zeros((16, 128), F32)
    for part in range(4):
        shift = (part + 1 if high else part) % 4 * CHANNELS
        piece = tile[part * 16 : part * 16 + 16]
        packed = jnp.where(lane == part, pltpu.roll(piece, shift, 1) if shift else piece, packed)
    faces_ref[base + 2 * EDGE : base + FACE, :128] = packed[:8]
    faces_ref[base + 2 * EDGE : base + FACE, 128:] = packed[8:]


def pack_all(bricks, halves_ref, faces_ref, high_out, low_out):
    put_halves(halves_ref, 0, bricks)
    for high, out_ref in ((True, high_out), (False, low_out)):
        for brick in range(BRICKS):
            pack_faces(faces_ref, brick * FACE, halves_ref, brick * CUBE, high)
        out_ref[...] = faces_ref[...].astype(BF16)


def to_partners(high_ref, low_ref, far_out, near_out):
    even = lax.axis_index("space") % 2 == 0
    far_out[...] = jnp.where(even, low_ref[...], high_ref[...])
    near_out[...] = jnp.where(even, high_ref[...], low_ref[...])


def faces_kernel(cotangent_ref, high_out, low_out, far_out, near_out, halves_ref, faces_ref):
    pack_all(cotangent_lines(cotangent_ref), halves_ref, faces_ref, high_out, low_out)
    to_partners(high_out, low_out, far_out, near_out)


def unpack_depth(halves, high):
    packed = jnp.concatenate(halves, axis=0)
    pieces = []
    for part in range(4):
        shift = ((3 - part) if high else (4 - part)) % 4 * CHANNELS
        pieces.append(pltpu.roll(packed, shift, 1) if shift else packed)
    return jnp.concatenate(pieces, axis=0).reshape(EDGE, EDGE, 128)


def first_kernel(
    links_in, received_ref, up_ref, band_ref,
    slope_out, hidden_out, turned_out, pad_out,
    volumes_ref, rows_ref, links_ref, links_sem,
):
    links_copy = pltpu.make_async_copy(links_in, links_ref, links_sem)
    links_copy.start()
    position = lax.axis_index("space")
    tiles = received_ref.shape[2] // (3 * BRICKS)
    received = received_ref[:, pl.ds(scene_of(received_ref), 1)]
    rows_ref[0 : 3 * BRICKS * tiles] = jnp.sum(received.astype(F32), axis=(0, 1))
    rows_ref[3 * BRICKS * tiles :] = jnp.zeros((2 * tiles, 128), F32)
    cells = []
    for tile in range(tiles):
        rows = rows_ref[pl.ds(tile, 8, stride=tiles), :]
        cells += [rows[:, :64], rows[:, 64:]]
    lifted = dot(jnp.concatenate(cells, axis=0).astype(BF16), up_ref[...])
    lifted = lifted.astype(BF16).astype(F32)
    for cell in range(8):
        a, b, c = cell // 4, cell // 2 % 2, cell % 2
        for sub in range(16):
            line = (4 * a + sub // 4) * EDGE + 4 * b + sub % 4
            volumes_ref[c, line * 8 : line * 8 + 8, :] = lifted[
                cell * 8 : cell * 8 + 8, sub * 128 : sub * 128 + 128
            ]
    links_copy.wait()
    for brick in range(BRICKS):

        def near(face):
            link = links_ref[0, brick, face]
            index = jnp.clip(link - BRICKS * (position - 1), 0, 3 * BRICKS - 1)
            return index, jnp.where(link >= 0, 1.0, 0.0).astype(F32)

        def x_face(face):
            index, present = near(face)
            line = EDGE * (EDGE - 1) if face % 2 == 0 else 0
            return [half * present for half in pair(volumes_ref, line * 8 + index, EDGE, 8)]

        def y_face(face):
            index, present = near(face)
            line = EDGE - 1 if face % 2 == 0 else 0
            return [half * present for half in pair(volumes_ref, line * 8 + index, EDGE, 8 * EDGE)]

        def z_face(face):
            index, present = near(face)
            tile = volumes_ref[1 if face % 2 == 0 else 0, pl.ds(index, CUBE, stride=8), :] * present
            return tile.reshape(EDGE, EDGE, HALF)

        own = [half.reshape(EDGE, EDGE, HALF) for half in pair(volumes_ref, BRICKS + brick, CUBE, 8)]
        put_padded(pad_out, brick, own, x_face(0), x_face(1), y_face(2), y_face(3), z_face(4), z_face(5))
    pre = convolve(pad_out, band_ref)
    sigmoid = 1.0 / (1.0 + jnp.exp(-pre))
    hidden = (pre / (1.0 + jnp.exp(-pre))).astype(BF16)
    slope_out[...] = sigmoid * (1.0 + pre * (1.0 - sigmoid))
    hidden_out[...] = hidden
    hidden = hidden.astype(F32)
    turned_out[...] = jnp.transpose(hidden).astype(BF16)


def hidden_faces_kernel(hidden_ref, _parts, high_out, low_out, far_out, near_out, halves_ref, faces_ref):
    pack_all(half_lines(hidden_ref[...].astype(F32)), halves_ref, faces_ref, high_out, low_out)
    to_partners(high_out, low_out, far_out, near_out)


def fold(outer, places):
    lane = lanes_of((CHANNELS, 128)) // CHANNELS
    folded = None
    for block in range(4):
        start, tile = places[block]
        rows = outer[start : start + CHANNELS, tile * 128 : tile * 128 + 128]
        folded = rows if folded is None else jnp.where(lane == block, rows, folded)
    quarter = [folded[8 * q : 8 * q + 8] for q in range(4)]
    small = lanes_of((8, 128)) // CHANNELS
    total = None
    for turn in range(4):
        mixed = quarter[0]
        for q in range(1, 4):
            mixed = jnp.where(small == (q + turn) % 4, quarter[q], mixed)
        if turn:
            mixed = pltpu.roll(mixed, 128 - turn * CHANNELS, 1)
        total = mixed if total is None else total + mixed
    return total


def diagonal(shift):
    places = [None] * 4
    for z in range(4):
        other = z + shift
        places[other % 4] = (z * CHANNELS, 0 if 0 <= other < 4 else 1)
    return places


def put_masks(masks_ref, links_ref):
    position = lax.axis_index("space")
    for brick in range(BRICKS):
        for face in range(6):
            first = links_ref[0, brick, face] - BRICKS * (position - 1 if face % 2 == 0 else position)
            for i in range(2 * BRICKS):
                row = (brick * 6 + face) * 2 * BRICKS + i
                masks_ref[row : row + 1, :] = jnp.full((1, 128), jnp.where(first == i, 1.0, 0.0).astype(F32))


def pad_all(pad_ref, bricks, masks_ref, high_pool, low_pool, high_own, low_own, far, near):
    position = lax.axis_index("space")
    half = BRICKS * FACE
    even = position % 2 == 0
    high_pool[0:half] = jnp.where(even, far[...], near[...]).astype(F32)
    high_pool[half:] = high_own[...].astype(F32)
    low_pool[0:half] = low_own[...].astype(F32)
    low_pool[half:] = jnp.where(even, near[...], far[...]).astype(F32)
    for brick, lines in enumerate(bricks):

        def face(number, axis):
            pool = high_pool if number % 2 == 0 else low_pool
            total = [0.0, 0.0]
            for i in range(2 * BRICKS):
                row = (brick * 6 + number) * 2 * BRICKS + i
                mask = masks_ref[row : row + 1, :]
                start = i * FACE + axis * EDGE
                for part in range(2):
                    found = pool[start : start + EDGE, part * HALF : part * HALF + HALF]
                    total[part] = total[part] + found * mask
            return total

        put_padded(
            pad_ref, brick, lines, face(0, 0), face(1, 0), face(2, 1), face(3, 1),
            unpack_depth(face(4, 2), True), unpack_depth(face(5, 2), False),
        )


def second_kernel(
    masks_ref, cotangent_ref, band_ref, slope_ref, hidden_ref, lifted_pad, high_own, low_own, far, near,
    sums_out, lifted_out,
    high_pool, low_pool, cotangent_pad, sums_ref,
):
    lifted_out[...] = window(lifted_pad, 4)[:, :HALF]
    bricks = cotangent_lines(cotangent_ref)
    pad_all(cotangent_pad, bricks, masks_ref, high_pool, low_pool, high_own, low_own, far, near)
    gradient = (convolve(cotangent_pad, band_ref) * slope_ref[...]).astype(BF16)
    gradient = jnp.transpose(gradient.astype(F32)).astype(BF16)
    hidden = hidden_ref[...]
    sums_ref[8 * BLOCKS :] = jnp.zeros((sums_ref.shape[0] - 8 * BLOCKS, 128), F32)
    for k in range(9):
        one = dot(gradient, window(lifted_pad, k))
        two = dot(hidden, window(cotangent_pad, 8 - k))
        for part in range(3):
            start = 8 * (3 * k + part)
            sums_ref[start : start + 8] = fold(one, diagonal(part - 1))
            start += 8 * 27
            sums_ref[start : start + 8] = fold(two, diagonal(1 - part))
    sums_out[...] = sums_ref[...].astype(BF16)


def fine_kernel(
    masks_ref, band_ref, lifted_ref, hidden_ref, high_own, low_own, far, near,
    fine_out, high_pool, low_pool, hidden_pad,
):
    bricks = half_lines(hidden_ref[...].astype(F32))
    pad_all(hidden_pad, bricks, masks_ref, high_pool, low_pool, high_own, low_own, far, near)
    fine = lifted_ref[...].astype(F32) + convolve(hidden_pad, band_ref)
    fine = fine.reshape(LINES // EDGE, 2, EDGE, HALF)
    fine = jnp.concatenate([fine[:, 0], fine[:, 1]], axis=-1)
    fine_out[...] = fine.astype(BF16).reshape(fine_out.shape)


def sum_kernel(devices, scale, parts_ref, out_hbm, rows_ref, shares_ref, sems):
    rows_ref[...] = parts_ref[...].astype(F32)
    share = rows_ref.shape[0] // devices
    pieces = [rows_ref[share * i : share * i + share] for i in range(devices)]
    while len(pieces) > 1:
        pairs = [a + b for a, b in zip(pieces[::2], pieces[1::2])]
        pieces = pairs + pieces[len(pieces) - len(pieces) % 2 :]
    total = pieces[0] * scale
    some = shares_ref.shape[0]
    for i in range(some // share):
        rows_ref[share * i : share * i + share] = total
    shares_ref[...] = rows_ref[0:some].astype(BF16)
    copies = []
    for i in range(out_hbm.shape[0] // some):
        copies.append(pltpu.make_async_copy(shares_ref, out_hbm.at[pl.ds(some * i, some)], sems.at[i]))
        copies[-1].start()
    for copy in copies:
        copy.wait()


def unpacked(tile):
    pieces = [tile] + [pltpu.roll(tile, 128 - q * CHANNELS, 1) for q in range(1, 4)]
    return jnp.concatenate(pieces, axis=0)[:, :CHANNELS]


def turned(tiles):
    lane = lanes_of((8, 128)) // CHANNELS
    rows = []
    for q in range(4):
        mixed = jnp.zeros((8, 128), F32)
        for n, tile in enumerate(tiles):
            shift = (n - q) % 4 * CHANNELS
            mixed = jnp.where(lane == n, pltpu.roll(tile, shift, 1) if shift else tile, mixed)
        rows.append(mixed)
    return jnp.transpose(jnp.concatenate(rows, axis=0))


def unpack_kernel(sums_ref, fine_ref, one_out, two_out, fine_out, rows_ref, one_ref, two_ref, sems, fine_sem):
    fine_copy = pltpu.make_async_copy(fine_ref, fine_out, fine_sem)
    fine_copy.start()
    rows_ref[...] = sums_ref[...].astype(F32)
    tiles = [rows_ref[8 * index : 8 * index + 8] for index in range(BLOCKS)]
    copies = []
    for which, (block_ref, out) in ((1, (two_ref, two_out)), (0, (one_ref, one_out))):
        for part, (first, last) in enumerate(((0, 8), (8, 16), (16, 27))):
            for index in range(first, last):
                if which:
                    block_ref[index] = unpacked(tiles[27 + index])
                elif index % 4 == 0:
                    blocks = turned(tiles[index : min(index + 4, 27)])
                    for n in range(min(4, 27 - index)):
                        block_ref[index + n] = blocks[CHANNELS * n : CHANNELS * n + CHANNELS]
            span = pl.ds(first, last - first)
            copies.append(pltpu.make_async_copy(block_ref.at[span], out.at[span], sems.at[which, part]))
            copies[-1].start()
    for copy in copies:
        copy.wait()
    fine_copy.wait()


def call(kernel, out_shape, scratch=(), hbm=(), inputs=1, limit=24, cost=None, out=pltpu.VMEM):
    spaces = [pl.ANY if i in hbm else pltpu.VMEM for i in range(inputs)]
    return pl.pallas_call(
        kernel,
        out_shape=out_shape,
        in_specs=[pl.BlockSpec(memory_space=space) for space in spaces],
        out_specs=jax.tree.map(lambda _: pl.BlockSpec(memory_space=out), out_shape),
        scratch_shapes=list(scratch),
        compiler_params=pltpu.CompilerParams(vmem_limit_bytes=limit * 2**20),
        cost_estimate=cost,
    )


def shape(*dims, dtype=BF16):
    return jax.ShapeDtypeStruct(dims, dtype)


def swapped(value, first):
    pairs = [(i, i + 1) for i in range(first, lax.axis_size("space") - 1, 2)]
    return lax.ppermute(value, "space", pairs + [(target, source) for source, target in pairs])


def exchanged(rows):
    everyone = lax.axis_size("space") * lax.axis_size("dp")
    shares = rows.reshape(everyone, -1, 2, 128)
    shares = lax.all_to_all(shares, ("space", "dp"), split_axis=0, concat_axis=0, tiled=True)
    return shares.reshape(rows.shape)


def body(coarse_latents, active_blocks, face_links, cotangent, up_weight, conv_one, conv_two):
    devices = lax.axis_size("space")
    everyone = devices * lax.axis_size("dp")
    held, width = coarse_latents.shape[1:]
    bricks = active_blocks.shape[1]
    tiles = width // 128
    scenes = 2 if lax.axis_size("dp") == 2 else 1
    count = 3 * BRICKS * tiles
    blocks = pltpu.VMEM((devices, count, 128), BF16)
    packed = call(
        pick_kernel,
        shape(devices, scenes, count, 128),
        [
            pltpu.VMEM((1, bricks), jnp.int32),
            pltpu.VMEM((1, held, width), BF16),
            pltpu.VMEM(((bricks + 16) * tiles, 128), F32),
            blocks,
            blocks,
            pltpu.SemaphoreType.DMA((7,)),
        ],
        hbm=(0, 1),
        inputs=2,
        limit=60,
        out=pl.ANY,
    )(active_blocks, coarse_latents)
    received = lax.all_to_all(
        packed.reshape(devices * scenes, count, 128),
        ("space", "dp") if scenes == 2 else "space",
        split_axis=0,
        concat_axis=0,
        tiled=True,
    ).reshape(packed.shape)
    cost = pl.CostEstimate(flops=10**9, bytes_accessed=2 * 10**6, transcendentals=0)
    face = shape(BRICKS * FACE, LINE)
    halves = pltpu.VMEM((2, LINES, HALF), F32)
    faces = pltpu.VMEM((BRICKS * FACE, LINE), F32)
    pool = pltpu.VMEM((2 * BRICKS * FACE, LINE), F32)
    volume = shape(ROWS, HALF)
    links = [pltpu.SMEM(face_links.shape, jnp.int32), pltpu.SemaphoreType.DMA]
    pad_shape = (3, BRICKS, EDGE + 2, 2 * EDGE, WIDE)
    pad = pltpu.VMEM(pad_shape, BF16)
    high, low, far, near = call(faces_kernel, (face,) * 4, [halves, faces])(cotangent)
    far = swapped(far, 1)
    near = swapped(near, 0)
    masks = shape(BRICKS * 6 * 2 * BRICKS, 128, dtype=F32)
    band_one, band_back, masks = call(
        masks_kernel, (shape(*BAND), shape(*BAND), masks), links, hbm=(0,), inputs=3, cost=cost
    )(face_links, conv_one, conv_two)
    slope, hidden, turned, lifted_pad = call(
        first_kernel,
        (
            shape(ROWS, HALF, dtype=F32), volume, shape(HALF, ROWS), shape(*pad_shape),
        ),
        [pltpu.VMEM((2, 8 * CUBE, 128), F32), pltpu.VMEM((8 * tiles, 128), F32), *links],
        hbm=(0,),
        inputs=4,
    )(face_links, received, up_weight, band_one)
    share = 2 * -(-4 * BLOCKS // everyone)
    packed_rows = (everyone * share, 128)
    sums, lifted = call(
        second_kernel,
        (shape(*packed_rows), volume),
        [pool, pool, pad, pltpu.VMEM(packed_rows, F32)],
        inputs=10,
    )(masks, cotangent, band_back, slope, turned, lifted_pad, high, low, far, near)
    parts = exchanged(sums)
    hidden_high, hidden_low, hidden_far, hidden_near = call(
        hidden_faces_kernel, (face,) * 4, [halves, faces], hbm=(1,), inputs=2
    )(hidden, parts)
    hidden_far = swapped(hidden_far, 1)
    hidden_near = swapped(hidden_near, 0)
    band_two = call(band_kernel, shape(*BAND), cost=cost)(conv_two)
    fine = call(fine_kernel, shape(*cotangent.shape), [pool, pool, pad], inputs=8, cost=cost)(
        masks, band_two, lifted, hidden, hidden_high, hidden_low, hidden_far, hidden_near
    )
    scale = 1.0 / math.sqrt(lax.axis_size("dp") * devices * BRICKS * EDGE**3)
    times = 4 if everyone % 32 == 0 else 1
    total = call(
        functools.partial(sum_kernel, everyone, scale),
        shape(*packed_rows),
        [
            pltpu.VMEM(packed_rows, F32),
            pltpu.VMEM((packed_rows[0] // times, 128), BF16),
            pltpu.SemaphoreType.DMA((times,)),
        ],
        out=pl.ANY,
    )(parts)
    gathered = exchanged(total)
    grads = shape(27, CHANNELS, CHANNELS, dtype=F32)
    block = pltpu.VMEM(grads.shape, F32)
    scratch = [pltpu.VMEM(packed_rows, F32), block, block]
    scratch += [pltpu.SemaphoreType.DMA((2, 3)), pltpu.SemaphoreType.DMA]
    grad_one, grad_two, fine = call(
        unpack_kernel, (grads, grads, shape(*fine.shape)), scratch, inputs=2, out=pl.ANY
    )(gathered, fine)
    return (fine, grad_one, grad_two)


def solution(mesh):
    return jax.shard_map(
        body,
        mesh=mesh,
        in_specs=(
            P("dp", "space", None),
            P("dp", None),
            P("dp", "space", None),
            P("dp", "space", None, None, None),
            P(),
            P(),
            P(),
        ),
        out_specs=(P("dp", "space", None, None, None), P(), P()),
        check_vma=False,
    )
```

```python
import functools
import math

import jax
import jax.numpy as jnp
from jax import lax
from jax.experimental import pallas as pl
from jax.experimental.pallas import tpu as pltpu
from jax.sharding import PartitionSpec as P

BF16 = jnp.bfloat16
F32 = jnp.float32
EDGE = 8
CHANNELS = 32
LINE = EDGE * CHANNELS
HALF = LINE // 2
WIDE = 2 * HALF
BRICKS = 2
CUBE = EDGE * EDGE
LINES = BRICKS * CUBE
BAND = (9, WIDE, HALF)
ROWS = 2 * LINES
FACE = 3 * EDGE
BLOCKS = 54


def dot(left, right):
    return jnp.dot(left, right, preferred_element_type=F32)


def dot_rows(left, right):
    return lax.dot_general(left, right, (((0,), (0,)), ((), ())), preferred_element_type=F32)


def pair(halves_ref, start, count, stride=1):
    index = pl.ds(start, count, stride=stride) if stride > 1 else pl.ds(start, count)
    return halves_ref[0, index, :], halves_ref[1, index, :]


def lanes_of(shape):
    return lax.broadcasted_iota(jnp.int32, shape, len(shape) - 1)


def scene_of(blocks_ref):
    return lax.axis_index("dp") if blocks_ref.shape[1] > 1 else 0


def pick_kernel(ids_hbm, latents_hbm, out_hbm, ids_ref, latents_ref, rows_ref, blocks_ref, zeros_ref, sems):
    ids_copy = pltpu.make_async_copy(ids_hbm, ids_ref, sems.at[0])
    ids_copy.start()
    held, width = latents_ref.shape[1:]
    copies = []
    for i in range(4):
        part = pl.ds(i * held // 4, held // 4)
        copies.append(pltpu.make_async_copy(latents_hbm.at[0, part], latents_ref.at[0, part], sems.at[1 + i]))
        copies[-1].start()
    scene = scene_of(out_hbm)
    others = None
    if out_hbm.shape[1] > 1:
        zeros_ref[...] = jnp.zeros(zeros_ref.shape, BF16)
        others = pltpu.make_async_copy(zeros_ref, out_hbm.at[:, 1 - scene], sems.at[5])
        others.start()
    bricks = ids_ref.shape[1]
    margin = 8 * width // 128
    tiles = width // 128
    rows_ref[0:margin] = jnp.zeros((margin, 128), F32)
    rows_ref[margin + bricks * tiles :] = jnp.zeros((margin, 128), F32)
    first = lax.axis_index("space") * held
    rows = lax.broadcasted_iota(jnp.int32, (held, bricks), 0) + first
    ids_copy.wait()
    hot = jnp.where(rows == ids_ref[...], 1.0, 0.0).astype(BF16)
    for copy in copies:
        copy.wait()
    picked = dot_rows(hot, latents_ref[0])
    for tile in range(tiles):
        rows_ref[pl.ds(margin + tile, bricks, stride=tiles), :] = picked[:, tile * 128 : tile * 128 + 128]
    some, quarters, count = blocks_ref.shape[:3]
    for quarter in range(quarters):
        for place in range(some):
            start = margin + BRICKS * (quarter * some + place - 1) * tiles
            blocks_ref[place, quarter] = rows_ref[start : start + count].astype(BF16)
    found = pltpu.make_async_copy(blocks_ref, out_hbm.at[:, scene], sems.at[6])
    found.start()
    found.wait()
    if others is not None:
        others.wait()


def build_band(band_ref, rows):
    shape = (3 * CHANNELS, HALF)
    row = lax.broadcasted_iota(jnp.int32, shape, 0)
    target = CHANNELS - (row // CHANNELS) * CHANNELS + row % CHANNELS
    distance = lanes_of(shape) - target
    band_ref[:, HALF:, :] = jnp.zeros((9, HALF, HALF), BF16)
    for z in range(-1, 5):
        select = jnp.where(distance == z * CHANNELS, 1.0, 0.0).astype(BF16)
        block = dot(rows, select).astype(BF16)
        start = z % 8 * CHANNELS
        band_ref[:, start : start + CHANNELS, :] = block.reshape(9, CHANNELS, HALF)


def weight_rows(weights):
    cube = weights.reshape(9, 3, CHANNELS, CHANNELS)
    rows = jnp.concatenate([cube[:, 0], cube[:, 1], cube[:, 2]], axis=-1)
    return rows.reshape(9 * CHANNELS, 3 * CHANNELS).astype(BF16)


def flipped_rows(weights):
    cube = jnp.swapaxes(weights, 1, 2).reshape(9, 3, CHANNELS, CHANNELS)
    pieces = [jnp.concatenate([cube[8 - k, 2], cube[8 - k, 1], cube[8 - k, 0]], axis=-1) for k in range(9)]
    return jnp.concatenate(pieces, axis=0).astype(BF16)


def band_kernel(weights_ref, band_ref):
    build_band(band_ref, weight_rows(weights_ref[...].astype(F32)))


def masks_kernel(links_in, one_ref, two_ref, band_ref, back_ref, masks_ref, links_ref, links_sem):
    links_copy = pltpu.make_async_copy(links_in, links_ref, links_sem)
    links_copy.start()
    build_band(band_ref, weight_rows(one_ref[...].astype(F32)))
    build_band(back_ref, flipped_rows(two_ref[...].astype(F32)))
    links_copy.wait()
    put_masks(masks_ref, links_ref)


def put_padded(pad_ref, brick, lines, x_low, x_high, y_low, y_high, z_low, z_high):
    def joined(halves, before, after):
        lane = lanes_of(halves[0].shape)
        first = jnp.where(lane < CHANNELS, halves[1], before)
        second = jnp.where(lane >= HALF - CHANNELS, halves[0], after)
        return jnp.concatenate([halves[0], first], axis=-1), jnp.concatenate([halves[1], second], axis=-1)

    inside = joined(lines, z_low, z_high)
    x_low, x_high, y_low, y_high = [joined(face, 0.0, 0.0) for face in (x_low, x_high, y_low, y_high)]
    none = jnp.zeros((1, WIDE), F32)
    shifted = [[], [], []]
    for half in range(2):
        slabs = jnp.concatenate([x_low[half][None], inside[half], x_high[half][None]], axis=0)
        row = lax.broadcasted_iota(jnp.int32, slabs.shape, 1)
        low = jnp.concatenate([none, y_low[half], none], axis=0)[:, None, :]
        high = jnp.concatenate([none, y_high[half], none], axis=0)[:, None, :]
        shifted[0].append(jnp.where(row == 0, low, pltpu.roll(slabs, 1, 1)))
        shifted[1].append(slabs)
        shifted[2].append(jnp.where(row == EDGE - 1, high, pltpu.roll(slabs, EDGE - 1, 1)))
    for dy in range(3):
        pad_ref[dy, brick] = jnp.concatenate(shifted[dy], axis=1).astype(BF16)


def window(pad_ref, k):
    return pad_ref[k % 3, :, k // 3 : k // 3 + EDGE].reshape(ROWS, WIDE)


def convolve(pad_ref, band_ref):
    both, last = None, None
    for dy in range(3):
        slabs = pad_ref[dy, :, : EDGE + 1].reshape(-1, WIDE)
        term = dot(slabs, jnp.concatenate([band_ref[dy], band_ref[3 + dy]], axis=1))
        both = term if both is None else both + term
        term = dot(window(pad_ref, 6 + dy), band_ref[6 + dy])
        last = term if last is None else last + term
    both = both.reshape(BRICKS, EDGE + 1, 2 * EDGE, 2 * HALF)
    total = both[:, :EDGE, :, :HALF] + both[:, 1:, :, HALF:]
    return total.reshape(ROWS, HALF) + last


def half_lines(values):
    cube = values.reshape(BRICKS, EDGE, 2, EDGE, HALF)
    return [(cube[brick, :, 0], cube[brick, :, 1]) for brick in range(BRICKS)]


def put_halves(halves_ref, start, bricks):
    for brick, lines in enumerate(bricks):
        for half in range(2):
            first = start + brick * CUBE
            halves_ref[half, first : first + CUBE, :] = lines[half].reshape(CUBE, HALF)


def cotangent_lines(cotangent_ref):
    cube = cotangent_ref[...].astype(F32).reshape(BRICKS, EDGE, EDGE, LINE)
    return [(cube[brick, :, :, :HALF], cube[brick, :, :, HALF:]) for brick in range(BRICKS)]


def pack_faces(faces_ref, base, halves_ref, start, high):
    x_face = pair(halves_ref, start + ((EDGE - 1) * EDGE if high else 0), EDGE)
    y_face = pair(halves_ref, start + (EDGE - 1 if high else 0), EDGE, EDGE)
    for half in range(2):
        lanes = slice(half * HALF, half * HALF + HALF)
        faces_ref[base : base + EDGE, lanes] = x_face[half]
        faces_ref[base + EDGE : base + 2 * EDGE, lanes] = y_face[half]
    tile = halves_ref[1 if high else 0, start : start + CUBE, :]
    lane = lanes_of((16, 128)) // CHANNELS
    packed = jnp.zeros((16, 128), F32)
    for part in range(4):
        shift = (part + 1 if high else part) % 4 * CHANNELS
        piece = tile[part * 16 : part * 16 + 16]
        packed = jnp.where(lane == part, pltpu.roll(piece, shift, 1) if shift else piece, packed)
    faces_ref[base + 2 * EDGE : base + FACE, :128] = packed[:8]
    faces_ref[base + 2 * EDGE : base + FACE, 128:] = packed[8:]


def pack_all(bricks, halves_ref, faces_ref, high_out, low_out):
    put_halves(halves_ref, 0, bricks)
    for high, out_ref in ((True, high_out), (False, low_out)):
        for brick in range(BRICKS):
            pack_faces(faces_ref, brick * FACE, halves_ref, brick * CUBE, high)
        out_ref[...] = faces_ref[...].astype(BF16)


def to_partners(high_ref, low_ref, far_out, near_out):
    even = lax.axis_index("space") % 2 == 0
    far_out[...] = jnp.where(even, low_ref[...], high_ref[...])
    near_out[...] = jnp.where(even, high_ref[...], low_ref[...])


def faces_kernel(cotangent_ref, high_out, low_out, far_out, near_out, halves_ref, faces_ref):
    pack_all(cotangent_lines(cotangent_ref), halves_ref, faces_ref, high_out, low_out)
    to_partners(high_out, low_out, far_out, near_out)


def unpack_depth(halves, high):
    packed = jnp.concatenate(halves, axis=0)
    pieces = []
    for part in range(4):
        shift = ((3 - part) if high else (4 - part)) % 4 * CHANNELS
        pieces.append(pltpu.roll(packed, shift, 1) if shift else packed)
    return jnp.concatenate(pieces, axis=0).reshape(EDGE, EDGE, 128)


def first_kernel(
    links_in, received_ref, up_ref, band_ref,
    slope_out, hidden_out, turned_out, pad_out,
    volumes_ref, rows_ref, links_ref, links_sem,
):
    links_copy = pltpu.make_async_copy(links_in, links_ref, links_sem)
    links_copy.start()
    position = lax.axis_index("space")
    tiles = received_ref.shape[3] // (3 * BRICKS)
    received = received_ref[:, pl.ds(scene_of(received_ref), 1)]
    rows_ref[0 : 3 * BRICKS * tiles] = jnp.sum(received.astype(F32), axis=(0, 1, 2))
    rows_ref[3 * BRICKS * tiles :] = jnp.zeros((2 * tiles, 128), F32)
    cells = []
    for tile in range(tiles):
        rows = rows_ref[pl.ds(tile, 8, stride=tiles), :]
        cells += [rows[:, :64], rows[:, 64:]]
    lifted = dot(jnp.concatenate(cells, axis=0).astype(BF16), up_ref[...])
    lifted = lifted.astype(BF16).astype(F32)
    for cell in range(8):
        a, b, c = cell // 4, cell // 2 % 2, cell % 2
        for sub in range(16):
            line = (4 * a + sub // 4) * EDGE + 4 * b + sub % 4
            volumes_ref[c, line * 8 : line * 8 + 8, :] = lifted[
                cell * 8 : cell * 8 + 8, sub * 128 : sub * 128 + 128
            ]
    links_copy.wait()
    for brick in range(BRICKS):

        def near(face):
            link = links_ref[0, brick, face]
            index = jnp.clip(link - BRICKS * (position - 1), 0, 3 * BRICKS - 1)
            return index, jnp.where(link >= 0, 1.0, 0.0).astype(F32)

        def x_face(face):
            index, present = near(face)
            line = EDGE * (EDGE - 1) if face % 2 == 0 else 0
            return [half * present for half in pair(volumes_ref, line * 8 + index, EDGE, 8)]

        def y_face(face):
            index, present = near(face)
            line = EDGE - 1 if face % 2 == 0 else 0
            return [half * present for half in pair(volumes_ref, line * 8 + index, EDGE, 8 * EDGE)]

        def z_face(face):
            index, present = near(face)
            tile = volumes_ref[1 if face % 2 == 0 else 0, pl.ds(index, CUBE, stride=8), :] * present
            return tile.reshape(EDGE, EDGE, HALF)

        own = [half.reshape(EDGE, EDGE, HALF) for half in pair(volumes_ref, BRICKS + brick, CUBE, 8)]
        put_padded(pad_out, brick, own, x_face(0), x_face(1), y_face(2), y_face(3), z_face(4), z_face(5))
    pre = convolve(pad_out, band_ref)
    sigmoid = 1.0 / (1.0 + jnp.exp(-pre))
    hidden = (pre / (1.0 + jnp.exp(-pre))).astype(BF16)
    slope_out[...] = sigmoid * (1.0 + pre * (1.0 - sigmoid))
    hidden_out[...] = hidden
    hidden = hidden.astype(F32)
    turned_out[...] = jnp.transpose(hidden).astype(BF16)


def hidden_faces_kernel(hidden_ref, _parts, high_out, low_out, far_out, near_out, halves_ref, faces_ref):
    pack_all(half_lines(hidden_ref[...].astype(F32)), halves_ref, faces_ref, high_out, low_out)
    to_partners(high_out, low_out, far_out, near_out)


def fold(outer, places):
    lane = lanes_of((CHANNELS, 128)) // CHANNELS
    folded = None
    for block in range(4):
        start, tile = places[block]
        rows = outer[start : start + CHANNELS, tile * 128 : tile * 128 + 128]
        folded = rows if folded is None else jnp.where(lane == block, rows, folded)
    quarter = [folded[8 * q : 8 * q + 8] for q in range(4)]
    small = lanes_of((8, 128)) // CHANNELS
    total = None
    for turn in range(4):
        mixed = quarter[0]
        for q in range(1, 4):
            mixed = jnp.where(small == (q + turn) % 4, quarter[q], mixed)
        if turn:
            mixed = pltpu.roll(mixed, 128 - turn * CHANNELS, 1)
        total = mixed if total is None else total + mixed
    return total


def diagonal(shift):
    places = [None] * 4
    for z in range(4):
        other = z + shift
        places[other % 4] = (z * CHANNELS, 0 if 0 <= other < 4 else 1)
    return places


def put_masks(masks_ref, links_ref):
    position = lax.axis_index("space")
    for brick in range(BRICKS):
        for face in range(6):
            first = links_ref[0, brick, face] - BRICKS * (position - 1 if face % 2 == 0 else position)
            for i in range(2 * BRICKS):
                row = (brick * 6 + face) * 2 * BRICKS + i
                masks_ref[row : row + 1, :] = jnp.full((1, 128), jnp.where(first == i, 1.0, 0.0).astype(F32))


def pad_all(pad_ref, bricks, masks_ref, high_pool, low_pool, high_own, low_own, far, near):
    position = lax.axis_index("space")
    half = BRICKS * FACE
    even = position % 2 == 0
    high_pool[0:half] = jnp.where(even, far[...], near[...]).astype(F32)
    high_pool[half:] = high_own[...].astype(F32)
    low_pool[0:half] = low_own[...].astype(F32)
    low_pool[half:] = jnp.where(even, near[...], far[...]).astype(F32)
    for brick, lines in enumerate(bricks):

        def face(number, axis):
            pool = high_pool if number % 2 == 0 else low_pool
            total = [0.0, 0.0]
            for i in range(2 * BRICKS):
                row = (brick * 6 + number) * 2 * BRICKS + i
                mask = masks_ref[row : row + 1, :]
                start = i * FACE + axis * EDGE
                for part in range(2):
                    found = pool[start : start + EDGE, part * HALF : part * HALF + HALF]
                    total[part] = total[part] + found * mask
            return total

        put_padded(
            pad_ref, brick, lines, face(0, 0), face(1, 0), face(2, 1), face(3, 1),
            unpack_depth(face(4, 2), True), unpack_depth(face(5, 2), False),
        )


def second_kernel(
    masks_ref, cotangent_ref, band_ref, slope_ref, hidden_ref, lifted_pad, high_own, low_own, far, near,
    sums_out, lifted_out,
    high_pool, low_pool, cotangent_pad, sums_ref,
):
    lifted_out[...] = window(lifted_pad, 4)[:, :HALF]
    bricks = cotangent_lines(cotangent_ref)
    pad_all(cotangent_pad, bricks, masks_ref, high_pool, low_pool, high_own, low_own, far, near)
    gradient = (convolve(cotangent_pad, band_ref) * slope_ref[...]).astype(BF16)
    gradient = jnp.transpose(gradient.astype(F32)).astype(BF16)
    hidden = hidden_ref[...]
    sums_ref[8 * BLOCKS :] = jnp.zeros((sums_ref.shape[0] - 8 * BLOCKS, 128), F32)
    for k in range(9):
        one = dot(gradient, window(lifted_pad, k))
        two = dot(hidden, window(cotangent_pad, 8 - k))
        for part in range(3):
            start = 8 * (3 * k + part)
            sums_ref[start : start + 8] = fold(one, diagonal(part - 1))
            start += 8 * 27
            sums_ref[start : start + 8] = fold(two, diagonal(1 - part))
    sums_out[...] = sums_ref[...].astype(BF16)


def fine_kernel(
    masks_ref, band_ref, lifted_ref, hidden_ref, high_own, low_own, far, near,
    fine_out, high_pool, low_pool, hidden_pad,
):
    bricks = half_lines(hidden_ref[...].astype(F32))
    pad_all(hidden_pad, bricks, masks_ref, high_pool, low_pool, high_own, low_own, far, near)
    fine = lifted_ref[...].astype(F32) + convolve(hidden_pad, band_ref)
    fine = fine.reshape(LINES // EDGE, 2, EDGE, HALF)
    fine = jnp.concatenate([fine[:, 0], fine[:, 1]], axis=-1)
    fine_out[...] = fine.astype(BF16).reshape(fine_out.shape)


def sum_kernel(devices, scale, parts_ref, out_hbm, rows_ref, shares_ref, sems):
    rows_ref[...] = parts_ref[...].astype(F32)
    share = rows_ref.shape[0] // devices
    pieces = [rows_ref[share * i : share * i + share] for i in range(devices)]
    while len(pieces) > 1:
        pairs = [a + b for a, b in zip(pieces[::2], pieces[1::2])]
        pieces = pairs + pieces[len(pieces) - len(pieces) % 2 :]
    total = pieces[0] * scale
    some = shares_ref.shape[0]
    for i in range(some // share):
        rows_ref[share * i : share * i + share] = total
    shares_ref[...] = rows_ref[0:some].astype(BF16)
    copies = []
    for i in range(out_hbm.shape[0] // some):
        copies.append(pltpu.make_async_copy(shares_ref, out_hbm.at[pl.ds(some * i, some)], sems.at[i]))
        copies[-1].start()
    for copy in copies:
        copy.wait()


def unpacked(tile):
    pieces = [tile] + [pltpu.roll(tile, 128 - q * CHANNELS, 1) for q in range(1, 4)]
    return jnp.concatenate(pieces, axis=0)[:, :CHANNELS]


def turned(tiles):
    lane = lanes_of((8, 128)) // CHANNELS
    rows = []
    for q in range(4):
        mixed = jnp.zeros((8, 128), F32)
        for n, tile in enumerate(tiles):
            shift = (n - q) % 4 * CHANNELS
            mixed = jnp.where(lane == n, pltpu.roll(tile, shift, 1) if shift else tile, mixed)
        rows.append(mixed)
    return jnp.transpose(jnp.concatenate(rows, axis=0))


def unpack_kernel(sums_ref, fine_ref, one_out, two_out, fine_out, rows_ref, one_ref, two_ref, sems, fine_sem):
    fine_copy = pltpu.make_async_copy(fine_ref, fine_out, fine_sem)
    fine_copy.start()
    rows_ref[...] = sums_ref[...].astype(F32)
    tiles = [rows_ref[8 * index : 8 * index + 8] for index in range(BLOCKS)]
    copies = []
    for which, (block_ref, out) in ((1, (two_ref, two_out)), (0, (one_ref, one_out))):
        for part, (first, last) in enumerate(((0, 8), (8, 16), (16, 27))):
            for index in range(first, last):
                if which:
                    block_ref[index] = unpacked(tiles[27 + index])
                elif index % 4 == 0:
                    blocks = turned(tiles[index : min(index + 4, 27)])
                    for n in range(min(4, 27 - index)):
                        block_ref[index + n] = blocks[CHANNELS * n : CHANNELS * n + CHANNELS]
            span = pl.ds(first, last - first)
            copies.append(pltpu.make_async_copy(block_ref.at[span], out.at[span], sems.at[which, part]))
            copies[-1].start()
    for copy in copies:
        copy.wait()
    fine_copy.wait()


def call(kernel, out_shape, scratch=(), hbm=(), inputs=1, limit=24, cost=None, out=pltpu.VMEM):
    spaces = [pl.ANY if i in hbm else pltpu.VMEM for i in range(inputs)]
    return pl.pallas_call(
        kernel,
        out_shape=out_shape,
        in_specs=[pl.BlockSpec(memory_space=space) for space in spaces],
        out_specs=jax.tree.map(lambda _: pl.BlockSpec(memory_space=out), out_shape),
        scratch_shapes=list(scratch),
        compiler_params=pltpu.CompilerParams(vmem_limit_bytes=limit * 2**20),
        cost_estimate=cost,
    )


def shape(*dims, dtype=BF16):
    return jax.ShapeDtypeStruct(dims, dtype)


def swapped(value, first):
    pairs = [(i, i + 1) for i in range(first, lax.axis_size("space") - 1, 2)]
    return lax.ppermute(value, "space", pairs + [(target, source) for source, target in pairs])


def crosswise(count):
    return [[i % 4 * (count // 4) + i // 4 for i in range(count)]]


def exchanged(rows):
    everyone = lax.axis_size("space") * lax.axis_size("dp")
    shares = rows.reshape(everyone, -1, 2, 128)
    shares = lax.all_to_all(
        shares, ("space", "dp"), split_axis=0, concat_axis=0, axis_index_groups=crosswise(everyone), tiled=True
    )
    return shares.reshape(rows.shape)


def body(coarse_latents, active_blocks, face_links, cotangent, up_weight, conv_one, conv_two):
    devices = lax.axis_size("space")
    everyone = devices * lax.axis_size("dp")
    held, width = coarse_latents.shape[1:]
    bricks = active_blocks.shape[1]
    tiles = width // 128
    scenes = 2 if lax.axis_size("dp") == 2 else 1
    count = 3 * BRICKS * tiles
    blocks = pltpu.VMEM((devices // 4, 4, count, 128), BF16)
    packed = call(
        pick_kernel,
        shape(devices // 4, scenes, 4, count, 128),
        [
            pltpu.VMEM((1, bricks), jnp.int32),
            pltpu.VMEM((1, held, width), BF16),
            pltpu.VMEM(((bricks + 16) * tiles, 128), F32),
            blocks,
            blocks,
            pltpu.SemaphoreType.DMA((7,)),
        ],
        hbm=(0, 1),
        inputs=2,
        limit=60,
        out=pl.ANY,
    )(active_blocks, coarse_latents)
    received = lax.all_to_all(
        packed.reshape(devices * scenes, count, 128),
        ("space", "dp") if scenes == 2 else "space",
        split_axis=0,
        concat_axis=0,
        axis_index_groups=crosswise(devices * scenes),
        tiled=True,
    ).reshape(packed.shape)
    cost = pl.CostEstimate(flops=10**9, bytes_accessed=2 * 10**6, transcendentals=0)
    face = shape(BRICKS * FACE, LINE)
    halves = pltpu.VMEM((2, LINES, HALF), F32)
    faces = pltpu.VMEM((BRICKS * FACE, LINE), F32)
    pool = pltpu.VMEM((2 * BRICKS * FACE, LINE), F32)
    volume = shape(ROWS, HALF)
    links = [pltpu.SMEM(face_links.shape, jnp.int32), pltpu.SemaphoreType.DMA]
    pad_shape = (3, BRICKS, EDGE + 2, 2 * EDGE, WIDE)
    pad = pltpu.VMEM(pad_shape, BF16)
    high, low, far, near = call(faces_kernel, (face,) * 4, [halves, faces])(cotangent)
    far = swapped(far, 1)
    near = swapped(near, 0)
    masks = shape(BRICKS * 6 * 2 * BRICKS, 128, dtype=F32)
    band_one, band_back, masks = call(
        masks_kernel, (shape(*BAND), shape(*BAND), masks), links, hbm=(0,), inputs=3, cost=cost
    )(face_links, conv_one, conv_two)
    slope, hidden, turned, lifted_pad = call(
        first_kernel,
        (
            shape(ROWS, HALF, dtype=F32), volume, shape(HALF, ROWS), shape(*pad_shape),
        ),
        [pltpu.VMEM((2, 8 * CUBE, 128), F32), pltpu.VMEM((8 * tiles, 128), F32), *links],
        hbm=(0,),
        inputs=4,
    )(face_links, received, up_weight, band_one)
    share = 2 * -(-4 * BLOCKS // everyone)
    packed_rows = (everyone * share, 128)
    sums, lifted = call(
        second_kernel,
        (shape(*packed_rows), volume),
        [pool, pool, pad, pltpu.VMEM(packed_rows, F32)],
        inputs=10,
    )(masks, cotangent, band_back, slope, turned, lifted_pad, high, low, far, near)
    parts = exchanged(sums)
    hidden_high, hidden_low, hidden_far, hidden_near = call(
        hidden_faces_kernel, (face,) * 4, [halves, faces], hbm=(1,), inputs=2
    )(hidden, parts)
    hidden_far = swapped(hidden_far, 1)
    hidden_near = swapped(hidden_near, 0)
    band_two = call(band_kernel, shape(*BAND), cost=cost)(conv_two)
    fine = call(fine_kernel, shape(*cotangent.shape), [pool, pool, pad], inputs=8, cost=cost)(
        masks, band_two, lifted, hidden, hidden_high, hidden_low, hidden_far, hidden_near
    )
    scale = 1.0 / math.sqrt(lax.axis_size("dp") * devices * BRICKS * EDGE**3)
    times = 4 if everyone % 32 == 0 else 1
    total = call(
        functools.partial(sum_kernel, everyone, scale),
        shape(*packed_rows),
        [
            pltpu.VMEM(packed_rows, F32),
            pltpu.VMEM((packed_rows[0] // times, 128), BF16),
            pltpu.SemaphoreType.DMA((times,)),
        ],
        out=pl.ANY,
    )(parts)
    gathered = exchanged(total)
    grads = shape(27, CHANNELS, CHANNELS, dtype=F32)
    block = pltpu.VMEM(grads.shape, F32)
    scratch = [pltpu.VMEM(packed_rows, F32), block, block]
    scratch += [pltpu.SemaphoreType.DMA((2, 3)), pltpu.SemaphoreType.DMA]
    grad_one, grad_two, fine = call(
        unpack_kernel, (grads, grads, shape(*fine.shape)), scratch, inputs=2, out=pl.ANY
    )(gathered, fine)
    return (fine, grad_one, grad_two)


def solution(mesh):
    return jax.shard_map(
        body,
        mesh=mesh,
        in_specs=(
            P("dp", "space", None),
            P("dp", None),
            P("dp", "space", None),
            P("dp", "space", None, None, None),
            P(),
            P(),
            P(),
        ),
        out_specs=(P("dp", "space", None, None, None), P(), P()),
        check_vma=False,
    )
```

```python
import functools
import math

import jax
import jax.numpy as jnp
from jax import lax
from jax.experimental import pallas as pl
from jax.experimental.pallas import tpu as pltpu
from jax.sharding import PartitionSpec as P

BF16 = jnp.bfloat16
F32 = jnp.float32
EDGE = 8
CHANNELS = 32
LINE = EDGE * CHANNELS
HALF = LINE // 2
WIDE = 2 * HALF
BRICKS = 2
CUBE = EDGE * EDGE
LINES = BRICKS * CUBE
BAND = (9, WIDE, HALF)
ROWS = 2 * LINES
FACE = 3 * EDGE
GROUPS = 7


def dot(left, right):
    return jnp.dot(left, right, preferred_element_type=F32)


def dot_rows(left, right):
    return lax.dot_general(left, right, (((0,), (0,)), ((), ())), preferred_element_type=F32)


def pair(halves_ref, start, count, stride=1):
    index = pl.ds(start, count, stride=stride) if stride > 1 else pl.ds(start, count)
    return halves_ref[0, index, :], halves_ref[1, index, :]


def lanes_of(shape):
    return lax.broadcasted_iota(jnp.int32, shape, len(shape) - 1)


def scene_of(blocks_ref):
    return lax.axis_index("dp") if blocks_ref.shape[1] > 1 else 0


def pick_kernel(ids_hbm, latents_hbm, out_hbm, ids_ref, latents_ref, rows_ref, blocks_ref, zeros_ref, sems):
    ids_copy = pltpu.make_async_copy(ids_hbm, ids_ref, sems.at[0])
    ids_copy.start()
    held, width = latents_ref.shape[1:]
    copies = []
    for i in range(4):
        part = pl.ds(i * held // 4, held // 4)
        copies.append(pltpu.make_async_copy(latents_hbm.at[0, part], latents_ref.at[0, part], sems.at[1 + i]))
        copies[-1].start()
    scene = scene_of(out_hbm)
    others = None
    if out_hbm.shape[1] > 1:
        zeros_ref[...] = jnp.zeros(zeros_ref.shape, BF16)
        others = pltpu.make_async_copy(zeros_ref, out_hbm.at[:, 1 - scene], sems.at[5])
        others.start()
    bricks = ids_ref.shape[1]
    margin = 8 * width // 128
    tiles = width // 128
    rows_ref[0:margin] = jnp.zeros((margin, 128), F32)
    rows_ref[margin + bricks * tiles :] = jnp.zeros((margin, 128), F32)
    first = lax.axis_index("space") * held
    rows = lax.broadcasted_iota(jnp.int32, (held, bricks), 0) + first
    ids_copy.wait()
    hot = jnp.where(rows == ids_ref[...], 1.0, 0.0).astype(BF16)
    for copy in copies:
        copy.wait()
    picked = dot_rows(hot, latents_ref[0])
    for tile in range(tiles):
        rows_ref[pl.ds(margin + tile, bricks, stride=tiles), :] = picked[:, tile * 128 : tile * 128 + 128]
    count = blocks_ref.shape[1]
    for receiver in range(blocks_ref.shape[0]):
        start = margin + BRICKS * (receiver - 1) * tiles
        blocks_ref[receiver] = rows_ref[start : start + count].astype(BF16)
    found = pltpu.make_async_copy(blocks_ref, out_hbm.at[:, scene], sems.at[6])
    found.start()
    found.wait()
    if others is not None:
        others.wait()


def build_band(band_ref, rows):
    shape = (3 * CHANNELS, HALF)
    row = lax.broadcasted_iota(jnp.int32, shape, 0)
    target = CHANNELS - (row // CHANNELS) * CHANNELS + row % CHANNELS
    distance = lanes_of(shape) - target
    band_ref[:, HALF:, :] = jnp.zeros((9, HALF, HALF), BF16)
    for z in range(-1, 5):
        select = jnp.where(distance == z * CHANNELS, 1.0, 0.0).astype(BF16)
        block = dot(rows, select).astype(BF16)
        start = z % 8 * CHANNELS
        band_ref[:, start : start + CHANNELS, :] = block.reshape(9, CHANNELS, HALF)


def weight_rows(weights):
    cube = weights.reshape(9, 3, CHANNELS, CHANNELS)
    rows = jnp.concatenate([cube[:, 0], cube[:, 1], cube[:, 2]], axis=-1)
    return rows.reshape(9 * CHANNELS, 3 * CHANNELS).astype(BF16)


def flipped_rows(weights):
    cube = jnp.swapaxes(weights, 1, 2).reshape(9, 3, CHANNELS, CHANNELS)
    pieces = [jnp.concatenate([cube[8 - k, 2], cube[8 - k, 1], cube[8 - k, 0]], axis=-1) for k in range(9)]
    return jnp.concatenate(pieces, axis=0).astype(BF16)


def band_kernel(weights_ref, band_ref):
    build_band(band_ref, weight_rows(weights_ref[...].astype(F32)))


def masks_kernel(links_in, one_ref, two_ref, band_ref, back_ref, masks_ref, links_ref, links_sem):
    links_copy = pltpu.make_async_copy(links_in, links_ref, links_sem)
    links_copy.start()
    build_band(band_ref, weight_rows(one_ref[...].astype(F32)))
    build_band(back_ref, flipped_rows(two_ref[...].astype(F32)))
    links_copy.wait()
    put_masks(masks_ref, links_ref)


def put_padded(pad_ref, brick, lines, x_low, x_high, y_low, y_high, z_low, z_high):
    def joined(halves, before, after):
        lane = lanes_of(halves[0].shape)
        first = jnp.where(lane < CHANNELS, halves[1], before)
        second = jnp.where(lane >= HALF - CHANNELS, halves[0], after)
        return jnp.concatenate([halves[0], first], axis=-1), jnp.concatenate([halves[1], second], axis=-1)

    inside = joined(lines, z_low, z_high)
    x_low, x_high, y_low, y_high = [joined(face, 0.0, 0.0) for face in (x_low, x_high, y_low, y_high)]
    none = jnp.zeros((1, WIDE), F32)
    shifted = [[], [], []]
    for half in range(2):
        slabs = jnp.concatenate([x_low[half][None], inside[half], x_high[half][None]], axis=0)
        row = lax.broadcasted_iota(jnp.int32, slabs.shape, 1)
        low = jnp.concatenate([none, y_low[half], none], axis=0)[:, None, :]
        high = jnp.concatenate([none, y_high[half], none], axis=0)[:, None, :]
        shifted[0].append(jnp.where(row == 0, low, pltpu.roll(slabs, 1, 1)))
        shifted[1].append(slabs)
        shifted[2].append(jnp.where(row == EDGE - 1, high, pltpu.roll(slabs, EDGE - 1, 1)))
    for dy in range(3):
        pad_ref[dy, brick] = jnp.concatenate(shifted[dy], axis=1).astype(BF16)


def window(pad_ref, k):
    return pad_ref[k % 3, :, k // 3 : k // 3 + EDGE].reshape(ROWS, WIDE)


def convolve(pad_ref, band_ref):
    both, last = None, None
    for dy in range(3):
        slabs = pad_ref[dy, :, : EDGE + 1].reshape(-1, WIDE)
        term = dot(slabs, jnp.concatenate([band_ref[dy], band_ref[3 + dy]], axis=1))
        both = term if both is None else both + term
        term = dot(window(pad_ref, 6 + dy), band_ref[6 + dy])
        last = term if last is None else last + term
    both = both.reshape(BRICKS, EDGE + 1, 2 * EDGE, 2 * HALF)
    total = both[:, :EDGE, :, :HALF] + both[:, 1:, :, HALF:]
    return total.reshape(ROWS, HALF) + last


def half_lines(values):
    cube = values.reshape(BRICKS, EDGE, 2, EDGE, HALF)
    return [(cube[brick, :, 0], cube[brick, :, 1]) for brick in range(BRICKS)]


def put_halves(halves_ref, start, bricks):
    for brick, lines in enumerate(bricks):
        for half in range(2):
            first = start + brick * CUBE
            halves_ref[half, first : first + CUBE, :] = lines[half].reshape(CUBE, HALF)


def cotangent_lines(cotangent_ref):
    cube = cotangent_ref[...].astype(F32).reshape(BRICKS, EDGE, EDGE, LINE)
    return [(cube[brick, :, :, :HALF], cube[brick, :, :, HALF:]) for brick in range(BRICKS)]


def pack_faces(faces_ref, base, halves_ref, start, high):
    x_face = pair(halves_ref, start + ((EDGE - 1) * EDGE if high else 0), EDGE)
    y_face = pair(halves_ref, start + (EDGE - 1 if high else 0), EDGE, EDGE)
    for half in range(2):
        lanes = slice(half * HALF, half * HALF + HALF)
        faces_ref[base : base + EDGE, lanes] = x_face[half]
        faces_ref[base + EDGE : base + 2 * EDGE, lanes] = y_face[half]
    tile = halves_ref[1 if high else 0, start : start + CUBE, :]
    lane = lanes_of((16, 128)) // CHANNELS
    packed = jnp.zeros((16, 128), F32)
    for part in range(4):
        shift = (part + 1 if high else part) % 4 * CHANNELS
        piece = tile[part * 16 : part * 16 + 16]
        packed = jnp.where(lane == part, pltpu.roll(piece, shift, 1) if shift else piece, packed)
    faces_ref[base + 2 * EDGE : base + FACE, :128] = packed[:8]
    faces_ref[base + 2 * EDGE : base + FACE, 128:] = packed[8:]


def pack_all(bricks, halves_ref, faces_ref, high_out, low_out):
    put_halves(halves_ref, 0, bricks)
    for high, out_ref in ((True, high_out), (False, low_out)):
        for brick in range(BRICKS):
            pack_faces(faces_ref, brick * FACE, halves_ref, brick * CUBE, high)
        out_ref[...] = faces_ref[...].astype(BF16)


def to_partners(high_ref, low_ref, far_out, near_out):
    even = lax.axis_index("space") % 2 == 0
    far_out[...] = jnp.where(even, low_ref[...], high_ref[...])
    near_out[...] = jnp.where(even, high_ref[...], low_ref[...])


def faces_kernel(cotangent_ref, high_out, low_out, far_out, near_out, halves_ref, faces_ref):
    pack_all(cotangent_lines(cotangent_ref), halves_ref, faces_ref, high_out, low_out)
    to_partners(high_out, low_out, far_out, near_out)


def unpack_depth(halves, high):
    packed = jnp.concatenate(halves, axis=0)
    pieces = []
    for part in range(4):
        shift = ((3 - part) if high else (4 - part)) % 4 * CHANNELS
        pieces.append(pltpu.roll(packed, shift, 1) if shift else packed)
    return jnp.concatenate(pieces, axis=0).reshape(EDGE, EDGE, 128)


def first_kernel(
    links_in, received_ref, up_ref, band_ref,
    slope_out, hidden_out, turned_out, pad_out,
    volumes_ref, rows_ref, links_ref, links_sem,
):
    links_copy = pltpu.make_async_copy(links_in, links_ref, links_sem)
    links_copy.start()
    position = lax.axis_index("space")
    tiles = received_ref.shape[2] // (3 * BRICKS)
    received = received_ref[:, pl.ds(scene_of(received_ref), 1)]
    rows_ref[0 : 3 * BRICKS * tiles] = jnp.sum(received.astype(F32), axis=(0, 1))
    rows_ref[3 * BRICKS * tiles :] = jnp.zeros((2 * tiles, 128), F32)
    cells = []
    for tile in range(tiles):
        rows = rows_ref[pl.ds(tile, 8, stride=tiles), :]
        cells += [rows[:, :64], rows[:, 64:]]
    lifted = dot(jnp.concatenate(cells, axis=0).astype(BF16), up_ref[...])
    lifted = lifted.astype(BF16).astype(F32)
    for cell in range(8):
        a, b, c = cell // 4, cell // 2 % 2, cell % 2
        for sub in range(16):
            line = (4 * a + sub // 4) * EDGE + 4 * b + sub % 4
            volumes_ref[c, line * 8 : line * 8 + 8, :] = lifted[
                cell * 8 : cell * 8 + 8, sub * 128 : sub * 128 + 128
            ]
    links_copy.wait()
    for brick in range(BRICKS):

        def near(face):
            link = links_ref[0, brick, face]
            index = jnp.clip(link - BRICKS * (position - 1), 0, 3 * BRICKS - 1)
            return index, jnp.where(link >= 0, 1.0, 0.0).astype(F32)

        def x_face(face):
            index, present = near(face)
            line = EDGE * (EDGE - 1) if face % 2 == 0 else 0
            return [half * present for half in pair(volumes_ref, line * 8 + index, EDGE, 8)]

        def y_face(face):
            index, present = near(face)
            line = EDGE - 1 if face % 2 == 0 else 0
            return [half * present for half in pair(volumes_ref, line * 8 + index, EDGE, 8 * EDGE)]

        def z_face(face):
            index, present = near(face)
            tile = volumes_ref[1 if face % 2 == 0 else 0, pl.ds(index, CUBE, stride=8), :] * present
            return tile.reshape(EDGE, EDGE, HALF)

        own = [half.reshape(EDGE, EDGE, HALF) for half in pair(volumes_ref, BRICKS + brick, CUBE, 8)]
        put_padded(pad_out, brick, own, x_face(0), x_face(1), y_face(2), y_face(3), z_face(4), z_face(5))
    pre = convolve(pad_out, band_ref)
    sigmoid = 1.0 / (1.0 + jnp.exp(-pre))
    hidden = (pre / (1.0 + jnp.exp(-pre))).astype(BF16)
    slope_out[...] = sigmoid * (1.0 + pre * (1.0 - sigmoid))
    hidden_out[...] = hidden
    hidden = hidden.astype(F32)
    turned_out[...] = jnp.transpose(hidden).astype(BF16)


def hidden_faces_kernel(hidden_ref, _parts, high_out, low_out, far_out, near_out, halves_ref, faces_ref):
    pack_all(half_lines(hidden_ref[...].astype(F32)), halves_ref, faces_ref, high_out, low_out)
    to_partners(high_out, low_out, far_out, near_out)


def picked(outer, places):
    lane = lanes_of((CHANNELS, 128)) // CHANNELS
    found = None
    for block in range(4):
        start, tile = places[block]
        rows = outer[start : start + CHANNELS, tile * 128 : tile * 128 + 128]
        found = rows if found is None else jnp.where(lane == block, rows, found)
    return found


def fold(four):
    lane = lanes_of((CHANNELS, 128)) // CHANNELS
    total = None
    for turn in range(4):
        mixed = four[0]
        for n in range(1, len(four)):
            mixed = jnp.where(lane == (n + turn) % 4, four[n], mixed)
        if turn:
            mixed = pltpu.roll(mixed, 128 - turn * CHANNELS, 1)
        total = mixed if total is None else total + mixed
    return total


def diagonal(shift):
    places = [None] * 4
    for z in range(4):
        other = z + shift
        places[other % 4] = (z * CHANNELS, 0 if 0 <= other < 4 else 1)
    return places


def put_masks(masks_ref, links_ref):
    position = lax.axis_index("space")
    for brick in range(BRICKS):
        for face in range(6):
            first = links_ref[0, brick, face] - BRICKS * (position - 1 if face % 2 == 0 else position)
            for i in range(2 * BRICKS):
                row = (brick * 6 + face) * 2 * BRICKS + i
                masks_ref[row : row + 1, :] = jnp.full((1, 128), jnp.where(first == i, 1.0, 0.0).astype(F32))


def pad_all(pad_ref, bricks, masks_ref, high_pool, low_pool, high_own, low_own, far, near):
    position = lax.axis_index("space")
    half = BRICKS * FACE
    even = position % 2 == 0
    high_pool[0:half] = jnp.where(even, far[...], near[...]).astype(F32)
    high_pool[half:] = high_own[...].astype(F32)
    low_pool[0:half] = low_own[...].astype(F32)
    low_pool[half:] = jnp.where(even, near[...], far[...]).astype(F32)
    for brick, lines in enumerate(bricks):

        def face(number, axis):
            pool = high_pool if number % 2 == 0 else low_pool
            total = [0.0, 0.0]
            for i in range(2 * BRICKS):
                row = (brick * 6 + number) * 2 * BRICKS + i
                mask = masks_ref[row : row + 1, :]
                start = i * FACE + axis * EDGE
                for part in range(2):
                    found = pool[start : start + EDGE, part * HALF : part * HALF + HALF]
                    total[part] = total[part] + found * mask
            return total

        put_padded(
            pad_ref, brick, lines, face(0, 0), face(1, 0), face(2, 1), face(3, 1),
            unpack_depth(face(4, 2), True), unpack_depth(face(5, 2), False),
        )


def second_kernel(
    masks_ref, cotangent_ref, band_ref, slope_ref, hidden_ref, lifted_pad, high_own, low_own, far, near,
    sums_out, lifted_out,
    high_pool, low_pool, cotangent_pad, sums_ref,
):
    lifted_out[...] = window(lifted_pad, 4)[:, :HALF]
    bricks = cotangent_lines(cotangent_ref)
    pad_all(cotangent_pad, bricks, masks_ref, high_pool, low_pool, high_own, low_own, far, near)
    gradient = (convolve(cotangent_pad, band_ref) * slope_ref[...]).astype(BF16)
    gradient = jnp.transpose(gradient.astype(F32)).astype(BF16)
    hidden = hidden_ref[...]
    if sums_ref.shape[0] > 2 * GROUPS * CHANNELS:
        rest = sums_ref.shape[0] - 2 * GROUPS * CHANNELS
        sums_ref[2 * GROUPS * CHANNELS :] = jnp.zeros((rest, 128), F32)
    ones, twos = [], []
    for k in range(9):
        one = dot(gradient, window(lifted_pad, k))
        two = dot(hidden, window(cotangent_pad, 8 - k))
        ones += [picked(one, diagonal(part - 1)) for part in range(3)]
        twos += [picked(two, diagonal(1 - part)) for part in range(3)]
        while len(ones) >= 4 or (k == 8 and ones):
            group = (3 * k + 3 - len(ones)) // 4
            for first, blocks in ((0, ones), (GROUPS, twos)):
                start = (first + group) * CHANNELS
                sums_ref[start : start + CHANNELS] = fold(blocks[:4])
            ones, twos = ones[4:], twos[4:]
    sums_out[...] = sums_ref[...].astype(BF16)


def fine_kernel(
    masks_ref, band_ref, lifted_ref, hidden_ref, high_own, low_own, far, near,
    fine_out, high_pool, low_pool, hidden_pad,
):
    bricks = half_lines(hidden_ref[...].astype(F32))
    pad_all(hidden_pad, bricks, masks_ref, high_pool, low_pool, high_own, low_own, far, near)
    fine = lifted_ref[...].astype(F32) + convolve(hidden_pad, band_ref)
    fine = fine.reshape(LINES // EDGE, 2, EDGE, HALF)
    fine = jnp.concatenate([fine[:, 0], fine[:, 1]], axis=-1)
    fine_out[...] = fine.astype(BF16).reshape(fine_out.shape)


def sum_kernel(devices, scale, parts_ref, out_hbm, rows_ref, shares_ref, sems):
    rows_ref[...] = parts_ref[...].astype(F32)
    share = rows_ref.shape[0] // devices
    pieces = [rows_ref[share * i : share * i + share] for i in range(devices)]
    while len(pieces) > 1:
        pairs = [a + b for a, b in zip(pieces[::2], pieces[1::2])]
        pieces = pairs + pieces[len(pieces) - len(pieces) % 2 :]
    total = pieces[0] * scale
    some = shares_ref.shape[0]
    for i in range(some // share):
        rows_ref[share * i : share * i + share] = total
    shares_ref[...] = rows_ref[0:some].astype(BF16)
    copies = []
    for i in range(out_hbm.shape[0] // some):
        copies.append(pltpu.make_async_copy(shares_ref, out_hbm.at[pl.ds(some * i, some)], sems.at[i]))
        copies[-1].start()
    for copy in copies:
        copy.wait()


def unpack_kernel(sums_ref, fine_ref, one_out, two_out, fine_out, rows_ref, one_ref, two_ref, sems, fine_sem):
    fine_copy = pltpu.make_async_copy(fine_ref, fine_out, fine_sem)
    fine_copy.start()
    rows_ref[...] = sums_ref[...].astype(F32)
    copies = []
    for which, (block_ref, out) in ((1, (two_ref, two_out)), (0, (one_ref, one_out))):
        for part, (first, last) in enumerate(((0, 2), (2, 4), (4, GROUPS))):
            for group in range(first, last):
                start = (which * GROUPS + group) * CHANNELS
                four = rows_ref[start : start + CHANNELS]
                turned = None if which else jnp.transpose(four)
                for n in range(min(4, 27 - 4 * group)):
                    if which:
                        block = pltpu.roll(four, 128 - n * CHANNELS, 1) if n else four
                        block_ref[4 * group + n] = block[:, :CHANNELS]
                    else:
                        block_ref[4 * group + n] = turned[CHANNELS * n : CHANNELS * n + CHANNELS]
            span = pl.ds(4 * first, min(4 * last, 27) - 4 * first)
            copies.append(pltpu.make_async_copy(block_ref.at[span], out.at[span], sems.at[which, part]))
            copies[-1].start()
    for copy in copies:
        copy.wait()
    fine_copy.wait()


def call(kernel, out_shape, scratch=(), hbm=(), inputs=1, limit=24, cost=None, out=pltpu.VMEM):
    spaces = [pl.ANY if i in hbm else pltpu.VMEM for i in range(inputs)]
    return pl.pallas_call(
        kernel,
        out_shape=out_shape,
        in_specs=[pl.BlockSpec(memory_space=space) for space in spaces],
        out_specs=jax.tree.map(lambda _: pl.BlockSpec(memory_space=out), out_shape),
        scratch_shapes=list(scratch),
        compiler_params=pltpu.CompilerParams(vmem_limit_bytes=limit * 2**20),
        cost_estimate=cost,
    )


def shape(*dims, dtype=BF16):
    return jax.ShapeDtypeStruct(dims, dtype)


def swapped(value, first):
    pairs = [(i, i + 1) for i in range(first, lax.axis_size("space") - 1, 2)]
    return lax.ppermute(value, "space", pairs + [(target, source) for source, target in pairs])


def exchanged(rows):
    everyone = lax.axis_size("space") * lax.axis_size("dp")
    shares = rows.reshape(everyone, -1, 2, 128)
    shares = lax.all_to_all(shares, ("space", "dp"), split_axis=0, concat_axis=0, tiled=True)
    return shares.reshape(rows.shape)


def body(coarse_latents, active_blocks, face_links, cotangent, up_weight, conv_one, conv_two):
    devices = lax.axis_size("space")
    everyone = devices * lax.axis_size("dp")
    held, width = coarse_latents.shape[1:]
    bricks = active_blocks.shape[1]
    tiles = width // 128
    scenes = 2 if lax.axis_size("dp") == 2 else 1
    count = 3 * BRICKS * tiles
    blocks = pltpu.VMEM((devices, count, 128), BF16)
    packed = call(
        pick_kernel,
        shape(devices, scenes, count, 128),
        [
            pltpu.VMEM((1, bricks), jnp.int32),
            pltpu.VMEM((1, held, width), BF16),
            pltpu.VMEM(((bricks + 16) * tiles, 128), F32),
            blocks,
            blocks,
            pltpu.SemaphoreType.DMA((7,)),
        ],
        hbm=(0, 1),
        inputs=2,
        limit=60,
        out=pl.ANY,
    )(active_blocks, coarse_latents)
    received = lax.all_to_all(
        packed.reshape(devices * scenes, count, 128),
        ("space", "dp") if scenes == 2 else "space",
        split_axis=0,
        concat_axis=0,
        tiled=True,
    ).reshape(packed.shape)
    cost = pl.CostEstimate(flops=10**9, bytes_accessed=2 * 10**6, transcendentals=0)
    face = shape(BRICKS * FACE, LINE)
    halves = pltpu.VMEM((2, LINES, HALF), F32)
    faces = pltpu.VMEM((BRICKS * FACE, LINE), F32)
    pool = pltpu.VMEM((2 * BRICKS * FACE, LINE), F32)
    volume = shape(ROWS, HALF)
    links = [pltpu.SMEM(face_links.shape, jnp.int32), pltpu.SemaphoreType.DMA]
    pad_shape = (3, BRICKS, EDGE + 2, 2 * EDGE, WIDE)
    pad = pltpu.VMEM(pad_shape, BF16)
    high, low, far, near = call(faces_kernel, (face,) * 4, [halves, faces])(cotangent)
    far = swapped(far, 1)
    near = swapped(near, 0)
    masks = shape(BRICKS * 6 * 2 * BRICKS, 128, dtype=F32)
    band_one, band_back, masks = call(
        masks_kernel, (shape(*BAND), shape(*BAND), masks), links, hbm=(0,), inputs=3, cost=cost
    )(face_links, conv_one, conv_two)
    slope, hidden, turned, lifted_pad = call(
        first_kernel,
        (
            shape(ROWS, HALF, dtype=F32), volume, shape(HALF, ROWS), shape(*pad_shape),
        ),
        [pltpu.VMEM((2, 8 * CUBE, 128), F32), pltpu.VMEM((8 * tiles, 128), F32), *links],
        hbm=(0,),
        inputs=4,
    )(face_links, received, up_weight, band_one)
    share = 2 * -(-GROUPS * CHANNELS // everyone)
    packed_rows = (everyone * share, 128)
    sums, lifted = call(
        second_kernel,
        (shape(*packed_rows), volume),
        [pool, pool, pad, pltpu.VMEM(packed_rows, F32)],
        inputs=10,
    )(masks, cotangent, band_back, slope, turned, lifted_pad, high, low, far, near)
    parts = exchanged(sums)
    hidden_high, hidden_low, hidden_far, hidden_near = call(
        hidden_faces_kernel, (face,) * 4, [halves, faces], hbm=(1,), inputs=2
    )(hidden, parts)
    hidden_far = swapped(hidden_far, 1)
    hidden_near = swapped(hidden_near, 0)
    band_two = call(band_kernel, shape(*BAND), cost=cost)(conv_two)
    fine = call(fine_kernel, shape(*cotangent.shape), [pool, pool, pad], inputs=8, cost=cost)(
        masks, band_two, lifted, hidden, hidden_high, hidden_low, hidden_far, hidden_near
    )
    scale = 1.0 / math.sqrt(lax.axis_size("dp") * devices * BRICKS * EDGE**3)
    times = 4 if everyone % 32 == 0 else 1
    total = call(
        functools.partial(sum_kernel, everyone, scale),
        shape(*packed_rows),
        [
            pltpu.VMEM(packed_rows, F32),
            pltpu.VMEM((packed_rows[0] // times, 128), BF16),
            pltpu.SemaphoreType.DMA((times,)),
        ],
        out=pl.ANY,
    )(parts)
    gathered = exchanged(total)
    grads = shape(27, CHANNELS, CHANNELS, dtype=F32)
    block = pltpu.VMEM(grads.shape, F32)
    scratch = [pltpu.VMEM(packed_rows, F32), block, block]
    scratch += [pltpu.SemaphoreType.DMA((2, 3)), pltpu.SemaphoreType.DMA]
    grad_one, grad_two, fine = call(
        unpack_kernel, (grads, grads, shape(*fine.shape)), scratch, inputs=2, out=pl.ANY
    )(gathered, fine)
    return (fine, grad_one, grad_two)


def solution(mesh):
    return jax.shard_map(
        body,
        mesh=mesh,
        in_specs=(
            P("dp", "space", None),
            P("dp", None),
            P("dp", "space", None),
            P("dp", "space", None, None, None),
            P(),
            P(),
            P(),
        ),
        out_specs=(P("dp", "space", None, None, None), P(), P()),
        check_vma=False,
    )
```

```python
import functools
import math

import jax
import jax.numpy as jnp
from jax import lax
from jax.experimental import pallas as pl
from jax.experimental.pallas import tpu as pltpu
from jax.sharding import PartitionSpec as P

BF16 = jnp.bfloat16
F32 = jnp.float32
EDGE = 8
CHANNELS = 32
LINE = EDGE * CHANNELS
HALF = LINE // 2
WIDE = 2 * HALF
BRICKS = 2
CUBE = EDGE * EDGE
LINES = BRICKS * CUBE
BAND = (9, WIDE, HALF)
ROWS = 2 * LINES
FACE = 3 * EDGE
GROUPS = 7


def dot(left, right):
    return jnp.dot(left, right, preferred_element_type=F32)


def dot_rows(left, right):
    return lax.dot_general(left, right, (((0,), (0,)), ((), ())), preferred_element_type=F32)


def pair(halves_ref, start, count, stride=1):
    index = pl.ds(start, count, stride=stride) if stride > 1 else pl.ds(start, count)
    return halves_ref[0, index, :], halves_ref[1, index, :]


def lanes_of(shape):
    return lax.broadcasted_iota(jnp.int32, shape, len(shape) - 1)


def first_half(split):
    return lax.axis_index("dp") if split else 0


def pick_kernel(split, ids_hbm, latents_hbm, out_ref, ids_ref, latents_ref, rows_ref, blocks_ref, sems):
    ids_copy = pltpu.make_async_copy(ids_hbm, ids_ref, sems.at[0])
    latents_copy = pltpu.make_async_copy(latents_hbm, latents_ref, sems.at[1])
    ids_copy.start()
    latents_copy.start()
    held, width = latents_ref.shape[1:]
    bricks = ids_ref.shape[1]
    tiles = width // 256
    margin = 8 * tiles
    empty = jnp.zeros((margin, 128), F32)
    for half in range(2):
        rows_ref[half, 0:margin] = empty
        rows_ref[half, margin + bricks * tiles :] = empty
    first = lax.axis_index("space") * held
    rows = lax.broadcasted_iota(jnp.int32, (held, bricks), 0) + first
    ids_copy.wait()
    hot = jnp.where(rows == ids_ref[...], 1.0, 0.0).astype(BF16)
    latents_copy.wait()
    picked = dot_rows(hot, latents_ref[0])
    for tile in range(2 * tiles):
        place = pl.ds(margin + tile % tiles, bricks, stride=tiles)
        rows_ref[tile // tiles, place, :] = picked[:, tile * 128 : tile * 128 + 128]
    count = 3 * BRICKS * tiles
    straight = first_half(split) == 0
    for receiver in range(blocks_ref.shape[0] // (2 * count)):
        start = margin + BRICKS * (receiver - 1) * tiles
        halves = [rows_ref[half, start : start + count] for half in range(2)]
        for half in range(2):
            block = jnp.where(straight, halves[half], halves[1 - half]) if split else halves[half]
            place = (2 * receiver + half) * count
            blocks_ref[place : place + count] = block
    out_ref[...] = blocks_ref[...].astype(BF16)


def relay_kernel(split, received_ref, own_out, other_out, rows_ref):
    rows_ref[...] = received_ref[...].astype(F32)
    count = own_out.shape[0] * 3 // 4
    sums = []
    for half in range(2):
        total = None
        for start in range(half * count, rows_ref.shape[0], 2 * count):
            piece = rows_ref[start : start + count]
            total = piece if total is None else total + piece
        sums.append(jnp.concatenate([total, jnp.zeros((count // 3, 128), F32)], axis=0))
    straight = first_half(split) == 0
    own_out[...] = jnp.where(straight, sums[0], sums[1]).astype(BF16)
    other_out[...] = jnp.where(straight, sums[1], sums[0]).astype(BF16)


def build_band(band_ref, rows):
    shape = (3 * CHANNELS, HALF)
    row = lax.broadcasted_iota(jnp.int32, shape, 0)
    target = CHANNELS - (row // CHANNELS) * CHANNELS + row % CHANNELS
    distance = lanes_of(shape) - target
    band_ref[:, HALF:, :] = jnp.zeros((9, HALF, HALF), BF16)
    for z in range(-1, 5):
        select = jnp.where(distance == z * CHANNELS, 1.0, 0.0).astype(BF16)
        block = dot(rows, select).astype(BF16)
        start = z % 8 * CHANNELS
        band_ref[:, start : start + CHANNELS, :] = block.reshape(9, CHANNELS, HALF)


def weight_rows(weights):
    cube = weights.reshape(9, 3, CHANNELS, CHANNELS)
    rows = jnp.concatenate([cube[:, 0], cube[:, 1], cube[:, 2]], axis=-1)
    return rows.reshape(9 * CHANNELS, 3 * CHANNELS).astype(BF16)


def flipped_rows(weights):
    cube = jnp.swapaxes(weights, 1, 2).reshape(9, 3, CHANNELS, CHANNELS)
    pieces = [jnp.concatenate([cube[8 - k, 2], cube[8 - k, 1], cube[8 - k, 0]], axis=-1) for k in range(9)]
    return jnp.concatenate(pieces, axis=0).astype(BF16)


def band_kernel(weights_ref, band_ref):
    build_band(band_ref, weight_rows(weights_ref[...].astype(F32)))


def masks_kernel(links_in, one_ref, two_ref, band_ref, back_ref, masks_ref, links_ref, links_sem):
    links_copy = pltpu.make_async_copy(links_in, links_ref, links_sem)
    links_copy.start()
    build_band(band_ref, weight_rows(one_ref[...].astype(F32)))
    build_band(back_ref, flipped_rows(two_ref[...].astype(F32)))
    links_copy.wait()
    put_masks(masks_ref, links_ref)


def put_padded(pad_ref, brick, lines, x_low, x_high, y_low, y_high, z_low, z_high):
    def joined(halves, before, after):
        lane = lanes_of(halves[0].shape)
        first = jnp.where(lane < CHANNELS, halves[1], before)
        second = jnp.where(lane >= HALF - CHANNELS, halves[0], after)
        return jnp.concatenate([halves[0], first], axis=-1), jnp.concatenate([halves[1], second], axis=-1)

    inside = joined(lines, z_low, z_high)
    x_low, x_high, y_low, y_high = [joined(face, 0.0, 0.0) for face in (x_low, x_high, y_low, y_high)]
    none = jnp.zeros((1, WIDE), F32)
    shifted = [[], [], []]
    for half in range(2):
        slabs = jnp.concatenate([x_low[half][None], inside[half], x_high[half][None]], axis=0)
        row = lax.broadcasted_iota(jnp.int32, slabs.shape, 1)
        low = jnp.concatenate([none, y_low[half], none], axis=0)[:, None, :]
        high = jnp.concatenate([none, y_high[half], none], axis=0)[:, None, :]
        shifted[0].append(jnp.where(row == 0, low, pltpu.roll(slabs, 1, 1)))
        shifted[1].append(slabs)
        shifted[2].append(jnp.where(row == EDGE - 1, high, pltpu.roll(slabs, EDGE - 1, 1)))
    for dy in range(3):
        pad_ref[dy, brick] = jnp.concatenate(shifted[dy], axis=1).astype(BF16)


def window(pad_ref, k):
    return pad_ref[k % 3, :, k // 3 : k // 3 + EDGE].reshape(ROWS, WIDE)


def convolve(pad_ref, band_ref):
    both, last = None, None
    for dy in range(3):
        slabs = pad_ref[dy, :, : EDGE + 1].reshape(-1, WIDE)
        term = dot(slabs, jnp.concatenate([band_ref[dy], band_ref[3 + dy]], axis=1))
        both = term if both is None else both + term
        term = dot(window(pad_ref, 6 + dy), band_ref[6 + dy])
        last = term if last is None else last + term
    both = both.reshape(BRICKS, EDGE + 1, 2 * EDGE, 2 * HALF)
    total = both[:, :EDGE, :, :HALF] + both[:, 1:, :, HALF:]
    return total.reshape(ROWS, HALF) + last


def half_lines(values):
    cube = values.reshape(BRICKS, EDGE, 2, EDGE, HALF)
    return [(cube[brick, :, 0], cube[brick, :, 1]) for brick in range(BRICKS)]


def put_halves(halves_ref, start, bricks):
    for brick, lines in enumerate(bricks):
        for half in range(2):
            first = start + brick * CUBE
            halves_ref[half, first : first + CUBE, :] = lines[half].reshape(CUBE, HALF)


def cotangent_lines(cotangent_ref):
    cube = cotangent_ref[...].astype(F32).reshape(BRICKS, EDGE, EDGE, LINE)
    return [(cube[brick, :, :, :HALF], cube[brick, :, :, HALF:]) for brick in range(BRICKS)]


def pack_faces(faces_ref, base, halves_ref, start, high):
    x_face = pair(halves_ref, start + ((EDGE - 1) * EDGE if high else 0), EDGE)
    y_face = pair(halves_ref, start + (EDGE - 1 if high else 0), EDGE, EDGE)
    for half in range(2):
        lanes = slice(half * HALF, half * HALF + HALF)
        faces_ref[base : base + EDGE, lanes] = x_face[half]
        faces_ref[base + EDGE : base + 2 * EDGE, lanes] = y_face[half]
    tile = halves_ref[1 if high else 0, start : start + CUBE, :]
    lane = lanes_of((16, 128)) // CHANNELS
    packed = jnp.zeros((16, 128), F32)
    for part in range(4):
        shift = (part + 1 if high else part) % 4 * CHANNELS
        piece = tile[part * 16 : part * 16 + 16]
        packed = jnp.where(lane == part, pltpu.roll(piece, shift, 1) if shift else piece, packed)
    faces_ref[base + 2 * EDGE : base + FACE, :128] = packed[:8]
    faces_ref[base + 2 * EDGE : base + FACE, 128:] = packed[8:]


def pack_all(bricks, halves_ref, faces_ref, high_out, low_out):
    put_halves(halves_ref, 0, bricks)
    for high, out_ref in ((True, high_out), (False, low_out)):
        for brick in range(BRICKS):
            pack_faces(faces_ref, brick * FACE, halves_ref, brick * CUBE, high)
        out_ref[...] = faces_ref[...].astype(BF16)


def to_partners(high_ref, low_ref, far_out, near_out):
    even = lax.axis_index("space") % 2 == 0
    far_out[...] = jnp.where(even, low_ref[...], high_ref[...])
    near_out[...] = jnp.where(even, high_ref[...], low_ref[...])


def faces_kernel(cotangent_ref, high_out, low_out, far_out, near_out, halves_ref, faces_ref):
    pack_all(cotangent_lines(cotangent_ref), halves_ref, faces_ref, high_out, low_out)
    to_partners(high_out, low_out, far_out, near_out)


def unpack_depth(halves, high):
    packed = jnp.concatenate(halves, axis=0)
    pieces = []
    for part in range(4):
        shift = ((3 - part) if high else (4 - part)) % 4 * CHANNELS
        pieces.append(pltpu.roll(packed, shift, 1) if shift else packed)
    return jnp.concatenate(pieces, axis=0).reshape(EDGE, EDGE, 128)


def first_kernel(
    links_in, own_ref, other_ref, up_ref, band_ref,
    slope_out, hidden_out, turned_out, pad_out,
    volumes_ref, rows_ref, links_ref, links_sem,
):
    links_copy = pltpu.make_async_copy(links_in, links_ref, links_sem)
    links_copy.start()
    position = lax.axis_index("space")
    cells = []
    for half, half_ref in enumerate((own_ref, other_ref)):
        tiles = half_ref.shape[0] // 8
        rows_ref[half] = half_ref[...].astype(F32)
        for tile in range(tiles):
            rows = rows_ref[half, pl.ds(tile, 8, stride=tiles), :]
            cells += [rows[:, :64], rows[:, 64:]]
    lifted = dot(jnp.concatenate(cells, axis=0).astype(BF16), up_ref[...])
    lifted = lifted.astype(BF16).astype(F32)
    for cell in range(8):
        a, b, c = cell // 4, cell // 2 % 2, cell % 2
        for sub in range(16):
            line = (4 * a + sub // 4) * EDGE + 4 * b + sub % 4
            volumes_ref[c, line * 8 : line * 8 + 8, :] = lifted[
                cell * 8 : cell * 8 + 8, sub * 128 : sub * 128 + 128
            ]
    links_copy.wait()
    for brick in range(BRICKS):

        def near(face):
            link = links_ref[0, brick, face]
            index = jnp.clip(link - BRICKS * (position - 1), 0, 3 * BRICKS - 1)
            return index, jnp.where(link >= 0, 1.0, 0.0).astype(F32)

        def x_face(face):
            index, present = near(face)
            line = EDGE * (EDGE - 1) if face % 2 == 0 else 0
            return [half * present for half in pair(volumes_ref, line * 8 + index, EDGE, 8)]

        def y_face(face):
            index, present = near(face)
            line = EDGE - 1 if face % 2 == 0 else 0
            return [half * present for half in pair(volumes_ref, line * 8 + index, EDGE, 8 * EDGE)]

        def z_face(face):
            index, present = near(face)
            tile = volumes_ref[1 if face % 2 == 0 else 0, pl.ds(index, CUBE, stride=8), :] * present
            return tile.reshape(EDGE, EDGE, HALF)

        own = [half.reshape(EDGE, EDGE, HALF) for half in pair(volumes_ref, BRICKS + brick, CUBE, 8)]
        put_padded(pad_out, brick, own, x_face(0), x_face(1), y_face(2), y_face(3), z_face(4), z_face(5))
    pre = convolve(pad_out, band_ref)
    sigmoid = 1.0 / (1.0 + jnp.exp(-pre))
    hidden = (pre / (1.0 + jnp.exp(-pre))).astype(BF16)
    slope_out[...] = sigmoid * (1.0 + pre * (1.0 - sigmoid))
    hidden_out[...] = hidden
    hidden = hidden.astype(F32)
    turned_out[...] = jnp.transpose(hidden).astype(BF16)


def hidden_faces_kernel(hidden_ref, _parts, high_out, low_out, far_out, near_out, halves_ref, faces_ref):
    pack_all(half_lines(hidden_ref[...].astype(F32)), halves_ref, faces_ref, high_out, low_out)
    to_partners(high_out, low_out, far_out, near_out)


def picked(outer, places):
    lane = lanes_of((CHANNELS, 128)) // CHANNELS
    found = None
    for block in range(4):
        start, tile = places[block]
        rows = outer[start : start + CHANNELS, tile * 128 : tile * 128 + 128]
        found = rows if found is None else jnp.where(lane == block, rows, found)
    return found


def fold(four):
    lane = lanes_of((CHANNELS, 128)) // CHANNELS
    total = None
    for turn in range(4):
        mixed = four[0]
        for n in range(1, len(four)):
            mixed = jnp.where(lane == (n + turn) % 4, four[n], mixed)
        if turn:
            mixed = pltpu.roll(mixed, 128 - turn * CHANNELS, 1)
        total = mixed if total is None else total + mixed
    return total


def diagonal(shift):
    places = [None] * 4
    for z in range(4):
        other = z + shift
        places[other % 4] = (z * CHANNELS, 0 if 0 <= other < 4 else 1)
    return places


def put_masks(masks_ref, links_ref):
    position = lax.axis_index("space")
    for brick in range(BRICKS):
        for face in range(6):
            first = links_ref[0, brick, face] - BRICKS * (position - 1 if face % 2 == 0 else position)
            for i in range(2 * BRICKS):
                row = (brick * 6 + face) * 2 * BRICKS + i
                masks_ref[row : row + 1, :] = jnp.full((1, 128), jnp.where(first == i, 1.0, 0.0).astype(F32))


def pad_all(pad_ref, bricks, masks_ref, high_pool, low_pool, high_own, low_own, far, near):
    position = lax.axis_index("space")
    half = BRICKS * FACE
    even = position % 2 == 0
    high_pool[0:half] = jnp.where(even, far[...], near[...]).astype(F32)
    high_pool[half:] = high_own[...].astype(F32)
    low_pool[0:half] = low_own[...].astype(F32)
    low_pool[half:] = jnp.where(even, near[...], far[...]).astype(F32)
    for brick, lines in enumerate(bricks):

        def face(number, axis):
            pool = high_pool if number % 2 == 0 else low_pool
            total = [0.0, 0.0]
            for i in range(2 * BRICKS):
                row = (brick * 6 + number) * 2 * BRICKS + i
                mask = masks_ref[row : row + 1, :]
                start = i * FACE + axis * EDGE
                for part in range(2):
                    found = pool[start : start + EDGE, part * HALF : part * HALF + HALF]
                    total[part] = total[part] + found * mask
            return total

        put_padded(
            pad_ref, brick, lines, face(0, 0), face(1, 0), face(2, 1), face(3, 1),
            unpack_depth(face(4, 2), True), unpack_depth(face(5, 2), False),
        )


def second_kernel(
    masks_ref, cotangent_ref, band_ref, slope_ref, hidden_ref, lifted_pad, high_own, low_own, far, near,
    sums_out, lifted_out,
    high_pool, low_pool, cotangent_pad, sums_ref,
):
    lifted_out[...] = window(lifted_pad, 4)[:, :HALF]
    bricks = cotangent_lines(cotangent_ref)
    pad_all(cotangent_pad, bricks, masks_ref, high_pool, low_pool, high_own, low_own, far, near)
    gradient = (convolve(cotangent_pad, band_ref) * slope_ref[...]).astype(BF16)
    gradient = jnp.transpose(gradient.astype(F32)).astype(BF16)
    hidden = hidden_ref[...]
    if sums_ref.shape[0] > 2 * GROUPS * CHANNELS:
        rest = sums_ref.shape[0] - 2 * GROUPS * CHANNELS
        sums_ref[2 * GROUPS * CHANNELS :] = jnp.zeros((rest, 128), F32)
    ones, twos = [], []
    for k in range(9):
        one = dot(gradient, window(lifted_pad, k))
        two = dot(hidden, window(cotangent_pad, 8 - k))
        ones += [picked(one, diagonal(part - 1)) for part in range(3)]
        twos += [picked(two, diagonal(1 - part)) for part in range(3)]
        while len(ones) >= 4 or (k == 8 and ones):
            group = (3 * k + 3 - len(ones)) // 4
            for first, blocks in ((0, ones), (GROUPS, twos)):
                start = (first + group) * CHANNELS
                sums_ref[start : start + CHANNELS] = fold(blocks[:4])
            ones, twos = ones[4:], twos[4:]
    sums_out[...] = sums_ref[...].astype(BF16)


def fine_kernel(
    masks_ref, band_ref, lifted_ref, hidden_ref, high_own, low_own, far, near,
    fine_out, high_pool, low_pool, hidden_pad,
):
    bricks = half_lines(hidden_ref[...].astype(F32))
    pad_all(hidden_pad, bricks, masks_ref, high_pool, low_pool, high_own, low_own, far, near)
    fine = lifted_ref[...].astype(F32) + convolve(hidden_pad, band_ref)
    fine = fine.reshape(LINES // EDGE, 2, EDGE, HALF)
    fine = jnp.concatenate([fine[:, 0], fine[:, 1]], axis=-1)
    fine_out[...] = fine.astype(BF16).reshape(fine_out.shape)


def sum_kernel(devices, scale, parts_ref, out_hbm, rows_ref, shares_ref, sems):
    rows_ref[...] = parts_ref[...].astype(F32)
    share = rows_ref.shape[0] // devices
    pieces = [rows_ref[share * i : share * i + share] for i in range(devices)]
    while len(pieces) > 1:
        pairs = [a + b for a, b in zip(pieces[::2], pieces[1::2])]
        pieces = pairs + pieces[len(pieces) - len(pieces) % 2 :]
    total = pieces[0] * scale
    some = shares_ref.shape[0]
    for i in range(some // share):
        rows_ref[share * i : share * i + share] = total
    shares_ref[...] = rows_ref[0:some].astype(BF16)
    copies = []
    for i in range(out_hbm.shape[0] // some):
        copies.append(pltpu.make_async_copy(shares_ref, out_hbm.at[pl.ds(some * i, some)], sems.at[i]))
        copies[-1].start()
    for copy in copies:
        copy.wait()


def unpack_kernel(sums_ref, fine_ref, one_out, two_out, fine_out, rows_ref, one_ref, two_ref, sems, fine_sem):
    fine_copy = pltpu.make_async_copy(fine_ref, fine_out, fine_sem)
    fine_copy.start()
    rows_ref[...] = sums_ref[...].astype(F32)
    copies = []
    for which, (block_ref, out) in ((1, (two_ref, two_out)), (0, (one_ref, one_out))):
        for part, (first, last) in enumerate(((0, 2), (2, 4), (4, GROUPS))):
            for group in range(first, last):
                start = (which * GROUPS + group) * CHANNELS
                four = rows_ref[start : start + CHANNELS]
                turned = None if which else jnp.transpose(four)
                for n in range(min(4, 27 - 4 * group)):
                    if which:
                        block = pltpu.roll(four, 128 - n * CHANNELS, 1) if n else four
                        block_ref[4 * group + n] = block[:, :CHANNELS]
                    else:
                        block_ref[4 * group + n] = turned[CHANNELS * n : CHANNELS * n + CHANNELS]
            span = pl.ds(4 * first, min(4 * last, 27) - 4 * first)
            copies.append(pltpu.make_async_copy(block_ref.at[span], out.at[span], sems.at[which, part]))
            copies[-1].start()
    for copy in copies:
        copy.wait()
    fine_copy.wait()


def call(kernel, out_shape, scratch=(), hbm=(), inputs=1, limit=24, cost=None, out=pltpu.VMEM):
    spaces = [pl.ANY if i in hbm else pltpu.VMEM for i in range(inputs)]
    return pl.pallas_call(
        kernel,
        out_shape=out_shape,
        in_specs=[pl.BlockSpec(memory_space=space) for space in spaces],
        out_specs=jax.tree.map(lambda _: pl.BlockSpec(memory_space=out), out_shape),
        scratch_shapes=list(scratch),
        compiler_params=pltpu.CompilerParams(vmem_limit_bytes=limit * 2**20),
        cost_estimate=cost,
    )


def shape(*dims, dtype=BF16):
    return jax.ShapeDtypeStruct(dims, dtype)


def swapped(value, first):
    pairs = [(i, i + 1) for i in range(first, lax.axis_size("space") - 1, 2)]
    return lax.ppermute(value, "space", pairs + [(target, source) for source, target in pairs])


def exchanged(rows, axes=("space", "dp")):
    count = math.prod(lax.axis_size(axis) for axis in axes)
    shares = rows.reshape(count, -1, 2, 128)
    shares = lax.all_to_all(shares, axes, split_axis=0, concat_axis=0, tiled=True)
    return shares.reshape(rows.shape)


def body(coarse_latents, active_blocks, face_links, cotangent, up_weight, conv_one, conv_two):
    devices = lax.axis_size("space")
    everyone = devices * lax.axis_size("dp")
    held, width = coarse_latents.shape[1:]
    bricks = active_blocks.shape[1]
    split = lax.axis_size("dp") == 2
    tiles = width // 256
    count = 3 * BRICKS * tiles
    blocks = (2 * devices * count, 128)
    packed = call(
        functools.partial(pick_kernel, split),
        shape(*blocks),
        [
            pltpu.VMEM((1, bricks), jnp.int32),
            pltpu.VMEM((1, held, width), BF16),
            pltpu.VMEM((2, (bricks + 16) * tiles, 128), F32),
            pltpu.VMEM(blocks, F32),
            pltpu.SemaphoreType.DMA((2,)),
        ],
        hbm=(0, 1),
        inputs=2,
        limit=60,
    )(active_blocks, coarse_latents)
    received = exchanged(packed, ("space", "dp") if split else ("space",))
    window_half = shape(8 * tiles, 128)
    own, other = call(
        functools.partial(relay_kernel, split), (window_half, window_half), [pltpu.VMEM(blocks, F32)]
    )(received)
    if split:
        other = lax.ppermute(other, "dp", [(0, 1), (1, 0)])
    cost = pl.CostEstimate(flops=10**9, bytes_accessed=2 * 10**6, transcendentals=0)
    face = shape(BRICKS * FACE, LINE)
    halves = pltpu.VMEM((2, LINES, HALF), F32)
    faces = pltpu.VMEM((BRICKS * FACE, LINE), F32)
    pool = pltpu.VMEM((2 * BRICKS * FACE, LINE), F32)
    volume = shape(ROWS, HALF)
    links = [pltpu.SMEM(face_links.shape, jnp.int32), pltpu.SemaphoreType.DMA]
    pad_shape = (3, BRICKS, EDGE + 2, 2 * EDGE, WIDE)
    pad = pltpu.VMEM(pad_shape, BF16)
    high, low, far, near = call(faces_kernel, (face,) * 4, [halves, faces])(cotangent)
    far = swapped(far, 1)
    near = swapped(near, 0)
    masks = shape(BRICKS * 6 * 2 * BRICKS, 128, dtype=F32)
    band_one, band_back, masks = call(
        masks_kernel, (shape(*BAND), shape(*BAND), masks), links, hbm=(0,), inputs=3, cost=cost
    )(face_links, conv_one, conv_two)
    slope, hidden, turned, lifted_pad = call(
        first_kernel,
        (
            shape(ROWS, HALF, dtype=F32), volume, shape(HALF, ROWS), shape(*pad_shape),
        ),
        [pltpu.VMEM((2, 8 * CUBE, 128), F32), pltpu.VMEM((2, 8 * tiles, 128), F32), *links],
        hbm=(0,),
        inputs=5,
    )(face_links, own, other, up_weight, band_one)
    share = 2 * -(-GROUPS * CHANNELS // everyone)
    packed_rows = (everyone * share, 128)
    sums, lifted = call(
        second_kernel,
        (shape(*packed_rows), volume),
        [pool, pool, pad, pltpu.VMEM(packed_rows, F32)],
        inputs=10,
    )(masks, cotangent, band_back, slope, turned, lifted_pad, high, low, far, near)
    parts = exchanged(sums)
    hidden_high, hidden_low, hidden_far, hidden_near = call(
        hidden_faces_kernel, (face,) * 4, [halves, faces], hbm=(1,), inputs=2
    )(hidden, parts)
    hidden_far = swapped(hidden_far, 1)
    hidden_near = swapped(hidden_near, 0)
    band_two = call(band_kernel, shape(*BAND), cost=cost)(conv_two)
    fine = call(fine_kernel, shape(*cotangent.shape), [pool, pool, pad], inputs=8, cost=cost)(
        masks, band_two, lifted, hidden, hidden_high, hidden_low, hidden_far, hidden_near
    )
    scale = 1.0 / math.sqrt(lax.axis_size("dp") * devices * BRICKS * EDGE**3)
    times = 4 if everyone % 32 == 0 else 1
    total = call(
        functools.partial(sum_kernel, everyone, scale),
        shape(*packed_rows),
        [
            pltpu.VMEM(packed_rows, F32),
            pltpu.VMEM((packed_rows[0] // times, 128), BF16),
            pltpu.SemaphoreType.DMA((times,)),
        ],
        out=pl.ANY,
    )(parts)
    gathered = exchanged(total)
    grads = shape(27, CHANNELS, CHANNELS, dtype=F32)
    block = pltpu.VMEM(grads.shape, F32)
    scratch = [pltpu.VMEM(packed_rows, F32), block, block]
    scratch += [pltpu.SemaphoreType.DMA((2, 3)), pltpu.SemaphoreType.DMA]
    grad_one, grad_two, fine = call(
        unpack_kernel, (grads, grads, shape(*fine.shape)), scratch, inputs=2, out=pl.ANY
    )(gathered, fine)
    return (fine, grad_one, grad_two)


def solution(mesh):
    return jax.shard_map(
        body,
        mesh=mesh,
        in_specs=(
            P("dp", "space", None),
            P("dp", None),
            P("dp", "space", None),
            P("dp", "space", None, None, None),
            P(),
            P(),
            P(),
        ),
        out_specs=(P("dp", "space", None, None, None), P(), P()),
        check_vma=False,
    )
```

```python
import functools
import math

import jax
import jax.numpy as jnp
from jax import lax
from jax.experimental import pallas as pl
from jax.experimental.pallas import tpu as pltpu
from jax.sharding import PartitionSpec as P

BF16 = jnp.bfloat16
F32 = jnp.float32
EDGE = 8
CHANNELS = 32
LINE = EDGE * CHANNELS
HALF = LINE // 2
WIDE = 2 * HALF
BRICKS = 2
CUBE = EDGE * EDGE
LINES = BRICKS * CUBE
BAND = (9, WIDE, HALF)
ROWS = 2 * LINES
FACE = 3 * EDGE
GROUPS = 7


def dot(left, right):
    return jnp.dot(left, right, preferred_element_type=F32)


def dot_rows(left, right):
    return lax.dot_general(left, right, (((0,), (0,)), ((), ())), preferred_element_type=F32)


def pair(halves_ref, start, count, stride=1):
    index = pl.ds(start, count, stride=stride) if stride > 1 else pl.ds(start, count)
    return halves_ref[0, index, :], halves_ref[1, index, :]


def lanes_of(shape):
    return lax.broadcasted_iota(jnp.int32, shape, len(shape) - 1)


def first_half(split):
    return lax.axis_index("dp") if split else 0


def pick_kernel(split, ids_hbm, latents_hbm, out_ref, ids_ref, latents_ref, rows_ref, blocks_ref, sems):
    ids_copy = pltpu.make_async_copy(ids_hbm, ids_ref, sems.at[0])
    latents_copy = pltpu.make_async_copy(latents_hbm, latents_ref, sems.at[1])
    ids_copy.start()
    latents_copy.start()
    held, width = latents_ref.shape[1:]
    bricks = ids_ref.shape[1]
    tiles = width // 256
    margin = 8 * tiles
    empty = jnp.zeros((margin, 128), F32)
    for half in range(2):
        rows_ref[half, 0:margin] = empty
        rows_ref[half, margin + bricks * tiles :] = empty
    first = lax.axis_index("space") * held
    rows = lax.broadcasted_iota(jnp.int32, (held, bricks), 0) + first
    ids_copy.wait()
    hot = jnp.where(rows == ids_ref[...], 1.0, 0.0).astype(BF16)
    latents_copy.wait()
    picked = dot_rows(hot, latents_ref[0])
    for tile in range(2 * tiles):
        place = pl.ds(margin + tile % tiles, bricks, stride=tiles)
        rows_ref[tile // tiles, place, :] = picked[:, tile * 128 : tile * 128 + 128]
    count = 3 * BRICKS * tiles
    straight = first_half(split) == 0
    for receiver in range(blocks_ref.shape[0] // (2 * count)):
        start = margin + BRICKS * (receiver - 1) * tiles
        halves = [rows_ref[half, start : start + count] for half in range(2)]
        for half in range(2):
            block = jnp.where(straight, halves[half], halves[1 - half]) if split else halves[half]
            place = (2 * receiver + half) * count
            blocks_ref[place : place + count] = block
    out_ref[...] = blocks_ref[...].astype(BF16)


def relay_kernel(split, received_ref, _masks, own_out, other_out, rows_ref):
    rows_ref[...] = received_ref[...].astype(F32)
    count = own_out.shape[0] * 3 // 4
    sums = []
    for half in range(2):
        total = None
        for start in range(half * count, rows_ref.shape[0], 2 * count):
            piece = rows_ref[start : start + count]
            total = piece if total is None else total + piece
        sums.append(jnp.concatenate([total, jnp.zeros((count // 3, 128), F32)], axis=0))
    straight = first_half(split) == 0
    own_out[...] = jnp.where(straight, sums[0], sums[1]).astype(BF16)
    other_out[...] = jnp.where(straight, sums[1], sums[0]).astype(BF16)


def build_band(band_ref, rows):
    shape = (3 * CHANNELS, HALF)
    row = lax.broadcasted_iota(jnp.int32, shape, 0)
    target = CHANNELS - (row // CHANNELS) * CHANNELS + row % CHANNELS
    distance = lanes_of(shape) - target
    band_ref[:, HALF:, :] = jnp.zeros((9, HALF, HALF), BF16)
    for z in range(-1, 5):
        select = jnp.where(distance == z * CHANNELS, 1.0, 0.0).astype(BF16)
        block = dot(rows, select).astype(BF16)
        start = z % 8 * CHANNELS
        band_ref[:, start : start + CHANNELS, :] = block.reshape(9, CHANNELS, HALF)


def weight_rows(weights):
    cube = weights.reshape(9, 3, CHANNELS, CHANNELS)
    rows = jnp.concatenate([cube[:, 0], cube[:, 1], cube[:, 2]], axis=-1)
    return rows.reshape(9 * CHANNELS, 3 * CHANNELS).astype(BF16)


def flipped_rows(weights):
    cube = jnp.swapaxes(weights, 1, 2).reshape(9, 3, CHANNELS, CHANNELS)
    pieces = [jnp.concatenate([cube[8 - k, 2], cube[8 - k, 1], cube[8 - k, 0]], axis=-1) for k in range(9)]
    return jnp.concatenate(pieces, axis=0).astype(BF16)


def band_kernel(weights_ref, band_ref):
    build_band(band_ref, weight_rows(weights_ref[...].astype(F32)))


def masks_kernel(links_in, one_ref, two_ref, band_ref, back_ref, masks_ref, links_ref, links_sem):
    links_copy = pltpu.make_async_copy(links_in, links_ref, links_sem)
    links_copy.start()
    build_band(band_ref, weight_rows(one_ref[...].astype(F32)))
    build_band(back_ref, flipped_rows(two_ref[...].astype(F32)))
    links_copy.wait()
    put_masks(masks_ref, links_ref)


def put_padded(pad_ref, brick, lines, x_low, x_high, y_low, y_high, z_low, z_high):
    def joined(halves, before, after):
        lane = lanes_of(halves[0].shape)
        first = jnp.where(lane < CHANNELS, halves[1], before)
        second = jnp.where(lane >= HALF - CHANNELS, halves[0], after)
        return jnp.concatenate([halves[0], first], axis=-1), jnp.concatenate([halves[1], second], axis=-1)

    inside = joined(lines, z_low, z_high)
    x_low, x_high, y_low, y_high = [joined(face, 0.0, 0.0) for face in (x_low, x_high, y_low, y_high)]
    none = jnp.zeros((1, WIDE), F32)
    shifted = [[], [], []]
    for half in range(2):
        slabs = jnp.concatenate([x_low[half][None], inside[half], x_high[half][None]], axis=0)
        row = lax.broadcasted_iota(jnp.int32, slabs.shape, 1)
        low = jnp.concatenate([none, y_low[half], none], axis=0)[:, None, :]
        high = jnp.concatenate([none, y_high[half], none], axis=0)[:, None, :]
        shifted[0].append(jnp.where(row == 0, low, pltpu.roll(slabs, 1, 1)))
        shifted[1].append(slabs)
        shifted[2].append(jnp.where(row == EDGE - 1, high, pltpu.roll(slabs, EDGE - 1, 1)))
    for dy in range(3):
        pad_ref[dy, brick] = jnp.concatenate(shifted[dy], axis=1).astype(BF16)


def window(pad_ref, k):
    return pad_ref[k % 3, :, k // 3 : k // 3 + EDGE].reshape(ROWS, WIDE)


def convolve(pad_ref, band_ref):
    both, last = None, None
    for dy in range(3):
        slabs = pad_ref[dy, :, : EDGE + 1].reshape(-1, WIDE)
        term = dot(slabs, jnp.concatenate([band_ref[dy], band_ref[3 + dy]], axis=1))
        both = term if both is None else both + term
        term = dot(window(pad_ref, 6 + dy), band_ref[6 + dy])
        last = term if last is None else last + term
    both = both.reshape(BRICKS, EDGE + 1, 2 * EDGE, 2 * HALF)
    total = both[:, :EDGE, :, :HALF] + both[:, 1:, :, HALF:]
    return total.reshape(ROWS, HALF) + last


def half_lines(values):
    cube = values.reshape(BRICKS, EDGE, 2, EDGE, HALF)
    return [(cube[brick, :, 0], cube[brick, :, 1]) for brick in range(BRICKS)]


def put_halves(halves_ref, start, bricks):
    for brick, lines in enumerate(bricks):
        for half in range(2):
            first = start + brick * CUBE
            halves_ref[half, first : first + CUBE, :] = lines[half].reshape(CUBE, HALF)


def cotangent_lines(cotangent_ref):
    cube = cotangent_ref[...].astype(F32).reshape(BRICKS, EDGE, EDGE, LINE)
    return [(cube[brick, :, :, :HALF], cube[brick, :, :, HALF:]) for brick in range(BRICKS)]


def pack_faces(faces_ref, base, halves_ref, start, high):
    x_face = pair(halves_ref, start + ((EDGE - 1) * EDGE if high else 0), EDGE)
    y_face = pair(halves_ref, start + (EDGE - 1 if high else 0), EDGE, EDGE)
    for half in range(2):
        lanes = slice(half * HALF, half * HALF + HALF)
        faces_ref[base : base + EDGE, lanes] = x_face[half]
        faces_ref[base + EDGE : base + 2 * EDGE, lanes] = y_face[half]
    tile = halves_ref[1 if high else 0, start : start + CUBE, :]
    lane = lanes_of((16, 128)) // CHANNELS
    packed = jnp.zeros((16, 128), F32)
    for part in range(4):
        shift = (part + 1 if high else part) % 4 * CHANNELS
        piece = tile[part * 16 : part * 16 + 16]
        packed = jnp.where(lane == part, pltpu.roll(piece, shift, 1) if shift else piece, packed)
    faces_ref[base + 2 * EDGE : base + FACE, :128] = packed[:8]
    faces_ref[base + 2 * EDGE : base + FACE, 128:] = packed[8:]


def pack_all(bricks, halves_ref, faces_ref, high_out, low_out):
    put_halves(halves_ref, 0, bricks)
    for high, out_ref in ((True, high_out), (False, low_out)):
        for brick in range(BRICKS):
            pack_faces(faces_ref, brick * FACE, halves_ref, brick * CUBE, high)
        out_ref[...] = faces_ref[...].astype(BF16)


def to_partners(high_ref, low_ref, far_out, near_out):
    even = lax.axis_index("space") % 2 == 0
    far_out[...] = jnp.where(even, low_ref[...], high_ref[...])
    near_out[...] = jnp.where(even, high_ref[...], low_ref[...])


def faces_kernel(cotangent_ref, high_out, low_out, far_out, near_out, halves_ref, faces_ref):
    pack_all(cotangent_lines(cotangent_ref), halves_ref, faces_ref, high_out, low_out)
    to_partners(high_out, low_out, far_out, near_out)


def unpack_depth(halves, high):
    packed = jnp.concatenate(halves, axis=0)
    pieces = []
    for part in range(4):
        shift = ((3 - part) if high else (4 - part)) % 4 * CHANNELS
        pieces.append(pltpu.roll(packed, shift, 1) if shift else packed)
    return jnp.concatenate(pieces, axis=0).reshape(EDGE, EDGE, 128)


def first_kernel(
    links_in, own_ref, other_ref, up_ref, band_ref,
    slope_out, hidden_out, turned_out, pad_out,
    volumes_ref, rows_ref, links_ref, links_sem,
):
    links_copy = pltpu.make_async_copy(links_in, links_ref, links_sem)
    links_copy.start()
    position = lax.axis_index("space")
    cells = []
    for half, half_ref in enumerate((own_ref, other_ref)):
        tiles = half_ref.shape[0] // 8
        rows_ref[half] = half_ref[...].astype(F32)
        for tile in range(tiles):
            rows = rows_ref[half, pl.ds(tile, 8, stride=tiles), :]
            cells += [rows[:, :64], rows[:, 64:]]
    lifted = dot(jnp.concatenate(cells, axis=0).astype(BF16), up_ref[...])
    lifted = lifted.astype(BF16).astype(F32)
    for cell in range(8):
        a, b, c = cell // 4, cell // 2 % 2, cell % 2
        for sub in range(16):
            line = (4 * a + sub // 4) * EDGE + 4 * b + sub % 4
            volumes_ref[c, line * 8 : line * 8 + 8, :] = lifted[
                cell * 8 : cell * 8 + 8, sub * 128 : sub * 128 + 128
            ]
    links_copy.wait()
    for brick in range(BRICKS):

        def near(face):
            link = links_ref[0, brick, face]
            index = jnp.clip(link - BRICKS * (position - 1), 0, 3 * BRICKS - 1)
            return index, jnp.where(link >= 0, 1.0, 0.0).astype(F32)

        def x_face(face):
            index, present = near(face)
            line = EDGE * (EDGE - 1) if face % 2 == 0 else 0
            return [half * present for half in pair(volumes_ref, line * 8 + index, EDGE, 8)]

        def y_face(face):
            index, present = near(face)
            line = EDGE - 1 if face % 2 == 0 else 0
            return [half * present for half in pair(volumes_ref, line * 8 + index, EDGE, 8 * EDGE)]

        def z_face(face):
            index, present = near(face)
            tile = volumes_ref[1 if face % 2 == 0 else 0, pl.ds(index, CUBE, stride=8), :] * present
            return tile.reshape(EDGE, EDGE, HALF)

        own = [half.reshape(EDGE, EDGE, HALF) for half in pair(volumes_ref, BRICKS + brick, CUBE, 8)]
        put_padded(pad_out, brick, own, x_face(0), x_face(1), y_face(2), y_face(3), z_face(4), z_face(5))
    pre = convolve(pad_out, band_ref)
    sigmoid = 1.0 / (1.0 + jnp.exp(-pre))
    hidden = (pre / (1.0 + jnp.exp(-pre))).astype(BF16)
    slope_out[...] = sigmoid * (1.0 + pre * (1.0 - sigmoid))
    hidden_out[...] = hidden
    hidden = hidden.astype(F32)
    turned_out[...] = jnp.transpose(hidden).astype(BF16)


def hidden_faces_kernel(hidden_ref, _parts, high_out, low_out, far_out, near_out, halves_ref, faces_ref):
    pack_all(half_lines(hidden_ref[...].astype(F32)), halves_ref, faces_ref, high_out, low_out)
    to_partners(high_out, low_out, far_out, near_out)


def picked(outer, places):
    lane = lanes_of((CHANNELS, 128)) // CHANNELS
    found = None
    for block in range(4):
        start, tile = places[block]
        rows = outer[start : start + CHANNELS, tile * 128 : tile * 128 + 128]
        found = rows if found is None else jnp.where(lane == block, rows, found)
    return found


def fold(four):
    lane = lanes_of((CHANNELS, 128)) // CHANNELS
    total = None
    for turn in range(4):
        mixed = four[0]
        for n in range(1, len(four)):
            mixed = jnp.where(lane == (n + turn) % 4, four[n], mixed)
        if turn:
            mixed = pltpu.roll(mixed, 128 - turn * CHANNELS, 1)
        total = mixed if total is None else total + mixed
    return total


def diagonal(shift):
    places = [None] * 4
    for z in range(4):
        other = z + shift
        places[other % 4] = (z * CHANNELS, 0 if 0 <= other < 4 else 1)
    return places


def put_masks(masks_ref, links_ref):
    position = lax.axis_index("space")
    for brick in range(BRICKS):
        for face in range(6):
            first = links_ref[0, brick, face] - BRICKS * (position - 1 if face % 2 == 0 else position)
            for i in range(2 * BRICKS):
                row = (brick * 6 + face) * 2 * BRICKS + i
                masks_ref[row : row + 1, :] = jnp.full((1, 128), jnp.where(first == i, 1.0, 0.0).astype(F32))


def pad_all(pad_ref, bricks, masks_ref, high_pool, low_pool, high_own, low_own, far, near):
    position = lax.axis_index("space")
    half = BRICKS * FACE
    even = position % 2 == 0
    high_pool[0:half] = jnp.where(even, far[...], near[...]).astype(F32)
    high_pool[half:] = high_own[...].astype(F32)
    low_pool[0:half] = low_own[...].astype(F32)
    low_pool[half:] = jnp.where(even, near[...], far[...]).astype(F32)
    for brick, lines in enumerate(bricks):

        def face(number, axis):
            pool = high_pool if number % 2 == 0 else low_pool
            total = [0.0, 0.0]
            for i in range(2 * BRICKS):
                row = (brick * 6 + number) * 2 * BRICKS + i
                mask = masks_ref[row : row + 1, :]
                start = i * FACE + axis * EDGE
                for part in range(2):
                    found = pool[start : start + EDGE, part * HALF : part * HALF + HALF]
                    total[part] = total[part] + found * mask
            return total

        put_padded(
            pad_ref, brick, lines, face(0, 0), face(1, 0), face(2, 1), face(3, 1),
            unpack_depth(face(4, 2), True), unpack_depth(face(5, 2), False),
        )


def second_kernel(
    masks_ref, cotangent_ref, band_ref, slope_ref, hidden_ref, lifted_pad, high_own, low_own, far, near,
    sums_out, lifted_out,
    high_pool, low_pool, cotangent_pad, sums_ref,
):
    lifted_out[...] = window(lifted_pad, 4)[:, :HALF]
    bricks = cotangent_lines(cotangent_ref)
    pad_all(cotangent_pad, bricks, masks_ref, high_pool, low_pool, high_own, low_own, far, near)
    gradient = (convolve(cotangent_pad, band_ref) * slope_ref[...]).astype(BF16)
    gradient = jnp.transpose(gradient.astype(F32)).astype(BF16)
    hidden = hidden_ref[...]
    if sums_ref.shape[0] > 2 * GROUPS * CHANNELS:
        rest = sums_ref.shape[0] - 2 * GROUPS * CHANNELS
        sums_ref[2 * GROUPS * CHANNELS :] = jnp.zeros((rest, 128), F32)
    ones, twos = [], []
    for k in range(9):
        one = dot(gradient, window(lifted_pad, k))
        two = dot(hidden, window(cotangent_pad, 8 - k))
        ones += [picked(one, diagonal(part - 1)) for part in range(3)]
        twos += [picked(two, diagonal(1 - part)) for part in range(3)]
        while len(ones) >= 4 or (k == 8 and ones):
            group = (3 * k + 3 - len(ones)) // 4
            for first, blocks in ((0, ones), (GROUPS, twos)):
                start = (first + group) * CHANNELS
                sums_ref[start : start + CHANNELS] = fold(blocks[:4])
            ones, twos = ones[4:], twos[4:]
    sums_out[...] = sums_ref[...].astype(BF16)


def fine_kernel(
    masks_ref, band_ref, lifted_ref, hidden_ref, high_own, low_own, far, near,
    fine_out, high_pool, low_pool, hidden_pad,
):
    bricks = half_lines(hidden_ref[...].astype(F32))
    pad_all(hidden_pad, bricks, masks_ref, high_pool, low_pool, high_own, low_own, far, near)
    fine = lifted_ref[...].astype(F32) + convolve(hidden_pad, band_ref)
    fine = fine.reshape(LINES // EDGE, 2, EDGE, HALF)
    fine = jnp.concatenate([fine[:, 0], fine[:, 1]], axis=-1)
    fine_out[...] = fine.astype(BF16).reshape(fine_out.shape)


def sum_kernel(devices, scale, parts_ref, out_hbm, rows_ref, shares_ref, sems):
    rows_ref[...] = parts_ref[...].astype(F32)
    share = rows_ref.shape[0] // devices
    pieces = [rows_ref[share * i : share * i + share] for i in range(devices)]
    while len(pieces) > 1:
        pairs = [a + b for a, b in zip(pieces[::2], pieces[1::2])]
        pieces = pairs + pieces[len(pieces) - len(pieces) % 2 :]
    total = pieces[0] * scale
    some = shares_ref.shape[0]
    for i in range(some // share):
        rows_ref[share * i : share * i + share] = total
    shares_ref[...] = rows_ref[0:some].astype(BF16)
    copies = []
    for i in range(out_hbm.shape[0] // some):
        copies.append(pltpu.make_async_copy(shares_ref, out_hbm.at[pl.ds(some * i, some)], sems.at[i]))
        copies[-1].start()
    for copy in copies:
        copy.wait()


def unpack_kernel(sums_ref, fine_ref, one_out, two_out, fine_out, rows_ref, one_ref, two_ref, sems, fine_sem):
    fine_copy = pltpu.make_async_copy(fine_ref, fine_out, fine_sem)
    fine_copy.start()
    rows_ref[...] = sums_ref[...].astype(F32)
    copies = []
    for which, (block_ref, out) in ((1, (two_ref, two_out)), (0, (one_ref, one_out))):
        for part, (first, last) in enumerate(((0, 2), (2, 4), (4, GROUPS))):
            for group in range(first, last):
                start = (which * GROUPS + group) * CHANNELS
                four = rows_ref[start : start + CHANNELS]
                turned = None if which else jnp.transpose(four)
                for n in range(min(4, 27 - 4 * group)):
                    if which:
                        block = pltpu.roll(four, 128 - n * CHANNELS, 1) if n else four
                        block_ref[4 * group + n] = block[:, :CHANNELS]
                    else:
                        block_ref[4 * group + n] = turned[CHANNELS * n : CHANNELS * n + CHANNELS]
            span = pl.ds(4 * first, min(4 * last, 27) - 4 * first)
            copies.append(pltpu.make_async_copy(block_ref.at[span], out.at[span], sems.at[which, part]))
            copies[-1].start()
    for copy in copies:
        copy.wait()
    fine_copy.wait()


def call(kernel, out_shape, scratch=(), hbm=(), inputs=1, limit=24, cost=None, out=pltpu.VMEM):
    spaces = [pl.ANY if i in hbm else pltpu.VMEM for i in range(inputs)]
    return pl.pallas_call(
        kernel,
        out_shape=out_shape,
        in_specs=[pl.BlockSpec(memory_space=space) for space in spaces],
        out_specs=jax.tree.map(lambda _: pl.BlockSpec(memory_space=out), out_shape),
        scratch_shapes=list(scratch),
        compiler_params=pltpu.CompilerParams(vmem_limit_bytes=limit * 2**20),
        cost_estimate=cost,
    )


def shape(*dims, dtype=BF16):
    return jax.ShapeDtypeStruct(dims, dtype)


def swapped(value, first):
    pairs = [(i, i + 1) for i in range(first, lax.axis_size("space") - 1, 2)]
    return lax.ppermute(value, "space", pairs + [(target, source) for source, target in pairs])


def exchanged(rows, axes=("space", "dp")):
    count = math.prod(lax.axis_size(axis) for axis in axes)
    shares = rows.reshape(count, -1, 2, 128)
    shares = lax.all_to_all(shares, axes, split_axis=0, concat_axis=0, tiled=True)
    return shares.reshape(rows.shape)


def body(coarse_latents, active_blocks, face_links, cotangent, up_weight, conv_one, conv_two):
    devices = lax.axis_size("space")
    everyone = devices * lax.axis_size("dp")
    held, width = coarse_latents.shape[1:]
    bricks = active_blocks.shape[1]
    split = lax.axis_size("dp") == 2
    tiles = width // 256
    count = 3 * BRICKS * tiles
    blocks = (2 * devices * count, 128)
    packed = call(
        functools.partial(pick_kernel, split),
        shape(*blocks),
        [
            pltpu.VMEM((1, bricks), jnp.int32),
            pltpu.VMEM((1, held, width), BF16),
            pltpu.VMEM((2, (bricks + 16) * tiles, 128), F32),
            pltpu.VMEM(blocks, F32),
            pltpu.SemaphoreType.DMA((2,)),
        ],
        hbm=(0, 1),
        inputs=2,
        limit=60,
    )(active_blocks, coarse_latents)
    received = exchanged(packed, ("space", "dp") if split else ("space",))
    window_half = shape(8 * tiles, 128)
    cost = pl.CostEstimate(flops=10**9, bytes_accessed=2 * 10**6, transcendentals=0)
    face = shape(BRICKS * FACE, LINE)
    halves = pltpu.VMEM((2, LINES, HALF), F32)
    faces = pltpu.VMEM((BRICKS * FACE, LINE), F32)
    pool = pltpu.VMEM((2 * BRICKS * FACE, LINE), F32)
    volume = shape(ROWS, HALF)
    links = [pltpu.SMEM(face_links.shape, jnp.int32), pltpu.SemaphoreType.DMA]
    pad_shape = (3, BRICKS, EDGE + 2, 2 * EDGE, WIDE)
    pad = pltpu.VMEM(pad_shape, BF16)
    high, low, far, near = call(faces_kernel, (face,) * 4, [halves, faces])(cotangent)
    far = swapped(far, 1)
    near = swapped(near, 0)
    masks = shape(BRICKS * 6 * 2 * BRICKS, 128, dtype=F32)
    band_one, band_back, masks = call(
        masks_kernel, (shape(*BAND), shape(*BAND), masks), links, hbm=(0,), inputs=3, cost=cost
    )(face_links, conv_one, conv_two)
    own, other = call(
        functools.partial(relay_kernel, split),
        (window_half, window_half),
        [pltpu.VMEM(blocks, F32)],
        hbm=(1,),
        inputs=2,
    )(received, masks)
    if split:
        other = lax.ppermute(other, "dp", [(0, 1), (1, 0)])
    slope, hidden, turned, lifted_pad = call(
        first_kernel,
        (
            shape(ROWS, HALF, dtype=F32), volume, shape(HALF, ROWS), shape(*pad_shape),
        ),
        [pltpu.VMEM((2, 8 * CUBE, 128), F32), pltpu.VMEM((2, 8 * tiles, 128), F32), *links],
        hbm=(0,),
        inputs=5,
    )(face_links, own, other, up_weight, band_one)
    share = 2 * -(-GROUPS * CHANNELS // everyone)
    packed_rows = (everyone * share, 128)
    sums, lifted = call(
        second_kernel,
        (shape(*packed_rows), volume),
        [pool, pool, pad, pltpu.VMEM(packed_rows, F32)],
        inputs=10,
    )(masks, cotangent, band_back, slope, turned, lifted_pad, high, low, far, near)
    parts = exchanged(sums)
    hidden_high, hidden_low, hidden_far, hidden_near = call(
        hidden_faces_kernel, (face,) * 4, [halves, faces], hbm=(1,), inputs=2
    )(hidden, parts)
    hidden_far = swapped(hidden_far, 1)
    hidden_near = swapped(hidden_near, 0)
    band_two = call(band_kernel, shape(*BAND), cost=cost)(conv_two)
    fine = call(fine_kernel, shape(*cotangent.shape), [pool, pool, pad], inputs=8, cost=cost)(
        masks, band_two, lifted, hidden, hidden_high, hidden_low, hidden_far, hidden_near
    )
    scale = 1.0 / math.sqrt(lax.axis_size("dp") * devices * BRICKS * EDGE**3)
    times = 4 if everyone % 32 == 0 else 1
    total = call(
        functools.partial(sum_kernel, everyone, scale),
        shape(*packed_rows),
        [
            pltpu.VMEM(packed_rows, F32),
            pltpu.VMEM((packed_rows[0] // times, 128), BF16),
            pltpu.SemaphoreType.DMA((times,)),
        ],
        out=pl.ANY,
    )(parts)
    gathered = exchanged(total)
    grads = shape(27, CHANNELS, CHANNELS, dtype=F32)
    block = pltpu.VMEM(grads.shape, F32)
    scratch = [pltpu.VMEM(packed_rows, F32), block, block]
    scratch += [pltpu.SemaphoreType.DMA((2, 3)), pltpu.SemaphoreType.DMA]
    grad_one, grad_two, fine = call(
        unpack_kernel, (grads, grads, shape(*fine.shape)), scratch, inputs=2, out=pl.ANY
    )(gathered, fine)
    return (fine, grad_one, grad_two)


def solution(mesh):
    return jax.shard_map(
        body,
        mesh=mesh,
        in_specs=(
            P("dp", "space", None),
            P("dp", None),
            P("dp", "space", None),
            P("dp", "space", None, None, None),
            P(),
            P(),
            P(),
        ),
        out_specs=(P("dp", "space", None, None, None), P(), P()),
        check_vma=False,
    )
```

```python
import functools
import math

import jax
import jax.numpy as jnp
from jax import lax
from jax.experimental import pallas as pl
from jax.experimental.pallas import tpu as pltpu
from jax.sharding import PartitionSpec as P

BF16 = jnp.bfloat16
F32 = jnp.float32
EDGE = 8
CHANNELS = 32
LINE = EDGE * CHANNELS
HALF = LINE // 2
WIDE = 2 * HALF
BRICKS = 2
CUBE = EDGE * EDGE
LINES = BRICKS * CUBE
BAND = (9, WIDE, HALF)
ROWS = 2 * LINES
FACE = 3 * EDGE
GROUPS = 7


def dot(left, right):
    return jnp.dot(left, right, preferred_element_type=F32)


def dot_rows(left, right):
    return lax.dot_general(left, right, (((0,), (0,)), ((), ())), preferred_element_type=F32)


def pair(halves_ref, start, count, stride=1):
    index = pl.ds(start, count, stride=stride) if stride > 1 else pl.ds(start, count)
    return halves_ref[0, index, :], halves_ref[1, index, :]


def lanes_of(shape):
    return lax.broadcasted_iota(jnp.int32, shape, len(shape) - 1)


def first_half(split):
    return lax.axis_index("dp") if split else 0


def pick_kernel(split, ids_hbm, latents_hbm, out_ref, ids_ref, latents_ref, rows_ref, blocks_ref, sems):
    ids_copy = pltpu.make_async_copy(ids_hbm, ids_ref, sems.at[0])
    latents_copy = pltpu.make_async_copy(latents_hbm, latents_ref, sems.at[1])
    ids_copy.start()
    latents_copy.start()
    held, width = latents_ref.shape[1:]
    bricks = ids_ref.shape[1]
    tiles = width // 256
    margin = 8 * tiles
    empty = jnp.zeros((margin, 128), F32)
    for half in range(2):
        rows_ref[half, 0:margin] = empty
        rows_ref[half, margin + bricks * tiles :] = empty
    first = lax.axis_index("space") * held
    rows = lax.broadcasted_iota(jnp.int32, (held, bricks), 0) + first
    ids_copy.wait()
    hot = jnp.where(rows == ids_ref[...], 1.0, 0.0).astype(BF16)
    latents_copy.wait()
    picked = dot_rows(hot, latents_ref[0])
    for tile in range(2 * tiles):
        place = pl.ds(margin + tile % tiles, bricks, stride=tiles)
        rows_ref[tile // tiles, place, :] = picked[:, tile * 128 : tile * 128 + 128]
    count = 3 * BRICKS * tiles
    straight = first_half(split) == 0
    for receiver in range(blocks_ref.shape[0] // (2 * count)):
        start = margin + BRICKS * (receiver - 1) * tiles
        halves = [rows_ref[half, start : start + count] for half in range(2)]
        for half in range(2):
            block = jnp.where(straight, halves[half], halves[1 - half]) if split else halves[half]
            place = (2 * receiver + half) * count
            blocks_ref[place : place + count] = block
    out_ref[...] = blocks_ref[...].astype(BF16)


def relay_kernel(split, received_ref, own_out, other_out, rows_ref):
    rows_ref[...] = received_ref[...].astype(F32)
    count = own_out.shape[0] * 3 // 4
    sums = []
    for half in range(2):
        total = None
        for start in range(half * count, rows_ref.shape[0], 2 * count):
            piece = rows_ref[start : start + count]
            total = piece if total is None else total + piece
        sums.append(jnp.concatenate([total, jnp.zeros((count // 3, 128), F32)], axis=0))
    straight = first_half(split) == 0
    own_out[...] = jnp.where(straight, sums[0], sums[1]).astype(BF16)
    other_out[...] = jnp.where(straight, sums[1], sums[0]).astype(BF16)


def build_band(band_ref, rows):
    shape = (3 * CHANNELS, HALF)
    row = lax.broadcasted_iota(jnp.int32, shape, 0)
    target = CHANNELS - (row // CHANNELS) * CHANNELS + row % CHANNELS
    distance = lanes_of(shape) - target
    band_ref[:, HALF:, :] = jnp.zeros((9, HALF, HALF), BF16)
    for z in range(-1, 5):
        select = jnp.where(distance == z * CHANNELS, 1.0, 0.0).astype(BF16)
        block = dot(rows, select).astype(BF16)
        start = z % 8 * CHANNELS
        band_ref[:, start : start + CHANNELS, :] = block.reshape(9, CHANNELS, HALF)


def weight_rows(weights):
    cube = weights.reshape(9, 3, CHANNELS, CHANNELS)
    rows = jnp.concatenate([cube[:, 0], cube[:, 1], cube[:, 2]], axis=-1)
    return rows.reshape(9 * CHANNELS, 3 * CHANNELS).astype(BF16)


def flipped_rows(weights):
    cube = jnp.swapaxes(weights, 1, 2).reshape(9, 3, CHANNELS, CHANNELS)
    pieces = [jnp.concatenate([cube[8 - k, 2], cube[8 - k, 1], cube[8 - k, 0]], axis=-1) for k in range(9)]
    return jnp.concatenate(pieces, axis=0).astype(BF16)


def band_kernel(weights_ref, band_ref):
    build_band(band_ref, weight_rows(weights_ref[...].astype(F32)))


def lift(half_ref, up_ref, rows_ref, volumes_ref, half):
    tiles = half_ref.shape[0] // 8
    rows_ref[...] = half_ref[...].astype(F32)
    cells = []
    for tile in range(tiles):
        rows = rows_ref[pl.ds(tile, 8, stride=tiles), :]
        cells += [rows[:, :64], rows[:, 64:]]
    lifted = dot(jnp.concatenate(cells, axis=0).astype(BF16), up_ref[...])
    lifted = lifted.astype(BF16).astype(F32)
    first = 4 * CUBE * half
    for cell in range(4):
        b, c = cell // 2, cell % 2
        for sub in range(16):
            line = first + 8 * (sub // 4 * EDGE + 4 * b + sub % 4)
            volumes_ref[c, line : line + 8, :] = lifted[cell * 8 : cell * 8 + 8, sub * 128 : sub * 128 + 128]


def early_kernel(
    links_in, own_ref, up_ref, weights_ref,
    band_ref, masks_ref, volumes_out,
    rows_ref, links_ref, links_sem,
):
    links_copy = pltpu.make_async_copy(links_in, links_ref, links_sem)
    links_copy.start()
    lift(own_ref, up_ref, rows_ref, volumes_out, 0)
    build_band(band_ref, weight_rows(weights_ref[...].astype(F32)))
    links_copy.wait()
    put_masks(masks_ref, links_ref)


def put_padded(pad_ref, brick, lines, x_low, x_high, y_low, y_high, z_low, z_high):
    def joined(halves, before, after):
        lane = lanes_of(halves[0].shape)
        first = jnp.where(lane < CHANNELS, halves[1], before)
        second = jnp.where(lane >= HALF - CHANNELS, halves[0], after)
        return jnp.concatenate([halves[0], first], axis=-1), jnp.concatenate([halves[1], second], axis=-1)

    inside = joined(lines, z_low, z_high)
    x_low, x_high, y_low, y_high = [joined(face, 0.0, 0.0) for face in (x_low, x_high, y_low, y_high)]
    none = jnp.zeros((1, WIDE), F32)
    shifted = [[], [], []]
    for half in range(2):
        slabs = jnp.concatenate([x_low[half][None], inside[half], x_high[half][None]], axis=0)
        row = lax.broadcasted_iota(jnp.int32, slabs.shape, 1)
        low = jnp.concatenate([none, y_low[half], none], axis=0)[:, None, :]
        high = jnp.concatenate([none, y_high[half], none], axis=0)[:, None, :]
        shifted[0].append(jnp.where(row == 0, low, pltpu.roll(slabs, 1, 1)))
        shifted[1].append(slabs)
        shifted[2].append(jnp.where(row == EDGE - 1, high, pltpu.roll(slabs, EDGE - 1, 1)))
    for dy in range(3):
        pad_ref[dy, brick] = jnp.concatenate(shifted[dy], axis=1).astype(BF16)


def window(pad_ref, k):
    return pad_ref[k % 3, :, k // 3 : k // 3 + EDGE].reshape(ROWS, WIDE)


def convolve(pad_ref, band_ref):
    both, last = None, None
    for dy in range(3):
        slabs = pad_ref[dy, :, : EDGE + 1].reshape(-1, WIDE)
        term = dot(slabs, jnp.concatenate([band_ref[dy], band_ref[3 + dy]], axis=1))
        both = term if both is None else both + term
        term = dot(window(pad_ref, 6 + dy), band_ref[6 + dy])
        last = term if last is None else last + term
    both = both.reshape(BRICKS, EDGE + 1, 2 * EDGE, 2 * HALF)
    total = both[:, :EDGE, :, :HALF] + both[:, 1:, :, HALF:]
    return total.reshape(ROWS, HALF) + last


def half_lines(values):
    cube = values.reshape(BRICKS, EDGE, 2, EDGE, HALF)
    return [(cube[brick, :, 0], cube[brick, :, 1]) for brick in range(BRICKS)]


def put_halves(halves_ref, start, bricks):
    for brick, lines in enumerate(bricks):
        for half in range(2):
            first = start + brick * CUBE
            halves_ref[half, first : first + CUBE, :] = lines[half].reshape(CUBE, HALF)


def cotangent_lines(cotangent_ref):
    cube = cotangent_ref[...].astype(F32).reshape(BRICKS, EDGE, EDGE, LINE)
    return [(cube[brick, :, :, :HALF], cube[brick, :, :, HALF:]) for brick in range(BRICKS)]


def pack_faces(faces_ref, base, halves_ref, start, high):
    x_face = pair(halves_ref, start + ((EDGE - 1) * EDGE if high else 0), EDGE)
    y_face = pair(halves_ref, start + (EDGE - 1 if high else 0), EDGE, EDGE)
    for half in range(2):
        lanes = slice(half * HALF, half * HALF + HALF)
        faces_ref[base : base + EDGE, lanes] = x_face[half]
        faces_ref[base + EDGE : base + 2 * EDGE, lanes] = y_face[half]
    tile = halves_ref[1 if high else 0, start : start + CUBE, :]
    lane = lanes_of((16, 128)) // CHANNELS
    packed = jnp.zeros((16, 128), F32)
    for part in range(4):
        shift = (part + 1 if high else part) % 4 * CHANNELS
        piece = tile[part * 16 : part * 16 + 16]
        packed = jnp.where(lane == part, pltpu.roll(piece, shift, 1) if shift else piece, packed)
    faces_ref[base + 2 * EDGE : base + FACE, :128] = packed[:8]
    faces_ref[base + 2 * EDGE : base + FACE, 128:] = packed[8:]


def pack_all(bricks, halves_ref, faces_ref, high_out, low_out):
    put_halves(halves_ref, 0, bricks)
    for high, out_ref in ((True, high_out), (False, low_out)):
        for brick in range(BRICKS):
            pack_faces(faces_ref, brick * FACE, halves_ref, brick * CUBE, high)
        out_ref[...] = faces_ref[...].astype(BF16)


def to_partners(high_ref, low_ref, far_out, near_out):
    even = lax.axis_index("space") % 2 == 0
    far_out[...] = jnp.where(even, low_ref[...], high_ref[...])
    near_out[...] = jnp.where(even, high_ref[...], low_ref[...])


def faces_kernel(cotangent_ref, high_out, low_out, far_out, near_out, halves_ref, faces_ref):
    pack_all(cotangent_lines(cotangent_ref), halves_ref, faces_ref, high_out, low_out)
    to_partners(high_out, low_out, far_out, near_out)


def unpack_depth(halves, high):
    packed = jnp.concatenate(halves, axis=0)
    pieces = []
    for part in range(4):
        shift = ((3 - part) if high else (4 - part)) % 4 * CHANNELS
        pieces.append(pltpu.roll(packed, shift, 1) if shift else packed)
    return jnp.concatenate(pieces, axis=0).reshape(EDGE, EDGE, 128)


def first_kernel(
    links_in, other_ref, up_ref, band_ref, lifted_half, weights_ref,
    slope_out, hidden_out, turned_out, pad_out, back_out,
    volumes_ref, rows_ref, links_ref, links_sem,
):
    links_copy = pltpu.make_async_copy(links_in, links_ref, links_sem)
    links_copy.start()
    position = lax.axis_index("space")
    volumes_ref[:, : 4 * CUBE] = lifted_half[...]
    lift(other_ref, up_ref, rows_ref, volumes_ref, 1)
    links_copy.wait()
    for brick in range(BRICKS):

        def near(face):
            link = links_ref[0, brick, face]
            index = jnp.clip(link - BRICKS * (position - 1), 0, 3 * BRICKS - 1)
            return index, jnp.where(link >= 0, 1.0, 0.0).astype(F32)

        def x_face(face):
            index, present = near(face)
            line = EDGE * (EDGE - 1) if face % 2 == 0 else 0
            return [half * present for half in pair(volumes_ref, line * 8 + index, EDGE, 8)]

        def y_face(face):
            index, present = near(face)
            line = EDGE - 1 if face % 2 == 0 else 0
            return [half * present for half in pair(volumes_ref, line * 8 + index, EDGE, 8 * EDGE)]

        def z_face(face):
            index, present = near(face)
            tile = volumes_ref[1 if face % 2 == 0 else 0, pl.ds(index, CUBE, stride=8), :] * present
            return tile.reshape(EDGE, EDGE, HALF)

        own = [half.reshape(EDGE, EDGE, HALF) for half in pair(volumes_ref, BRICKS + brick, CUBE, 8)]
        put_padded(pad_out, brick, own, x_face(0), x_face(1), y_face(2), y_face(3), z_face(4), z_face(5))
    pre = convolve(pad_out, band_ref)
    sigmoid = 1.0 / (1.0 + jnp.exp(-pre))
    hidden = (pre / (1.0 + jnp.exp(-pre))).astype(BF16)
    slope_out[...] = sigmoid * (1.0 + pre * (1.0 - sigmoid))
    hidden_out[...] = hidden
    hidden = hidden.astype(F32)
    turned_out[...] = jnp.transpose(hidden).astype(BF16)
    build_band(back_out, flipped_rows(weights_ref[...].astype(F32)))


def hidden_faces_kernel(hidden_ref, _parts, high_out, low_out, far_out, near_out, halves_ref, faces_ref):
    pack_all(half_lines(hidden_ref[...].astype(F32)), halves_ref, faces_ref, high_out, low_out)
    to_partners(high_out, low_out, far_out, near_out)


def picked(outer, places):
    lane = lanes_of((CHANNELS, 128)) // CHANNELS
    found = None
    for block in range(4):
        start, tile = places[block]
        rows = outer[start : start + CHANNELS, tile * 128 : tile * 128 + 128]
        found = rows if found is None else jnp.where(lane == block, rows, found)
    return found


def fold(four):
    lane = lanes_of((CHANNELS, 128)) // CHANNELS
    total = None
    for turn in range(4):
        mixed = four[0]
        for n in range(1, len(four)):
            mixed = jnp.where(lane == (n + turn) % 4, four[n], mixed)
        if turn:
            mixed = pltpu.roll(mixed, 128 - turn * CHANNELS, 1)
        total = mixed if total is None else total + mixed
    return total


def diagonal(shift):
    places = [None] * 4
    for z in range(4):
        other = z + shift
        places[other % 4] = (z * CHANNELS, 0 if 0 <= other < 4 else 1)
    return places


def put_masks(masks_ref, links_ref):
    position = lax.axis_index("space")
    for brick in range(BRICKS):
        for face in range(6):
            first = links_ref[0, brick, face] - BRICKS * (position - 1 if face % 2 == 0 else position)
            for i in range(2 * BRICKS):
                row = (brick * 6 + face) * 2 * BRICKS + i
                masks_ref[row : row + 1, :] = jnp.full((1, 128), jnp.where(first == i, 1.0, 0.0).astype(F32))


def pad_all(pad_ref, bricks, masks_ref, high_pool, low_pool, high_own, low_own, far, near):
    position = lax.axis_index("space")
    half = BRICKS * FACE
    even = position % 2 == 0
    high_pool[0:half] = jnp.where(even, far[...], near[...]).astype(F32)
    high_pool[half:] = high_own[...].astype(F32)
    low_pool[0:half] = low_own[...].astype(F32)
    low_pool[half:] = jnp.where(even, near[...], far[...]).astype(F32)
    for brick, lines in enumerate(bricks):

        def face(number, axis):
            pool = high_pool if number % 2 == 0 else low_pool
            total = [0.0, 0.0]
            for i in range(2 * BRICKS):
                row = (brick * 6 + number) * 2 * BRICKS + i
                mask = masks_ref[row : row + 1, :]
                start = i * FACE + axis * EDGE
                for part in range(2):
                    found = pool[start : start + EDGE, part * HALF : part * HALF + HALF]
                    total[part] = total[part] + found * mask
            return total

        put_padded(
            pad_ref, brick, lines, face(0, 0), face(1, 0), face(2, 1), face(3, 1),
            unpack_depth(face(4, 2), True), unpack_depth(face(5, 2), False),
        )


def second_kernel(
    masks_ref, cotangent_ref, band_ref, slope_ref, hidden_ref, lifted_pad, high_own, low_own, far, near,
    sums_out, lifted_out,
    high_pool, low_pool, cotangent_pad, sums_ref,
):
    lifted_out[...] = window(lifted_pad, 4)[:, :HALF]
    bricks = cotangent_lines(cotangent_ref)
    pad_all(cotangent_pad, bricks, masks_ref, high_pool, low_pool, high_own, low_own, far, near)
    gradient = (convolve(cotangent_pad, band_ref) * slope_ref[...]).astype(BF16)
    gradient = jnp.transpose(gradient.astype(F32)).astype(BF16)
    hidden = hidden_ref[...]
    if sums_ref.shape[0] > 2 * GROUPS * CHANNELS:
        rest = sums_ref.shape[0] - 2 * GROUPS * CHANNELS
        sums_ref[2 * GROUPS * CHANNELS :] = jnp.zeros((rest, 128), F32)
    ones, twos = [], []
    for k in range(9):
        one = dot(gradient, window(lifted_pad, k))
        two = dot(hidden, window(cotangent_pad, 8 - k))
        ones += [picked(one, diagonal(part - 1)) for part in range(3)]
        twos += [picked(two, diagonal(1 - part)) for part in range(3)]
        while len(ones) >= 4 or (k == 8 and ones):
            group = (3 * k + 3 - len(ones)) // 4
            for first, blocks in ((0, ones), (GROUPS, twos)):
                start = (first + group) * CHANNELS
                sums_ref[start : start + CHANNELS] = fold(blocks[:4])
            ones, twos = ones[4:], twos[4:]
    sums_out[...] = sums_ref[...].astype(BF16)


def fine_kernel(
    masks_ref, band_ref, lifted_ref, hidden_ref, high_own, low_own, far, near,
    fine_out, high_pool, low_pool, hidden_pad,
):
    bricks = half_lines(hidden_ref[...].astype(F32))
    pad_all(hidden_pad, bricks, masks_ref, high_pool, low_pool, high_own, low_own, far, near)
    fine = lifted_ref[...].astype(F32) + convolve(hidden_pad, band_ref)
    fine = fine.reshape(LINES // EDGE, 2, EDGE, HALF)
    fine = jnp.concatenate([fine[:, 0], fine[:, 1]], axis=-1)
    fine_out[...] = fine.astype(BF16).reshape(fine_out.shape)


def sum_kernel(devices, scale, parts_ref, out_hbm, rows_ref, shares_ref, sems):
    rows_ref[...] = parts_ref[...].astype(F32)
    share = rows_ref.shape[0] // devices
    pieces = [rows_ref[share * i : share * i + share] for i in range(devices)]
    while len(pieces) > 1:
        pairs = [a + b for a, b in zip(pieces[::2], pieces[1::2])]
        pieces = pairs + pieces[len(pieces) - len(pieces) % 2 :]
    total = pieces[0] * scale
    some = shares_ref.shape[0]
    for i in range(some // share):
        rows_ref[share * i : share * i + share] = total
    shares_ref[...] = rows_ref[0:some].astype(BF16)
    copies = []
    for i in range(out_hbm.shape[0] // some):
        copies.append(pltpu.make_async_copy(shares_ref, out_hbm.at[pl.ds(some * i, some)], sems.at[i]))
        copies[-1].start()
    for copy in copies:
        copy.wait()


def unpack_kernel(sums_ref, fine_ref, one_out, two_out, fine_out, rows_ref, one_ref, two_ref, sems, fine_sem):
    fine_copy = pltpu.make_async_copy(fine_ref, fine_out, fine_sem)
    fine_copy.start()
    rows_ref[...] = sums_ref[...].astype(F32)
    copies = []
    for which, (block_ref, out) in ((1, (two_ref, two_out)), (0, (one_ref, one_out))):
        for part, (first, last) in enumerate(((0, 2), (2, 4), (4, GROUPS))):
            for group in range(first, last):
                start = (which * GROUPS + group) * CHANNELS
                four = rows_ref[start : start + CHANNELS]
                turned = None if which else jnp.transpose(four)
                for n in range(min(4, 27 - 4 * group)):
                    if which:
                        block = pltpu.roll(four, 128 - n * CHANNELS, 1) if n else four
                        block_ref[4 * group + n] = block[:, :CHANNELS]
                    else:
                        block_ref[4 * group + n] = turned[CHANNELS * n : CHANNELS * n + CHANNELS]
            span = pl.ds(4 * first, min(4 * last, 27) - 4 * first)
            copies.append(pltpu.make_async_copy(block_ref.at[span], out.at[span], sems.at[which, part]))
            copies[-1].start()
    for copy in copies:
        copy.wait()
    fine_copy.wait()


def call(kernel, out_shape, scratch=(), hbm=(), inputs=1, limit=24, cost=None, out=pltpu.VMEM):
    spaces = [pl.ANY if i in hbm else pltpu.VMEM for i in range(inputs)]
    return pl.pallas_call(
        kernel,
        out_shape=out_shape,
        in_specs=[pl.BlockSpec(memory_space=space) for space in spaces],
        out_specs=jax.tree.map(lambda _: pl.BlockSpec(memory_space=out), out_shape),
        scratch_shapes=list(scratch),
        compiler_params=pltpu.CompilerParams(vmem_limit_bytes=limit * 2**20),
        cost_estimate=cost,
    )


def shape(*dims, dtype=BF16):
    return jax.ShapeDtypeStruct(dims, dtype)


def swapped(value, first):
    pairs = [(i, i + 1) for i in range(first, lax.axis_size("space") - 1, 2)]
    return lax.ppermute(value, "space", pairs + [(target, source) for source, target in pairs])


def exchanged(rows, axes=("space", "dp")):
    count = math.prod(lax.axis_size(axis) for axis in axes)
    shares = rows.reshape(count, -1, 2, 128)
    shares = lax.all_to_all(shares, axes, split_axis=0, concat_axis=0, tiled=True)
    return shares.reshape(rows.shape)


def body(coarse_latents, active_blocks, face_links, cotangent, up_weight, conv_one, conv_two):
    devices = lax.axis_size("space")
    everyone = devices * lax.axis_size("dp")
    held, width = coarse_latents.shape[1:]
    bricks = active_blocks.shape[1]
    split = lax.axis_size("dp") == 2
    tiles = width // 256
    count = 3 * BRICKS * tiles
    blocks = (2 * devices * count, 128)
    packed = call(
        functools.partial(pick_kernel, split),
        shape(*blocks),
        [
            pltpu.VMEM((1, bricks), jnp.int32),
            pltpu.VMEM((1, held, width), BF16),
            pltpu.VMEM((2, (bricks + 16) * tiles, 128), F32),
            pltpu.VMEM(blocks, F32),
            pltpu.SemaphoreType.DMA((2,)),
        ],
        hbm=(0, 1),
        inputs=2,
        limit=60,
    )(active_blocks, coarse_latents)
    received = exchanged(packed, ("space", "dp") if split else ("space",))
    window_half = shape(8 * tiles, 128)
    own, other = call(
        functools.partial(relay_kernel, split), (window_half, window_half), [pltpu.VMEM(blocks, F32)]
    )(received)
    if split:
        other = lax.ppermute(other, "dp", [(0, 1), (1, 0)])
    cost = pl.CostEstimate(flops=10**9, bytes_accessed=2 * 10**6, transcendentals=0)
    face = shape(BRICKS * FACE, LINE)
    halves = pltpu.VMEM((2, LINES, HALF), F32)
    faces = pltpu.VMEM((BRICKS * FACE, LINE), F32)
    pool = pltpu.VMEM((2 * BRICKS * FACE, LINE), F32)
    volume = shape(ROWS, HALF)
    links = [pltpu.SMEM(face_links.shape, jnp.int32), pltpu.SemaphoreType.DMA]
    pad_shape = (3, BRICKS, EDGE + 2, 2 * EDGE, WIDE)
    pad = pltpu.VMEM(pad_shape, BF16)
    high, low, far, near = call(faces_kernel, (face,) * 4, [halves, faces])(cotangent)
    far = swapped(far, 1)
    near = swapped(near, 0)
    masks = shape(BRICKS * 6 * 2 * BRICKS, 128, dtype=F32)
    lifted_half = shape(2, 4 * CUBE, 128, dtype=F32)
    window_rows = pltpu.VMEM((8 * tiles, 128), F32)
    band_one, masks, lifted_half = call(
        early_kernel, (shape(*BAND), masks, lifted_half), [window_rows, *links], hbm=(0,), inputs=4, cost=cost
    )(face_links, own, up_weight, conv_one)
    slope, hidden, turned, lifted_pad, band_back = call(
        first_kernel,
        (
            shape(ROWS, HALF, dtype=F32), volume, shape(HALF, ROWS), shape(*pad_shape), shape(*BAND),
        ),
        [pltpu.VMEM((2, 8 * CUBE, 128), F32), window_rows, *links],
        hbm=(0,),
        inputs=6,
    )(face_links, other, up_weight, band_one, lifted_half, conv_two)
    share = 2 * -(-GROUPS * CHANNELS // everyone)
    packed_rows = (everyone * share, 128)
    sums, lifted = call(
        second_kernel,
        (shape(*packed_rows), volume),
        [pool, pool, pad, pltpu.VMEM(packed_rows, F32)],
        inputs=10,
    )(masks, cotangent, band_back, slope, turned, lifted_pad, high, low, far, near)
    parts = exchanged(sums)
    hidden_high, hidden_low, hidden_far, hidden_near = call(
        hidden_faces_kernel, (face,) * 4, [halves, faces], hbm=(1,), inputs=2
    )(hidden, parts)
    hidden_far = swapped(hidden_far, 1)
    hidden_near = swapped(hidden_near, 0)
    band_two = call(band_kernel, shape(*BAND), cost=cost)(conv_two)
    fine = call(fine_kernel, shape(*cotangent.shape), [pool, pool, pad], inputs=8, cost=cost)(
        masks, band_two, lifted, hidden, hidden_high, hidden_low, hidden_far, hidden_near
    )
    scale = 1.0 / math.sqrt(lax.axis_size("dp") * devices * BRICKS * EDGE**3)
    times = 4 if everyone % 32 == 0 else 1
    total = call(
        functools.partial(sum_kernel, everyone, scale),
        shape(*packed_rows),
        [
            pltpu.VMEM(packed_rows, F32),
            pltpu.VMEM((packed_rows[0] // times, 128), BF16),
            pltpu.SemaphoreType.DMA((times,)),
        ],
        out=pl.ANY,
    )(parts)
    gathered = exchanged(total)
    grads = shape(27, CHANNELS, CHANNELS, dtype=F32)
    block = pltpu.VMEM(grads.shape, F32)
    scratch = [pltpu.VMEM(packed_rows, F32), block, block]
    scratch += [pltpu.SemaphoreType.DMA((2, 3)), pltpu.SemaphoreType.DMA]
    grad_one, grad_two, fine = call(
        unpack_kernel, (grads, grads, shape(*fine.shape)), scratch, inputs=2, out=pl.ANY
    )(gathered, fine)
    return (fine, grad_one, grad_two)


def solution(mesh):
    return jax.shard_map(
        body,
        mesh=mesh,
        in_specs=(
            P("dp", "space", None),
            P("dp", None),
            P("dp", "space", None),
            P("dp", "space", None, None, None),
            P(),
            P(),
            P(),
        ),
        out_specs=(P("dp", "space", None, None, None), P(), P()),
        check_vma=False,
    )
```

```python
import functools
import math

import jax
import jax.numpy as jnp
from jax import lax
from jax.experimental import pallas as pl
from jax.experimental.pallas import tpu as pltpu
from jax.sharding import PartitionSpec as P

BF16 = jnp.bfloat16
F32 = jnp.float32
EDGE = 8
CHANNELS = 32
LINE = EDGE * CHANNELS
HALF = LINE // 2
WIDE = 2 * HALF
BRICKS = 2
CUBE = EDGE * EDGE
LINES = BRICKS * CUBE
BAND = (9, WIDE, HALF)
ROWS = 2 * LINES
FACE = 3 * EDGE
GROUPS = 7


def dot(left, right):
    return jnp.dot(left, right, preferred_element_type=F32)


def dot_rows(left, right):
    return lax.dot_general(left, right, (((0,), (0,)), ((), ())), preferred_element_type=F32)


def pair(halves_ref, start, count, stride=1):
    index = pl.ds(start, count, stride=stride) if stride > 1 else pl.ds(start, count)
    return halves_ref[0, index, :], halves_ref[1, index, :]


def lanes_of(shape):
    return lax.broadcasted_iota(jnp.int32, shape, len(shape) - 1)


def first_half(split):
    return lax.axis_index("dp") if split else 0


def pick_kernel(split, extras, ids_hbm, latents_hbm, *refs):
    brought = zip(refs[:extras], refs[extras + 1 : 2 * extras + 1])
    out_ref = refs[extras]
    ids_ref, latents_ref, rows_ref, blocks_ref, sems = refs[2 * extras + 1 :]
    ids_copy = pltpu.make_async_copy(ids_hbm, ids_ref, sems.at[0])
    latents_copy = pltpu.make_async_copy(latents_hbm, latents_ref, sems.at[1])
    ids_copy.start()
    latents_copy.start()
    others = [pltpu.make_async_copy(*pair, sems.at[2 + i]) for i, pair in enumerate(brought)]
    for copy in others:
        copy.start()
    held, width = latents_ref.shape[1:]
    bricks = ids_ref.shape[1]
    tiles = width // 256
    margin = 8 * tiles
    empty = jnp.zeros((margin, 128), F32)
    for half in range(2):
        rows_ref[half, 0:margin] = empty
        rows_ref[half, margin + bricks * tiles :] = empty
    first = lax.axis_index("space") * held
    rows = lax.broadcasted_iota(jnp.int32, (held, bricks), 0) + first
    ids_copy.wait()
    hot = jnp.where(rows == ids_ref[...], 1.0, 0.0).astype(BF16)
    latents_copy.wait()
    picked = dot_rows(hot, latents_ref[0])
    for tile in range(2 * tiles):
        place = pl.ds(margin + tile % tiles, bricks, stride=tiles)
        rows_ref[tile // tiles, place, :] = picked[:, tile * 128 : tile * 128 + 128]
    count = 3 * BRICKS * tiles
    straight = first_half(split) == 0
    for receiver in range(blocks_ref.shape[0] // (2 * count)):
        start = margin + BRICKS * (receiver - 1) * tiles
        halves = [rows_ref[half, start : start + count] for half in range(2)]
        for half in range(2):
            block = jnp.where(straight, halves[half], halves[1 - half]) if split else halves[half]
            place = (2 * receiver + half) * count
            blocks_ref[place : place + count] = block
    out_ref[...] = blocks_ref[...].astype(BF16)
    for copy in others:
        copy.wait()


def relay_kernel(split, received_ref, own_out, other_out, rows_ref):
    rows_ref[...] = received_ref[...].astype(F32)
    count = own_out.shape[0] * 3 // 4
    sums = []
    for half in range(2):
        total = None
        for start in range(half * count, rows_ref.shape[0], 2 * count):
            piece = rows_ref[start : start + count]
            total = piece if total is None else total + piece
        sums.append(jnp.concatenate([total, jnp.zeros((count // 3, 128), F32)], axis=0))
    straight = first_half(split) == 0
    own_out[...] = jnp.where(straight, sums[0], sums[1]).astype(BF16)
    other_out[...] = jnp.where(straight, sums[1], sums[0]).astype(BF16)


def build_band(band_ref, rows):
    shape = (3 * CHANNELS, HALF)
    row = lax.broadcasted_iota(jnp.int32, shape, 0)
    target = CHANNELS - (row // CHANNELS) * CHANNELS + row % CHANNELS
    distance = lanes_of(shape) - target
    band_ref[:, HALF:, :] = jnp.zeros((9, HALF, HALF), BF16)
    for z in range(-1, 5):
        select = jnp.where(distance == z * CHANNELS, 1.0, 0.0).astype(BF16)
        block = dot(rows, select).astype(BF16)
        start = z % 8 * CHANNELS
        band_ref[:, start : start + CHANNELS, :] = block.reshape(9, CHANNELS, HALF)


def weight_rows(weights):
    cube = weights.reshape(9, 3, CHANNELS, CHANNELS)
    rows = jnp.concatenate([cube[:, 0], cube[:, 1], cube[:, 2]], axis=-1)
    return rows.reshape(9 * CHANNELS, 3 * CHANNELS).astype(BF16)


def flipped_rows(weights):
    cube = jnp.swapaxes(weights, 1, 2).reshape(9, 3, CHANNELS, CHANNELS)
    pieces = [jnp.concatenate([cube[8 - k, 2], cube[8 - k, 1], cube[8 - k, 0]], axis=-1) for k in range(9)]
    return jnp.concatenate(pieces, axis=0).astype(BF16)


def band_kernel(weights_ref, band_ref):
    build_band(band_ref, weight_rows(weights_ref[...].astype(F32)))


def lift(half_ref, up_ref, rows_ref, volumes_ref, half):
    tiles = half_ref.shape[0] // 8
    rows_ref[...] = half_ref[...].astype(F32)
    cells = []
    for tile in range(tiles):
        rows = rows_ref[pl.ds(tile, 8, stride=tiles), :]
        cells += [rows[:, :64], rows[:, 64:]]
    lifted = dot(jnp.concatenate(cells, axis=0).astype(BF16), up_ref[...])
    lifted = lifted.astype(BF16).astype(F32)
    first = 4 * CUBE * half
    for cell in range(4):
        b, c = cell // 2, cell % 2
        for sub in range(16):
            line = first + 8 * (sub // 4 * EDGE + 4 * b + sub % 4)
            volumes_ref[c, line : line + 8, :] = lifted[cell * 8 : cell * 8 + 8, sub * 128 : sub * 128 + 128]


def early_kernel(
    links_in, own_ref, up_ref, weights_ref,
    band_ref, masks_ref, volumes_out,
    rows_ref, links_ref, links_sem,
):
    links_copy = pltpu.make_async_copy(links_in, links_ref, links_sem)
    links_copy.start()
    lift(own_ref, up_ref, rows_ref, volumes_out, 0)
    build_band(band_ref, weight_rows(weights_ref[...].astype(F32)))
    links_copy.wait()
    put_masks(masks_ref, links_ref)


def put_padded(pad_ref, brick, lines, x_low, x_high, y_low, y_high, z_low, z_high):
    def joined(halves, before, after):
        lane = lanes_of(halves[0].shape)
        first = jnp.where(lane < CHANNELS, halves[1], before)
        second = jnp.where(lane >= HALF - CHANNELS, halves[0], after)
        return jnp.concatenate([halves[0], first], axis=-1), jnp.concatenate([halves[1], second], axis=-1)

    inside = joined(lines, z_low, z_high)
    x_low, x_high, y_low, y_high = [joined(face, 0.0, 0.0) for face in (x_low, x_high, y_low, y_high)]
    none = jnp.zeros((1, WIDE), F32)
    shifted = [[], [], []]
    for half in range(2):
        slabs = jnp.concatenate([x_low[half][None], inside[half], x_high[half][None]], axis=0)
        row = lax.broadcasted_iota(jnp.int32, slabs.shape, 1)
        low = jnp.concatenate([none, y_low[half], none], axis=0)[:, None, :]
        high = jnp.concatenate([none, y_high[half], none], axis=0)[:, None, :]
        shifted[0].append(jnp.where(row == 0, low, pltpu.roll(slabs, 1, 1)))
        shifted[1].append(slabs)
        shifted[2].append(jnp.where(row == EDGE - 1, high, pltpu.roll(slabs, EDGE - 1, 1)))
    for dy in range(3):
        pad_ref[dy, brick] = jnp.concatenate(shifted[dy], axis=1).astype(BF16)


def window(pad_ref, k):
    return pad_ref[k % 3, :, k // 3 : k // 3 + EDGE].reshape(ROWS, WIDE)


def convolve(pad_ref, band_ref):
    both, last = None, None
    for dy in range(3):
        slabs = pad_ref[dy, :, : EDGE + 1].reshape(-1, WIDE)
        term = dot(slabs, jnp.concatenate([band_ref[dy], band_ref[3 + dy]], axis=1))
        both = term if both is None else both + term
        term = dot(window(pad_ref, 6 + dy), band_ref[6 + dy])
        last = term if last is None else last + term
    both = both.reshape(BRICKS, EDGE + 1, 2 * EDGE, 2 * HALF)
    total = both[:, :EDGE, :, :HALF] + both[:, 1:, :, HALF:]
    return total.reshape(ROWS, HALF) + last


def half_lines(values):
    cube = values.reshape(BRICKS, EDGE, 2, EDGE, HALF)
    return [(cube[brick, :, 0], cube[brick, :, 1]) for brick in range(BRICKS)]


def put_halves(halves_ref, start, bricks):
    for brick, lines in enumerate(bricks):
        for half in range(2):
            first = start + brick * CUBE
            halves_ref[half, first : first + CUBE, :] = lines[half].reshape(CUBE, HALF)


def cotangent_lines(cotangent_ref):
    cube = cotangent_ref[...].astype(F32).reshape(BRICKS, EDGE, EDGE, LINE)
    return [(cube[brick, :, :, :HALF], cube[brick, :, :, HALF:]) for brick in range(BRICKS)]


def pack_faces(faces_ref, base, halves_ref, start, high):
    x_face = pair(halves_ref, start + ((EDGE - 1) * EDGE if high else 0), EDGE)
    y_face = pair(halves_ref, start + (EDGE - 1 if high else 0), EDGE, EDGE)
    for half in range(2):
        lanes = slice(half * HALF, half * HALF + HALF)
        faces_ref[base : base + EDGE, lanes] = x_face[half]
        faces_ref[base + EDGE : base + 2 * EDGE, lanes] = y_face[half]
    tile = halves_ref[1 if high else 0, start : start + CUBE, :]
    lane = lanes_of((16, 128)) // CHANNELS
    packed = jnp.zeros((16, 128), F32)
    for part in range(4):
        shift = (part + 1 if high else part) % 4 * CHANNELS
        piece = tile[part * 16 : part * 16 + 16]
        packed = jnp.where(lane == part, pltpu.roll(piece, shift, 1) if shift else piece, packed)
    faces_ref[base + 2 * EDGE : base + FACE, :128] = packed[:8]
    faces_ref[base + 2 * EDGE : base + FACE, 128:] = packed[8:]


def pack_all(bricks, halves_ref, faces_ref, high_out, low_out):
    put_halves(halves_ref, 0, bricks)
    for high, out_ref in ((True, high_out), (False, low_out)):
        for brick in range(BRICKS):
            pack_faces(faces_ref, brick * FACE, halves_ref, brick * CUBE, high)
        out_ref[...] = faces_ref[...].astype(BF16)


def to_partners(high_ref, low_ref, far_out, near_out):
    even = lax.axis_index("space") % 2 == 0
    far_out[...] = jnp.where(even, low_ref[...], high_ref[...])
    near_out[...] = jnp.where(even, high_ref[...], low_ref[...])


def faces_kernel(cotangent_ref, high_out, low_out, far_out, near_out, halves_ref, faces_ref):
    pack_all(cotangent_lines(cotangent_ref), halves_ref, faces_ref, high_out, low_out)
    to_partners(high_out, low_out, far_out, near_out)


def unpack_depth(halves, high):
    packed = jnp.concatenate(halves, axis=0)
    pieces = []
    for part in range(4):
        shift = ((3 - part) if high else (4 - part)) % 4 * CHANNELS
        pieces.append(pltpu.roll(packed, shift, 1) if shift else packed)
    return jnp.concatenate(pieces, axis=0).reshape(EDGE, EDGE, 128)


def first_kernel(
    links_in, other_ref, up_ref, band_ref, lifted_half, weights_ref,
    slope_out, hidden_out, turned_out, pad_out, back_out,
    volumes_ref, rows_ref, links_ref, links_sem,
):
    links_copy = pltpu.make_async_copy(links_in, links_ref, links_sem)
    links_copy.start()
    position = lax.axis_index("space")
    volumes_ref[:, : 4 * CUBE] = lifted_half[...]
    lift(other_ref, up_ref, rows_ref, volumes_ref, 1)
    links_copy.wait()
    for brick in range(BRICKS):

        def near(face):
            link = links_ref[0, brick, face]
            index = jnp.clip(link - BRICKS * (position - 1), 0, 3 * BRICKS - 1)
            return index, jnp.where(link >= 0, 1.0, 0.0).astype(F32)

        def x_face(face):
            index, present = near(face)
            line = EDGE * (EDGE - 1) if face % 2 == 0 else 0
            return [half * present for half in pair(volumes_ref, line * 8 + index, EDGE, 8)]

        def y_face(face):
            index, present = near(face)
            line = EDGE - 1 if face % 2 == 0 else 0
            return [half * present for half in pair(volumes_ref, line * 8 + index, EDGE, 8 * EDGE)]

        def z_face(face):
            index, present = near(face)
            tile = volumes_ref[1 if face % 2 == 0 else 0, pl.ds(index, CUBE, stride=8), :] * present
            return tile.reshape(EDGE, EDGE, HALF)

        own = [half.reshape(EDGE, EDGE, HALF) for half in pair(volumes_ref, BRICKS + brick, CUBE, 8)]
        put_padded(pad_out, brick, own, x_face(0), x_face(1), y_face(2), y_face(3), z_face(4), z_face(5))
    pre = convolve(pad_out, band_ref)
    sigmoid = 1.0 / (1.0 + jnp.exp(-pre))
    hidden = (pre / (1.0 + jnp.exp(-pre))).astype(BF16)
    slope_out[...] = sigmoid * (1.0 + pre * (1.0 - sigmoid))
    hidden_out[...] = hidden
    hidden = hidden.astype(F32)
    turned_out[...] = jnp.transpose(hidden).astype(BF16)
    build_band(back_out, flipped_rows(weights_ref[...].astype(F32)))


def hidden_faces_kernel(hidden_ref, _parts, high_out, low_out, far_out, near_out, halves_ref, faces_ref):
    pack_all(half_lines(hidden_ref[...].astype(F32)), halves_ref, faces_ref, high_out, low_out)
    to_partners(high_out, low_out, far_out, near_out)


def picked(outer, places):
    lane = lanes_of((CHANNELS, 128)) // CHANNELS
    found = None
    for block in range(4):
        start, tile = places[block]
        rows = outer[start : start + CHANNELS, tile * 128 : tile * 128 + 128]
        found = rows if found is None else jnp.where(lane == block, rows, found)
    return found


def fold(four):
    lane = lanes_of((CHANNELS, 128)) // CHANNELS
    total = None
    for turn in range(4):
        mixed = four[0]
        for n in range(1, len(four)):
            mixed = jnp.where(lane == (n + turn) % 4, four[n], mixed)
        if turn:
            mixed = pltpu.roll(mixed, 128 - turn * CHANNELS, 1)
        total = mixed if total is None else total + mixed
    return total


def diagonal(shift):
    places = [None] * 4
    for z in range(4):
        other = z + shift
        places[other % 4] = (z * CHANNELS, 0 if 0 <= other < 4 else 1)
    return places


def put_masks(masks_ref, links_ref):
    position = lax.axis_index("space")
    for brick in range(BRICKS):
        for face in range(6):
            first = links_ref[0, brick, face] - BRICKS * (position - 1 if face % 2 == 0 else position)
            for i in range(2 * BRICKS):
                row = (brick * 6 + face) * 2 * BRICKS + i
                masks_ref[row : row + 1, :] = jnp.full((1, 128), jnp.where(first == i, 1.0, 0.0).astype(F32))


def pad_all(pad_ref, bricks, masks_ref, high_pool, low_pool, high_own, low_own, far, near):
    position = lax.axis_index("space")
    half = BRICKS * FACE
    even = position % 2 == 0
    high_pool[0:half] = jnp.where(even, far[...], near[...]).astype(F32)
    high_pool[half:] = high_own[...].astype(F32)
    low_pool[0:half] = low_own[...].astype(F32)
    low_pool[half:] = jnp.where(even, near[...], far[...]).astype(F32)
    for brick, lines in enumerate(bricks):

        def face(number, axis):
            pool = high_pool if number % 2 == 0 else low_pool
            total = [0.0, 0.0]
            for i in range(2 * BRICKS):
                row = (brick * 6 + number) * 2 * BRICKS + i
                mask = masks_ref[row : row + 1, :]
                start = i * FACE + axis * EDGE
                for part in range(2):
                    found = pool[start : start + EDGE, part * HALF : part * HALF + HALF]
                    total[part] = total[part] + found * mask
            return total

        put_padded(
            pad_ref, brick, lines, face(0, 0), face(1, 0), face(2, 1), face(3, 1),
            unpack_depth(face(4, 2), True), unpack_depth(face(5, 2), False),
        )


def second_kernel(
    masks_ref, cotangent_ref, band_ref, slope_ref, hidden_ref, lifted_pad, high_own, low_own, far, near,
    sums_out, lifted_out,
    high_pool, low_pool, cotangent_pad, sums_ref,
):
    lifted_out[...] = window(lifted_pad, 4)[:, :HALF]
    bricks = cotangent_lines(cotangent_ref)
    pad_all(cotangent_pad, bricks, masks_ref, high_pool, low_pool, high_own, low_own, far, near)
    gradient = (convolve(cotangent_pad, band_ref) * slope_ref[...]).astype(BF16)
    gradient = jnp.transpose(gradient.astype(F32)).astype(BF16)
    hidden = hidden_ref[...]
    if sums_ref.shape[0] > 2 * GROUPS * CHANNELS:
        rest = sums_ref.shape[0] - 2 * GROUPS * CHANNELS
        sums_ref[2 * GROUPS * CHANNELS :] = jnp.zeros((rest, 128), F32)
    ones, twos = [], []
    for k in range(9):
        one = dot(gradient, window(lifted_pad, k))
        two = dot(hidden, window(cotangent_pad, 8 - k))
        ones += [picked(one, diagonal(part - 1)) for part in range(3)]
        twos += [picked(two, diagonal(1 - part)) for part in range(3)]
        while len(ones) >= 4 or (k == 8 and ones):
            group = (3 * k + 3 - len(ones)) // 4
            for first, blocks in ((0, ones), (GROUPS, twos)):
                start = (first + group) * CHANNELS
                sums_ref[start : start + CHANNELS] = fold(blocks[:4])
            ones, twos = ones[4:], twos[4:]
    sums_out[...] = sums_ref[...].astype(BF16)


def fine_kernel(
    masks_ref, band_ref, lifted_ref, hidden_ref, high_own, low_own, far, near,
    fine_out, high_pool, low_pool, hidden_pad,
):
    bricks = half_lines(hidden_ref[...].astype(F32))
    pad_all(hidden_pad, bricks, masks_ref, high_pool, low_pool, high_own, low_own, far, near)
    fine = lifted_ref[...].astype(F32) + convolve(hidden_pad, band_ref)
    fine = fine.reshape(LINES // EDGE, 2, EDGE, HALF)
    fine = jnp.concatenate([fine[:, 0], fine[:, 1]], axis=-1)
    fine_out[...] = fine.astype(BF16).reshape(fine_out.shape)


def sum_kernel(devices, scale, parts_ref, out_hbm, rows_ref, shares_ref, sems):
    rows_ref[...] = parts_ref[...].astype(F32)
    share = rows_ref.shape[0] // devices
    pieces = [rows_ref[share * i : share * i + share] for i in range(devices)]
    while len(pieces) > 1:
        pairs = [a + b for a, b in zip(pieces[::2], pieces[1::2])]
        pieces = pairs + pieces[len(pieces) - len(pieces) % 2 :]
    total = pieces[0] * scale
    some = shares_ref.shape[0]
    for i in range(some // share):
        rows_ref[share * i : share * i + share] = total
    shares_ref[...] = rows_ref[0:some].astype(BF16)
    copies = []
    for i in range(out_hbm.shape[0] // some):
        copies.append(pltpu.make_async_copy(shares_ref, out_hbm.at[pl.ds(some * i, some)], sems.at[i]))
        copies[-1].start()
    for copy in copies:
        copy.wait()


def unpack_kernel(sums_ref, fine_ref, one_out, two_out, fine_out, rows_ref, one_ref, two_ref, sems, fine_sem):
    fine_copy = pltpu.make_async_copy(fine_ref, fine_out, fine_sem)
    fine_copy.start()
    rows_ref[...] = sums_ref[...].astype(F32)
    copies = []
    for which, (block_ref, out) in ((1, (two_ref, two_out)), (0, (one_ref, one_out))):
        for part, (first, last) in enumerate(((0, 2), (2, 4), (4, GROUPS))):
            for group in range(first, last):
                start = (which * GROUPS + group) * CHANNELS
                four = rows_ref[start : start + CHANNELS]
                turned = None if which else jnp.transpose(four)
                for n in range(min(4, 27 - 4 * group)):
                    if which:
                        block = pltpu.roll(four, 128 - n * CHANNELS, 1) if n else four
                        block_ref[4 * group + n] = block[:, :CHANNELS]
                    else:
                        block_ref[4 * group + n] = turned[CHANNELS * n : CHANNELS * n + CHANNELS]
            span = pl.ds(4 * first, min(4 * last, 27) - 4 * first)
            copies.append(pltpu.make_async_copy(block_ref.at[span], out.at[span], sems.at[which, part]))
            copies[-1].start()
    for copy in copies:
        copy.wait()
    fine_copy.wait()


def call(kernel, out_shape, scratch=(), hbm=(), inputs=1, limit=24, cost=None, out=pltpu.VMEM):
    spaces = [pl.ANY if i in hbm else pltpu.VMEM for i in range(inputs)]
    return pl.pallas_call(
        kernel,
        out_shape=out_shape,
        in_specs=[pl.BlockSpec(memory_space=space) for space in spaces],
        out_specs=jax.tree.map(lambda _: pl.BlockSpec(memory_space=out), out_shape),
        scratch_shapes=list(scratch),
        compiler_params=pltpu.CompilerParams(vmem_limit_bytes=limit * 2**20),
        cost_estimate=cost,
    )


def shape(*dims, dtype=BF16):
    return jax.ShapeDtypeStruct(dims, dtype)


def kept_in_hbm(value):
    return pltpu.with_memory_space_constraint(value, pltpu.HBM)


def swapped(value, first):
    pairs = [(i, i + 1) for i in range(first, lax.axis_size("space") - 1, 2)]
    return lax.ppermute(value, "space", pairs + [(target, source) for source, target in pairs])


def exchanged(rows, axes=("space", "dp")):
    count = math.prod(lax.axis_size(axis) for axis in axes)
    shares = rows.reshape(count, -1, 2, 128)
    shares = lax.all_to_all(shares, axes, split_axis=0, concat_axis=0, tiled=True)
    return shares.reshape(rows.shape)


def body(coarse_latents, active_blocks, face_links, cotangent, up_weight, conv_one, conv_two):
    devices = lax.axis_size("space")
    everyone = devices * lax.axis_size("dp")
    held, width = coarse_latents.shape[1:]
    bricks = active_blocks.shape[1]
    split = lax.axis_size("dp") == 2
    tiles = width // 256
    count = 3 * BRICKS * tiles
    blocks = (2 * devices * count, 128)
    extras = (up_weight, conv_one, conv_two, face_links)
    packed, up_weight, conv_one, conv_two, face_links = call(
        functools.partial(pick_kernel, split, len(extras)),
        (shape(*blocks), *[shape(*extra.shape, dtype=extra.dtype) for extra in extras]),
        [
            pltpu.VMEM((1, bricks), jnp.int32),
            pltpu.VMEM((1, held, width), BF16),
            pltpu.VMEM((2, (bricks + 16) * tiles, 128), F32),
            pltpu.VMEM(blocks, F32),
            pltpu.SemaphoreType.DMA((2 + len(extras),)),
        ],
        hbm=range(2 + len(extras)),
        inputs=2 + len(extras),
    )(*[kept_in_hbm(operand) for operand in (active_blocks, coarse_latents, *extras)])
    received = exchanged(packed, ("space", "dp") if split else ("space",))
    window_half = shape(8 * tiles, 128)
    own, other = call(
        functools.partial(relay_kernel, split), (window_half, window_half), [pltpu.VMEM(blocks, F32)]
    )(received)
    if split:
        other = lax.ppermute(other, "dp", [(0, 1), (1, 0)])
    cost = pl.CostEstimate(flops=10**9, bytes_accessed=2 * 10**6, transcendentals=0)
    face = shape(BRICKS * FACE, LINE)
    halves = pltpu.VMEM((2, LINES, HALF), F32)
    faces = pltpu.VMEM((BRICKS * FACE, LINE), F32)
    pool = pltpu.VMEM((2 * BRICKS * FACE, LINE), F32)
    volume = shape(ROWS, HALF)
    links = [pltpu.SMEM(face_links.shape, jnp.int32), pltpu.SemaphoreType.DMA]
    pad_shape = (3, BRICKS, EDGE + 2, 2 * EDGE, WIDE)
    pad = pltpu.VMEM(pad_shape, BF16)
    high, low, far, near = call(faces_kernel, (face,) * 4, [halves, faces])(cotangent)
    far = swapped(far, 1)
    near = swapped(near, 0)
    masks = shape(BRICKS * 6 * 2 * BRICKS, 128, dtype=F32)
    lifted_half = shape(2, 4 * CUBE, 128, dtype=F32)
    window_rows = pltpu.VMEM((8 * tiles, 128), F32)
    band_one, masks, lifted_half = call(
        early_kernel, (shape(*BAND), masks, lifted_half), [window_rows, *links], hbm=(0,), inputs=4, cost=cost
    )(face_links, own, up_weight, conv_one)
    slope, hidden, turned, lifted_pad, band_back = call(
        first_kernel,
        (
            shape(ROWS, HALF, dtype=F32), volume, shape(HALF, ROWS), shape(*pad_shape), shape(*BAND),
        ),
        [pltpu.VMEM((2, 8 * CUBE, 128), F32), window_rows, *links],
        hbm=(0,),
        inputs=6,
    )(face_links, other, up_weight, band_one, lifted_half, conv_two)
    share = 2 * -(-GROUPS * CHANNELS // everyone)
    packed_rows = (everyone * share, 128)
    sums, lifted = call(
        second_kernel,
        (shape(*packed_rows), volume),
        [pool, pool, pad, pltpu.VMEM(packed_rows, F32)],
        inputs=10,
    )(masks, cotangent, band_back, slope, turned, lifted_pad, high, low, far, near)
    parts = exchanged(sums)
    hidden_high, hidden_low, hidden_far, hidden_near = call(
        hidden_faces_kernel, (face,) * 4, [halves, faces], hbm=(1,), inputs=2
    )(hidden, parts)
    hidden_far = swapped(hidden_far, 1)
    hidden_near = swapped(hidden_near, 0)
    band_two = call(band_kernel, shape(*BAND), cost=cost)(conv_two)
    fine = call(fine_kernel, shape(*cotangent.shape), [pool, pool, pad], inputs=8, cost=cost)(
        masks, band_two, lifted, hidden, hidden_high, hidden_low, hidden_far, hidden_near
    )
    scale = 1.0 / math.sqrt(lax.axis_size("dp") * devices * BRICKS * EDGE**3)
    times = 4 if everyone % 32 == 0 else 1
    total = call(
        functools.partial(sum_kernel, everyone, scale),
        shape(*packed_rows),
        [
            pltpu.VMEM(packed_rows, F32),
            pltpu.VMEM((packed_rows[0] // times, 128), BF16),
            pltpu.SemaphoreType.DMA((times,)),
        ],
        out=pl.ANY,
    )(parts)
    gathered = exchanged(total)
    grads = shape(27, CHANNELS, CHANNELS, dtype=F32)
    block = pltpu.VMEM(grads.shape, F32)
    scratch = [pltpu.VMEM(packed_rows, F32), block, block]
    scratch += [pltpu.SemaphoreType.DMA((2, 3)), pltpu.SemaphoreType.DMA]
    grad_one, grad_two, fine = call(
        unpack_kernel, (grads, grads, shape(*fine.shape)), scratch, inputs=2, out=pl.ANY
    )(gathered, fine)
    return (fine, grad_one, grad_two)


def solution(mesh):
    return jax.shard_map(
        body,
        mesh=mesh,
        in_specs=(
            P("dp", "space", None),
            P("dp", None),
            P("dp", "space", None),
            P("dp", "space", None, None, None),
            P(),
            P(),
            P(),
        ),
        out_specs=(P("dp", "space", None, None, None), P(), P()),
        check_vma=False,
    )
```

```python
import functools
import math

import jax
import jax.numpy as jnp
from jax import lax
from jax.experimental import pallas as pl
from jax.experimental.pallas import tpu as pltpu
from jax.sharding import PartitionSpec as P

BF16 = jnp.bfloat16
F32 = jnp.float32
EDGE = 8
CHANNELS = 32
LINE = EDGE * CHANNELS
HALF = LINE // 2
WIDE = 2 * HALF
BRICKS = 2
CUBE = EDGE * EDGE
LINES = BRICKS * CUBE
BAND = (9, WIDE, HALF)
ROWS = 2 * LINES
FACE = 3 * EDGE
GROUPS = 7


def dot(left, right):
    return jnp.dot(left, right, preferred_element_type=F32)


def dot_rows(left, right):
    return lax.dot_general(left, right, (((0,), (0,)), ((), ())), preferred_element_type=F32)


def pair(halves_ref, start, count, stride=1):
    index = pl.ds(start, count, stride=stride) if stride > 1 else pl.ds(start, count)
    return halves_ref[0, index, :], halves_ref[1, index, :]


def lanes_of(shape):
    return lax.broadcasted_iota(jnp.int32, shape, len(shape) - 1)


def first_half(split):
    return lax.axis_index("dp") if split else 0


def pick_kernel(split, extras, ids_hbm, latents_hbm, *refs):
    brought = zip(refs[:extras], refs[extras + 1 : 2 * extras + 1])
    out_ref = refs[extras]
    ids_ref, latents_ref, rows_ref, blocks_ref, sems = refs[2 * extras + 1 :]
    ids_copy = pltpu.make_async_copy(ids_hbm, ids_ref, sems.at[0])
    latents_copy = pltpu.make_async_copy(latents_hbm, latents_ref, sems.at[1])
    ids_copy.start()
    latents_copy.start()
    others = [pltpu.make_async_copy(*pair, sems.at[2 + i]) for i, pair in enumerate(brought)]
    for copy in others:
        copy.start()
    held, width = latents_ref.shape[1:]
    bricks = ids_ref.shape[1]
    tiles = width // 256
    margin = 8 * tiles
    empty = jnp.zeros((margin, 128), F32)
    for half in range(2):
        rows_ref[half, 0:margin] = empty
        rows_ref[half, margin + bricks * tiles :] = empty
    first = lax.axis_index("space") * held
    rows = lax.broadcasted_iota(jnp.int32, (held, bricks), 0) + first
    ids_copy.wait()
    hot = jnp.where(rows == ids_ref[...], 1.0, 0.0).astype(BF16)
    latents_copy.wait()
    picked = dot_rows(hot, latents_ref[0])
    for tile in range(2 * tiles):
        place = pl.ds(margin + tile % tiles, bricks, stride=tiles)
        rows_ref[tile // tiles, place, :] = picked[:, tile * 128 : tile * 128 + 128]
    count = 3 * BRICKS * tiles
    straight = first_half(split) == 0
    for receiver in range(blocks_ref.shape[0] // (2 * count)):
        start = margin + BRICKS * (receiver - 1) * tiles
        halves = [rows_ref[half, start : start + count] for half in range(2)]
        for half in range(2):
            block = jnp.where(straight, halves[half], halves[1 - half]) if split else halves[half]
            place = (2 * receiver + half) * count
            blocks_ref[place : place + count] = block
    out_ref[...] = blocks_ref[...].astype(BF16)
    for copy in others:
        copy.wait()


def relay_kernel(split, received_ref, own_out, other_out, rows_ref):
    rows_ref[...] = received_ref[...].astype(F32)
    count = own_out.shape[0] * 3 // 4
    sums = []
    for half in range(2):
        total = None
        for start in range(half * count, rows_ref.shape[0], 2 * count):
            piece = rows_ref[start : start + count]
            total = piece if total is None else total + piece
        sums.append(jnp.concatenate([total, jnp.zeros((count // 3, 128), F32)], axis=0))
    straight = first_half(split) == 0
    own_out[...] = jnp.where(straight, sums[0], sums[1]).astype(BF16)
    other_out[...] = jnp.where(straight, sums[1], sums[0]).astype(BF16)


def build_band(band_ref, rows):
    shape = (3 * CHANNELS, HALF)
    row = lax.broadcasted_iota(jnp.int32, shape, 0)
    target = CHANNELS - (row // CHANNELS) * CHANNELS + row % CHANNELS
    distance = lanes_of(shape) - target
    band_ref[:, HALF:, :] = jnp.zeros((9, HALF, HALF), BF16)
    for z in range(-1, 5):
        select = jnp.where(distance == z * CHANNELS, 1.0, 0.0).astype(BF16)
        block = dot(rows, select).astype(BF16)
        start = z % 8 * CHANNELS
        band_ref[:, start : start + CHANNELS, :] = block.reshape(9, CHANNELS, HALF)


def weight_rows(weights):
    cube = weights.reshape(9, 3, CHANNELS, CHANNELS)
    rows = jnp.concatenate([cube[:, 0], cube[:, 1], cube[:, 2]], axis=-1)
    return rows.reshape(9 * CHANNELS, 3 * CHANNELS).astype(BF16)


def flipped_rows(weights):
    cube = jnp.swapaxes(weights, 1, 2).reshape(9, 3, CHANNELS, CHANNELS)
    pieces = [jnp.concatenate([cube[8 - k, 2], cube[8 - k, 1], cube[8 - k, 0]], axis=-1) for k in range(9)]
    return jnp.concatenate(pieces, axis=0).astype(BF16)


def band_kernel(weights_ref, band_ref):
    build_band(band_ref, weight_rows(weights_ref[...].astype(F32)))


def lift(half_ref, up_ref, rows_ref, volumes_ref, half):
    tiles = half_ref.shape[0] // 8
    rows_ref[...] = half_ref[...].astype(F32)
    cells = []
    for tile in range(tiles):
        rows = rows_ref[pl.ds(tile, 8, stride=tiles), :]
        cells += [rows[:, :64], rows[:, 64:]]
    lifted = dot(jnp.concatenate(cells, axis=0).astype(BF16), up_ref[...])
    lifted = lifted.astype(BF16).astype(F32)
    first = 4 * CUBE * half
    for cell in range(4):
        b, c = cell // 2, cell % 2
        for sub in range(16):
            line = first + 8 * (sub // 4 * EDGE + 4 * b + sub % 4)
            volumes_ref[c, line : line + 8, :] = lifted[cell * 8 : cell * 8 + 8, sub * 128 : sub * 128 + 128]


def early_kernel(
    links_in, own_ref, up_ref, one_ref, two_ref,
    band_ref, back_ref, masks_ref, volumes_out,
    rows_ref, links_ref, links_sem,
):
    links_copy = pltpu.make_async_copy(links_in, links_ref, links_sem)
    links_copy.start()
    lift(own_ref, up_ref, rows_ref, volumes_out, 0)
    build_band(band_ref, weight_rows(one_ref[...].astype(F32)))
    build_band(back_ref, flipped_rows(two_ref[...].astype(F32)))
    links_copy.wait()
    put_masks(masks_ref, links_ref)


def put_padded(pad_ref, brick, lines, x_low, x_high, y_low, y_high, z_low, z_high):
    def joined(halves, before, after):
        lane = lanes_of(halves[0].shape)
        first = jnp.where(lane < CHANNELS, halves[1], before)
        second = jnp.where(lane >= HALF - CHANNELS, halves[0], after)
        return jnp.concatenate([halves[0], first], axis=-1), jnp.concatenate([halves[1], second], axis=-1)

    inside = joined(lines, z_low, z_high)
    x_low, x_high, y_low, y_high = [joined(face, 0.0, 0.0) for face in (x_low, x_high, y_low, y_high)]
    none = jnp.zeros((1, WIDE), F32)
    shifted = [[], [], []]
    for half in range(2):
        slabs = jnp.concatenate([x_low[half][None], inside[half], x_high[half][None]], axis=0)
        row = lax.broadcasted_iota(jnp.int32, slabs.shape, 1)
        low = jnp.concatenate([none, y_low[half], none], axis=0)[:, None, :]
        high = jnp.concatenate([none, y_high[half], none], axis=0)[:, None, :]
        shifted[0].append(jnp.where(row == 0, low, pltpu.roll(slabs, 1, 1)))
        shifted[1].append(slabs)
        shifted[2].append(jnp.where(row == EDGE - 1, high, pltpu.roll(slabs, EDGE - 1, 1)))
    for dy in range(3):
        pad_ref[dy, brick] = jnp.concatenate(shifted[dy], axis=1).astype(BF16)


def window(pad_ref, k):
    return pad_ref[k % 3, :, k // 3 : k // 3 + EDGE].reshape(ROWS, WIDE)


def convolve(pad_ref, band_ref):
    both, last = None, None
    for dy in range(3):
        slabs = pad_ref[dy, :, : EDGE + 1].reshape(-1, WIDE)
        term = dot(slabs, jnp.concatenate([band_ref[dy], band_ref[3 + dy]], axis=1))
        both = term if both is None else both + term
        term = dot(window(pad_ref, 6 + dy), band_ref[6 + dy])
        last = term if last is None else last + term
    both = both.reshape(BRICKS, EDGE + 1, 2 * EDGE, 2 * HALF)
    total = both[:, :EDGE, :, :HALF] + both[:, 1:, :, HALF:]
    return total.reshape(ROWS, HALF) + last


def half_lines(values):
    cube = values.reshape(BRICKS, EDGE, 2, EDGE, HALF)
    return [(cube[brick, :, 0], cube[brick, :, 1]) for brick in range(BRICKS)]


def put_halves(halves_ref, start, bricks):
    for brick, lines in enumerate(bricks):
        for half in range(2):
            first = start + brick * CUBE
            halves_ref[half, first : first + CUBE, :] = lines[half].reshape(CUBE, HALF)


def cotangent_lines(cotangent_ref):
    cube = cotangent_ref[...].astype(F32).reshape(BRICKS, EDGE, EDGE, LINE)
    return [(cube[brick, :, :, :HALF], cube[brick, :, :, HALF:]) for brick in range(BRICKS)]


def pack_faces(faces_ref, base, halves_ref, start, high):
    x_face = pair(halves_ref, start + ((EDGE - 1) * EDGE if high else 0), EDGE)
    y_face = pair(halves_ref, start + (EDGE - 1 if high else 0), EDGE, EDGE)
    for half in range(2):
        lanes = slice(half * HALF, half * HALF + HALF)
        faces_ref[base : base + EDGE, lanes] = x_face[half]
        faces_ref[base + EDGE : base + 2 * EDGE, lanes] = y_face[half]
    tile = halves_ref[1 if high else 0, start : start + CUBE, :]
    lane = lanes_of((16, 128)) // CHANNELS
    packed = jnp.zeros((16, 128), F32)
    for part in range(4):
        shift = (part + 1 if high else part) % 4 * CHANNELS
        piece = tile[part * 16 : part * 16 + 16]
        packed = jnp.where(lane == part, pltpu.roll(piece, shift, 1) if shift else piece, packed)
    faces_ref[base + 2 * EDGE : base + FACE, :128] = packed[:8]
    faces_ref[base + 2 * EDGE : base + FACE, 128:] = packed[8:]


def pack_all(bricks, halves_ref, faces_ref, high_out, low_out):
    put_halves(halves_ref, 0, bricks)
    for high, out_ref in ((True, high_out), (False, low_out)):
        for brick in range(BRICKS):
            pack_faces(faces_ref, brick * FACE, halves_ref, brick * CUBE, high)
        out_ref[...] = faces_ref[...].astype(BF16)


def to_partners(high_ref, low_ref, far_out, near_out):
    even = lax.axis_index("space") % 2 == 0
    far_out[...] = jnp.where(even, low_ref[...], high_ref[...])
    near_out[...] = jnp.where(even, high_ref[...], low_ref[...])


def faces_kernel(cotangent_ref, high_out, low_out, far_out, near_out, halves_ref, faces_ref):
    pack_all(cotangent_lines(cotangent_ref), halves_ref, faces_ref, high_out, low_out)
    to_partners(high_out, low_out, far_out, near_out)


def unpack_depth(halves, high):
    packed = jnp.concatenate(halves, axis=0)
    pieces = []
    for part in range(4):
        shift = ((3 - part) if high else (4 - part)) % 4 * CHANNELS
        pieces.append(pltpu.roll(packed, shift, 1) if shift else packed)
    return jnp.concatenate(pieces, axis=0).reshape(EDGE, EDGE, 128)


def first_kernel(
    links_in, other_ref, up_ref, band_ref, lifted_half,
    slope_out, hidden_out, turned_out, pad_out,
    volumes_ref, rows_ref, links_ref, links_sem,
):
    links_copy = pltpu.make_async_copy(links_in, links_ref, links_sem)
    links_copy.start()
    position = lax.axis_index("space")
    volumes_ref[:, : 4 * CUBE] = lifted_half[...]
    lift(other_ref, up_ref, rows_ref, volumes_ref, 1)
    links_copy.wait()
    for brick in range(BRICKS):

        def near(face):
            link = links_ref[0, brick, face]
            index = jnp.clip(link - BRICKS * (position - 1), 0, 3 * BRICKS - 1)
            return index, jnp.where(link >= 0, 1.0, 0.0).astype(F32)

        def x_face(face):
            index, present = near(face)
            line = EDGE * (EDGE - 1) if face % 2 == 0 else 0
            return [half * present for half in pair(volumes_ref, line * 8 + index, EDGE, 8)]

        def y_face(face):
            index, present = near(face)
            line = EDGE - 1 if face % 2 == 0 else 0
            return [half * present for half in pair(volumes_ref, line * 8 + index, EDGE, 8 * EDGE)]

        def z_face(face):
            index, present = near(face)
            tile = volumes_ref[1 if face % 2 == 0 else 0, pl.ds(index, CUBE, stride=8), :] * present
            return tile.reshape(EDGE, EDGE, HALF)

        own = [half.reshape(EDGE, EDGE, HALF) for half in pair(volumes_ref, BRICKS + brick, CUBE, 8)]
        put_padded(pad_out, brick, own, x_face(0), x_face(1), y_face(2), y_face(3), z_face(4), z_face(5))
    pre = convolve(pad_out, band_ref)
    sigmoid = 1.0 / (1.0 + jnp.exp(-pre))
    hidden = (pre * sigmoid).astype(BF16)
    slope_out[...] = sigmoid * (1.0 + pre * (1.0 - sigmoid))
    hidden_out[...] = hidden
    hidden = hidden.astype(F32)
    turned_out[...] = jnp.transpose(hidden).astype(BF16)


def hidden_faces_kernel(hidden_ref, _parts, high_out, low_out, far_out, near_out, halves_ref, faces_ref):
    pack_all(half_lines(hidden_ref[...].astype(F32)), halves_ref, faces_ref, high_out, low_out)
    to_partners(high_out, low_out, far_out, near_out)


def picked(outer, places):
    lane = lanes_of((CHANNELS, 128)) // CHANNELS
    found = None
    for block in range(4):
        start, tile = places[block]
        rows = outer[start : start + CHANNELS, tile * 128 : tile * 128 + 128]
        found = rows if found is None else jnp.where(lane == block, rows, found)
    return found


def fold(four):
    lane = lanes_of((CHANNELS, 128)) // CHANNELS
    total = None
    for turn in range(4):
        mixed = four[0]
        for n in range(1, len(four)):
            mixed = jnp.where(lane == (n + turn) % 4, four[n], mixed)
        if turn:
            mixed = pltpu.roll(mixed, 128 - turn * CHANNELS, 1)
        total = mixed if total is None else total + mixed
    return total


def diagonal(shift):
    places = [None] * 4
    for z in range(4):
        other = z + shift
        places[other % 4] = (z * CHANNELS, 0 if 0 <= other < 4 else 1)
    return places


def put_masks(masks_ref, links_ref):
    position = lax.axis_index("space")
    for brick in range(BRICKS):
        for face in range(6):
            first = links_ref[0, brick, face] - BRICKS * (position - 1 if face % 2 == 0 else position)
            for i in range(2 * BRICKS):
                row = (brick * 6 + face) * 2 * BRICKS + i
                masks_ref[row : row + 1, :] = jnp.full((1, 128), jnp.where(first == i, 1.0, 0.0).astype(F32))


def pad_all(pad_ref, bricks, masks_ref, high_pool, low_pool, high_own, low_own, far, near):
    position = lax.axis_index("space")
    half = BRICKS * FACE
    even = position % 2 == 0
    high_pool[0:half] = jnp.where(even, far[...], near[...]).astype(F32)
    high_pool[half:] = high_own[...].astype(F32)
    low_pool[0:half] = low_own[...].astype(F32)
    low_pool[half:] = jnp.where(even, near[...], far[...]).astype(F32)
    for brick, lines in enumerate(bricks):

        def face(number, axis):
            pool = high_pool if number % 2 == 0 else low_pool
            total = [0.0, 0.0]
            for i in range(2 * BRICKS):
                row = (brick * 6 + number) * 2 * BRICKS + i
                mask = masks_ref[row : row + 1, :]
                start = i * FACE + axis * EDGE
                for part in range(2):
                    found = pool[start : start + EDGE, part * HALF : part * HALF + HALF]
                    total[part] = total[part] + found * mask
            return total

        put_padded(
            pad_ref, brick, lines, face(0, 0), face(1, 0), face(2, 1), face(3, 1),
            unpack_depth(face(4, 2), True), unpack_depth(face(5, 2), False),
        )


def second_kernel(
    masks_ref, cotangent_ref, band_ref, slope_ref, hidden_ref, lifted_pad, high_own, low_own, far, near,
    sums_out, lifted_out,
    high_pool, low_pool, cotangent_pad, sums_ref,
):
    lifted_out[...] = window(lifted_pad, 4)[:, :HALF]
    bricks = cotangent_lines(cotangent_ref)
    pad_all(cotangent_pad, bricks, masks_ref, high_pool, low_pool, high_own, low_own, far, near)
    gradient = (convolve(cotangent_pad, band_ref) * slope_ref[...]).astype(BF16)
    gradient = jnp.transpose(gradient.astype(F32)).astype(BF16)
    hidden = hidden_ref[...]
    if sums_ref.shape[0] > 2 * GROUPS * CHANNELS:
        rest = sums_ref.shape[0] - 2 * GROUPS * CHANNELS
        sums_ref[2 * GROUPS * CHANNELS :] = jnp.zeros((rest, 128), F32)
    ones, twos = [], []
    for k in range(9):
        one = dot(gradient, window(lifted_pad, k))
        two = dot(hidden, window(cotangent_pad, 8 - k))
        ones += [picked(one, diagonal(part - 1)) for part in range(3)]
        twos += [picked(two, diagonal(1 - part)) for part in range(3)]
        while len(ones) >= 4 or (k == 8 and ones):
            group = (3 * k + 3 - len(ones)) // 4
            for first, blocks in ((0, ones), (GROUPS, twos)):
                start = (first + group) * CHANNELS
                sums_ref[start : start + CHANNELS] = fold(blocks[:4])
            ones, twos = ones[4:], twos[4:]
    sums_out[...] = sums_ref[...].astype(BF16)


def fine_kernel(
    masks_ref, band_ref, lifted_ref, hidden_ref, high_own, low_own, far, near,
    fine_out, high_pool, low_pool, hidden_pad,
):
    bricks = half_lines(hidden_ref[...].astype(F32))
    pad_all(hidden_pad, bricks, masks_ref, high_pool, low_pool, high_own, low_own, far, near)
    fine = lifted_ref[...].astype(F32) + convolve(hidden_pad, band_ref)
    fine = fine.reshape(LINES // EDGE, 2, EDGE, HALF)
    fine = jnp.concatenate([fine[:, 0], fine[:, 1]], axis=-1)
    fine_out[...] = fine.astype(BF16).reshape(fine_out.shape)


def sum_kernel(devices, scale, parts_ref, out_hbm, rows_ref, shares_ref, sems):
    rows_ref[...] = parts_ref[...].astype(F32)
    share = rows_ref.shape[0] // devices
    pieces = [rows_ref[share * i : share * i + share] for i in range(devices)]
    while len(pieces) > 1:
        pairs = [a + b for a, b in zip(pieces[::2], pieces[1::2])]
        pieces = pairs + pieces[len(pieces) - len(pieces) % 2 :]
    total = pieces[0] * scale
    some = shares_ref.shape[0]
    for i in range(some // share):
        rows_ref[share * i : share * i + share] = total
    shares_ref[...] = rows_ref[0:some].astype(BF16)
    copies = []
    for i in range(out_hbm.shape[0] // some):
        copies.append(pltpu.make_async_copy(shares_ref, out_hbm.at[pl.ds(some * i, some)], sems.at[i]))
        copies[-1].start()
    for copy in copies:
        copy.wait()


def unpack_kernel(sums_ref, fine_ref, one_out, two_out, fine_out, rows_ref, one_ref, two_ref, sems, fine_sem):
    fine_copy = pltpu.make_async_copy(fine_ref, fine_out, fine_sem)
    fine_copy.start()
    rows_ref[...] = sums_ref[...].astype(F32)
    copies = []
    for which, (block_ref, out) in ((1, (two_ref, two_out)), (0, (one_ref, one_out))):
        for part, (first, last) in enumerate(((0, 2), (2, 4), (4, GROUPS))):
            for group in range(first, last):
                start = (which * GROUPS + group) * CHANNELS
                four = rows_ref[start : start + CHANNELS]
                turned = None if which else jnp.transpose(four)
                for n in range(min(4, 27 - 4 * group)):
                    if which:
                        block = pltpu.roll(four, 128 - n * CHANNELS, 1) if n else four
                        block_ref[4 * group + n] = block[:, :CHANNELS]
                    else:
                        block_ref[4 * group + n] = turned[CHANNELS * n : CHANNELS * n + CHANNELS]
            span = pl.ds(4 * first, min(4 * last, 27) - 4 * first)
            copies.append(pltpu.make_async_copy(block_ref.at[span], out.at[span], sems.at[which, part]))
            copies[-1].start()
    for copy in copies:
        copy.wait()
    fine_copy.wait()


def call(kernel, out_shape, scratch=(), hbm=(), inputs=1, limit=24, cost=None, out=pltpu.VMEM):
    spaces = [pl.ANY if i in hbm else pltpu.VMEM for i in range(inputs)]
    return pl.pallas_call(
        kernel,
        out_shape=out_shape,
        in_specs=[pl.BlockSpec(memory_space=space) for space in spaces],
        out_specs=jax.tree.map(lambda _: pl.BlockSpec(memory_space=out), out_shape),
        scratch_shapes=list(scratch),
        compiler_params=pltpu.CompilerParams(vmem_limit_bytes=limit * 2**20),
        cost_estimate=cost,
    )


def shape(*dims, dtype=BF16):
    return jax.ShapeDtypeStruct(dims, dtype)


def kept_in_hbm(value):
    return pltpu.with_memory_space_constraint(value, pltpu.HBM)


def swapped(value, first):
    pairs = [(i, i + 1) for i in range(first, lax.axis_size("space") - 1, 2)]
    return lax.ppermute(value, "space", pairs + [(target, source) for source, target in pairs])


def exchanged(rows, axes=("space", "dp")):
    count = math.prod(lax.axis_size(axis) for axis in axes)
    shares = rows.reshape(count, -1, 2, 128)
    shares = lax.all_to_all(shares, axes, split_axis=0, concat_axis=0, tiled=True)
    return shares.reshape(rows.shape)


def body(coarse_latents, active_blocks, face_links, cotangent, up_weight, conv_one, conv_two):
    devices = lax.axis_size("space")
    everyone = devices * lax.axis_size("dp")
    held, width = coarse_latents.shape[1:]
    bricks = active_blocks.shape[1]
    split = lax.axis_size("dp") == 2
    tiles = width // 256
    count = 3 * BRICKS * tiles
    blocks = (2 * devices * count, 128)
    extras = (up_weight, conv_one, conv_two, face_links)
    packed, up_weight, conv_one, conv_two, face_links = call(
        functools.partial(pick_kernel, split, len(extras)),
        (shape(*blocks), *[shape(*extra.shape, dtype=extra.dtype) for extra in extras]),
        [
            pltpu.VMEM((1, bricks), jnp.int32),
            pltpu.VMEM((1, held, width), BF16),
            pltpu.VMEM((2, (bricks + 16) * tiles, 128), F32),
            pltpu.VMEM(blocks, F32),
            pltpu.SemaphoreType.DMA((2 + len(extras),)),
        ],
        hbm=range(2 + len(extras)),
        inputs=2 + len(extras),
    )(*[kept_in_hbm(operand) for operand in (active_blocks, coarse_latents, *extras)])
    received = exchanged(packed, ("space", "dp") if split else ("space",))
    window_half = shape(8 * tiles, 128)
    own, other = call(
        functools.partial(relay_kernel, split), (window_half, window_half), [pltpu.VMEM(blocks, F32)]
    )(received)
    if split:
        other = lax.ppermute(other, "dp", [(0, 1), (1, 0)])
    cost = pl.CostEstimate(flops=10**9, bytes_accessed=2 * 10**6, transcendentals=0)
    face = shape(BRICKS * FACE, LINE)
    halves = pltpu.VMEM((2, LINES, HALF), F32)
    faces = pltpu.VMEM((BRICKS * FACE, LINE), F32)
    pool = pltpu.VMEM((2 * BRICKS * FACE, LINE), F32)
    volume = shape(ROWS, HALF)
    links = [pltpu.SMEM(face_links.shape, jnp.int32), pltpu.SemaphoreType.DMA]
    pad_shape = (3, BRICKS, EDGE + 2, 2 * EDGE, WIDE)
    pad = pltpu.VMEM(pad_shape, BF16)
    high, low, far, near = call(faces_kernel, (face,) * 4, [halves, faces])(cotangent)
    far = swapped(far, 1)
    near = swapped(near, 0)
    masks = shape(BRICKS * 6 * 2 * BRICKS, 128, dtype=F32)
    lifted_half = shape(2, 4 * CUBE, 128, dtype=F32)
    window_rows = pltpu.VMEM((8 * tiles, 128), F32)
    band_one, band_back, masks, lifted_half = call(
        early_kernel,
        (shape(*BAND), shape(*BAND), masks, lifted_half),
        [window_rows, *links],
        hbm=(0,),
        inputs=5,
        cost=cost,
    )(face_links, own, up_weight, conv_one, conv_two)
    slope, hidden, turned, lifted_pad = call(
        first_kernel,
        (
            shape(ROWS, HALF, dtype=F32), volume, shape(HALF, ROWS), shape(*pad_shape),
        ),
        [pltpu.VMEM((2, 8 * CUBE, 128), F32), window_rows, *links],
        hbm=(0,),
        inputs=5,
    )(face_links, other, up_weight, band_one, lifted_half)
    share = 2 * -(-GROUPS * CHANNELS // everyone)
    packed_rows = (everyone * share, 128)
    sums, lifted = call(
        second_kernel,
        (shape(*packed_rows), volume),
        [pool, pool, pad, pltpu.VMEM(packed_rows, F32)],
        inputs=10,
    )(masks, cotangent, band_back, slope, turned, lifted_pad, high, low, far, near)
    parts = exchanged(sums)
    hidden_high, hidden_low, hidden_far, hidden_near = call(
        hidden_faces_kernel, (face,) * 4, [halves, faces], hbm=(1,), inputs=2
    )(hidden, parts)
    hidden_far = swapped(hidden_far, 1)
    hidden_near = swapped(hidden_near, 0)
    band_two = call(band_kernel, shape(*BAND), cost=cost)(conv_two)
    fine = call(fine_kernel, shape(*cotangent.shape), [pool, pool, pad], inputs=8, cost=cost)(
        masks, band_two, lifted, hidden, hidden_high, hidden_low, hidden_far, hidden_near
    )
    scale = 1.0 / math.sqrt(lax.axis_size("dp") * devices * BRICKS * EDGE**3)
    times = 4 if everyone % 32 == 0 else 1
    total = call(
        functools.partial(sum_kernel, everyone, scale),
        shape(*packed_rows),
        [
            pltpu.VMEM(packed_rows, F32),
            pltpu.VMEM((packed_rows[0] // times, 128), BF16),
            pltpu.SemaphoreType.DMA((times,)),
        ],
        out=pl.ANY,
    )(parts)
    gathered = exchanged(total)
    grads = shape(27, CHANNELS, CHANNELS, dtype=F32)
    block = pltpu.VMEM(grads.shape, F32)
    scratch = [pltpu.VMEM(packed_rows, F32), block, block]
    scratch += [pltpu.SemaphoreType.DMA((2, 3)), pltpu.SemaphoreType.DMA]
    grad_one, grad_two, fine = call(
        unpack_kernel, (grads, grads, shape(*fine.shape)), scratch, inputs=2, out=pl.ANY
    )(gathered, fine)
    return (fine, grad_one, grad_two)


def solution(mesh):
    return jax.shard_map(
        body,
        mesh=mesh,
        in_specs=(
            P("dp", "space", None),
            P("dp", None),
            P("dp", "space", None),
            P("dp", "space", None, None, None),
            P(),
            P(),
            P(),
        ),
        out_specs=(P("dp", "space", None, None, None), P(), P()),
        check_vma=False,
    )
```

```python
import functools
import math

import jax
import jax.numpy as jnp
from jax import lax
from jax.experimental import pallas as pl
from jax.experimental.pallas import tpu as pltpu
from jax.sharding import PartitionSpec as P

BF16 = jnp.bfloat16
F32 = jnp.float32
EDGE = 8
CHANNELS = 32
LINE = EDGE * CHANNELS
HALF = LINE // 2
WIDE = 2 * HALF
BRICKS = 2
CUBE = EDGE * EDGE
LINES = BRICKS * CUBE
BAND = (9, WIDE, HALF)
ROWS = 2 * LINES
FACE = 3 * EDGE
GROUPS = 7


def dot(left, right):
    return jnp.dot(left, right, preferred_element_type=F32)


def dot_rows(left, right):
    return lax.dot_general(left, right, (((0,), (0,)), ((), ())), preferred_element_type=F32)


def pair(halves_ref, start, count, stride=1):
    index = pl.ds(start, count, stride=stride) if stride > 1 else pl.ds(start, count)
    return halves_ref[0, index, :], halves_ref[1, index, :]


def lanes_of(shape):
    return lax.broadcasted_iota(jnp.int32, shape, len(shape) - 1)


def first_half(split):
    return lax.axis_index("dp") if split else 0


def pick_kernel(split, extras, ids_hbm, latents_hbm, *refs):
    brought = zip(refs[:extras], refs[extras + 1 : 2 * extras + 1])
    out_ref = refs[extras]
    ids_ref, latents_ref, rows_ref, blocks_ref, sems = refs[2 * extras + 1 :]
    ids_copy = pltpu.make_async_copy(ids_hbm, ids_ref, sems.at[0])
    latents_copy = pltpu.make_async_copy(latents_hbm, latents_ref, sems.at[1])
    ids_copy.start()
    latents_copy.start()
    others = [pltpu.make_async_copy(*pair, sems.at[2 + i]) for i, pair in enumerate(brought)]
    for copy in others:
        copy.start()
    held, width = latents_ref.shape[1:]
    bricks = ids_ref.shape[1]
    tiles = width // 256
    margin = 8 * tiles
    empty = jnp.zeros((margin, 128), F32)
    for half in range(2):
        rows_ref[half, 0:margin] = empty
        rows_ref[half, margin + bricks * tiles :] = empty
    first = lax.axis_index("space") * held
    rows = lax.broadcasted_iota(jnp.int32, (held, bricks), 0) + first
    ids_copy.wait()
    hot = jnp.where(rows == ids_ref[...], 1.0, 0.0).astype(BF16)
    latents_copy.wait()
    picked = dot_rows(hot, latents_ref[0])
    for tile in range(2 * tiles):
        place = pl.ds(margin + tile % tiles, bricks, stride=tiles)
        rows_ref[tile // tiles, place, :] = picked[:, tile * 128 : tile * 128 + 128]
    count = 3 * BRICKS * tiles
    straight = first_half(split) == 0
    for receiver in range(blocks_ref.shape[0] // (2 * count)):
        start = margin + BRICKS * (receiver - 1) * tiles
        halves = [rows_ref[half, start : start + count] for half in range(2)]
        for half in range(2):
            block = jnp.where(straight, halves[half], halves[1 - half]) if split else halves[half]
            place = (2 * receiver + half) * count
            blocks_ref[place : place + count] = block
    out_ref[...] = blocks_ref[...].astype(BF16)
    for copy in others:
        copy.wait()


def relay_kernel(split, received_ref, own_out, other_out, rows_ref):
    rows_ref[...] = received_ref[...].astype(F32)
    count = own_out.shape[0] * 3 // 4
    sums = []
    for half in range(2):
        total = None
        for start in range(half * count, rows_ref.shape[0], 2 * count):
            piece = rows_ref[start : start + count]
            total = piece if total is None else total + piece
        sums.append(jnp.concatenate([total, jnp.zeros((count // 3, 128), F32)], axis=0))
    straight = first_half(split) == 0
    own_out[...] = jnp.where(straight, sums[0], sums[1]).astype(BF16)
    other_out[...] = jnp.where(straight, sums[1], sums[0]).astype(BF16)


def build_band(band_ref, rows):
    shape = (3 * CHANNELS, HALF)
    row = lax.broadcasted_iota(jnp.int32, shape, 0)
    target = CHANNELS - (row // CHANNELS) * CHANNELS + row % CHANNELS
    distance = lanes_of(shape) - target
    band_ref[:, HALF:, :] = jnp.zeros((9, HALF, HALF), BF16)
    for z in range(-1, 5):
        select = jnp.where(distance == z * CHANNELS, 1.0, 0.0).astype(BF16)
        block = dot(rows, select).astype(BF16)
        start = z % 8 * CHANNELS
        band_ref[:, start : start + CHANNELS, :] = block.reshape(9, CHANNELS, HALF)


def weight_rows(weights):
    cube = weights.reshape(9, 3, CHANNELS, CHANNELS)
    rows = jnp.concatenate([cube[:, 0], cube[:, 1], cube[:, 2]], axis=-1)
    return rows.reshape(9 * CHANNELS, 3 * CHANNELS).astype(BF16)


def flipped_rows(weights):
    cube = jnp.swapaxes(weights, 1, 2).reshape(9, 3, CHANNELS, CHANNELS)
    pieces = [jnp.concatenate([cube[8 - k, 2], cube[8 - k, 1], cube[8 - k, 0]], axis=-1) for k in range(9)]
    return jnp.concatenate(pieces, axis=0).astype(BF16)


def band_kernel(weights_ref, band_ref):
    build_band(band_ref, weight_rows(weights_ref[...].astype(F32)))


def lift(half_ref, up_ref, rows_ref, volumes_ref, half):
    tiles = half_ref.shape[0] // 8
    rows_ref[...] = half_ref[...].astype(F32)
    cells = []
    for tile in range(tiles):
        rows = rows_ref[pl.ds(tile, 8, stride=tiles), :]
        cells += [rows[:, :64], rows[:, 64:]]
    lifted = dot(jnp.concatenate(cells, axis=0).astype(BF16), up_ref[...])
    lifted = lifted.astype(BF16).astype(F32)
    first = 4 * CUBE * half
    for cell in range(4):
        b, c = cell // 2, cell % 2
        for sub in range(16):
            line = first + 8 * (sub // 4 * EDGE + 4 * b + sub % 4)
            volumes_ref[c, line : line + 8, :] = lifted[cell * 8 : cell * 8 + 8, sub * 128 : sub * 128 + 128]


def early_kernel(
    links_in, own_ref, up_ref, one_ref, two_ref,
    band_ref, back_ref, masks_ref, volumes_out,
    rows_ref, links_ref, links_sem,
):
    links_copy = pltpu.make_async_copy(links_in, links_ref, links_sem)
    links_copy.start()
    lift(own_ref, up_ref, rows_ref, volumes_out, 0)
    build_band(band_ref, weight_rows(one_ref[...].astype(F32)))
    build_band(back_ref, flipped_rows(two_ref[...].astype(F32)))
    links_copy.wait()
    put_masks(masks_ref, links_ref)


def put_padded(pad_ref, brick, lines, x_low, x_high, y_low, y_high, z_low, z_high):
    def joined(halves, before, after):
        lane = lanes_of(halves[0].shape)
        first = jnp.where(lane < CHANNELS, halves[1], before)
        second = jnp.where(lane >= HALF - CHANNELS, halves[0], after)
        return jnp.concatenate([halves[0], first], axis=-1), jnp.concatenate([halves[1], second], axis=-1)

    inside = joined(lines, z_low, z_high)
    x_low, x_high, y_low, y_high = [joined(face, 0.0, 0.0) for face in (x_low, x_high, y_low, y_high)]
    none = jnp.zeros((1, WIDE), F32)
    shifted = [[], [], []]
    for half in range(2):
        slabs = jnp.concatenate([x_low[half][None], inside[half], x_high[half][None]], axis=0)
        row = lax.broadcasted_iota(jnp.int32, slabs.shape, 1)
        low = jnp.concatenate([none, y_low[half], none], axis=0)[:, None, :]
        high = jnp.concatenate([none, y_high[half], none], axis=0)[:, None, :]
        shifted[0].append(jnp.where(row == 0, low, pltpu.roll(slabs, 1, 1)))
        shifted[1].append(slabs)
        shifted[2].append(jnp.where(row == EDGE - 1, high, pltpu.roll(slabs, EDGE - 1, 1)))
    for dy in range(3):
        pad_ref[dy, brick] = jnp.concatenate(shifted[dy], axis=1).astype(BF16)


def window(pad_ref, k):
    return pad_ref[k % 3, :, k // 3 : k // 3 + EDGE].reshape(ROWS, WIDE)


def convolve(pad_ref, band_ref):
    both, last = None, None
    for dy in range(3):
        slabs = pad_ref[dy, :, : EDGE + 1].reshape(-1, WIDE)
        term = dot(slabs, jnp.concatenate([band_ref[dy], band_ref[3 + dy]], axis=1))
        both = term if both is None else both + term
        term = dot(window(pad_ref, 6 + dy), band_ref[6 + dy])
        last = term if last is None else last + term
    both = both.reshape(BRICKS, EDGE + 1, 2 * EDGE, 2 * HALF)
    total = both[:, :EDGE, :, :HALF] + both[:, 1:, :, HALF:]
    return total.reshape(ROWS, HALF) + last


def half_lines(values):
    cube = values.reshape(BRICKS, EDGE, 2, EDGE, HALF)
    return [(cube[brick, :, 0], cube[brick, :, 1]) for brick in range(BRICKS)]


def put_halves(halves_ref, start, bricks):
    for brick, lines in enumerate(bricks):
        for half in range(2):
            first = start + brick * CUBE
            halves_ref[half, first : first + CUBE, :] = lines[half].reshape(CUBE, HALF)


def cotangent_lines(cotangent_ref):
    cube = cotangent_ref[...].astype(F32).reshape(BRICKS, EDGE, EDGE, LINE)
    return [(cube[brick, :, :, :HALF], cube[brick, :, :, HALF:]) for brick in range(BRICKS)]


def pack_faces(faces_ref, base, halves_ref, start, high):
    x_face = pair(halves_ref, start + ((EDGE - 1) * EDGE if high else 0), EDGE)
    y_face = pair(halves_ref, start + (EDGE - 1 if high else 0), EDGE, EDGE)
    for half in range(2):
        lanes = slice(half * HALF, half * HALF + HALF)
        faces_ref[base : base + EDGE, lanes] = x_face[half]
        faces_ref[base + EDGE : base + 2 * EDGE, lanes] = y_face[half]
    tile = halves_ref[1 if high else 0, start : start + CUBE, :]
    lane = lanes_of((16, 128)) // CHANNELS
    packed = jnp.zeros((16, 128), F32)
    for part in range(4):
        shift = (part + 1 if high else part) % 4 * CHANNELS
        piece = tile[part * 16 : part * 16 + 16]
        packed = jnp.where(lane == part, pltpu.roll(piece, shift, 1) if shift else piece, packed)
    faces_ref[base + 2 * EDGE : base + FACE, :128] = packed[:8]
    faces_ref[base + 2 * EDGE : base + FACE, 128:] = packed[8:]


def pack_all(bricks, halves_ref, faces_ref, high_out, low_out):
    put_halves(halves_ref, 0, bricks)
    for high, out_ref in ((True, high_out), (False, low_out)):
        for brick in range(BRICKS):
            pack_faces(faces_ref, brick * FACE, halves_ref, brick * CUBE, high)
        out_ref[...] = faces_ref[...].astype(BF16)


def to_partners(high_ref, low_ref, far_out, near_out):
    even = lax.axis_index("space") % 2 == 0
    far_out[...] = jnp.where(even, low_ref[...], high_ref[...])
    near_out[...] = jnp.where(even, high_ref[...], low_ref[...])


def faces_kernel(cotangent_ref, high_out, low_out, far_out, near_out, halves_ref, faces_ref):
    pack_all(cotangent_lines(cotangent_ref), halves_ref, faces_ref, high_out, low_out)
    to_partners(high_out, low_out, far_out, near_out)


def unpack_depth(halves, high):
    packed = jnp.concatenate(halves, axis=0)
    pieces = []
    for part in range(4):
        shift = ((3 - part) if high else (4 - part)) % 4 * CHANNELS
        pieces.append(pltpu.roll(packed, shift, 1) if shift else packed)
    return jnp.concatenate(pieces, axis=0).reshape(EDGE, EDGE, 128)


def first_kernel(
    links_in, other_ref, up_ref, band_ref, lifted_half,
    slope_out, hidden_out, turned_out, pad_out,
    volumes_ref, rows_ref, links_ref, links_sem,
):
    links_copy = pltpu.make_async_copy(links_in, links_ref, links_sem)
    links_copy.start()
    position = lax.axis_index("space")
    volumes_ref[:, : 4 * CUBE] = lifted_half[...]
    lift(other_ref, up_ref, rows_ref, volumes_ref, 1)
    links_copy.wait()
    for brick in range(BRICKS):

        def near(face):
            link = links_ref[0, brick, face]
            index = jnp.clip(link - BRICKS * (position - 1), 0, 3 * BRICKS - 1)
            return index, jnp.where(link >= 0, 1.0, 0.0).astype(F32)

        def x_face(face):
            index, present = near(face)
            line = EDGE * (EDGE - 1) if face % 2 == 0 else 0
            return [half * present for half in pair(volumes_ref, line * 8 + index, EDGE, 8)]

        def y_face(face):
            index, present = near(face)
            line = EDGE - 1 if face % 2 == 0 else 0
            return [half * present for half in pair(volumes_ref, line * 8 + index, EDGE, 8 * EDGE)]

        def z_face(face):
            index, present = near(face)
            tile = volumes_ref[1 if face % 2 == 0 else 0, pl.ds(index, CUBE, stride=8), :] * present
            return tile.reshape(EDGE, EDGE, HALF)

        own = [half.reshape(EDGE, EDGE, HALF) for half in pair(volumes_ref, BRICKS + brick, CUBE, 8)]
        put_padded(pad_out, brick, own, x_face(0), x_face(1), y_face(2), y_face(3), z_face(4), z_face(5))
    pre = convolve(pad_out, band_ref)
    sigmoid = 1.0 / (1.0 + jnp.exp(-pre))
    hidden = (pre * sigmoid).astype(BF16)
    slope_out[...] = sigmoid * (1.0 + pre * (1.0 - sigmoid))
    hidden_out[...] = hidden
    hidden = hidden.astype(F32)
    turned_out[...] = jnp.transpose(hidden).astype(BF16)


def hidden_faces_kernel(hidden_ref, _parts, high_out, low_out, far_out, near_out, halves_ref, faces_ref):
    pack_all(half_lines(hidden_ref[...].astype(F32)), halves_ref, faces_ref, high_out, low_out)
    to_partners(high_out, low_out, far_out, near_out)


def picked(outer, places):
    lane = lanes_of((CHANNELS, 128)) // CHANNELS
    found = None
    for block in range(4):
        start, tile = places[block]
        rows = outer[start : start + CHANNELS, tile * 128 : tile * 128 + 128]
        found = rows if found is None else jnp.where(lane == block, rows, found)
    return found


def fold(four):
    lane = lanes_of((CHANNELS, 128)) // CHANNELS
    total = None
    for turn in range(4):
        mixed = four[0]
        for n in range(1, len(four)):
            mixed = jnp.where(lane == (n + turn) % 4, four[n], mixed)
        if turn:
            mixed = pltpu.roll(mixed, 128 - turn * CHANNELS, 1)
        total = mixed if total is None else total + mixed
    return total


def diagonal(shift):
    places = [None] * 4
    for z in range(4):
        other = z + shift
        places[other % 4] = (z * CHANNELS, 0 if 0 <= other < 4 else 1)
    return places


def put_masks(masks_ref, links_ref):
    position = lax.axis_index("space")
    for brick in range(BRICKS):
        for face in range(6):
            first = links_ref[0, brick, face] - BRICKS * (position - 1 if face % 2 == 0 else position)
            for i in range(2 * BRICKS):
                row = (brick * 6 + face) * 2 * BRICKS + i
                masks_ref[row : row + 1, :] = jnp.full((1, 128), jnp.where(first == i, 1.0, 0.0).astype(F32))


def pad_all(pad_ref, bricks, masks_ref, high_pool, low_pool, high_own, low_own, far, near):
    position = lax.axis_index("space")
    half = BRICKS * FACE
    even = position % 2 == 0
    high_pool[0:half] = jnp.where(even, far[...], near[...]).astype(F32)
    high_pool[half:] = high_own[...].astype(F32)
    low_pool[0:half] = low_own[...].astype(F32)
    low_pool[half:] = jnp.where(even, near[...], far[...]).astype(F32)
    for brick, lines in enumerate(bricks):

        def face(number, axis):
            pool = high_pool if number % 2 == 0 else low_pool
            total = [0.0, 0.0]
            for i in range(2 * BRICKS):
                row = (brick * 6 + number) * 2 * BRICKS + i
                mask = masks_ref[row : row + 1, :]
                start = i * FACE + axis * EDGE
                for part in range(2):
                    found = pool[start : start + EDGE, part * HALF : part * HALF + HALF]
                    total[part] = total[part] + found * mask
            return total

        put_padded(
            pad_ref, brick, lines, face(0, 0), face(1, 0), face(2, 1), face(3, 1),
            unpack_depth(face(4, 2), True), unpack_depth(face(5, 2), False),
        )


def second_kernel(
    masks_ref, cotangent_ref, band_ref, slope_ref, hidden_ref, lifted_pad, high_own, low_own, far, near,
    sums_out, lifted_out,
    high_pool, low_pool, cotangent_pad, sums_ref,
):
    lifted_out[...] = window(lifted_pad, 4)[:, :HALF]
    bricks = cotangent_lines(cotangent_ref)
    pad_all(cotangent_pad, bricks, masks_ref, high_pool, low_pool, high_own, low_own, far, near)
    gradient = (convolve(cotangent_pad, band_ref) * slope_ref[...]).astype(BF16)
    gradient = jnp.transpose(gradient.astype(F32)).astype(BF16)
    hidden = hidden_ref[...]
    if sums_ref.shape[0] > 2 * GROUPS * CHANNELS:
        rest = sums_ref.shape[0] - 2 * GROUPS * CHANNELS
        sums_ref[2 * GROUPS * CHANNELS :] = jnp.zeros((rest, 128), F32)
    ones, twos = [], []
    for k in range(9):
        one = dot(gradient, window(lifted_pad, k))
        two = dot(hidden, window(cotangent_pad, 8 - k))
        ones += [picked(one, diagonal(part - 1)) for part in range(3)]
        twos += [picked(two, diagonal(1 - part)) for part in range(3)]
        while len(ones) >= 4 or (k == 8 and ones):
            group = (3 * k + 3 - len(ones)) // 4
            for first, blocks in ((0, ones), (GROUPS, twos)):
                start = (first + group) * CHANNELS
                sums_ref[start : start + CHANNELS] = fold(blocks[:4])
            ones, twos = ones[4:], twos[4:]
    sums_out[...] = sums_ref[...].astype(BF16)


def fine_kernel(
    masks_ref, band_ref, lifted_ref, hidden_ref, high_own, low_own, far, near,
    fine_out, high_pool, low_pool, hidden_pad,
):
    bricks = half_lines(hidden_ref[...].astype(F32))
    pad_all(hidden_pad, bricks, masks_ref, high_pool, low_pool, high_own, low_own, far, near)
    fine = lifted_ref[...].astype(F32) + convolve(hidden_pad, band_ref)
    fine = fine.reshape(LINES // EDGE, 2, EDGE, HALF)
    fine = jnp.concatenate([fine[:, 0], fine[:, 1]], axis=-1)
    fine_out[...] = fine.astype(BF16).reshape(fine_out.shape)


def sum_kernel(devices, scale, parts_ref, out_ref, rows_ref):
    rows_ref[...] = parts_ref[...].astype(F32)
    share = rows_ref.shape[0] // devices
    pieces = [rows_ref[share * i : share * i + share] for i in range(devices)]
    while len(pieces) > 1:
        pairs = [a + b for a, b in zip(pieces[::2], pieces[1::2])]
        pieces = pairs + pieces[len(pieces) - len(pieces) % 2 :]
    out_ref[...] = (pieces[0] * scale).astype(BF16)


def unpack_kernel(sums_ref, fine_ref, one_out, two_out, fine_out, rows_ref, one_ref, two_ref, sems, fine_sem):
    fine_copy = pltpu.make_async_copy(fine_ref, fine_out, fine_sem)
    fine_copy.start()
    rows_ref[...] = sums_ref[...].astype(F32)
    copies = []
    for which, (block_ref, out) in ((1, (two_ref, two_out)), (0, (one_ref, one_out))):
        for part, (first, last) in enumerate(((0, 2), (2, 4), (4, GROUPS))):
            for group in range(first, last):
                start = (which * GROUPS + group) * CHANNELS
                four = rows_ref[start : start + CHANNELS]
                turned = None if which else jnp.transpose(four)
                for n in range(min(4, 27 - 4 * group)):
                    if which:
                        block = pltpu.roll(four, 128 - n * CHANNELS, 1) if n else four
                        block_ref[4 * group + n] = block[:, :CHANNELS]
                    else:
                        block_ref[4 * group + n] = turned[CHANNELS * n : CHANNELS * n + CHANNELS]
            span = pl.ds(4 * first, min(4 * last, 27) - 4 * first)
            copies.append(pltpu.make_async_copy(block_ref.at[span], out.at[span], sems.at[which, part]))
            copies[-1].start()
    for copy in copies:
        copy.wait()
    fine_copy.wait()


def call(kernel, out_shape, scratch=(), hbm=(), inputs=1, limit=24, cost=None, out=pltpu.VMEM):
    spaces = [pl.ANY if i in hbm else pltpu.VMEM for i in range(inputs)]
    return pl.pallas_call(
        kernel,
        out_shape=out_shape,
        in_specs=[pl.BlockSpec(memory_space=space) for space in spaces],
        out_specs=jax.tree.map(lambda _: pl.BlockSpec(memory_space=out), out_shape),
        scratch_shapes=list(scratch),
        compiler_params=pltpu.CompilerParams(vmem_limit_bytes=limit * 2**20),
        cost_estimate=cost,
    )


def shape(*dims, dtype=BF16):
    return jax.ShapeDtypeStruct(dims, dtype)


def kept_in_hbm(value):
    return pltpu.with_memory_space_constraint(value, pltpu.HBM)


def swapped(value, first):
    pairs = [(i, i + 1) for i in range(first, lax.axis_size("space") - 1, 2)]
    return lax.ppermute(value, "space", pairs + [(target, source) for source, target in pairs])


def exchanged(rows, axes=("space", "dp")):
    count = math.prod(lax.axis_size(axis) for axis in axes)
    shares = rows.reshape(count, -1, 2, 128)
    shares = lax.all_to_all(shares, axes, split_axis=0, concat_axis=0, tiled=True)
    return shares.reshape(rows.shape)


def body(coarse_latents, active_blocks, face_links, cotangent, up_weight, conv_one, conv_two):
    devices = lax.axis_size("space")
    everyone = devices * lax.axis_size("dp")
    held, width = coarse_latents.shape[1:]
    bricks = active_blocks.shape[1]
    split = lax.axis_size("dp") == 2
    tiles = width // 256
    count = 3 * BRICKS * tiles
    blocks = (2 * devices * count, 128)
    extras = (up_weight, conv_one, conv_two, face_links)
    packed, up_weight, conv_one, conv_two, face_links = call(
        functools.partial(pick_kernel, split, len(extras)),
        (shape(*blocks), *[shape(*extra.shape, dtype=extra.dtype) for extra in extras]),
        [
            pltpu.VMEM((1, bricks), jnp.int32),
            pltpu.VMEM((1, held, width), BF16),
            pltpu.VMEM((2, (bricks + 16) * tiles, 128), F32),
            pltpu.VMEM(blocks, F32),
            pltpu.SemaphoreType.DMA((2 + len(extras),)),
        ],
        hbm=range(2 + len(extras)),
        inputs=2 + len(extras),
    )(*[kept_in_hbm(operand) for operand in (active_blocks, coarse_latents, *extras)])
    received = exchanged(packed, ("space", "dp") if split else ("space",))
    window_half = shape(8 * tiles, 128)
    own, other = call(
        functools.partial(relay_kernel, split), (window_half, window_half), [pltpu.VMEM(blocks, F32)]
    )(received)
    if split:
        other = lax.ppermute(other, "dp", [(0, 1), (1, 0)])
    cost = pl.CostEstimate(flops=10**9, bytes_accessed=2 * 10**6, transcendentals=0)
    face = shape(BRICKS * FACE, LINE)
    halves = pltpu.VMEM((2, LINES, HALF), F32)
    faces = pltpu.VMEM((BRICKS * FACE, LINE), F32)
    pool = pltpu.VMEM((2 * BRICKS * FACE, LINE), F32)
    volume = shape(ROWS, HALF)
    links = [pltpu.SMEM(face_links.shape, jnp.int32), pltpu.SemaphoreType.DMA]
    pad_shape = (3, BRICKS, EDGE + 2, 2 * EDGE, WIDE)
    pad = pltpu.VMEM(pad_shape, BF16)
    high, low, far, near = call(faces_kernel, (face,) * 4, [halves, faces])(cotangent)
    far = swapped(far, 1)
    near = swapped(near, 0)
    masks = shape(BRICKS * 6 * 2 * BRICKS, 128, dtype=F32)
    lifted_half = shape(2, 4 * CUBE, 128, dtype=F32)
    window_rows = pltpu.VMEM((8 * tiles, 128), F32)
    band_one, band_back, masks, lifted_half = call(
        early_kernel,
        (shape(*BAND), shape(*BAND), masks, lifted_half),
        [window_rows, *links],
        hbm=(0,),
        inputs=5,
        cost=cost,
    )(face_links, own, up_weight, conv_one, conv_two)
    slope, hidden, turned, lifted_pad = call(
        first_kernel,
        (
            shape(ROWS, HALF, dtype=F32), volume, shape(HALF, ROWS), shape(*pad_shape),
        ),
        [pltpu.VMEM((2, 8 * CUBE, 128), F32), window_rows, *links],
        hbm=(0,),
        inputs=5,
    )(face_links, other, up_weight, band_one, lifted_half)
    share = 2 * -(-GROUPS * CHANNELS // everyone)
    packed_rows = (everyone * share, 128)
    sums, lifted = call(
        second_kernel,
        (shape(*packed_rows), volume),
        [pool, pool, pad, pltpu.VMEM(packed_rows, F32)],
        inputs=10,
    )(masks, cotangent, band_back, slope, turned, lifted_pad, high, low, far, near)
    parts = exchanged(sums)
    hidden_high, hidden_low, hidden_far, hidden_near = call(
        hidden_faces_kernel, (face,) * 4, [halves, faces], hbm=(1,), inputs=2
    )(hidden, parts)
    hidden_far = swapped(hidden_far, 1)
    hidden_near = swapped(hidden_near, 0)
    band_two = call(band_kernel, shape(*BAND), cost=cost)(conv_two)
    fine = call(fine_kernel, shape(*cotangent.shape), [pool, pool, pad], inputs=8, cost=cost)(
        masks, band_two, lifted, hidden, hidden_high, hidden_low, hidden_far, hidden_near
    )
    scale = 1.0 / math.sqrt(lax.axis_size("dp") * devices * BRICKS * EDGE**3)
    total = call(
        functools.partial(sum_kernel, everyone, scale), shape(share, 128), [pltpu.VMEM(packed_rows, F32)]
    )(parts)
    gathered = lax.all_gather(total.reshape(-1, 2, 128), ("space", "dp"), tiled=True).reshape(packed_rows)
    grads = shape(27, CHANNELS, CHANNELS, dtype=F32)
    block = pltpu.VMEM(grads.shape, F32)
    scratch = [pltpu.VMEM(packed_rows, F32), block, block]
    scratch += [pltpu.SemaphoreType.DMA((2, 3)), pltpu.SemaphoreType.DMA]
    grad_one, grad_two, fine = call(
        unpack_kernel, (grads, grads, shape(*fine.shape)), scratch, inputs=2, out=pl.ANY
    )(gathered, fine)
    return (fine, grad_one, grad_two)


def solution(mesh):
    return jax.shard_map(
        body,
        mesh=mesh,
        in_specs=(
            P("dp", "space", None),
            P("dp", None),
            P("dp", "space", None),
            P("dp", "space", None, None, None),
            P(),
            P(),
            P(),
        ),
        out_specs=(P("dp", "space", None, None, None), P(), P()),
        check_vma=False,
    )
```

```python
import functools
import math

import jax
import jax.numpy as jnp
from jax import lax
from jax.experimental import pallas as pl
from jax.experimental.pallas import tpu as pltpu
from jax.sharding import PartitionSpec as P

BF16 = jnp.bfloat16
F32 = jnp.float32
EDGE = 8
CHANNELS = 32
LINE = EDGE * CHANNELS
HALF = LINE // 2
WIDE = 2 * HALF
BRICKS = 2
CUBE = EDGE * EDGE
LINES = BRICKS * CUBE
BAND = (9, WIDE, HALF)
ROWS = 2 * LINES
FACE = 3 * EDGE
GROUPS = 7


def dot(left, right):
    return jnp.dot(left, right, preferred_element_type=F32)


def dot_rows(left, right):
    return lax.dot_general(left, right, (((0,), (0,)), ((), ())), preferred_element_type=F32)


def pair(halves_ref, start, count, stride=1):
    index = pl.ds(start, count, stride=stride) if stride > 1 else pl.ds(start, count)
    return halves_ref[0, index, :], halves_ref[1, index, :]


def lanes_of(shape):
    return lax.broadcasted_iota(jnp.int32, shape, len(shape) - 1)


def first_half(split):
    return lax.axis_index("dp") if split else 0


def pick_kernel(split, extras, ids_hbm, latents_hbm, *refs):
    brought = zip(refs[:extras], refs[extras + 1 : 2 * extras + 1])
    out_ref = refs[extras]
    ids_ref, latents_ref, rows_ref, blocks_ref, sems = refs[2 * extras + 1 :]
    ids_copy = pltpu.make_async_copy(ids_hbm, ids_ref, sems.at[0])
    latents_copy = pltpu.make_async_copy(latents_hbm, latents_ref, sems.at[1])
    ids_copy.start()
    latents_copy.start()
    others = [pltpu.make_async_copy(*pair, sems.at[2 + i]) for i, pair in enumerate(brought)]
    for copy in others:
        copy.start()
    held, width = latents_ref.shape[1:]
    bricks = ids_ref.shape[1]
    tiles = width // 256
    margin = 8 * tiles
    empty = jnp.zeros((margin, 128), F32)
    for half in range(2):
        rows_ref[half, 0:margin] = empty
        rows_ref[half, margin + bricks * tiles :] = empty
    first = lax.axis_index("space") * held
    rows = lax.broadcasted_iota(jnp.int32, (held, bricks), 0) + first
    ids_copy.wait()
    hot = jnp.where(rows == ids_ref[...], 1.0, 0.0).astype(BF16)
    latents_copy.wait()
    picked = dot_rows(hot, latents_ref[0])
    for tile in range(2 * tiles):
        place = pl.ds(margin + tile % tiles, bricks, stride=tiles)
        rows_ref[tile // tiles, place, :] = picked[:, tile * 128 : tile * 128 + 128]
    count = 3 * BRICKS * tiles
    straight = first_half(split) == 0
    for receiver in range(blocks_ref.shape[0] // (2 * count)):
        start = margin + BRICKS * (receiver - 1) * tiles
        halves = [rows_ref[half, start : start + count] for half in range(2)]
        for half in range(2):
            block = jnp.where(straight, halves[half], halves[1 - half]) if split else halves[half]
            place = (2 * receiver + half) * count
            blocks_ref[place : place + count] = block
    out_ref[...] = blocks_ref[...].astype(BF16)
    for copy in others:
        copy.wait()


def relay_kernel(split, received_ref, own_out, other_out, rows_ref):
    rows_ref[...] = received_ref[...].astype(F32)
    count = own_out.shape[0] * 3 // 4
    sums = []
    for half in range(2):
        total = None
        for start in range(half * count, rows_ref.shape[0], 2 * count):
            piece = rows_ref[start : start + count]
            total = piece if total is None else total + piece
        sums.append(jnp.concatenate([total, jnp.zeros((count // 3, 128), F32)], axis=0))
    straight = first_half(split) == 0
    own_out[...] = jnp.where(straight, sums[0], sums[1]).astype(BF16)
    other_out[...] = jnp.where(straight, sums[1], sums[0]).astype(BF16)


def build_band(band_ref, rows):
    shape = (3 * CHANNELS, HALF)
    row = lax.broadcasted_iota(jnp.int32, shape, 0)
    target = CHANNELS - (row // CHANNELS) * CHANNELS + row % CHANNELS
    distance = lanes_of(shape) - target
    band_ref[:, HALF:, :] = jnp.zeros((9, HALF, HALF), BF16)
    for z in range(-1, 5):
        select = jnp.where(distance == z * CHANNELS, 1.0, 0.0).astype(BF16)
        block = dot(rows, select).astype(BF16)
        start = z % 8 * CHANNELS
        band_ref[:, start : start + CHANNELS, :] = block.reshape(9, CHANNELS, HALF)


def weight_rows(weights):
    cube = weights.reshape(9, 3, CHANNELS, CHANNELS)
    rows = jnp.concatenate([cube[:, 0], cube[:, 1], cube[:, 2]], axis=-1)
    return rows.reshape(9 * CHANNELS, 3 * CHANNELS).astype(BF16)


def flipped_rows(weights):
    cube = jnp.swapaxes(weights, 1, 2).reshape(9, 3, CHANNELS, CHANNELS)
    pieces = [jnp.concatenate([cube[8 - k, 2], cube[8 - k, 1], cube[8 - k, 0]], axis=-1) for k in range(9)]
    return jnp.concatenate(pieces, axis=0).astype(BF16)


def band_kernel(weights_ref, band_ref):
    build_band(band_ref, weight_rows(weights_ref[...].astype(F32)))


def lift(half_ref, up_ref, rows_ref, volumes_ref, half):
    tiles = half_ref.shape[0] // 8
    rows_ref[...] = half_ref[...].astype(F32)
    cells = []
    for tile in range(tiles):
        rows = rows_ref[pl.ds(tile, 8, stride=tiles), :]
        cells += [rows[:, :64], rows[:, 64:]]
    lifted = dot(jnp.concatenate(cells, axis=0).astype(BF16), up_ref[...])
    lifted = lifted.astype(BF16).astype(F32)
    first = 4 * CUBE * half
    for cell in range(4):
        b, c = cell // 2, cell % 2
        for sub in range(16):
            line = first + 8 * (sub // 4 * EDGE + 4 * b + sub % 4)
            volumes_ref[c, line : line + 8, :] = lifted[cell * 8 : cell * 8 + 8, sub * 128 : sub * 128 + 128]


def early_kernel(
    links_in, own_ref, up_ref, one_ref, two_ref,
    band_ref, back_ref, masks_ref, volumes_out,
    rows_ref, links_ref, links_sem,
):
    links_copy = pltpu.make_async_copy(links_in, links_ref, links_sem)
    links_copy.start()
    lift(own_ref, up_ref, rows_ref, volumes_out, 0)
    build_band(band_ref, weight_rows(one_ref[...].astype(F32)))
    build_band(back_ref, flipped_rows(two_ref[...].astype(F32)))
    links_copy.wait()
    put_masks(masks_ref, links_ref)


def put_padded(pad_ref, brick, lines, x_low, x_high, y_low, y_high, z_low, z_high):
    def joined(halves, before, after):
        lane = lanes_of(halves[0].shape)
        first = jnp.where(lane < CHANNELS, halves[1], before)
        second = jnp.where(lane >= HALF - CHANNELS, halves[0], after)
        return jnp.concatenate([halves[0], first], axis=-1), jnp.concatenate([halves[1], second], axis=-1)

    inside = joined(lines, z_low, z_high)
    x_low, x_high, y_low, y_high = [joined(face, 0.0, 0.0) for face in (x_low, x_high, y_low, y_high)]
    none = jnp.zeros((1, WIDE), F32)
    shifted = [[], [], []]
    for half in range(2):
        slabs = jnp.concatenate([x_low[half][None], inside[half], x_high[half][None]], axis=0)
        row = lax.broadcasted_iota(jnp.int32, slabs.shape, 1)
        low = jnp.concatenate([none, y_low[half], none], axis=0)[:, None, :]
        high = jnp.concatenate([none, y_high[half], none], axis=0)[:, None, :]
        shifted[0].append(jnp.where(row == 0, low, pltpu.roll(slabs, 1, 1)))
        shifted[1].append(slabs)
        shifted[2].append(jnp.where(row == EDGE - 1, high, pltpu.roll(slabs, EDGE - 1, 1)))
    for dy in range(3):
        pad_ref[dy, brick] = jnp.concatenate(shifted[dy], axis=1).astype(BF16)


def window(pad_ref, k):
    return pad_ref[k % 3, :, k // 3 : k // 3 + EDGE].reshape(ROWS, WIDE)


def convolve(pad_ref, band_ref):
    both, last = None, None
    for dy in range(3):
        slabs = pad_ref[dy, :, : EDGE + 1].reshape(-1, WIDE)
        term = dot(slabs, jnp.concatenate([band_ref[dy], band_ref[3 + dy]], axis=1))
        both = term if both is None else both + term
        term = dot(window(pad_ref, 6 + dy), band_ref[6 + dy])
        last = term if last is None else last + term
    both = both.reshape(BRICKS, EDGE + 1, 2 * EDGE, 2 * HALF)
    total = both[:, :EDGE, :, :HALF] + both[:, 1:, :, HALF:]
    return total.reshape(ROWS, HALF) + last


def half_lines(values):
    cube = values.reshape(BRICKS, EDGE, 2, EDGE, HALF)
    return [(cube[brick, :, 0], cube[brick, :, 1]) for brick in range(BRICKS)]


def put_halves(halves_ref, start, bricks):
    for brick, lines in enumerate(bricks):
        for half in range(2):
            first = start + brick * CUBE
            halves_ref[half, first : first + CUBE, :] = lines[half].reshape(CUBE, HALF)


def cotangent_lines(cotangent_ref):
    cube = cotangent_ref[...].astype(F32).reshape(BRICKS, EDGE, EDGE, LINE)
    return [(cube[brick, :, :, :HALF], cube[brick, :, :, HALF:]) for brick in range(BRICKS)]


def pack_faces(faces_ref, base, halves_ref, start, high):
    x_face = pair(halves_ref, start + ((EDGE - 1) * EDGE if high else 0), EDGE)
    y_face = pair(halves_ref, start + (EDGE - 1 if high else 0), EDGE, EDGE)
    for half in range(2):
        lanes = slice(half * HALF, half * HALF + HALF)
        faces_ref[base : base + EDGE, lanes] = x_face[half]
        faces_ref[base + EDGE : base + 2 * EDGE, lanes] = y_face[half]
    tile = halves_ref[1 if high else 0, start : start + CUBE, :]
    lane = lanes_of((16, 128)) // CHANNELS
    packed = jnp.zeros((16, 128), F32)
    for part in range(4):
        shift = (part + 1 if high else part) % 4 * CHANNELS
        piece = tile[part * 16 : part * 16 + 16]
        packed = jnp.where(lane == part, pltpu.roll(piece, shift, 1) if shift else piece, packed)
    faces_ref[base + 2 * EDGE : base + FACE, :128] = packed[:8]
    faces_ref[base + 2 * EDGE : base + FACE, 128:] = packed[8:]


def pack_all(bricks, halves_ref, faces_ref, high_out, low_out):
    put_halves(halves_ref, 0, bricks)
    for high, out_ref in ((True, high_out), (False, low_out)):
        for brick in range(BRICKS):
            pack_faces(faces_ref, brick * FACE, halves_ref, brick * CUBE, high)
        out_ref[...] = faces_ref[...].astype(BF16)


def to_partners(high_ref, low_ref, far_out, near_out):
    even = lax.axis_index("space") % 2 == 0
    far_out[...] = jnp.where(even, low_ref[...], high_ref[...])
    near_out[...] = jnp.where(even, high_ref[...], low_ref[...])


def faces_kernel(cotangent_ref, high_out, low_out, far_out, near_out, halves_ref, faces_ref):
    pack_all(cotangent_lines(cotangent_ref), halves_ref, faces_ref, high_out, low_out)
    to_partners(high_out, low_out, far_out, near_out)


def unpack_depth(halves, high):
    packed = jnp.concatenate(halves, axis=0)
    pieces = []
    for part in range(4):
        shift = ((3 - part) if high else (4 - part)) % 4 * CHANNELS
        pieces.append(pltpu.roll(packed, shift, 1) if shift else packed)
    return jnp.concatenate(pieces, axis=0).reshape(EDGE, EDGE, 128)


def first_kernel(
    links_in, other_ref, up_ref, band_ref, lifted_half,
    slope_out, hidden_out, turned_out, pad_out,
    volumes_ref, rows_ref, links_ref, links_sem,
):
    links_copy = pltpu.make_async_copy(links_in, links_ref, links_sem)
    links_copy.start()
    position = lax.axis_index("space")
    volumes_ref[:, : 4 * CUBE] = lifted_half[...]
    lift(other_ref, up_ref, rows_ref, volumes_ref, 1)
    links_copy.wait()
    for brick in range(BRICKS):

        def near(face):
            link = links_ref[0, brick, face]
            index = jnp.clip(link - BRICKS * (position - 1), 0, 3 * BRICKS - 1)
            return index, jnp.where(link >= 0, 1.0, 0.0).astype(F32)

        def x_face(face):
            index, present = near(face)
            line = EDGE * (EDGE - 1) if face % 2 == 0 else 0
            return [half * present for half in pair(volumes_ref, line * 8 + index, EDGE, 8)]

        def y_face(face):
            index, present = near(face)
            line = EDGE - 1 if face % 2 == 0 else 0
            return [half * present for half in pair(volumes_ref, line * 8 + index, EDGE, 8 * EDGE)]

        def z_face(face):
            index, present = near(face)
            tile = volumes_ref[1 if face % 2 == 0 else 0, pl.ds(index, CUBE, stride=8), :] * present
            return tile.reshape(EDGE, EDGE, HALF)

        own = [half.reshape(EDGE, EDGE, HALF) for half in pair(volumes_ref, BRICKS + brick, CUBE, 8)]
        put_padded(pad_out, brick, own, x_face(0), x_face(1), y_face(2), y_face(3), z_face(4), z_face(5))
    pre = convolve(pad_out, band_ref)
    sigmoid = 1.0 / (1.0 + jnp.exp(-pre))
    hidden = (pre * sigmoid).astype(BF16)
    slope_out[...] = sigmoid * (1.0 + pre * (1.0 - sigmoid))
    hidden_out[...] = hidden
    turned_out[...] = jnp.transpose(hidden)


def hidden_faces_kernel(hidden_ref, _parts, high_out, low_out, far_out, near_out, halves_ref, faces_ref):
    pack_all(half_lines(hidden_ref[...].astype(F32)), halves_ref, faces_ref, high_out, low_out)
    to_partners(high_out, low_out, far_out, near_out)


def picked(outer, places):
    lane = lanes_of((CHANNELS, 128)) // CHANNELS
    found = None
    for block in range(4):
        start, tile = places[block]
        rows = outer[start : start + CHANNELS, tile * 128 : tile * 128 + 128]
        found = rows if found is None else jnp.where(lane == block, rows, found)
    return found


def fold(four):
    lane = lanes_of((CHANNELS, 128)) // CHANNELS
    total = None
    for turn in range(4):
        mixed = four[0]
        for n in range(1, len(four)):
            mixed = jnp.where(lane == (n + turn) % 4, four[n], mixed)
        if turn:
            mixed = pltpu.roll(mixed, 128 - turn * CHANNELS, 1)
        total = mixed if total is None else total + mixed
    return total


def diagonal(shift):
    places = [None] * 4
    for z in range(4):
        other = z + shift
        places[other % 4] = (z * CHANNELS, 0 if 0 <= other < 4 else 1)
    return places


def put_masks(masks_ref, links_ref):
    position = lax.axis_index("space")
    for brick in range(BRICKS):
        for face in range(6):
            first = links_ref[0, brick, face] - BRICKS * (position - 1 if face % 2 == 0 else position)
            for i in range(2 * BRICKS):
                row = (brick * 6 + face) * 2 * BRICKS + i
                masks_ref[row : row + 1, :] = jnp.full((1, 128), jnp.where(first == i, 1.0, 0.0).astype(F32))


def pad_all(pad_ref, bricks, masks_ref, high_pool, low_pool, high_own, low_own, far, near):
    position = lax.axis_index("space")
    half = BRICKS * FACE
    even = position % 2 == 0
    high_pool[0:half] = jnp.where(even, far[...], near[...]).astype(F32)
    high_pool[half:] = high_own[...].astype(F32)
    low_pool[0:half] = low_own[...].astype(F32)
    low_pool[half:] = jnp.where(even, near[...], far[...]).astype(F32)
    for brick, lines in enumerate(bricks):

        def face(number, axis):
            pool = high_pool if number % 2 == 0 else low_pool
            total = [0.0, 0.0]
            for i in range(2 * BRICKS):
                row = (brick * 6 + number) * 2 * BRICKS + i
                mask = masks_ref[row : row + 1, :]
                start = i * FACE + axis * EDGE
                for part in range(2):
                    found = pool[start : start + EDGE, part * HALF : part * HALF + HALF]
                    total[part] = total[part] + found * mask
            return total

        put_padded(
            pad_ref, brick, lines, face(0, 0), face(1, 0), face(2, 1), face(3, 1),
            unpack_depth(face(4, 2), True), unpack_depth(face(5, 2), False),
        )


def second_kernel(
    masks_ref, cotangent_ref, band_ref, slope_ref, hidden_ref, lifted_pad, high_own, low_own, far, near,
    sums_out, lifted_out,
    high_pool, low_pool, cotangent_pad, sums_ref,
):
    lifted_out[...] = window(lifted_pad, 4)[:, :HALF]
    bricks = cotangent_lines(cotangent_ref)
    pad_all(cotangent_pad, bricks, masks_ref, high_pool, low_pool, high_own, low_own, far, near)
    gradient = (convolve(cotangent_pad, band_ref) * slope_ref[...]).astype(BF16)
    gradient = jnp.transpose(gradient)
    hidden = hidden_ref[...]
    if sums_ref.shape[0] > 2 * GROUPS * CHANNELS:
        rest = sums_ref.shape[0] - 2 * GROUPS * CHANNELS
        sums_ref[2 * GROUPS * CHANNELS :] = jnp.zeros((rest, 128), F32)
    ones, twos = [], []
    for k in range(9):
        one = dot(gradient, window(lifted_pad, k))
        two = dot(hidden, window(cotangent_pad, 8 - k))
        ones += [picked(one, diagonal(part - 1)) for part in range(3)]
        twos += [picked(two, diagonal(1 - part)) for part in range(3)]
        while len(ones) >= 4 or (k == 8 and ones):
            group = (3 * k + 3 - len(ones)) // 4
            for first, blocks in ((0, ones), (GROUPS, twos)):
                start = (first + group) * CHANNELS
                sums_ref[start : start + CHANNELS] = fold(blocks[:4])
            ones, twos = ones[4:], twos[4:]
    sums_out[...] = sums_ref[...].astype(BF16)


def fine_kernel(
    masks_ref, band_ref, lifted_ref, hidden_ref, high_own, low_own, far, near,
    fine_out, high_pool, low_pool, hidden_pad,
):
    bricks = half_lines(hidden_ref[...].astype(F32))
    pad_all(hidden_pad, bricks, masks_ref, high_pool, low_pool, high_own, low_own, far, near)
    fine = lifted_ref[...].astype(F32) + convolve(hidden_pad, band_ref)
    fine = fine.reshape(LINES // EDGE, 2, EDGE, HALF)
    fine = jnp.concatenate([fine[:, 0], fine[:, 1]], axis=-1)
    fine_out[...] = fine.astype(BF16).reshape(fine_out.shape)


def sum_kernel(devices, scale, parts_ref, out_hbm, rows_ref, shares_ref, sems):
    rows_ref[...] = parts_ref[...].astype(F32)
    share = rows_ref.shape[0] // devices
    pieces = [rows_ref[share * i : share * i + share] for i in range(devices)]
    while len(pieces) > 1:
        pairs = [a + b for a, b in zip(pieces[::2], pieces[1::2])]
        pieces = pairs + pieces[len(pieces) - len(pieces) % 2 :]
    total = pieces[0] * scale
    some = shares_ref.shape[0]
    for i in range(some // share):
        rows_ref[share * i : share * i + share] = total
    shares_ref[...] = rows_ref[0:some].astype(BF16)
    copies = []
    for i in range(out_hbm.shape[0] // some):
        copies.append(pltpu.make_async_copy(shares_ref, out_hbm.at[pl.ds(some * i, some)], sems.at[i]))
        copies[-1].start()
    for copy in copies:
        copy.wait()


def unpack_kernel(sums_ref, fine_ref, one_out, two_out, fine_out, rows_ref, one_ref, two_ref, sems, fine_sem):
    fine_copy = pltpu.make_async_copy(fine_ref, fine_out, fine_sem)
    fine_copy.start()
    rows_ref[...] = sums_ref[...].astype(F32)
    copies = []
    for which, (block_ref, out) in ((1, (two_ref, two_out)), (0, (one_ref, one_out))):
        for group in range(GROUPS):
            start = (which * GROUPS + group) * CHANNELS
            four = rows_ref[start : start + CHANNELS]
            turned = None if which else jnp.transpose(four)
            count = min(4, 27 - 4 * group)
            for n in range(count):
                if which:
                    block = pltpu.roll(four, 128 - n * CHANNELS, 1) if n else four
                    block_ref[4 * group + n] = block[:, :CHANNELS]
                else:
                    block_ref[4 * group + n] = turned[CHANNELS * n : CHANNELS * n + CHANNELS]
            span = pl.ds(4 * group, count)
            copies.append(pltpu.make_async_copy(block_ref.at[span], out.at[span], sems.at[which, group]))
            copies[-1].start()
    for copy in copies:
        copy.wait()
    fine_copy.wait()


def call(kernel, out_shape, scratch=(), hbm=(), inputs=1, limit=24, cost=None, out=pltpu.VMEM):
    spaces = [pl.ANY if i in hbm else pltpu.VMEM for i in range(inputs)]
    return pl.pallas_call(
        kernel,
        out_shape=out_shape,
        in_specs=[pl.BlockSpec(memory_space=space) for space in spaces],
        out_specs=jax.tree.map(lambda _: pl.BlockSpec(memory_space=out), out_shape),
        scratch_shapes=list(scratch),
        compiler_params=pltpu.CompilerParams(vmem_limit_bytes=limit * 2**20),
        cost_estimate=cost,
    )


def shape(*dims, dtype=BF16):
    return jax.ShapeDtypeStruct(dims, dtype)


def kept_in_hbm(value):
    return pltpu.with_memory_space_constraint(value, pltpu.HBM)


def swapped(value, first):
    pairs = [(i, i + 1) for i in range(first, lax.axis_size("space") - 1, 2)]
    return lax.ppermute(value, "space", pairs + [(target, source) for source, target in pairs])


def exchanged(rows, axes=("space", "dp")):
    count = math.prod(lax.axis_size(axis) for axis in axes)
    shares = rows.reshape(count, -1, 2, 128)
    shares = lax.all_to_all(shares, axes, split_axis=0, concat_axis=0, tiled=True)
    return shares.reshape(rows.shape)


def body(coarse_latents, active_blocks, face_links, cotangent, up_weight, conv_one, conv_two):
    devices = lax.axis_size("space")
    everyone = devices * lax.axis_size("dp")
    held, width = coarse_latents.shape[1:]
    bricks = active_blocks.shape[1]
    split = lax.axis_size("dp") == 2
    tiles = width // 256
    count = 3 * BRICKS * tiles
    blocks = (2 * devices * count, 128)
    extras = (up_weight, conv_one, conv_two, face_links)
    packed, up_weight, conv_one, conv_two, face_links = call(
        functools.partial(pick_kernel, split, len(extras)),
        (shape(*blocks), *[shape(*extra.shape, dtype=extra.dtype) for extra in extras]),
        [
            pltpu.VMEM((1, bricks), jnp.int32),
            pltpu.VMEM((1, held, width), BF16),
            pltpu.VMEM((2, (bricks + 16) * tiles, 128), F32),
            pltpu.VMEM(blocks, F32),
            pltpu.SemaphoreType.DMA((2 + len(extras),)),
        ],
        hbm=range(2 + len(extras)),
        inputs=2 + len(extras),
    )(*[kept_in_hbm(operand) for operand in (active_blocks, coarse_latents, *extras)])
    received = exchanged(packed, ("space", "dp") if split else ("space",))
    window_half = shape(8 * tiles, 128)
    own, other = call(
        functools.partial(relay_kernel, split), (window_half, window_half), [pltpu.VMEM(blocks, F32)]
    )(received)
    if split:
        other = lax.ppermute(other, "dp", [(0, 1), (1, 0)])
    cost = pl.CostEstimate(flops=10**9, bytes_accessed=2 * 10**6, transcendentals=0)
    face = shape(BRICKS * FACE, LINE)
    halves = pltpu.VMEM((2, LINES, HALF), F32)
    faces = pltpu.VMEM((BRICKS * FACE, LINE), F32)
    pool = pltpu.VMEM((2 * BRICKS * FACE, LINE), F32)
    volume = shape(ROWS, HALF)
    links = [pltpu.SMEM(face_links.shape, jnp.int32), pltpu.SemaphoreType.DMA]
    pad_shape = (3, BRICKS, EDGE + 2, 2 * EDGE, WIDE)
    pad = pltpu.VMEM(pad_shape, BF16)
    high, low, far, near = call(faces_kernel, (face,) * 4, [halves, faces])(cotangent)
    far = swapped(far, 1)
    near = swapped(near, 0)
    masks = shape(BRICKS * 6 * 2 * BRICKS, 128, dtype=F32)
    lifted_half = shape(2, 4 * CUBE, 128, dtype=F32)
    window_rows = pltpu.VMEM((8 * tiles, 128), F32)
    band_one, band_back, masks, lifted_half = call(
        early_kernel,
        (shape(*BAND), shape(*BAND), masks, lifted_half),
        [window_rows, *links],
        hbm=(0,),
        inputs=5,
        cost=cost,
    )(face_links, own, up_weight, conv_one, conv_two)
    slope, hidden, turned, lifted_pad = call(
        first_kernel,
        (
            shape(ROWS, HALF, dtype=F32), volume, shape(HALF, ROWS), shape(*pad_shape),
        ),
        [pltpu.VMEM((2, 8 * CUBE, 128), F32), window_rows, *links],
        hbm=(0,),
        inputs=5,
    )(face_links, other, up_weight, band_one, lifted_half)
    share = 2 * -(-GROUPS * CHANNELS // everyone)
    packed_rows = (everyone * share, 128)
    sums, lifted = call(
        second_kernel,
        (shape(*packed_rows), volume),
        [pool, pool, pad, pltpu.VMEM(packed_rows, F32)],
        inputs=10,
    )(masks, cotangent, band_back, slope, turned, lifted_pad, high, low, far, near)
    parts = exchanged(sums)
    hidden_high, hidden_low, hidden_far, hidden_near = call(
        hidden_faces_kernel, (face,) * 4, [halves, faces], hbm=(1,), inputs=2
    )(hidden, parts)
    hidden_far = swapped(hidden_far, 1)
    hidden_near = swapped(hidden_near, 0)
    band_two = call(band_kernel, shape(*BAND), cost=cost)(conv_two)
    fine = call(fine_kernel, shape(*cotangent.shape), [pool, pool, pad], inputs=8, cost=cost)(
        masks, band_two, lifted, hidden, hidden_high, hidden_low, hidden_far, hidden_near
    )
    scale = 1.0 / math.sqrt(lax.axis_size("dp") * devices * BRICKS * EDGE**3)
    times = 4 if everyone % 32 == 0 else 1
    total = call(
        functools.partial(sum_kernel, everyone, scale),
        shape(*packed_rows),
        [
            pltpu.VMEM(packed_rows, F32),
            pltpu.VMEM((packed_rows[0] // times, 128), BF16),
            pltpu.SemaphoreType.DMA((times,)),
        ],
        out=pl.ANY,
    )(parts)
    gathered = exchanged(total)
    grads = shape(27, CHANNELS, CHANNELS, dtype=F32)
    block = pltpu.VMEM(grads.shape, F32)
    scratch = [pltpu.VMEM(packed_rows, F32), block, block]
    scratch += [pltpu.SemaphoreType.DMA((2, GROUPS)), pltpu.SemaphoreType.DMA]
    grad_one, grad_two, fine = call(
        unpack_kernel, (grads, grads, shape(*fine.shape)), scratch, inputs=2, out=pl.ANY
    )(gathered, fine)
    return (fine, grad_one, grad_two)


def solution(mesh):
    return jax.shard_map(
        body,
        mesh=mesh,
        in_specs=(
            P("dp", "space", None),
            P("dp", None),
            P("dp", "space", None),
            P("dp", "space", None, None, None),
            P(),
            P(),
            P(),
        ),
        out_specs=(P("dp", "space", None, None, None), P(), P()),
        check_vma=False,
    )
```

```python
import functools
import math

import jax
import jax.numpy as jnp
from jax import lax
from jax.experimental import pallas as pl
from jax.experimental.pallas import tpu as pltpu
from jax.sharding import PartitionSpec as P

BF16 = jnp.bfloat16
F32 = jnp.float32
EDGE = 8
CHANNELS = 32
LINE = EDGE * CHANNELS
HALF = LINE // 2
WIDE = 2 * HALF
BRICKS = 2
CUBE = EDGE * EDGE
LINES = BRICKS * CUBE
BAND = (9, WIDE, HALF)
ROWS = 2 * LINES
FACE = 3 * EDGE
GROUPS = 7


def dot(left, right):
    return jnp.dot(left, right, preferred_element_type=F32)


def dot_rows(left, right):
    return lax.dot_general(left, right, (((0,), (0,)), ((), ())), preferred_element_type=F32)


def pair(halves_ref, start, count, stride=1):
    index = pl.ds(start, count, stride=stride) if stride > 1 else pl.ds(start, count)
    return halves_ref[0, index, :], halves_ref[1, index, :]


def lanes_of(shape):
    return lax.broadcasted_iota(jnp.int32, shape, len(shape) - 1)


def first_half(split):
    return lax.axis_index("dp") if split else 0


def pick_kernel(split, extras, ids_hbm, latents_hbm, *refs):
    brought = zip(refs[:extras], refs[extras + 1 : 2 * extras + 1])
    out_ref = refs[extras]
    ids_ref, latents_ref, rows_ref, blocks_ref, sems = refs[2 * extras + 1 :]
    ids_copy = pltpu.make_async_copy(ids_hbm, ids_ref, sems.at[0])
    latents_copy = pltpu.make_async_copy(latents_hbm, latents_ref, sems.at[1])
    ids_copy.start()
    latents_copy.start()
    others = [pltpu.make_async_copy(*pair, sems.at[2 + i]) for i, pair in enumerate(brought)]
    for copy in others:
        copy.start()
    held, width = latents_ref.shape[1:]
    bricks = ids_ref.shape[1]
    tiles = width // 256
    margin = 8 * tiles
    empty = jnp.zeros((margin, 128), F32)
    for half in range(2):
        rows_ref[half, 0:margin] = empty
        rows_ref[half, margin + bricks * tiles :] = empty
    first = lax.axis_index("space") * held
    rows = lax.broadcasted_iota(jnp.int32, (held, bricks), 0) + first
    ids_copy.wait()
    hot = jnp.where(rows == ids_ref[...], 1.0, 0.0).astype(BF16)
    latents_copy.wait()
    picked = dot_rows(hot, latents_ref[0])
    for tile in range(2 * tiles):
        place = pl.ds(margin + tile % tiles, bricks, stride=tiles)
        rows_ref[tile // tiles, place, :] = picked[:, tile * 128 : tile * 128 + 128]
    count = 3 * BRICKS * tiles
    straight = first_half(split) == 0
    for receiver in range(blocks_ref.shape[0] // (2 * count)):
        start = margin + BRICKS * (receiver - 1) * tiles
        halves = [rows_ref[half, start : start + count] for half in range(2)]
        for half in range(2):
            block = jnp.where(straight, halves[half], halves[1 - half]) if split else halves[half]
            place = (2 * receiver + half) * count
            blocks_ref[place : place + count] = block
    out_ref[...] = blocks_ref[...].astype(BF16)
    for copy in others:
        copy.wait()


def relay_kernel(split, received_ref, own_out, other_out, rows_ref):
    rows_ref[...] = received_ref[...].astype(F32)
    count = own_out.shape[0] * 3 // 4
    sums = []
    for half in range(2):
        total = None
        for start in range(half * count, rows_ref.shape[0], 2 * count):
            piece = rows_ref[start : start + count]
            total = piece if total is None else total + piece
        sums.append(jnp.concatenate([total, jnp.zeros((count // 3, 128), F32)], axis=0))
    straight = first_half(split) == 0
    own_out[...] = jnp.where(straight, sums[0], sums[1]).astype(BF16)
    other_out[...] = jnp.where(straight, sums[1], sums[0]).astype(BF16)


def build_band(band_ref, rows):
    shape = (3 * CHANNELS, HALF)
    row = lax.broadcasted_iota(jnp.int32, shape, 0)
    target = CHANNELS - (row // CHANNELS) * CHANNELS + row % CHANNELS
    distance = lanes_of(shape) - target
    band_ref[:, HALF:, :] = jnp.zeros((9, HALF, HALF), BF16)
    for z in range(-1, 5):
        select = jnp.where(distance == z * CHANNELS, 1.0, 0.0).astype(BF16)
        block = dot(rows, select).astype(BF16)
        start = z % 8 * CHANNELS
        band_ref[:, start : start + CHANNELS, :] = block.reshape(9, CHANNELS, HALF)


def weight_rows(weights):
    cube = weights.reshape(9, 3, CHANNELS, CHANNELS)
    rows = jnp.concatenate([cube[:, 0], cube[:, 1], cube[:, 2]], axis=-1)
    return rows.reshape(9 * CHANNELS, 3 * CHANNELS).astype(BF16)


def flipped_rows(weights):
    cube = jnp.swapaxes(weights, 1, 2).reshape(9, 3, CHANNELS, CHANNELS)
    pieces = [jnp.concatenate([cube[8 - k, 2], cube[8 - k, 1], cube[8 - k, 0]], axis=-1) for k in range(9)]
    return jnp.concatenate(pieces, axis=0).astype(BF16)


def band_kernel(weights_ref, band_ref):
    build_band(band_ref, weight_rows(weights_ref[...].astype(F32)))


def lift(half_ref, up_ref, rows_ref, volumes_ref, half):
    tiles = half_ref.shape[0] // 8
    rows_ref[: 8 * tiles] = half_ref[...].astype(F32)
    cells = []
    for tile in range(tiles):
        rows = rows_ref[pl.ds(tile, 8, stride=tiles), :]
        cells += [rows[:, :64], rows[:, 64:]]
    lifted = dot(jnp.concatenate(cells, axis=0).astype(BF16), up_ref[...])
    lifted = lifted.astype(BF16).astype(F32)
    first = 4 * CUBE * half
    for cell in range(4):
        b, c = cell // 2, cell % 2
        for sub in range(16):
            line = first + 8 * (sub // 4 * EDGE + 4 * b + sub % 4)
            volumes_ref[c, line : line + 8, :] = lifted[cell * 8 : cell * 8 + 8, sub * 128 : sub * 128 + 128]


def early_kernel(
    links_in, own_ref, up_ref, one_ref, two_ref,
    band_ref, back_ref, masks_ref, volumes_out,
    rows_ref, links_ref, links_sem,
):
    links_copy = pltpu.make_async_copy(links_in, links_ref, links_sem)
    links_copy.start()
    lift(own_ref, up_ref, rows_ref, volumes_out, 0)
    build_band(band_ref, weight_rows(one_ref[...].astype(F32)))
    build_band(back_ref, flipped_rows(two_ref[...].astype(F32)))
    links_copy.wait()
    put_masks(masks_ref, links_ref)


def put_padded(pad_ref, brick, lines, x_low, x_high, y_low, y_high, z_low, z_high):
    def joined(halves, before, after):
        lane = lanes_of(halves[0].shape)
        first = jnp.where(lane < CHANNELS, halves[1], before)
        second = jnp.where(lane >= HALF - CHANNELS, halves[0], after)
        return jnp.concatenate([halves[0], first], axis=-1), jnp.concatenate([halves[1], second], axis=-1)

    inside = joined(lines, z_low, z_high)
    x_low, x_high, y_low, y_high = [joined(face, 0.0, 0.0) for face in (x_low, x_high, y_low, y_high)]
    none = jnp.zeros((1, WIDE), F32)
    shifted = [[], [], []]
    for half in range(2):
        slabs = jnp.concatenate([x_low[half][None], inside[half], x_high[half][None]], axis=0)
        row = lax.broadcasted_iota(jnp.int32, slabs.shape, 1)
        low = jnp.concatenate([none, y_low[half], none], axis=0)[:, None, :]
        high = jnp.concatenate([none, y_high[half], none], axis=0)[:, None, :]
        shifted[0].append(jnp.where(row == 0, low, pltpu.roll(slabs, 1, 1)))
        shifted[1].append(slabs)
        shifted[2].append(jnp.where(row == EDGE - 1, high, pltpu.roll(slabs, EDGE - 1, 1)))
    for dy in range(3):
        pad_ref[dy, brick] = jnp.concatenate(shifted[dy], axis=1).astype(BF16)


def window(pad_ref, k):
    return pad_ref[k % 3, :, k // 3 : k // 3 + EDGE].reshape(ROWS, WIDE)


def convolve(pad_ref, band_ref):
    both, last = None, None
    for dy in range(3):
        slabs = pad_ref[dy, :, : EDGE + 1].reshape(-1, WIDE)
        term = dot(slabs, jnp.concatenate([band_ref[dy], band_ref[3 + dy]], axis=1))
        both = term if both is None else both + term
        term = dot(window(pad_ref, 6 + dy), band_ref[6 + dy])
        last = term if last is None else last + term
    both = both.reshape(BRICKS, EDGE + 1, 2 * EDGE, 2 * HALF)
    total = both[:, :EDGE, :, :HALF] + both[:, 1:, :, HALF:]
    return total.reshape(ROWS, HALF) + last


def half_lines(values):
    cube = values.reshape(BRICKS, EDGE, 2, EDGE, HALF)
    return [(cube[brick, :, 0], cube[brick, :, 1]) for brick in range(BRICKS)]


def put_halves(halves_ref, start, bricks):
    for brick, lines in enumerate(bricks):
        for half in range(2):
            first = start + brick * CUBE
            halves_ref[half, first : first + CUBE, :] = lines[half].reshape(CUBE, HALF)


def cotangent_lines(cotangent_ref):
    cube = cotangent_ref[...].astype(F32).reshape(BRICKS, EDGE, EDGE, LINE)
    return [(cube[brick, :, :, :HALF], cube[brick, :, :, HALF:]) for brick in range(BRICKS)]


def pack_faces(faces_ref, base, halves_ref, start, high):
    x_face = pair(halves_ref, start + ((EDGE - 1) * EDGE if high else 0), EDGE)
    y_face = pair(halves_ref, start + (EDGE - 1 if high else 0), EDGE, EDGE)
    for half in range(2):
        lanes = slice(half * HALF, half * HALF + HALF)
        faces_ref[base : base + EDGE, lanes] = x_face[half]
        faces_ref[base + EDGE : base + 2 * EDGE, lanes] = y_face[half]
    tile = halves_ref[1 if high else 0, start : start + CUBE, :]
    lane = lanes_of((16, 128)) // CHANNELS
    packed = jnp.zeros((16, 128), F32)
    for part in range(4):
        shift = (part + 1 if high else part) % 4 * CHANNELS
        piece = tile[part * 16 : part * 16 + 16]
        packed = jnp.where(lane == part, pltpu.roll(piece, shift, 1) if shift else piece, packed)
    faces_ref[base + 2 * EDGE : base + FACE, :128] = packed[:8]
    faces_ref[base + 2 * EDGE : base + FACE, 128:] = packed[8:]


def pack_all(bricks, halves_ref, faces_ref, high_out, low_out):
    put_halves(halves_ref, 0, bricks)
    for high, out_ref in ((True, high_out), (False, low_out)):
        for brick in range(BRICKS):
            pack_faces(faces_ref, brick * FACE, halves_ref, brick * CUBE, high)
        out_ref[...] = faces_ref[...].astype(BF16)


def to_partners(high_ref, low_ref, far_out, near_out):
    even = lax.axis_index("space") % 2 == 0
    far_out[...] = jnp.where(even, low_ref[...], high_ref[...])
    near_out[...] = jnp.where(even, high_ref[...], low_ref[...])


def faces_kernel(cotangent_ref, high_out, low_out, far_out, near_out, halves_ref, faces_ref):
    pack_all(cotangent_lines(cotangent_ref), halves_ref, faces_ref, high_out, low_out)
    to_partners(high_out, low_out, far_out, near_out)


def unpack_depth(halves, high):
    packed = jnp.concatenate(halves, axis=0)
    pieces = []
    for part in range(4):
        shift = ((3 - part) if high else (4 - part)) % 4 * CHANNELS
        pieces.append(pltpu.roll(packed, shift, 1) if shift else packed)
    return jnp.concatenate(pieces, axis=0).reshape(EDGE, EDGE, 128)


def first_kernel(
    links_in, other_ref, up_ref, band_ref, lifted_half,
    slope_out, hidden_out, turned_out, pad_out,
    volumes_ref, rows_ref, links_ref, links_sem,
):
    links_copy = pltpu.make_async_copy(links_in, links_ref, links_sem)
    links_copy.start()
    position = lax.axis_index("space")
    volumes_ref[:, : 4 * CUBE] = lifted_half[...]
    lift(other_ref, up_ref, rows_ref, volumes_ref, 1)
    links_copy.wait()
    for brick in range(BRICKS):

        def near(face):
            link = links_ref[0, brick, face]
            index = jnp.clip(link - BRICKS * (position - 1), 0, 3 * BRICKS - 1)
            return index, jnp.where(link >= 0, 1.0, 0.0).astype(F32)

        def x_face(face):
            index, present = near(face)
            line = EDGE * (EDGE - 1) if face % 2 == 0 else 0
            return [half * present for half in pair(volumes_ref, line * 8 + index, EDGE, 8)]

        def y_face(face):
            index, present = near(face)
            line = EDGE - 1 if face % 2 == 0 else 0
            return [half * present for half in pair(volumes_ref, line * 8 + index, EDGE, 8 * EDGE)]

        def z_face(face):
            index, present = near(face)
            tile = volumes_ref[1 if face % 2 == 0 else 0, pl.ds(index, CUBE, stride=8), :] * present
            return tile.reshape(EDGE, EDGE, HALF)

        own = [half.reshape(EDGE, EDGE, HALF) for half in pair(volumes_ref, BRICKS + brick, CUBE, 8)]
        put_padded(pad_out, brick, own, x_face(0), x_face(1), y_face(2), y_face(3), z_face(4), z_face(5))
    pre = convolve(pad_out, band_ref)
    sigmoid = 1.0 / (1.0 + jnp.exp(-pre))
    hidden = (pre * sigmoid).astype(BF16)
    slope_out[...] = sigmoid * (1.0 + pre * (1.0 - sigmoid))
    hidden_out[...] = hidden
    turned_out[...] = jnp.transpose(hidden)


def hidden_faces_kernel(hidden_ref, _parts, high_out, low_out, far_out, near_out, halves_ref, faces_ref):
    pack_all(half_lines(hidden_ref[...].astype(F32)), halves_ref, faces_ref, high_out, low_out)
    to_partners(high_out, low_out, far_out, near_out)


def picked(outer, places):
    lane = lanes_of((CHANNELS, 128)) // CHANNELS
    found = None
    for block in range(4):
        start, tile = places[block]
        rows = outer[start : start + CHANNELS, tile * 128 : tile * 128 + 128]
        found = rows if found is None else jnp.where(lane == block, rows, found)
    return found


def fold(four):
    lane = lanes_of((CHANNELS, 128)) // CHANNELS
    total = None
    for turn in range(4):
        mixed = four[0]
        for n in range(1, len(four)):
            mixed = jnp.where(lane == (n + turn) % 4, four[n], mixed)
        if turn:
            mixed = pltpu.roll(mixed, 128 - turn * CHANNELS, 1)
        total = mixed if total is None else total + mixed
    return total


def diagonal(shift):
    places = [None] * 4
    for z in range(4):
        other = z + shift
        places[other % 4] = (z * CHANNELS, 0 if 0 <= other < 4 else 1)
    return places


def put_masks(masks_ref, links_ref):
    position = lax.axis_index("space")
    for brick in range(BRICKS):
        for face in range(6):
            first = links_ref[0, brick, face] - BRICKS * (position - 1 if face % 2 == 0 else position)
            for i in range(2 * BRICKS):
                row = (brick * 6 + face) * 2 * BRICKS + i
                masks_ref[row : row + 1, :] = jnp.full((1, 128), jnp.where(first == i, 1.0, 0.0).astype(F32))


def pad_all(pad_ref, bricks, masks_ref, high_pool, low_pool, high_own, low_own, far, near):
    position = lax.axis_index("space")
    half = BRICKS * FACE
    even = position % 2 == 0
    high_pool[0:half] = jnp.where(even, far[...], near[...]).astype(F32)
    high_pool[half:] = high_own[...].astype(F32)
    low_pool[0:half] = low_own[...].astype(F32)
    low_pool[half:] = jnp.where(even, near[...], far[...]).astype(F32)
    for brick, lines in enumerate(bricks):

        def face(number, axis):
            pool = high_pool if number % 2 == 0 else low_pool
            total = [0.0, 0.0]
            for i in range(2 * BRICKS):
                row = (brick * 6 + number) * 2 * BRICKS + i
                mask = masks_ref[row : row + 1, :]
                start = i * FACE + axis * EDGE
                for part in range(2):
                    found = pool[start : start + EDGE, part * HALF : part * HALF + HALF]
                    total[part] = total[part] + found * mask
            return total

        put_padded(
            pad_ref, brick, lines, face(0, 0), face(1, 0), face(2, 1), face(3, 1),
            unpack_depth(face(4, 2), True), unpack_depth(face(5, 2), False),
        )


def second_kernel(
    masks_ref, cotangent_ref, band_ref, slope_ref, hidden_ref, lifted_pad, high_own, low_own, far, near,
    sums_out, lifted_out,
    high_pool, low_pool, cotangent_pad, sums_ref,
):
    lifted_out[...] = window(lifted_pad, 4)[:, :HALF]
    bricks = cotangent_lines(cotangent_ref)
    pad_all(cotangent_pad, bricks, masks_ref, high_pool, low_pool, high_own, low_own, far, near)
    gradient = (convolve(cotangent_pad, band_ref) * slope_ref[...]).astype(BF16)
    gradient = jnp.transpose(gradient)
    hidden = hidden_ref[...]
    if sums_ref.shape[0] > 2 * GROUPS * CHANNELS:
        rest = sums_ref.shape[0] - 2 * GROUPS * CHANNELS
        sums_ref[2 * GROUPS * CHANNELS :] = jnp.zeros((rest, 128), F32)
    ones, twos = [], []
    for k in range(9):
        one = dot(gradient, window(lifted_pad, k))
        two = dot(hidden, window(cotangent_pad, 8 - k))
        ones += [picked(one, diagonal(part - 1)) for part in range(3)]
        twos += [picked(two, diagonal(1 - part)) for part in range(3)]
        while len(ones) >= 4 or (k == 8 and ones):
            group = (3 * k + 3 - len(ones)) // 4
            for first, blocks in ((0, ones), (GROUPS, twos)):
                start = (first + group) * CHANNELS
                sums_ref[start : start + CHANNELS] = fold(blocks[:4])
            ones, twos = ones[4:], twos[4:]
    sums_out[...] = sums_ref[...].astype(BF16)


def fine_kernel(
    masks_ref, band_ref, lifted_ref, hidden_ref, high_own, low_own, far, near,
    fine_out, high_pool, low_pool, hidden_pad,
):
    bricks = half_lines(hidden_ref[...].astype(F32))
    pad_all(hidden_pad, bricks, masks_ref, high_pool, low_pool, high_own, low_own, far, near)
    fine = lifted_ref[...].astype(F32) + convolve(hidden_pad, band_ref)
    fine = fine.reshape(LINES // EDGE, 2, EDGE, HALF)
    fine = jnp.concatenate([fine[:, 0], fine[:, 1]], axis=-1)
    fine_out[...] = fine.astype(BF16).reshape(fine_out.shape)


def sum_kernel(devices, scale, parts_ref, out_hbm, rows_ref, shares_ref, sems):
    rows_ref[...] = parts_ref[...].astype(F32)
    share = rows_ref.shape[0] // devices
    pieces = [rows_ref[share * i : share * i + share] for i in range(devices)]
    while len(pieces) > 1:
        pairs = [a + b for a, b in zip(pieces[::2], pieces[1::2])]
        pieces = pairs + pieces[len(pieces) - len(pieces) % 2 :]
    total = pieces[0] * scale
    some = shares_ref.shape[0]
    for i in range(some // share):
        rows_ref[share * i : share * i + share] = total
    shares_ref[...] = rows_ref[0:some].astype(BF16)
    copies = []
    for i in range(out_hbm.shape[0] // some):
        copies.append(pltpu.make_async_copy(shares_ref, out_hbm.at[pl.ds(some * i, some)], sems.at[i]))
        copies[-1].start()
    for copy in copies:
        copy.wait()


def unpack_kernel(sums_ref, fine_ref, one_out, two_out, fine_out, rows_ref, one_ref, two_ref, sems, fine_sem):
    fine_copy = pltpu.make_async_copy(fine_ref, fine_out, fine_sem)
    fine_copy.start()
    rows_ref[...] = sums_ref[...].astype(F32)
    copies = []
    for which, (block_ref, out) in ((1, (two_ref, two_out)), (0, (one_ref, one_out))):
        for part, (first, last) in enumerate(((0, 2), (2, 4), (4, GROUPS))):
            for group in range(first, last):
                start = (which * GROUPS + group) * CHANNELS
                four = rows_ref[start : start + CHANNELS]
                turned = None if which else jnp.transpose(four)
                for n in range(min(4, 27 - 4 * group)):
                    if which:
                        block = pltpu.roll(four, 128 - n * CHANNELS, 1) if n else four
                        block_ref[4 * group + n] = block[:, :CHANNELS]
                    else:
                        block_ref[4 * group + n] = turned[CHANNELS * n : CHANNELS * n + CHANNELS]
            span = pl.ds(4 * first, min(4 * last, 27) - 4 * first)
            copies.append(pltpu.make_async_copy(block_ref.at[span], out.at[span], sems.at[which, part]))
            copies[-1].start()
    for copy in copies:
        copy.wait()
    fine_copy.wait()


def call(kernel, out_shape, scratch=(), hbm=(), inputs=1, limit=24, cost=None, out=pltpu.VMEM):
    spaces = [pl.ANY if i in hbm else pltpu.VMEM for i in range(inputs)]
    return pl.pallas_call(
        kernel,
        out_shape=out_shape,
        in_specs=[pl.BlockSpec(memory_space=space) for space in spaces],
        out_specs=jax.tree.map(lambda _: pl.BlockSpec(memory_space=out), out_shape),
        scratch_shapes=list(scratch),
        compiler_params=pltpu.CompilerParams(vmem_limit_bytes=limit * 2**20),
        cost_estimate=cost,
    )


def shape(*dims, dtype=BF16):
    return jax.ShapeDtypeStruct(dims, dtype)


def kept_in_hbm(value):
    return pltpu.with_memory_space_constraint(value, pltpu.HBM)


def swapped(value, first):
    pairs = [(i, i + 1) for i in range(first, lax.axis_size("space") - 1, 2)]
    return lax.ppermute(value, "space", pairs + [(target, source) for source, target in pairs])


def exchanged(rows, axes=("space", "dp")):
    count = math.prod(lax.axis_size(axis) for axis in axes)
    shares = rows.reshape(count, -1, 2, 128)
    shares = lax.all_to_all(shares, axes, split_axis=0, concat_axis=0, tiled=True)
    return shares.reshape(rows.shape)


def body(coarse_latents, active_blocks, face_links, cotangent, up_weight, conv_one, conv_two):
    devices = lax.axis_size("space")
    everyone = devices * lax.axis_size("dp")
    held, width = coarse_latents.shape[1:]
    bricks = active_blocks.shape[1]
    split = lax.axis_size("dp") == 2
    tiles = width // 256
    count = 3 * BRICKS * tiles
    blocks = (2 * devices * count, 128)
    extras = (up_weight, conv_one, conv_two, face_links)
    packed, up_weight, conv_one, conv_two, face_links = call(
        functools.partial(pick_kernel, split, len(extras)),
        (shape(*blocks), *[shape(*extra.shape, dtype=extra.dtype) for extra in extras]),
        [
            pltpu.VMEM((1, bricks), jnp.int32),
            pltpu.VMEM((1, held, width), BF16),
            pltpu.VMEM((2, (bricks + 16) * tiles, 128), F32),
            pltpu.VMEM(blocks, F32),
            pltpu.SemaphoreType.DMA((2 + len(extras),)),
        ],
        hbm=range(2 + len(extras)),
        inputs=2 + len(extras),
    )(*[kept_in_hbm(operand) for operand in (active_blocks, coarse_latents, *extras)])
    received = exchanged(packed, ("space", "dp") if split else ("space",))
    window_half = shape(8 * tiles, 128)
    own, other = call(
        functools.partial(relay_kernel, split), (window_half, window_half), [pltpu.VMEM(blocks, F32)]
    )(received)
    if split:
        other = lax.ppermute(other, "dp", [(0, 1), (1, 0)])
    cost = pl.CostEstimate(flops=10**9, bytes_accessed=2 * 10**6, transcendentals=0)
    face = shape(BRICKS * FACE, LINE)
    halves = pltpu.VMEM((2, LINES + 8, HALF), F32)
    faces = pltpu.VMEM((BRICKS * FACE, LINE), F32)
    pool = pltpu.VMEM((2 * BRICKS * FACE, LINE), F32)
    volume = shape(ROWS, HALF)
    links = [pltpu.SMEM(face_links.shape, jnp.int32), pltpu.SemaphoreType.DMA]
    pad_shape = (3, BRICKS, EDGE + 2, 2 * EDGE, WIDE)
    pad = pltpu.VMEM(pad_shape, BF16)
    high, low, far, near = call(faces_kernel, (face,) * 4, [halves, faces])(cotangent)
    far = swapped(far, 1)
    near = swapped(near, 0)
    masks = shape(BRICKS * 6 * 2 * BRICKS, 128, dtype=F32)
    lifted_half = shape(2, 4 * CUBE, 128, dtype=F32)
    window_rows = pltpu.VMEM((8 * tiles + 8, 128), F32)
    band_one, band_back, masks, lifted_half = call(
        early_kernel,
        (shape(*BAND), shape(*BAND), masks, lifted_half),
        [window_rows, *links],
        hbm=(0,),
        inputs=5,
        cost=cost,
    )(face_links, own, up_weight, conv_one, conv_two)
    slope, hidden, turned, lifted_pad = call(
        first_kernel,
        (
            shape(ROWS, HALF, dtype=F32), volume, shape(HALF, ROWS), shape(*pad_shape),
        ),
        [pltpu.VMEM((2, 9 * CUBE, 128), F32), window_rows, *links],
        hbm=(0,),
        inputs=5,
    )(face_links, other, up_weight, band_one, lifted_half)
    share = 2 * -(-GROUPS * CHANNELS // everyone)
    packed_rows = (everyone * share, 128)
    sums, lifted = call(
        second_kernel,
        (shape(*packed_rows), volume),
        [pool, pool, pad, pltpu.VMEM(packed_rows, F32)],
        inputs=10,
    )(masks, cotangent, band_back, slope, turned, lifted_pad, high, low, far, near)
    parts = exchanged(sums)
    hidden_high, hidden_low, hidden_far, hidden_near = call(
        hidden_faces_kernel, (face,) * 4, [halves, faces], hbm=(1,), inputs=2
    )(hidden, parts)
    hidden_far = swapped(hidden_far, 1)
    hidden_near = swapped(hidden_near, 0)
    band_two = call(band_kernel, shape(*BAND), cost=cost)(conv_two)
    fine = call(fine_kernel, shape(*cotangent.shape), [pool, pool, pad], inputs=8, cost=cost)(
        masks, band_two, lifted, hidden, hidden_high, hidden_low, hidden_far, hidden_near
    )
    scale = 1.0 / math.sqrt(lax.axis_size("dp") * devices * BRICKS * EDGE**3)
    times = 4 if everyone % 32 == 0 else 1
    total = call(
        functools.partial(sum_kernel, everyone, scale),
        shape(*packed_rows),
        [
            pltpu.VMEM(packed_rows, F32),
            pltpu.VMEM((packed_rows[0] // times, 128), BF16),
            pltpu.SemaphoreType.DMA((times,)),
        ],
        out=pl.ANY,
    )(parts)
    gathered = exchanged(total)
    grads = shape(27, CHANNELS, CHANNELS, dtype=F32)
    block = pltpu.VMEM(grads.shape, F32)
    scratch = [pltpu.VMEM(packed_rows, F32), block, block]
    scratch += [pltpu.SemaphoreType.DMA((2, 3)), pltpu.SemaphoreType.DMA]
    grad_one, grad_two, fine = call(
        unpack_kernel, (grads, grads, shape(*fine.shape)), scratch, inputs=2, out=pl.ANY
    )(gathered, fine)
    return (fine, grad_one, grad_two)


def solution(mesh):
    return jax.shard_map(
        body,
        mesh=mesh,
        in_specs=(
            P("dp", "space", None),
            P("dp", None),
            P("dp", "space", None),
            P("dp", "space", None, None, None),
            P(),
            P(),
            P(),
        ),
        out_specs=(P("dp", "space", None, None, None), P(), P()),
        check_vma=False,
    )
```

```python
import functools
import math

import jax
import jax.numpy as jnp
from jax import lax
from jax.experimental import pallas as pl
from jax.experimental.pallas import tpu as pltpu
from jax.sharding import PartitionSpec as P

BF16 = jnp.bfloat16
F32 = jnp.float32
EDGE = 8
CHANNELS = 32
LINE = EDGE * CHANNELS
HALF = LINE // 2
WIDE = 2 * HALF
BRICKS = 2
CUBE = EDGE * EDGE
LINES = BRICKS * CUBE
BAND = (9, WIDE, HALF)
ROWS = 2 * LINES
FACE = 3 * EDGE
GROUPS = 7


def dot(left, right):
    return jnp.dot(left, right, preferred_element_type=F32)


def dot_rows(left, right):
    return lax.dot_general(left, right, (((0,), (0,)), ((), ())), preferred_element_type=F32)


def pair(halves_ref, start, count, stride=1):
    index = pl.ds(start, count, stride=stride) if stride > 1 else pl.ds(start, count)
    return halves_ref[0, index, :], halves_ref[1, index, :]


def lanes_of(shape):
    return lax.broadcasted_iota(jnp.int32, shape, len(shape) - 1)


def first_half(split):
    return lax.axis_index("dp") if split else 0


def pick_kernel(split, extras, ids_hbm, latents_hbm, *refs):
    brought = zip(refs[:extras], refs[extras + 1 : 2 * extras + 1])
    out_ref = refs[extras]
    ids_ref, latents_ref, rows_ref, blocks_ref, sems = refs[2 * extras + 1 :]
    ids_copy = pltpu.make_async_copy(ids_hbm, ids_ref, sems.at[0])
    latents_copy = pltpu.make_async_copy(latents_hbm, latents_ref, sems.at[1])
    ids_copy.start()
    latents_copy.start()
    others = [pltpu.make_async_copy(*pair, sems.at[2 + i]) for i, pair in enumerate(brought)]
    for copy in others:
        copy.start()
    held, width = latents_ref.shape[1:]
    bricks = ids_ref.shape[1]
    tiles = width // 256
    margin = 8 * tiles
    empty = jnp.zeros((margin, 128), F32)
    for half in range(2):
        rows_ref[half, 0:margin] = empty
        rows_ref[half, margin + bricks * tiles :] = empty
    first = lax.axis_index("space") * held
    rows = lax.broadcasted_iota(jnp.int32, (held, bricks), 0) + first
    ids_copy.wait()
    hot = jnp.where(rows == ids_ref[...], 1.0, 0.0).astype(BF16)
    latents_copy.wait()
    picked = dot_rows(hot, latents_ref[0])
    for tile in range(2 * tiles):
        place = pl.ds(margin + tile % tiles, bricks, stride=tiles)
        rows_ref[tile // tiles, place, :] = picked[:, tile * 128 : tile * 128 + 128]
    count = 3 * BRICKS * tiles
    straight = first_half(split) == 0
    for receiver in range(blocks_ref.shape[0] // (2 * count)):
        start = margin + BRICKS * (receiver - 1) * tiles
        halves = [rows_ref[half, start : start + count] for half in range(2)]
        for half in range(2):
            block = jnp.where(straight, halves[half], halves[1 - half]) if split else halves[half]
            place = (2 * receiver + half) * count
            blocks_ref[place : place + count] = block
    out_ref[...] = blocks_ref[...].astype(BF16)
    for copy in others:
        copy.wait()


def relay_kernel(split, received_ref, own_out, other_out, rows_ref):
    rows_ref[...] = received_ref[...].astype(F32)
    count = own_out.shape[0] * 3 // 4
    sums = []
    for half in range(2):
        total = None
        for start in range(half * count, rows_ref.shape[0], 2 * count):
            piece = rows_ref[start : start + count]
            total = piece if total is None else total + piece
        sums.append(jnp.concatenate([total, jnp.zeros((count // 3, 128), F32)], axis=0))
    straight = first_half(split) == 0
    own_out[...] = jnp.where(straight, sums[0], sums[1]).astype(BF16)
    other_out[...] = jnp.where(straight, sums[1], sums[0]).astype(BF16)


def build_band(band_ref, rows):
    shape = (3 * CHANNELS, HALF)
    row = lax.broadcasted_iota(jnp.int32, shape, 0)
    target = CHANNELS - (row // CHANNELS) * CHANNELS + row % CHANNELS
    distance = lanes_of(shape) - target
    band_ref[:, HALF:, :] = jnp.zeros((9, HALF, HALF), BF16)
    for z in range(-1, 5):
        select = jnp.where(distance == z * CHANNELS, 1.0, 0.0).astype(BF16)
        block = dot(rows, select).astype(BF16)
        start = z % 8 * CHANNELS
        band_ref[:, start : start + CHANNELS, :] = block.reshape(9, CHANNELS, HALF)


def weight_rows(weights):
    cube = weights.reshape(9, 3, CHANNELS, CHANNELS)
    rows = jnp.concatenate([cube[:, 0], cube[:, 1], cube[:, 2]], axis=-1)
    return rows.reshape(9 * CHANNELS, 3 * CHANNELS).astype(BF16)


def flipped_rows(weights):
    cube = jnp.swapaxes(weights, 1, 2).reshape(9, 3, CHANNELS, CHANNELS)
    pieces = [jnp.concatenate([cube[8 - k, 2], cube[8 - k, 1], cube[8 - k, 0]], axis=-1) for k in range(9)]
    return jnp.concatenate(pieces, axis=0).astype(BF16)


def band_kernel(weights_ref, band_ref):
    build_band(band_ref, weight_rows(weights_ref[...].astype(F32)))


def lift(half_ref, up_ref, rows_ref, volumes_ref, half):
    tiles = half_ref.shape[0] // 8
    rows_ref[: 8 * tiles] = half_ref[...].astype(F32)
    cells = []
    for tile in range(tiles):
        rows = rows_ref[pl.ds(tile, 8, stride=tiles), :]
        cells += [rows[:, :64], rows[:, 64:]]
    lifted = dot(jnp.concatenate(cells, axis=0).astype(BF16), up_ref[...])
    lifted = lifted.astype(BF16).astype(F32)
    first = 4 * CUBE * half
    for cell in range(4):
        b, c = cell // 2, cell % 2
        for sub in range(16):
            line = first + 8 * (sub // 4 * EDGE + 4 * b + sub % 4)
            volumes_ref[c, line : line + 8, :] = lifted[cell * 8 : cell * 8 + 8, sub * 128 : sub * 128 + 128]


def early_kernel(
    links_in, own_ref, up_ref, one_ref, two_ref,
    band_ref, back_ref, masks_ref, volumes_out,
    rows_ref, links_ref, links_sem,
):
    links_copy = pltpu.make_async_copy(links_in, links_ref, links_sem)
    links_copy.start()
    lift(own_ref, up_ref, rows_ref, volumes_out, 0)
    build_band(band_ref, weight_rows(one_ref[...].astype(F32)))
    build_band(back_ref, flipped_rows(two_ref[...].astype(F32)))
    links_copy.wait()
    put_masks(masks_ref, links_ref)


def put_padded(pad_ref, brick, lines, x_low, x_high, y_low, y_high, z_low, z_high):
    def joined(halves, before, after):
        lane = lanes_of(halves[0].shape)
        first = jnp.where(lane < CHANNELS, halves[1], before)
        second = jnp.where(lane >= HALF - CHANNELS, halves[0], after)
        return jnp.concatenate([halves[0], first], axis=-1), jnp.concatenate([halves[1], second], axis=-1)

    inside = joined(lines, z_low, z_high)
    x_low, x_high, y_low, y_high = [joined(face, 0.0, 0.0) for face in (x_low, x_high, y_low, y_high)]
    none = jnp.zeros((1, WIDE), F32)
    shifted = [[], [], []]
    for half in range(2):
        slabs = jnp.concatenate([x_low[half][None], inside[half], x_high[half][None]], axis=0)
        row = lax.broadcasted_iota(jnp.int32, slabs.shape, 1)
        low = jnp.concatenate([none, y_low[half], none], axis=0)[:, None, :]
        high = jnp.concatenate([none, y_high[half], none], axis=0)[:, None, :]
        shifted[0].append(jnp.where(row == 0, low, pltpu.roll(slabs, 1, 1)))
        shifted[1].append(slabs)
        shifted[2].append(jnp.where(row == EDGE - 1, high, pltpu.roll(slabs, EDGE - 1, 1)))
    for dy in range(3):
        pad_ref[dy, brick] = jnp.concatenate(shifted[dy], axis=1).astype(BF16)


def window(pad_ref, k):
    return pad_ref[k % 3, :, k // 3 : k // 3 + EDGE].reshape(ROWS, WIDE)


def convolve(pad_ref, band_ref):
    both, last = None, None
    for dy in range(3):
        slabs = pad_ref[dy, :, : EDGE + 1].reshape(-1, WIDE)
        term = dot(slabs, jnp.concatenate([band_ref[dy], band_ref[3 + dy]], axis=1))
        both = term if both is None else both + term
        term = dot(window(pad_ref, 6 + dy), band_ref[6 + dy])
        last = term if last is None else last + term
    both = both.reshape(BRICKS, EDGE + 1, 2 * EDGE, 2 * HALF)
    total = both[:, :EDGE, :, :HALF] + both[:, 1:, :, HALF:]
    return total.reshape(ROWS, HALF) + last


def half_lines(values):
    cube = values.reshape(BRICKS, EDGE, 2, EDGE, HALF)
    return [(cube[brick, :, 0], cube[brick, :, 1]) for brick in range(BRICKS)]


def put_halves(halves_ref, start, bricks):
    for brick, lines in enumerate(bricks):
        for half in range(2):
            first = start + brick * CUBE
            halves_ref[half, first : first + CUBE, :] = lines[half].reshape(CUBE, HALF)


def cotangent_lines(cotangent_ref):
    cube = cotangent_ref[...].astype(F32).reshape(BRICKS, EDGE, EDGE, LINE)
    return [(cube[brick, :, :, :HALF], cube[brick, :, :, HALF:]) for brick in range(BRICKS)]


def pack_faces(faces_ref, base, halves_ref, start, high):
    x_face = pair(halves_ref, start + ((EDGE - 1) * EDGE if high else 0), EDGE)
    y_face = pair(halves_ref, start + (EDGE - 1 if high else 0), EDGE, EDGE)
    for half in range(2):
        lanes = slice(half * HALF, half * HALF + HALF)
        faces_ref[base : base + EDGE, lanes] = x_face[half]
        faces_ref[base + EDGE : base + 2 * EDGE, lanes] = y_face[half]
    tile = halves_ref[1 if high else 0, start : start + CUBE, :]
    lane = lanes_of((16, 128)) // CHANNELS
    packed = jnp.zeros((16, 128), F32)
    for part in range(4):
        shift = (part + 1 if high else part) % 4 * CHANNELS
        piece = tile[part * 16 : part * 16 + 16]
        packed = jnp.where(lane == part, pltpu.roll(piece, shift, 1) if shift else piece, packed)
    faces_ref[base + 2 * EDGE : base + FACE, :128] = packed[:8]
    faces_ref[base + 2 * EDGE : base + FACE, 128:] = packed[8:]


def pack_all(bricks, halves_ref, faces_ref, high_out, low_out):
    put_halves(halves_ref, 0, bricks)
    for high, out_ref in ((True, high_out), (False, low_out)):
        for brick in range(BRICKS):
            pack_faces(faces_ref, brick * FACE, halves_ref, brick * CUBE, high)
        out_ref[...] = faces_ref[...].astype(BF16)


def to_partners(high_ref, low_ref, far_out, near_out):
    even = lax.axis_index("space") % 2 == 0
    far_out[...] = jnp.where(even, low_ref[...], high_ref[...])
    near_out[...] = jnp.where(even, high_ref[...], low_ref[...])


def faces_kernel(cotangent_ref, high_out, low_out, far_out, near_out, halves_ref, faces_ref):
    pack_all(cotangent_lines(cotangent_ref), halves_ref, faces_ref, high_out, low_out)
    to_partners(high_out, low_out, far_out, near_out)


def unpack_depth(halves, high):
    packed = jnp.concatenate(halves, axis=0)
    pieces = []
    for part in range(4):
        shift = ((3 - part) if high else (4 - part)) % 4 * CHANNELS
        pieces.append(pltpu.roll(packed, shift, 1) if shift else packed)
    return jnp.concatenate(pieces, axis=0).reshape(EDGE, EDGE, 128)


def first_kernel(
    links_in, other_ref, up_ref, band_ref, lifted_half,
    slope_out, hidden_out, turned_out, pad_out,
    volumes_ref, rows_ref, links_ref, links_sem,
):
    links_copy = pltpu.make_async_copy(links_in, links_ref, links_sem)
    links_copy.start()
    position = lax.axis_index("space")
    volumes_ref[:, : 4 * CUBE] = lifted_half[...]
    lift(other_ref, up_ref, rows_ref, volumes_ref, 1)
    links_copy.wait()
    for brick in range(BRICKS):

        def near(face):
            link = links_ref[0, brick, face]
            index = jnp.clip(link - BRICKS * (position - 1), 0, 3 * BRICKS - 1)
            return index, jnp.where(link >= 0, 1.0, 0.0).astype(F32)

        def x_face(face):
            index, present = near(face)
            line = EDGE * (EDGE - 1) if face % 2 == 0 else 0
            return [half * present for half in pair(volumes_ref, line * 8 + index, EDGE, 8)]

        def y_face(face):
            index, present = near(face)
            line = EDGE - 1 if face % 2 == 0 else 0
            return [half * present for half in pair(volumes_ref, line * 8 + index, EDGE, 8 * EDGE)]

        def z_face(face):
            index, present = near(face)
            tile = volumes_ref[1 if face % 2 == 0 else 0, pl.ds(index, CUBE, stride=8), :] * present
            return tile.reshape(EDGE, EDGE, HALF)

        own = [half.reshape(EDGE, EDGE, HALF) for half in pair(volumes_ref, BRICKS + brick, CUBE, 8)]
        put_padded(pad_out, brick, own, x_face(0), x_face(1), y_face(2), y_face(3), z_face(4), z_face(5))
    pre = convolve(pad_out, band_ref)
    sigmoid = 1.0 / (1.0 + jnp.exp(-pre))
    hidden = (pre * sigmoid).astype(BF16)
    slope_out[...] = sigmoid * (1.0 + pre * (1.0 - sigmoid))
    hidden_out[...] = hidden
    turned_out[...] = jnp.transpose(hidden)


def hidden_faces_kernel(hidden_ref, _parts, high_out, low_out, far_out, near_out, halves_ref, faces_ref):
    pack_all(half_lines(hidden_ref[...].astype(F32)), halves_ref, faces_ref, high_out, low_out)
    to_partners(high_out, low_out, far_out, near_out)


def picked(outer, places):
    lane = lanes_of((CHANNELS, 128)) // CHANNELS
    found = None
    for block in range(4):
        start, tile = places[block]
        rows = outer[start : start + CHANNELS, tile * 128 : tile * 128 + 128]
        found = rows if found is None else jnp.where(lane == block, rows, found)
    return found


def fold(four):
    lane = lanes_of((CHANNELS, 128)) // CHANNELS
    total = None
    for turn in range(4):
        mixed = four[0]
        for n in range(1, len(four)):
            mixed = jnp.where(lane == (n + turn) % 4, four[n], mixed)
        if turn:
            mixed = pltpu.roll(mixed, 128 - turn * CHANNELS, 1)
        total = mixed if total is None else total + mixed
    return total


def diagonal(shift):
    places = [None] * 4
    for z in range(4):
        other = z + shift
        places[other % 4] = (z * CHANNELS, 0 if 0 <= other < 4 else 1)
    return places


def put_masks(masks_ref, links_ref):
    position = lax.axis_index("space")
    for brick in range(BRICKS):
        for face in range(6):
            first = links_ref[0, brick, face] - BRICKS * (position - 1 if face % 2 == 0 else position)
            for i in range(2 * BRICKS):
                row = (brick * 6 + face) * 2 * BRICKS + i
                masks_ref[row : row + 1, :] = jnp.full((1, 128), jnp.where(first == i, 1.0, 0.0).astype(F32))


def pad_all(pad_ref, bricks, masks_ref, high_pool, low_pool, high_own, low_own, far, near):
    position = lax.axis_index("space")
    half = BRICKS * FACE
    even = position % 2 == 0
    high_pool[0:half] = jnp.where(even, far[...], near[...]).astype(F32)
    high_pool[half:] = high_own[...].astype(F32)
    low_pool[0:half] = low_own[...].astype(F32)
    low_pool[half:] = jnp.where(even, near[...], far[...]).astype(F32)
    for brick, lines in enumerate(bricks):

        def face(number, axis):
            pool = high_pool if number % 2 == 0 else low_pool
            total = [0.0, 0.0]
            for i in range(2 * BRICKS):
                row = (brick * 6 + number) * 2 * BRICKS + i
                mask = masks_ref[row : row + 1, :]
                start = i * FACE + axis * EDGE
                for part in range(2):
                    found = pool[start : start + EDGE, part * HALF : part * HALF + HALF]
                    total[part] = total[part] + found * mask
            return total

        put_padded(
            pad_ref, brick, lines, face(0, 0), face(1, 0), face(2, 1), face(3, 1),
            unpack_depth(face(4, 2), True), unpack_depth(face(5, 2), False),
        )


def second_kernel(
    masks_ref, cotangent_ref, band_ref, slope_ref, hidden_ref, lifted_pad, high_own, low_own, far, near,
    sums_out, lifted_out,
    high_pool, low_pool, cotangent_pad, sums_ref,
):
    lifted_out[...] = window(lifted_pad, 4)[:, :HALF]
    bricks = cotangent_lines(cotangent_ref)
    pad_all(cotangent_pad, bricks, masks_ref, high_pool, low_pool, high_own, low_own, far, near)
    gradient = (convolve(cotangent_pad, band_ref) * slope_ref[...]).astype(BF16)
    gradient = jnp.transpose(gradient)
    hidden = hidden_ref[...]
    if sums_ref.shape[0] > 2 * GROUPS * CHANNELS:
        rest = sums_ref.shape[0] - 2 * GROUPS * CHANNELS
        sums_ref[2 * GROUPS * CHANNELS :] = jnp.zeros((rest, 128), F32)
    ones, twos = [], []
    for k in range(9):
        one = dot(gradient, window(lifted_pad, k))
        two = dot(hidden, window(cotangent_pad, 8 - k))
        ones += [picked(one, diagonal(part - 1)) for part in range(3)]
        twos += [picked(two, diagonal(1 - part)) for part in range(3)]
        while len(ones) >= 4 or (k == 8 and ones):
            group = (3 * k + 3 - len(ones)) // 4
            for first, blocks in ((0, ones), (GROUPS, twos)):
                start = (first + group) * CHANNELS
                sums_ref[start : start + CHANNELS] = fold(blocks[:4])
            ones, twos = ones[4:], twos[4:]
    sums_out[...] = sums_ref[...].astype(BF16)


def fine_kernel(
    masks_ref, band_ref, lifted_ref, hidden_ref, high_own, low_own, far, near,
    fine_out, high_pool, low_pool, hidden_pad,
):
    bricks = half_lines(hidden_ref[...].astype(F32))
    pad_all(hidden_pad, bricks, masks_ref, high_pool, low_pool, high_own, low_own, far, near)
    fine = lifted_ref[...].astype(F32) + convolve(hidden_pad, band_ref)
    fine = fine.reshape(LINES // EDGE, 2, EDGE, HALF)
    fine = jnp.concatenate([fine[:, 0], fine[:, 1]], axis=-1)
    fine_out[...] = fine.astype(BF16).reshape(fine_out.shape)


def sum_kernel(devices, scale, parts_ref, out_hbm, rows_ref, shares_ref, sems):
    rows_ref[...] = parts_ref[...].astype(F32)
    share = rows_ref.shape[0] // devices
    pieces = [rows_ref[share * i : share * i + share] for i in range(devices)]
    while len(pieces) > 1:
        pairs = [a + b for a, b in zip(pieces[::2], pieces[1::2])]
        pieces = pairs + pieces[len(pieces) - len(pieces) % 2 :]
    total = pieces[0] * scale
    some = shares_ref.shape[0]
    for i in range(some // share):
        rows_ref[share * i : share * i + share] = total
    shares_ref[...] = rows_ref[0:some].astype(BF16)
    copies = []
    for i in range(out_hbm.shape[0] // some):
        copies.append(pltpu.make_async_copy(shares_ref, out_hbm.at[pl.ds(some * i, some)], sems.at[i]))
        copies[-1].start()
    for copy in copies:
        copy.wait()


def unpack_kernel(sums_ref, fine_ref, one_out, two_out, fine_out, rows_ref, one_ref, two_ref, sems, fine_sem):
    fine_copy = pltpu.make_async_copy(fine_ref, fine_out, fine_sem)
    fine_copy.start()
    rows_ref[...] = sums_ref[...].astype(F32)
    copies = []
    for which, (block_ref, out) in ((1, (two_ref, two_out)), (0, (one_ref, one_out))):
        for part, (first, last) in enumerate(((0, 2), (2, 4), (4, GROUPS))):
            for group in range(first, last):
                start = (which * GROUPS + group) * CHANNELS
                four = rows_ref[start : start + CHANNELS]
                turned = None if which else jnp.transpose(four)
                for n in range(min(4, 27 - 4 * group)):
                    if which:
                        block = pltpu.roll(four, 128 - n * CHANNELS, 1) if n else four
                        block_ref[4 * group + n] = block[:, :CHANNELS]
                    else:
                        block_ref[4 * group + n] = turned[CHANNELS * n : CHANNELS * n + CHANNELS]
            span = pl.ds(4 * first, min(4 * last, 27) - 4 * first)
            copies.append(pltpu.make_async_copy(block_ref.at[span], out.at[span], sems.at[which, part]))
            copies[-1].start()
    for copy in copies:
        copy.wait()
    fine_copy.wait()


def call(kernel, out_shape, scratch=(), hbm=(), inputs=1, limit=24, cost=None, out=pltpu.VMEM):
    spaces = [pl.ANY if i in hbm else pltpu.VMEM for i in range(inputs)]
    return pl.pallas_call(
        kernel,
        out_shape=out_shape,
        in_specs=[pl.BlockSpec(memory_space=space) for space in spaces],
        out_specs=jax.tree.map(lambda _: pl.BlockSpec(memory_space=out), out_shape),
        scratch_shapes=list(scratch),
        compiler_params=pltpu.CompilerParams(vmem_limit_bytes=limit * 2**20),
        cost_estimate=cost,
    )


def shape(*dims, dtype=BF16):
    return jax.ShapeDtypeStruct(dims, dtype)


def kept_in_hbm(value):
    return pltpu.with_memory_space_constraint(value, pltpu.HBM)


def swapped(value, first):
    pairs = [(i, i + 1) for i in range(first, lax.axis_size("space") - 1, 2)]
    return lax.ppermute(value, "space", pairs + [(target, source) for source, target in pairs])


def exchanged(rows, axes=("space", "dp")):
    count = math.prod(lax.axis_size(axis) for axis in axes)
    shares = rows.reshape(count, -1, 2, 128)
    shares = lax.all_to_all(shares, axes, split_axis=0, concat_axis=0, tiled=True)
    return shares.reshape(rows.shape)


def body(coarse_latents, active_blocks, face_links, cotangent, up_weight, conv_one, conv_two):
    devices = lax.axis_size("space")
    everyone = devices * lax.axis_size("dp")
    held, width = coarse_latents.shape[1:]
    bricks = active_blocks.shape[1]
    split = lax.axis_size("dp") == 2
    tiles = width // 256
    count = 3 * BRICKS * tiles
    blocks = (2 * devices * count, 128)
    extras = (conv_one, conv_two, face_links)
    packed, conv_one, conv_two, face_links = call(
        functools.partial(pick_kernel, split, len(extras)),
        (shape(*blocks), *[shape(*extra.shape, dtype=extra.dtype) for extra in extras]),
        [
            pltpu.VMEM((1, bricks), jnp.int32),
            pltpu.VMEM((1, held, width), BF16),
            pltpu.VMEM((2, (bricks + 16) * tiles, 128), F32),
            pltpu.VMEM(blocks, F32),
            pltpu.SemaphoreType.DMA((2 + len(extras),)),
        ],
        hbm=range(2 + len(extras)),
        inputs=2 + len(extras),
    )(*[kept_in_hbm(operand) for operand in (active_blocks, coarse_latents, *extras)])
    received = exchanged(packed, ("space", "dp") if split else ("space",))
    window_half = shape(8 * tiles, 128)
    own, other = call(
        functools.partial(relay_kernel, split), (window_half, window_half), [pltpu.VMEM(blocks, F32)]
    )(received)
    if split:
        other = lax.ppermute(other, "dp", [(0, 1), (1, 0)])
    cost = pl.CostEstimate(flops=10**9, bytes_accessed=2 * 10**6, transcendentals=0)
    face = shape(BRICKS * FACE, LINE)
    halves = pltpu.VMEM((2, LINES + 8, HALF), F32)
    faces = pltpu.VMEM((BRICKS * FACE, LINE), F32)
    pool = pltpu.VMEM((2 * BRICKS * FACE, LINE), F32)
    volume = shape(ROWS, HALF)
    links = [pltpu.SMEM(face_links.shape, jnp.int32), pltpu.SemaphoreType.DMA]
    pad_shape = (3, BRICKS, EDGE + 2, 2 * EDGE, WIDE)
    pad = pltpu.VMEM(pad_shape, BF16)
    high, low, far, near = call(faces_kernel, (face,) * 4, [halves, faces])(cotangent)
    far = swapped(far, 1)
    near = swapped(near, 0)
    masks = shape(BRICKS * 6 * 2 * BRICKS, 128, dtype=F32)
    lifted_half = shape(2, 4 * CUBE, 128, dtype=F32)
    window_rows = pltpu.VMEM((8 * tiles + 8, 128), F32)
    band_one, band_back, masks, lifted_half = call(
        early_kernel,
        (shape(*BAND), shape(*BAND), masks, lifted_half),
        [window_rows, *links],
        hbm=(0,),
        inputs=5,
        cost=cost,
    )(face_links, own, up_weight, conv_one, conv_two)
    slope, hidden, turned, lifted_pad = call(
        first_kernel,
        (
            shape(ROWS, HALF, dtype=F32), volume, shape(HALF, ROWS), shape(*pad_shape),
        ),
        [pltpu.VMEM((2, 9 * CUBE, 128), F32), window_rows, *links],
        hbm=(0,),
        inputs=5,
    )(face_links, other, up_weight, band_one, lifted_half)
    share = 2 * -(-GROUPS * CHANNELS // everyone)
    packed_rows = (everyone * share, 128)
    sums, lifted = call(
        second_kernel,
        (shape(*packed_rows), volume),
        [pool, pool, pad, pltpu.VMEM(packed_rows, F32)],
        inputs=10,
    )(masks, cotangent, band_back, slope, turned, lifted_pad, high, low, far, near)
    parts = exchanged(sums)
    hidden_high, hidden_low, hidden_far, hidden_near = call(
        hidden_faces_kernel, (face,) * 4, [halves, faces], hbm=(1,), inputs=2
    )(hidden, parts)
    hidden_far = swapped(hidden_far, 1)
    hidden_near = swapped(hidden_near, 0)
    band_two = call(band_kernel, shape(*BAND), cost=cost)(conv_two)
    fine = call(fine_kernel, shape(*cotangent.shape), [pool, pool, pad], inputs=8, cost=cost)(
        masks, band_two, lifted, hidden, hidden_high, hidden_low, hidden_far, hidden_near
    )
    scale = 1.0 / math.sqrt(lax.axis_size("dp") * devices * BRICKS * EDGE**3)
    times = 4 if everyone % 32 == 0 else 1
    total = call(
        functools.partial(sum_kernel, everyone, scale),
        shape(*packed_rows),
        [
            pltpu.VMEM(packed_rows, F32),
            pltpu.VMEM((packed_rows[0] // times, 128), BF16),
            pltpu.SemaphoreType.DMA((times,)),
        ],
        out=pl.ANY,
    )(parts)
    gathered = exchanged(total)
    grads = shape(27, CHANNELS, CHANNELS, dtype=F32)
    block = pltpu.VMEM(grads.shape, F32)
    scratch = [pltpu.VMEM(packed_rows, F32), block, block]
    scratch += [pltpu.SemaphoreType.DMA((2, 3)), pltpu.SemaphoreType.DMA]
    grad_one, grad_two, fine = call(
        unpack_kernel, (grads, grads, shape(*fine.shape)), scratch, inputs=2, out=pl.ANY
    )(gathered, fine)
    return (fine, grad_one, grad_two)


def solution(mesh):
    return jax.shard_map(
        body,
        mesh=mesh,
        in_specs=(
            P("dp", "space", None),
            P("dp", None),
            P("dp", "space", None),
            P("dp", "space", None, None, None),
            P(),
            P(),
            P(),
        ),
        out_specs=(P("dp", "space", None, None, None), P(), P()),
        check_vma=False,
    )
```

```python
import functools
import math

import jax
import jax.numpy as jnp
from jax import lax
from jax.experimental import pallas as pl
from jax.experimental.pallas import tpu as pltpu
from jax.sharding import PartitionSpec as P

BF16 = jnp.bfloat16
F32 = jnp.float32
EDGE = 8
CHANNELS = 32
LINE = EDGE * CHANNELS
HALF = LINE // 2
WIDE = 2 * HALF
BRICKS = 2
CUBE = EDGE * EDGE
LINES = BRICKS * CUBE
BAND = (9, WIDE, HALF)
ROWS = 2 * LINES
FACE = 3 * EDGE
GROUPS = 7


def dot(left, right):
    return jnp.dot(left, right, preferred_element_type=F32)


def dot_rows(left, right):
    return lax.dot_general(left, right, (((0,), (0,)), ((), ())), preferred_element_type=F32)


def pair(halves_ref, start, count, stride=1):
    index = pl.ds(start, count, stride=stride) if stride > 1 else pl.ds(start, count)
    return halves_ref[0, index, :], halves_ref[1, index, :]


def lanes_of(shape):
    return lax.broadcasted_iota(jnp.int32, shape, len(shape) - 1)


def first_half(split):
    return lax.axis_index("dp") if split else 0


def pick_kernel(split, extras, ids_hbm, latents_hbm, *refs):
    brought = zip(refs[:extras], refs[extras + 1 : 2 * extras + 1])
    out_ref = refs[extras]
    ids_ref, latents_ref, rows_ref, blocks_ref, sems = refs[2 * extras + 1 :]
    ids_copy = pltpu.make_async_copy(ids_hbm, ids_ref, sems.at[0])
    latents_copy = pltpu.make_async_copy(latents_hbm, latents_ref, sems.at[1])
    ids_copy.start()
    latents_copy.start()
    others = [pltpu.make_async_copy(*pair, sems.at[2 + i]) for i, pair in enumerate(brought)]
    for copy in others:
        copy.start(priority=1)
    held, width = latents_ref.shape[1:]
    bricks = ids_ref.shape[1]
    tiles = width // 256
    margin = 8 * tiles
    empty = jnp.zeros((margin, 128), F32)
    for half in range(2):
        rows_ref[half, 0:margin] = empty
        rows_ref[half, margin + bricks * tiles :] = empty
    first = lax.axis_index("space") * held
    rows = lax.broadcasted_iota(jnp.int32, (held, bricks), 0) + first
    ids_copy.wait()
    hot = jnp.where(rows == ids_ref[...], 1.0, 0.0).astype(BF16)
    latents_copy.wait()
    picked = dot_rows(hot, latents_ref[0])
    for tile in range(2 * tiles):
        place = pl.ds(margin + tile % tiles, bricks, stride=tiles)
        rows_ref[tile // tiles, place, :] = picked[:, tile * 128 : tile * 128 + 128]
    count = 3 * BRICKS * tiles
    straight = first_half(split) == 0
    for receiver in range(blocks_ref.shape[0] // (2 * count)):
        start = margin + BRICKS * (receiver - 1) * tiles
        halves = [rows_ref[half, start : start + count] for half in range(2)]
        for half in range(2):
            block = jnp.where(straight, halves[half], halves[1 - half]) if split else halves[half]
            place = (2 * receiver + half) * count
            blocks_ref[place : place + count] = block
    out_ref[...] = blocks_ref[...].astype(BF16)
    for copy in others:
        copy.wait()


def relay_kernel(split, received_ref, own_out, other_out, rows_ref):
    rows_ref[...] = received_ref[...].astype(F32)
    count = own_out.shape[0] * 3 // 4
    sums = []
    for half in range(2):
        total = None
        for start in range(half * count, rows_ref.shape[0], 2 * count):
            piece = rows_ref[start : start + count]
            total = piece if total is None else total + piece
        sums.append(jnp.concatenate([total, jnp.zeros((count // 3, 128), F32)], axis=0))
    straight = first_half(split) == 0
    own_out[...] = jnp.where(straight, sums[0], sums[1]).astype(BF16)
    other_out[...] = jnp.where(straight, sums[1], sums[0]).astype(BF16)


def build_band(band_ref, rows):
    shape = (3 * CHANNELS, HALF)
    row = lax.broadcasted_iota(jnp.int32, shape, 0)
    target = CHANNELS - (row // CHANNELS) * CHANNELS + row % CHANNELS
    distance = lanes_of(shape) - target
    band_ref[:, HALF:, :] = jnp.zeros((9, HALF, HALF), BF16)
    for z in range(-1, 5):
        select = jnp.where(distance == z * CHANNELS, 1.0, 0.0).astype(BF16)
        block = dot(rows, select).astype(BF16)
        start = z % 8 * CHANNELS
        band_ref[:, start : start + CHANNELS, :] = block.reshape(9, CHANNELS, HALF)


def weight_rows(weights):
    cube = weights.reshape(9, 3, CHANNELS, CHANNELS)
    rows = jnp.concatenate([cube[:, 0], cube[:, 1], cube[:, 2]], axis=-1)
    return rows.reshape(9 * CHANNELS, 3 * CHANNELS).astype(BF16)


def flipped_rows(weights):
    cube = jnp.swapaxes(weights, 1, 2).reshape(9, 3, CHANNELS, CHANNELS)
    pieces = [jnp.concatenate([cube[8 - k, 2], cube[8 - k, 1], cube[8 - k, 0]], axis=-1) for k in range(9)]
    return jnp.concatenate(pieces, axis=0).astype(BF16)


def band_kernel(weights_ref, band_ref):
    build_band(band_ref, weight_rows(weights_ref[...].astype(F32)))


def lift(half_ref, up_ref, rows_ref, volumes_ref, half):
    tiles = half_ref.shape[0] // 8
    rows_ref[: 8 * tiles] = half_ref[...].astype(F32)
    cells = []
    for tile in range(tiles):
        rows = rows_ref[pl.ds(tile, 8, stride=tiles), :]
        cells += [rows[:, :64], rows[:, 64:]]
    lifted = dot(jnp.concatenate(cells, axis=0).astype(BF16), up_ref[...])
    lifted = lifted.astype(BF16).astype(F32)
    first = 4 * CUBE * half
    for cell in range(4):
        b, c = cell // 2, cell % 2
        for sub in range(16):
            line = first + 8 * (sub // 4 * EDGE + 4 * b + sub % 4)
            volumes_ref[c, line : line + 8, :] = lifted[cell * 8 : cell * 8 + 8, sub * 128 : sub * 128 + 128]


def early_kernel(
    links_in, own_ref, up_ref, one_ref, two_ref,
    band_ref, back_ref, masks_ref, volumes_out,
    rows_ref, links_ref, links_sem,
):
    links_copy = pltpu.make_async_copy(links_in, links_ref, links_sem)
    links_copy.start()
    lift(own_ref, up_ref, rows_ref, volumes_out, 0)
    build_band(band_ref, weight_rows(one_ref[...].astype(F32)))
    build_band(back_ref, flipped_rows(two_ref[...].astype(F32)))
    links_copy.wait()
    put_masks(masks_ref, links_ref)


def put_padded(pad_ref, brick, lines, x_low, x_high, y_low, y_high, z_low, z_high):
    def joined(halves, before, after):
        lane = lanes_of(halves[0].shape)
        first = jnp.where(lane < CHANNELS, halves[1], before)
        second = jnp.where(lane >= HALF - CHANNELS, halves[0], after)
        return jnp.concatenate([halves[0], first], axis=-1), jnp.concatenate([halves[1], second], axis=-1)

    inside = joined(lines, z_low, z_high)
    x_low, x_high, y_low, y_high = [joined(face, 0.0, 0.0) for face in (x_low, x_high, y_low, y_high)]
    none = jnp.zeros((1, WIDE), F32)
    shifted = [[], [], []]
    for half in range(2):
        slabs = jnp.concatenate([x_low[half][None], inside[half], x_high[half][None]], axis=0)
        row = lax.broadcasted_iota(jnp.int32, slabs.shape, 1)
        low = jnp.concatenate([none, y_low[half], none], axis=0)[:, None, :]
        high = jnp.concatenate([none, y_high[half], none], axis=0)[:, None, :]
        shifted[0].append(jnp.where(row == 0, low, pltpu.roll(slabs, 1, 1)))
        shifted[1].append(slabs)
        shifted[2].append(jnp.where(row == EDGE - 1, high, pltpu.roll(slabs, EDGE - 1, 1)))
    for dy in range(3):
        pad_ref[dy, brick] = jnp.concatenate(shifted[dy], axis=1).astype(BF16)


def window(pad_ref, k):
    return pad_ref[k % 3, :, k // 3 : k // 3 + EDGE].reshape(ROWS, WIDE)


def convolve(pad_ref, band_ref):
    both, last = None, None
    for dy in range(3):
        slabs = pad_ref[dy, :, : EDGE + 1].reshape(-1, WIDE)
        term = dot(slabs, jnp.concatenate([band_ref[dy], band_ref[3 + dy]], axis=1))
        both = term if both is None else both + term
        term = dot(window(pad_ref, 6 + dy), band_ref[6 + dy])
        last = term if last is None else last + term
    both = both.reshape(BRICKS, EDGE + 1, 2 * EDGE, 2 * HALF)
    total = both[:, :EDGE, :, :HALF] + both[:, 1:, :, HALF:]
    return total.reshape(ROWS, HALF) + last


def half_lines(values):
    cube = values.reshape(BRICKS, EDGE, 2, EDGE, HALF)
    return [(cube[brick, :, 0], cube[brick, :, 1]) for brick in range(BRICKS)]


def put_halves(halves_ref, start, bricks):
    for brick, lines in enumerate(bricks):
        for half in range(2):
            first = start + brick * CUBE
            halves_ref[half, first : first + CUBE, :] = lines[half].reshape(CUBE, HALF)


def cotangent_lines(cotangent_ref):
    cube = cotangent_ref[...].astype(F32).reshape(BRICKS, EDGE, EDGE, LINE)
    return [(cube[brick, :, :, :HALF], cube[brick, :, :, HALF:]) for brick in range(BRICKS)]


def pack_faces(faces_ref, base, halves_ref, start, high):
    x_face = pair(halves_ref, start + ((EDGE - 1) * EDGE if high else 0), EDGE)
    y_face = pair(halves_ref, start + (EDGE - 1 if high else 0), EDGE, EDGE)
    for half in range(2):
        lanes = slice(half * HALF, half * HALF + HALF)
        faces_ref[base : base + EDGE, lanes] = x_face[half]
        faces_ref[base + EDGE : base + 2 * EDGE, lanes] = y_face[half]
    tile = halves_ref[1 if high else 0, start : start + CUBE, :]
    lane = lanes_of((16, 128)) // CHANNELS
    packed = jnp.zeros((16, 128), F32)
    for part in range(4):
        shift = (part + 1 if high else part) % 4 * CHANNELS
        piece = tile[part * 16 : part * 16 + 16]
        packed = jnp.where(lane == part, pltpu.roll(piece, shift, 1) if shift else piece, packed)
    faces_ref[base + 2 * EDGE : base + FACE, :128] = packed[:8]
    faces_ref[base + 2 * EDGE : base + FACE, 128:] = packed[8:]


def pack_all(bricks, halves_ref, faces_ref, high_out, low_out):
    put_halves(halves_ref, 0, bricks)
    for high, out_ref in ((True, high_out), (False, low_out)):
        for brick in range(BRICKS):
            pack_faces(faces_ref, brick * FACE, halves_ref, brick * CUBE, high)
        out_ref[...] = faces_ref[...].astype(BF16)


def to_partners(high_ref, low_ref, far_out, near_out):
    even = lax.axis_index("space") % 2 == 0
    far_out[...] = jnp.where(even, low_ref[...], high_ref[...])
    near_out[...] = jnp.where(even, high_ref[...], low_ref[...])


def faces_kernel(cotangent_ref, high_out, low_out, far_out, near_out, halves_ref, faces_ref):
    pack_all(cotangent_lines(cotangent_ref), halves_ref, faces_ref, high_out, low_out)
    to_partners(high_out, low_out, far_out, near_out)


def unpack_depth(halves, high):
    packed = jnp.concatenate(halves, axis=0)
    pieces = []
    for part in range(4):
        shift = ((3 - part) if high else (4 - part)) % 4 * CHANNELS
        pieces.append(pltpu.roll(packed, shift, 1) if shift else packed)
    return jnp.concatenate(pieces, axis=0).reshape(EDGE, EDGE, 128)


def first_kernel(
    links_in, other_ref, up_ref, band_ref, lifted_half,
    slope_out, hidden_out, turned_out, pad_out,
    volumes_ref, rows_ref, links_ref, links_sem,
):
    links_copy = pltpu.make_async_copy(links_in, links_ref, links_sem)
    links_copy.start()
    position = lax.axis_index("space")
    volumes_ref[:, : 4 * CUBE] = lifted_half[...]
    lift(other_ref, up_ref, rows_ref, volumes_ref, 1)
    links_copy.wait()
    for brick in range(BRICKS):

        def near(face):
            link = links_ref[0, brick, face]
            index = jnp.clip(link - BRICKS * (position - 1), 0, 3 * BRICKS - 1)
            return index, jnp.where(link >= 0, 1.0, 0.0).astype(F32)

        def x_face(face):
            index, present = near(face)
            line = EDGE * (EDGE - 1) if face % 2 == 0 else 0
            return [half * present for half in pair(volumes_ref, line * 8 + index, EDGE, 8)]

        def y_face(face):
            index, present = near(face)
            line = EDGE - 1 if face % 2 == 0 else 0
            return [half * present for half in pair(volumes_ref, line * 8 + index, EDGE, 8 * EDGE)]

        def z_face(face):
            index, present = near(face)
            tile = volumes_ref[1 if face % 2 == 0 else 0, pl.ds(index, CUBE, stride=8), :] * present
            return tile.reshape(EDGE, EDGE, HALF)

        own = [half.reshape(EDGE, EDGE, HALF) for half in pair(volumes_ref, BRICKS + brick, CUBE, 8)]
        put_padded(pad_out, brick, own, x_face(0), x_face(1), y_face(2), y_face(3), z_face(4), z_face(5))
    pre = convolve(pad_out, band_ref)
    sigmoid = 1.0 / (1.0 + jnp.exp(-pre))
    hidden = (pre * sigmoid).astype(BF16)
    slope_out[...] = sigmoid * (1.0 + pre * (1.0 - sigmoid))
    hidden_out[...] = hidden
    turned_out[...] = jnp.transpose(hidden)


def hidden_faces_kernel(hidden_ref, _parts, high_out, low_out, far_out, near_out, halves_ref, faces_ref):
    pack_all(half_lines(hidden_ref[...].astype(F32)), halves_ref, faces_ref, high_out, low_out)
    to_partners(high_out, low_out, far_out, near_out)


def picked(outer, places):
    lane = lanes_of((CHANNELS, 128)) // CHANNELS
    found = None
    for block in range(4):
        start, tile = places[block]
        rows = outer[start : start + CHANNELS, tile * 128 : tile * 128 + 128]
        found = rows if found is None else jnp.where(lane == block, rows, found)
    return found


def fold(four):
    lane = lanes_of((CHANNELS, 128)) // CHANNELS
    total = None
    for turn in range(4):
        mixed = four[0]
        for n in range(1, len(four)):
            mixed = jnp.where(lane == (n + turn) % 4, four[n], mixed)
        if turn:
            mixed = pltpu.roll(mixed, 128 - turn * CHANNELS, 1)
        total = mixed if total is None else total + mixed
    return total


def diagonal(shift):
    places = [None] * 4
    for z in range(4):
        other = z + shift
        places[other % 4] = (z * CHANNELS, 0 if 0 <= other < 4 else 1)
    return places


def put_masks(masks_ref, links_ref):
    position = lax.axis_index("space")
    for brick in range(BRICKS):
        for face in range(6):
            first = links_ref[0, brick, face] - BRICKS * (position - 1 if face % 2 == 0 else position)
            for i in range(2 * BRICKS):
                row = (brick * 6 + face) * 2 * BRICKS + i
                masks_ref[row : row + 1, :] = jnp.full((1, 128), jnp.where(first == i, 1.0, 0.0).astype(F32))


def pad_all(pad_ref, bricks, masks_ref, high_pool, low_pool, high_own, low_own, far, near):
    position = lax.axis_index("space")
    half = BRICKS * FACE
    even = position % 2 == 0
    high_pool[0:half] = jnp.where(even, far[...], near[...]).astype(F32)
    high_pool[half:] = high_own[...].astype(F32)
    low_pool[0:half] = low_own[...].astype(F32)
    low_pool[half:] = jnp.where(even, near[...], far[...]).astype(F32)
    for brick, lines in enumerate(bricks):

        def face(number, axis):
            pool = high_pool if number % 2 == 0 else low_pool
            total = [0.0, 0.0]
            for i in range(2 * BRICKS):
                row = (brick * 6 + number) * 2 * BRICKS + i
                mask = masks_ref[row : row + 1, :]
                start = i * FACE + axis * EDGE
                for part in range(2):
                    found = pool[start : start + EDGE, part * HALF : part * HALF + HALF]
                    total[part] = total[part] + found * mask
            return total

        put_padded(
            pad_ref, brick, lines, face(0, 0), face(1, 0), face(2, 1), face(3, 1),
            unpack_depth(face(4, 2), True), unpack_depth(face(5, 2), False),
        )


def second_kernel(
    masks_ref, cotangent_ref, band_ref, slope_ref, hidden_ref, lifted_pad, high_own, low_own, far, near,
    sums_out, lifted_out,
    high_pool, low_pool, cotangent_pad, sums_ref,
):
    lifted_out[...] = window(lifted_pad, 4)[:, :HALF]
    bricks = cotangent_lines(cotangent_ref)
    pad_all(cotangent_pad, bricks, masks_ref, high_pool, low_pool, high_own, low_own, far, near)
    gradient = (convolve(cotangent_pad, band_ref) * slope_ref[...]).astype(BF16)
    gradient = jnp.transpose(gradient)
    hidden = hidden_ref[...]
    if sums_ref.shape[0] > 2 * GROUPS * CHANNELS:
        rest = sums_ref.shape[0] - 2 * GROUPS * CHANNELS
        sums_ref[2 * GROUPS * CHANNELS :] = jnp.zeros((rest, 128), F32)
    ones, twos = [], []
    for k in range(9):
        one = dot(gradient, window(lifted_pad, k))
        two = dot(hidden, window(cotangent_pad, 8 - k))
        ones += [picked(one, diagonal(part - 1)) for part in range(3)]
        twos += [picked(two, diagonal(1 - part)) for part in range(3)]
        while len(ones) >= 4 or (k == 8 and ones):
            group = (3 * k + 3 - len(ones)) // 4
            for first, blocks in ((0, ones), (GROUPS, twos)):
                start = (first + group) * CHANNELS
                sums_ref[start : start + CHANNELS] = fold(blocks[:4])
            ones, twos = ones[4:], twos[4:]
    sums_out[...] = sums_ref[...].astype(BF16)


def fine_kernel(
    masks_ref, band_ref, lifted_ref, hidden_ref, high_own, low_own, far, near,
    fine_out, high_pool, low_pool, hidden_pad,
):
    bricks = half_lines(hidden_ref[...].astype(F32))
    pad_all(hidden_pad, bricks, masks_ref, high_pool, low_pool, high_own, low_own, far, near)
    fine = lifted_ref[...].astype(F32) + convolve(hidden_pad, band_ref)
    fine = fine.reshape(LINES // EDGE, 2, EDGE, HALF)
    fine = jnp.concatenate([fine[:, 0], fine[:, 1]], axis=-1)
    fine_out[...] = fine.astype(BF16).reshape(fine_out.shape)


def sum_kernel(devices, scale, parts_ref, out_hbm, rows_ref, shares_ref, sems):
    rows_ref[...] = parts_ref[...].astype(F32)
    share = rows_ref.shape[0] // devices
    pieces = [rows_ref[share * i : share * i + share] for i in range(devices)]
    while len(pieces) > 1:
        pairs = [a + b for a, b in zip(pieces[::2], pieces[1::2])]
        pieces = pairs + pieces[len(pieces) - len(pieces) % 2 :]
    total = pieces[0] * scale
    some = shares_ref.shape[0]
    for i in range(some // share):
        rows_ref[share * i : share * i + share] = total
    shares_ref[...] = rows_ref[0:some].astype(BF16)
    copies = []
    for i in range(out_hbm.shape[0] // some):
        copies.append(pltpu.make_async_copy(shares_ref, out_hbm.at[pl.ds(some * i, some)], sems.at[i]))
        copies[-1].start()
    for copy in copies:
        copy.wait()


def unpack_kernel(sums_ref, fine_ref, one_out, two_out, fine_out, rows_ref, one_ref, two_ref, sems, fine_sem):
    fine_copy = pltpu.make_async_copy(fine_ref, fine_out, fine_sem)
    fine_copy.start()
    rows_ref[...] = sums_ref[...].astype(F32)
    copies = []
    for which, (block_ref, out) in ((1, (two_ref, two_out)), (0, (one_ref, one_out))):
        for part, (first, last) in enumerate(((0, 2), (2, 4), (4, GROUPS))):
            for group in range(first, last):
                start = (which * GROUPS + group) * CHANNELS
                four = rows_ref[start : start + CHANNELS]
                turned = None if which else jnp.transpose(four)
                for n in range(min(4, 27 - 4 * group)):
                    if which:
                        block = pltpu.roll(four, 128 - n * CHANNELS, 1) if n else four
                        block_ref[4 * group + n] = block[:, :CHANNELS]
                    else:
                        block_ref[4 * group + n] = turned[CHANNELS * n : CHANNELS * n + CHANNELS]
            span = pl.ds(4 * first, min(4 * last, 27) - 4 * first)
            copies.append(pltpu.make_async_copy(block_ref.at[span], out.at[span], sems.at[which, part]))
            copies[-1].start()
    for copy in copies:
        copy.wait()
    fine_copy.wait()


def call(kernel, out_shape, scratch=(), hbm=(), inputs=1, limit=24, cost=None, out=pltpu.VMEM):
    spaces = [pl.ANY if i in hbm else pltpu.VMEM for i in range(inputs)]
    return pl.pallas_call(
        kernel,
        out_shape=out_shape,
        in_specs=[pl.BlockSpec(memory_space=space) for space in spaces],
        out_specs=jax.tree.map(lambda _: pl.BlockSpec(memory_space=out), out_shape),
        scratch_shapes=list(scratch),
        compiler_params=pltpu.CompilerParams(vmem_limit_bytes=limit * 2**20),
        cost_estimate=cost,
    )


def shape(*dims, dtype=BF16):
    return jax.ShapeDtypeStruct(dims, dtype)


def kept_in_hbm(value):
    return pltpu.with_memory_space_constraint(value, pltpu.HBM)


def swapped(value, first):
    pairs = [(i, i + 1) for i in range(first, lax.axis_size("space") - 1, 2)]
    return lax.ppermute(value, "space", pairs + [(target, source) for source, target in pairs])


def exchanged(rows, axes=("space", "dp")):
    count = math.prod(lax.axis_size(axis) for axis in axes)
    shares = rows.reshape(count, -1, 2, 128)
    shares = lax.all_to_all(shares, axes, split_axis=0, concat_axis=0, tiled=True)
    return shares.reshape(rows.shape)


def body(coarse_latents, active_blocks, face_links, cotangent, up_weight, conv_one, conv_two):
    devices = lax.axis_size("space")
    everyone = devices * lax.axis_size("dp")
    held, width = coarse_latents.shape[1:]
    bricks = active_blocks.shape[1]
    split = lax.axis_size("dp") == 2
    tiles = width // 256
    count = 3 * BRICKS * tiles
    blocks = (2 * devices * count, 128)
    extras = (up_weight, conv_one, conv_two, face_links)
    packed, up_weight, conv_one, conv_two, face_links = call(
        functools.partial(pick_kernel, split, len(extras)),
        (shape(*blocks), *[shape(*extra.shape, dtype=extra.dtype) for extra in extras]),
        [
            pltpu.VMEM((1, bricks), jnp.int32),
            pltpu.VMEM((1, held, width), BF16),
            pltpu.VMEM((2, (bricks + 16) * tiles, 128), F32),
            pltpu.VMEM(blocks, F32),
            pltpu.SemaphoreType.DMA((2 + len(extras),)),
        ],
        hbm=range(2 + len(extras)),
        inputs=2 + len(extras),
    )(*[kept_in_hbm(operand) for operand in (active_blocks, coarse_latents, *extras)])
    received = exchanged(packed, ("space", "dp") if split else ("space",))
    window_half = shape(8 * tiles, 128)
    own, other = call(
        functools.partial(relay_kernel, split), (window_half, window_half), [pltpu.VMEM(blocks, F32)]
    )(received)
    if split:
        other = lax.ppermute(other, "dp", [(0, 1), (1, 0)])
    cost = pl.CostEstimate(flops=10**9, bytes_accessed=2 * 10**6, transcendentals=0)
    face = shape(BRICKS * FACE, LINE)
    halves = pltpu.VMEM((2, LINES + 8, HALF), F32)
    faces = pltpu.VMEM((BRICKS * FACE, LINE), F32)
    pool = pltpu.VMEM((2 * BRICKS * FACE, LINE), F32)
    volume = shape(ROWS, HALF)
    links = [pltpu.SMEM(face_links.shape, jnp.int32), pltpu.SemaphoreType.DMA]
    pad_shape = (3, BRICKS, EDGE + 2, 2 * EDGE, WIDE)
    pad = pltpu.VMEM(pad_shape, BF16)
    high, low, far, near = call(faces_kernel, (face,) * 4, [halves, faces])(cotangent)
    far = swapped(far, 1)
    near = swapped(near, 0)
    masks = shape(BRICKS * 6 * 2 * BRICKS, 128, dtype=F32)
    lifted_half = shape(2, 4 * CUBE, 128, dtype=F32)
    window_rows = pltpu.VMEM((8 * tiles + 8, 128), F32)
    band_one, band_back, masks, lifted_half = call(
        early_kernel,
        (shape(*BAND), shape(*BAND), masks, lifted_half),
        [window_rows, *links],
        hbm=(0,),
        inputs=5,
        cost=cost,
    )(face_links, own, up_weight, conv_one, conv_two)
    slope, hidden, turned, lifted_pad = call(
        first_kernel,
        (
            shape(ROWS, HALF, dtype=F32), volume, shape(HALF, ROWS), shape(*pad_shape),
        ),
        [pltpu.VMEM((2, 9 * CUBE, 128), F32), window_rows, *links],
        hbm=(0,),
        inputs=5,
    )(face_links, other, up_weight, band_one, lifted_half)
    share = 2 * -(-GROUPS * CHANNELS // everyone)
    packed_rows = (everyone * share, 128)
    sums, lifted = call(
        second_kernel,
        (shape(*packed_rows), volume),
        [pool, pool, pad, pltpu.VMEM(packed_rows, F32)],
        inputs=10,
    )(masks, cotangent, band_back, slope, turned, lifted_pad, high, low, far, near)
    parts = exchanged(sums)
    hidden_high, hidden_low, hidden_far, hidden_near = call(
        hidden_faces_kernel, (face,) * 4, [halves, faces], hbm=(1,), inputs=2
    )(hidden, parts)
    hidden_far = swapped(hidden_far, 1)
    hidden_near = swapped(hidden_near, 0)
    band_two = call(band_kernel, shape(*BAND), cost=cost)(conv_two)
    fine = call(fine_kernel, shape(*cotangent.shape), [pool, pool, pad], inputs=8, cost=cost)(
        masks, band_two, lifted, hidden, hidden_high, hidden_low, hidden_far, hidden_near
    )
    scale = 1.0 / math.sqrt(lax.axis_size("dp") * devices * BRICKS * EDGE**3)
    times = 4 if everyone % 32 == 0 else 1
    total = call(
        functools.partial(sum_kernel, everyone, scale),
        shape(*packed_rows),
        [
            pltpu.VMEM(packed_rows, F32),
            pltpu.VMEM((packed_rows[0] // times, 128), BF16),
            pltpu.SemaphoreType.DMA((times,)),
        ],
        out=pl.ANY,
    )(parts)
    gathered = exchanged(total)
    grads = shape(27, CHANNELS, CHANNELS, dtype=F32)
    block = pltpu.VMEM(grads.shape, F32)
    scratch = [pltpu.VMEM(packed_rows, F32), block, block]
    scratch += [pltpu.SemaphoreType.DMA((2, 3)), pltpu.SemaphoreType.DMA]
    grad_one, grad_two, fine = call(
        unpack_kernel, (grads, grads, shape(*fine.shape)), scratch, inputs=2, out=pl.ANY
    )(gathered, fine)
    return (fine, grad_one, grad_two)


def solution(mesh):
    return jax.shard_map(
        body,
        mesh=mesh,
        in_specs=(
            P("dp", "space", None),
            P("dp", None),
            P("dp", "space", None),
            P("dp", "space", None, None, None),
            P(),
            P(),
            P(),
        ),
        out_specs=(P("dp", "space", None, None, None), P(), P()),
        check_vma=False,
    )
```

```python
import functools
import math

import jax
import jax.numpy as jnp
from jax import lax
from jax.experimental import pallas as pl
from jax.experimental.pallas import tpu as pltpu
from jax.sharding import PartitionSpec as P

BF16 = jnp.bfloat16
F32 = jnp.float32
EDGE = 8
CHANNELS = 32
LINE = EDGE * CHANNELS
HALF = LINE // 2
WIDE = 2 * HALF
BRICKS = 2
CUBE = EDGE * EDGE
LINES = BRICKS * CUBE
BAND = (9, WIDE, HALF)
ROWS = 2 * LINES
FACE = 3 * EDGE
GROUPS = 7


def dot(left, right):
    return jnp.dot(left, right, preferred_element_type=F32)


def dot_rows(left, right):
    return lax.dot_general(left, right, (((0,), (0,)), ((), ())), preferred_element_type=F32)


def pair(halves_ref, start, count, stride=1):
    index = pl.ds(start, count, stride=stride) if stride > 1 else pl.ds(start, count)
    return halves_ref[0, index, :], halves_ref[1, index, :]


def lanes_of(shape):
    return lax.broadcasted_iota(jnp.int32, shape, len(shape) - 1)


def first_half(split):
    return lax.axis_index("dp") if split else 0


def pick_kernel(split, extras, ids_hbm, latents_hbm, *refs):
    brought = zip(refs[:extras], refs[extras + 1 : 2 * extras + 1])
    out_ref = refs[extras]
    ids_ref, latents_ref, rows_ref, blocks_ref, sems = refs[2 * extras + 1 :]
    ids_copy = pltpu.make_async_copy(ids_hbm, ids_ref, sems.at[0])
    latents_copy = pltpu.make_async_copy(latents_hbm, latents_ref, sems.at[1])
    ids_copy.start()
    latents_copy.start()
    others = [pltpu.make_async_copy(*pair, sems.at[2 + i]) for i, pair in enumerate(brought)]
    for copy in others:
        copy.start(priority=1)
    held, width = latents_ref.shape[1:]
    bricks = ids_ref.shape[1]
    tiles = width // 256
    margin = 8 * tiles
    empty = jnp.zeros((margin, 128), F32)
    for half in range(2):
        rows_ref[half, 0:margin] = empty
        rows_ref[half, margin + bricks * tiles :] = empty
    first = lax.axis_index("space") * held
    rows = lax.broadcasted_iota(jnp.int32, (held, bricks), 0) + first
    ids_copy.wait()
    hot = jnp.where(rows == ids_ref[...], 1.0, 0.0).astype(BF16)
    latents_copy.wait()
    picked = dot_rows(hot, latents_ref[0])
    for tile in range(2 * tiles):
        place = pl.ds(margin + tile % tiles, bricks, stride=tiles)
        rows_ref[tile // tiles, place, :] = picked[:, tile * 128 : tile * 128 + 128]
    count = 3 * BRICKS * tiles
    straight = first_half(split) == 0
    for receiver in range(blocks_ref.shape[0] // (2 * count)):
        start = margin + BRICKS * (receiver - 1) * tiles
        halves = [rows_ref[half, start : start + count] for half in range(2)]
        for half in range(2):
            block = jnp.where(straight, halves[half], halves[1 - half]) if split else halves[half]
            place = (2 * receiver + half) * count
            blocks_ref[place : place + count] = block
    out_ref[...] = blocks_ref[...].astype(BF16)
    for copy in others:
        copy.wait()


def relay_kernel(split, received_ref, own_out, other_out, rows_ref):
    rows_ref[...] = received_ref[...].astype(F32)
    count = own_out.shape[0] * 3 // 4
    sums = []
    for half in range(2):
        total = None
        for start in range(half * count, rows_ref.shape[0], 2 * count):
            piece = rows_ref[start : start + count]
            total = piece if total is None else total + piece
        sums.append(jnp.concatenate([total, jnp.zeros((count // 3, 128), F32)], axis=0))
    straight = first_half(split) == 0
    own_out[...] = jnp.where(straight, sums[0], sums[1]).astype(BF16)
    other_out[...] = jnp.where(straight, sums[1], sums[0]).astype(BF16)


def build_band(band_ref, rows):
    shape = (3 * CHANNELS, HALF)
    row = lax.broadcasted_iota(jnp.int32, shape, 0)
    target = CHANNELS - (row // CHANNELS) * CHANNELS + row % CHANNELS
    distance = lanes_of(shape) - target
    band_ref[:, HALF:, :] = jnp.zeros((9, HALF, HALF), BF16)
    for z in range(-1, 5):
        select = jnp.where(distance == z * CHANNELS, 1.0, 0.0).astype(BF16)
        block = dot(rows, select).astype(BF16)
        start = z % 8 * CHANNELS
        band_ref[:, start : start + CHANNELS, :] = block.reshape(9, CHANNELS, HALF)


def weight_rows(weights):
    cube = weights.reshape(9, 3, CHANNELS, CHANNELS)
    rows = jnp.concatenate([cube[:, 0], cube[:, 1], cube[:, 2]], axis=-1)
    return rows.reshape(9 * CHANNELS, 3 * CHANNELS).astype(BF16)


def flipped_rows(weights):
    cube = jnp.swapaxes(weights, 1, 2).reshape(9, 3, CHANNELS, CHANNELS)
    pieces = [jnp.concatenate([cube[8 - k, 2], cube[8 - k, 1], cube[8 - k, 0]], axis=-1) for k in range(9)]
    return jnp.concatenate(pieces, axis=0).astype(BF16)


def band_kernel(weights_ref, band_ref):
    build_band(band_ref, weight_rows(weights_ref[...].astype(F32)))


def lift(half_ref, up_ref, rows_ref, volumes_ref, half):
    tiles = half_ref.shape[0] // 8
    rows_ref[: 8 * tiles] = half_ref[...].astype(F32)
    cells = []
    for tile in range(tiles):
        rows = rows_ref[pl.ds(tile, 8, stride=tiles), :]
        cells += [rows[:, :64], rows[:, 64:]]
    lifted = dot(jnp.concatenate(cells, axis=0).astype(BF16), up_ref[...])
    lifted = lifted.astype(BF16).astype(F32)
    first = 4 * CUBE * half
    for cell in range(4):
        b, c = cell // 2, cell % 2
        for sub in range(16):
            line = first + 8 * (sub // 4 * EDGE + 4 * b + sub % 4)
            volumes_ref[c, line : line + 8, :] = lifted[cell * 8 : cell * 8 + 8, sub * 128 : sub * 128 + 128]


def early_kernel(
    links_in, own_ref, up_ref, one_ref, two_ref,
    band_ref, back_ref, masks_ref, volumes_out,
    rows_ref, links_ref, links_sem,
):
    links_copy = pltpu.make_async_copy(links_in, links_ref, links_sem)
    links_copy.start()
    lift(own_ref, up_ref, rows_ref, volumes_out, 0)
    build_band(band_ref, weight_rows(one_ref[...].astype(F32)))
    build_band(back_ref, flipped_rows(two_ref[...].astype(F32)))
    links_copy.wait()
    put_masks(masks_ref, links_ref)


def put_padded(pad_ref, brick, lines, x_low, x_high, y_low, y_high, z_low, z_high):
    def joined(halves, before, after):
        lane = lanes_of(halves[0].shape)
        first = jnp.where(lane < CHANNELS, halves[1], before)
        second = jnp.where(lane >= HALF - CHANNELS, halves[0], after)
        return jnp.concatenate([halves[0], first], axis=-1), jnp.concatenate([halves[1], second], axis=-1)

    inside = joined(lines, z_low, z_high)
    x_low, x_high, y_low, y_high = [joined(face, 0.0, 0.0) for face in (x_low, x_high, y_low, y_high)]
    none = jnp.zeros((1, WIDE), F32)
    shifted = [[], [], []]
    for half in range(2):
        slabs = jnp.concatenate([x_low[half][None], inside[half], x_high[half][None]], axis=0)
        row = lax.broadcasted_iota(jnp.int32, slabs.shape, 1)
        low = jnp.concatenate([none, y_low[half], none], axis=0)[:, None, :]
        high = jnp.concatenate([none, y_high[half], none], axis=0)[:, None, :]
        shifted[0].append(jnp.where(row == 0, low, pltpu.roll(slabs, 1, 1)))
        shifted[1].append(slabs)
        shifted[2].append(jnp.where(row == EDGE - 1, high, pltpu.roll(slabs, EDGE - 1, 1)))
    for dy in range(3):
        pad_ref[dy, brick] = jnp.concatenate(shifted[dy], axis=1).astype(BF16)


def window(pad_ref, k):
    return pad_ref[k % 3, :, k // 3 : k // 3 + EDGE].reshape(ROWS, WIDE)


def convolve(pad_ref, band_ref):
    both, last = None, None
    for dy in range(3):
        slabs = pad_ref[dy, :, : EDGE + 1].reshape(-1, WIDE)
        term = dot(slabs, jnp.concatenate([band_ref[dy], band_ref[3 + dy]], axis=1))
        both = term if both is None else both + term
        term = dot(window(pad_ref, 6 + dy), band_ref[6 + dy])
        last = term if last is None else last + term
    both = both.reshape(BRICKS, EDGE + 1, 2 * EDGE, 2 * HALF)
    total = both[:, :EDGE, :, :HALF] + both[:, 1:, :, HALF:]
    return total.reshape(ROWS, HALF) + last


def half_lines(values):
    cube = values.reshape(BRICKS, EDGE, 2, EDGE, HALF)
    return [(cube[brick, :, 0], cube[brick, :, 1]) for brick in range(BRICKS)]


def put_halves(halves_ref, start, bricks):
    for brick, lines in enumerate(bricks):
        for half in range(2):
            first = start + brick * CUBE
            halves_ref[half, first : first + CUBE, :] = lines[half].reshape(CUBE, HALF)


def cotangent_lines(cotangent_ref):
    cube = cotangent_ref[...].astype(F32).reshape(BRICKS, EDGE, EDGE, LINE)
    return [(cube[brick, :, :, :HALF], cube[brick, :, :, HALF:]) for brick in range(BRICKS)]


def pack_faces(faces_ref, base, halves_ref, start, high):
    x_face = pair(halves_ref, start + ((EDGE - 1) * EDGE if high else 0), EDGE)
    y_face = pair(halves_ref, start + (EDGE - 1 if high else 0), EDGE, EDGE)
    for half in range(2):
        lanes = slice(half * HALF, half * HALF + HALF)
        faces_ref[base : base + EDGE, lanes] = x_face[half]
        faces_ref[base + EDGE : base + 2 * EDGE, lanes] = y_face[half]
    tile = halves_ref[1 if high else 0, start : start + CUBE, :]
    lane = lanes_of((16, 128)) // CHANNELS
    packed = jnp.zeros((16, 128), F32)
    for part in range(4):
        shift = (part + 1 if high else part) % 4 * CHANNELS
        piece = tile[part * 16 : part * 16 + 16]
        packed = jnp.where(lane == part, pltpu.roll(piece, shift, 1) if shift else piece, packed)
    faces_ref[base + 2 * EDGE : base + FACE, :128] = packed[:8]
    faces_ref[base + 2 * EDGE : base + FACE, 128:] = packed[8:]


def pack_all(bricks, halves_ref, faces_ref, high_out, low_out):
    put_halves(halves_ref, 0, bricks)
    for high, out_ref in ((True, high_out), (False, low_out)):
        for brick in range(BRICKS):
            pack_faces(faces_ref, brick * FACE, halves_ref, brick * CUBE, high)
        out_ref[...] = faces_ref[...].astype(BF16)


def to_partners(high_ref, low_ref, far_out, near_out):
    even = lax.axis_index("space") % 2 == 0
    far_out[...] = jnp.where(even, low_ref[...], high_ref[...])
    near_out[...] = jnp.where(even, high_ref[...], low_ref[...])


def faces_kernel(cotangent_ref, high_out, low_out, far_out, near_out, halves_ref, faces_ref):
    pack_all(cotangent_lines(cotangent_ref), halves_ref, faces_ref, high_out, low_out)
    to_partners(high_out, low_out, far_out, near_out)


def unpack_depth(halves, high):
    packed = jnp.concatenate(halves, axis=0)
    pieces = []
    for part in range(4):
        shift = ((3 - part) if high else (4 - part)) % 4 * CHANNELS
        pieces.append(pltpu.roll(packed, shift, 1) if shift else packed)
    return jnp.concatenate(pieces, axis=0).reshape(EDGE, EDGE, 128)


def first_kernel(
    links_in, other_ref, up_ref, band_ref, lifted_half,
    slope_out, hidden_out, turned_out, pad_out,
    volumes_ref, rows_ref, links_ref, links_sem,
):
    links_copy = pltpu.make_async_copy(links_in, links_ref, links_sem)
    links_copy.start()
    position = lax.axis_index("space")
    volumes_ref[:, : 4 * CUBE] = lifted_half[...]
    lift(other_ref, up_ref, rows_ref, volumes_ref, 1)
    links_copy.wait()
    for brick in range(BRICKS):

        def near(face):
            link = links_ref[0, brick, face]
            index = jnp.clip(link - BRICKS * (position - 1), 0, 3 * BRICKS - 1)
            return index, jnp.where(link >= 0, 1.0, 0.0).astype(F32)

        def x_face(face):
            index, present = near(face)
            line = EDGE * (EDGE - 1) if face % 2 == 0 else 0
            return [half * present for half in pair(volumes_ref, line * 8 + index, EDGE, 8)]

        def y_face(face):
            index, present = near(face)
            line = EDGE - 1 if face % 2 == 0 else 0
            return [half * present for half in pair(volumes_ref, line * 8 + index, EDGE, 8 * EDGE)]

        def z_face(face):
            index, present = near(face)
            tile = volumes_ref[1 if face % 2 == 0 else 0, pl.ds(index, CUBE, stride=8), :] * present
            return tile.reshape(EDGE, EDGE, HALF)

        own = [half.reshape(EDGE, EDGE, HALF) for half in pair(volumes_ref, BRICKS + brick, CUBE, 8)]
        put_padded(pad_out, brick, own, x_face(0), x_face(1), y_face(2), y_face(3), z_face(4), z_face(5))
    pre = convolve(pad_out, band_ref)
    sigmoid = 1.0 / (1.0 + jnp.exp(-pre))
    hidden = (pre * sigmoid).astype(BF16)
    slope_out[...] = sigmoid * (1.0 + pre * (1.0 - sigmoid))
    hidden_out[...] = hidden
    turned_out[...] = jnp.transpose(hidden)


def hidden_faces_kernel(hidden_ref, _parts, high_out, low_out, far_out, near_out, halves_ref, faces_ref):
    pack_all(half_lines(hidden_ref[...].astype(F32)), halves_ref, faces_ref, high_out, low_out)
    to_partners(high_out, low_out, far_out, near_out)


def picked(outer, places):
    lane = lanes_of((CHANNELS, 128)) // CHANNELS
    found = None
    for block in range(4):
        start, tile = places[block]
        rows = outer[start : start + CHANNELS, tile * 128 : tile * 128 + 128]
        found = rows if found is None else jnp.where(lane == block, rows, found)
    return found


def fold(four):
    lane = lanes_of((CHANNELS, 128)) // CHANNELS
    total = None
    for turn in range(4):
        mixed = four[0]
        for n in range(1, len(four)):
            mixed = jnp.where(lane == (n + turn) % 4, four[n], mixed)
        if turn:
            mixed = pltpu.roll(mixed, 128 - turn * CHANNELS, 1)
        total = mixed if total is None else total + mixed
    return total


def diagonal(shift):
    places = [None] * 4
    for z in range(4):
        other = z + shift
        places[other % 4] = (z * CHANNELS, 0 if 0 <= other < 4 else 1)
    return places


def put_masks(masks_ref, links_ref):
    position = lax.axis_index("space")
    for brick in range(BRICKS):
        for face in range(6):
            first = links_ref[0, brick, face] - BRICKS * (position - 1 if face % 2 == 0 else position)
            for i in range(2 * BRICKS):
                row = (brick * 6 + face) * 2 * BRICKS + i
                masks_ref[row : row + 1, :] = jnp.full((1, 128), jnp.where(first == i, 1.0, 0.0).astype(F32))


def pad_all(pad_ref, bricks, masks_ref, high_pool, low_pool, high_own, low_own, far, near):
    position = lax.axis_index("space")
    half = BRICKS * FACE
    even = position % 2 == 0
    high_pool[0:half] = jnp.where(even, far[...], near[...]).astype(F32)
    high_pool[half:] = high_own[...].astype(F32)
    low_pool[0:half] = low_own[...].astype(F32)
    low_pool[half:] = jnp.where(even, near[...], far[...]).astype(F32)
    for brick, lines in enumerate(bricks):

        def face(number, axis):
            pool = high_pool if number % 2 == 0 else low_pool
            total = [0.0, 0.0]
            for i in range(2 * BRICKS):
                row = (brick * 6 + number) * 2 * BRICKS + i
                mask = masks_ref[row : row + 1, :]
                start = i * FACE + axis * EDGE
                for part in range(2):
                    found = pool[start : start + EDGE, part * HALF : part * HALF + HALF]
                    total[part] = total[part] + found * mask
            return total

        put_padded(
            pad_ref, brick, lines, face(0, 0), face(1, 0), face(2, 1), face(3, 1),
            unpack_depth(face(4, 2), True), unpack_depth(face(5, 2), False),
        )


def second_kernel(
    masks_ref, cotangent_ref, band_ref, slope_ref, hidden_ref, lifted_pad, high_own, low_own, far, near,
    sums_out, lifted_out,
    high_pool, low_pool, cotangent_pad, sums_ref,
):
    lifted_out[...] = window(lifted_pad, 4)[:, :HALF]
    bricks = cotangent_lines(cotangent_ref)
    pad_all(cotangent_pad, bricks, masks_ref, high_pool, low_pool, high_own, low_own, far, near)
    gradient = (convolve(cotangent_pad, band_ref) * slope_ref[...]).astype(BF16)
    gradient = jnp.transpose(gradient)
    hidden = hidden_ref[...]
    if sums_ref.shape[0] > 2 * GROUPS * CHANNELS:
        rest = sums_ref.shape[0] - 2 * GROUPS * CHANNELS
        sums_ref[2 * GROUPS * CHANNELS :] = jnp.zeros((rest, 128), F32)
    ones, twos = [], []
    for k in range(9):
        one = dot(gradient, window(lifted_pad, k))
        two = dot(hidden, window(cotangent_pad, 8 - k))
        ones += [picked(one, diagonal(part - 1)) for part in range(3)]
        twos += [picked(two, diagonal(1 - part)) for part in range(3)]
        while len(ones) >= 4 or (k == 8 and ones):
            group = (3 * k + 3 - len(ones)) // 4
            for first, blocks in ((0, ones), (GROUPS, twos)):
                start = (first + group) * CHANNELS
                sums_ref[start : start + CHANNELS] = fold(blocks[:4])
            ones, twos = ones[4:], twos[4:]
    sums_out[...] = sums_ref[...].astype(BF16)


def fine_kernel(
    masks_ref, band_ref, lifted_ref, hidden_ref, high_own, low_own, far, near,
    fine_out, high_pool, low_pool, hidden_pad,
):
    bricks = half_lines(hidden_ref[...].astype(F32))
    pad_all(hidden_pad, bricks, masks_ref, high_pool, low_pool, high_own, low_own, far, near)
    fine = lifted_ref[...].astype(F32) + convolve(hidden_pad, band_ref)
    fine = fine.reshape(LINES // EDGE, 2, EDGE, HALF)
    fine = jnp.concatenate([fine[:, 0], fine[:, 1]], axis=-1)
    fine_out[...] = fine.astype(BF16).reshape(fine_out.shape)


def sum_kernel(devices, scale, parts_ref, out_hbm, rows_ref, shares_ref, sems):
    rows_ref[...] = parts_ref[...].astype(F32)
    share = rows_ref.shape[0] // devices
    pieces = [rows_ref[share * i : share * i + share] for i in range(devices)]
    while len(pieces) > 1:
        pairs = [a + b for a, b in zip(pieces[::2], pieces[1::2])]
        pieces = pairs + pieces[len(pieces) - len(pieces) % 2 :]
    total = pieces[0] * scale
    some = shares_ref.shape[0]
    for i in range(some // share):
        rows_ref[share * i : share * i + share] = total
    shares_ref[...] = rows_ref[0:some].astype(BF16)
    copies = []
    for i in range(out_hbm.shape[0] // some):
        copies.append(pltpu.make_async_copy(shares_ref, out_hbm.at[pl.ds(some * i, some)], sems.at[i]))
        copies[-1].start()
    for copy in copies:
        copy.wait()


def unpack_kernel(sums_ref, fine_ref, one_out, two_out, fine_out, rows_ref, one_ref, two_ref, sems, fine_sem):
    fine_copy = pltpu.make_async_copy(fine_ref, fine_out, fine_sem)
    fine_copy.start(priority=1)
    rows_ref[...] = sums_ref[...].astype(F32)
    copies = []
    for which, (block_ref, out) in ((1, (two_ref, two_out)), (0, (one_ref, one_out))):
        for part, (first, last) in enumerate(((0, 2), (2, 4), (4, GROUPS))):
            for group in range(first, last):
                start = (which * GROUPS + group) * CHANNELS
                four = rows_ref[start : start + CHANNELS]
                turned = None if which else jnp.transpose(four)
                for n in range(min(4, 27 - 4 * group)):
                    if which:
                        block = pltpu.roll(four, 128 - n * CHANNELS, 1) if n else four
                        block_ref[4 * group + n] = block[:, :CHANNELS]
                    else:
                        block_ref[4 * group + n] = turned[CHANNELS * n : CHANNELS * n + CHANNELS]
            span = pl.ds(4 * first, min(4 * last, 27) - 4 * first)
            copies.append(pltpu.make_async_copy(block_ref.at[span], out.at[span], sems.at[which, part]))
            copies[-1].start()
    for copy in copies:
        copy.wait()
    fine_copy.wait()


def call(kernel, out_shape, scratch=(), hbm=(), inputs=1, limit=24, cost=None, out=pltpu.VMEM):
    spaces = [pl.ANY if i in hbm else pltpu.VMEM for i in range(inputs)]
    return pl.pallas_call(
        kernel,
        out_shape=out_shape,
        in_specs=[pl.BlockSpec(memory_space=space) for space in spaces],
        out_specs=jax.tree.map(lambda _: pl.BlockSpec(memory_space=out), out_shape),
        scratch_shapes=list(scratch),
        compiler_params=pltpu.CompilerParams(vmem_limit_bytes=limit * 2**20),
        cost_estimate=cost,
    )


def shape(*dims, dtype=BF16):
    return jax.ShapeDtypeStruct(dims, dtype)


def kept_in_hbm(value):
    return pltpu.with_memory_space_constraint(value, pltpu.HBM)


def swapped(value, first):
    pairs = [(i, i + 1) for i in range(first, lax.axis_size("space") - 1, 2)]
    return lax.ppermute(value, "space", pairs + [(target, source) for source, target in pairs])


def exchanged(rows, axes=("space", "dp")):
    count = math.prod(lax.axis_size(axis) for axis in axes)
    shares = rows.reshape(count, -1, 2, 128)
    shares = lax.all_to_all(shares, axes, split_axis=0, concat_axis=0, tiled=True)
    return shares.reshape(rows.shape)


def body(coarse_latents, active_blocks, face_links, cotangent, up_weight, conv_one, conv_two):
    devices = lax.axis_size("space")
    everyone = devices * lax.axis_size("dp")
    held, width = coarse_latents.shape[1:]
    bricks = active_blocks.shape[1]
    split = lax.axis_size("dp") == 2
    tiles = width // 256
    count = 3 * BRICKS * tiles
    blocks = (2 * devices * count, 128)
    extras = (up_weight, conv_one, conv_two, face_links)
    packed, up_weight, conv_one, conv_two, face_links = call(
        functools.partial(pick_kernel, split, len(extras)),
        (shape(*blocks), *[shape(*extra.shape, dtype=extra.dtype) for extra in extras]),
        [
            pltpu.VMEM((1, bricks), jnp.int32),
            pltpu.VMEM((1, held, width), BF16),
            pltpu.VMEM((2, (bricks + 16) * tiles, 128), F32),
            pltpu.VMEM(blocks, F32),
            pltpu.SemaphoreType.DMA((2 + len(extras),)),
        ],
        hbm=range(2 + len(extras)),
        inputs=2 + len(extras),
    )(*[kept_in_hbm(operand) for operand in (active_blocks, coarse_latents, *extras)])
    received = exchanged(packed, ("space", "dp") if split else ("space",))
    window_half = shape(8 * tiles, 128)
    own, other = call(
        functools.partial(relay_kernel, split), (window_half, window_half), [pltpu.VMEM(blocks, F32)]
    )(received)
    if split:
        other = lax.ppermute(other, "dp", [(0, 1), (1, 0)])
    cost = pl.CostEstimate(flops=10**9, bytes_accessed=2 * 10**6, transcendentals=0)
    face = shape(BRICKS * FACE, LINE)
    halves = pltpu.VMEM((2, LINES + 8, HALF), F32)
    faces = pltpu.VMEM((BRICKS * FACE, LINE), F32)
    pool = pltpu.VMEM((2 * BRICKS * FACE, LINE), F32)
    volume = shape(ROWS, HALF)
    links = [pltpu.SMEM(face_links.shape, jnp.int32), pltpu.SemaphoreType.DMA]
    pad_shape = (3, BRICKS, EDGE + 2, 2 * EDGE, WIDE)
    pad = pltpu.VMEM(pad_shape, BF16)
    high, low, far, near = call(faces_kernel, (face,) * 4, [halves, faces])(cotangent)
    far = swapped(far, 1)
    near = swapped(near, 0)
    masks = shape(BRICKS * 6 * 2 * BRICKS, 128, dtype=F32)
    lifted_half = shape(2, 4 * CUBE, 128, dtype=F32)
    window_rows = pltpu.VMEM((8 * tiles + 8, 128), F32)
    band_one, band_back, masks, lifted_half = call(
        early_kernel,
        (shape(*BAND), shape(*BAND), masks, lifted_half),
        [window_rows, *links],
        hbm=(0,),
        inputs=5,
        cost=cost,
    )(face_links, own, up_weight, conv_one, conv_two)
    slope, hidden, turned, lifted_pad = call(
        first_kernel,
        (
            shape(ROWS, HALF, dtype=F32), volume, shape(HALF, ROWS), shape(*pad_shape),
        ),
        [pltpu.VMEM((2, 9 * CUBE, 128), F32), window_rows, *links],
        hbm=(0,),
        inputs=5,
    )(face_links, other, up_weight, band_one, lifted_half)
    share = 2 * -(-GROUPS * CHANNELS // everyone)
    packed_rows = (everyone * share, 128)
    sums, lifted = call(
        second_kernel,
        (shape(*packed_rows), volume),
        [pool, pool, pad, pltpu.VMEM(packed_rows, F32)],
        inputs=10,
    )(masks, cotangent, band_back, slope, turned, lifted_pad, high, low, far, near)
    parts = exchanged(sums)
    hidden_high, hidden_low, hidden_far, hidden_near = call(
        hidden_faces_kernel, (face,) * 4, [halves, faces], hbm=(1,), inputs=2
    )(hidden, parts)
    hidden_far = swapped(hidden_far, 1)
    hidden_near = swapped(hidden_near, 0)
    band_two = call(band_kernel, shape(*BAND), cost=cost)(conv_two)
    fine = call(fine_kernel, shape(*cotangent.shape), [pool, pool, pad], inputs=8, cost=cost)(
        masks, band_two, lifted, hidden, hidden_high, hidden_low, hidden_far, hidden_near
    )
    scale = 1.0 / math.sqrt(lax.axis_size("dp") * devices * BRICKS * EDGE**3)
    times = 4 if everyone % 32 == 0 else 1
    total = call(
        functools.partial(sum_kernel, everyone, scale),
        shape(*packed_rows),
        [
            pltpu.VMEM(packed_rows, F32),
            pltpu.VMEM((packed_rows[0] // times, 128), BF16),
            pltpu.SemaphoreType.DMA((times,)),
        ],
        out=pl.ANY,
    )(parts)
    gathered = exchanged(total)
    grads = shape(27, CHANNELS, CHANNELS, dtype=F32)
    block = pltpu.VMEM(grads.shape, F32)
    scratch = [pltpu.VMEM(packed_rows, F32), block, block]
    scratch += [pltpu.SemaphoreType.DMA((2, 3)), pltpu.SemaphoreType.DMA]
    grad_one, grad_two, fine = call(
        unpack_kernel, (grads, grads, shape(*fine.shape)), scratch, inputs=2, out=pl.ANY
    )(gathered, fine)
    return (fine, grad_one, grad_two)


def solution(mesh):
    return jax.shard_map(
        body,
        mesh=mesh,
        in_specs=(
            P("dp", "space", None),
            P("dp", None),
            P("dp", "space", None),
            P("dp", "space", None, None, None),
            P(),
            P(),
            P(),
        ),
        out_specs=(P("dp", "space", None, None, None), P(), P()),
        check_vma=False,
    )
```
